32 devices in a mesh: depth: 8 (over z, y), chan: 4 (over x, core).
Axes of the slice: x: 2, y: 2, z: 4, core: 2. Of those that a mesh axis runs over, the one named last changes fastest.
Arguments:
- skip: bfloat16 [64, 16, 24, 128], P('chan', 'depth'), may hold values from -11 to 11
- cotangent: bfloat16 [64, 16, 24, 128], P('chan', 'depth'), may hold values from -6 to 6
- enc_conv1: float32 [128, 1728], P('chan'), may hold values from -0.15625 to 0.15625
- enc_conv2: float32 [128, 3456], P('chan'), may hold values from -0.109375 to 0.109375
- gate_proj: float32 [32, 192], P('chan'), may hold values from -0.4375 to 0.4375
- gate_vector: float32 [2, 32], P(None, 'chan'), may hold values from -3 to 3
- dec_conv1: float32 [64, 5184], P('chan'), may hold values from -0.078125 to 0.078125
- dec_conv2: float32 [64, 1728], P('chan'), may hold values from -0.15625 to 0.15625
- enc_norms: float32 [2, 2, 128], P(None, None, 'chan'), may hold values from 0.5 to 1.5
- dec_norms: float32 [2, 2, 64], P(None, None, 'chan'), may hold values from 0.5 to 1.5
- moment_enc_conv1: float32 [128, 1728], P('chan'), may hold values from -14 to 14
- moment_enc_conv2: float32 [128, 3456], P('chan'), may hold values from -14 to 14
- moment_gate_proj: float32 [32, 192], P('chan'), may hold values from -4 to 4
- moment_gate_vector: float32 [2, 32], P(None, 'chan'), may hold values from -14 to 14
- moment_dec_conv1: float32 [64, 5184], P('chan'), may hold values from -28 to 28
- moment_dec_conv2: float32 [64, 1728], P('chan'), may hold values from -40 to 40
- moment_enc_norms: float32 [2, 2, 128], P(None, None, 'chan'), may hold values from -20 to 20
- moment_dec_norms: float32 [2, 2, 64], P(None, None, 'chan'), may hold values from -64 to 64
- square_enc_conv1: float32 [128, 1728], P('chan'), may hold values from 0.24576 to 3.93216
- square_enc_conv2: float32 [128, 3456], P('chan'), may hold values from 0.24576 to 3.93216
- square_gate_proj: float32 [32, 192], P('chan'), may hold values from 0.0221184 to 0.3538944
- square_gate_vector: float32 [2, 32], P(None, 'chan'), may hold values from 0.24576 to 3.93216
- square_dec_conv1: float32 [64, 5184], P('chan'), may hold values from 0.98304 to 15.72864
- square_dec_conv2: float32 [64, 1728], P('chan'), may hold values from 2.21184 to 35.38944
- square_enc_norms: float32 [2, 2, 128], P(None, None, 'chan'), may hold values from 0.540672 to 8.84736
- square_dec_norms: float32 [2, 2, 64], P(None, None, 'chan'), may hold values from 6.144 to 98.304
Outputs:
- output: bfloat16 [64, 16, 24, 128], P('chan', 'depth')
- skip_grad: float32 [64, 16, 24, 128], P('chan', 'depth')
- new_enc_conv1: float32 [128, 1728], P('chan')
- new_moment_enc_conv1: float32 [128, 1728], P('chan')
- new_square_enc_conv1: float32 [128, 1728], P('chan')
- new_enc_conv2: float32 [128, 3456], P('chan')
- new_moment_enc_conv2: float32 [128, 3456], P('chan')
- new_square_enc_conv2: float32 [128, 3456], P('chan')
- new_gate_proj: float32 [32, 192], P('chan')
- new_moment_gate_proj: float32 [32, 192], P('chan')
- new_square_gate_proj: float32 [32, 192], P('chan')
- new_gate_vector: float32 [2, 32], P(None, 'chan')
- new_moment_gate_vector: float32 [2, 32], P(None, 'chan')
- new_square_gate_vector: float32 [2, 32], P(None, 'chan')
- new_dec_conv1: float32 [64, 5184], P('chan')
- new_moment_dec_conv1: float32 [64, 5184], P('chan')
- new_square_dec_conv1: float32 [64, 5184], P('chan')
- new_dec_conv2: float32 [64, 1728], P('chan')
- new_moment_dec_conv2: float32 [64, 1728], P('chan')
- new_square_dec_conv2: float32 [64, 1728], P('chan')
- new_enc_norms: float32 [2, 2, 128], P(None, None, 'chan')
- new_moment_enc_norms: float32 [2, 2, 128], P(None, None, 'chan')
- new_square_enc_norms: float32 [2, 2, 128], P(None, None, 'chan')
- new_dec_norms: float32 [2, 2, 64], P(None, None, 'chan')
- new_moment_dec_norms: float32 [2, 2, 64], P(None, None, 'chan')
- new_square_dec_norms: float32 [2, 2, 64], P(None, None, 'chan')
The draws below stay inside these ranges and needn't reach their ends.
All inputs are finite; a program needn't handle non-finite values.
Results may differ from the reference program's by a relative error of at most 0.02125.
The reference program's roundings to bfloat16 on the way (of `pooled`, `enc_hidden`, `coarse_out`, `up_full`, `gated` and `dec_hidden`) count: a program that leaves them out, or rounds other values in their place, can miss the bound.
Values may be sent and summed in bfloat16 or wider, within the bound.
A program may use at most 128 MiB of HBM per device.

```python
import math
import jax
import jax.numpy as jnp
from jax import lax

C_SKIP = 64
C_ENC = 128
C_GATE = 32
C_DEC = 64
ROWS = 24
PLANE = 128
STEP = 5
IN_DEC = 192
DEPTH = 16
VOXELS = 49152


def draw_skip(key, part):
    key = jax.random.fold_in(key, 11)
    shape = (C_SKIP, DEPTH, ROWS, PLANE)
    position = jnp.arange(DEPTH, dtype=jnp.float32) / max(DEPTH - 1, 1)
    base = jnp.clip(jax.random.normal(key, shape, jnp.float32), -6.0, 6.0) * 0.6
    rise = 3.0 ** position
    return (base * rise[None, :, None, None]).astype(jnp.bfloat16)


def shard_levels(own_key, shape, cuts, low, top_value):
    loudness, own = 1.0, jax.random.fold_in(own_key, 6)
    for axis_at, shards_of in cuts:
        steps = jnp.exp(jax.random.uniform(jax.random.fold_in(own, axis_at), (shards_of,), jnp.float32, low / len(cuts), top_value / len(cuts)))
        loudness = loudness * jnp.repeat(steps, shape[axis_at] // shards_of).reshape([-1 if axis == axis_at else 1 for axis in range(len(shape))])
    return loudness


def gaussian(own_key, extent, scale, reach, shards=(), kind=jnp.bfloat16):
    values = jax.random.normal(own_key, extent, jnp.float32) * scale
    if len(shards) > 0:
        values = shard_levels(own_key, extent, shards, -0.22, 0.18) * values
    return jnp.clip(values, min=-reach, max=reach).astype(kind)


def setup_inputs(seed: int = 0) -> dict:
    streams_of = jax.random.split(jax.random.key(seed), 27)
    skip = draw_skip(jax.random.fold_in(streams_of[26], 71), 0)
    cotangent = gaussian(streams_of[1], (C_DEC, DEPTH, ROWS, PLANE), 1.0, 6.0, ((0, 4), (1, 8)))
    enc_conv1 = gaussian(streams_of[2], (C_ENC, C_SKIP * 27), (C_SKIP * 27) ** -0.5, 0.15625, ((0, 4),), jnp.float32)
    enc_conv2 = gaussian(streams_of[3], (C_ENC, C_ENC * 27), (C_ENC * 27) ** -0.5, 0.109375, ((0, 4),), jnp.float32)
    gate_proj = gaussian(streams_of[4], (C_GATE, IN_DEC), IN_DEC ** -0.5, 0.4375, ((0, 4),), jnp.float32)
    gate_vector = gaussian(streams_of[5], (2, C_GATE), 0.5, 3.0, ((1, 4),), jnp.float32)
    dec_conv1 = gaussian(streams_of[6], (C_DEC, IN_DEC * 27), (IN_DEC * 27) ** -0.5, 0.078125, ((0, 4),), jnp.float32)
    dec_conv2 = gaussian(streams_of[7], (C_DEC, C_DEC * 27), (C_DEC * 27) ** -0.5, 0.15625, ((0, 4),), jnp.float32)
    enc_norms = jnp.clip(0.5 + 1.0 * jax.random.uniform(streams_of[8], (2, 2, C_ENC), jnp.float32) ** shard_levels(streams_of[8], (2, 2, C_ENC), ((2, 4),), -0.2, 0.2), 0.5, 1.5)
    dec_norms = jnp.clip(0.5 + 1.0 * jax.random.uniform(streams_of[9], (2, 2, C_DEC), jnp.float32) ** shard_levels(streams_of[9], (2, 2, C_DEC), ((2, 4),), -0.2, 0.2), 0.5, 1.5)
    moment_enc_conv1 = gaussian(streams_of[10], (C_ENC, C_SKIP * 27), (0.011 * VOXELS ** 0.5), 14.0, ((0, 4),), jnp.float32)
    moment_enc_conv2 = gaussian(streams_of[11], (C_ENC, C_ENC * 27), (0.011 * VOXELS ** 0.5), 14.0, ((0, 4),), jnp.float32)
    moment_gate_proj = gaussian(streams_of[12], (C_GATE, IN_DEC), (0.0033 * VOXELS ** 0.5), 4.0, ((0, 4),), jnp.float32)
    moment_gate_vector = gaussian(streams_of[13], (2, C_GATE), (0.011 * VOXELS ** 0.5), 14.0, ((1, 4),), jnp.float32)
    moment_dec_conv1 = gaussian(streams_of[14], (C_DEC, IN_DEC * 27), (0.022 * VOXELS ** 0.5), 28.0, ((0, 4),), jnp.float32)
    moment_dec_conv2 = gaussian(streams_of[15], (C_DEC, C_DEC * 27), (0.033 * VOXELS ** 0.5), 40.0, ((0, 4),), jnp.float32)
    moment_enc_norms = gaussian(streams_of[16], (2, 2, C_ENC), (0.0165 * VOXELS ** 0.5), 20.0, ((2, 4),), jnp.float32)
    moment_dec_norms = gaussian(streams_of[17], (2, 2, C_DEC), (0.055 * VOXELS ** 0.5), 64.0, ((2, 4),), jnp.float32)
    square_enc_conv1 = jnp.clip(jnp.exp(math.log(3.93216) - 2.7725887 * jax.random.uniform(streams_of[18], (C_ENC, C_SKIP * 27), jnp.float32) ** shard_levels(streams_of[18], (C_ENC, C_SKIP * 27), ((0, 4),), -0.2, 0.2)), 0.24576, 3.93216)
    square_enc_conv2 = jnp.clip(jnp.exp(math.log(3.93216) - 2.7725887 * jax.random.uniform(streams_of[19], (C_ENC, C_ENC * 27), jnp.float32) ** shard_levels(streams_of[19], (C_ENC, C_ENC * 27), ((0, 4),), -0.2, 0.2)), 0.24576, 3.93216)
    square_gate_proj = jnp.clip(jnp.exp(math.log(0.3538944) - 2.7725887 * jax.random.uniform(streams_of[20], (C_GATE, IN_DEC), jnp.float32) ** shard_levels(streams_of[20], (C_GATE, IN_DEC), ((0, 4),), -0.2, 0.2)), 0.0221184, 0.3538944)
    square_gate_vector = jnp.clip(jnp.exp(math.log(3.93216) - 2.7725887 * jax.random.uniform(streams_of[21], (2, C_GATE), jnp.float32) ** shard_levels(streams_of[21], (2, C_GATE), ((1, 4),), -0.2, 0.2)), 0.24576, 3.93216)
    square_dec_conv1 = jnp.clip(jnp.exp(math.log(15.72864) - 2.7725887 * jax.random.uniform(streams_of[22], (C_DEC, IN_DEC * 27), jnp.float32) ** shard_levels(streams_of[22], (C_DEC, IN_DEC * 27), ((0, 4),), -0.2, 0.2)), 0.98304, 15.72864)
    square_dec_conv2 = jnp.clip(jnp.exp(math.log(35.38944) - 2.7725887 * jax.random.uniform(streams_of[23], (C_DEC, C_DEC * 27), jnp.float32) ** shard_levels(streams_of[23], (C_DEC, C_DEC * 27), ((0, 4),), -0.2, 0.2)), 2.21184, 35.38944)
    square_enc_norms = jnp.clip(jnp.exp(math.log(8.84736) - 2.7950615 * jax.random.uniform(streams_of[24], (2, 2, C_ENC), jnp.float32) ** shard_levels(streams_of[24], (2, 2, C_ENC), ((2, 4),), -0.2, 0.2)), 0.540672, 8.84736)
    square_dec_norms = jnp.clip(jnp.exp(math.log(98.304) - 2.7725887 * jax.random.uniform(streams_of[25], (2, 2, C_DEC), jnp.float32) ** shard_levels(streams_of[25], (2, 2, C_DEC), ((2, 4),), -0.2, 0.2)), 6.144, 98.304)
    return dict(skip=skip, cotangent=cotangent, enc_conv1=enc_conv1, enc_conv2=enc_conv2, gate_proj=gate_proj, gate_vector=gate_vector, dec_conv1=dec_conv1, dec_conv2=dec_conv2, enc_norms=enc_norms, dec_norms=dec_norms, moment_enc_conv1=moment_enc_conv1, moment_enc_conv2=moment_enc_conv2, moment_gate_proj=moment_gate_proj, moment_gate_vector=moment_gate_vector, moment_dec_conv1=moment_dec_conv1, moment_dec_conv2=moment_dec_conv2, moment_enc_norms=moment_enc_norms, moment_dec_norms=moment_dec_norms, square_enc_conv1=square_enc_conv1, square_enc_conv2=square_enc_conv2, square_gate_proj=square_gate_proj, square_gate_vector=square_gate_vector, square_dec_conv1=square_dec_conv1, square_dec_conv2=square_dec_conv2, square_enc_norms=square_enc_norms, square_dec_norms=square_dec_norms)


@jax.custom_vjp
def low(v):
    return lax.optimization_barrier(v.astype(jnp.bfloat16)).astype(jnp.float32)

@jax.custom_vjp
def low_back(v):
    return v

def low_keep(v):
    return (low(v), None)

def low_pass(kept, grad):
    return (grad,)

def back_keep(v):
    return (v, None)

def back_low(kept, grad):
    return (low(grad),)
low.defvjp(low_keep, low_pass)
low_back.defvjp(back_keep, back_low)
norm_epsilon = 1e-05
conv_rate = 0.03
gate_rate = 0.1
vector_rate = 0.5
highest = lax.Precision.HIGHEST

def upsample_table(length):
    rows = jnp.arange(2 * length, dtype=jnp.int32)
    base = rows // 2
    other = jnp.clip(base + jnp.where(rows % 2 == 0, -1, 1), 0, length - 1)
    cols = jnp.arange(length, dtype=jnp.int32)
    near = (cols[None, :] == base[:, None]).astype(jnp.float32)
    far = (cols[None, :] == other[:, None]).astype(jnp.float32)
    return 0.75 * near + 0.25 * far

def upsample(values):
    depth_table = upsample_table(values.shape[1])
    row_table = upsample_table(values.shape[2])
    col_table = upsample_table(values.shape[3])
    out = jnp.einsum('ed,cdhw->cehw', depth_table, values, precision=highest)
    out = jnp.einsum('yh,cdhw->cdyw', row_table, out, precision=highest)
    return jnp.einsum('xw,cdhw->cdhx', col_table, out, precision=highest)

def pool_mean(values):
    chans, depth, rows, cols = values.shape
    return values.reshape(chans, depth // 2, 2, rows // 2, 2, cols // 2, 2).mean(axis=(2, 4, 6))

def conv3(values, weight):
    kernel = low(weight).reshape(weight.shape[0], values.shape[0], 3, 3, 3)
    return lax.conv_general_dilated(values[None], kernel, (1, 1, 1), ((1, 1), (1, 1), (1, 1)), precision=highest)[0]

def batch_norm(norm_output, norm_scale, norm_offset):
    channel_average = lax.optimization_barrier(jnp.mean(norm_output, axis=(1, 2, 3), keepdims=True))
    channel_variance = lax.optimization_barrier(jnp.mean(norm_output * norm_output, axis=(1, 2, 3), keepdims=True)) - channel_average * channel_average
    normalized_input = (norm_output - channel_average) * lax.rsqrt(channel_variance + norm_epsilon)
    return jax.nn.silu(norm_scale[:, None, None, None] * normalized_input + norm_offset[:, None, None, None])

def forward(skip, enc_conv1, enc_conv2, gate_proj, gate_vector, dec_conv1, dec_conv2, enc_norms, dec_norms):
    pooled = low(pool_mean(skip))
    enc_z1 = low_back(conv3(pooled, enc_conv1))
    enc_hidden = low(batch_norm(enc_z1, enc_norms[0, 0], enc_norms[1, 0]))
    enc_z2 = low_back(conv3(enc_hidden, enc_conv2))
    coarse_out = low(batch_norm(enc_z2, enc_norms[0, 1], enc_norms[1, 1]))
    up_full = low(upsample(coarse_out))
    enc_width = up_full.shape[0]
    gate_weight = low(gate_proj)
    pre = jnp.einsum('oc,cdhw->odhw', gate_weight[:, :enc_width], up_full, precision=highest)
    pre = pre + jnp.einsum('oc,cdhw->odhw', gate_weight[:, enc_width:], skip, precision=highest)
    pre = low_back(pre + gate_vector[0][:, None, None, None])
    logit = jnp.einsum('o,odhw->dhw', gate_vector[1], jax.nn.silu(pre), precision=highest)
    alpha = jax.nn.sigmoid(logit)
    gated = low(alpha[None] * skip)
    dec_input = jnp.concatenate([up_full, gated], 0)
    dec_z1 = low_back(conv3(dec_input, dec_conv1))
    dec_hidden = low(batch_norm(dec_z1, dec_norms[0, 0], dec_norms[1, 0]))
    dec_z2 = low_back(conv3(dec_hidden, dec_conv2))
    return batch_norm(dec_z2, dec_norms[0, 1], dec_norms[1, 1])

def adamw(weight, grad, moment, square, rate):
    new_moment = 0.9 * moment + 0.1 * grad
    new_square = 0.999 * square + 0.001 * grad * grad
    moment_hat = new_moment / (1.0 - 0.9 ** STEP)
    square_hat = new_square / (1.0 - 0.999 ** STEP)
    new_weight = weight - rate * (moment_hat / (jnp.sqrt(square_hat) + 1e-08) + 0.01 * weight)
    return (new_weight, new_moment, new_square)

def reference(skip, cotangent, enc_conv1, enc_conv2, gate_proj, gate_vector, dec_conv1, dec_conv2, enc_norms, dec_norms, moment_enc_conv1, moment_enc_conv2, moment_gate_proj, moment_gate_vector, moment_dec_conv1, moment_dec_conv2, moment_enc_norms, moment_dec_norms, square_enc_conv1, square_enc_conv2, square_gate_proj, square_gate_vector, square_dec_conv1, square_dec_conv2, square_enc_norms, square_dec_norms):
    params = (enc_conv1, enc_conv2, gate_proj, gate_vector, dec_conv1, dec_conv2, enc_norms, dec_norms)
    moments = (moment_enc_conv1, moment_enc_conv2, moment_gate_proj, moment_gate_vector, moment_dec_conv1, moment_dec_conv2, moment_enc_norms, moment_dec_norms)
    squares = (square_enc_conv1, square_enc_conv2, square_gate_proj, square_gate_vector, square_dec_conv1, square_dec_conv2, square_enc_norms, square_dec_norms)
    rates = (conv_rate, conv_rate, gate_rate, vector_rate, conv_rate, conv_rate, vector_rate, vector_rate)
    result, pullback = jax.vjp(forward, skip.astype(jnp.float32), *params)
    grads = pullback(cotangent.astype(jnp.float32))
    skip_grad = grads[0]
    upd = [adamw(params[i], grads[i + 1], moments[i], squares[i], rates[i]) for i in range(8)]
    return (result.astype(jnp.bfloat16), skip_grad, upd[0][0], upd[0][1], upd[0][2], upd[1][0], upd[1][1], upd[1][2], upd[2][0], upd[2][1], upd[2][2], upd[3][0], upd[3][1], upd[3][2], upd[4][0], upd[4][1], upd[4][2], upd[5][0], upd[5][1], upd[5][2], upd[6][0], upd[6][1], upd[6][2], upd[7][0], upd[7][1], upd[7][2])
```

```python
import functools

import jax
import jax.numpy as jnp
from jax import lax
from jax.experimental import pallas as pl
from jax.experimental.pallas import tpu as pltpu
from jax.sharding import PartitionSpec as P

STEP = 5
EPS = 1e-05
CONV_RATE = 0.03
GATE_RATE = 0.1
VECTOR_RATE = 0.5
LANES = 128
MESH = pl.DeviceIdType.MESH
F32 = jnp.float32
BF16 = jnp.bfloat16


def iota(shape, dim):
    return lax.broadcasted_iota(jnp.int32, shape, dim)


def dot(a, b):
    return jnp.dot(a, b, preferred_element_type=F32)


def dot_nt(a, b):
    return lax.dot_general(a, b, (((1,), (1,)), ((), ())), preferred_element_type=F32)


def from_left(v, width):
    return jnp.where(iota(v.shape, 1) == 0, 0.0, pltpu.roll(v, 1, 1))


def from_right(v, width):
    return jnp.where(iota(v.shape, 1) == width - 1, 0.0, pltpu.roll(v, LANES - 1, 1))


def keep(v, width):
    if width == LANES:
        return v
    return jnp.where(iota(v.shape, 1) < width, v, 0.0)


def split(v):
    high = v.astype(BF16)
    return jnp.concatenate([high, (v - high.astype(F32)).astype(BF16)], 1)


def storage(block):
    return BF16 if block % 16 == 0 else F32


def flat(ref, s, r):
    v = ref[s, r]
    if v.ndim == 3:
        v = v.reshape(v.shape[0] * v.shape[1], LANES)
    return v.astype(BF16)


class Dims:
    def __init__(self, nd, nc, skip, enc, dec, gate):
        self.nd, self.nc = nd, nc
        self.s, self.rows, self.cols = skip[1:]
        self.cs, self.ce, self.cd, self.g = skip[0], enc, dec, gate
        self.half, self.hcols = self.rows // 2, self.cols // 2
        self.fine_total = nd * self.s * self.rows * self.cols
        self.coarse_total = self.fine_total // 8
        self.enc_all = nc * enc
        self.skip_all = nc * skip[0]
        self.dec_all = nc * dec


GATHERS = ("pooled", "skip", "hidden", "coarse", "dhidden", "dz4", "dz3", "dz2", "dz1")
SUMS_ENC = ("e1", "e2", "b2", "b1")
SUMS_DEC = ("d1", "d2", "b4", "b3")


def kernel(
    dm,
    skip_ref,
    cot_ref,
    w1f, w2f, w3f, w4f,
    w1b, w2b, w3bu, w3bg, w4b,
    wg, wgu, wgs, gbias, gout,
    en, dn,
    out_ref, sg_ref,
    dw1, dw2, dw3, dw4, dgate, dvec, den1, den2, ddn1, ddn2,
    xp, xs, xh, xc, d1, xd, xz4, xz3, xz2, xz1,
    z1, z2, z3, z4, du_c, du_f, pre_ref, al_ref, pg_ref, ug_ref, dt, gg, cg,
    dzf, dzc, fs, fr, st_e, st_d,
    g_send, g_recv, t_send, t_recv, f_send, f_recv,
):
    nd, nc, S, R, H = dm.nd, dm.nc, dm.s, dm.rows, dm.half
    W, V = dm.cols, dm.hcols
    place = lax.axis_index("depth")
    me = lax.axis_index("chan")
    first, last = place == 0, place == nd - 1
    pending = []

    def peer_copy(src, dst, send, recv, depth, chan):
        return pltpu.make_async_remote_copy(
            src_ref=src, dst_ref=dst, send_sem=send, recv_sem=recv,
            device_id={"depth": depth, "chan": chan}, device_id_type=MESH,
        )

    def gather_parts(ref, which, pad):
        n = ref.shape[0] - 2
        rows = ref.shape[1] - 2 * pad
        k = GATHERS.index(which)
        span = pl.ds(pad, rows)
        parts = []
        for side, own, theirs, size in ((0, n, 0, 1), (2, 1, n + 1, 1), (1, 1, 1, n)):
            step = 1 - side
            for t in range(nc):
                if side == 1 and t == 0:
                    continue
                to, source = lax.rem(me + t, nc), lax.rem(me + nc - t, nc)
                can_send = None if side == 1 else (jnp.logical_not(last) if side == 0 else jnp.logical_not(first))
                can_recv = None if side == 1 else (jnp.logical_not(first) if side == 0 else jnp.logical_not(last))
                sems = (g_send.at[k, side * nc + t], g_recv.at[k, side * nc + t])
                out = lambda own=own, theirs=theirs, size=size, step=step, to=to, sems=sems: peer_copy(
                    ref.at[pl.ds(own, size), span, me],
                    ref.at[pl.ds(theirs, size), span, me],
                    *sems, place + step, to,
                )
                back = lambda theirs=theirs, size=size, source=source, sems=sems: peer_copy(
                    ref.at[pl.ds(theirs, size), span, source],
                    ref.at[pl.ds(theirs, size), span, source],
                    *sems, place, source,
                )
                parts.append((can_send, can_recv, out, back))
        return parts

    def guarded(cond, fn):
        if cond is None:
            fn()
        else:
            pl.when(cond)(fn)

    def gather_start(ref, which, pad):
        for can_send, _, out, _ in gather_parts(ref, which, pad):
            guarded(can_send, lambda out=out: out().start())
            pending.append((can_send, lambda out=out: out().wait_send()))

    def gather_wait(ref, which, pad):
        for _, can_recv, _, back in gather_parts(ref, which, pad):
            guarded(can_recv, lambda back=back: back().wait_recv())

    def sum_depth(ref, k, slot, tile):
        ref[slot, place] = tile

        def send(t, _):
            peer_copy(
                ref.at[slot, place], ref.at[slot, place], t_send.at[k, t], t_recv.at[k, t], lax.rem(place + t, nd), me
            ).start()
            return _

        def receive(t, _):
            source = lax.rem(place + nd - t, nd)
            peer_copy(
                ref.at[slot, source], ref.at[slot, source], t_send.at[k, t], t_recv.at[k, t], source, me
            ).wait_recv()
            return _

        def sent(t, _):
            peer_copy(
                ref.at[slot, place], ref.at[slot, place], t_send.at[k, t], t_recv.at[k, t], lax.rem(place + t, nd), me
            ).wait_send()
            return _

        lax.fori_loop(1, nd, send, 0)
        lax.fori_loop(1, nd, receive, 0)
        pending.append((None, lambda: lax.fori_loop(1, nd, sent, 0)))
        return jnp.sum(ref[slot], axis=0)

    def clear_edges(ref):
        n = ref.shape[0]
        blank = jnp.zeros(ref.shape[2:], ref.dtype)

        for s in range(n):
            ref[s, 0] = blank
            ref[s, ref.shape[1] - 1] = blank

    def clear_halos(ref):
        def clear(s):
            ref[s] = jnp.zeros(ref.shape[1:], ref.dtype)

        pl.when(first)(lambda: clear(0))
        pl.when(last)(lambda: clear(ref.shape[0] - 1))

    def conv(ref, weight, slices, rows, m, n, width, emit, init):
        per = rows // n

        def body(i, carry):
            d = i // per
            r0 = (i - d * per) * n
            x = jnp.concatenate(
                [
                    jnp.concatenate([flat(ref, d + kz, r0 + j) for j in range(n + 2)], 1)
                    for kz in range(3)
                ],
                0,
            )
            y = dot(weight[...], x)
            results = []
            for j in range(n):
                acc = []
                for kx in range(3):
                    terms = [
                        y[(3 * ky + kx) * m : (3 * ky + kx + 1) * m, (j + ky) * LANES : (j + ky + 1) * LANES]
                        for ky in range(3)
                    ]
                    acc.append(terms[0] + terms[1] + terms[2])
                results.append(keep(from_left(acc[0], width) + acc[1] + from_right(acc[2], width), width))
            return emit(d, r0, results, carry)

        return lax.fori_loop(0, slices * per, body, init)

    def weight_grad(ref, dz, out, slices, rows, n):
        per = rows // n
        out[...] = jnp.zeros(out.shape, F32)

        def body(i, carry):
            d = i // per
            r0 = (i - d * per) * n
            x = jnp.concatenate(
                [
                    jnp.concatenate([flat(ref, d + kz, r0 + 1 + j) for j in range(n)], 1)
                    for kz in range(3)
                ],
                0,
            )
            y = jnp.concatenate(
                [
                    jnp.concatenate([dz[kx, d, r0 + j + 2 - ky] for j in range(n)], 1)
                    for ky in range(3)
                    for kx in range(3)
                ],
                0,
            ).astype(BF16)
            out[...] += dot_nt(x, y)
            return carry

        lax.fori_loop(0, slices * per, body, 0)

    def conv_stats(ref, weight, z, slices, rows, m, n, width):
        def emit(d, r0, results, carry):
            total, square = carry
            for j, v in enumerate(results):
                z[d * rows + r0 + j] = v
                total, square = total + v, square + v * v
            return total, square

        blank = jnp.zeros((m, LANES), F32)
        total, square = conv(ref, weight, slices, rows, m, n, width, emit, (blank, blank))
        return pack(total, square)

    def pack(a, b):
        a = jnp.sum(a, axis=1, keepdims=True)
        b = jnp.sum(b, axis=1, keepdims=True)
        lane = iota((a.shape[0], LANES), 1)
        return jnp.where(lane == 0, a, jnp.where(lane == 1, b, 0.0))

    def moments(total, count):
        mean = total[:, 0:1] / count
        var = total[:, 1:2] / count - mean * mean
        return mean, lax.rsqrt(var + EPS)

    def norm_apply(z, mean, inv, gain, shift):
        xhat = (z - mean) * inv
        u = gain * xhat + shift
        return xhat, u, jax.nn.sigmoid(u)

    def norm_rows(z, stats, norm, emit, n):
        mean, inv = stats
        gain, shift = norm

        def body(i, carry):
            for j in range(n):
                p = i * n + j
                _, u, sigma = norm_apply(z[p], mean, inv, gain, shift)
                emit(p, u * sigma)
            return carry

        lax.fori_loop(0, z.shape[0] // n, body, 0)

    def norm_back_sums(z, du, stats, norm, grad, n):
        mean, inv = stats
        gain, shift = norm
        m = z.shape[1]

        def body(i, carry):
            a, b = carry
            for j in range(n):
                p = i * n + j
                xhat, u, sigma = norm_apply(z[p], mean, inv, gain, shift)
                v = grad(p) * sigma * (1.0 + u * (1.0 - sigma))
                du[p] = v
                a, b = a + v, b + v * xhat
            return a, b

        blank = jnp.zeros((m, LANES), F32)
        return pack(*lax.fori_loop(0, z.shape[0] // n, body, (blank, blank)))

    def norm_back(z, du, stats, norm, total, count, x, dz, rows, width, n):
        mean, inv = stats
        gain, _ = norm
        scale = gain * inv
        a = total[:, 0:1] / count
        b = total[:, 1:2] / count
        per = rows // n

        def body(i, carry):
            d = i // per
            r0 = (i - d * per) * n
            for j in range(n):
                p = i * n + j
                xhat = (z[p] - mean) * inv
                v = keep(scale * (du[p] - a - xhat * b), width)
                low = v.astype(BF16)
                x[1 + d, 1 + r0 + j, me] = low.astype(x.dtype)
                v = low.astype(F32)
                dz[0, d, 1 + r0 + j] = from_right(v, width).astype(dz.dtype)
                dz[1, d, 1 + r0 + j] = low.astype(dz.dtype)
                dz[2, d, 1 + r0 + j] = from_left(v, width).astype(dz.dtype)
            return carry

        lax.fori_loop(0, z.shape[0] // n, body, 0)

    hc = iota((LANES, LANES), 0)
    fc = iota((LANES, LANES), 1)
    pool = (hc // 2 == fc).astype(BF16)
    spread = (hc == fc // 2).astype(BF16)

    def up_table(coarse, fine):
        base = fine // 2
        other = jnp.clip(base + jnp.where(fine % 2 == 0, -1, 1), 0, V - 1)
        near = (coarse == base).astype(F32)
        far = (coarse == other).astype(F32)
        return (0.75 * near + 0.25 * far).astype(BF16)

    up = up_table(hc, fc)
    down = up_table(fc, hc)
    down2 = jnp.concatenate([down, down], 0)
    spread2 = jnp.concatenate([spread, spread], 0)

    clear_halos(xp)
    clear_edges(xp)
    for i in range(H):
        v = skip_ref[:, 2 * i : 2 * i + 2].reshape(2 * S * dm.cs, LANES)
        v = jnp.sum(dot(v, pool).reshape(2 * S, dm.cs, LANES), axis=0) * 0.125
        xp[1, 1 + i, me] = v.astype(BF16).astype(xp.dtype)
    gather_start(xp, "pooled", 1)
    for s in range(S):
        xs[1 + s, :, me] = skip_ref[s].astype(xs.dtype)
    clear_halos(xs)
    gather_start(xs, "skip", 0)
    for ref in (xh, xd, d1, xz4, xz3, xz2, xz1):
        clear_edges(ref)
    for ref in (xh, xd, xz4, xz3, xz2, xz1):
        clear_halos(ref)
    for ref in (dzf, dzc):
        for kx in range(3):
            for s in range(ref.shape[1]):
                ref[kx, s, 0] = jnp.zeros(ref.shape[3:], ref.dtype)
                ref[kx, s, ref.shape[2] - 1] = jnp.zeros(ref.shape[3:], ref.dtype)

    norm_e1 = (en[0, 0], en[1, 0])
    norm_e2 = (en[0, 1], en[1, 1])
    norm_d1 = (dn[0, 0], dn[1, 0])
    norm_d2 = (dn[0, 1], dn[1, 1])

    gather_wait(xp, "pooled", 1)
    total = sum_depth(st_e, 0, 0, conv_stats(xp, w1f, z1, 1, H, dm.ce, H // 2, V))
    stats_e1 = moments(total, dm.coarse_total)

    def keep_hidden(p, v):
        xh[1, 1 + p, me] = keep(v, V).astype(BF16).astype(xh.dtype)

    norm_rows(z1, stats_e1, norm_e1, keep_hidden, 4)
    gather_start(xh, "hidden", 1)
    gather_wait(xh, "hidden", 1)
    total = sum_depth(st_e, 1, 1, conv_stats(xh, w2f, z2, 1, H, dm.ce, H // 2, V))
    stats_e2 = moments(total, dm.coarse_total)

    def keep_coarse(p, v):
        xc[1, p, me] = keep(v, V).astype(BF16).astype(xc.dtype)

    norm_rows(z2, stats_e2, norm_e2, keep_coarse, 4)
    gather_start(xc, "coarse", 0)
    gather_wait(xc, "coarse", 0)

    def up_depth(i, carry):
        t = [
            dot(jnp.concatenate([flat(xc, s, i * 2 + j) for j in range(2)], 0), up).reshape(2, dm.enc_all, LANES)
            for s in range(3)
        ]
        below = jnp.where(first, t[1], t[0])
        above = jnp.where(last, t[1], t[2])
        near = 0.75 * t[1]
        here = 0.25 * t[1]
        rows = pl.ds(i * 2, 2)
        dt[0, rows] = jnp.where(first, 0.0, 0.75 * below + here)
        dt[1, rows] = near + 0.25 * below
        dt[2, rows] = near + 0.25 * above
        dt[3, rows] = jnp.where(last, 0.0, 0.75 * above + here)
        return carry

    lax.fori_loop(0, H // 2, up_depth, 0)

    def up_rows(i, carry):
        before, after = jnp.maximum(i - 1, 0), jnp.minimum(i + 1, H - 1)
        for s in range(S + 2):
            v = 0.75 * dt[s, i]
            d1[s, 1 + 2 * i, 0 : dm.enc_all] = (v + 0.25 * dt[s, before]).astype(BF16)
            d1[s, 2 + 2 * i, 0 : dm.enc_all] = (v + 0.25 * dt[s, after]).astype(BF16)
        return carry

    lax.fori_loop(0, H, up_rows, 0)

    gather_wait(xs, "skip", 0)
    gate_n = 4

    def gate(i, carry):
        s = i // (R // gate_n)
        r0 = (i - s * (R // gate_n)) * gate_n
        skips = [flat(xs, s, r0 + j) for j in range(gate_n)]
        x = jnp.concatenate(
            [
                jnp.concatenate([d1[s, 1 + r0 + j, 0 : dm.enc_all] for j in range(gate_n)], 1),
                jnp.concatenate(skips, 1),
            ],
            0,
        )
        pre = dot(wg[...], x) + gbias[...]
        act = pre * jax.nn.sigmoid(pre)
        alpha = jax.nn.sigmoid(jnp.sum(gout[...] * act, axis=0, keepdims=True))
        for j in range(gate_n):
            lanes = slice(j * LANES, (j + 1) * LANES)
            d1[s, 1 + r0 + j, dm.enc_all :] = (alpha[:, lanes] * skips[j].astype(F32)).astype(BF16)
            pre_ref[s, r0 + j] = pre[:, lanes]
            al_ref[s, r0 + j] = alpha[:, lanes]
        return carry

    lax.fori_loop(0, (S + 2) * R // gate_n, gate, 0)

    total = sum_depth(st_d, 4, 0, conv_stats(d1, w3f, z3, S, R, dm.cd, 6, W))
    stats_d1 = moments(total, dm.fine_total)

    def keep_dec(p, v):
        s = p // R
        xd[1 + s, 1 + p - s * R, me] = v.astype(BF16).astype(xd.dtype)

    norm_rows(z3, stats_d1, norm_d1, keep_dec, 8)
    gather_start(xd, "dhidden", 1)
    gather_wait(xd, "dhidden", 1)
    total = sum_depth(st_d, 5, 1, conv_stats(xd, w4f, z4, S, R, dm.cd, 6, W))
    stats_d2 = moments(total, dm.fine_total)

    def cot(p):
        s = p // R
        return cot_ref[s, p - s * R].astype(F32)

    total = sum_depth(st_d, 6, 2, norm_back_sums(z4, du_f, stats_d2, norm_d2, cot, 8))
    ddn2[...] = total
    norm_back(z4, du_f, stats_d2, norm_d2, total, dm.fine_total, xz4, dzf, R, W, 8)
    gather_start(xz4, "dz4", 1)

    def keep_result(p, v):
        s = p // R
        out_ref[s, p - s * R] = v.astype(BF16)

    norm_rows(z4, stats_d2, norm_d2, keep_result, 8)
    weight_grad(xd, dzf, dw4, S, R, 6)
    gather_wait(xz4, "dz4", 1)

    def keep_grad(d, r0, results, carry):
        for j, v in enumerate(results):
            gg[d * R + r0 + j] = v
        return carry

    conv(xz4, w4b, S, R, dm.cd, 6, W, keep_grad, 0)
    total = sum_depth(st_d, 7, 3, norm_back_sums(z3, du_f, stats_d1, norm_d1, lambda p: gg[p], 8))
    ddn1[...] = total
    norm_back(z3, du_f, stats_d1, norm_d1, total, dm.fine_total, xz3, dzf, R, W, 8)
    gather_start(xz3, "dz3", 1)
    weight_grad(d1, dzf, dw3, S, R, 6)
    gather_wait(xz3, "dz3", 1)

    def keep_up(d, r0, results, carry):
        for j, v in enumerate(results):
            ug_ref[d * R + r0 + j] = v
        return carry

    conv(xz3, w3bu, S, R, dm.ce, 4, W, keep_up, 0)

    def gate_back(d, r0, results, carry):
        bias, psi = carry
        for j, v in enumerate(results):
            p = d * R + r0 + j
            s, r = d + 1, r0 + j
            grad = jnp.zeros((1, LANES), F32)
            for t in range(nc):
                block = xs[s, r, lax.rem(me + t, nc)].astype(F32)
                grad += jnp.sum(v[t * dm.cs : (t + 1) * dm.cs] * block, axis=0, keepdims=True)
            alpha = al_ref[s, r]
            logit = grad * alpha * (1.0 - alpha)
            pre = pre_ref[s, r]
            sigma = jax.nn.sigmoid(pre)
            psi = psi + pre * sigma * logit
            low = (logit * gout[...] * sigma * (1.0 + pre * (1.0 - sigma))).astype(BF16)
            bias = bias + low.astype(F32)
            pg_ref[p] = low
            ug_ref[p] += dot(wgu[...], low)
            sg_ref[d, r] = alpha * v[0 : dm.cs] + dot(wgs[...], low)
        return bias, psi

    blank = jnp.zeros((dm.g, LANES), F32)
    bias, psi = conv(xz3, w3bg, S, R, dm.skip_all, 4, W, gate_back, (blank, blank))
    dvec[...] = pack(bias, psi)

    def down_rows(i, carry):
        terms = []
        for s in range(S):
            for j in range(2):
                r = i * 2 + j
                near = ug_ref[s * R + 2 * r] + ug_ref[s * R + 2 * r + 1]
                far = ug_ref[s * R + jnp.minimum(2 * r + 2, R - 1)] + ug_ref[s * R + jnp.maximum(2 * r - 1, 0)]
                terms.append(split(0.75 * near + 0.25 * far))
        v = dot(jnp.concatenate(terms, 0), down2).reshape(S, 2, dm.ce, LANES)
        even, odd = v[0], v[1]
        rows = pl.ds(i * 2, 2)
        fs[0, rows] = 0.25 * even
        fs[1, rows] = 0.25 * odd
        middle = 0.75 * (even + odd)
        cg[rows] = middle + jnp.where(first, 0.25 * even, 0.0) + jnp.where(last, 0.25 * odd, 0.0)
        return carry

    lax.fori_loop(0, H // 2, down_rows, 0)

    def fold(side, step):
        return peer_copy(fs.at[side], fr.at[1 - side], f_send.at[side], f_recv.at[1 - side], place + step, me)

    pl.when(jnp.logical_not(first))(lambda: fold(0, -1).start())
    pl.when(jnp.logical_not(last))(lambda: fold(1, 1).start())
    pending.append((jnp.logical_not(first), lambda: fold(0, -1).wait_send()))
    pending.append((jnp.logical_not(last), lambda: fold(1, 1).wait_send()))

    def fold_in(side):
        peer_copy(fs.at[side], fr.at[side], f_send.at[side], f_recv.at[side], place, me).wait_recv()
        cg[...] += fr[side]

    pl.when(jnp.logical_not(first))(lambda: fold_in(0))
    pl.when(jnp.logical_not(last))(lambda: fold_in(1))

    total = sum_depth(st_e, 2, 2, norm_back_sums(z2, du_c, stats_e2, norm_e2, lambda p: cg[p], 4))
    den2[...] = total
    norm_back(z2, du_c, stats_e2, norm_e2, total, dm.coarse_total, xz2, dzc, H, V, 4)
    gather_start(xz2, "dz2", 1)
    weight_grad(xh, dzc, dw2, 1, H, H // 2)
    gather_wait(xz2, "dz2", 1)

    def keep_coarse_grad(d, r0, results, carry):
        for j, v in enumerate(results):
            cg[r0 + j] = v
        return carry

    conv(xz2, w2b, 1, H, dm.ce, H // 2, V, keep_coarse_grad, 0)
    total = sum_depth(st_e, 3, 3, norm_back_sums(z1, du_c, stats_e1, norm_e1, lambda p: cg[p], 4))
    den1[...] = total
    norm_back(z1, du_c, stats_e1, norm_e1, total, dm.coarse_total, xz1, dzc, H, V, 4)
    gather_start(xz1, "dz1", 1)
    weight_grad(xp, dzc, dw1, 1, H, H // 2)

    dgate[...] = jnp.zeros(dgate.shape, F32)

    def gate_weight(i, carry):
        d = i // (R // 6)
        r0 = (i - d * (R // 6)) * 6
        x = jnp.concatenate(
            [
                jnp.concatenate([d1[1 + d, 1 + r0 + j, 0 : dm.enc_all] for j in range(6)], 1),
                jnp.concatenate([flat(xs, 1 + d, r0 + j) for j in range(6)], 1),
            ],
            0,
        )
        y = jnp.concatenate([pg_ref[d * R + r0 + j] for j in range(6)], 1)
        dgate[...] += dot_nt(x, y)
        return carry

    lax.fori_loop(0, S * R // 6, gate_weight, 0)
    gather_wait(xz1, "dz1", 1)

    def skip_grad(d, r0, results, carry):
        for j, v in enumerate(results):
            v = dot(split(v), spread2) * 0.125
            r = 2 * (r0 + j)
            for s in range(S):
                sg_ref[s, r] += v
                sg_ref[s, r + 1] += v
        return carry

    conv(xz1, w1b, 1, H, dm.cs, H // 2, V, skip_grad, 0)
    for cond, fn in pending:
        guarded(cond, fn)


def forward_weight(w, inputs):
    w = w.astype(BF16).reshape(w.shape[0], inputs, 3, 3, 3)
    return jnp.transpose(w, (3, 4, 0, 2, 1)).reshape(9 * w.shape[0], 3 * inputs)


def backward_weight(w):
    outputs, inputs = w.shape[:2]
    w = w.reshape(outputs, inputs, 3, 3, 3)[:, :, ::-1, ::-1, ::-1]
    return jnp.transpose(w, (3, 4, 1, 2, 0)).reshape(9 * inputs, 3 * outputs)


def weight_order(grad, inputs):
    outputs = grad.shape[1] // 9
    grad = grad.reshape(3, inputs, 3, 3, outputs)
    return jnp.transpose(grad, (4, 1, 0, 2, 3)).reshape(outputs, inputs * 27)


def adamw(weight, grad, moment, square, rate):
    new_moment = 0.9 * moment + 0.1 * grad
    new_square = 0.999 * square + 0.001 * grad * grad
    moment_hat = new_moment / (1.0 - 0.9**STEP)
    square_hat = new_square / (1.0 - 0.999**STEP)
    new_weight = weight - rate * (moment_hat / (jnp.sqrt(square_hat) + 1e-08) + 0.01 * weight)
    return (new_weight, new_moment, new_square)


def per_device(
    skip, cotangent, enc_conv1, enc_conv2, gate_proj, gate_vector, dec_conv1, dec_conv2, enc_norms, dec_norms, *states
):
    moments, squares = states[:8], states[8:]
    nd, nc = lax.axis_size("depth"), lax.axis_size("chan")
    me = lax.axis_index("chan")
    dm = Dims(nd, nc, skip.shape, enc_conv1.shape[0], dec_conv1.shape[0], gate_proj.shape[0] * nc)
    S, R, H = dm.s, dm.rows, dm.half

    def whole(w, inputs):
        full = lax.all_gather(w.astype(BF16), "chan", axis=0, tiled=True)
        return full.reshape(full.shape[0], inputs, 27)

    def mine(full, size):
        return lax.dynamic_slice_in_dim(full, me * size, size, axis=1)

    full3 = whole(dec_conv1, dm.enc_all + dm.skip_all)
    gated = jnp.roll(full3[:, dm.enc_all :], -me * dm.cs, axis=1)
    gate_full = lax.all_gather(gate_proj.astype(BF16), "chan", axis=0, tiled=True)
    vector_full = lax.all_gather(gate_vector, "chan", axis=1, tiled=True)
    inputs = (
        jnp.transpose(skip, (1, 2, 0, 3)),
        jnp.transpose(cotangent, (1, 2, 0, 3)),
        forward_weight(enc_conv1, dm.skip_all),
        forward_weight(enc_conv2, dm.enc_all),
        forward_weight(dec_conv1, dm.enc_all + dm.skip_all),
        forward_weight(dec_conv2, dm.dec_all),
        backward_weight(mine(whole(enc_conv1, dm.skip_all), dm.cs)),
        backward_weight(mine(whole(enc_conv2, dm.enc_all), dm.ce)),
        backward_weight(mine(full3[:, : dm.enc_all], dm.ce)),
        backward_weight(gated),
        backward_weight(mine(whole(dec_conv2, dm.dec_all), dm.cd)),
        gate_full,
        jnp.transpose(mine(gate_full[:, : dm.enc_all], dm.ce)),
        jnp.transpose(mine(gate_full[:, dm.enc_all :], dm.cs)),
        vector_full[0][:, None],
        vector_full[1][:, None],
        enc_norms[..., None],
        dec_norms[..., None],
    )
    shape = jax.ShapeDtypeStruct
    cin3 = dm.enc_all + dm.skip_all
    outs = (
        shape((S, R, dm.cd, LANES), BF16),
        shape((S, R, dm.cs, LANES), F32),
        shape((3 * dm.skip_all, 9 * dm.ce), F32),
        shape((3 * dm.enc_all, 9 * dm.ce), F32),
        shape((3 * cin3, 9 * dm.cd), F32),
        shape((3 * dm.dec_all, 9 * dm.cd), F32),
        shape((cin3, dm.g), F32),
        shape((dm.g, LANES), F32),
        shape((dm.ce, LANES), F32),
        shape((dm.ce, LANES), F32),
        shape((dm.cd, LANES), F32),
        shape((dm.cd, LANES), F32),
    )

    def ext(slices, rows, block):
        return pltpu.VMEM((slices, rows, nc, block, LANES), storage(block))

    scratch = [
        ext(3, H + 2, dm.cs),
        ext(S + 2, R, dm.cs),
        ext(3, H + 2, dm.ce),
        ext(3, H, dm.ce),
        pltpu.VMEM((S + 2, R + 2, cin3, LANES), BF16),
        ext(S + 2, R + 2, dm.cd),
        ext(S + 2, R + 2, dm.cd),
        ext(S + 2, R + 2, dm.cd),
        ext(3, H + 2, dm.ce),
        ext(3, H + 2, dm.ce),
        pltpu.VMEM((H, dm.ce, LANES), F32),
        pltpu.VMEM((H, dm.ce, LANES), F32),
        pltpu.VMEM((S * R, dm.cd, LANES), F32),
        pltpu.VMEM((S * R, dm.cd, LANES), F32),
        pltpu.VMEM((H, dm.ce, LANES), F32),
        pltpu.VMEM((S * R, dm.cd, LANES), F32),
        pltpu.VMEM((S + 2, R, dm.g, LANES), F32),
        pltpu.VMEM((S + 2, R, 1, LANES), F32),
        pltpu.VMEM((S * R, dm.g, LANES), BF16),
        pltpu.VMEM((S * R, dm.ce, LANES), F32),
        pltpu.VMEM((S + 2, H, dm.enc_all, LANES), F32),
        pltpu.VMEM((S * R, dm.cd, LANES), F32),
        pltpu.VMEM((H, dm.ce, LANES), F32),
        pltpu.VMEM((3, S, R + 2, dm.cd, LANES), storage(dm.cd)),
        pltpu.VMEM((3, 1, H + 2, dm.ce, LANES), storage(dm.ce)),
        pltpu.VMEM((2, H, dm.ce, LANES), F32),
        pltpu.VMEM((2, H, dm.ce, LANES), F32),
        pltpu.VMEM((4, nd, dm.ce, LANES), F32),
        pltpu.VMEM((4, nd, dm.cd, LANES), F32),
        pltpu.SemaphoreType.DMA((len(GATHERS), 3 * nc)),
        pltpu.SemaphoreType.DMA((len(GATHERS), 3 * nc)),
        pltpu.SemaphoreType.DMA((8, nd)),
        pltpu.SemaphoreType.DMA((8, nd)),
        pltpu.SemaphoreType.DMA((2,)),
        pltpu.SemaphoreType.DMA((2,)),
    ]
    vmem = pl.BlockSpec(memory_space=pltpu.VMEM)
    done = pl.pallas_call(
        functools.partial(kernel, dm),
        out_shape=outs,
        in_specs=[vmem] * len(inputs),
        out_specs=[vmem] * len(outs),
        scratch_shapes=scratch,
        compiler_params=pltpu.CompilerParams(
            has_side_effects=True, vmem_limit_bytes=60 * 1024 * 1024
        ),
        name="step",
    )(*inputs)
    out, sg, dw1, dw2, dw3, dw4, dgate, dvec, den1, den2, ddn1, ddn2 = done
    dw1, dw2, dw3, dw4, dgate, dvec = lax.psum((dw1, dw2, dw3, dw4, dgate, dvec), "depth")
    gate_rows = gate_proj.shape[0]
    dgate = jnp.transpose(lax.dynamic_slice_in_dim(dgate, me * gate_rows, gate_rows, axis=1))
    dvec = jnp.transpose(lax.dynamic_slice_in_dim(dvec, me * gate_rows, gate_rows, axis=0)[:, :2])

    def norm_grad(a, b):
        return jnp.stack([jnp.stack([a[:, 1], b[:, 1]], 0), jnp.stack([a[:, 0], b[:, 0]], 0)], 0)

    params = (enc_conv1, enc_conv2, gate_proj, gate_vector, dec_conv1, dec_conv2, enc_norms, dec_norms)
    grads = (
        weight_order(dw1, dm.skip_all),
        weight_order(dw2, dm.enc_all),
        dgate,
        dvec,
        weight_order(dw3, cin3),
        weight_order(dw4, dm.dec_all),
        norm_grad(den1, den2),
        norm_grad(ddn1, ddn2),
    )
    rates = (CONV_RATE, CONV_RATE, GATE_RATE, VECTOR_RATE, CONV_RATE, CONV_RATE, VECTOR_RATE, VECTOR_RATE)
    results = [jnp.transpose(out, (2, 0, 1, 3)), jnp.transpose(sg, (2, 0, 1, 3))]
    for args in zip(params, grads, moments, squares, rates):
        results.extend(adamw(*args))
    return tuple(results)


def solution(mesh):
    volume = P("chan", "depth", None, None)
    row, column, norms = P("chan", None), P(None, "chan"), P(None, None, "chan")
    params = (row, row, row, column, row, row, norms, norms)
    return jax.shard_map(
        per_device,
        mesh=mesh,
        in_specs=(volume, volume) + params * 3,
        out_specs=(volume, volume) + tuple(spec for spec in params for _ in range(3)),
        check_vma=False,
    )
```

```python
import functools

import jax
import jax.numpy as jnp
from jax import lax
from jax.experimental import pallas as pl
from jax.experimental.pallas import tpu as pltpu
from jax.sharding import PartitionSpec as P

STEP = 5
EPS = 1e-05
CONV_RATE = 0.03
GATE_RATE = 0.1
VECTOR_RATE = 0.5
LANES = 128
MESH = pl.DeviceIdType.MESH
F32 = jnp.float32
BF16 = jnp.bfloat16


def iota(shape, dim):
    return lax.broadcasted_iota(jnp.int32, shape, dim)


def dot(a, b):
    return jnp.dot(a, b, preferred_element_type=F32)


def dot_nt(a, b):
    return lax.dot_general(a, b, (((1,), (1,)), ((), ())), preferred_element_type=F32)


def from_left(v, width):
    return jnp.where(iota(v.shape, 1) == 0, 0.0, pltpu.roll(v, 1, 1))


def from_right(v, width):
    return jnp.where(iota(v.shape, 1) == width - 1, 0.0, pltpu.roll(v, LANES - 1, 1))


def keep(v, width):
    if width == LANES:
        return v
    return jnp.where(iota(v.shape, 1) < width, v, 0.0)


def split(v):
    high = v.astype(BF16)
    return jnp.concatenate([high, (v - high.astype(F32)).astype(BF16)], 1)


def storage(block):
    return BF16 if block % 16 == 0 else F32


def flat(ref, s, r):
    v = ref[s, r]
    if v.ndim == 3:
        v = v.reshape(v.shape[0] * v.shape[1], LANES)
    return v.astype(BF16)


class Dims:
    def __init__(self, nd, nc, skip, enc, dec, gate):
        self.nd, self.nc = nd, nc
        self.s, self.rows, self.cols = skip[1:]
        self.cs, self.ce, self.cd, self.g = skip[0], enc, dec, gate
        self.half, self.hcols = self.rows // 2, self.cols // 2
        self.fine_total = nd * self.s * self.rows * self.cols
        self.coarse_total = self.fine_total // 8
        self.enc_all = nc * enc
        self.skip_all = nc * skip[0]
        self.dec_all = nc * dec


GATHERS = ("pooled", "skip", "hidden", "coarse", "dhidden", "dz4", "dz3", "dz2", "dz1")
CONVS = ("enc1", "enc2", "dec1", "dec2")


class Conv:
    def __init__(self, dm, o, c, blocks):
        self.o, self.c, self.blocks = o, c, blocks
        self.length = 27 * c
        self.chunks = -(-self.length // LANES)
        self.per = LANES // o
        self.tiles = -(-9 // self.per)
        self.wide = self.tiles * LANES
        self.kind = storage(min(size for size, _ in blocks))
        self.count = 3 * c // 16 * self.tiles
        self.share = -(-self.count // dm.nd)


def kernel(
    dm,
    skip_ref, cot_ref, w1, w2, w3, w4, gate_ref, vector_ref, en_ref, dn_ref,
    out_ref, sg_ref, g1, g2, g3, g4, ggate, gvector, gen, gdn,
    xp, xs, xh, xc, d1, xd, xz4, xz3, xz2, xz1,
    z1, z2, z3, z4, du_c, du_f, pre_ref, al_ref, pg_ref, ug_ref, dt, gg, cg,
    dzf, dzc, fs, fr, st_e, st_d, st_g, rows_ref, turned, wide_ref, acc, gate_all, gate_t, gate_own, gate_block,
    wt1, wt2, wt3, wt4, wf1, wf2, wf3, wf4, wx1, wx2, wx3u, wx3g, wx4, wb1, wb2, wb3u, wb3g, wb4,
    gt1, gt2, gt3, gt4, gr1, gr2, gr3, gr4, ga1, ga2, ga3, ga4,
    g_send, g_recv, t_send, t_recv, f_send, f_recv, w_send, w_recv, v_send, v_recv, r_send, r_recv, a_send, a_recv,
):
    nd, nc, S, R, H = dm.nd, dm.nc, dm.s, dm.rows, dm.half
    W, V = dm.cols, dm.hcols
    place = lax.axis_index("depth")
    me = lax.axis_index("chan")
    first, last = place == 0, place == nd - 1
    convs = dm.convs
    pending = []

    def peer_copy(src, dst, send, recv, depth, chan):
        return pltpu.make_async_remote_copy(
            src_ref=src, dst_ref=dst, send_sem=send, recv_sem=recv,
            device_id={"depth": depth, "chan": chan}, device_id_type=MESH,
        )

    def gather_parts(ref, which, pad):
        n = ref.shape[0] - 2
        rows = ref.shape[1] - 2 * pad
        k = GATHERS.index(which)
        span = pl.ds(pad, rows)
        parts = []
        for side, own, theirs, size in ((0, n, 0, 1), (2, 1, n + 1, 1), (1, 1, 1, n)):
            step = 1 - side
            for t in range(nc):
                if side == 1 and t == 0:
                    continue
                to, source = lax.rem(me + t, nc), lax.rem(me + nc - t, nc)
                can_send = None if side == 1 else (jnp.logical_not(last) if side == 0 else jnp.logical_not(first))
                can_recv = None if side == 1 else (jnp.logical_not(first) if side == 0 else jnp.logical_not(last))
                sems = (g_send.at[k, side * nc + t], g_recv.at[k, side * nc + t])
                out = lambda own=own, theirs=theirs, size=size, step=step, to=to, sems=sems: peer_copy(
                    ref.at[pl.ds(own, size), span, me],
                    ref.at[pl.ds(theirs, size), span, me],
                    *sems, place + step, to,
                )
                back = lambda theirs=theirs, size=size, source=source, sems=sems: peer_copy(
                    ref.at[pl.ds(theirs, size), span, source],
                    ref.at[pl.ds(theirs, size), span, source],
                    *sems, place, source,
                )
                parts.append((can_send, can_recv, out, back))
        return parts

    def guarded(cond, fn):
        if cond is None:
            fn()
        else:
            pl.when(cond)(fn)

    def gather_start(ref, which, pad):
        for can_send, _, out, _ in gather_parts(ref, which, pad):
            guarded(can_send, lambda out=out: out().start())
            pending.append((can_send, lambda out=out: out().wait_send()))

    def gather_wait(ref, which, pad):
        for _, can_recv, _, back in gather_parts(ref, which, pad):
            guarded(can_recv, lambda back=back: back().wait_recv())

    def sum_copy(ref, k, slot, t):
        return peer_copy(
            ref.at[slot, place], ref.at[slot, place], t_send.at[k, t], t_recv.at[k, t], lax.rem(place + t, nd), me
        )

    def sum_start(ref, k, slot, tile):
        ref[slot, place] = tile

        def send(t, _):
            sum_copy(ref, k, slot, t).start()
            return _

        def sent(t, _):
            sum_copy(ref, k, slot, t).wait_send()
            return _

        lax.fori_loop(1, nd, send, 0)
        pending.append((None, lambda: lax.fori_loop(1, nd, sent, 0)))

    def sum_finish(ref, k, slot):
        def receive(t, _):
            source = lax.rem(place + nd - t, nd)
            peer_copy(
                ref.at[slot, source], ref.at[slot, source], t_send.at[k, t], t_recv.at[k, t], source, me
            ).wait_recv()
            return _

        lax.fori_loop(1, nd, receive, 0)
        return jnp.sum(ref[slot], axis=0)

    def turn_in(w, cv):
        def chunk(a):
            return jnp.transpose(jnp.concatenate([a] * cv.per, 0))

        full = cv.length // LANES

        def body(i, carry):
            at = pl.multiple_of(i * LANES, LANES)
            turned[pl.ds(at, LANES)] = chunk(w[:, pl.ds(at, LANES)])
            return carry

        lax.fori_loop(0, full, body, 0)
        if full < cv.chunks:
            a = w[:, full * LANES :]
            a = jnp.concatenate([a, jnp.zeros((cv.o, LANES - a.shape[1]), F32)], 1)
            turned[full * LANES : (full + 1) * LANES] = chunk(a)

    def prepare(k):
        cv, w, wt, wf = convs[k], (w1, w2, w3, w4)[k], (wt1, wt2, wt3, wt4)[k], (wf1, wf2, wf3, wf4)[k]
        turn_in(w, cv)
        group = iota((cv.c, LANES), 1) // cv.o
        for kz in range(3):
            for j in range(cv.tiles):
                tile = None
                for g in range(cv.per):
                    t = j * cv.per + g
                    if t < 9:
                        v = turned[pl.ds(9 * kz + t, cv.c, stride=27)]
                        tile = v if tile is None else jnp.where(group == g, v, tile)
                tile = tile.astype(BF16)
                wt[kz, :, j * LANES : (j + 1) * LANES] = tile.astype(wt.dtype)
                wide_ref[kz * cv.c : (kz + 1) * cv.c, j * LANES : (j + 1) * LANES] = tile.astype(F32)
        rows = -(-3 * cv.c // LANES) * LANES
        for i in range(rows // LANES):
            v = jnp.transpose(wide_ref[i * LANES : (i + 1) * LANES, 0 : cv.wide])
            size = min(LANES, 3 * cv.c - i * LANES)
            wf[:, i * LANES : i * LANES + size] = v[0 : 9 * cv.o, 0:size].astype(BF16)

    def weight_parts(k):
        cv, wt = convs[k], (wt1, wt2, wt3, wt4)[k]
        into = ((wx1,), (wx2,), (wx3u, wx3g), (wx4,))[k]
        parts = []
        for b, (size, start) in enumerate(cv.blocks):
            for t in range(1, nc):
                to, source = lax.rem(me + t, nc), lax.rem(me + nc - t, nc)
                at = start(to)
                sems = (w_send.at[k, b, t], w_recv.at[k, b, t])
                out = lambda b=b, at=at, size=size, to=to, sems=sems: peer_copy(
                    wt.at[:, pl.ds(at, size)], into[b].at[me], *sems, place, to
                )
                back = lambda b=b, source=source, sems=sems: peer_copy(
                    into[b].at[source], into[b].at[source], *sems, place, source
                )
                parts.append((out, back))
        return parts

    def weights_start(k):
        cv, wt = convs[k], (wt1, wt2, wt3, wt4)[k]
        into = ((wx1,), (wx2,), (wx3u, wx3g), (wx4,))[k]
        for b, (size, start) in enumerate(cv.blocks):
            into[b][me] = wt[:, pl.ds(start(me), size)]
        for out, _ in weight_parts(k):
            out().start()
            pending.append((None, lambda out=out: out().wait_send()))

    def weights_finish(k):
        cv = convs[k]
        into = ((wx1,), (wx2,), (wx3u, wx3g), (wx4,))[k]
        outs = ((wb1,), (wb2,), (wb3u, wb3g), (wb4,))[k]
        for _, back in weight_parts(k):
            back().wait_recv()
        for b, (size, _) in enumerate(cv.blocks):
            for t in range(9):
                pieces = [
                    into[b][j, 2 - kz, :, t * cv.o : (t + 1) * cv.o].astype(F32)
                    for kz in range(3)
                    for j in range(nc)
                ]
                outs[b][(8 - t) * size : (9 - t) * size] = jnp.concatenate(pieces, 1).astype(BF16)

    def reduce_copy(k, t):
        cv, gt, gr = convs[k], (gt1, gt2, gt3, gt4)[k], (gr1, gr2, gr3, gr4)[k]
        to = lax.rem(place + t, nd)
        return peer_copy(
            gt.at[pl.ds(to * cv.share, cv.share)], gr.at[place], r_send.at[k, t], r_recv.at[k, t], to, me
        )

    def reduce_start(k):
        cv, gt, gr = convs[k], (gt1, gt2, gt3, gt4)[k], (gr1, gr2, gr3, gr4)[k]

        def tile(i, carry):
            for j in range(cv.tiles):
                at = pl.multiple_of(i * 16, 16)
                gt[i * cv.tiles + j] = acc[pl.ds(at, 16), j * LANES : (j + 1) * LANES].astype(BF16)
            return carry

        lax.fori_loop(0, 3 * cv.c // 16, tile, 0)
        for i in range(cv.count, cv.share * nd):
            gt[i] = jnp.zeros((16, LANES), BF16)
        gr[place] = gt[pl.ds(place * cv.share, cv.share)]

        def send(t, _):
            reduce_copy(k, t).start()
            return _

        def sent(t, _):
            reduce_copy(k, t).wait_send()
            return _

        lax.fori_loop(1, nd, send, 0)
        pending.append((None, lambda: lax.fori_loop(1, nd, sent, 0)))

    def share_copy(k, t):
        cv, ga = convs[k], (ga1, ga2, ga3, ga4)[k]
        own = ga.at[pl.ds(place * cv.share, cv.share)]
        return peer_copy(own, own, a_send.at[k, t], a_recv.at[k, t], lax.rem(place + t, nd), me)

    def reduce_finish(k):
        cv, gr, ga = convs[k], (gr1, gr2, gr3, gr4)[k], (ga1, ga2, ga3, ga4)[k]

        def receive(t, _):
            source = lax.rem(place + nd - t, nd)
            peer_copy(gr.at[source], gr.at[source], r_send.at[k, t], r_recv.at[k, t], source, me).wait_recv()
            return _

        lax.fori_loop(1, nd, receive, 0)
        ga[pl.ds(place * cv.share, cv.share)] = jnp.sum(gr[...].astype(F32), axis=0).astype(BF16)

        def send(t, _):
            share_copy(k, t).start()
            return _

        def sent(t, _):
            share_copy(k, t).wait_send()
            return _

        lax.fori_loop(1, nd, send, 0)
        pending.append((None, lambda: lax.fori_loop(1, nd, sent, 0)))

    def gradient_out(k):
        cv, ga, out = convs[k], (ga1, ga2, ga3, ga4)[k], (g1, g2, g3, g4)[k]

        def receive(t, _):
            source = lax.rem(place + nd - t, nd)
            theirs = ga.at[pl.ds(source * cv.share, cv.share)]
            peer_copy(theirs, theirs, a_send.at[k, t], a_recv.at[k, t], source, me).wait_recv()
            return _

        lax.fori_loop(1, nd, receive, 0)
        group = iota((16, LANES), 1) // cv.o

        def scatter(i, carry):
            for kz in range(3):
                for j in range(cv.tiles):
                    v = ga[(kz * (cv.c // 16) + i) * cv.tiles + j].astype(F32)
                    for g in range(cv.per):
                        t = j * cv.per + g
                        if t < 9:
                            turned[pl.ds(9 * kz + t + i * (16 * 27), 16, stride=27)] = jnp.where(group == g, v, 0.0)
            return carry

        lax.fori_loop(0, cv.c // 16, scatter, 0)

        def chunk(at):
            v = jnp.transpose(turned[pl.ds(at, LANES)])
            return jnp.sum(v.reshape(cv.per, cv.o, LANES), axis=0)

        full = cv.length // LANES

        def body(i, carry):
            at = pl.multiple_of(i * LANES, LANES)
            out[:, pl.ds(at, LANES)] = chunk(at)
            return carry

        lax.fori_loop(0, full, body, 0)
        if full < cv.chunks:
            out[:, full * LANES :] = chunk(full * LANES)[:, 0 : cv.length - full * LANES]

    def column(row):
        n = row.shape[1]
        eye = iota((n, n), 0) == iota((n, n), 1)
        return jnp.sum(jnp.where(eye, row, 0.0), axis=1, keepdims=True)

    def row_of(col):
        n = col.shape[0]
        eye = iota((n, n), 0) == iota((n, n), 1)
        return jnp.sum(jnp.where(eye, col, 0.0), axis=0, keepdims=True)

    def clear_edges(ref):
        n = ref.shape[0]
        blank = jnp.zeros(ref.shape[2:], ref.dtype)

        for s in range(n):
            ref[s, 0] = blank
            ref[s, ref.shape[1] - 1] = blank

    def clear_halos(ref):
        def clear(s):
            ref[s] = jnp.zeros(ref.shape[1:], ref.dtype)

        pl.when(first)(lambda: clear(0))
        pl.when(last)(lambda: clear(ref.shape[0] - 1))

    def conv(ref, weight, slices, rows, m, n, width, emit, init):
        per = rows // n

        def body(i, carry):
            d = i // per
            r0 = (i - d * per) * n
            x = jnp.concatenate(
                [
                    jnp.concatenate([flat(ref, d + kz, r0 + j) for j in range(n + 2)], 1)
                    for kz in range(3)
                ],
                0,
            )
            y = dot(weight[...], x)
            results = []
            for j in range(n):
                acc = []
                for kx in range(3):
                    terms = [
                        y[(3 * ky + kx) * m : (3 * ky + kx + 1) * m, (j + ky) * LANES : (j + ky + 1) * LANES]
                        for ky in range(3)
                    ]
                    acc.append(terms[0] + terms[1] + terms[2])
                results.append(keep(from_left(acc[0], width) + acc[1] + from_right(acc[2], width), width))
            return emit(d, r0, results, carry)

        return lax.fori_loop(0, slices * per, body, init)

    def weight_grad(ref, dz, k, slices, rows, n):
        per = rows // n
        cv = convs[k]
        acc[0 : 3 * cv.c, 0 : cv.wide] = jnp.zeros((3 * cv.c, cv.wide), F32)

        def body(i, carry):
            d = i // per
            r0 = (i - d * per) * n
            x = jnp.concatenate(
                [
                    jnp.concatenate([flat(ref, d + kz, r0 + 1 + j) for j in range(n)], 1)
                    for kz in range(3)
                ],
                0,
            )
            y = jnp.concatenate(
                [
                    jnp.concatenate([dz[kx, d, r0 + j + 2 - ky] for j in range(n)], 1)
                    for ky in range(3)
                    for kx in range(3)
                ],
                0,
            ).astype(BF16)
            acc[0 : 3 * cv.c, 0 : 9 * cv.o] += dot_nt(x, y)
            return carry

        lax.fori_loop(0, slices * per, body, 0)

    def conv_stats(ref, weight, z, slices, rows, m, n, width):
        def emit(d, r0, results, carry):
            total, square = carry
            for j, v in enumerate(results):
                z[d * rows + r0 + j] = v
                total, square = total + v, square + v * v
            return total, square

        blank = jnp.zeros((m, LANES), F32)
        total, square = conv(ref, weight, slices, rows, m, n, width, emit, (blank, blank))
        return pack(total, square)

    def pack(a, b):
        a = jnp.sum(a, axis=1, keepdims=True)
        b = jnp.sum(b, axis=1, keepdims=True)
        lane = iota((a.shape[0], LANES), 1)
        return jnp.where(lane == 0, a, jnp.where(lane == 1, b, 0.0))

    def moments(total, count):
        mean = total[:, 0:1] / count
        var = total[:, 1:2] / count - mean * mean
        return mean, lax.rsqrt(var + EPS)

    def norm_apply(z, mean, inv, gain, shift):
        xhat = (z - mean) * inv
        u = gain * xhat + shift
        return xhat, u, jax.nn.sigmoid(u)

    def norm_rows(z, stats, norm, emit, n):
        mean, inv = stats
        gain, shift = norm

        def body(i, carry):
            for j in range(n):
                p = i * n + j
                _, u, sigma = norm_apply(z[p], mean, inv, gain, shift)
                emit(p, u * sigma)
            return carry

        lax.fori_loop(0, z.shape[0] // n, body, 0)

    def norm_back_sums(z, du, stats, norm, grad, n):
        mean, inv = stats
        gain, shift = norm
        m = z.shape[1]

        def body(i, carry):
            a, b = carry
            for j in range(n):
                p = i * n + j
                xhat, u, sigma = norm_apply(z[p], mean, inv, gain, shift)
                v = grad(p) * sigma * (1.0 + u * (1.0 - sigma))
                du[p] = v
                a, b = a + v, b + v * xhat
            return a, b

        blank = jnp.zeros((m, LANES), F32)
        return pack(*lax.fori_loop(0, z.shape[0] // n, body, (blank, blank)))

    def norm_back(z, du, stats, norm, total, count, x, dz, rows, width, n):
        mean, inv = stats
        gain, _ = norm
        scale = gain * inv
        a = total[:, 0:1] / count
        b = total[:, 1:2] / count
        per = rows // n

        def body(i, carry):
            d = i // per
            r0 = (i - d * per) * n
            for j in range(n):
                p = i * n + j
                xhat = (z[p] - mean) * inv
                v = keep(scale * (du[p] - a - xhat * b), width)
                low = v.astype(BF16)
                x[1 + d, 1 + r0 + j, me] = low.astype(x.dtype)
                v = low.astype(F32)
                dz[0, d, 1 + r0 + j] = from_right(v, width).astype(dz.dtype)
                dz[1, d, 1 + r0 + j] = low.astype(dz.dtype)
                dz[2, d, 1 + r0 + j] = from_left(v, width).astype(dz.dtype)
            return carry

        lax.fori_loop(0, z.shape[0] // n, body, 0)

    hc = iota((LANES, LANES), 0)
    fc = iota((LANES, LANES), 1)
    pool = (hc // 2 == fc).astype(BF16)
    spread = (hc == fc // 2).astype(BF16)

    def up_table(coarse, fine):
        base = fine // 2
        other = jnp.clip(base + jnp.where(fine % 2 == 0, -1, 1), 0, V - 1)
        near = (coarse == base).astype(F32)
        far = (coarse == other).astype(F32)
        return (0.75 * near + 0.25 * far).astype(BF16)

    up = up_table(hc, fc)
    down = up_table(fc, hc)
    down2 = jnp.concatenate([down, down], 0)
    spread2 = jnp.concatenate([spread, spread], 0)

    def take_rows(ref):
        for c in range(dm.cs):
            rows_ref[c * S * R : (c + 1) * S * R] = ref[c].astype(F32).reshape(S * R, LANES)

    def row(p):
        return rows_ref[pl.ds(p, dm.cs, stride=S * R)]

    clear_halos(xp)
    clear_edges(xp)
    take_rows(skip_ref)

    def take_skip(i, carry):
        parts = []
        for s in range(S):
            for j in range(2):
                v = row(s * R + 2 * i + j).astype(BF16)
                xs[1 + s, 2 * i + j, me] = v.astype(xs.dtype)
                parts.append(v)
        v = dot(jnp.concatenate(parts, 0), pool).reshape(2 * S, dm.cs, LANES)
        xp[1, 1 + i, me] = (jnp.sum(v, axis=0) * 0.125).astype(BF16).astype(xp.dtype)
        return carry

    lax.fori_loop(0, H, take_skip, 0)
    gather_start(xp, "pooled", 1)
    clear_halos(xs)
    gather_start(xs, "skip", 0)

    gq = dm.g // nc
    gate_all[me, :, 0 : gate_ref.shape[1]] = gate_ref[...]
    lane = iota((gq, LANES), 1)
    gate_all[me, :, 2 * LANES :] = jnp.where(
        lane == 0, column(vector_ref[0:1]), jnp.where(lane == 1, column(vector_ref[1:2]), 0.0)
    )
    for t in range(1, nc):
        to, source = lax.rem(me + t, nc), lax.rem(me + nc - t, nc)
        out = peer_copy(gate_all.at[me], gate_all.at[me], v_send.at[t], v_recv.at[t], place, to)
        out.start()
        pending.append((None, out.wait_send))

    prepare(0)
    for ref in (xh, xd, d1, xz4, xz3, xz2, xz1):
        clear_edges(ref)
    for ref in (xh, xd, xz4, xz3, xz2, xz1):
        clear_halos(ref)
    for ref in (dzf, dzc):
        for kx in range(3):
            for s in range(ref.shape[1]):
                ref[kx, s, 0] = jnp.zeros(ref.shape[3:], ref.dtype)
                ref[kx, s, ref.shape[2] - 1] = jnp.zeros(ref.shape[3:], ref.dtype)

    def norm_of(ref, layer):
        return column(ref[0, layer : layer + 1]), column(ref[1, layer : layer + 1])

    norm_e1, norm_e2 = norm_of(en_ref, 0), norm_of(en_ref, 1)
    norm_d1, norm_d2 = norm_of(dn_ref, 0), norm_of(dn_ref, 1)

    gather_wait(xp, "pooled", 1)
    sum_start(st_e, 0, 0, conv_stats(xp, wf1, z1, 1, H, dm.ce, H // 2, V))
    prepare(1)
    stats_e1 = moments(sum_finish(st_e, 0, 0), dm.coarse_total)

    def keep_hidden(p, v):
        xh[1, 1 + p, me] = keep(v, V).astype(BF16).astype(xh.dtype)

    norm_rows(z1, stats_e1, norm_e1, keep_hidden, 4)
    gather_start(xh, "hidden", 1)
    prepare(2)
    gather_wait(xh, "hidden", 1)
    sum_start(st_e, 1, 1, conv_stats(xh, wf2, z2, 1, H, dm.ce, H // 2, V))
    prepare(3)
    stats_e2 = moments(sum_finish(st_e, 1, 1), dm.coarse_total)

    def keep_coarse(p, v):
        xc[1, p, me] = keep(v, V).astype(BF16).astype(xc.dtype)

    norm_rows(z2, stats_e2, norm_e2, keep_coarse, 4)
    gather_start(xc, "coarse", 0)
    for k in (3, 2, 1, 0):
        weights_start(k)
    for t in range(1, nc):
        source = lax.rem(me + nc - t, nc)
        peer_copy(
            gate_all.at[source], gate_all.at[source], v_send.at[t], v_recv.at[t], place, source
        ).wait_recv()
    gate_full = gate_all[...].reshape(dm.g, 3 * LANES)
    wg = gate_full[:, 0 : dm.enc_all + dm.skip_all].astype(BF16)
    gbias = gate_full[:, 2 * LANES : 2 * LANES + 1]
    gout = gate_full[:, 2 * LANES + 1 : 2 * LANES + 2]
    gate_t[...] = jnp.transpose(gate_full[:, 0 : 2 * LANES])
    gate_own[...] = jnp.concatenate(
        [
            gate_t[pl.ds(pl.multiple_of(me * dm.ce, dm.ce), dm.ce)],
            gate_t[pl.ds(pl.multiple_of(dm.enc_all + me * dm.cs, dm.cs), dm.cs)],
        ],
        0,
    )
    gather_wait(xc, "coarse", 0)

    def up_depth(i, carry):
        t = [
            dot(jnp.concatenate([flat(xc, s, i * 2 + j) for j in range(2)], 0), up).reshape(2, dm.enc_all, LANES)
            for s in range(3)
        ]
        below = jnp.where(first, t[1], t[0])
        above = jnp.where(last, t[1], t[2])
        near = 0.75 * t[1]
        here = 0.25 * t[1]
        rows = pl.ds(i * 2, 2)
        dt[0, rows] = jnp.where(first, 0.0, 0.75 * below + here)
        dt[1, rows] = near + 0.25 * below
        dt[2, rows] = near + 0.25 * above
        dt[3, rows] = jnp.where(last, 0.0, 0.75 * above + here)
        return carry

    lax.fori_loop(0, H // 2, up_depth, 0)

    def up_rows(i, carry):
        before, after = jnp.maximum(i - 1, 0), jnp.minimum(i + 1, H - 1)
        for s in range(S + 2):
            v = 0.75 * dt[s, i]
            d1[s, 1 + 2 * i, 0 : dm.enc_all] = (v + 0.25 * dt[s, before]).astype(BF16)
            d1[s, 2 + 2 * i, 0 : dm.enc_all] = (v + 0.25 * dt[s, after]).astype(BF16)
        return carry

    lax.fori_loop(0, H, up_rows, 0)

    gather_wait(xs, "skip", 0)
    gate_n = 4

    def gate(i, carry):
        s = i // (R // gate_n)
        r0 = (i - s * (R // gate_n)) * gate_n
        skips = [flat(xs, s, r0 + j) for j in range(gate_n)]
        x = jnp.concatenate(
            [
                jnp.concatenate([d1[s, 1 + r0 + j, 0 : dm.enc_all] for j in range(gate_n)], 1),
                jnp.concatenate(skips, 1),
            ],
            0,
        )
        pre = dot(wg, x) + gbias
        act = pre * jax.nn.sigmoid(pre)
        alpha = jax.nn.sigmoid(jnp.sum(gout * act, axis=0, keepdims=True))
        for j in range(gate_n):
            lanes = slice(j * LANES, (j + 1) * LANES)
            d1[s, 1 + r0 + j, dm.enc_all :] = (alpha[:, lanes] * skips[j].astype(F32)).astype(BF16)
            pre_ref[s, r0 + j] = pre[:, lanes]
            al_ref[s, r0 + j] = alpha[:, lanes]
        return carry

    lax.fori_loop(0, (S + 2) * R // gate_n, gate, 0)

    sum_start(st_d, 4, 0, conv_stats(d1, wf3, z3, S, R, dm.cd, 6, W))
    weights_finish(3)
    stats_d1 = moments(sum_finish(st_d, 4, 0), dm.fine_total)

    def keep_dec(p, v):
        s = p // R
        xd[1 + s, 1 + p - s * R, me] = v.astype(BF16).astype(xd.dtype)

    norm_rows(z3, stats_d1, norm_d1, keep_dec, 8)
    gather_start(xd, "dhidden", 1)
    weights_finish(2)
    take_rows(cot_ref)
    gather_wait(xd, "dhidden", 1)
    sum_start(st_d, 5, 1, conv_stats(xd, wf4, z4, S, R, dm.cd, 6, W))
    weights_finish(1)
    weights_finish(0)
    stats_d2 = moments(sum_finish(st_d, 5, 1), dm.fine_total)

    sum_start(st_d, 6, 2, norm_back_sums(z4, du_f, stats_d2, norm_d2, row, 8))

    def keep_result(p, v):
        s = p // R
        out_ref[s, p - s * R] = v.astype(BF16)

    norm_rows(z4, stats_d2, norm_d2, keep_result, 8)
    total_d2 = sum_finish(st_d, 6, 2)
    norm_back(z4, du_f, stats_d2, norm_d2, total_d2, dm.fine_total, xz4, dzf, R, W, 8)
    gather_start(xz4, "dz4", 1)
    weight_grad(xd, dzf, 3, S, R, 6)
    reduce_start(3)
    gather_wait(xz4, "dz4", 1)

    def keep_grad(d, r0, results, carry):
        for j, v in enumerate(results):
            gg[d * R + r0 + j] = v
        return carry

    conv(xz4, wb4, S, R, dm.cd, 6, W, keep_grad, 0)
    sum_start(st_d, 7, 3, norm_back_sums(z3, du_f, stats_d1, norm_d1, lambda p: gg[p], 8))
    total_d1 = sum_finish(st_d, 7, 3)
    norm_back(z3, du_f, stats_d1, norm_d1, total_d1, dm.fine_total, xz3, dzf, R, W, 8)
    gather_start(xz3, "dz3", 1)
    reduce_finish(3)
    weight_grad(d1, dzf, 2, S, R, 6)
    reduce_start(2)
    gather_wait(xz3, "dz3", 1)

    def keep_up(d, r0, results, carry):
        for j, v in enumerate(results):
            ug_ref[d * R + r0 + j] = v
        return carry

    conv(xz3, wb3u, S, R, dm.ce, 4, W, keep_up, 0)

    def gate_back(d, r0, results, carry):
        bias, psi = carry
        lows = []
        for j, v in enumerate(results):
            s, r = d + 1, r0 + j
            grad = jnp.sum(v * flat(xs, s, r).astype(F32), axis=0, keepdims=True)
            alpha = al_ref[s, r]
            logit = grad * alpha * (1.0 - alpha)
            pre = pre_ref[s, r]
            sigma = jax.nn.sigmoid(pre)
            psi = psi + pre * sigma * logit
            low = (logit * gout * sigma * (1.0 + pre * (1.0 - sigma))).astype(BF16)
            bias = bias + low.astype(F32)
            pg_ref[d * R + r] = low
            lows.append(low)
            for t in range(nc):
                gg[t] = v[t * dm.cs : (t + 1) * dm.cs]
            sg_ref[d, r] = alpha * gg[me]
        back = dot(gate_own[...].astype(BF16), jnp.concatenate(lows, 1))
        for j in range(len(results)):
            lanes = slice(j * LANES, (j + 1) * LANES)
            ug_ref[d * R + r0 + j] += back[0 : dm.ce, lanes]
            sg_ref[d, r0 + j] += back[dm.ce :, lanes]
        return bias, psi

    blank = jnp.zeros((dm.g, LANES), F32)
    bias, psi = conv(xz3, wb3g, S, R, dm.skip_all, 4, W, gate_back, (blank, blank))

    def down_rows(i, carry):
        terms = []
        for s in range(S):
            for j in range(2):
                r = i * 2 + j
                near = ug_ref[s * R + 2 * r] + ug_ref[s * R + 2 * r + 1]
                far = ug_ref[s * R + jnp.minimum(2 * r + 2, R - 1)] + ug_ref[s * R + jnp.maximum(2 * r - 1, 0)]
                terms.append(split(0.75 * near + 0.25 * far))
        v = dot(jnp.concatenate(terms, 0), down2).reshape(S, 2, dm.ce, LANES)
        even, odd = v[0], v[1]
        rows = pl.ds(i * 2, 2)
        fs[0, rows] = 0.25 * even
        fs[1, rows] = 0.25 * odd
        middle = 0.75 * (even + odd)
        cg[rows] = middle + jnp.where(first, 0.25 * even, 0.0) + jnp.where(last, 0.25 * odd, 0.0)
        return carry

    lax.fori_loop(0, H // 2, down_rows, 0)

    def fold(side, step):
        return peer_copy(fs.at[side], fr.at[1 - side], f_send.at[side], f_recv.at[1 - side], place + step, me)

    pl.when(jnp.logical_not(first))(lambda: fold(0, -1).start())
    pl.when(jnp.logical_not(last))(lambda: fold(1, 1).start())
    pending.append((jnp.logical_not(first), lambda: fold(0, -1).wait_send()))
    pending.append((jnp.logical_not(last), lambda: fold(1, 1).wait_send()))
    reduce_finish(2)

    def fold_in(side):
        peer_copy(fs.at[side], fr.at[side], f_send.at[side], f_recv.at[side], place, me).wait_recv()
        cg[...] += fr[side]

    pl.when(jnp.logical_not(first))(lambda: fold_in(0))
    pl.when(jnp.logical_not(last))(lambda: fold_in(1))

    sum_start(st_e, 2, 2, norm_back_sums(z2, du_c, stats_e2, norm_e2, lambda p: cg[p], 4))

    columns = gate_ref.shape[1]
    acc[0 : dm.g, 0:columns] = jnp.zeros((dm.g, columns), F32)

    def gate_weight(i, carry):
        d = i // (R // 6)
        r0 = (i - d * (R // 6)) * 6
        x = jnp.concatenate(
            [
                jnp.concatenate([d1[1 + d, 1 + r0 + j, 0 : dm.enc_all] for j in range(6)], 1),
                jnp.concatenate([flat(xs, 1 + d, r0 + j) for j in range(6)], 1),
            ],
            0,
        )
        y = jnp.concatenate([pg_ref[d * R + r0 + j] for j in range(6)], 1)
        acc[0 : dm.g, 0:columns] += dot_nt(y, x)
        return carry

    lax.fori_loop(0, S * R // 6, gate_weight, 0)
    vectors = pack(bias, psi)
    for j in range(nc):
        mine = slice(j * gq, (j + 1) * gq)
        gate_block[j, :, 0:columns] = acc[mine, 0:columns]
        gate_block[j, :, columns : 2 * LANES] = jnp.zeros((gq, 2 * LANES - columns), F32)
        gate_block[j, :, 2 * LANES :] = vectors[mine]
    sum_start(st_g, 8, 0, gate_block[me])
    total_e2 = sum_finish(st_e, 2, 2)
    norm_back(z2, du_c, stats_e2, norm_e2, total_e2, dm.coarse_total, xz2, dzc, H, V, 4)
    gather_start(xz2, "dz2", 1)
    weight_grad(xh, dzc, 1, 1, H, H // 2)
    reduce_start(1)
    gradient_out(3)
    gather_wait(xz2, "dz2", 1)

    def keep_coarse_grad(d, r0, results, carry):
        for j, v in enumerate(results):
            cg[r0 + j] = v
        return carry

    conv(xz2, wb2, 1, H, dm.ce, H // 2, V, keep_coarse_grad, 0)
    sum_start(st_e, 3, 3, norm_back_sums(z1, du_c, stats_e1, norm_e1, lambda p: cg[p], 4))
    reduce_finish(1)
    total_e1 = sum_finish(st_e, 3, 3)
    norm_back(z1, du_c, stats_e1, norm_e1, total_e1, dm.coarse_total, xz1, dzc, H, V, 4)
    gather_start(xz1, "dz1", 1)
    weight_grad(xp, dzc, 0, 1, H, H // 2)
    reduce_start(0)
    gradient_out(2)
    gather_wait(xz1, "dz1", 1)

    def skip_grad(d, r0, results, carry):
        for j, v in enumerate(results):
            v = dot(split(v), spread2) * 0.125
            r = 2 * (r0 + j)
            for s in range(S):
                sg_ref[s, r] += v
                sg_ref[s, r + 1] += v
        return carry

    conv(xz1, wb1, 1, H, dm.cs, H // 2, V, skip_grad, 0)
    reduce_finish(0)
    gradient_out(1)
    gate_total = sum_finish(st_g, 8, 0)
    ggate[...] = gate_total[:, 0:columns]
    gvector[0:1] = row_of(gate_total[:, 2 * LANES : 2 * LANES + 1])
    gvector[1:2] = row_of(gate_total[:, 2 * LANES + 1 : 2 * LANES + 2])
    for ref, totals in ((gen, (total_e1, total_e2)), (gdn, (total_d1, total_d2))):
        for layer, total in enumerate(totals):
            ref[0, layer : layer + 1] = row_of(total[:, 1:2])
            ref[1, layer : layer + 1] = row_of(total[:, 0:1])
    gradient_out(0)
    for cond, fn in pending:
        guarded(cond, fn)


def adamw(weight, grad, moment, square, rate):
    new_moment = 0.9 * moment + 0.1 * grad
    new_square = 0.999 * square + 0.001 * grad * grad
    moment_hat = new_moment / (1.0 - 0.9**STEP)
    square_hat = new_square / (1.0 - 0.999**STEP)
    new_weight = weight - rate * (moment_hat / (jnp.sqrt(square_hat) + 1e-08) + 0.01 * weight)
    return (new_weight, new_moment, new_square)


RATES = (CONV_RATE, CONV_RATE, GATE_RATE, VECTOR_RATE, CONV_RATE, CONV_RATE, VECTOR_RATE, VECTOR_RATE)


def update_kernel(*refs):
    n = len(RATES)
    params, grads, moments, squares = (refs[i * n : (i + 1) * n] for i in range(4))
    outs = refs[4 * n :]
    for k, rate in enumerate(RATES):
        rows = params[k].shape[0]
        step = 8 if rows % 8 == 0 and rows > 8 else rows
        for r in range(0, rows, step):
            at = slice(r, r + step)
            new = adamw(params[k][at], grads[k][at], moments[k][at], squares[k][at], rate)
            for ref, value in zip(outs[3 * k : 3 * k + 3], new):
                ref[at] = value


def per_device(
    skip, cotangent, enc_conv1, enc_conv2, gate_proj, gate_vector, dec_conv1, dec_conv2, enc_norms, dec_norms, *states
):
    nd, nc = lax.axis_size("depth"), lax.axis_size("chan")
    dm = Dims(nd, nc, skip.shape, enc_conv1.shape[0], dec_conv1.shape[0], gate_proj.shape[0] * nc)
    S, R, H = dm.s, dm.rows, dm.half
    cin3 = dm.enc_all + dm.skip_all

    def block_of(size):
        return (size, lambda j: pl.multiple_of(j * size, size))

    dm.convs = convs = (
        Conv(dm, dm.ce, dm.skip_all, (block_of(dm.cs),)),
        Conv(dm, dm.ce, dm.enc_all, (block_of(dm.ce),)),
        Conv(dm, dm.cd, cin3, (block_of(dm.ce), (dm.skip_all, lambda j: dm.enc_all))),
        Conv(dm, dm.cd, dm.dec_all, (block_of(dm.cd),)),
    )
    params = (enc_conv1, enc_conv2, gate_proj, gate_vector, dec_conv1, dec_conv2, enc_norms, dec_norms)
    inputs = (
        skip, cotangent, enc_conv1, enc_conv2, dec_conv1, dec_conv2, gate_proj, gate_vector, enc_norms, dec_norms
    )
    shape = jax.ShapeDtypeStruct
    outs = (
        shape((S, R, dm.cd, LANES), BF16),
        shape((S, R, dm.cs, LANES), F32),
        *(shape(a.shape, F32) for a in (enc_conv1, enc_conv2, dec_conv1, dec_conv2)),
        *(shape(a.shape, F32) for a in (gate_proj, gate_vector, enc_norms, dec_norms)),
    )

    def ext(slices, rows, block):
        return pltpu.VMEM((slices, rows, nc, block, LANES), storage(block))

    def exchange(cv):
        return [pltpu.VMEM((nc, 3, size, cv.wide), cv.kind) for size, _ in cv.blocks]

    def backward(cv):
        return [pltpu.VMEM((9 * size, 3 * nc * cv.o), BF16) for size, _ in cv.blocks]

    gq = dm.g // nc
    scratch = [
        ext(3, H + 2, dm.cs),
        ext(S + 2, R, dm.cs),
        ext(3, H + 2, dm.ce),
        ext(3, H, dm.ce),
        pltpu.VMEM((S + 2, R + 2, cin3, LANES), BF16),
        ext(S + 2, R + 2, dm.cd),
        ext(S + 2, R + 2, dm.cd),
        ext(S + 2, R + 2, dm.cd),
        ext(3, H + 2, dm.ce),
        ext(3, H + 2, dm.ce),
        pltpu.VMEM((H, dm.ce, LANES), F32),
        pltpu.VMEM((H, dm.ce, LANES), F32),
        pltpu.VMEM((S * R, dm.cd, LANES), F32),
        pltpu.VMEM((S * R, dm.cd, LANES), F32),
        pltpu.VMEM((H, dm.ce, LANES), F32),
        pltpu.VMEM((S * R, dm.cd, LANES), F32),
        pltpu.VMEM((S + 2, R, dm.g, LANES), F32),
        pltpu.VMEM((S + 2, R, 1, LANES), F32),
        pltpu.VMEM((S * R, dm.g, LANES), BF16),
        pltpu.VMEM((S * R, dm.ce, LANES), F32),
        pltpu.VMEM((S + 2, H, dm.enc_all, LANES), F32),
        pltpu.VMEM((S * R, dm.cd, LANES), F32),
        pltpu.VMEM((H, dm.ce, LANES), F32),
        pltpu.VMEM((3, S, R + 2, dm.cd, LANES), storage(dm.cd)),
        pltpu.VMEM((3, 1, H + 2, dm.ce, LANES), storage(dm.ce)),
        pltpu.VMEM((2, H, dm.ce, LANES), F32),
        pltpu.VMEM((2, H, dm.ce, LANES), F32),
        pltpu.VMEM((4, nd, dm.ce, LANES), F32),
        pltpu.VMEM((4, nd, dm.cd, LANES), F32),
        pltpu.VMEM((1, nd, gq, 3 * LANES), F32),
        pltpu.VMEM((dm.cs * S * R, LANES), F32),
        pltpu.VMEM((max(cv.chunks for cv in convs) * LANES, LANES), F32),
        pltpu.VMEM((max(-(-3 * cv.c // LANES) for cv in convs) * LANES, max(cv.wide for cv in convs)), F32),
        pltpu.VMEM((max(3 * cv.c for cv in convs), max(cv.wide for cv in convs)), F32),
        pltpu.VMEM((nc, gq, 3 * LANES), F32),
        pltpu.VMEM((2 * LANES, dm.g), F32),
        pltpu.VMEM((dm.ce + dm.cs, dm.g), F32),
        pltpu.VMEM((nc, gq, 3 * LANES), F32),
        *(pltpu.VMEM((3, cv.c, cv.wide), cv.kind) for cv in convs),
        *(pltpu.VMEM((9 * cv.o, 3 * cv.c), BF16) for cv in convs),
        *(ref for cv in convs for ref in exchange(cv)),
        *(ref for cv in convs for ref in backward(cv)),
        *(pltpu.VMEM((cv.share * nd, 16, LANES), BF16) for cv in convs),
        *(pltpu.VMEM((nd, cv.share, 16, LANES), BF16) for cv in convs),
        *(pltpu.VMEM((cv.share * nd, 16, LANES), BF16) for cv in convs),
        *[pltpu.SemaphoreType.DMA((len(GATHERS), 3 * nc))] * 2,
        *[pltpu.SemaphoreType.DMA((9, nd))] * 2,
        *[pltpu.SemaphoreType.DMA((2,))] * 2,
        *[pltpu.SemaphoreType.DMA((4, 2, nc))] * 2,
        *[pltpu.SemaphoreType.DMA((nc,))] * 2,
        *[pltpu.SemaphoreType.DMA((4, nd))] * 4,
    ]
    vmem = pl.BlockSpec(memory_space=pltpu.VMEM)
    out, sg, grad1, grad2, grad3, grad4, ggate, gvector, gen, gdn = pl.pallas_call(
        functools.partial(kernel, dm),
        out_shape=outs,
        in_specs=[vmem] * len(inputs),
        out_specs=[vmem] * len(outs),
        scratch_shapes=scratch,
        compiler_params=pltpu.CompilerParams(has_side_effects=True, vmem_limit_bytes=60 * 1024 * 1024),
        name="step",
    )(*inputs)
    grads = (grad1, grad2, ggate, gvector, grad3, grad4, gen, gdn)
    updated = pl.pallas_call(
        update_kernel,
        out_shape=tuple(shape(p.shape, F32) for p in params for _ in range(3)),
        in_specs=[vmem] * 32,
        out_specs=[vmem] * 24,
        compiler_params=pltpu.CompilerParams(vmem_limit_bytes=60 * 1024 * 1024),
        name="update",
    )(*params, *grads, *states)
    return (jnp.transpose(out, (2, 0, 1, 3)), jnp.transpose(sg, (2, 0, 1, 3)), *updated)


def solution(mesh):
    volume = P("chan", "depth", None, None)
    row, column, norms = P("chan", None), P(None, "chan"), P(None, None, "chan")
    params = (row, row, row, column, row, row, norms, norms)
    return jax.shard_map(
        per_device,
        mesh=mesh,
        in_specs=(volume, volume) + params * 3,
        out_specs=(volume, volume) + tuple(spec for spec in params for _ in range(3)),
        check_vma=False,
    )
```

```python
import functools

import jax
import jax.numpy as jnp
from jax import lax
from jax.experimental import pallas as pl
from jax.experimental.pallas import tpu as pltpu
from jax.sharding import PartitionSpec as P

STEP = 5
EPS = 1e-05
CONV_RATE = 0.03
GATE_RATE = 0.1
VECTOR_RATE = 0.5
LANES = 128
MESH = pl.DeviceIdType.MESH
F32 = jnp.float32
BF16 = jnp.bfloat16


def iota(shape, dim):
    return lax.broadcasted_iota(jnp.int32, shape, dim)


def dot(a, b):
    return jnp.dot(a, b, preferred_element_type=F32)


def dot_nt(a, b):
    return lax.dot_general(a, b, (((1,), (1,)), ((), ())), preferred_element_type=F32)


def from_left(v, width):
    return jnp.where(iota(v.shape, 1) % width == 0, 0.0, pltpu.roll(v, 1, 1))


def from_right(v, width):
    return jnp.where(iota(v.shape, 1) % width == width - 1, 0.0, pltpu.roll(v, LANES - 1, 1))


def halves(low, high):
    return pltpu.roll(jnp.where(iota(low.shape, 1) < LANES // 2, low, high), LANES // 2, 1)


def split(v):
    high = v.astype(BF16)
    return jnp.concatenate([high, (v - high.astype(F32)).astype(BF16)], 1)


def storage(block):
    return BF16 if block % 16 == 0 else F32


def flat(ref, s, r):
    v = ref[s, r]
    if v.ndim == 3:
        v = v.reshape(v.shape[0] * v.shape[1], LANES)
    return v.astype(BF16)


class Dims:
    def __init__(self, nd, nc, skip, enc, dec, gate):
        self.nd, self.nc = nd, nc
        self.s, self.rows, self.cols = skip[1:]
        self.cs, self.ce, self.cd, self.g = skip[0], enc, dec, gate
        self.half, self.hcols = self.rows // 2, self.cols // 2
        self.fine_total = nd * self.s * self.rows * self.cols
        self.coarse_total = self.fine_total // 8
        self.enc_all = nc * enc
        self.skip_all = nc * skip[0]
        self.dec_all = nc * dec


GATHERS = ("pooled", "skip", "hidden", "coarse", "dhidden", "dz4", "dz3", "dz2", "dz1")
CONVS = ("enc1", "enc2", "dec1", "dec2")


class Conv:
    def __init__(self, dm, o, c, blocks):
        self.o, self.c, self.blocks = o, c, blocks
        self.length = 27 * c
        self.chunks = -(-self.length // LANES)
        self.per = LANES // o
        self.tiles = -(-9 // self.per)
        self.wide = self.tiles * LANES
        self.kind = storage(min(size for size, _ in blocks))
        self.count = 3 * c // 16 * self.tiles
        self.share = -(-self.count // dm.nd)


def kernel(
    dm,
    skip_ref, cot_ref, w1, w2, w3, w4, gate_ref, vector_ref, en_ref, dn_ref,
    out_ref, sg_ref, g1, g2, g3, g4, ggate, gvector, gen, gdn,
    xp, xs, xh, xc, d1, xd, xz4, xz3, xz2, xz1,
    z1, z2, z3, z4, du_c, du_f, pre_ref, al_ref, pg_ref, ug_ref, dt, gg, cg,
    dzf, dzc, fs, fr, st, st_g, rows_ref, turned, wide_ref, acc, gate_all, gate_t, gate_own, gate_block,
    wt1, wt2, wt3, wt4, wf1, wf2, wf3, wf4, wx1, wx2, wx3u, wx3g, wx4, wb1, wb2, wb3u, wb3g, wb4,
    gt1, gt2, gt3, gt4, gr1, gr2, gr3, gr4, ga1, ga2, ga3, ga4,
    g_send, g_recv, t_send, t_recv, f_send, f_recv, w_send, w_recv, v_send, v_recv, r_send, r_recv, a_send, a_recv,
):
    nd, nc, S, R, H = dm.nd, dm.nc, dm.s, dm.rows, dm.half
    W, V = dm.cols, dm.hcols
    Q = H // 2
    place = lax.axis_index("depth")
    me = lax.axis_index("chan")
    first, last = place == 0, place == nd - 1
    convs = dm.convs
    pending = []

    def peer_copy(src, dst, send, recv, depth, chan):
        return pltpu.make_async_remote_copy(
            src_ref=src, dst_ref=dst, send_sem=send, recv_sem=recv,
            device_id={"depth": depth, "chan": chan}, device_id_type=MESH,
        )

    def gather_parts(ref, which, pad):
        n = ref.shape[0] - 2
        span = pl.ds(pad, ref.shape[1] - 2 * pad)
        k = GATHERS.index(which)
        other = me + 1 - 2 * lax.rem(me, 2)
        parts = []
        for side, own, theirs, size in ((0, n, 0, 1), (2, 1, n + 1, 1), (1, 1, 1, n)):
            step = 1 - side
            can_send = (jnp.logical_not(last), None, jnp.logical_not(first))[side]
            can_recv = (jnp.logical_not(first), None, jnp.logical_not(last))[side]
            for t in range(nc // 2):
                to, source = lax.rem(me + 2 * t, nc), lax.rem(me + nc - 2 * t, nc)
                mate = lax.rem(other + nc - 2 * t, nc)
                i = side * (nc // 2) + t

                def copy(own, block, at, hop, depth, chan, size=size, i=i):
                    return peer_copy(
                        ref.at[pl.ds(own, size), span, block],
                        ref.at[pl.ds(at, size), span, block],
                        g_send.at[k, hop, i], g_recv.at[k, hop, i], depth, chan,
                    )

                mine = side == 1 and t == 0
                out = None if mine else functools.partial(copy, own, me, theirs, 0, place + step, to)
                back = None if mine else functools.partial(copy, theirs, source, theirs, 0, place, source)
                on = functools.partial(copy, theirs, source, theirs, 1, place, other)
                mates = functools.partial(copy, theirs, mate, theirs, 1, place, other)
                parts.append((can_send, can_recv, out, back, on, mates))
        return parts

    def guarded(cond, fn):
        if cond is None:
            fn()
        else:
            pl.when(cond)(fn)

    def gather_start(ref, which, pad):
        for can_send, can_recv, out, _, on, _ in gather_parts(ref, which, pad):
            if out is None:
                on().start()
            else:
                guarded(can_send, lambda out=out: out().start())
                pending.append((can_send, lambda out=out: out().wait_send()))
            pending.append((can_recv, lambda on=on: on().wait_send()))

    def gather_pass(ref, which, pad):
        for _, can_recv, out, back, on, _ in gather_parts(ref, which, pad):
            if out is not None:

                def relay(back=back, on=on):
                    back().wait_recv()
                    on().start()

                guarded(can_recv, relay)

    def gather_wait(ref, which, pad):
        for _, can_recv, _, _, _, mates in gather_parts(ref, which, pad):
            guarded(can_recv, lambda mates=mates: mates().wait_recv())

    def sum_copy(ref, k, slot, t):
        return peer_copy(
            ref.at[slot, place], ref.at[slot, place], t_send.at[k, t], t_recv.at[k, t], lax.rem(place + t, nd), me
        )

    def sum_start(ref, k, slot, tile):
        ref[slot, place] = tile

        def send(t, _):
            sum_copy(ref, k, slot, t).start()
            return _

        def sent(t, _):
            sum_copy(ref, k, slot, t).wait_send()
            return _

        lax.fori_loop(1, nd, send, 0)
        pending.append((None, lambda: lax.fori_loop(1, nd, sent, 0)))

    def sum_finish(ref, k, slot):
        def receive(t, _):
            source = lax.rem(place + nd - t, nd)
            peer_copy(
                ref.at[slot, source], ref.at[slot, source], t_send.at[k, t], t_recv.at[k, t], source, me
            ).wait_recv()
            return _

        lax.fori_loop(1, nd, receive, 0)
        return jnp.sum(ref[slot], axis=0)

    def totals(k, slot, m):
        row = sum_finish(st, k, slot)
        lane, channel = iota((m, LANES), 1), iota((m, LANES), 0)
        return tuple(
            jnp.sum(jnp.where(lane == channel + i * m, row, 0.0), axis=1, keepdims=True) for i in range(2)
        )

    def turn_in(w, cv):
        def chunk(a):
            return jnp.transpose(jnp.concatenate([a] * cv.per, 0))

        full = cv.length // LANES

        def body(i, carry):
            at = pl.multiple_of(i * LANES, LANES)
            turned[pl.ds(at, LANES)] = chunk(w[:, pl.ds(at, LANES)])
            return carry

        lax.fori_loop(0, full, body, 0)
        if full < cv.chunks:
            a = w[:, full * LANES :]
            a = jnp.concatenate([a, jnp.zeros((cv.o, LANES - a.shape[1]), F32)], 1)
            turned[full * LANES : (full + 1) * LANES] = chunk(a)

    def prepare(k):
        cv, w, wt, wf = convs[k], (w1, w2, w3, w4)[k], (wt1, wt2, wt3, wt4)[k], (wf1, wf2, wf3, wf4)[k]
        turn_in(w, cv)
        group = iota((cv.c, LANES), 1) // cv.o
        for kz in range(3):
            for j in range(cv.tiles):
                tile = None
                for g in range(cv.per):
                    t = j * cv.per + g
                    if t < 9:
                        v = turned[pl.ds(9 * kz + t, cv.c, stride=27)]
                        tile = v if tile is None else jnp.where(group == g, v, tile)
                tile = tile.astype(BF16)
                wt[kz, :, j * LANES : (j + 1) * LANES] = tile.astype(wt.dtype)
                wide_ref[kz * cv.c : (kz + 1) * cv.c, j * LANES : (j + 1) * LANES] = tile.astype(F32)
        rows = -(-3 * cv.c // LANES) * LANES
        for i in range(rows // LANES):
            v = jnp.transpose(wide_ref[i * LANES : (i + 1) * LANES, 0 : cv.wide])
            size = min(LANES, 3 * cv.c - i * LANES)
            wf[:, i * LANES : i * LANES + size] = v[0 : 9 * cv.o, 0:size].astype(BF16)

    def weight_parts(k):
        cv, wt = convs[k], (wt1, wt2, wt3, wt4)[k]
        into = ((wx1,), (wx2,), (wx3u, wx3g), (wx4,))[k]
        parts = []
        for b, (size, start) in enumerate(cv.blocks):
            for t in range(1, nc):
                to, source = lax.rem(me + t, nc), lax.rem(me + nc - t, nc)
                at = start(to)
                sems = (w_send.at[k, b, t], w_recv.at[k, b, t])
                out = lambda b=b, at=at, size=size, to=to, sems=sems: peer_copy(
                    wt.at[:, pl.ds(at, size)], into[b].at[me], *sems, place, to
                )
                back = lambda b=b, source=source, sems=sems: peer_copy(
                    into[b].at[source], into[b].at[source], *sems, place, source
                )
                parts.append((out, back))
        return parts

    def weights_start(k):
        cv, wt = convs[k], (wt1, wt2, wt3, wt4)[k]
        into = ((wx1,), (wx2,), (wx3u, wx3g), (wx4,))[k]
        for b, (size, start) in enumerate(cv.blocks):
            into[b][me] = wt[:, pl.ds(start(me), size)]
        for out, _ in weight_parts(k):
            out().start()
            pending.append((None, lambda out=out: out().wait_send()))

    def weights_finish(k):
        cv = convs[k]
        into = ((wx1,), (wx2,), (wx3u, wx3g), (wx4,))[k]
        outs = ((wb1,), (wb2,), (wb3u, wb3g), (wb4,))[k]
        for _, back in weight_parts(k):
            back().wait_recv()
        for b, (size, _) in enumerate(cv.blocks):
            for t in range(9):
                pieces = [
                    into[b][j, 2 - kz, :, t * cv.o : (t + 1) * cv.o].astype(F32)
                    for kz in range(3)
                    for j in range(nc)
                ]
                outs[b][(8 - t) * size : (9 - t) * size] = jnp.concatenate(pieces, 1).astype(BF16)

    def reduce_copy(k, t):
        cv, gt, gr = convs[k], (gt1, gt2, gt3, gt4)[k], (gr1, gr2, gr3, gr4)[k]
        to = lax.rem(place + t, nd)
        return peer_copy(
            gt.at[pl.ds(to * cv.share, cv.share)], gr.at[place], r_send.at[k, t], r_recv.at[k, t], to, me
        )

    def reduce_start(k):
        cv, gt, gr = convs[k], (gt1, gt2, gt3, gt4)[k], (gr1, gr2, gr3, gr4)[k]

        def tile(i, carry):
            for j in range(cv.tiles):
                at = pl.multiple_of(i * 16, 16)
                gt[i * cv.tiles + j] = acc[pl.ds(at, 16), j * LANES : (j + 1) * LANES].astype(BF16)
            return carry

        lax.fori_loop(0, 3 * cv.c // 16, tile, 0)
        for i in range(cv.count, cv.share * nd):
            gt[i] = jnp.zeros((16, LANES), BF16)
        gr[place] = gt[pl.ds(place * cv.share, cv.share)]

        def send(t, _):
            reduce_copy(k, t).start()
            return _

        def sent(t, _):
            reduce_copy(k, t).wait_send()
            return _

        lax.fori_loop(1, nd, send, 0)
        pending.append((None, lambda: lax.fori_loop(1, nd, sent, 0)))

    def share_copy(k, t):
        cv, ga = convs[k], (ga1, ga2, ga3, ga4)[k]
        own = ga.at[pl.ds(place * cv.share, cv.share)]
        return peer_copy(own, own, a_send.at[k, t], a_recv.at[k, t], lax.rem(place + t, nd), me)

    def reduce_finish(k):
        cv, gr, ga = convs[k], (gr1, gr2, gr3, gr4)[k], (ga1, ga2, ga3, ga4)[k]

        def receive(t, _):
            source = lax.rem(place + nd - t, nd)
            peer_copy(gr.at[source], gr.at[source], r_send.at[k, t], r_recv.at[k, t], source, me).wait_recv()
            return _

        lax.fori_loop(1, nd, receive, 0)
        ga[pl.ds(place * cv.share, cv.share)] = jnp.sum(gr[...].astype(F32), axis=0).astype(BF16)

        def send(t, _):
            share_copy(k, t).start()
            return _

        def sent(t, _):
            share_copy(k, t).wait_send()
            return _

        lax.fori_loop(1, nd, send, 0)
        pending.append((None, lambda: lax.fori_loop(1, nd, sent, 0)))

    def gradient_out(k):
        cv, ga, out = convs[k], (ga1, ga2, ga3, ga4)[k], (g1, g2, g3, g4)[k]

        def receive(t, _):
            source = lax.rem(place + nd - t, nd)
            theirs = ga.at[pl.ds(source * cv.share, cv.share)]
            peer_copy(theirs, theirs, a_send.at[k, t], a_recv.at[k, t], source, me).wait_recv()
            return _

        lax.fori_loop(1, nd, receive, 0)
        group = iota((16, LANES), 1) // cv.o

        def scatter(i, carry):
            for kz in range(3):
                for j in range(cv.tiles):
                    v = ga[(kz * (cv.c // 16) + i) * cv.tiles + j].astype(F32)
                    for g in range(cv.per):
                        t = j * cv.per + g
                        if t < 9:
                            turned[pl.ds(9 * kz + t + i * (16 * 27), 16, stride=27)] = jnp.where(group == g, v, 0.0)
            return carry

        lax.fori_loop(0, cv.c // 16, scatter, 0)

        def chunk(at):
            v = jnp.transpose(turned[pl.ds(at, LANES)])
            return jnp.sum(v.reshape(cv.per, cv.o, LANES), axis=0)

        full = cv.length // LANES

        def body(i, carry):
            at = pl.multiple_of(i * LANES, LANES)
            out[:, pl.ds(at, LANES)] = chunk(at)
            return carry

        lax.fori_loop(0, full, body, 0)
        if full < cv.chunks:
            out[:, full * LANES :] = chunk(full * LANES)[:, 0 : cv.length - full * LANES]

    def column(row):
        n = row.shape[1]
        eye = iota((n, n), 0) == iota((n, n), 1)
        return jnp.sum(jnp.where(eye, row, 0.0), axis=1, keepdims=True)

    def row_of(col):
        n = col.shape[0]
        eye = iota((n, n), 0) == iota((n, n), 1)
        return jnp.sum(jnp.where(eye, col, 0.0), axis=0, keepdims=True)

    def clear_edges(ref):
        n = ref.shape[0]
        blank = jnp.zeros(ref.shape[2:], ref.dtype)

        for s in range(n):
            ref[s, 0] = blank
            ref[s, ref.shape[1] - 1] = blank

    def clear_halos(ref):
        def clear(s):
            ref[s] = jnp.zeros(ref.shape[1:], ref.dtype)

        pl.when(first)(lambda: clear(0))
        pl.when(last)(lambda: clear(ref.shape[0] - 1))

    def conv(ref, weight, slices, rows, m, n, width, emit, init):
        per = rows // n

        def body(i, carry):
            d = i // per
            r0 = (i - d * per) * n
            x = jnp.concatenate(
                [
                    jnp.concatenate([flat(ref, d + kz, r0 + j) for j in range(n + 2)], 1)
                    for kz in range(3)
                ],
                0,
            )
            y = dot(weight[...], x)
            results = []
            for j in range(n):
                acc = []
                for kx in range(3):
                    terms = [
                        y[(3 * ky + kx) * m : (3 * ky + kx + 1) * m, (j + ky) * LANES : (j + ky + 1) * LANES]
                        for ky in range(3)
                    ]
                    acc.append(terms[0] + terms[1] + terms[2])
                results.append(from_left(acc[0], width) + acc[1] + from_right(acc[2], width))
            return emit(d, r0, results, carry)

        return lax.fori_loop(0, slices * per, body, init)

    def weight_grad(ref, dz, k, slices, rows, n):
        per = rows // n
        cv = convs[k]
        acc[0 : 3 * cv.c, 0 : cv.wide] = jnp.zeros((3 * cv.c, cv.wide), F32)

        def body(i, carry):
            d = i // per
            r0 = (i - d * per) * n
            x = jnp.concatenate(
                [
                    jnp.concatenate([flat(ref, d + kz, r0 + 1 + j) for j in range(n)], 1)
                    for kz in range(3)
                ],
                0,
            )
            y = jnp.concatenate(
                [
                    jnp.concatenate([dz[kx, d, r0 + j + 2 - ky] for j in range(n)], 1)
                    for ky in range(3)
                    for kx in range(3)
                ],
                0,
            ).astype(BF16)
            acc[0 : 3 * cv.c, 0 : 9 * cv.o] += dot_nt(x, y)
            return carry

        lax.fori_loop(0, slices * per, body, 0)

    def conv_coarse(ref, weight, m):
        x = jnp.concatenate(
            [jnp.concatenate([flat(ref, kz, i) for i in range(Q)], 1) for kz in range(3)], 0
        )
        y = dot(weight[...], x)
        blank = jnp.zeros((m, LANES), F32)

        def shifted(ky, i):
            if not 0 <= i < Q:
                return blank
            a, b, c = (
                y[(3 * ky + kx) * m : (3 * ky + kx + 1) * m, i * LANES : (i + 1) * LANES] for kx in range(3)
            )
            return from_left(a, V) + b + from_right(c, V)

        before = [shifted(0, i) for i in range(-1, Q)]
        after = [shifted(2, i) for i in range(Q + 1)]
        return [
            shifted(1, i) + halves(before[i + 1] + after[i + 1], before[i] + after[i]) for i in range(Q)
        ]

    def conv_stats_coarse(ref, weight, z, m):
        total = square = jnp.zeros((m, LANES), F32)
        for i, v in enumerate(conv_coarse(ref, weight, m)):
            z[i] = v
            total, square = total + v, square + v * v
        return pack(total, square)

    def weight_grad_coarse(ref, k):
        cv = convs[k]
        x = jnp.concatenate(
            [jnp.concatenate([flat(ref, kz, i) for i in range(Q)], 1) for kz in range(3)], 0
        )
        y = jnp.concatenate([jnp.concatenate([dzc[t, i] for i in range(Q)], 1) for t in range(9)], 0)
        acc[0 : 3 * cv.c, 0 : 9 * cv.o] = dot_nt(x, y.astype(BF16))

    def norm_back_coarse(z, du, stats, norm, total, x):
        mean, inv = stats
        scale = norm[0] * inv
        a = total[0] / dm.coarse_total
        b = total[1] / dm.coarse_total
        rows = []
        for i in range(Q):
            v = scale * (du[i] - a - (z[i] - mean) * inv * b)
            low = v.astype(BF16)
            x[1, i, me] = low.astype(x.dtype)
            rows.append(low.astype(F32))
        blank = jnp.zeros_like(rows[0])
        rows = [blank] + rows + [blank]
        for i in range(Q):
            before, here, after = rows[i : i + 3]
            for ky, v in enumerate((halves(after, here), here, halves(here, before))):
                for kx, u in enumerate((from_right(v, V), v, from_left(v, V))):
                    dzc[3 * ky + kx, i] = u.astype(dzc.dtype)

    def conv_stats(ref, weight, z, slices, rows, m, n, width):
        def emit(d, r0, results, carry):
            total, square = carry
            for j, v in enumerate(results):
                z[d * rows + r0 + j] = v
                total, square = total + v, square + v * v
            return total, square

        blank = jnp.zeros((m, LANES), F32)
        total, square = conv(ref, weight, slices, rows, m, n, width, emit, (blank, blank))
        return pack(total, square)

    def pack(a, b):
        m = a.shape[0]
        a = jnp.sum(a, axis=1, keepdims=True)
        b = jnp.sum(b, axis=1, keepdims=True)
        lane, channel = iota((m, LANES), 1), iota((m, LANES), 0)
        both = jnp.where(lane == channel, a, jnp.where(lane == channel + m, b, 0.0))
        return jnp.sum(both, axis=0, keepdims=True)

    def moments(total, count):
        mean = total[0] / count
        var = total[1] / count - mean * mean
        return mean, lax.rsqrt(var + EPS)

    def norm_apply(z, mean, inv, gain, shift):
        xhat = (z - mean) * inv
        u = gain * xhat + shift
        return xhat, u, jax.nn.sigmoid(u)

    def norm_rows(z, stats, norm, emit, n):
        mean, inv = stats
        gain, shift = norm

        def body(i, carry):
            for j in range(n):
                p = i * n + j
                _, u, sigma = norm_apply(z[p], mean, inv, gain, shift)
                emit(p, u * sigma)
            return carry

        lax.fori_loop(0, z.shape[0] // n, body, 0)

    def norm_back_sums(z, du, stats, norm, grad, n):
        mean, inv = stats
        gain, shift = norm
        m = z.shape[1]

        def body(i, carry):
            a, b = carry
            for j in range(n):
                p = i * n + j
                xhat, u, sigma = norm_apply(z[p], mean, inv, gain, shift)
                v = grad(p) * sigma * (1.0 + u * (1.0 - sigma))
                du[p] = v
                a, b = a + v, b + v * xhat
            return a, b

        blank = jnp.zeros((m, LANES), F32)
        return pack(*lax.fori_loop(0, z.shape[0] // n, body, (blank, blank)))

    def norm_back(z, du, stats, norm, total, count, x, dz, rows, width, n):
        mean, inv = stats
        gain, _ = norm
        scale = gain * inv
        a = total[0] / count
        b = total[1] / count
        per = rows // n

        def body(i, carry):
            d = i // per
            r0 = (i - d * per) * n
            for j in range(n):
                p = i * n + j
                xhat = (z[p] - mean) * inv
                v = scale * (du[p] - a - xhat * b)
                low = v.astype(BF16)
                x[1 + d, 1 + r0 + j, me] = low.astype(x.dtype)
                v = low.astype(F32)
                dz[0, d, 1 + r0 + j] = from_right(v, width).astype(dz.dtype)
                dz[1, d, 1 + r0 + j] = low.astype(dz.dtype)
                dz[2, d, 1 + r0 + j] = from_left(v, width).astype(dz.dtype)
            return carry

        lax.fori_loop(0, z.shape[0] // n, body, 0)

    hc = iota((LANES, LANES), 0)
    fc = iota((LANES, LANES), 1)
    half = LANES // 2

    def up_table(coarse, fine):
        base = fine // 2
        other = jnp.clip(base + jnp.where(fine % 2 == 0, -1, 1), 0, V - 1)
        near = (coarse == base).astype(F32)
        far = (coarse == other).astype(F32)
        return (0.75 * near + 0.25 * far).astype(BF16)

    pool = jnp.concatenate([(hc // 2 == fc - at).astype(BF16) for at in (0, half)], 0)
    spread = jnp.concatenate([(hc - at == fc // 2).astype(BF16) for at in (0, half)], 1)
    up = jnp.concatenate([up_table(hc - at, fc) for at in (0, half)], 1)
    down = jnp.concatenate([up_table(fc - at, hc) for at in (0, 0, half, half)], 0)
    spread2 = jnp.concatenate([spread, spread], 0)

    def take_rows(ref):
        for c in range(dm.cs):
            rows_ref[c * S * R : (c + 1) * S * R] = ref[c].astype(F32).reshape(S * R, LANES)

    def row(p):
        return rows_ref[pl.ds(p, dm.cs, stride=S * R)]

    clear_halos(xp)
    take_rows(skip_ref)

    def take_skip(i, carry):
        parts = []
        for s in range(S):
            v = [row(s * R + 4 * i + j).astype(BF16) for j in range(4)]
            for j in range(4):
                xs[1 + s, 4 * i + j, me] = v[j].astype(xs.dtype)
            parts += [jnp.concatenate([v[j], v[2 + j]], 1) for j in range(2)]
        v = dot(jnp.concatenate(parts, 0), pool).reshape(2 * S, dm.cs, LANES)
        xp[1, i, me] = (jnp.sum(v, axis=0) * 0.125).astype(BF16).astype(xp.dtype)
        return carry

    lax.fori_loop(0, Q, take_skip, 0)
    gather_start(xp, "pooled", 0)
    clear_halos(xs)
    gather_start(xs, "skip", 0)

    gq = dm.g // nc
    gate_all[me, :, 0 : gate_ref.shape[1]] = gate_ref[...]
    lane = iota((gq, LANES), 1)
    gate_all[me, :, 2 * LANES :] = jnp.where(
        lane == 0, column(vector_ref[0:1]), jnp.where(lane == 1, column(vector_ref[1:2]), 0.0)
    )
    for t in range(1, nc):
        to, source = lax.rem(me + t, nc), lax.rem(me + nc - t, nc)
        out = peer_copy(gate_all.at[me], gate_all.at[me], v_send.at[t], v_recv.at[t], place, to)
        out.start()
        pending.append((None, out.wait_send))

    prepare(0)
    for ref in (xd, d1, xz4, xz3):
        clear_edges(ref)
    for ref in (xh, xd, xz4, xz3, xz2, xz1):
        clear_halos(ref)
    for kx in range(3):
        for s in range(S):
            dzf[kx, s, 0] = jnp.zeros(dzf.shape[3:], dzf.dtype)
            dzf[kx, s, R + 1] = jnp.zeros(dzf.shape[3:], dzf.dtype)

    def norm_of(ref, layer):
        return column(ref[0, layer : layer + 1]), column(ref[1, layer : layer + 1])

    norm_e1, norm_e2 = norm_of(en_ref, 0), norm_of(en_ref, 1)
    norm_d1, norm_d2 = norm_of(dn_ref, 0), norm_of(dn_ref, 1)

    gather_pass(xp, "pooled", 0)
    gather_wait(xp, "pooled", 0)
    sum_start(st, 0, 0, conv_stats_coarse(xp, wf1, z1, dm.ce))
    prepare(1)
    stats_e1 = moments(totals(0, 0, dm.ce), dm.coarse_total)

    def keep_hidden(p, v):
        xh[1, p, me] = v.astype(BF16).astype(xh.dtype)

    norm_rows(z1, stats_e1, norm_e1, keep_hidden, 3)
    gather_start(xh, "hidden", 0)
    prepare(2)
    gather_pass(xh, "hidden", 0)
    gather_pass(xs, "skip", 0)
    gather_wait(xh, "hidden", 0)
    sum_start(st, 1, 1, conv_stats_coarse(xh, wf2, z2, dm.ce))
    prepare(3)
    stats_e2 = moments(totals(1, 1, dm.ce), dm.coarse_total)

    def keep_coarse(p, v):
        xc[1, p, me] = v.astype(BF16).astype(xc.dtype)

    norm_rows(z2, stats_e2, norm_e2, keep_coarse, 3)
    gather_start(xc, "coarse", 0)
    for k in (3, 2, 1, 0):
        weights_start(k)
    for t in range(1, nc):
        source = lax.rem(me + nc - t, nc)
        peer_copy(
            gate_all.at[source], gate_all.at[source], v_send.at[t], v_recv.at[t], place, source
        ).wait_recv()
    gate_full = gate_all[...].reshape(dm.g, 3 * LANES)
    wg = gate_full[:, 0 : dm.enc_all + dm.skip_all].astype(BF16)
    gbias = gate_full[:, 2 * LANES : 2 * LANES + 1]
    gout = gate_full[:, 2 * LANES + 1 : 2 * LANES + 2]
    gate_t[...] = jnp.transpose(gate_full[:, 0 : 2 * LANES])
    gate_own[...] = jnp.concatenate(
        [
            gate_t[pl.ds(pl.multiple_of(me * dm.ce, dm.ce), dm.ce)],
            gate_t[pl.ds(pl.multiple_of(dm.enc_all + me * dm.cs, dm.cs), dm.cs)],
        ],
        0,
    )
    gather_pass(xc, "coarse", 0)
    gather_wait(xc, "coarse", 0)

    def up_depth(i, carry):
        t = []
        for s in range(3):
            v = dot(flat(xc, s, i), up)
            t.append(jnp.stack([v[:, 0:LANES], v[:, LANES:]], 0))
        below = jnp.where(first, t[1], t[0])
        above = jnp.where(last, t[1], t[2])
        near = 0.75 * t[1]
        here = 0.25 * t[1]
        rows = pl.ds(i * 2, 2)
        dt[0, rows] = jnp.where(first, 0.0, 0.75 * below + here)
        dt[1, rows] = near + 0.25 * below
        dt[2, rows] = near + 0.25 * above
        dt[3, rows] = jnp.where(last, 0.0, 0.75 * above + here)
        return carry

    lax.fori_loop(0, Q, up_depth, 0)

    def up_rows(i, carry):
        before, after = jnp.maximum(i - 1, 0), jnp.minimum(i + 1, H - 1)
        for s in range(S + 2):
            v = 0.75 * dt[s, i]
            d1[s, 1 + 2 * i, 0 : dm.enc_all] = (v + 0.25 * dt[s, before]).astype(BF16)
            d1[s, 2 + 2 * i, 0 : dm.enc_all] = (v + 0.25 * dt[s, after]).astype(BF16)
        return carry

    lax.fori_loop(0, H, up_rows, 0)

    gather_wait(xs, "skip", 0)
    gate_n = 4

    def gate(i, carry):
        s = i // (R // gate_n)
        r0 = (i - s * (R // gate_n)) * gate_n
        skips = [flat(xs, s, r0 + j) for j in range(gate_n)]
        x = jnp.concatenate(
            [
                jnp.concatenate([d1[s, 1 + r0 + j, 0 : dm.enc_all] for j in range(gate_n)], 1),
                jnp.concatenate(skips, 1),
            ],
            0,
        )
        pre = dot(wg, x) + gbias
        act = pre * jax.nn.sigmoid(pre)
        alpha = jax.nn.sigmoid(jnp.sum(gout * act, axis=0, keepdims=True))
        for j in range(gate_n):
            lanes = slice(j * LANES, (j + 1) * LANES)
            d1[s, 1 + r0 + j, dm.enc_all :] = (alpha[:, lanes] * skips[j].astype(F32)).astype(BF16)
            pre_ref[s, r0 + j] = pre[:, lanes]
            al_ref[s, r0 + j] = alpha[:, lanes]
        return carry

    lax.fori_loop(0, (S + 2) * R // gate_n, gate, 0)

    sum_start(st, 4, 4, conv_stats(d1, wf3, z3, S, R, dm.cd, 6, W))
    weights_finish(3)
    stats_d1 = moments(totals(4, 4, dm.cd), dm.fine_total)

    def keep_dec(p, v):
        s = p // R
        xd[1 + s, 1 + p - s * R, me] = v.astype(BF16).astype(xd.dtype)

    norm_rows(z3, stats_d1, norm_d1, keep_dec, 8)
    gather_start(xd, "dhidden", 1)
    weights_finish(2)
    take_rows(cot_ref)
    gather_pass(xd, "dhidden", 1)
    gather_wait(xd, "dhidden", 1)
    sum_start(st, 5, 5, conv_stats(xd, wf4, z4, S, R, dm.cd, 6, W))
    weights_finish(1)
    weights_finish(0)
    stats_d2 = moments(totals(5, 5, dm.cd), dm.fine_total)

    sum_start(st, 6, 6, norm_back_sums(z4, du_f, stats_d2, norm_d2, row, 8))

    def keep_result(p, v):
        s = p // R
        out_ref[s, p - s * R] = v.astype(BF16)

    norm_rows(z4, stats_d2, norm_d2, keep_result, 8)
    total_d2 = totals(6, 6, dm.cd)
    norm_back(z4, du_f, stats_d2, norm_d2, total_d2, dm.fine_total, xz4, dzf, R, W, 8)
    gather_start(xz4, "dz4", 1)
    weight_grad(xd, dzf, 3, S, R, 6)
    reduce_start(3)
    gather_pass(xz4, "dz4", 1)
    gather_wait(xz4, "dz4", 1)

    def keep_grad(d, r0, results, carry):
        for j, v in enumerate(results):
            gg[d * R + r0 + j] = v
        return carry

    conv(xz4, wb4, S, R, dm.cd, 6, W, keep_grad, 0)
    sum_start(st, 7, 7, norm_back_sums(z3, du_f, stats_d1, norm_d1, lambda p: gg[p], 8))
    total_d1 = totals(7, 7, dm.cd)
    norm_back(z3, du_f, stats_d1, norm_d1, total_d1, dm.fine_total, xz3, dzf, R, W, 8)
    gather_start(xz3, "dz3", 1)
    reduce_finish(3)
    weight_grad(d1, dzf, 2, S, R, 6)
    reduce_start(2)
    gather_pass(xz3, "dz3", 1)
    gather_wait(xz3, "dz3", 1)

    def keep_up(d, r0, results, carry):
        for j, v in enumerate(results):
            ug_ref[d * R + r0 + j] = v
        return carry

    conv(xz3, wb3u, S, R, dm.ce, 4, W, keep_up, 0)

    def gate_back(d, r0, results, carry):
        bias, psi = carry
        lows = []
        for j, v in enumerate(results):
            s, r = d + 1, r0 + j
            grad = jnp.sum(v * flat(xs, s, r).astype(F32), axis=0, keepdims=True)
            alpha = al_ref[s, r]
            logit = grad * alpha * (1.0 - alpha)
            pre = pre_ref[s, r]
            sigma = jax.nn.sigmoid(pre)
            psi = psi + pre * sigma * logit
            low = (logit * gout * sigma * (1.0 + pre * (1.0 - sigma))).astype(BF16)
            bias = bias + low.astype(F32)
            pg_ref[d * R + r] = low
            lows.append(low)
            for t in range(nc):
                gg[t] = v[t * dm.cs : (t + 1) * dm.cs]
            sg_ref[d, r] = alpha * gg[me]
        back = dot(gate_own[...].astype(BF16), jnp.concatenate(lows, 1))
        for j in range(len(results)):
            lanes = slice(j * LANES, (j + 1) * LANES)
            ug_ref[d * R + r0 + j] += back[0 : dm.ce, lanes]
            sg_ref[d, r0 + j] += back[dm.ce :, lanes]
        return bias, psi

    blank = jnp.zeros((dm.g, LANES), F32)
    bias, psi = conv(xz3, wb3g, S, R, dm.skip_all, 4, W, gate_back, (blank, blank))

    def down_rows(i, carry):
        terms = []
        for s in range(S):
            pair = []
            for j in range(2):
                r = i * 2 + j
                near = ug_ref[s * R + 2 * r] + ug_ref[s * R + 2 * r + 1]
                far = ug_ref[s * R + jnp.minimum(2 * r + 2, R - 1)] + ug_ref[s * R + jnp.maximum(2 * r - 1, 0)]
                pair.append(split(0.75 * near + 0.25 * far))
            terms.append(jnp.concatenate(pair, 1))
        v = dot(jnp.concatenate(terms, 0), down)
        even, odd = v[0 : dm.ce], v[dm.ce :]
        fs[0, i] = 0.25 * even
        fs[1, i] = 0.25 * odd
        cg[i] = 0.75 * (even + odd) + jnp.where(first, 0.25 * even, 0.0) + jnp.where(last, 0.25 * odd, 0.0)
        return carry

    lax.fori_loop(0, Q, down_rows, 0)

    def fold(side, step):
        return peer_copy(fs.at[side], fr.at[1 - side], f_send.at[side], f_recv.at[1 - side], place + step, me)

    pl.when(jnp.logical_not(first))(lambda: fold(0, -1).start())
    pl.when(jnp.logical_not(last))(lambda: fold(1, 1).start())
    pending.append((jnp.logical_not(first), lambda: fold(0, -1).wait_send()))
    pending.append((jnp.logical_not(last), lambda: fold(1, 1).wait_send()))
    reduce_finish(2)

    def fold_in(side):
        peer_copy(fs.at[side], fr.at[side], f_send.at[side], f_recv.at[side], place, me).wait_recv()
        cg[...] += fr[side]

    pl.when(jnp.logical_not(first))(lambda: fold_in(0))
    pl.when(jnp.logical_not(last))(lambda: fold_in(1))

    sum_start(st, 2, 2, norm_back_sums(z2, du_c, stats_e2, norm_e2, lambda p: cg[p], 3))

    columns = gate_ref.shape[1]
    acc[0 : dm.g, 0:columns] = jnp.zeros((dm.g, columns), F32)

    def gate_weight(i, carry):
        d = i // (R // 6)
        r0 = (i - d * (R // 6)) * 6
        x = jnp.concatenate(
            [
                jnp.concatenate([d1[1 + d, 1 + r0 + j, 0 : dm.enc_all] for j in range(6)], 1),
                jnp.concatenate([flat(xs, 1 + d, r0 + j) for j in range(6)], 1),
            ],
            0,
        )
        y = jnp.concatenate([pg_ref[d * R + r0 + j] for j in range(6)], 1)
        acc[0 : dm.g, 0:columns] += dot_nt(y, x)
        return carry

    lax.fori_loop(0, S * R // 6, gate_weight, 0)
    lane = iota((dm.g, LANES), 1)
    vectors = jnp.where(
        lane == 0,
        jnp.sum(bias, axis=1, keepdims=True),
        jnp.where(lane == 1, jnp.sum(psi, axis=1, keepdims=True), 0.0),
    )
    for j in range(nc):
        mine = slice(j * gq, (j + 1) * gq)
        gate_block[j, :, 0:columns] = acc[mine, 0:columns]
        gate_block[j, :, columns : 2 * LANES] = jnp.zeros((gq, 2 * LANES - columns), F32)
        gate_block[j, :, 2 * LANES :] = vectors[mine]
    sum_start(st_g, 8, 0, gate_block[me])
    total_e2 = totals(2, 2, dm.ce)
    norm_back_coarse(z2, du_c, stats_e2, norm_e2, total_e2, xz2)
    gather_start(xz2, "dz2", 0)
    weight_grad_coarse(xh, 1)
    reduce_start(1)
    gather_pass(xz2, "dz2", 0)
    gradient_out(3)
    gather_wait(xz2, "dz2", 0)
    for i, v in enumerate(conv_coarse(xz2, wb2, dm.ce)):
        cg[i] = v
    sum_start(st, 3, 3, norm_back_sums(z1, du_c, stats_e1, norm_e1, lambda p: cg[p], 3))
    reduce_finish(1)
    total_e1 = totals(3, 3, dm.ce)
    norm_back_coarse(z1, du_c, stats_e1, norm_e1, total_e1, xz1)
    gather_start(xz1, "dz1", 0)
    weight_grad_coarse(xp, 0)
    reduce_start(0)
    gather_pass(xz1, "dz1", 0)
    gradient_out(2)
    gather_wait(xz1, "dz1", 0)
    for i, v in enumerate(conv_coarse(xz1, wb1, dm.cs)):
        v = dot(split(v), spread2) * 0.125
        for j in range(4):
            part = v[:, (j // 2) * LANES : (j // 2 + 1) * LANES]
            for s in range(S):
                sg_ref[s, 4 * i + j] += part
    reduce_finish(0)
    gradient_out(1)
    gate_total = sum_finish(st_g, 8, 0)
    ggate[...] = gate_total[:, 0:columns]
    gvector[0:1] = row_of(gate_total[:, 2 * LANES : 2 * LANES + 1])
    gvector[1:2] = row_of(gate_total[:, 2 * LANES + 1 : 2 * LANES + 2])
    for ref, sums in ((gen, (total_e1, total_e2)), (gdn, (total_d1, total_d2))):
        for layer, total in enumerate(sums):
            ref[0, layer : layer + 1] = row_of(total[1])
            ref[1, layer : layer + 1] = row_of(total[0])
    gradient_out(0)
    for cond, fn in pending:
        guarded(cond, fn)


def adamw(weight, grad, moment, square, rate):
    new_moment = 0.9 * moment + 0.1 * grad
    new_square = 0.999 * square + 0.001 * grad * grad
    moment_hat = new_moment / (1.0 - 0.9**STEP)
    square_hat = new_square / (1.0 - 0.999**STEP)
    new_weight = weight - rate * (moment_hat / (jnp.sqrt(square_hat) + 1e-08) + 0.01 * weight)
    return (new_weight, new_moment, new_square)


RATES = (CONV_RATE, CONV_RATE, GATE_RATE, VECTOR_RATE, CONV_RATE, CONV_RATE, VECTOR_RATE, VECTOR_RATE)


def update_kernel(*refs):
    n = len(RATES)
    params, grads, moments, squares = (refs[i * n : (i + 1) * n] for i in range(4))
    outs = refs[4 * n :]
    for k, rate in enumerate(RATES):
        rows = params[k].shape[0]
        step = 8 if rows % 8 == 0 and rows > 8 else rows
        for r in range(0, rows, step):
            at = slice(r, r + step)
            new = adamw(params[k][at], grads[k][at], moments[k][at], squares[k][at], rate)
            for ref, value in zip(outs[3 * k : 3 * k + 3], new):
                ref[at] = value


def per_device(
    skip, cotangent, enc_conv1, enc_conv2, gate_proj, gate_vector, dec_conv1, dec_conv2, enc_norms, dec_norms, *states
):
    nd, nc = lax.axis_size("depth"), lax.axis_size("chan")
    dm = Dims(nd, nc, skip.shape, enc_conv1.shape[0], dec_conv1.shape[0], gate_proj.shape[0] * nc)
    S, R, H = dm.s, dm.rows, dm.half
    cin3 = dm.enc_all + dm.skip_all

    def block_of(size):
        return (size, lambda j: pl.multiple_of(j * size, size))

    dm.convs = convs = (
        Conv(dm, dm.ce, dm.skip_all, (block_of(dm.cs),)),
        Conv(dm, dm.ce, dm.enc_all, (block_of(dm.ce),)),
        Conv(dm, dm.cd, cin3, (block_of(dm.ce), (dm.skip_all, lambda j: dm.enc_all))),
        Conv(dm, dm.cd, dm.dec_all, (block_of(dm.cd),)),
    )
    params = (enc_conv1, enc_conv2, gate_proj, gate_vector, dec_conv1, dec_conv2, enc_norms, dec_norms)
    inputs = (
        skip, cotangent, enc_conv1, enc_conv2, dec_conv1, dec_conv2, gate_proj, gate_vector, enc_norms, dec_norms
    )
    shape = jax.ShapeDtypeStruct
    outs = (
        shape((S, R, dm.cd, LANES), BF16),
        shape((S, R, dm.cs, LANES), F32),
        *(shape(a.shape, F32) for a in (enc_conv1, enc_conv2, dec_conv1, dec_conv2)),
        *(shape(a.shape, F32) for a in (gate_proj, gate_vector, enc_norms, dec_norms)),
    )

    def ext(slices, rows, block):
        return pltpu.VMEM((slices, rows, nc, block, LANES), storage(block))

    def exchange(cv):
        return [pltpu.VMEM((nc, 3, size, cv.wide), cv.kind) for size, _ in cv.blocks]

    def backward(cv):
        return [pltpu.VMEM((9 * size, 3 * nc * cv.o), BF16) for size, _ in cv.blocks]

    gq = dm.g // nc
    Q = H // 2
    scratch = [
        ext(3, Q, dm.cs),
        ext(S + 2, R, dm.cs),
        ext(3, Q, dm.ce),
        ext(3, Q, dm.ce),
        pltpu.VMEM((S + 2, R + 2, cin3, LANES), BF16),
        ext(S + 2, R + 2, dm.cd),
        ext(S + 2, R + 2, dm.cd),
        ext(S + 2, R + 2, dm.cd),
        ext(3, Q, dm.ce),
        ext(3, Q, dm.ce),
        pltpu.VMEM((Q, dm.ce, LANES), F32),
        pltpu.VMEM((Q, dm.ce, LANES), F32),
        pltpu.VMEM((S * R, dm.cd, LANES), F32),
        pltpu.VMEM((S * R, dm.cd, LANES), F32),
        pltpu.VMEM((Q, dm.ce, LANES), F32),
        pltpu.VMEM((S * R, dm.cd, LANES), F32),
        pltpu.VMEM((S + 2, R, dm.g, LANES), F32),
        pltpu.VMEM((S + 2, R, 1, LANES), F32),
        pltpu.VMEM((S * R, dm.g, LANES), BF16),
        pltpu.VMEM((S * R, dm.ce, LANES), F32),
        pltpu.VMEM((S + 2, H, dm.enc_all, LANES), F32),
        pltpu.VMEM((S * R, dm.cd, LANES), F32),
        pltpu.VMEM((Q, dm.ce, LANES), F32),
        pltpu.VMEM((3, S, R + 2, dm.cd, LANES), storage(dm.cd)),
        pltpu.VMEM((9, Q, dm.ce, LANES), BF16),
        pltpu.VMEM((2, Q, dm.ce, LANES), F32),
        pltpu.VMEM((2, Q, dm.ce, LANES), F32),
        pltpu.VMEM((8, nd, 1, LANES), F32),
        pltpu.VMEM((1, nd, gq, 3 * LANES), F32),
        pltpu.VMEM((dm.cs * S * R, LANES), F32),
        pltpu.VMEM((max(cv.chunks for cv in convs) * LANES, LANES), F32),
        pltpu.VMEM((max(-(-3 * cv.c // LANES) for cv in convs) * LANES, max(cv.wide for cv in convs)), F32),
        pltpu.VMEM((max(3 * cv.c for cv in convs), max(cv.wide for cv in convs)), F32),
        pltpu.VMEM((nc, gq, 3 * LANES), F32),
        pltpu.VMEM((2 * LANES, dm.g), F32),
        pltpu.VMEM((dm.ce + dm.cs, dm.g), F32),
        pltpu.VMEM((nc, gq, 3 * LANES), F32),
        *(pltpu.VMEM((3, cv.c, cv.wide), cv.kind) for cv in convs),
        *(pltpu.VMEM((9 * cv.o, 3 * cv.c), BF16) for cv in convs),
        *(ref for cv in convs for ref in exchange(cv)),
        *(ref for cv in convs for ref in backward(cv)),
        *(pltpu.VMEM((cv.share * nd, 16, LANES), BF16) for cv in convs),
        *(pltpu.VMEM((nd, cv.share, 16, LANES), BF16) for cv in convs),
        *(pltpu.VMEM((cv.share * nd, 16, LANES), BF16) for cv in convs),
        *[pltpu.SemaphoreType.DMA((len(GATHERS), 2, 3 * nc // 2))] * 2,
        *[pltpu.SemaphoreType.DMA((9, nd))] * 2,
        *[pltpu.SemaphoreType.DMA((2,))] * 2,
        *[pltpu.SemaphoreType.DMA((4, 2, nc))] * 2,
        *[pltpu.SemaphoreType.DMA((nc,))] * 2,
        *[pltpu.SemaphoreType.DMA((4, nd))] * 4,
    ]
    vmem = pl.BlockSpec(memory_space=pltpu.VMEM)
    out, sg, grad1, grad2, grad3, grad4, ggate, gvector, gen, gdn = pl.pallas_call(
        functools.partial(kernel, dm),
        out_shape=outs,
        in_specs=[vmem] * len(inputs),
        out_specs=[vmem] * len(outs),
        scratch_shapes=scratch,
        compiler_params=pltpu.CompilerParams(has_side_effects=True, vmem_limit_bytes=60 * 1024 * 1024),
        name="step",
    )(*inputs)
    grads = (grad1, grad2, ggate, gvector, grad3, grad4, gen, gdn)
    updated = pl.pallas_call(
        update_kernel,
        out_shape=tuple(shape(p.shape, F32) for p in params for _ in range(3)),
        in_specs=[vmem] * 32,
        out_specs=[vmem] * 24,
        compiler_params=pltpu.CompilerParams(vmem_limit_bytes=60 * 1024 * 1024),
        name="update",
    )(*params, *grads, *states)
    return (jnp.transpose(out, (2, 0, 1, 3)), jnp.transpose(sg, (2, 0, 1, 3)), *updated)


def solution(mesh):
    volume = P("chan", "depth", None, None)
    row, column, norms = P("chan", None), P(None, "chan"), P(None, None, "chan")
    params = (row, row, row, column, row, row, norms, norms)
    return jax.shard_map(
        per_device,
        mesh=mesh,
        in_specs=(volume, volume) + params * 3,
        out_specs=(volume, volume) + tuple(spec for spec in params for _ in range(3)),
        check_vma=False,
    )
```

```python
import functools

import jax
import jax.numpy as jnp
from jax import lax
from jax.experimental import pallas as pl
from jax.experimental.pallas import tpu as pltpu
from jax.sharding import PartitionSpec as P

STEP = 5
EPS = 1e-05
CONV_RATE = 0.03
GATE_RATE = 0.1
VECTOR_RATE = 0.5
LANES = 128
MESH = pl.DeviceIdType.MESH
F32 = jnp.float32
BF16 = jnp.bfloat16


def iota(shape, dim):
    return lax.broadcasted_iota(jnp.int32, shape, dim)


def dot(a, b):
    return jnp.dot(a, b, preferred_element_type=F32)


def dot_nt(a, b):
    return lax.dot_general(a, b, (((1,), (1,)), ((), ())), preferred_element_type=F32)


def from_left(v, width):
    return jnp.where(iota(v.shape, 1) % width == 0, 0.0, pltpu.roll(v, 1, 1))


def from_right(v, width):
    return jnp.where(iota(v.shape, 1) % width == width - 1, 0.0, pltpu.roll(v, LANES - 1, 1))


def halves(low, high):
    return pltpu.roll(jnp.where(iota(low.shape, 1) < LANES // 2, low, high), LANES // 2, 1)


def split(v):
    high = v.astype(BF16)
    return jnp.concatenate([high, (v - high.astype(F32)).astype(BF16)], 1)


def storage(block):
    return BF16 if block % 16 == 0 else F32


def flat(ref, s, r):
    v = ref[s, r]
    if v.ndim == 3:
        v = v.reshape(v.shape[0] * v.shape[1], LANES)
    return v.astype(BF16)


class Dims:
    def __init__(self, nd, nc, skip, enc, dec, gate):
        self.nd, self.nc = nd, nc
        self.s, self.rows, self.cols = skip[1:]
        self.cs, self.ce, self.cd, self.g = skip[0], enc, dec, gate
        self.half, self.hcols = self.rows // 2, self.cols // 2
        self.fine_total = nd * self.s * self.rows * self.cols
        self.coarse_total = self.fine_total // 8
        self.enc_all = nc * enc
        self.skip_all = nc * skip[0]
        self.dec_all = nc * dec


GATHERS = ("pooled", "skip", "hidden", "coarse", "dhidden", "dz4", "dz3", "dz2", "dz1")
CONVS = ("enc1", "enc2", "dec1", "dec2")


class Conv:
    def __init__(self, dm, o, c, blocks):
        self.o, self.c, self.blocks = o, c, blocks
        self.length = 27 * c
        self.chunks = -(-self.length // LANES)
        self.per = LANES // o
        self.tiles = -(-9 // self.per)
        self.wide = self.tiles * LANES
        self.kind = storage(min(size for size, _ in blocks))
        self.count = 3 * c // 16 * self.tiles
        self.share = -(-self.count // dm.nd)


def kernel(
    dm,
    skip_ref, cot_ref, w1, w2, w3, w4, gate_ref, vector_ref, en_ref, dn_ref,
    out_ref, sg_ref, g1, g2, g3, g4, ggate, gvector, gen, gdn,
    xp, xs, xh, xc, d1, xd, xz4, xz3, xz2, xz1,
    z1, z2, z3, z4, du_c, du_f, pre_ref, al_ref, pg_ref, ug_ref, dt, gg, cg,
    dzf, dzc, fs, fr, st, st_g, rows_ref, turned, wide_ref, acc, gate_all, gate_t, gate_own, gate_block,
    wt1, wt2, wt3, wt4, wf1, wf2, wf3, wf4, wx1, wx2, wx3u, wx3g, wx4, wb1, wb2, wb3, wb4,
    gt1, gt2, gt3, gt4, gr1, gr2, gr3, gr4, ga1, ga2, ga3, ga4,
    g_send, g_recv, t_send, t_recv, f_send, f_recv, w_send, w_recv, v_send, v_recv, r_send, r_recv, a_send, a_recv,
):
    nd, nc, S, R, H = dm.nd, dm.nc, dm.s, dm.rows, dm.half
    W, V = dm.cols, dm.hcols
    Q = H // 2
    place = lax.axis_index("depth")
    me = lax.axis_index("chan")
    first, last = place == 0, place == nd - 1
    convs = dm.convs
    pending = []

    def peer_copy(src, dst, send, recv, depth, chan):
        return pltpu.make_async_remote_copy(
            src_ref=src, dst_ref=dst, send_sem=send, recv_sem=recv,
            device_id={"depth": depth, "chan": chan}, device_id_type=MESH,
        )

    def gather_parts(ref, which, pad):
        n = ref.shape[0] - 2
        span = pl.ds(pad, ref.shape[1] - 2 * pad)
        k = GATHERS.index(which)
        other = me + 1 - 2 * lax.rem(me, 2)
        parts = []
        for side, own, theirs, size in ((0, n, 0, 1), (2, 1, n + 1, 1), (1, 1, 1, n)):
            step = 1 - side
            can_send = (jnp.logical_not(last), None, jnp.logical_not(first))[side]
            can_recv = (jnp.logical_not(first), None, jnp.logical_not(last))[side]
            for t in range(nc // 2):
                to, source = lax.rem(me + 2 * t, nc), lax.rem(me + nc - 2 * t, nc)
                mate = lax.rem(other + nc - 2 * t, nc)
                i = side * (nc // 2) + t

                def copy(own, block, at, hop, depth, chan, size=size, i=i):
                    return peer_copy(
                        ref.at[pl.ds(own, size), span, block],
                        ref.at[pl.ds(at, size), span, block],
                        g_send.at[k, hop, i], g_recv.at[k, hop, i], depth, chan,
                    )

                mine = side == 1 and t == 0
                out = None if mine else functools.partial(copy, own, me, theirs, 0, place + step, to)
                back = None if mine else functools.partial(copy, theirs, source, theirs, 0, place, source)
                on = functools.partial(copy, theirs, source, theirs, 1, place, other)
                mates = functools.partial(copy, theirs, mate, theirs, 1, place, other)
                parts.append((can_send, can_recv, out, back, on, mates))
        return parts

    def guarded(cond, fn):
        if cond is None:
            fn()
        else:
            pl.when(cond)(fn)

    def gather_start(ref, which, pad):
        for can_send, can_recv, out, _, on, _ in gather_parts(ref, which, pad):
            if out is None:
                on().start()
            else:
                guarded(can_send, lambda out=out: out().start())
                pending.append((can_send, lambda out=out: out().wait_send()))
            pending.append((can_recv, lambda on=on: on().wait_send()))

    def gather_pass(ref, which, pad):
        for _, can_recv, out, back, on, _ in gather_parts(ref, which, pad):
            if out is not None:

                def relay(back=back, on=on):
                    back().wait_recv()
                    on().start()

                guarded(can_recv, relay)

    def gather_wait(ref, which, pad):
        for _, can_recv, _, _, _, mates in gather_parts(ref, which, pad):
            guarded(can_recv, lambda mates=mates: mates().wait_recv())

    def sum_copy(ref, k, slot, t):
        return peer_copy(
            ref.at[slot, place], ref.at[slot, place], t_send.at[k, t], t_recv.at[k, t], lax.rem(place + t, nd), me
        )

    def sum_start(ref, k, slot, tile):
        ref[slot, place] = tile

        def send(t, _):
            sum_copy(ref, k, slot, t).start()
            return _

        def sent(t, _):
            sum_copy(ref, k, slot, t).wait_send()
            return _

        lax.fori_loop(1, nd, send, 0)
        pending.append((None, lambda: lax.fori_loop(1, nd, sent, 0)))

    def sum_finish(ref, k, slot):
        def receive(t, _):
            source = lax.rem(place + nd - t, nd)
            peer_copy(
                ref.at[slot, source], ref.at[slot, source], t_send.at[k, t], t_recv.at[k, t], source, me
            ).wait_recv()
            return _

        lax.fori_loop(1, nd, receive, 0)
        return jnp.sum(ref[slot], axis=0)

    def totals(k, slot, m):
        row = sum_finish(st, k, slot)
        lane, channel = iota((m, LANES), 1), iota((m, LANES), 0)
        return tuple(
            jnp.sum(jnp.where(lane == channel + i * m, row, 0.0), axis=1, keepdims=True) for i in range(2)
        )

    def turn_in(w, cv):
        def chunk(a):
            return jnp.transpose(jnp.concatenate([a] * cv.per, 0))

        full = cv.length // LANES

        def body(i, carry):
            at = pl.multiple_of(i * LANES, LANES)
            turned[pl.ds(at, LANES)] = chunk(w[:, pl.ds(at, LANES)])
            return carry

        lax.fori_loop(0, full, body, 0, unroll=4)
        if full < cv.chunks:
            a = w[:, full * LANES :]
            a = jnp.concatenate([a, jnp.zeros((cv.o, LANES - a.shape[1]), F32)], 1)
            turned[full * LANES : (full + 1) * LANES] = chunk(a)

    def prepare(k):
        cv, w, wt, wf = convs[k], (w1, w2, w3, w4)[k], (wt1, wt2, wt3, wt4)[k], (wf1, wf2, wf3, wf4)[k]
        turn_in(w, cv)
        group = iota((cv.c, LANES), 1) // cv.o
        for kz in range(3):
            for j in range(cv.tiles):
                tile = None
                for g in range(cv.per):
                    t = j * cv.per + g
                    if t < 9:
                        v = turned[pl.ds(9 * kz + t, cv.c, stride=27)]
                        tile = v if tile is None else jnp.where(group == g, v, tile)
                tile = tile.astype(BF16)
                wt[kz, :, j * LANES : (j + 1) * LANES] = tile.astype(wt.dtype)
                wide_ref[kz * cv.c : (kz + 1) * cv.c, j * LANES : (j + 1) * LANES] = tile.astype(F32)
        rows = -(-3 * cv.c // LANES) * LANES
        for i in range(rows // LANES):
            v = jnp.transpose(wide_ref[i * LANES : (i + 1) * LANES, 0 : cv.wide])
            size = min(LANES, 3 * cv.c - i * LANES)
            wf[:, i * LANES : i * LANES + size] = v[0 : 9 * cv.o, 0:size].astype(BF16)

    def weight_parts(k):
        cv, wt = convs[k], (wt1, wt2, wt3, wt4)[k]
        into = ((wx1,), (wx2,), (wx3u, wx3g), (wx4,))[k]
        parts = []
        for b, (size, start) in enumerate(cv.blocks):
            for t in range(1, nc):
                to, source = lax.rem(me + t, nc), lax.rem(me + nc - t, nc)
                at = start(to)
                sems = (w_send.at[k, b, t], w_recv.at[k, b, t])
                out = lambda b=b, at=at, size=size, to=to, sems=sems: peer_copy(
                    wt.at[:, pl.ds(at, size)], into[b].at[me], *sems, place, to
                )
                back = lambda b=b, source=source, sems=sems: peer_copy(
                    into[b].at[source], into[b].at[source], *sems, place, source
                )
                parts.append((out, back))
        return parts

    def weights_start(k):
        cv, wt = convs[k], (wt1, wt2, wt3, wt4)[k]
        into = ((wx1,), (wx2,), (wx3u, wx3g), (wx4,))[k]
        for b, (size, start) in enumerate(cv.blocks):
            into[b][me] = wt[:, pl.ds(start(me), size)]
        for out, _ in weight_parts(k):
            out().start()
            pending.append((None, lambda out=out: out().wait_send()))

    def weights_finish(k):
        cv = convs[k]
        into = ((wx1,), (wx2,), (wx3u, wx3g), (wx4,))[k]
        out = (wb1, wb2, wb3, wb4)[k]
        every = sum(size for size, _ in cv.blocks)
        offset = 0
        for _, back in weight_parts(k):
            back().wait_recv()
        for b, (size, _) in enumerate(cv.blocks):
            for t in range(9):
                pieces = [
                    into[b][j, 2 - kz, :, t * cv.o : (t + 1) * cv.o].astype(F32)
                    for kz in range(3)
                    for j in range(nc)
                ]
                at = (8 - t) * every + offset
                out[at : at + size] = jnp.concatenate(pieces, 1).astype(BF16)
            offset += size

    def reduce_copy(k, t):
        cv, gt, gr = convs[k], (gt1, gt2, gt3, gt4)[k], (gr1, gr2, gr3, gr4)[k]
        to = lax.rem(place + t, nd)
        return peer_copy(
            gt.at[pl.ds(to * cv.share, cv.share)], gr.at[place], r_send.at[k, t], r_recv.at[k, t], to, me
        )

    def reduce_start(k):
        cv, gt, gr = convs[k], (gt1, gt2, gt3, gt4)[k], (gr1, gr2, gr3, gr4)[k]

        def tile(i, carry):
            for j in range(cv.tiles):
                at = pl.multiple_of(i * 16, 16)
                gt[i * cv.tiles + j] = acc[pl.ds(at, 16), j * LANES : (j + 1) * LANES].astype(BF16)
            return carry

        lax.fori_loop(0, 3 * cv.c // 16, tile, 0, unroll=4)
        for i in range(cv.count, cv.share * nd):
            gt[i] = jnp.zeros((16, LANES), BF16)
        gr[place] = gt[pl.ds(place * cv.share, cv.share)]

        def send(t, _):
            reduce_copy(k, t).start()
            return _

        def sent(t, _):
            reduce_copy(k, t).wait_send()
            return _

        lax.fori_loop(1, nd, send, 0)
        pending.append((None, lambda: lax.fori_loop(1, nd, sent, 0)))

    def share_copy(k, t):
        cv, ga = convs[k], (ga1, ga2, ga3, ga4)[k]
        own = ga.at[pl.ds(place * cv.share, cv.share)]
        return peer_copy(own, own, a_send.at[k, t], a_recv.at[k, t], lax.rem(place + t, nd), me)

    def reduce_finish(k):
        cv, gr, ga = convs[k], (gr1, gr2, gr3, gr4)[k], (ga1, ga2, ga3, ga4)[k]

        def receive(t, _):
            source = lax.rem(place + nd - t, nd)
            peer_copy(gr.at[source], gr.at[source], r_send.at[k, t], r_recv.at[k, t], source, me).wait_recv()
            return _

        lax.fori_loop(1, nd, receive, 0)
        ga[pl.ds(place * cv.share, cv.share)] = jnp.sum(gr[...].astype(F32), axis=0).astype(BF16)

        def send(t, _):
            share_copy(k, t).start()
            return _

        def sent(t, _):
            share_copy(k, t).wait_send()
            return _

        lax.fori_loop(1, nd, send, 0)
        pending.append((None, lambda: lax.fori_loop(1, nd, sent, 0)))

    def gradient_out(k):
        cv, ga, out = convs[k], (ga1, ga2, ga3, ga4)[k], (g1, g2, g3, g4)[k]

        def receive(t, _):
            source = lax.rem(place + nd - t, nd)
            theirs = ga.at[pl.ds(source * cv.share, cv.share)]
            peer_copy(theirs, theirs, a_send.at[k, t], a_recv.at[k, t], source, me).wait_recv()
            return _

        lax.fori_loop(1, nd, receive, 0)
        group = iota((16, LANES), 1) // cv.o

        def scatter(i, carry):
            for kz in range(3):
                for j in range(cv.tiles):
                    v = ga[(kz * (cv.c // 16) + i) * cv.tiles + j].astype(F32)
                    for g in range(cv.per):
                        t = j * cv.per + g
                        if t < 9:
                            turned[pl.ds(9 * kz + t + i * (16 * 27), 16, stride=27)] = jnp.where(group == g, v, 0.0)
            return carry

        lax.fori_loop(0, cv.c // 16, scatter, 0, unroll=2)

        def chunk(at):
            v = jnp.transpose(turned[pl.ds(at, LANES)])
            return jnp.sum(v.reshape(cv.per, cv.o, LANES), axis=0)

        full = cv.length // LANES

        def body(i, carry):
            at = pl.multiple_of(i * LANES, LANES)
            out[:, pl.ds(at, LANES)] = chunk(at)
            return carry

        lax.fori_loop(0, full, body, 0, unroll=4)
        if full < cv.chunks:
            out[:, full * LANES :] = chunk(full * LANES)[:, 0 : cv.length - full * LANES]

    def column(row):
        n = row.shape[1]
        eye = iota((n, n), 0) == iota((n, n), 1)
        return jnp.sum(jnp.where(eye, row, 0.0), axis=1, keepdims=True)

    def row_of(col):
        n = col.shape[0]
        eye = iota((n, n), 0) == iota((n, n), 1)
        return jnp.sum(jnp.where(eye, col, 0.0), axis=0, keepdims=True)

    def clear_edges(ref):
        n = ref.shape[0]
        blank = jnp.zeros(ref.shape[2:], ref.dtype)

        for s in range(n):
            ref[s, 0] = blank
            ref[s, ref.shape[1] - 1] = blank

    def clear_halos(ref):
        def clear(s):
            ref[s] = jnp.zeros(ref.shape[1:], ref.dtype)

        pl.when(first)(lambda: clear(0))
        pl.when(last)(lambda: clear(ref.shape[0] - 1))

    def conv(ref, weight, slices, rows, m, n, width, emit, init):
        per = rows // n

        def body(i, carry):
            d = i // per
            r0 = (i - d * per) * n
            x = jnp.concatenate(
                [
                    jnp.concatenate([flat(ref, d + kz, r0 + j) for j in range(n + 2)], 1)
                    for kz in range(3)
                ],
                0,
            )
            y = dot(weight[...], x)
            results = []
            for j in range(n):
                acc = []
                for kx in range(3):
                    terms = [
                        y[(3 * ky + kx) * m : (3 * ky + kx + 1) * m, (j + ky) * LANES : (j + ky + 1) * LANES]
                        for ky in range(3)
                    ]
                    acc.append(terms[0] + terms[1] + terms[2])
                results.append(from_left(acc[0], width) + acc[1] + from_right(acc[2], width))
            return emit(d, r0, results, carry)

        return lax.fori_loop(0, slices * per, body, init)

    def weight_grad(ref, dz, k, slices, rows, n):
        per = rows // n
        cv = convs[k]
        acc[0 : 3 * cv.c, 0 : cv.wide] = jnp.zeros((3 * cv.c, cv.wide), F32)

        def body(i, carry):
            d = i // per
            r0 = (i - d * per) * n
            x = jnp.concatenate(
                [
                    jnp.concatenate([flat(ref, d + kz, r0 + 1 + j) for j in range(n)], 1)
                    for kz in range(3)
                ],
                0,
            )
            y = jnp.concatenate(
                [
                    jnp.concatenate([dz[kx, d, r0 + j + 2 - ky] for j in range(n)], 1)
                    for ky in range(3)
                    for kx in range(3)
                ],
                0,
            ).astype(BF16)
            acc[0 : 3 * cv.c, 0 : 9 * cv.o] += dot_nt(x, y)
            return carry

        lax.fori_loop(0, slices * per, body, 0)

    def conv_coarse(ref, weight, m):
        x = jnp.concatenate(
            [jnp.concatenate([flat(ref, kz, i) for i in range(Q)], 1) for kz in range(3)], 0
        )
        y = dot(weight[...], x)
        blank = jnp.zeros((m, LANES), F32)

        def shifted(ky, i):
            if not 0 <= i < Q:
                return blank
            a, b, c = (
                y[(3 * ky + kx) * m : (3 * ky + kx + 1) * m, i * LANES : (i + 1) * LANES] for kx in range(3)
            )
            return from_left(a, V) + b + from_right(c, V)

        before = [shifted(0, i) for i in range(-1, Q)]
        after = [shifted(2, i) for i in range(Q + 1)]
        return [
            shifted(1, i) + halves(before[i + 1] + after[i + 1], before[i] + after[i]) for i in range(Q)
        ]

    def conv_stats_coarse(ref, weight, z, m):
        total = square = jnp.zeros((m, LANES), F32)
        for i, v in enumerate(conv_coarse(ref, weight, m)):
            z[i] = v
            total, square = total + v, square + v * v
        return pack(total, square)

    def weight_grad_coarse(ref, k):
        cv = convs[k]
        x = jnp.concatenate(
            [jnp.concatenate([flat(ref, kz, i) for i in range(Q)], 1) for kz in range(3)], 0
        )
        y = jnp.concatenate([jnp.concatenate([dzc[t, i] for i in range(Q)], 1) for t in range(9)], 0)
        acc[0 : 3 * cv.c, 0 : 9 * cv.o] = dot_nt(x, y.astype(BF16))

    def norm_back_coarse(z, du, stats, norm, total, x):
        mean, inv = stats
        scale = norm[0] * inv
        a = total[0] / dm.coarse_total
        b = total[1] / dm.coarse_total
        rows = []
        for i in range(Q):
            v = scale * (du[i] - a - (z[i] - mean) * inv * b)
            low = v.astype(BF16)
            x[1, i, me] = low.astype(x.dtype)
            rows.append(low.astype(F32))
        blank = jnp.zeros_like(rows[0])
        rows = [blank] + rows + [blank]
        for i in range(Q):
            before, here, after = rows[i : i + 3]
            for ky, v in enumerate((halves(after, here), here, halves(here, before))):
                for kx, u in enumerate((from_right(v, V), v, from_left(v, V))):
                    dzc[3 * ky + kx, i] = u.astype(dzc.dtype)

    def conv_stats(ref, weight, z, slices, rows, m, n, width):
        def emit(d, r0, results, carry):
            total, square = carry
            for j, v in enumerate(results):
                z[d * rows + r0 + j] = v
                total, square = total + v, square + v * v
            return total, square

        blank = jnp.zeros((m, LANES), F32)
        total, square = conv(ref, weight, slices, rows, m, n, width, emit, (blank, blank))
        return pack(total, square)

    def pack(a, b):
        m = a.shape[0]
        a = jnp.sum(a, axis=1, keepdims=True)
        b = jnp.sum(b, axis=1, keepdims=True)
        lane, channel = iota((m, LANES), 1), iota((m, LANES), 0)
        both = jnp.where(lane == channel, a, jnp.where(lane == channel + m, b, 0.0))
        return jnp.sum(both, axis=0, keepdims=True)

    def moments(total, count):
        mean = total[0] / count
        var = total[1] / count - mean * mean
        return mean, lax.rsqrt(var + EPS)

    def norm_apply(z, mean, inv, gain, shift):
        xhat = (z - mean) * inv
        u = gain * xhat + shift
        return xhat, u, jax.nn.sigmoid(u)

    def norm_rows(z, stats, norm, emit, n):
        mean, inv = stats
        gain, shift = norm

        def body(i, carry):
            for j in range(n):
                p = i * n + j
                _, u, sigma = norm_apply(z[p], mean, inv, gain, shift)
                emit(p, u * sigma)
            return carry

        lax.fori_loop(0, z.shape[0] // n, body, 0)

    def norm_back_sums(z, du, stats, norm, grad, n):
        mean, inv = stats
        gain, shift = norm
        m = z.shape[1]

        def body(i, carry):
            a, b = carry
            for j in range(n):
                p = i * n + j
                xhat, u, sigma = norm_apply(z[p], mean, inv, gain, shift)
                v = grad(p) * sigma * (1.0 + u * (1.0 - sigma))
                du[p] = v
                a, b = a + v, b + v * xhat
            return a, b

        blank = jnp.zeros((m, LANES), F32)
        return pack(*lax.fori_loop(0, z.shape[0] // n, body, (blank, blank)))

    def norm_back(z, du, stats, norm, total, count, x, dz, rows, width, n):
        mean, inv = stats
        gain, _ = norm
        scale = gain * inv
        a = total[0] / count
        b = total[1] / count
        per = rows // n

        def body(i, carry):
            d = i // per
            r0 = (i - d * per) * n
            for j in range(n):
                p = i * n + j
                xhat = (z[p] - mean) * inv
                v = scale * (du[p] - a - xhat * b)
                low = v.astype(BF16)
                x[1 + d, 1 + r0 + j, me] = low.astype(x.dtype)
                v = low.astype(F32)
                dz[0, d, 1 + r0 + j] = from_right(v, width).astype(dz.dtype)
                dz[1, d, 1 + r0 + j] = low.astype(dz.dtype)
                dz[2, d, 1 + r0 + j] = from_left(v, width).astype(dz.dtype)
            return carry

        lax.fori_loop(0, z.shape[0] // n, body, 0)

    hc = iota((LANES, LANES), 0)
    fc = iota((LANES, LANES), 1)
    half = LANES // 2

    def up_table(coarse, fine):
        base = fine // 2
        other = jnp.clip(base + jnp.where(fine % 2 == 0, -1, 1), 0, V - 1)
        near = (coarse == base).astype(F32)
        far = (coarse == other).astype(F32)
        return (0.75 * near + 0.25 * far).astype(BF16)

    pool = jnp.concatenate([(hc // 2 == fc - at).astype(BF16) for at in (0, half)], 0)
    spread = jnp.concatenate([(hc - at == fc // 2).astype(BF16) for at in (0, half)], 1)
    up = jnp.concatenate([up_table(hc - at, fc) for at in (0, half)], 1)
    down = jnp.concatenate([up_table(fc - at, hc) for at in (0, 0, half, half)], 0)
    spread2 = jnp.concatenate([spread, spread], 0)

    def take_rows(ref):
        for c in range(dm.cs):
            rows_ref[c * S * R : (c + 1) * S * R] = ref[c].astype(F32).reshape(S * R, LANES)

    def row(p):
        return rows_ref[pl.ds(p, dm.cs, stride=S * R)]

    clear_halos(xp)
    take_rows(skip_ref)

    def take_skip(i, carry):
        parts = []
        for s in range(S):
            v = [row(s * R + 4 * i + j).astype(BF16) for j in range(4)]
            for j in range(4):
                xs[1 + s, 4 * i + j, me] = v[j].astype(xs.dtype)
            parts += [jnp.concatenate([v[j], v[2 + j]], 1) for j in range(2)]
        v = dot(jnp.concatenate(parts, 0), pool).reshape(2 * S, dm.cs, LANES)
        xp[1, i, me] = (jnp.sum(v, axis=0) * 0.125).astype(BF16).astype(xp.dtype)
        return carry

    lax.fori_loop(0, Q, take_skip, 0, unroll=3)
    gather_start(xp, "pooled", 0)
    clear_halos(xs)
    gather_start(xs, "skip", 0)

    gq = dm.g // nc
    gate_all[me, :, 0 : gate_ref.shape[1]] = gate_ref[...]
    lane = iota((gq, LANES), 1)
    gate_all[me, :, 2 * LANES :] = jnp.where(
        lane == 0, column(vector_ref[0:1]), jnp.where(lane == 1, column(vector_ref[1:2]), 0.0)
    )
    for t in range(1, nc):
        to, source = lax.rem(me + t, nc), lax.rem(me + nc - t, nc)
        out = peer_copy(gate_all.at[me], gate_all.at[me], v_send.at[t], v_recv.at[t], place, to)
        out.start()
        pending.append((None, out.wait_send))

    prepare(0)
    for ref in (xd, d1, xz4, xz3):
        clear_edges(ref)
    for ref in (xh, xd, xz4, xz3, xz2, xz1):
        clear_halos(ref)
    for kx in range(3):
        for s in range(S):
            dzf[kx, s, 0] = jnp.zeros(dzf.shape[3:], dzf.dtype)
            dzf[kx, s, R + 1] = jnp.zeros(dzf.shape[3:], dzf.dtype)

    def norm_of(ref, layer):
        return column(ref[0, layer : layer + 1]), column(ref[1, layer : layer + 1])

    norm_e1, norm_e2 = norm_of(en_ref, 0), norm_of(en_ref, 1)
    norm_d1, norm_d2 = norm_of(dn_ref, 0), norm_of(dn_ref, 1)

    gather_pass(xp, "pooled", 0)
    gather_wait(xp, "pooled", 0)
    sum_start(st, 0, 0, conv_stats_coarse(xp, wf1, z1, dm.ce))
    prepare(1)
    stats_e1 = moments(totals(0, 0, dm.ce), dm.coarse_total)

    def keep_hidden(p, v):
        xh[1, p, me] = v.astype(BF16).astype(xh.dtype)

    norm_rows(z1, stats_e1, norm_e1, keep_hidden, 3)
    gather_start(xh, "hidden", 0)
    prepare(2)
    gather_pass(xh, "hidden", 0)
    gather_pass(xs, "skip", 0)
    gather_wait(xh, "hidden", 0)
    sum_start(st, 1, 1, conv_stats_coarse(xh, wf2, z2, dm.ce))
    prepare(3)
    stats_e2 = moments(totals(1, 1, dm.ce), dm.coarse_total)

    def keep_coarse(p, v):
        xc[1, p, me] = v.astype(BF16).astype(xc.dtype)

    norm_rows(z2, stats_e2, norm_e2, keep_coarse, 3)
    gather_start(xc, "coarse", 0)
    for k in (3, 2, 1, 0):
        weights_start(k)
    for t in range(1, nc):
        source = lax.rem(me + nc - t, nc)
        peer_copy(
            gate_all.at[source], gate_all.at[source], v_send.at[t], v_recv.at[t], place, source
        ).wait_recv()
    gate_full = gate_all[...].reshape(dm.g, 3 * LANES)
    wg = gate_full[:, 0 : dm.enc_all + dm.skip_all].astype(BF16)
    gbias = gate_full[:, 2 * LANES : 2 * LANES + 1]
    gout = gate_full[:, 2 * LANES + 1 : 2 * LANES + 2]
    gate_t[...] = jnp.transpose(gate_full[:, 0 : 2 * LANES])
    gate_own[...] = jnp.concatenate(
        [
            gate_t[pl.ds(pl.multiple_of(me * dm.ce, dm.ce), dm.ce)],
            gate_t[pl.ds(pl.multiple_of(dm.enc_all + me * dm.cs, dm.cs), dm.cs)],
        ],
        0,
    )
    gather_pass(xc, "coarse", 0)
    gather_wait(xc, "coarse", 0)

    def up_depth(i, carry):
        t = []
        for s in range(3):
            v = dot(flat(xc, s, i), up)
            t.append(jnp.stack([v[:, 0:LANES], v[:, LANES:]], 0))
        below = jnp.where(first, t[1], t[0])
        above = jnp.where(last, t[1], t[2])
        near = 0.75 * t[1]
        here = 0.25 * t[1]
        rows = pl.ds(i * 2, 2)
        dt[0, rows] = jnp.where(first, 0.0, 0.75 * below + here)
        dt[1, rows] = near + 0.25 * below
        dt[2, rows] = near + 0.25 * above
        dt[3, rows] = jnp.where(last, 0.0, 0.75 * above + here)
        return carry

    lax.fori_loop(0, Q, up_depth, 0)

    def up_rows(i, carry):
        before, after = jnp.maximum(i - 1, 0), jnp.minimum(i + 1, H - 1)
        for s in range(S + 2):
            v = 0.75 * dt[s, i]
            d1[s, 1 + 2 * i, 0 : dm.enc_all] = (v + 0.25 * dt[s, before]).astype(BF16)
            d1[s, 2 + 2 * i, 0 : dm.enc_all] = (v + 0.25 * dt[s, after]).astype(BF16)
        return carry

    lax.fori_loop(0, H, up_rows, 0)

    gather_wait(xs, "skip", 0)
    gate_n = 12

    def gate(i, carry):
        s = i // (R // gate_n)
        r0 = (i - s * (R // gate_n)) * gate_n
        skips = [flat(xs, s, r0 + j) for j in range(gate_n)]
        x = jnp.concatenate(
            [
                jnp.concatenate([d1[s, 1 + r0 + j, 0 : dm.enc_all] for j in range(gate_n)], 1),
                jnp.concatenate(skips, 1),
            ],
            0,
        )
        pre = dot(wg, x) + gbias
        act = pre * jax.nn.sigmoid(pre)
        alpha = jax.nn.sigmoid(jnp.sum(gout * act, axis=0, keepdims=True))
        for j in range(gate_n):
            lanes = slice(j * LANES, (j + 1) * LANES)
            d1[s, 1 + r0 + j, dm.enc_all :] = (alpha[:, lanes] * skips[j].astype(F32)).astype(BF16)
            pre_ref[s, r0 + j] = pre[:, lanes]
            al_ref[s, r0 + j] = alpha[:, lanes]
        return carry

    lax.fori_loop(0, (S + 2) * R // gate_n, gate, 0)

    sum_start(st, 4, 4, conv_stats(d1, wf3, z3, S, R, dm.cd, 12, W))
    weights_finish(3)
    stats_d1 = moments(totals(4, 4, dm.cd), dm.fine_total)

    def keep_dec(p, v):
        s = p // R
        xd[1 + s, 1 + p - s * R, me] = v.astype(BF16).astype(xd.dtype)

    norm_rows(z3, stats_d1, norm_d1, keep_dec, 8)
    gather_start(xd, "dhidden", 1)
    weights_finish(2)
    take_rows(cot_ref)
    gather_pass(xd, "dhidden", 1)
    gather_wait(xd, "dhidden", 1)
    sum_start(st, 5, 5, conv_stats(xd, wf4, z4, S, R, dm.cd, 12, W))
    weights_finish(1)
    weights_finish(0)
    stats_d2 = moments(totals(5, 5, dm.cd), dm.fine_total)

    sum_start(st, 6, 6, norm_back_sums(z4, du_f, stats_d2, norm_d2, row, 8))

    def keep_result(p, v):
        s = p // R
        out_ref[s, p - s * R] = v.astype(BF16)

    norm_rows(z4, stats_d2, norm_d2, keep_result, 8)
    total_d2 = totals(6, 6, dm.cd)
    norm_back(z4, du_f, stats_d2, norm_d2, total_d2, dm.fine_total, xz4, dzf, R, W, 8)
    gather_start(xz4, "dz4", 1)
    weight_grad(xd, dzf, 3, S, R, 12)
    reduce_start(3)
    gather_pass(xz4, "dz4", 1)
    gather_wait(xz4, "dz4", 1)

    def keep_grad(d, r0, results, carry):
        for j, v in enumerate(results):
            gg[d * R + r0 + j] = v
        return carry

    conv(xz4, wb4, S, R, dm.cd, 12, W, keep_grad, 0)
    sum_start(st, 7, 7, norm_back_sums(z3, du_f, stats_d1, norm_d1, lambda p: gg[p], 8))
    total_d1 = totals(7, 7, dm.cd)
    norm_back(z3, du_f, stats_d1, norm_d1, total_d1, dm.fine_total, xz3, dzf, R, W, 8)
    gather_start(xz3, "dz3", 1)
    reduce_finish(3)
    weight_grad(d1, dzf, 2, S, R, 12)
    reduce_start(2)
    gather_pass(xz3, "dz3", 1)
    gather_wait(xz3, "dz3", 1)

    def gate_back(d, r0, results, carry):
        bias, psi = carry
        lows = []
        for j, both in enumerate(results):
            s, r = d + 1, r0 + j
            ug_ref[d * R + r] = both[0 : dm.ce]
            v = both[dm.ce :]
            grad = jnp.sum(v * flat(xs, s, r).astype(F32), axis=0, keepdims=True)
            alpha = al_ref[s, r]
            logit = grad * alpha * (1.0 - alpha)
            pre = pre_ref[s, r]
            sigma = jax.nn.sigmoid(pre)
            psi = psi + pre * sigma * logit
            low = (logit * gout * sigma * (1.0 + pre * (1.0 - sigma))).astype(BF16)
            bias = bias + low.astype(F32)
            pg_ref[d * R + r] = low
            lows.append(low)
            for t in range(nc):
                gg[t] = v[t * dm.cs : (t + 1) * dm.cs]
            sg_ref[d, r] = alpha * gg[me]
        back = dot(gate_own[...].astype(BF16), jnp.concatenate(lows, 1))
        for j in range(len(results)):
            lanes = slice(j * LANES, (j + 1) * LANES)
            ug_ref[d * R + r0 + j] += back[0 : dm.ce, lanes]
            sg_ref[d, r0 + j] += back[dm.ce :, lanes]
        return bias, psi

    blank = jnp.zeros((dm.g, LANES), F32)
    bias, psi = conv(xz3, wb3, S, R, dm.ce + dm.skip_all, 8, W, gate_back, (blank, blank))

    def down_rows(i, carry):
        terms = []
        for s in range(S):
            pair = []
            for j in range(2):
                r = i * 2 + j
                near = ug_ref[s * R + 2 * r] + ug_ref[s * R + 2 * r + 1]
                far = ug_ref[s * R + jnp.minimum(2 * r + 2, R - 1)] + ug_ref[s * R + jnp.maximum(2 * r - 1, 0)]
                pair.append(split(0.75 * near + 0.25 * far))
            terms.append(jnp.concatenate(pair, 1))
        v = dot(jnp.concatenate(terms, 0), down)
        even, odd = v[0 : dm.ce], v[dm.ce :]
        fs[0, i] = 0.25 * even
        fs[1, i] = 0.25 * odd
        cg[i] = 0.75 * (even + odd) + jnp.where(first, 0.25 * even, 0.0) + jnp.where(last, 0.25 * odd, 0.0)
        return carry

    lax.fori_loop(0, Q, down_rows, 0)

    def fold(side, step):
        return peer_copy(fs.at[side], fr.at[1 - side], f_send.at[side], f_recv.at[1 - side], place + step, me)

    pl.when(jnp.logical_not(first))(lambda: fold(0, -1).start())
    pl.when(jnp.logical_not(last))(lambda: fold(1, 1).start())
    pending.append((jnp.logical_not(first), lambda: fold(0, -1).wait_send()))
    pending.append((jnp.logical_not(last), lambda: fold(1, 1).wait_send()))
    reduce_finish(2)

    def fold_in(side):
        peer_copy(fs.at[side], fr.at[side], f_send.at[side], f_recv.at[side], place, me).wait_recv()
        cg[...] += fr[side]

    pl.when(jnp.logical_not(first))(lambda: fold_in(0))
    pl.when(jnp.logical_not(last))(lambda: fold_in(1))

    sum_start(st, 2, 2, norm_back_sums(z2, du_c, stats_e2, norm_e2, lambda p: cg[p], 3))

    columns = gate_ref.shape[1]
    acc[0 : dm.g, 0:columns] = jnp.zeros((dm.g, columns), F32)

    weight_n = 12

    def gate_weight(i, carry):
        d = i // (R // weight_n)
        r0 = (i - d * (R // weight_n)) * weight_n
        x = jnp.concatenate(
            [
                jnp.concatenate([d1[1 + d, 1 + r0 + j, 0 : dm.enc_all] for j in range(weight_n)], 1),
                jnp.concatenate([flat(xs, 1 + d, r0 + j) for j in range(weight_n)], 1),
            ],
            0,
        )
        y = jnp.concatenate([pg_ref[d * R + r0 + j] for j in range(weight_n)], 1)
        acc[0 : dm.g, 0:columns] += dot_nt(y, x)
        return carry

    lax.fori_loop(0, S * R // weight_n, gate_weight, 0)
    lane = iota((dm.g, LANES), 1)
    vectors = jnp.where(
        lane == 0,
        jnp.sum(bias, axis=1, keepdims=True),
        jnp.where(lane == 1, jnp.sum(psi, axis=1, keepdims=True), 0.0),
    )
    for j in range(nc):
        mine = slice(j * gq, (j + 1) * gq)
        gate_block[j, :, 0:columns] = acc[mine, 0:columns]
        gate_block[j, :, columns : 2 * LANES] = jnp.zeros((gq, 2 * LANES - columns), F32)
        gate_block[j, :, 2 * LANES :] = vectors[mine]
    sum_start(st_g, 8, 0, gate_block[me])
    total_e2 = totals(2, 2, dm.ce)
    norm_back_coarse(z2, du_c, stats_e2, norm_e2, total_e2, xz2)
    gather_start(xz2, "dz2", 0)
    weight_grad_coarse(xh, 1)
    reduce_start(1)
    gather_pass(xz2, "dz2", 0)
    gradient_out(3)
    gather_wait(xz2, "dz2", 0)
    for i, v in enumerate(conv_coarse(xz2, wb2, dm.ce)):
        cg[i] = v
    sum_start(st, 3, 3, norm_back_sums(z1, du_c, stats_e1, norm_e1, lambda p: cg[p], 3))
    reduce_finish(1)
    total_e1 = totals(3, 3, dm.ce)
    norm_back_coarse(z1, du_c, stats_e1, norm_e1, total_e1, xz1)
    gather_start(xz1, "dz1", 0)
    weight_grad_coarse(xp, 0)
    reduce_start(0)
    gather_pass(xz1, "dz1", 0)
    gradient_out(2)
    gather_wait(xz1, "dz1", 0)
    for i, v in enumerate(conv_coarse(xz1, wb1, dm.cs)):
        v = dot(split(v), spread2) * 0.125
        for j in range(4):
            part = v[:, (j // 2) * LANES : (j // 2 + 1) * LANES]
            for s in range(S):
                sg_ref[s, 4 * i + j] += part
    reduce_finish(0)
    gradient_out(1)
    gate_total = sum_finish(st_g, 8, 0)
    ggate[...] = gate_total[:, 0:columns]
    gvector[0:1] = row_of(gate_total[:, 2 * LANES : 2 * LANES + 1])
    gvector[1:2] = row_of(gate_total[:, 2 * LANES + 1 : 2 * LANES + 2])
    for ref, sums in ((gen, (total_e1, total_e2)), (gdn, (total_d1, total_d2))):
        for layer, total in enumerate(sums):
            ref[0, layer : layer + 1] = row_of(total[1])
            ref[1, layer : layer + 1] = row_of(total[0])
    gradient_out(0)
    for cond, fn in pending:
        guarded(cond, fn)


def adamw(weight, grad, moment, square, rate):
    new_moment = 0.9 * moment + 0.1 * grad
    new_square = 0.999 * square + 0.001 * grad * grad
    moment_hat = new_moment / (1.0 - 0.9**STEP)
    square_hat = new_square / (1.0 - 0.999**STEP)
    new_weight = weight - rate * (moment_hat / (jnp.sqrt(square_hat) + 1e-08) + 0.01 * weight)
    return (new_weight, new_moment, new_square)


RATES = (CONV_RATE, CONV_RATE, GATE_RATE, VECTOR_RATE, CONV_RATE, CONV_RATE, VECTOR_RATE, VECTOR_RATE)


def update_kernel(*refs):
    n = len(RATES)
    params, grads, moments, squares = (refs[i * n : (i + 1) * n] for i in range(4))
    outs = refs[4 * n :]
    for k, rate in enumerate(RATES):
        rows = params[k].shape[0]
        step = 8 if rows % 8 == 0 and rows > 8 else rows
        for r in range(0, rows, step):
            at = slice(r, r + step)
            new = adamw(params[k][at], grads[k][at], moments[k][at], squares[k][at], rate)
            for ref, value in zip(outs[3 * k : 3 * k + 3], new):
                ref[at] = value


def per_device(
    skip, cotangent, enc_conv1, enc_conv2, gate_proj, gate_vector, dec_conv1, dec_conv2, enc_norms, dec_norms, *states
):
    nd, nc = lax.axis_size("depth"), lax.axis_size("chan")
    dm = Dims(nd, nc, skip.shape, enc_conv1.shape[0], dec_conv1.shape[0], gate_proj.shape[0] * nc)
    S, R, H = dm.s, dm.rows, dm.half
    cin3 = dm.enc_all + dm.skip_all

    def block_of(size):
        return (size, lambda j: pl.multiple_of(j * size, size))

    dm.convs = convs = (
        Conv(dm, dm.ce, dm.skip_all, (block_of(dm.cs),)),
        Conv(dm, dm.ce, dm.enc_all, (block_of(dm.ce),)),
        Conv(dm, dm.cd, cin3, (block_of(dm.ce), (dm.skip_all, lambda j: dm.enc_all))),
        Conv(dm, dm.cd, dm.dec_all, (block_of(dm.cd),)),
    )
    params = (enc_conv1, enc_conv2, gate_proj, gate_vector, dec_conv1, dec_conv2, enc_norms, dec_norms)
    inputs = (
        skip, cotangent, enc_conv1, enc_conv2, dec_conv1, dec_conv2, gate_proj, gate_vector, enc_norms, dec_norms
    )
    shape = jax.ShapeDtypeStruct
    outs = (
        shape((S, R, dm.cd, LANES), BF16),
        shape((S, R, dm.cs, LANES), F32),
        *(shape(a.shape, F32) for a in (enc_conv1, enc_conv2, dec_conv1, dec_conv2)),
        *(shape(a.shape, F32) for a in (gate_proj, gate_vector, enc_norms, dec_norms)),
    )

    def ext(slices, rows, block):
        return pltpu.VMEM((slices, rows, nc, block, LANES), storage(block))

    def exchange(cv):
        return [pltpu.VMEM((nc, 3, size, cv.wide), cv.kind) for size, _ in cv.blocks]

    def backward(cv):
        return [pltpu.VMEM((9 * sum(size for size, _ in cv.blocks), 3 * nc * cv.o), BF16)]

    gq = dm.g // nc
    Q = H // 2
    scratch = [
        ext(3, Q, dm.cs),
        ext(S + 2, R, dm.cs),
        ext(3, Q, dm.ce),
        ext(3, Q, dm.ce),
        pltpu.VMEM((S + 2, R + 2, cin3, LANES), BF16),
        ext(S + 2, R + 2, dm.cd),
        ext(S + 2, R + 2, dm.cd),
        ext(S + 2, R + 2, dm.cd),
        ext(3, Q, dm.ce),
        ext(3, Q, dm.ce),
        pltpu.VMEM((Q, dm.ce, LANES), F32),
        pltpu.VMEM((Q, dm.ce, LANES), F32),
        pltpu.VMEM((S * R, dm.cd, LANES), F32),
        pltpu.VMEM((S * R, dm.cd, LANES), F32),
        pltpu.VMEM((Q, dm.ce, LANES), F32),
        pltpu.VMEM((S * R, dm.cd, LANES), F32),
        pltpu.VMEM((S + 2, R, dm.g, LANES), F32),
        pltpu.VMEM((S + 2, R, 1, LANES), F32),
        pltpu.VMEM((S * R, dm.g, LANES), BF16),
        pltpu.VMEM((S * R, dm.ce, LANES), F32),
        pltpu.VMEM((S + 2, H, dm.enc_all, LANES), F32),
        pltpu.VMEM((S * R, dm.cd, LANES), F32),
        pltpu.VMEM((Q, dm.ce, LANES), F32),
        pltpu.VMEM((3, S, R + 2, dm.cd, LANES), storage(dm.cd)),
        pltpu.VMEM((9, Q, dm.ce, LANES), BF16),
        pltpu.VMEM((2, Q, dm.ce, LANES), F32),
        pltpu.VMEM((2, Q, dm.ce, LANES), F32),
        pltpu.VMEM((8, nd, 1, LANES), F32),
        pltpu.VMEM((1, nd, gq, 3 * LANES), F32),
        pltpu.VMEM((dm.cs * S * R, LANES), F32),
        pltpu.VMEM((max(cv.chunks for cv in convs) * LANES, LANES), F32),
        pltpu.VMEM((max(-(-3 * cv.c // LANES) for cv in convs) * LANES, max(cv.wide for cv in convs)), F32),
        pltpu.VMEM((max(3 * cv.c for cv in convs), max(cv.wide for cv in convs)), F32),
        pltpu.VMEM((nc, gq, 3 * LANES), F32),
        pltpu.VMEM((2 * LANES, dm.g), F32),
        pltpu.VMEM((dm.ce + dm.cs, dm.g), F32),
        pltpu.VMEM((nc, gq, 3 * LANES), F32),
        *(pltpu.VMEM((3, cv.c, cv.wide), cv.kind) for cv in convs),
        *(pltpu.VMEM((9 * cv.o, 3 * cv.c), BF16) for cv in convs),
        *(ref for cv in convs for ref in exchange(cv)),
        *(ref for cv in convs for ref in backward(cv)),
        *(pltpu.VMEM((cv.share * nd, 16, LANES), BF16) for cv in convs),
        *(pltpu.VMEM((nd, cv.share, 16, LANES), BF16) for cv in convs),
        *(pltpu.VMEM((cv.share * nd, 16, LANES), BF16) for cv in convs),
        *[pltpu.SemaphoreType.DMA((len(GATHERS), 2, 3 * nc // 2))] * 2,
        *[pltpu.SemaphoreType.DMA((9, nd))] * 2,
        *[pltpu.SemaphoreType.DMA((2,))] * 2,
        *[pltpu.SemaphoreType.DMA((4, 2, nc))] * 2,
        *[pltpu.SemaphoreType.DMA((nc,))] * 2,
        *[pltpu.SemaphoreType.DMA((4, nd))] * 4,
    ]
    vmem = pl.BlockSpec(memory_space=pltpu.VMEM)
    out, sg, grad1, grad2, grad3, grad4, ggate, gvector, gen, gdn = pl.pallas_call(
        functools.partial(kernel, dm),
        out_shape=outs,
        in_specs=[vmem] * len(inputs),
        out_specs=[vmem] * len(outs),
        scratch_shapes=scratch,
        compiler_params=pltpu.CompilerParams(has_side_effects=True, vmem_limit_bytes=60 * 1024 * 1024),
        name="step",
    )(*inputs)
    grads = (grad1, grad2, ggate, gvector, grad3, grad4, gen, gdn)
    updated = pl.pallas_call(
        update_kernel,
        out_shape=tuple(shape(p.shape, F32) for p in params for _ in range(3)),
        in_specs=[vmem] * 32,
        out_specs=[vmem] * 24,
        compiler_params=pltpu.CompilerParams(vmem_limit_bytes=60 * 1024 * 1024),
        name="update",
    )(*params, *grads, *states)
    return (jnp.transpose(out, (2, 0, 1, 3)), jnp.transpose(sg, (2, 0, 1, 3)), *updated)


def solution(mesh):
    volume = P("chan", "depth", None, None)
    row, column, norms = P("chan", None), P(None, "chan"), P(None, None, "chan")
    params = (row, row, row, column, row, row, norms, norms)
    return jax.shard_map(
        per_device,
        mesh=mesh,
        in_specs=(volume, volume) + params * 3,
        out_specs=(volume, volume) + tuple(spec for spec in params for _ in range(3)),
        check_vma=False,
    )
```

```python
import functools

import jax
import jax.numpy as jnp
from jax import lax
from jax.experimental import pallas as pl
from jax.experimental.pallas import tpu as pltpu
from jax.sharding import PartitionSpec as P

STEP = 5
EPS = 1e-05
CONV_RATE = 0.03
GATE_RATE = 0.1
VECTOR_RATE = 0.5
LANES = 128
MESH = pl.DeviceIdType.MESH
F32 = jnp.float32
BF16 = jnp.bfloat16


def iota(shape, dim):
    return lax.broadcasted_iota(jnp.int32, shape, dim)


def dot(a, b):
    return jnp.dot(a, b, preferred_element_type=F32)


def dot_nt(a, b):
    return lax.dot_general(a, b, (((1,), (1,)), ((), ())), preferred_element_type=F32)


def from_left(v, width):
    return jnp.where(iota(v.shape, 1) % width == 0, 0.0, pltpu.roll(v, 1, 1))


def from_right(v, width):
    return jnp.where(iota(v.shape, 1) % width == width - 1, 0.0, pltpu.roll(v, LANES - 1, 1))


def halves(low, high):
    return pltpu.roll(jnp.where(iota(low.shape, 1) < LANES // 2, low, high), LANES // 2, 1)


def split(v):
    high = v.astype(BF16)
    return jnp.concatenate([high, (v - high.astype(F32)).astype(BF16)], 1)


def storage(block):
    return BF16 if block % 16 == 0 else F32


def flat(ref, s, r):
    v = ref[s, r]
    if v.ndim == 3:
        v = v.reshape(v.shape[0] * v.shape[1], LANES)
    return v.astype(BF16)


class Dims:
    def __init__(self, nd, nc, skip, enc, dec, gate):
        self.nd, self.nc = nd, nc
        self.s, self.rows, self.cols = skip[1:]
        self.cs, self.ce, self.cd, self.g = skip[0], enc, dec, gate
        self.half, self.hcols = self.rows // 2, self.cols // 2
        self.fine_total = nd * self.s * self.rows * self.cols
        self.coarse_total = self.fine_total // 8
        self.enc_all = nc * enc
        self.skip_all = nc * skip[0]
        self.dec_all = nc * dec


GATHERS = ("pooled", "skip", "hidden", "coarse", "dhidden", "dz4", "dz3", "dz2", "dz1")
CONVS = ("enc1", "enc2", "dec1", "dec2")


class Conv:
    def __init__(self, dm, o, c, blocks):
        self.o, self.c, self.blocks = o, c, blocks
        self.length = 27 * c
        self.chunks = -(-self.length // LANES)
        self.per = LANES // o
        self.tiles = -(-9 // self.per)
        self.wide = self.tiles * LANES
        self.kind = storage(min(size for size, _ in blocks))
        self.count = 3 * c // 16 * self.tiles
        self.share = -(-self.count // dm.nd)


def kernel(
    dm,
    skip_ref, cot_ref, w1, w2, w3, w4, gate_ref, vector_ref, en_ref, dn_ref,
    out_ref, sg_ref, g1, g2, g3, g4, ggate, gvector, gen, gdn,
    xp, xs, xh, xc, d1, xd, xz4, xz3, xz2, xz1,
    z1, z2, z3, z4, du_c, du_f, pre_ref, al_ref, pg_ref, ug_ref, dt, gg, cg,
    dzf, dzc, fs, fr, st, st_g, rows_ref, turned, wide_ref, acc, gate_all, gate_t, gate_own, gate_block,
    wt1, wt2, wt3, wt4, wf1, wf2, wf3, wf4, wx1, wx2, wx3u, wx3g, wx4, wb1, wb2, wb3, wb4,
    gt1, gt2, gt3, gt4, gr1, gr2, gr3, gr4, ga1, ga2, ga3, ga4,
    g_send, g_recv, t_send, t_recv, f_send, f_recv, w_send, w_recv, v_send, v_recv, r_send, r_recv, a_send, a_recv,
):
    nd, nc, S, R, H = dm.nd, dm.nc, dm.s, dm.rows, dm.half
    W, V = dm.cols, dm.hcols
    Q = H // 2
    place = lax.axis_index("depth")
    me = lax.axis_index("chan")
    first, last = place == 0, place == nd - 1
    convs = dm.convs
    pending = []

    def peer_copy(src, dst, send, recv, depth, chan):
        return pltpu.make_async_remote_copy(
            src_ref=src, dst_ref=dst, send_sem=send, recv_sem=recv,
            device_id={"depth": depth, "chan": chan}, device_id_type=MESH,
        )

    def gather_parts(ref, which, pad, sides=(1, 0, 2)):
        n = ref.shape[0] - 2
        span = pl.ds(pad, ref.shape[1] - 2 * pad)
        k = GATHERS.index(which)
        other = me + 1 - 2 * lax.rem(me, 2)
        parts = []
        for side, own, theirs, size in ((1, 1, 1, n), (0, n, 0, 1), (2, 1, n + 1, 1)):
            step = 1 - side
            if side not in sides:
                continue
            can_send = (jnp.logical_not(last), None, jnp.logical_not(first))[side]
            can_recv = (jnp.logical_not(first), None, jnp.logical_not(last))[side]
            for t in range(nc // 2):
                to, source = lax.rem(me + 2 * t, nc), lax.rem(me + nc - 2 * t, nc)
                mate = lax.rem(other + nc - 2 * t, nc)
                i = side * (nc // 2) + t

                def copy(own, block, at, hop, depth, chan, size=size, i=i):
                    return peer_copy(
                        ref.at[pl.ds(own, size), span, block],
                        ref.at[pl.ds(at, size), span, block],
                        g_send.at[k, hop, i], g_recv.at[k, hop, i], depth, chan,
                    )

                mine = side == 1 and t == 0
                out = None if mine else functools.partial(copy, own, me, theirs, 0, place + step, to)
                back = None if mine else functools.partial(copy, theirs, source, theirs, 0, place, source)
                on = functools.partial(copy, theirs, source, theirs, 1, place, other)
                mates = functools.partial(copy, theirs, mate, theirs, 1, place, other)
                parts.append((can_send, can_recv, out, back, on, mates))
        return parts

    def guarded(cond, fn):
        if cond is None:
            fn()
        else:
            pl.when(cond)(fn)

    def gather_start(ref, which, pad):
        for can_send, can_recv, out, _, on, _ in gather_parts(ref, which, pad):
            if out is None:
                on().start()
            else:
                guarded(can_send, lambda out=out: out().start())
                pending.append((can_send, lambda out=out: out().wait_send()))
            pending.append((can_recv, lambda on=on: on().wait_send()))

    def gather_pass(*where):
        for _, can_recv, out, back, on, _ in gather_parts(*where):
            if out is not None:

                def relay(back=back, on=on):
                    back().wait_recv()
                    on().start()

                guarded(can_recv, relay)

    def gather_wait(*where):
        for _, can_recv, _, _, _, mates in gather_parts(*where):
            guarded(can_recv, lambda mates=mates: mates().wait_recv())

    def sum_copy(ref, k, slot, t):
        return peer_copy(
            ref.at[slot, place], ref.at[slot, place], t_send.at[k, t], t_recv.at[k, t], lax.rem(place + t, nd), me
        )

    def sum_start(ref, k, slot, tile):
        ref[slot, place] = tile

        def send(t, _):
            sum_copy(ref, k, slot, t).start()
            return _

        def sent(t, _):
            sum_copy(ref, k, slot, t).wait_send()
            return _

        lax.fori_loop(1, nd, send, 0)
        pending.append((None, lambda: lax.fori_loop(1, nd, sent, 0)))

    def sum_finish(ref, k, slot):
        def receive(t, _):
            source = lax.rem(place + nd - t, nd)
            peer_copy(
                ref.at[slot, source], ref.at[slot, source], t_send.at[k, t], t_recv.at[k, t], source, me
            ).wait_recv()
            return _

        lax.fori_loop(1, nd, receive, 0)
        return jnp.sum(ref[slot], axis=0)

    def totals(k, slot, m):
        row = sum_finish(st, k, slot)
        lane, channel = iota((m, LANES), 1), iota((m, LANES), 0)
        return tuple(
            jnp.sum(jnp.where(lane == channel + i * m, row, 0.0), axis=1, keepdims=True) for i in range(2)
        )

    def turn_in(w, cv):
        def chunk(a):
            return jnp.transpose(jnp.concatenate([a] * cv.per, 0))

        full = cv.length // LANES

        def body(i, carry):
            at = pl.multiple_of(i * LANES, LANES)
            turned[pl.ds(at, LANES)] = chunk(w[:, pl.ds(at, LANES)])
            return carry

        lax.fori_loop(0, full, body, 0, unroll=4)
        if full < cv.chunks:
            a = w[:, full * LANES :]
            a = jnp.concatenate([a, jnp.zeros((cv.o, LANES - a.shape[1]), F32)], 1)
            turned[full * LANES : (full + 1) * LANES] = chunk(a)

    def prepare(k):
        cv, w, wt, wf = convs[k], (w1, w2, w3, w4)[k], (wt1, wt2, wt3, wt4)[k], (wf1, wf2, wf3, wf4)[k]
        turn_in(w, cv)
        group = iota((cv.c, LANES), 1) // cv.o
        for kz in range(3):
            for j in range(cv.tiles):
                tile = None
                for g in range(cv.per):
                    t = j * cv.per + g
                    if t < 9:
                        v = turned[pl.ds(9 * kz + t, cv.c, stride=27)]
                        tile = v if tile is None else jnp.where(group == g, v, tile)
                tile = tile.astype(BF16)
                wt[kz, :, j * LANES : (j + 1) * LANES] = tile.astype(wt.dtype)
                wide_ref[kz * cv.c : (kz + 1) * cv.c, j * LANES : (j + 1) * LANES] = tile.astype(F32)
        rows = -(-3 * cv.c // LANES) * LANES
        for i in range(rows // LANES):
            v = jnp.transpose(wide_ref[i * LANES : (i + 1) * LANES, 0 : cv.wide])
            size = min(LANES, 3 * cv.c - i * LANES)
            wf[:, i * LANES : i * LANES + size] = v[0 : 9 * cv.o, 0:size].astype(BF16)

    def weight_parts(k):
        cv, wt = convs[k], (wt1, wt2, wt3, wt4)[k]
        into = ((wx1,), (wx2,), (wx3u, wx3g), (wx4,))[k]
        parts = []
        for b, (size, start) in enumerate(cv.blocks):
            for t in range(1, nc):
                to, source = lax.rem(me + t, nc), lax.rem(me + nc - t, nc)
                at = start(to)
                sems = (w_send.at[k, b, t], w_recv.at[k, b, t])
                out = lambda b=b, at=at, size=size, to=to, sems=sems: peer_copy(
                    wt.at[:, pl.ds(at, size)], into[b].at[me], *sems, place, to
                )
                back = lambda b=b, source=source, sems=sems: peer_copy(
                    into[b].at[source], into[b].at[source], *sems, place, source
                )
                parts.append((out, back))
        return parts

    def weights_start(k):
        cv, wt = convs[k], (wt1, wt2, wt3, wt4)[k]
        into = ((wx1,), (wx2,), (wx3u, wx3g), (wx4,))[k]
        for b, (size, start) in enumerate(cv.blocks):
            into[b][me] = wt[:, pl.ds(start(me), size)]
        for out, _ in weight_parts(k):
            out().start()
            pending.append((None, lambda out=out: out().wait_send()))

    def weights_finish(k):
        cv = convs[k]
        into = ((wx1,), (wx2,), (wx3u, wx3g), (wx4,))[k]
        out = (wb1, wb2, wb3, wb4)[k]
        every = sum(size for size, _ in cv.blocks)
        offset = 0
        for _, back in weight_parts(k):
            back().wait_recv()
        for b, (size, _) in enumerate(cv.blocks):
            for t in range(9):
                pieces = [
                    into[b][j, 2 - kz, :, t * cv.o : (t + 1) * cv.o].astype(F32)
                    for kz in range(3)
                    for j in range(nc)
                ]
                at = (8 - t) * every + offset
                out[at : at + size] = jnp.concatenate(pieces, 1).astype(BF16)
            offset += size

    def reduce_copy(k, t):
        cv, gt, gr = convs[k], (gt1, gt2, gt3, gt4)[k], (gr1, gr2, gr3, gr4)[k]
        to = lax.rem(place + t, nd)
        return peer_copy(
            gt.at[pl.ds(to * cv.share, cv.share)], gr.at[place], r_send.at[k, t], r_recv.at[k, t], to, me
        )

    def reduce_start(k):
        cv, gt, gr = convs[k], (gt1, gt2, gt3, gt4)[k], (gr1, gr2, gr3, gr4)[k]

        def tile(i, carry):
            for j in range(cv.tiles):
                at = pl.multiple_of(i * 16, 16)
                gt[i * cv.tiles + j] = acc[pl.ds(at, 16), j * LANES : (j + 1) * LANES].astype(BF16)
            return carry

        lax.fori_loop(0, 3 * cv.c // 16, tile, 0, unroll=4)
        for i in range(cv.count, cv.share * nd):
            gt[i] = jnp.zeros((16, LANES), BF16)
        gr[place] = gt[pl.ds(place * cv.share, cv.share)]

        def send(t, _):
            reduce_copy(k, t).start()
            return _

        def sent(t, _):
            reduce_copy(k, t).wait_send()
            return _

        lax.fori_loop(1, nd, send, 0)
        pending.append((None, lambda: lax.fori_loop(1, nd, sent, 0)))

    def share_copy(k, t):
        cv, ga = convs[k], (ga1, ga2, ga3, ga4)[k]
        own = ga.at[pl.ds(place * cv.share, cv.share)]
        return peer_copy(own, own, a_send.at[k, t], a_recv.at[k, t], lax.rem(place + t, nd), me)

    def reduce_finish(k):
        cv, gr, ga = convs[k], (gr1, gr2, gr3, gr4)[k], (ga1, ga2, ga3, ga4)[k]

        def receive(t, _):
            source = lax.rem(place + nd - t, nd)
            peer_copy(gr.at[source], gr.at[source], r_send.at[k, t], r_recv.at[k, t], source, me).wait_recv()
            return _

        lax.fori_loop(1, nd, receive, 0)
        ga[pl.ds(place * cv.share, cv.share)] = jnp.sum(gr[...].astype(F32), axis=0).astype(BF16)

        def send(t, _):
            share_copy(k, t).start()
            return _

        def sent(t, _):
            share_copy(k, t).wait_send()
            return _

        lax.fori_loop(1, nd, send, 0)
        pending.append((None, lambda: lax.fori_loop(1, nd, sent, 0)))

    def gradient_out(k):
        cv, ga, out = convs[k], (ga1, ga2, ga3, ga4)[k], (g1, g2, g3, g4)[k]

        def receive(t, _):
            source = lax.rem(place + nd - t, nd)
            theirs = ga.at[pl.ds(source * cv.share, cv.share)]
            peer_copy(theirs, theirs, a_send.at[k, t], a_recv.at[k, t], source, me).wait_recv()
            return _

        lax.fori_loop(1, nd, receive, 0)
        group = iota((16, LANES), 1) // cv.o

        def scatter(i, carry):
            for kz in range(3):
                for j in range(cv.tiles):
                    v = ga[(kz * (cv.c // 16) + i) * cv.tiles + j].astype(F32)
                    for g in range(cv.per):
                        t = j * cv.per + g
                        if t < 9:
                            turned[pl.ds(9 * kz + t + i * (16 * 27), 16, stride=27)] = jnp.where(group == g, v, 0.0)
            return carry

        lax.fori_loop(0, cv.c // 16, scatter, 0, unroll=2)

        def chunk(at):
            v = jnp.transpose(turned[pl.ds(at, LANES)])
            return jnp.sum(v.reshape(cv.per, cv.o, LANES), axis=0)

        full = cv.length // LANES

        def body(i, carry):
            at = pl.multiple_of(i * LANES, LANES)
            out[:, pl.ds(at, LANES)] = chunk(at)
            return carry

        lax.fori_loop(0, full, body, 0, unroll=4)
        if full < cv.chunks:
            out[:, full * LANES :] = chunk(full * LANES)[:, 0 : cv.length - full * LANES]

    def column(row):
        n = row.shape[1]
        eye = iota((n, n), 0) == iota((n, n), 1)
        return jnp.sum(jnp.where(eye, row, 0.0), axis=1, keepdims=True)

    def row_of(col):
        n = col.shape[0]
        eye = iota((n, n), 0) == iota((n, n), 1)
        return jnp.sum(jnp.where(eye, col, 0.0), axis=0, keepdims=True)

    def clear_edges(ref):
        n = ref.shape[0]
        blank = jnp.zeros(ref.shape[2:], ref.dtype)

        for s in range(n):
            ref[s, 0] = blank
            ref[s, ref.shape[1] - 1] = blank

    def clear_halos(ref):
        def clear(s):
            ref[s] = jnp.zeros(ref.shape[1:], ref.dtype)

        pl.when(first)(lambda: clear(0))
        pl.when(last)(lambda: clear(ref.shape[0] - 1))

    def conv(ref, weight, slices, rows, m, n, width, emit, init, which=None):
        per = rows // n

        def body(i, carry):
            if which is not None:
                pl.when(i == (slices - 1) * per - 1)(lambda: gather_pass(ref, which, 1, (2,)))
                pl.when(i == (slices - 1) * per)(lambda: gather_wait(ref, which, 1, (2,)))
            d = i // per
            r0 = (i - d * per) * n
            x = jnp.concatenate(
                [
                    jnp.concatenate([flat(ref, d + kz, r0 + j) for j in range(n + 2)], 1)
                    for kz in range(3)
                ],
                0,
            )
            y = dot(weight[...], x)
            results = []
            for j in range(n):
                acc = []
                for kx in range(3):
                    terms = [
                        y[(3 * ky + kx) * m : (3 * ky + kx + 1) * m, (j + ky) * LANES : (j + ky + 1) * LANES]
                        for ky in range(3)
                    ]
                    acc.append(terms[0] + terms[1] + terms[2])
                results.append(from_left(acc[0], width) + acc[1] + from_right(acc[2], width))
            return emit(d, r0, results, carry)

        return lax.fori_loop(0, slices * per, body, init)

    def weight_grad(ref, dz, k, slices, rows, n):
        per = rows // n
        cv = convs[k]
        acc[0 : 3 * cv.c, 0 : cv.wide] = jnp.zeros((3 * cv.c, cv.wide), F32)

        def body(i, carry):
            d = i // per
            r0 = (i - d * per) * n
            x = jnp.concatenate(
                [
                    jnp.concatenate([flat(ref, d + kz, r0 + 1 + j) for j in range(n)], 1)
                    for kz in range(3)
                ],
                0,
            )
            y = jnp.concatenate(
                [
                    jnp.concatenate([dz[kx, d, r0 + j + 2 - ky] for j in range(n)], 1)
                    for ky in range(3)
                    for kx in range(3)
                ],
                0,
            ).astype(BF16)
            acc[0 : 3 * cv.c, 0 : 9 * cv.o] += dot_nt(x, y)
            return carry

        lax.fori_loop(0, slices * per, body, 0)

    def conv_coarse(ref, weight, m):
        x = jnp.concatenate(
            [jnp.concatenate([flat(ref, kz, i) for i in range(Q)], 1) for kz in range(3)], 0
        )
        y = dot(weight[...], x)
        blank = jnp.zeros((m, LANES), F32)

        def shifted(ky, i):
            if not 0 <= i < Q:
                return blank
            a, b, c = (
                y[(3 * ky + kx) * m : (3 * ky + kx + 1) * m, i * LANES : (i + 1) * LANES] for kx in range(3)
            )
            return from_left(a, V) + b + from_right(c, V)

        before = [shifted(0, i) for i in range(-1, Q)]
        after = [shifted(2, i) for i in range(Q + 1)]
        return [
            shifted(1, i) + halves(before[i + 1] + after[i + 1], before[i] + after[i]) for i in range(Q)
        ]

    def conv_stats_coarse(ref, weight, z, m):
        total = square = jnp.zeros((m, LANES), F32)
        for i, v in enumerate(conv_coarse(ref, weight, m)):
            z[i] = v
            total, square = total + v, square + v * v
        return pack(total, square)

    def weight_grad_coarse(ref, k):
        cv = convs[k]
        x = jnp.concatenate(
            [jnp.concatenate([flat(ref, kz, i) for i in range(Q)], 1) for kz in range(3)], 0
        )
        y = jnp.concatenate([jnp.concatenate([dzc[t, i] for i in range(Q)], 1) for t in range(9)], 0)
        acc[0 : 3 * cv.c, 0 : 9 * cv.o] = dot_nt(x, y.astype(BF16))

    def norm_back_coarse(z, du, stats, norm, total, x):
        mean, inv = stats
        scale = norm[0] * inv
        a = total[0] / dm.coarse_total
        b = total[1] / dm.coarse_total
        rows = []
        for i in range(Q):
            v = scale * (du[i] - a - (z[i] - mean) * inv * b)
            low = v.astype(BF16)
            x[1, i, me] = low.astype(x.dtype)
            rows.append(low.astype(F32))
        blank = jnp.zeros_like(rows[0])
        rows = [blank] + rows + [blank]
        for i in range(Q):
            before, here, after = rows[i : i + 3]
            for ky, v in enumerate((halves(after, here), here, halves(here, before))):
                for kx, u in enumerate((from_right(v, V), v, from_left(v, V))):
                    dzc[3 * ky + kx, i] = u.astype(dzc.dtype)

    def conv_stats(ref, weight, z, slices, rows, m, n, width, which=None):
        def emit(d, r0, results, carry):
            total, square = carry
            for j, v in enumerate(results):
                z[d * rows + r0 + j] = v
                total, square = total + v, square + v * v
            return total, square

        blank = jnp.zeros((m, LANES), F32)
        total, square = conv(ref, weight, slices, rows, m, n, width, emit, (blank, blank), which)
        return pack(total, square)

    def pack(a, b):
        m = a.shape[0]
        a = jnp.sum(a, axis=1, keepdims=True)
        b = jnp.sum(b, axis=1, keepdims=True)
        lane, channel = iota((m, LANES), 1), iota((m, LANES), 0)
        both = jnp.where(lane == channel, a, jnp.where(lane == channel + m, b, 0.0))
        return jnp.sum(both, axis=0, keepdims=True)

    def moments(total, count):
        mean = total[0] / count
        var = total[1] / count - mean * mean
        return mean, lax.rsqrt(var + EPS)

    def norm_apply(z, mean, inv, gain, shift):
        xhat = (z - mean) * inv
        u = gain * xhat + shift
        return xhat, u, jax.nn.sigmoid(u)

    def norm_rows(z, stats, norm, emit, n):
        mean, inv = stats
        gain, shift = norm

        def body(i, carry):
            for j in range(n):
                p = i * n + j
                _, u, sigma = norm_apply(z[p], mean, inv, gain, shift)
                emit(p, u * sigma)
            return carry

        lax.fori_loop(0, z.shape[0] // n, body, 0)

    def norm_back_sums(z, du, stats, norm, grad, n):
        mean, inv = stats
        gain, shift = norm
        m = z.shape[1]

        def body(i, carry):
            a, b = carry
            for j in range(n):
                p = i * n + j
                xhat, u, sigma = norm_apply(z[p], mean, inv, gain, shift)
                v = grad(p) * sigma * (1.0 + u * (1.0 - sigma))
                du[p] = v
                a, b = a + v, b + v * xhat
            return a, b

        blank = jnp.zeros((m, LANES), F32)
        return pack(*lax.fori_loop(0, z.shape[0] // n, body, (blank, blank)))

    def norm_back(z, du, stats, norm, total, count, x, dz, rows, width, n):
        mean, inv = stats
        gain, _ = norm
        scale = gain * inv
        a = total[0] / count
        b = total[1] / count
        per = rows // n

        def body(i, carry):
            d = i // per
            r0 = (i - d * per) * n
            for j in range(n):
                p = i * n + j
                xhat = (z[p] - mean) * inv
                v = scale * (du[p] - a - xhat * b)
                low = v.astype(BF16)
                x[1 + d, 1 + r0 + j, me] = low.astype(x.dtype)
                v = low.astype(F32)
                dz[0, d, 1 + r0 + j] = from_right(v, width).astype(dz.dtype)
                dz[1, d, 1 + r0 + j] = low.astype(dz.dtype)
                dz[2, d, 1 + r0 + j] = from_left(v, width).astype(dz.dtype)
            return carry

        lax.fori_loop(0, z.shape[0] // n, body, 0)

    hc = iota((LANES, LANES), 0)
    fc = iota((LANES, LANES), 1)
    half = LANES // 2

    def up_table(coarse, fine):
        base = fine // 2
        other = jnp.clip(base + jnp.where(fine % 2 == 0, -1, 1), 0, V - 1)
        near = (coarse == base).astype(F32)
        far = (coarse == other).astype(F32)
        return (0.75 * near + 0.25 * far).astype(BF16)

    pool = jnp.concatenate([(hc // 2 == fc - at).astype(BF16) for at in (0, half)], 0)
    spread = jnp.concatenate([(hc - at == fc // 2).astype(BF16) for at in (0, half)], 1)
    up = jnp.concatenate([up_table(hc - at, fc) for at in (0, half)], 1)
    down = jnp.concatenate([up_table(fc - at, hc) for at in (0, 0, half, half)], 0)
    spread2 = jnp.concatenate([spread, spread], 0)

    def take_rows(ref):
        for c in range(dm.cs):
            rows_ref[c * S * R : (c + 1) * S * R] = ref[c].astype(F32).reshape(S * R, LANES)

    def row(p):
        return rows_ref[pl.ds(p, dm.cs, stride=S * R)]

    barrier = pltpu.get_barrier_semaphore()

    def greet(depth, chan):
        pl.semaphore_signal(barrier, inc=1, device_id={"depth": depth, "chan": chan}, device_id_type=MESH)

    for t in range(1, nc):
        greet(place, lax.rem(me + t, nc))

    def greet_slab(t, _):
        greet(lax.rem(place + t, nd), me)
        return _

    lax.fori_loop(1, nd, greet_slab, 0)
    for t in range(1, nc // 2):
        to = lax.rem(me + 2 * t, nc)
        pl.when(jnp.logical_not(first))(lambda to=to: greet(place - 1, to))
        pl.when(jnp.logical_not(last))(lambda to=to: greet(place + 1, to))
    clear_halos(xp)
    take_rows(skip_ref)

    def take_skip(i, carry):
        parts = []
        for s in range(S):
            v = [row(s * R + 4 * i + j).astype(BF16) for j in range(4)]
            for j in range(4):
                xs[1 + s, 4 * i + j, me] = v[j].astype(xs.dtype)
            parts += [jnp.concatenate([v[j], v[2 + j]], 1) for j in range(2)]
        v = dot(jnp.concatenate(parts, 0), pool).reshape(2 * S, dm.cs, LANES)
        xp[1, i, me] = (jnp.sum(v, axis=0) * 0.125).astype(BF16).astype(xp.dtype)
        return carry

    lax.fori_loop(0, Q, take_skip, 0, unroll=3)
    clear_halos(xs)
    beside = jnp.where(first, 0, 1) + jnp.where(last, 0, 1)
    pl.semaphore_wait(barrier, nc - 1 + nd - 1 + (nc // 2 - 1) * beside)
    gather_start(xp, "pooled", 0)
    gather_start(xs, "skip", 0)

    gq = dm.g // nc
    gate_all[me, :, 0 : gate_ref.shape[1]] = gate_ref[...]
    lane = iota((gq, LANES), 1)
    gate_all[me, :, 2 * LANES :] = jnp.where(
        lane == 0, column(vector_ref[0:1]), jnp.where(lane == 1, column(vector_ref[1:2]), 0.0)
    )
    for t in range(1, nc):
        to, source = lax.rem(me + t, nc), lax.rem(me + nc - t, nc)
        out = peer_copy(gate_all.at[me], gate_all.at[me], v_send.at[t], v_recv.at[t], place, to)
        out.start()
        pending.append((None, out.wait_send))

    prepare(0)
    for ref in (xd, d1, xz4, xz3):
        clear_edges(ref)
    for ref in (xh, xd, xz4, xz3, xz2, xz1):
        clear_halos(ref)
    for kx in range(3):
        for s in range(S):
            dzf[kx, s, 0] = jnp.zeros(dzf.shape[3:], dzf.dtype)
            dzf[kx, s, R + 1] = jnp.zeros(dzf.shape[3:], dzf.dtype)

    def norm_of(ref, layer):
        return column(ref[0, layer : layer + 1]), column(ref[1, layer : layer + 1])

    norm_e1, norm_e2 = norm_of(en_ref, 0), norm_of(en_ref, 1)
    norm_d1, norm_d2 = norm_of(dn_ref, 0), norm_of(dn_ref, 1)

    gather_pass(xp, "pooled", 0)
    gather_wait(xp, "pooled", 0)
    sum_start(st, 0, 0, conv_stats_coarse(xp, wf1, z1, dm.ce))
    prepare(3)
    stats_e1 = moments(totals(0, 0, dm.ce), dm.coarse_total)

    def keep_hidden(p, v):
        xh[1, p, me] = v.astype(BF16).astype(xh.dtype)

    norm_rows(z1, stats_e1, norm_e1, keep_hidden, 3)
    gather_start(xh, "hidden", 0)
    prepare(1)
    gather_pass(xh, "hidden", 0)
    gather_pass(xs, "skip", 0)
    gather_wait(xh, "hidden", 0)
    sum_start(st, 1, 1, conv_stats_coarse(xh, wf2, z2, dm.ce))
    stats_e2 = moments(totals(1, 1, dm.ce), dm.coarse_total)

    def keep_coarse(p, v):
        xc[1, p, me] = v.astype(BF16).astype(xc.dtype)

    norm_rows(z2, stats_e2, norm_e2, keep_coarse, 3)
    gather_start(xc, "coarse", 0)
    prepare(2)
    for t in range(1, nc):
        source = lax.rem(me + nc - t, nc)
        peer_copy(
            gate_all.at[source], gate_all.at[source], v_send.at[t], v_recv.at[t], place, source
        ).wait_recv()
    gate_full = gate_all[...].reshape(dm.g, 3 * LANES)
    wg = gate_full[:, 0 : dm.enc_all + dm.skip_all].astype(BF16)
    gbias = gate_full[:, 2 * LANES : 2 * LANES + 1]
    gout = gate_full[:, 2 * LANES + 1 : 2 * LANES + 2]
    gate_t[...] = jnp.transpose(gate_full[:, 0 : 2 * LANES])
    gate_own[...] = jnp.concatenate(
        [
            gate_t[pl.ds(pl.multiple_of(me * dm.ce, dm.ce), dm.ce)],
            gate_t[pl.ds(pl.multiple_of(dm.enc_all + me * dm.cs, dm.cs), dm.cs)],
        ],
        0,
    )
    gather_pass(xc, "coarse", 0)
    gather_wait(xc, "coarse", 0)
    for k in (3, 2, 1, 0):
        weights_start(k)

    def up_depth(i, carry):
        t = []
        for s in range(3):
            v = dot(flat(xc, s, i), up)
            t.append(jnp.stack([v[:, 0:LANES], v[:, LANES:]], 0))
        below = jnp.where(first, t[1], t[0])
        above = jnp.where(last, t[1], t[2])
        near = 0.75 * t[1]
        here = 0.25 * t[1]
        rows = pl.ds(i * 2, 2)
        dt[0, rows] = jnp.where(first, 0.0, 0.75 * below + here)
        dt[1, rows] = near + 0.25 * below
        dt[2, rows] = near + 0.25 * above
        dt[3, rows] = jnp.where(last, 0.0, 0.75 * above + here)
        return carry

    lax.fori_loop(0, Q, up_depth, 0)

    def up_rows(i, carry):
        before, after = jnp.maximum(i - 1, 0), jnp.minimum(i + 1, H - 1)
        for s in range(S + 2):
            v = 0.75 * dt[s, i]
            d1[s, 1 + 2 * i, 0 : dm.enc_all] = (v + 0.25 * dt[s, before]).astype(BF16)
            d1[s, 2 + 2 * i, 0 : dm.enc_all] = (v + 0.25 * dt[s, after]).astype(BF16)
        return carry

    lax.fori_loop(0, H, up_rows, 0)

    gather_wait(xs, "skip", 0)
    gate_n = 12

    def gate(i, carry):
        s = i // (R // gate_n)
        r0 = (i - s * (R // gate_n)) * gate_n
        skips = [flat(xs, s, r0 + j) for j in range(gate_n)]
        x = jnp.concatenate(
            [
                jnp.concatenate([d1[s, 1 + r0 + j, 0 : dm.enc_all] for j in range(gate_n)], 1),
                jnp.concatenate(skips, 1),
            ],
            0,
        )
        pre = dot(wg, x) + gbias
        act = pre * jax.nn.sigmoid(pre)
        alpha = jax.nn.sigmoid(jnp.sum(gout * act, axis=0, keepdims=True))
        for j in range(gate_n):
            lanes = slice(j * LANES, (j + 1) * LANES)
            d1[s, 1 + r0 + j, dm.enc_all :] = (alpha[:, lanes] * skips[j].astype(F32)).astype(BF16)
            pre_ref[s, r0 + j] = pre[:, lanes]
            al_ref[s, r0 + j] = alpha[:, lanes]
        return carry

    lax.fori_loop(0, (S + 2) * R // gate_n, gate, 0)

    sum_start(st, 4, 4, conv_stats(d1, wf3, z3, S, R, dm.cd, 12, W))
    weights_finish(3)
    stats_d1 = moments(totals(4, 4, dm.cd), dm.fine_total)

    def keep_dec(p, v):
        s = p // R
        xd[1 + s, 1 + p - s * R, me] = v.astype(BF16).astype(xd.dtype)

    norm_rows(z3, stats_d1, norm_d1, keep_dec, 8)
    gather_start(xd, "dhidden", 1)
    weights_finish(2)
    take_rows(cot_ref)
    gather_pass(xd, "dhidden", 1, (1, 0))
    gather_wait(xd, "dhidden", 1, (1, 0))
    sum_start(st, 5, 5, conv_stats(xd, wf4, z4, S, R, dm.cd, 12, W, "dhidden"))
    weights_finish(1)
    stats_d2 = moments(totals(5, 5, dm.cd), dm.fine_total)

    sum_start(st, 6, 6, norm_back_sums(z4, du_f, stats_d2, norm_d2, row, 8))

    def keep_result(p, v):
        out_ref[pl.ds(pl.multiple_of(p * dm.cd, dm.cd), dm.cd)] = v

    norm_rows(z4, stats_d2, norm_d2, keep_result, 8)
    total_d2 = totals(6, 6, dm.cd)
    norm_back(z4, du_f, stats_d2, norm_d2, total_d2, dm.fine_total, xz4, dzf, R, W, 8)
    gather_start(xz4, "dz4", 1)
    weight_grad(xd, dzf, 3, S, R, 12)
    reduce_start(3)
    weights_finish(0)
    gather_pass(xz4, "dz4", 1, (1, 0))
    gather_wait(xz4, "dz4", 1, (1, 0))

    def keep_grad(d, r0, results, carry):
        for j, v in enumerate(results):
            gg[d * R + r0 + j] = v
        return carry

    conv(xz4, wb4, S, R, dm.cd, 12, W, keep_grad, 0, "dz4")
    sum_start(st, 7, 7, norm_back_sums(z3, du_f, stats_d1, norm_d1, lambda p: gg[p], 8))
    total_d1 = totals(7, 7, dm.cd)
    norm_back(z3, du_f, stats_d1, norm_d1, total_d1, dm.fine_total, xz3, dzf, R, W, 8)
    gather_start(xz3, "dz3", 1)
    weight_grad(d1, dzf, 2, S, R, 12)
    reduce_finish(3)
    gather_pass(xz3, "dz3", 1, (1, 0))
    reduce_start(2)
    gather_wait(xz3, "dz3", 1, (1, 0))

    def gate_back(d, r0, results, carry):
        bias, psi = carry
        lows = []
        for j, both in enumerate(results):
            s, r = d + 1, r0 + j
            ug_ref[d * R + r] = both[0 : dm.ce]
            v = both[dm.ce :]
            grad = jnp.sum(v * flat(xs, s, r).astype(F32), axis=0, keepdims=True)
            alpha = al_ref[s, r]
            logit = grad * alpha * (1.0 - alpha)
            pre = pre_ref[s, r]
            sigma = jax.nn.sigmoid(pre)
            psi = psi + pre * sigma * logit
            low = (logit * gout * sigma * (1.0 + pre * (1.0 - sigma))).astype(BF16)
            bias = bias + low.astype(F32)
            pg_ref[d * R + r] = low
            lows.append(low)
            for t in range(nc):
                gg[t] = v[t * dm.cs : (t + 1) * dm.cs]
            sg_at = pl.ds(pl.multiple_of((d * R + r) * dm.cs, dm.cs), dm.cs)
            sg_ref[sg_at] = alpha * gg[me]
        back = dot(gate_own[...].astype(BF16), jnp.concatenate(lows, 1))
        for j in range(len(results)):
            lanes = slice(j * LANES, (j + 1) * LANES)
            ug_ref[d * R + r0 + j] += back[0 : dm.ce, lanes]
            sg_at = pl.ds(pl.multiple_of((d * R + r0 + j) * dm.cs, dm.cs), dm.cs)
            sg_ref[sg_at] += back[dm.ce :, lanes]
        return bias, psi

    blank = jnp.zeros((dm.g, LANES), F32)
    bias, psi = conv(
        xz3, wb3, S, R, dm.ce + dm.skip_all, 8, W, gate_back, (blank, blank), "dz3"
    )

    def down_rows(i, carry):
        terms = []
        for s in range(S):
            pair = []
            for j in range(2):
                r = i * 2 + j
                near = ug_ref[s * R + 2 * r] + ug_ref[s * R + 2 * r + 1]
                far = ug_ref[s * R + jnp.minimum(2 * r + 2, R - 1)] + ug_ref[s * R + jnp.maximum(2 * r - 1, 0)]
                pair.append(split(0.75 * near + 0.25 * far))
            terms.append(jnp.concatenate(pair, 1))
        v = dot(jnp.concatenate(terms, 0), down)
        even, odd = v[0 : dm.ce], v[dm.ce :]
        fs[0, i] = 0.25 * even
        fs[1, i] = 0.25 * odd
        cg[i] = 0.75 * (even + odd) + jnp.where(first, 0.25 * even, 0.0) + jnp.where(last, 0.25 * odd, 0.0)
        return carry

    lax.fori_loop(0, Q, down_rows, 0)

    def fold(side, step):
        return peer_copy(fs.at[side], fr.at[1 - side], f_send.at[side], f_recv.at[1 - side], place + step, me)

    pl.when(jnp.logical_not(first))(lambda: fold(0, -1).start())
    pl.when(jnp.logical_not(last))(lambda: fold(1, 1).start())
    pending.append((jnp.logical_not(first), lambda: fold(0, -1).wait_send()))
    pending.append((jnp.logical_not(last), lambda: fold(1, 1).wait_send()))
    reduce_finish(2)

    def fold_in(side):
        peer_copy(fs.at[side], fr.at[side], f_send.at[side], f_recv.at[side], place, me).wait_recv()
        cg[...] += fr[side]

    pl.when(jnp.logical_not(first))(lambda: fold_in(0))
    pl.when(jnp.logical_not(last))(lambda: fold_in(1))

    sum_start(st, 2, 2, norm_back_sums(z2, du_c, stats_e2, norm_e2, lambda p: cg[p], 3))

    columns = gate_ref.shape[1]
    acc[0 : dm.g, 0:columns] = jnp.zeros((dm.g, columns), F32)

    weight_n = 12

    def gate_weight(i, carry):
        d = i // (R // weight_n)
        r0 = (i - d * (R // weight_n)) * weight_n
        x = jnp.concatenate(
            [
                jnp.concatenate([d1[1 + d, 1 + r0 + j, 0 : dm.enc_all] for j in range(weight_n)], 1),
                jnp.concatenate([flat(xs, 1 + d, r0 + j) for j in range(weight_n)], 1),
            ],
            0,
        )
        y = jnp.concatenate([pg_ref[d * R + r0 + j] for j in range(weight_n)], 1)
        acc[0 : dm.g, 0:columns] += dot_nt(y, x)
        return carry

    lax.fori_loop(0, S * R // weight_n, gate_weight, 0)
    lane = iota((dm.g, LANES), 1)
    vectors = jnp.where(
        lane == 0,
        jnp.sum(bias, axis=1, keepdims=True),
        jnp.where(lane == 1, jnp.sum(psi, axis=1, keepdims=True), 0.0),
    )
    for j in range(nc):
        mine = slice(j * gq, (j + 1) * gq)
        gate_block[j, :, 0:columns] = acc[mine, 0:columns]
        gate_block[j, :, columns : 2 * LANES] = jnp.zeros((gq, 2 * LANES - columns), F32)
        gate_block[j, :, 2 * LANES :] = vectors[mine]
    sum_start(st_g, 8, 0, gate_block[me])
    gradient_out(3)
    total_e2 = totals(2, 2, dm.ce)
    norm_back_coarse(z2, du_c, stats_e2, norm_e2, total_e2, xz2)
    gather_start(xz2, "dz2", 0)
    weight_grad_coarse(xh, 1)
    reduce_start(1)
    gather_pass(xz2, "dz2", 0)
    gradient_out(2)
    gather_wait(xz2, "dz2", 0)
    for i, v in enumerate(conv_coarse(xz2, wb2, dm.ce)):
        cg[i] = v
    sum_start(st, 3, 3, norm_back_sums(z1, du_c, stats_e1, norm_e1, lambda p: cg[p], 3))
    reduce_finish(1)
    total_e1 = totals(3, 3, dm.ce)
    norm_back_coarse(z1, du_c, stats_e1, norm_e1, total_e1, xz1)
    gather_start(xz1, "dz1", 0)
    weight_grad_coarse(xp, 0)
    reduce_start(0)
    gather_pass(xz1, "dz1", 0)
    gradient_out(1)
    reduce_finish(0)
    gather_wait(xz1, "dz1", 0)
    for i, v in enumerate(conv_coarse(xz1, wb1, dm.cs)):
        v = dot(split(v), spread2) * 0.125
        for j in range(4):
            part = v[:, (j // 2) * LANES : (j // 2 + 1) * LANES]
            for s in range(S):
                at = (s * R + 4 * i + j) * dm.cs
                sg_ref[at : at + dm.cs] += part
    gate_total = sum_finish(st_g, 8, 0)
    ggate[...] = gate_total[:, 0:columns]
    gvector[0:1] = row_of(gate_total[:, 2 * LANES : 2 * LANES + 1])
    gvector[1:2] = row_of(gate_total[:, 2 * LANES + 1 : 2 * LANES + 2])
    for ref, sums in ((gen, (total_e1, total_e2)), (gdn, (total_d1, total_d2))):
        for layer, total in enumerate(sums):
            ref[0, layer : layer + 1] = row_of(total[1])
            ref[1, layer : layer + 1] = row_of(total[0])
    gradient_out(0)
    for cond, fn in pending:
        guarded(cond, fn)


def adamw(weight, grad, moment, square, rate):
    new_moment = 0.9 * moment + 0.1 * grad
    new_square = 0.999 * square + 0.001 * grad * grad
    moment_hat = new_moment / (1.0 - 0.9**STEP)
    square_hat = new_square / (1.0 - 0.999**STEP)
    new_weight = weight - rate * (moment_hat / (jnp.sqrt(square_hat) + 1e-08) + 0.01 * weight)
    return (new_weight, new_moment, new_square)


RATES = (CONV_RATE, CONV_RATE, GATE_RATE, VECTOR_RATE, CONV_RATE, CONV_RATE, VECTOR_RATE, VECTOR_RATE)


def update_kernel(*refs):
    n = len(RATES)
    sources, targets = refs[: 2 + 4 * n], refs[2 + 4 * n : 4 + 7 * n]
    inside, outside = refs[4 + 7 * n : 6 + 11 * n], refs[6 + 11 * n : 8 + 14 * n]
    in_sem, out_sem = refs[8 + 14 * n :]
    order = (4, 1, 0, 5, 2, 3, 6, 7)

    def load(i):
        return pltpu.make_async_copy(sources[i], inside[i], in_sem.at[i])

    def store(i):
        return pltpu.make_async_copy(outside[i], targets[i], out_sem.at[i])

    for i in (1, 0):
        load(i).start()
    for k in order:
        for part in range(4):
            load(2 + part * n + k).start()
    for i in (1, 0):
        load(i).wait()
        chans, (slabs, rows) = outside[i].shape[0], outside[i].shape[1:3]
        for c in range(chans):
            v = inside[i][pl.ds(c, slabs * rows, stride=chans)]
            outside[i][c] = v.reshape(slabs, rows, LANES).astype(outside[i].dtype)
        store(i).start()
    for k in order:
        own = [2 + part * n + k for part in range(4)]
        for i in own:
            load(i).wait()
        rows = inside[own[0]].shape[0]
        step = 8 if rows % 8 == 0 and rows > 8 else rows
        for r in range(0, rows, step):
            at = slice(r, r + step)
            new = adamw(*(inside[i][at] for i in own), RATES[k])
            for part, value in enumerate(new):
                outside[2 + 3 * k + part][at] = value
        for part in range(3):
            store(2 + 3 * k + part).start()
    for i in range(len(targets)):
        store(i).wait()


def per_device(
    skip, cotangent, enc_conv1, enc_conv2, gate_proj, gate_vector, dec_conv1, dec_conv2, enc_norms, dec_norms, *states
):
    nd, nc = lax.axis_size("depth"), lax.axis_size("chan")
    dm = Dims(nd, nc, skip.shape, enc_conv1.shape[0], dec_conv1.shape[0], gate_proj.shape[0] * nc)
    S, R, H = dm.s, dm.rows, dm.half
    cin3 = dm.enc_all + dm.skip_all

    def block_of(size):
        return (size, lambda j: pl.multiple_of(j * size, size))

    dm.convs = convs = (
        Conv(dm, dm.ce, dm.skip_all, (block_of(dm.cs),)),
        Conv(dm, dm.ce, dm.enc_all, (block_of(dm.ce),)),
        Conv(dm, dm.cd, cin3, (block_of(dm.ce), (dm.skip_all, lambda j: dm.enc_all))),
        Conv(dm, dm.cd, dm.dec_all, (block_of(dm.cd),)),
    )
    params = (enc_conv1, enc_conv2, gate_proj, gate_vector, dec_conv1, dec_conv2, enc_norms, dec_norms)
    inputs = (
        skip, cotangent, enc_conv1, enc_conv2, dec_conv1, dec_conv2, gate_proj, gate_vector, enc_norms, dec_norms
    )
    shape = jax.ShapeDtypeStruct
    outs = (
        shape((S * R * dm.cd, LANES), F32),
        shape((S * R * dm.cs, LANES), F32),
        *(shape(a.shape, F32) for a in (enc_conv1, enc_conv2, dec_conv1, dec_conv2)),
        *(shape(a.shape, F32) for a in (gate_proj, gate_vector, enc_norms, dec_norms)),
    )

    def ext(slices, rows, block):
        return pltpu.VMEM((slices, rows, nc, block, LANES), storage(block))

    def exchange(cv):
        return [pltpu.VMEM((nc, 3, size, cv.wide), cv.kind) for size, _ in cv.blocks]

    def backward(cv):
        return [pltpu.VMEM((9 * sum(size for size, _ in cv.blocks), 3 * nc * cv.o), BF16)]

    gq = dm.g // nc
    Q = H // 2
    scratch = [
        ext(3, Q, dm.cs),
        ext(S + 2, R, dm.cs),
        ext(3, Q, dm.ce),
        ext(3, Q, dm.ce),
        pltpu.VMEM((S + 2, R + 2, cin3, LANES), BF16),
        ext(S + 2, R + 2, dm.cd),
        ext(S + 2, R + 2, dm.cd),
        ext(S + 2, R + 2, dm.cd),
        ext(3, Q, dm.ce),
        ext(3, Q, dm.ce),
        pltpu.VMEM((Q, dm.ce, LANES), F32),
        pltpu.VMEM((Q, dm.ce, LANES), F32),
        pltpu.VMEM((S * R, dm.cd, LANES), F32),
        pltpu.VMEM((S * R, dm.cd, LANES), F32),
        pltpu.VMEM((Q, dm.ce, LANES), F32),
        pltpu.VMEM((S * R, dm.cd, LANES), F32),
        pltpu.VMEM((S + 2, R, dm.g, LANES), F32),
        pltpu.VMEM((S + 2, R, 1, LANES), F32),
        pltpu.VMEM((S * R, dm.g, LANES), BF16),
        pltpu.VMEM((S * R, dm.ce, LANES), F32),
        pltpu.VMEM((S + 2, H, dm.enc_all, LANES), F32),
        pltpu.VMEM((S * R, dm.cd, LANES), F32),
        pltpu.VMEM((Q, dm.ce, LANES), F32),
        pltpu.VMEM((3, S, R + 2, dm.cd, LANES), storage(dm.cd)),
        pltpu.VMEM((9, Q, dm.ce, LANES), BF16),
        pltpu.VMEM((2, Q, dm.ce, LANES), F32),
        pltpu.VMEM((2, Q, dm.ce, LANES), F32),
        pltpu.VMEM((8, nd, 1, LANES), F32),
        pltpu.VMEM((1, nd, gq, 3 * LANES), F32),
        pltpu.VMEM((dm.cs * S * R, LANES), F32),
        pltpu.VMEM((max(cv.chunks for cv in convs) * LANES, LANES), F32),
        pltpu.VMEM((max(-(-3 * cv.c // LANES) for cv in convs) * LANES, max(cv.wide for cv in convs)), F32),
        pltpu.VMEM((max(3 * cv.c for cv in convs), max(cv.wide for cv in convs)), F32),
        pltpu.VMEM((nc, gq, 3 * LANES), F32),
        pltpu.VMEM((2 * LANES, dm.g), F32),
        pltpu.VMEM((dm.ce + dm.cs, dm.g), F32),
        pltpu.VMEM((nc, gq, 3 * LANES), F32),
        *(pltpu.VMEM((3, cv.c, cv.wide), cv.kind) for cv in convs),
        *(pltpu.VMEM((9 * cv.o, 3 * cv.c), BF16) for cv in convs),
        *(ref for cv in convs for ref in exchange(cv)),
        *(ref for cv in convs for ref in backward(cv)),
        *(pltpu.VMEM((cv.share * nd, 16, LANES), BF16) for cv in convs),
        *(pltpu.VMEM((nd, cv.share, 16, LANES), BF16) for cv in convs),
        *(pltpu.VMEM((cv.share * nd, 16, LANES), BF16) for cv in convs),
        *[pltpu.SemaphoreType.DMA((len(GATHERS), 2, 3 * nc // 2))] * 2,
        *[pltpu.SemaphoreType.DMA((9, nd))] * 2,
        *[pltpu.SemaphoreType.DMA((2,))] * 2,
        *[pltpu.SemaphoreType.DMA((4, 2, nc))] * 2,
        *[pltpu.SemaphoreType.DMA((nc,))] * 2,
        *[pltpu.SemaphoreType.DMA((4, nd))] * 4,
    ]
    vmem = pl.BlockSpec(memory_space=pltpu.VMEM)
    out, sg, grad1, grad2, grad3, grad4, ggate, gvector, gen, gdn = pl.pallas_call(
        functools.partial(kernel, dm),
        out_shape=outs,
        in_specs=[vmem] * len(inputs),
        out_specs=[vmem] * len(outs),
        scratch_shapes=scratch,
        compiler_params=pltpu.CompilerParams(
            has_side_effects=True, collective_id=0, vmem_limit_bytes=60 * 1024 * 1024
        ),
        name="step",
    )(*inputs)
    grads = (grad1, grad2, ggate, gvector, grad3, grad4, gen, gdn)
    operands = (out, sg, *params, *grads, *states)
    updated = (
        shape(cotangent.shape, BF16),
        shape(skip.shape, F32),
        *(shape(p.shape, F32) for p in params for _ in range(3)),
    )
    anywhere = pl.BlockSpec(memory_space=pl.ANY)
    return pl.pallas_call(
        update_kernel,
        out_shape=updated,
        in_specs=[anywhere] * len(operands),
        out_specs=[anywhere] * len(updated),
        scratch_shapes=[
            *(pltpu.VMEM(a.shape, a.dtype) for a in operands),
            *(pltpu.VMEM(a.shape, a.dtype) for a in updated),
            pltpu.SemaphoreType.DMA((len(operands),)),
            pltpu.SemaphoreType.DMA((len(updated),)),
        ],
        compiler_params=pltpu.CompilerParams(vmem_limit_bytes=60 * 1024 * 1024),
        name="update",
    )(*operands)


def solution(mesh):
    volume = P("chan", "depth", None, None)
    row, column, norms = P("chan", None), P(None, "chan"), P(None, None, "chan")
    params = (row, row, row, column, row, row, norms, norms)
    return jax.shard_map(
        per_device,
        mesh=mesh,
        in_specs=(volume, volume) + params * 3,
        out_specs=(volume, volume) + tuple(spec for spec in params for _ in range(3)),
        check_vma=False,
    )
```

```python
import functools

import jax
import jax.numpy as jnp
from jax import lax
from jax.experimental import pallas as pl
from jax.experimental.pallas import tpu as pltpu
from jax.sharding import PartitionSpec as P

STEP = 5
EPS = 1e-05
CONV_RATE = 0.03
GATE_RATE = 0.1
VECTOR_RATE = 0.5
LANES = 128
MESH = pl.DeviceIdType.MESH
F32 = jnp.float32
BF16 = jnp.bfloat16


def iota(shape, dim):
    return lax.broadcasted_iota(jnp.int32, shape, dim)


def dot(a, b):
    return jnp.dot(a, b, preferred_element_type=F32)


def dot_nt(a, b):
    return lax.dot_general(a, b, (((1,), (1,)), ((), ())), preferred_element_type=F32)


def from_left(v, width):
    return jnp.where(iota(v.shape, 1) % width == 0, 0.0, pltpu.roll(v, 1, 1))


def from_right(v, width):
    return jnp.where(iota(v.shape, 1) % width == width - 1, 0.0, pltpu.roll(v, LANES - 1, 1))


def halves(low, high):
    return pltpu.roll(jnp.where(iota(low.shape, 1) < LANES // 2, low, high), LANES // 2, 1)


def split(v):
    high = v.astype(BF16)
    return jnp.concatenate([high, (v - high.astype(F32)).astype(BF16)], 1)


def storage(block):
    return BF16 if block % 16 == 0 else F32


def flat(ref, s, r):
    if len(ref.shape) == 4:
        return ref[s, r]
    v = ref[:, s, r]
    return v.reshape(v.shape[0] * v.shape[1], LANES).astype(BF16)


class Dims:
    def __init__(self, nd, nc, skip, enc, dec, gate):
        self.nd, self.nc = nd, nc
        self.s, self.rows, self.cols = skip[1:]
        self.cs, self.ce, self.cd, self.g = skip[0], enc, dec, gate
        self.half, self.hcols = self.rows // 2, self.cols // 2
        self.fine_total = nd * self.s * self.rows * self.cols
        self.coarse_total = self.fine_total // 8
        self.enc_all = nc * enc
        self.skip_all = nc * skip[0]
        self.dec_all = nc * dec


GATHERS = ("pooled", "skip", "z1", "z2", "z3", "dz4", "du3", "du2", "du1")
CONVS = ("enc1", "enc2", "dec1", "dec2")


class Conv:
    def __init__(self, dm, o, c, blocks):
        self.o, self.c, self.blocks = o, c, blocks
        self.length = 27 * c
        self.chunks = -(-self.length // LANES)
        self.per = LANES // o
        self.tiles = -(-9 // self.per)
        self.wide = self.tiles * LANES
        self.kind = storage(min(size for size, _ in blocks))
        self.count = 3 * c // 16 * self.tiles
        self.share = -(-self.count // dm.nd)


def kernel(
    dm,
    skip_ref, cot_ref, w1, w2, w3, w4, gate_ref, vector_ref, en_ref, dn_ref,
    out_ref, sg_ref, g1, g2, g3, g4, ggate, gvector, gen, gdn,
    xp, xs, xh, xc, d1, xd, xz4, xz3, xz2, xz1,
    pz1, pz2, pz3, pu3, pu2, pu1, z1, z2, z3, z4, du_c, du_f, pre_ref, al_ref, pg_ref, ug_ref, dt, gg, cg,
    dzf, dzc, fs, fr, st, tt, norm_all, st_g, rows_ref, turned, wide_ref, acc, gate_all, gate_t, gate_own, gate_block,
    wt1, wt2, wt3, wt4, wf1, wf2, wf3, wf4, wx1, wx2, wx3u, wx3g, wx4, wb1, wb2, wb3, wb4,
    gt1, gt2, gt3, gt4, gr1, gr2, gr3, gr4, ga1, ga2, ga3, ga4,
    g_send, g_recv, t_send, t_recv, f_send, f_recv, w_send, w_recv, v_send, v_recv, c_send, c_recv, r_send, r_recv, a_send, a_recv,
):
    nd, nc, S, R, H = dm.nd, dm.nc, dm.s, dm.rows, dm.half
    W, V = dm.cols, dm.hcols
    Q = H // 2
    place = lax.axis_index("depth")
    me = lax.axis_index("chan")
    first, last = place == 0, place == nd - 1
    convs = dm.convs
    pending = []

    def peer_copy(src, dst, send, recv, depth, chan):
        return pltpu.make_async_remote_copy(
            src_ref=src, dst_ref=dst, send_sem=send, recv_sem=recv,
            device_id={"depth": depth, "chan": chan}, device_id_type=MESH,
        )

    def gather_parts(ref, which, pad, sides=(1, 0, 2)):
        n = ref.shape[1] - 2
        span = pl.ds(pad, ref.shape[2] - 2 * pad)
        k = GATHERS.index(which)
        other = me + 1 - 2 * lax.rem(me, 2)
        parts = []
        for side, own, theirs, size in ((1, 1, 1, n), (0, n, 0, 1), (2, 1, n + 1, 1)):
            step = 1 - side
            if side not in sides:
                continue
            can_send = (jnp.logical_not(last), None, jnp.logical_not(first))[side]
            can_recv = (jnp.logical_not(first), None, jnp.logical_not(last))[side]
            for t in range(nc // 2):
                to, source = lax.rem(me + 2 * t, nc), lax.rem(me + nc - 2 * t, nc)
                mate = lax.rem(other + nc - 2 * t, nc)
                i = side * (nc // 2) + t

                def copy(own, block, at, hop, depth, chan, size=size, i=i):
                    return peer_copy(
                        ref.at[block, pl.ds(own, size), span],
                        ref.at[block, pl.ds(at, size), span],
                        g_send.at[k, hop, i], g_recv.at[k, hop, i], depth, chan,
                    )

                mine = side == 1 and t == 0
                out = None if mine else functools.partial(copy, own, me, theirs, 0, place + step, to)
                back = None if mine else functools.partial(copy, theirs, source, theirs, 0, place, source)
                on = functools.partial(copy, theirs, source, theirs, 1, place, other)
                mates = functools.partial(copy, theirs, mate, theirs, 1, place, other)
                parts.append((can_send, can_recv, out, back, on, mates))
        return parts

    def guarded(cond, fn):
        if cond is None:
            fn()
        else:
            pl.when(cond)(fn)

    def gather_start(ref, which, pad):
        for can_send, can_recv, out, _, on, _ in gather_parts(ref, which, pad):
            if out is None:
                on().start()
            else:
                guarded(can_send, lambda out=out: out().start())
                pending.append((can_send, lambda out=out: out().wait_send()))
            pending.append((can_recv, lambda on=on: on().wait_send()))

    def gather_pass(*where):
        for _, can_recv, out, back, on, _ in gather_parts(*where):
            if out is not None:

                def relay(back=back, on=on):
                    back().wait_recv()
                    on().start()

                guarded(can_recv, relay)

    def gather_wait(*where):
        for _, can_recv, _, _, _, mates in gather_parts(*where):
            guarded(can_recv, lambda mates=mates: mates().wait_recv())

    def sum_copy(ref, k, slot, t):
        return peer_copy(
            ref.at[slot, place], ref.at[slot, place], t_send.at[k, t], t_recv.at[k, t], lax.rem(place + t, nd), me
        )

    def sum_start(ref, k, slot, tile):
        ref[slot, place] = tile

        def send(t, _):
            sum_copy(ref, k, slot, t).start()
            return _

        def sent(t, _):
            sum_copy(ref, k, slot, t).wait_send()
            return _

        lax.fori_loop(1, nd, send, 0)
        pending.append((None, lambda: lax.fori_loop(1, nd, sent, 0)))

    def sum_finish(ref, k, slot):
        def receive(t, _):
            source = lax.rem(place + nd - t, nd)
            peer_copy(
                ref.at[slot, source], ref.at[slot, source], t_send.at[k, t], t_recv.at[k, t], source, me
            ).wait_recv()
            return _

        lax.fori_loop(1, nd, receive, 0)
        return jnp.sum(ref[slot], axis=0)

    def totals(k, slot, m):
        return columns_of(sum_finish(st, k, slot), m)

    def totals_start(k, slot):
        tt[slot, me] = sum_finish(st, k, slot)
        for t in range(1, nc):
            out = functools.partial(
                peer_copy, tt.at[slot, me], tt.at[slot, me], c_send.at[k, t], c_recv.at[k, t], place, lax.rem(me + t, nc)
            )
            out().start()
            pending.append((None, lambda out=out: out().wait_send()))

    def totals_wait(k, slot):
        for t in range(1, nc):
            source = lax.rem(me + nc - t, nc)
            theirs = tt.at[slot, source]
            peer_copy(theirs, theirs, c_send.at[k, t], c_recv.at[k, t], place, source).wait_recv()

    def columns_of(row, m):
        lane, channel = iota((m, LANES), 1), iota((m, LANES), 0)
        return tuple(
            jnp.sum(jnp.where(lane == channel + i * m, row, 0.0), axis=1, keepdims=True) for i in range(2)
        )

    def turn_in(w, cv):
        def chunk(a):
            return jnp.transpose(jnp.concatenate([a] * cv.per, 0))

        full = cv.length // LANES

        def body(i, carry):
            at = pl.multiple_of(i * LANES, LANES)
            turned[pl.ds(at, LANES)] = chunk(w[:, pl.ds(at, LANES)])
            return carry

        lax.fori_loop(0, full, body, 0, unroll=4)
        if full < cv.chunks:
            a = w[:, full * LANES :]
            a = jnp.concatenate([a, jnp.zeros((cv.o, LANES - a.shape[1]), F32)], 1)
            turned[full * LANES : (full + 1) * LANES] = chunk(a)

    def prepare(k):
        cv, w, wt, wf = convs[k], (w1, w2, w3, w4)[k], (wt1, wt2, wt3, wt4)[k], (wf1, wf2, wf3, wf4)[k]
        turn_in(w, cv)
        group = iota((cv.c, LANES), 1) // cv.o
        for kz in range(3):
            for j in range(cv.tiles):
                tile = None
                for g in range(cv.per):
                    t = j * cv.per + g
                    if t < 9:
                        v = turned[pl.ds(9 * kz + t, cv.c, stride=27)]
                        tile = v if tile is None else jnp.where(group == g, v, tile)
                tile = tile.astype(BF16)
                wt[kz, :, j * LANES : (j + 1) * LANES] = tile.astype(wt.dtype)
                wide_ref[kz * cv.c : (kz + 1) * cv.c, j * LANES : (j + 1) * LANES] = tile.astype(F32)
        rows = -(-3 * cv.c // LANES) * LANES
        for i in range(rows // LANES):
            v = jnp.transpose(wide_ref[i * LANES : (i + 1) * LANES, 0 : cv.wide])
            size = min(LANES, 3 * cv.c - i * LANES)
            wf[:, i * LANES : i * LANES + size] = v[0 : 9 * cv.o, 0:size].astype(BF16)

    def weight_parts(k):
        cv, wt = convs[k], (wt1, wt2, wt3, wt4)[k]
        into = ((wx1,), (wx2,), (wx3u, wx3g), (wx4,))[k]
        parts = []
        for b, (size, start) in enumerate(cv.blocks):
            for t in range(1, nc):
                to, source = lax.rem(me + t, nc), lax.rem(me + nc - t, nc)
                at = start(to)
                sems = (w_send.at[k, b, t], w_recv.at[k, b, t])
                out = lambda b=b, at=at, size=size, to=to, sems=sems: peer_copy(
                    wt.at[:, pl.ds(at, size)], into[b].at[me], *sems, place, to
                )
                back = lambda b=b, source=source, sems=sems: peer_copy(
                    into[b].at[source], into[b].at[source], *sems, place, source
                )
                parts.append((out, back))
        return parts

    def weights_start(k):
        cv, wt = convs[k], (wt1, wt2, wt3, wt4)[k]
        into = ((wx1,), (wx2,), (wx3u, wx3g), (wx4,))[k]
        for b, (size, start) in enumerate(cv.blocks):
            into[b][me] = wt[:, pl.ds(start(me), size)]
        for out, _ in weight_parts(k):
            out().start()
            pending.append((None, lambda out=out: out().wait_send()))

    def weights_finish(k):
        cv = convs[k]
        into = ((wx1,), (wx2,), (wx3u, wx3g), (wx4,))[k]
        out = (wb1, wb2, wb3, wb4)[k]
        every = sum(size for size, _ in cv.blocks)
        offset = 0
        for _, back in weight_parts(k):
            back().wait_recv()
        for b, (size, _) in enumerate(cv.blocks):
            for t in range(9):
                pieces = [
                    into[b][j, 2 - kz, :, t * cv.o : (t + 1) * cv.o].astype(F32)
                    for kz in range(3)
                    for j in range(nc)
                ]
                at = (8 - t) * every + offset
                out[at : at + size] = jnp.concatenate(pieces, 1).astype(BF16)
            offset += size

    def reduce_copy(k, t):
        cv, gt, gr = convs[k], (gt1, gt2, gt3, gt4)[k], (gr1, gr2, gr3, gr4)[k]
        to = lax.rem(place + t, nd)
        return peer_copy(
            gt.at[pl.ds(to * cv.share, cv.share)], gr.at[place], r_send.at[k, t], r_recv.at[k, t], to, me
        )

    def reduce_start(k):
        cv, gt, gr = convs[k], (gt1, gt2, gt3, gt4)[k], (gr1, gr2, gr3, gr4)[k]

        def tile(i, carry):
            for j in range(cv.tiles):
                at = pl.multiple_of(i * 16, 16)
                gt[i * cv.tiles + j] = acc[pl.ds(at, 16), j * LANES : (j + 1) * LANES].astype(BF16)
            return carry

        lax.fori_loop(0, 3 * cv.c // 16, tile, 0, unroll=4)
        for i in range(cv.count, cv.share * nd):
            gt[i] = jnp.zeros((16, LANES), BF16)
        gr[place] = gt[pl.ds(place * cv.share, cv.share)]

        def send(t, _):
            reduce_copy(k, t).start()
            return _

        def sent(t, _):
            reduce_copy(k, t).wait_send()
            return _

        lax.fori_loop(1, nd, send, 0)
        pending.append((None, lambda: lax.fori_loop(1, nd, sent, 0)))

    def share_copy(k, t):
        cv, ga = convs[k], (ga1, ga2, ga3, ga4)[k]
        own = ga.at[pl.ds(place * cv.share, cv.share)]
        return peer_copy(own, own, a_send.at[k, t], a_recv.at[k, t], lax.rem(place + t, nd), me)

    def reduce_finish(k):
        cv, gr, ga = convs[k], (gr1, gr2, gr3, gr4)[k], (ga1, ga2, ga3, ga4)[k]

        def receive(t, _):
            source = lax.rem(place + nd - t, nd)
            peer_copy(gr.at[source], gr.at[source], r_send.at[k, t], r_recv.at[k, t], source, me).wait_recv()
            return _

        lax.fori_loop(1, nd, receive, 0)
        ga[pl.ds(place * cv.share, cv.share)] = jnp.sum(gr[...].astype(F32), axis=0).astype(BF16)

        def send(t, _):
            share_copy(k, t).start()
            return _

        def sent(t, _):
            share_copy(k, t).wait_send()
            return _

        lax.fori_loop(1, nd, send, 0)
        pending.append((None, lambda: lax.fori_loop(1, nd, sent, 0)))

    def gradient_out(k):
        cv, ga, out = convs[k], (ga1, ga2, ga3, ga4)[k], (g1, g2, g3, g4)[k]

        def receive(t, _):
            source = lax.rem(place + nd - t, nd)
            theirs = ga.at[pl.ds(source * cv.share, cv.share)]
            peer_copy(theirs, theirs, a_send.at[k, t], a_recv.at[k, t], source, me).wait_recv()
            return _

        lax.fori_loop(1, nd, receive, 0)
        group = iota((16, LANES), 1) // cv.o

        def scatter(i, carry):
            for kz in range(3):
                for j in range(cv.tiles):
                    v = ga[(kz * (cv.c // 16) + i) * cv.tiles + j].astype(F32)
                    for g in range(cv.per):
                        t = j * cv.per + g
                        if t < 9:
                            turned[pl.ds(9 * kz + t + i * (16 * 27), 16, stride=27)] = jnp.where(group == g, v, 0.0)
            return carry

        lax.fori_loop(0, cv.c // 16, scatter, 0, unroll=2)

        def chunk(at):
            v = jnp.transpose(turned[pl.ds(at, LANES)])
            return jnp.sum(v.reshape(cv.per, cv.o, LANES), axis=0)

        full = cv.length // LANES

        def body(i, carry):
            at = pl.multiple_of(i * LANES, LANES)
            out[:, pl.ds(at, LANES)] = chunk(at)
            return carry

        lax.fori_loop(0, full, body, 0, unroll=4)
        if full < cv.chunks:
            out[:, full * LANES :] = chunk(full * LANES)[:, 0 : cv.length - full * LANES]

    def column(row):
        n = row.shape[1]
        eye = iota((n, n), 0) == iota((n, n), 1)
        return jnp.sum(jnp.where(eye, row, 0.0), axis=1, keepdims=True)

    def row_of(col):
        n = col.shape[0]
        eye = iota((n, n), 0) == iota((n, n), 1)
        return jnp.sum(jnp.where(eye, col, 0.0), axis=0, keepdims=True)

    def clear_edges(ref):
        if len(ref.shape) == 5:
            for j in range(nc):
                clear_edges(ref.at[j])
            return
        blank = jnp.zeros(ref.shape[2:], ref.dtype)
        for s in range(ref.shape[0]):
            ref[s, 0] = blank
            ref[s, ref.shape[1] - 1] = blank

    def clear_slice(ref, s):
        for j in range(nc):
            ref[j, s] = jnp.zeros(ref.shape[2:], ref.dtype)

    def clear_halos(ref):
        pl.when(first)(lambda: clear_slice(ref, 0))
        pl.when(last)(lambda: clear_slice(ref, ref.shape[1] - 1))

    def conv(ref, weight, slices, rows, m, n, width, emit, init, late=None):
        per = rows // n

        def body(i, carry):
            if late is not None:
                pl.when(i == (slices - 1) * per - 1)(late[0])
                pl.when(i == (slices - 1) * per)(late[1])
            d = i // per
            r0 = (i - d * per) * n
            x = jnp.concatenate(
                [
                    jnp.concatenate([flat(ref, d + kz, r0 + j) for j in range(n + 2)], 1)
                    for kz in range(3)
                ],
                0,
            )
            y = dot(weight[...], x)
            results = []
            for j in range(n):
                acc = []
                for kx in range(3):
                    terms = [
                        y[(3 * ky + kx) * m : (3 * ky + kx + 1) * m, (j + ky) * LANES : (j + ky + 1) * LANES]
                        for ky in range(3)
                    ]
                    acc.append(terms[0] + terms[1] + terms[2])
                results.append(from_left(acc[0], width) + acc[1] + from_right(acc[2], width))
            return emit(d, r0, results, carry)

        return lax.fori_loop(0, slices * per, body, init)

    def weight_grad(ref, dz, k, slices, rows, n):
        per = rows // n
        cv = convs[k]
        acc[0 : 3 * cv.c, 0 : cv.wide] = jnp.zeros((3 * cv.c, cv.wide), F32)

        def body(i, carry):
            d = i // per
            r0 = (i - d * per) * n
            x = jnp.concatenate(
                [
                    jnp.concatenate([flat(ref, d + kz, r0 + 1 + j) for j in range(n)], 1)
                    for kz in range(3)
                ],
                0,
            )
            y = jnp.concatenate(
                [
                    jnp.concatenate([dz[kx, d, r0 + j + 2 - ky] for j in range(n)], 1)
                    for ky in range(3)
                    for kx in range(3)
                ],
                0,
            ).astype(BF16)
            acc[0 : 3 * cv.c, 0 : 9 * cv.o] += dot_nt(x, y)
            return carry

        lax.fori_loop(0, slices * per, body, 0)

    def conv_coarse(ref, weight, m):
        x = jnp.concatenate(
            [jnp.concatenate([flat(ref, kz, i) for i in range(Q)], 1) for kz in range(3)], 0
        )
        y = dot(weight[...], x)
        blank = jnp.zeros((m, LANES), F32)

        def shifted(ky, i):
            if not 0 <= i < Q:
                return blank
            a, b, c = (
                y[(3 * ky + kx) * m : (3 * ky + kx + 1) * m, i * LANES : (i + 1) * LANES] for kx in range(3)
            )
            return from_left(a, V) + b + from_right(c, V)

        before = [shifted(0, i) for i in range(-1, Q)]
        after = [shifted(2, i) for i in range(Q + 1)]
        return [
            shifted(1, i) + halves(before[i + 1] + after[i + 1], before[i] + after[i]) for i in range(Q)
        ]

    def conv_stats_coarse(ref, weight, z, m):
        total = square = jnp.zeros((m, LANES), F32)
        for i, v in enumerate(conv_coarse(ref, weight, m)):
            z[i] = v
            total, square = total + v, square + v * v
        return total, square

    def weight_grad_coarse(ref, k):
        cv = convs[k]
        x = jnp.concatenate(
            [jnp.concatenate([flat(ref, kz, i) for i in range(Q)], 1) for kz in range(3)], 0
        )
        y = jnp.concatenate([jnp.concatenate([dzc[t, i] for i in range(Q)], 1) for t in range(9)], 0)
        acc[0 : 3 * cv.c, 0 : 9 * cv.o] = dot_nt(x, y.astype(BF16))

    def shifted_copies(z, given):
        mean, scale, level, slope = given
        rows = []
        for i in range(Q):
            v = scale * du_c[i] + level + slope * (z[i] - mean)
            rows.append(v.astype(BF16).astype(F32))
        blank = jnp.zeros_like(rows[0])
        rows = [blank] + rows + [blank]
        for i in range(Q):
            before, here, after = rows[i : i + 3]
            for ky, v in enumerate((halves(after, here), here, halves(here, before))):
                for kx, u in enumerate((from_right(v, V), v, from_left(v, V))):
                    dzc[3 * ky + kx, i] = u.astype(dzc.dtype)

    def conv_stats(ref, weight, z, slices, rows, m, n, width, late=None):
        def emit(d, r0, results, carry):
            total, square = carry
            for j, v in enumerate(results):
                z[d * rows + r0 + j] = v
                total, square = total + v, square + v * v
            return total, square

        blank = jnp.zeros((m, LANES), F32)
        return conv(ref, weight, slices, rows, m, n, width, emit, (blank, blank), late)

    def pack(a, b):
        m = a.shape[0]
        a = jnp.sum(a, axis=1, keepdims=True)
        b = jnp.sum(b, axis=1, keepdims=True)
        lane, channel = iota((m, LANES), 1), iota((m, LANES), 0)
        both = jnp.where(lane == channel, a, jnp.where(lane == channel + m, b, 0.0))
        return jnp.sum(both, axis=0, keepdims=True)

    def moments(total, count):
        mean = total[0] / count
        var = total[1] / count - mean * mean
        return mean, lax.rsqrt(var + EPS)

    def wide(column):
        return jnp.broadcast_to(column, (column.shape[0], LANES))

    def factors(stats, norm):
        mean, inv = stats
        gain, shift = norm
        return wide(mean), wide(gain * inv), wide(shift)

    def norm_rows(z, stats, norm, emit, n):
        mean, scale, shift = factors(stats, norm)

        def body(i, carry):
            for j in range(n):
                p = i * n + j
                u = (z[p] - mean) * scale + shift
                emit(p, u * jax.nn.sigmoid(u))
            return carry

        lax.fori_loop(0, z.shape[0] // n, body, 0)

    def norm_back_sums(z, keep_du, stats, norm, grad, n):
        mean, scale, shift = factors(stats, norm)
        inv = wide(stats[1])
        m = z.shape[1]

        def body(i, carry):
            a, b = carry
            for j in range(n):
                p = i * n + j
                centred = z[p] - mean
                u = centred * scale + shift
                sigma = jax.nn.sigmoid(u)
                v = grad(p) * sigma * (1.0 + u * (1.0 - sigma))
                keep_du(p, v)
                a, b = a + v, b + v * (centred * inv)
            return a, b

        blank = jnp.zeros((m, LANES), F32)
        return lax.fori_loop(0, z.shape[0] // n, body, (blank, blank))

    def back_factors(stats, norm, total, count):
        mean, inv = stats
        scale = norm[0] * inv
        return wide(mean), wide(scale), wide(-scale * total[0] / count), wide(-scale * inv * total[1] / count)

    def norm_back(z, du, given, x, rows, width, n):
        mean, scale, level, slope = given
        per = rows // n

        def body(i, carry):
            d = i // per
            r0 = (i - d * per) * n
            for j in range(n):
                r = r0 + j
                v = scale * du(d, r) + level + slope * (z(d, r) - mean)
                low = v.astype(BF16)
                if x is not None:
                    x[me, 1 + d, 1 + r] = low.astype(x.dtype)
                v = low.astype(F32)
                dzf[0, d, 1 + r] = from_right(v, width).astype(dzf.dtype)
                dzf[1, d, 1 + r] = low.astype(dzf.dtype)
                dzf[2, d, 1 + r] = from_left(v, width).astype(dzf.dtype)
            return carry

        lax.fori_loop(0, S * per, body, 0)

    def norm_cols(j, layer, m):
        return column(norm_all[j, 2 * layer : 2 * layer + 1, 0:m]), column(norm_all[j, 2 * layer + 1 : 2 * layer + 2, 0:m])

    def each_row(s0, s1, rows, n, fn):
        per = rows // n

        def body(i, carry):
            s = s0 + i // per
            r0 = (i - (i // per) * per) * n
            for q in range(n):
                fn(s, r0 + q)
            return carry

        lax.fori_loop(0, (s1 - s0) * per, body, 0)

    def norm_blocks(z, dst, pad, slot, layer, m, count, s0, s1, n):
        rows = z.shape[2] - 1
        for j in range(nc):
            mean, scale, shift = factors(moments(columns_of(tt[slot, j], m), count), norm_cols(j, layer, m))

            def one(s, r, j=j, mean=mean, scale=scale, shift=shift):
                centred = z[j, s, r].astype(F32) + (z[j, s, rows].astype(F32) - mean)
                u = centred * scale + shift
                dst[j, s, r + pad] = (u * jax.nn.sigmoid(u)).astype(BF16).astype(dst.dtype)

            each_row(s0, s1, rows, n, one)

    def back_blocks(z, du, dst, pad, slot, back_slot, layer, m, count, s0, s1, n):
        rows = z.shape[2] - 1
        for j in range(nc):
            stats = moments(columns_of(tt[slot, j], m), count)
            given = back_factors(stats, norm_cols(j, layer, m), columns_of(tt[back_slot, j], m), count)

            spread_by = wide(norm_cols(j, layer, m)[0] * stats[1] * stats[1])

            def one(s, r, j=j, given=given, spread_by=spread_by):
                mean, scale, level, slope = given
                if du.shape[2] > rows:
                    level = level + scale * du[j, s, rows].astype(F32)
                    slope = slope + spread_by * du[j, s, rows + 1].astype(F32)
                centred = z[j, s, r].astype(F32) + (z[j, s, rows].astype(F32) - mean)
                v = scale * du[j, s, r].astype(F32) + level + slope * centred
                dst[j, s, r + pad] = v.astype(BF16).astype(dst.dtype)

            each_row(s0, s1, rows, n, one)

    hc = iota((LANES, LANES), 0)
    fc = iota((LANES, LANES), 1)
    half = LANES // 2

    def up_table(coarse, fine):
        base = fine // 2
        other = jnp.clip(base + jnp.where(fine % 2 == 0, -1, 1), 0, V - 1)
        near = (coarse == base).astype(F32)
        far = (coarse == other).astype(F32)
        return (0.75 * near + 0.25 * far).astype(BF16)

    pool = jnp.concatenate([(hc // 2 == fc - at).astype(BF16) for at in (0, half)], 0)
    spread = jnp.concatenate([(hc - at == fc // 2).astype(BF16) for at in (0, half)], 1)
    up = jnp.concatenate([up_table(hc - at, fc) for at in (0, half)], 1)
    down = jnp.concatenate([up_table(fc - at, hc) for at in (0, 0, half, half)], 0)
    spread2 = jnp.concatenate([spread, spread], 0)

    def take_rows(ref):
        for c in range(dm.cs):
            rows_ref[c * S * R : (c + 1) * S * R] = ref[c].astype(F32).reshape(S * R, LANES)

    def row(p):
        return rows_ref[pl.ds(p, dm.cs, stride=S * R)]

    barrier = pltpu.get_barrier_semaphore()

    def greet(depth, chan):
        pl.semaphore_signal(barrier, inc=1, device_id={"depth": depth, "chan": chan}, device_id_type=MESH)

    for t in range(1, nc):
        greet(place, lax.rem(me + t, nc))

    def greet_slab(t, _):
        greet(lax.rem(place + t, nd), me)
        return _

    lax.fori_loop(1, nd, greet_slab, 0)
    for t in range(1, nc // 2):
        to = lax.rem(me + 2 * t, nc)
        pl.when(jnp.logical_not(first))(lambda to=to: greet(place - 1, to))
        pl.when(jnp.logical_not(last))(lambda to=to: greet(place + 1, to))
    clear_halos(xp)
    take_rows(skip_ref)

    def take_skip(i, carry):
        parts = []
        for s in range(S):
            v = [row(s * R + 4 * i + j).astype(BF16) for j in range(4)]
            for j in range(4):
                xs[me, 1 + s, 4 * i + j] = v[j].astype(xs.dtype)
            parts += [jnp.concatenate([v[j], v[2 + j]], 1) for j in range(2)]
        v = dot(jnp.concatenate(parts, 0), pool).reshape(2 * S, dm.cs, LANES)
        xp[me, 1, i] = (jnp.sum(v, axis=0) * 0.125).astype(BF16).astype(xp.dtype)
        return carry

    lax.fori_loop(0, Q, take_skip, 0, unroll=3)
    clear_halos(xs)
    beside = jnp.where(first, 0, 1) + jnp.where(last, 0, 1)
    pl.semaphore_wait(barrier, nc - 1 + nd - 1 + (nc // 2 - 1) * beside)
    gather_start(xp, "pooled", 0)
    gather_start(xs, "skip", 0)

    gq = dm.g // nc
    gate_all[me, :, 0 : gate_ref.shape[1]] = gate_ref[...]
    lane = iota((gq, LANES), 1)
    gate_all[me, :, 2 * LANES :] = jnp.where(
        lane == 0, column(vector_ref[0:1]), jnp.where(lane == 1, column(vector_ref[1:2]), 0.0)
    )
    for i, (ref, width) in enumerate(((en_ref, dm.ce), (dn_ref, dm.cd))):
        for layer in range(2):
            for part in range(2):
                at = 4 * i + 2 * layer + part
                norm_all[me, at : at + 1, 0:width] = ref[part, layer : layer + 1]

    def constants(i, t, source, to):
        ref = (norm_all, gate_all)[i]
        return peer_copy(ref.at[source], ref.at[source], v_send.at[i, t], v_recv.at[i, t], place, to)

    def constants_wait(i):
        for t in range(1, nc):
            source = lax.rem(me + nc - t, nc)
            constants(i, t, source, source).wait_recv()

    for i in range(2):
        for t in range(1, nc):
            out = functools.partial(constants, i, t, me, lax.rem(me + t, nc))
            out().start()
            pending.append((None, lambda out=out: out().wait_send()))

    prepare(0)
    for ref in (xd, d1, xz4, xz3):
        clear_edges(ref)
    clear_halos(xz4)
    for kx in range(3):
        for s in range(S):
            dzf[kx, s, 0] = jnp.zeros(dzf.shape[3:], dzf.dtype)
            dzf[kx, s, R + 1] = jnp.zeros(dzf.shape[3:], dzf.dtype)

    def norm_of(ref, layer):
        return column(ref[0, layer : layer + 1]), column(ref[1, layer : layer + 1])

    norm_e1, norm_e2 = norm_of(en_ref, 0), norm_of(en_ref, 1)
    norm_d1, norm_d2 = norm_of(dn_ref, 0), norm_of(dn_ref, 1)

    def send_z(z, total, ref, which, n):
        rows = ref.shape[2] - 1
        slabs = ref.shape[1] - 2
        level = wide(jnp.sum(total, axis=1, keepdims=True) / (slabs * rows * LANES)).astype(BF16)
        for d in range(slabs):
            ref[me, 1 + d, rows] = level.astype(ref.dtype)
        level = level.astype(F32)

        def store(s, r):
            ref[me, s, r] = (z[(s - 1) * rows + r] - level).astype(BF16).astype(ref.dtype)

        each_row(1, 1 + slabs, rows, n, store)
        gather_start(ref, which, 0)

    gather_pass(xp, "pooled", 0)
    gather_wait(xp, "pooled", 0)
    sums = conv_stats_coarse(xp, wf1, z1, dm.ce)
    sum_start(st, 0, 0, pack(*sums))
    send_z(z1, sums[0], pz1, "z1", Q)
    prepare(1)
    constants_wait(0)
    totals_start(0, 0)
    gather_pass(pz1, "z1", 0)
    totals_wait(0, 0)
    gather_wait(pz1, "z1", 0)
    norm_blocks(pz1, xh, 0, 0, 0, dm.ce, dm.coarse_total, 0, 3, Q)
    clear_halos(xh)
    sums = conv_stats_coarse(xh, wf2, z2, dm.ce)
    sum_start(st, 1, 1, pack(*sums))
    send_z(z2, sums[0], pz2, "z2", Q)
    gather_pass(xs, "skip", 0)
    prepare(3)
    totals_start(1, 1)
    gather_pass(pz2, "z2", 0)
    prepare(2)
    totals_wait(1, 1)
    gather_wait(pz2, "z2", 0)
    for k in (3, 2, 1, 0):
        weights_start(k)
    norm_blocks(pz2, xc, 0, 1, 1, dm.ce, dm.coarse_total, 0, 3, Q)
    constants_wait(1)
    gate_full = gate_all[...].reshape(dm.g, 3 * LANES)
    wg = gate_full[:, 0 : dm.enc_all + dm.skip_all].astype(BF16)
    gbias = gate_full[:, 2 * LANES : 2 * LANES + 1]
    gout = gate_full[:, 2 * LANES + 1 : 2 * LANES + 2]
    gate_t[...] = jnp.transpose(gate_full[:, 0 : 2 * LANES])
    gate_own[...] = jnp.concatenate(
        [
            gate_t[pl.ds(pl.multiple_of(me * dm.ce, dm.ce), dm.ce)],
            gate_t[pl.ds(pl.multiple_of(dm.enc_all + me * dm.cs, dm.cs), dm.cs)],
        ],
        0,
    )

    def up_depth(i, carry):
        t = []
        for s in range(3):
            v = dot(flat(xc, s, i), up)
            t.append(jnp.stack([v[:, 0:LANES], v[:, LANES:]], 0))
        below = jnp.where(first, t[1], t[0])
        above = jnp.where(last, t[1], t[2])
        near = 0.75 * t[1]
        here = 0.25 * t[1]
        rows = pl.ds(i * 2, 2)
        dt[0, rows] = jnp.where(first, 0.0, 0.75 * below + here)
        dt[1, rows] = near + 0.25 * below
        dt[2, rows] = near + 0.25 * above
        dt[3, rows] = jnp.where(last, 0.0, 0.75 * above + here)
        return carry

    lax.fori_loop(0, Q, up_depth, 0)

    def up_rows(i, carry):
        before, after = jnp.maximum(i - 1, 0), jnp.minimum(i + 1, H - 1)
        for s in range(S + 2):
            v = 0.75 * dt[s, i]
            d1[s, 1 + 2 * i, 0 : dm.enc_all] = (v + 0.25 * dt[s, before]).astype(BF16)
            d1[s, 2 + 2 * i, 0 : dm.enc_all] = (v + 0.25 * dt[s, after]).astype(BF16)
        return carry

    lax.fori_loop(0, H, up_rows, 0)

    gather_wait(xs, "skip", 0)
    gate_n = 12

    def gate(i, carry):
        s = i // (R // gate_n)
        r0 = (i - s * (R // gate_n)) * gate_n
        skips = [flat(xs, s, r0 + j) for j in range(gate_n)]
        x = jnp.concatenate(
            [
                jnp.concatenate([d1[s, 1 + r0 + j, 0 : dm.enc_all] for j in range(gate_n)], 1),
                jnp.concatenate(skips, 1),
            ],
            0,
        )
        pre = dot(wg, x) + gbias
        act = pre * jax.nn.sigmoid(pre)
        alpha = jax.nn.sigmoid(jnp.sum(gout * act, axis=0, keepdims=True))
        for j in range(gate_n):
            lanes = slice(j * LANES, (j + 1) * LANES)
            d1[s, 1 + r0 + j, dm.enc_all :] = (alpha[:, lanes] * skips[j].astype(F32)).astype(BF16)
            pre_ref[s, r0 + j] = pre[:, lanes]
            al_ref[s, r0 + j] = alpha[:, lanes]
        return carry

    lax.fori_loop(0, (S + 2) * R // gate_n, gate, 0)

    sums = conv_stats(d1, wf3, z3, S, R, dm.cd, 12, W)
    sum_start(st, 4, 4, pack(*sums))
    send_z(z3, sums[0], pz3, "z3", R)
    weights_finish(3)
    totals_start(4, 4)
    weights_finish(2)
    take_rows(cot_ref)
    gather_pass(pz3, "z3", 0, (1, 0))
    totals_wait(4, 4)
    gather_wait(pz3, "z3", 0, (1, 0))

    def norm_slices(s0, s1):
        norm_blocks(pz3, xd, 1, 4, 2, dm.cd, dm.fine_total, s0, s1, R)

    norm_slices(0, S + 1)
    pl.when(first)(lambda: clear_slice(xd, 0))

    def last_hidden():
        gather_wait(pz3, "z3", 0, (2,))
        norm_slices(S + 1, S + 2)
        pl.when(last)(lambda: clear_slice(xd, S + 1))

    late = (lambda: gather_pass(pz3, "z3", 0, (2,)), last_hidden)
    sum_start(st, 5, 5, pack(*conv_stats(xd, wf4, z4, S, R, dm.cd, 12, W, late)))
    weights_finish(1)
    stats_d2 = moments(totals(5, 5, dm.cd), dm.fine_total)

    def keep_du(p, v):
        du_f[p] = v

    sum_start(st, 6, 6, pack(*norm_back_sums(z4, keep_du, stats_d2, norm_d2, row, R)))

    def keep_result(p, v):
        out_ref[pl.ds(pl.multiple_of(p * dm.cd, dm.cd), dm.cd)] = v

    norm_rows(z4, stats_d2, norm_d2, keep_result, R)
    total_d2 = totals(6, 6, dm.cd)
    given = back_factors(stats_d2, norm_d2, total_d2, dm.fine_total)
    norm_back(lambda d, r: z4[d * R + r], lambda d, r: du_f[d * R + r], given, xz4, R, W, 12)
    gather_start(xz4, "dz4", 1)
    weight_grad(xd, dzf, 3, S, R, 12)
    reduce_start(3)
    weights_finish(0)
    gather_pass(xz4, "dz4", 1, (1, 0))
    gather_wait(xz4, "dz4", 1, (1, 0))

    def keep_grad(d, r0, results, carry):
        for j, v in enumerate(results):
            gg[d * R + r0 + j] = v
        return carry

    late = (lambda: gather_pass(xz4, "dz4", 1, (2,)), lambda: gather_wait(xz4, "dz4", 1, (2,)))
    conv(xz4, wb4, S, R, dm.cd, 12, W, keep_grad, 0, late)
    stats_d1 = moments(columns_of(tt[4, me], dm.cd), dm.fine_total)

    sums = norm_back_sums(z3, keep_du, stats_d1, norm_d1, lambda p: gg[p], R)
    sum_start(st, 7, 7, pack(*sums))
    levels = [wide(jnp.sum(v, axis=1, keepdims=True) / (S * R * LANES)).astype(BF16) for v in sums]
    for d in range(S):
        for i in range(2):
            pu3[me, 1 + d, R + i] = levels[i].astype(pu3.dtype)
    own_level, own_slope = (v.astype(F32) for v in levels)
    own_slope = own_slope * wide(stats_d1[1])
    own_mean = wide(stats_d1[0])

    def send_du3(s, r):
        p = (s - 1) * R + r
        v = du_f[p] - own_level - own_slope * (z3[p] - own_mean)
        pu3[me, s, r] = v.astype(BF16).astype(pu3.dtype)

    each_row(1, 1 + S, R, R, send_du3)
    gather_start(pu3, "du3", 0)
    reduce_finish(3)
    totals_start(7, 7)
    total_d1 = columns_of(tt[7, me], dm.cd)
    given = back_factors(stats_d1, norm_d1, total_d1, dm.fine_total)
    norm_back(lambda d, r: z3[d * R + r], lambda d, r: du_f[d * R + r], given, None, R, W, 12)
    weight_grad(d1, dzf, 2, S, R, 12)
    gather_pass(pu3, "du3", 0, (1, 0))
    reduce_start(2)
    totals_wait(7, 7)
    gather_wait(pu3, "du3", 0, (1, 0))

    def back_slices(s0, s1):
        back_blocks(pz3, pu3, xz3, 1, 4, 7, 2, dm.cd, dm.fine_total, s0, s1, R)

    back_slices(0, S + 1)
    pl.when(first)(lambda: clear_slice(xz3, 0))

    def last_dz():
        gather_wait(pu3, "du3", 0, (2,))
        back_slices(S + 1, S + 2)
        pl.when(last)(lambda: clear_slice(xz3, S + 1))

    late = (lambda: gather_pass(pu3, "du3", 0, (2,)), last_dz)

    def gate_back(d, r0, results, carry):
        bias, psi = carry
        lows = []
        for j, both in enumerate(results):
            s, r = d + 1, r0 + j
            ug_ref[d * R + r] = both[0 : dm.ce]
            v = both[dm.ce :]
            grad = jnp.sum(v * flat(xs, s, r).astype(F32), axis=0, keepdims=True)
            alpha = al_ref[s, r]
            logit = grad * alpha * (1.0 - alpha)
            pre = pre_ref[s, r]
            sigma = jax.nn.sigmoid(pre)
            psi = psi + pre * sigma * logit
            low = (logit * gout * sigma * (1.0 + pre * (1.0 - sigma))).astype(BF16)
            bias = bias + low.astype(F32)
            pg_ref[d * R + r] = low
            lows.append(low)
            for t in range(nc):
                gg[t] = v[t * dm.cs : (t + 1) * dm.cs]
            sg_at = pl.ds(pl.multiple_of((d * R + r) * dm.cs, dm.cs), dm.cs)
            sg_ref[sg_at] = alpha * gg[me]
        back = dot(gate_own[...].astype(BF16), jnp.concatenate(lows, 1))
        for j in range(len(results)):
            lanes = slice(j * LANES, (j + 1) * LANES)
            ug_ref[d * R + r0 + j] += back[0 : dm.ce, lanes]
            sg_at = pl.ds(pl.multiple_of((d * R + r0 + j) * dm.cs, dm.cs), dm.cs)
            sg_ref[sg_at] += back[dm.ce :, lanes]
        return bias, psi

    blank = jnp.zeros((dm.g, LANES), F32)
    bias, psi = conv(xz3, wb3, S, R, dm.ce + dm.skip_all, 8, W, gate_back, (blank, blank), late)

    def down_rows(i, carry):
        terms = []
        for s in range(S):
            pair = []
            for j in range(2):
                r = i * 2 + j
                near = ug_ref[s * R + 2 * r] + ug_ref[s * R + 2 * r + 1]
                far = ug_ref[s * R + jnp.minimum(2 * r + 2, R - 1)] + ug_ref[s * R + jnp.maximum(2 * r - 1, 0)]
                pair.append(split(0.75 * near + 0.25 * far))
            terms.append(jnp.concatenate(pair, 1))
        v = dot(jnp.concatenate(terms, 0), down)
        even, odd = v[0 : dm.ce], v[dm.ce :]
        fs[0, i] = (0.25 * even).astype(BF16)
        fs[1, i] = (0.25 * odd).astype(BF16)
        cg[i] = 0.75 * (even + odd) + jnp.where(first, 0.25 * even, 0.0) + jnp.where(last, 0.25 * odd, 0.0)
        return carry

    lax.fori_loop(0, Q, down_rows, 0)

    def fold(side, step):
        return peer_copy(fs.at[side], fr.at[1 - side], f_send.at[side], f_recv.at[1 - side], place + step, me)

    pl.when(jnp.logical_not(first))(lambda: fold(0, -1).start())
    pl.when(jnp.logical_not(last))(lambda: fold(1, 1).start())
    pending.append((jnp.logical_not(first), lambda: fold(0, -1).wait_send()))
    pending.append((jnp.logical_not(last), lambda: fold(1, 1).wait_send()))
    reduce_finish(2)

    def fold_in(side):
        peer_copy(fs.at[side], fr.at[side], f_send.at[side], f_recv.at[side], place, me).wait_recv()
        cg[...] += fr[side].astype(F32)

    pl.when(jnp.logical_not(first))(lambda: fold_in(0))
    pl.when(jnp.logical_not(last))(lambda: fold_in(1))

    stats_e1 = moments(columns_of(tt[0, me], dm.ce), dm.coarse_total)
    stats_e2 = moments(columns_of(tt[1, me], dm.ce), dm.coarse_total)

    def keep_du_in(ref):
        def store(p, v):
            ref[me, 1, p] = v.astype(BF16).astype(ref.dtype)
            du_c[p] = v

        return store

    sums = norm_back_sums(z2, keep_du_in(pu2), stats_e2, norm_e2, lambda p: cg[p], Q)
    gather_start(pu2, "du2", 0)
    sum_start(st, 2, 2, pack(*sums))

    columns = gate_ref.shape[1]
    acc[0 : dm.g, 0:columns] = jnp.zeros((dm.g, columns), F32)

    weight_n = 12

    def gate_weight(i, carry):
        d = i // (R // weight_n)
        r0 = (i - d * (R // weight_n)) * weight_n
        x = jnp.concatenate(
            [
                jnp.concatenate([d1[1 + d, 1 + r0 + j, 0 : dm.enc_all] for j in range(weight_n)], 1),
                jnp.concatenate([flat(xs, 1 + d, r0 + j) for j in range(weight_n)], 1),
            ],
            0,
        )
        y = jnp.concatenate([pg_ref[d * R + r0 + j] for j in range(weight_n)], 1)
        acc[0 : dm.g, 0:columns] += dot_nt(y, x)
        return carry

    lax.fori_loop(0, S * R // weight_n, gate_weight, 0)
    lane = iota((dm.g, LANES), 1)
    vectors = jnp.where(
        lane == 0,
        jnp.sum(bias, axis=1, keepdims=True),
        jnp.where(lane == 1, jnp.sum(psi, axis=1, keepdims=True), 0.0),
    )
    for j in range(nc):
        mine = slice(j * gq, (j + 1) * gq)
        gate_block[j, :, 0:columns] = acc[mine, 0:columns]
        gate_block[j, :, columns : 2 * LANES] = jnp.zeros((gq, 2 * LANES - columns), F32)
        gate_block[j, :, 2 * LANES :] = vectors[mine]
    sum_start(st_g, 8, 0, gate_block[me])
    gradient_out(3)
    totals_start(2, 2)
    total_e2 = columns_of(tt[2, me], dm.ce)
    gather_pass(pu2, "du2", 0)
    shifted_copies(z2, back_factors(stats_e2, norm_e2, total_e2, dm.coarse_total))
    weight_grad_coarse(xh, 1)
    reduce_start(1)
    totals_wait(2, 2)
    gather_wait(pu2, "du2", 0)
    back_blocks(pz2, pu2, xz2, 0, 1, 2, 1, dm.ce, dm.coarse_total, 0, 3, Q)
    clear_halos(xz2)
    for i, v in enumerate(conv_coarse(xz2, wb2, dm.ce)):
        cg[i] = v
    sums = norm_back_sums(z1, keep_du_in(pu1), stats_e1, norm_e1, lambda p: cg[p], Q)
    gather_start(pu1, "du1", 0)
    sum_start(st, 3, 3, pack(*sums))
    gradient_out(2)
    reduce_finish(1)
    totals_start(3, 3)
    total_e1 = columns_of(tt[3, me], dm.ce)
    gather_pass(pu1, "du1", 0)
    shifted_copies(z1, back_factors(stats_e1, norm_e1, total_e1, dm.coarse_total))
    weight_grad_coarse(xp, 0)
    reduce_start(0)
    totals_wait(3, 3)
    gather_wait(pu1, "du1", 0)
    back_blocks(pz1, pu1, xz1, 0, 0, 3, 0, dm.ce, dm.coarse_total, 0, 3, Q)
    clear_halos(xz1)
    for i, v in enumerate(conv_coarse(xz1, wb1, dm.cs)):
        v = dot(split(v), spread2) * 0.125
        for j in range(4):
            part = v[:, (j // 2) * LANES : (j // 2 + 1) * LANES]
            for s in range(S):
                at = (s * R + 4 * i + j) * dm.cs
                sg_ref[at : at + dm.cs] += part
    gradient_out(1)
    reduce_finish(0)
    gate_total = sum_finish(st_g, 8, 0)
    ggate[...] = gate_total[:, 0:columns]
    gvector[0:1] = row_of(gate_total[:, 2 * LANES : 2 * LANES + 1])
    gvector[1:2] = row_of(gate_total[:, 2 * LANES + 1 : 2 * LANES + 2])
    for ref, both in ((gen, (total_e1, total_e2)), (gdn, (total_d1, total_d2))):
        for layer, total in enumerate(both):
            ref[0, layer : layer + 1] = row_of(total[1])
            ref[1, layer : layer + 1] = row_of(total[0])
    gradient_out(0)
    for cond, fn in pending:
        guarded(cond, fn)


def adamw(weight, grad, moment, square, rate):
    new_moment = 0.9 * moment + 0.1 * grad
    new_square = 0.999 * square + 0.001 * grad * grad
    moment_hat = new_moment / (1.0 - 0.9**STEP)
    square_hat = new_square / (1.0 - 0.999**STEP)
    new_weight = weight - rate * (moment_hat / (jnp.sqrt(square_hat) + 1e-08) + 0.01 * weight)
    return (new_weight, new_moment, new_square)


RATES = (CONV_RATE, CONV_RATE, GATE_RATE, VECTOR_RATE, CONV_RATE, CONV_RATE, VECTOR_RATE, VECTOR_RATE)


def update_kernel(*refs):
    n = len(RATES)
    sources, targets = refs[: 2 + 4 * n], refs[2 + 4 * n : 4 + 7 * n]
    inside, outside = refs[4 + 7 * n : 6 + 11 * n], refs[6 + 11 * n : 8 + 14 * n]
    in_sem, out_sem = refs[8 + 14 * n :]
    order = (4, 1, 0, 5, 2, 3, 6, 7)

    def load(i):
        return pltpu.make_async_copy(sources[i], inside[i], in_sem.at[i])

    def store(i):
        return pltpu.make_async_copy(outside[i], targets[i], out_sem.at[i])

    for i in (1, 0):
        load(i).start()
    for k in order:
        for part in range(4):
            load(2 + part * n + k).start()
    for i in (1, 0):
        load(i).wait()
        chans, (slabs, rows) = outside[i].shape[0], outside[i].shape[1:3]
        for c in range(chans):
            v = inside[i][pl.ds(c, slabs * rows, stride=chans)]
            outside[i][c] = v.reshape(slabs, rows, LANES).astype(outside[i].dtype)
        store(i).start()
    for k in order:
        own = [2 + part * n + k for part in range(4)]
        for i in own:
            load(i).wait()
        rows = inside[own[0]].shape[0]
        step = 8 if rows % 8 == 0 and rows > 8 else rows
        for r in range(0, rows, step):
            at = slice(r, r + step)
            new = adamw(*(inside[i][at] for i in own), RATES[k])
            for part, value in enumerate(new):
                outside[2 + 3 * k + part][at] = value
        for part in range(3):
            store(2 + 3 * k + part).start()
    for i in range(len(targets)):
        store(i).wait()


def per_device(
    skip, cotangent, enc_conv1, enc_conv2, gate_proj, gate_vector, dec_conv1, dec_conv2, enc_norms, dec_norms, *states
):
    nd, nc = lax.axis_size("depth"), lax.axis_size("chan")
    dm = Dims(nd, nc, skip.shape, enc_conv1.shape[0], dec_conv1.shape[0], gate_proj.shape[0] * nc)
    S, R, H = dm.s, dm.rows, dm.half
    cin3 = dm.enc_all + dm.skip_all

    def block_of(size):
        return (size, lambda j: pl.multiple_of(j * size, size))

    dm.convs = convs = (
        Conv(dm, dm.ce, dm.skip_all, (block_of(dm.cs),)),
        Conv(dm, dm.ce, dm.enc_all, (block_of(dm.ce),)),
        Conv(dm, dm.cd, cin3, (block_of(dm.ce), (dm.skip_all, lambda j: dm.enc_all))),
        Conv(dm, dm.cd, dm.dec_all, (block_of(dm.cd),)),
    )
    params = (enc_conv1, enc_conv2, gate_proj, gate_vector, dec_conv1, dec_conv2, enc_norms, dec_norms)
    inputs = (
        skip, cotangent, enc_conv1, enc_conv2, dec_conv1, dec_conv2, gate_proj, gate_vector, enc_norms, dec_norms
    )
    shape = jax.ShapeDtypeStruct
    outs = (
        shape((S * R * dm.cd, LANES), F32),
        shape((S * R * dm.cs, LANES), F32),
        *(shape(a.shape, F32) for a in (enc_conv1, enc_conv2, dec_conv1, dec_conv2)),
        *(shape(a.shape, F32) for a in (gate_proj, gate_vector, enc_norms, dec_norms)),
    )

    def ext(slices, rows, block):
        return pltpu.VMEM((nc, slices, rows, block, LANES), storage(block))

    def exchange(cv):
        return [pltpu.VMEM((nc, 3, size, cv.wide), cv.kind) for size, _ in cv.blocks]

    def backward(cv):
        return [pltpu.VMEM((9 * sum(size for size, _ in cv.blocks), 3 * nc * cv.o), BF16)]

    gq = dm.g // nc
    Q = H // 2
    scratch = [
        ext(3, Q, dm.cs),
        ext(S + 2, R, dm.cs),
        ext(3, Q, dm.ce),
        ext(3, Q, dm.ce),
        pltpu.VMEM((S + 2, R + 2, cin3, LANES), BF16),
        ext(S + 2, R + 2, dm.cd),
        ext(S + 2, R + 2, dm.cd),
        ext(S + 2, R + 2, dm.cd),
        ext(3, Q, dm.ce),
        ext(3, Q, dm.ce),
        ext(3, Q + 1, dm.ce),
        ext(3, Q + 1, dm.ce),
        ext(S + 2, R + 1, dm.cd),
        ext(S + 2, R + 2, dm.cd),
        ext(3, Q, dm.ce),
        ext(3, Q, dm.ce),
        pltpu.VMEM((Q, dm.ce, LANES), F32),
        pltpu.VMEM((Q, dm.ce, LANES), F32),
        pltpu.VMEM((S * R, dm.cd, LANES), F32),
        pltpu.VMEM((S * R, dm.cd, LANES), F32),
        pltpu.VMEM((Q, dm.ce, LANES), F32),
        pltpu.VMEM((S * R, dm.cd, LANES), F32),
        pltpu.VMEM((S + 2, R, dm.g, LANES), F32),
        pltpu.VMEM((S + 2, R, 1, LANES), F32),
        pltpu.VMEM((S * R, dm.g, LANES), BF16),
        pltpu.VMEM((S * R, dm.ce, LANES), F32),
        pltpu.VMEM((S + 2, H, dm.enc_all, LANES), F32),
        pltpu.VMEM((S * R, dm.cd, LANES), F32),
        pltpu.VMEM((Q, dm.ce, LANES), F32),
        pltpu.VMEM((3, S, R + 2, dm.cd, LANES), storage(dm.cd)),
        pltpu.VMEM((9, Q, dm.ce, LANES), BF16),
        pltpu.VMEM((2, Q, dm.ce, LANES), BF16),
        pltpu.VMEM((2, Q, dm.ce, LANES), BF16),
        pltpu.VMEM((8, nd, 1, LANES), F32),
        pltpu.VMEM((8, nc, 1, LANES), F32),
        pltpu.VMEM((nc, 8, LANES), F32),
        pltpu.VMEM((1, nd, gq, 3 * LANES), F32),
        pltpu.VMEM((dm.cs * S * R, LANES), F32),
        pltpu.VMEM((max(cv.chunks for cv in convs) * LANES, LANES), F32),
        pltpu.VMEM((max(-(-3 * cv.c // LANES) for cv in convs) * LANES, max(cv.wide for cv in convs)), F32),
        pltpu.VMEM((max(3 * cv.c for cv in convs), max(cv.wide for cv in convs)), F32),
        pltpu.VMEM((nc, gq, 3 * LANES), F32),
        pltpu.VMEM((2 * LANES, dm.g), F32),
        pltpu.VMEM((dm.ce + dm.cs, dm.g), F32),
        pltpu.VMEM((nc, gq, 3 * LANES), F32),
        *(pltpu.VMEM((3, cv.c, cv.wide), cv.kind) for cv in convs),
        *(pltpu.VMEM((9 * cv.o, 3 * cv.c), BF16) for cv in convs),
        *(ref for cv in convs for ref in exchange(cv)),
        *(ref for cv in convs for ref in backward(cv)),
        *(pltpu.VMEM((cv.share * nd, 16, LANES), BF16) for cv in convs),
        *(pltpu.VMEM((nd, cv.share, 16, LANES), BF16) for cv in convs),
        *(pltpu.VMEM((cv.share * nd, 16, LANES), BF16) for cv in convs),
        *[pltpu.SemaphoreType.DMA((len(GATHERS), 2, 3 * nc // 2))] * 2,
        *[pltpu.SemaphoreType.DMA((9, nd))] * 2,
        *[pltpu.SemaphoreType.DMA((2,))] * 2,
        *[pltpu.SemaphoreType.DMA((4, 2, nc))] * 2,
        *[pltpu.SemaphoreType.DMA((2, nc))] * 2,
        *[pltpu.SemaphoreType.DMA((8, nc))] * 2,
        *[pltpu.SemaphoreType.DMA((4, nd))] * 4,
    ]
    vmem = pl.BlockSpec(memory_space=pltpu.VMEM)
    out, sg, grad1, grad2, grad3, grad4, ggate, gvector, gen, gdn = pl.pallas_call(
        functools.partial(kernel, dm),
        out_shape=outs,
        in_specs=[vmem] * len(inputs),
        out_specs=[vmem] * len(outs),
        scratch_shapes=scratch,
        compiler_params=pltpu.CompilerParams(
            has_side_effects=True, collective_id=0, vmem_limit_bytes=60 * 1024 * 1024
        ),
        name="step",
    )(*inputs)
    grads = (grad1, grad2, ggate, gvector, grad3, grad4, gen, gdn)
    operands = (out, sg, *params, *grads, *states)
    updated = (
        shape(cotangent.shape, BF16),
        shape(skip.shape, F32),
        *(shape(p.shape, F32) for p in params for _ in range(3)),
    )
    anywhere = pl.BlockSpec(memory_space=pl.ANY)
    return pl.pallas_call(
        update_kernel,
        out_shape=updated,
        in_specs=[anywhere] * len(operands),
        out_specs=[anywhere] * len(updated),
        scratch_shapes=[
            *(pltpu.VMEM(a.shape, a.dtype) for a in operands),
            *(pltpu.VMEM(a.shape, a.dtype) for a in updated),
            pltpu.SemaphoreType.DMA((len(operands),)),
            pltpu.SemaphoreType.DMA((len(updated),)),
        ],
        compiler_params=pltpu.CompilerParams(vmem_limit_bytes=60 * 1024 * 1024),
        name="update",
    )(*operands)


def solution(mesh):
    volume = P("chan", "depth", None, None)
    row, column, norms = P("chan", None), P(None, "chan"), P(None, None, "chan")
    params = (row, row, row, column, row, row, norms, norms)
    return jax.shard_map(
        per_device,
        mesh=mesh,
        in_specs=(volume, volume) + params * 3,
        out_specs=(volume, volume) + tuple(spec for spec in params for _ in range(3)),
        check_vma=False,
    )
```

```python
import functools

import jax
import jax.numpy as jnp
from jax import lax
from jax.experimental import pallas as pl
from jax.experimental.pallas import tpu as pltpu
from jax.sharding import PartitionSpec as P

STEP = 5
EPS = 1e-05
CONV_RATE = 0.03
GATE_RATE = 0.1
VECTOR_RATE = 0.5
LANES = 128
MESH = pl.DeviceIdType.MESH
F32 = jnp.float32
BF16 = jnp.bfloat16


def iota(shape, dim):
    return lax.broadcasted_iota(jnp.int32, shape, dim)


def dot(a, b):
    return jnp.dot(a, b, preferred_element_type=F32)


def dot_nt(a, b):
    return lax.dot_general(a, b, (((1,), (1,)), ((), ())), preferred_element_type=F32)


def from_left(v, width):
    return jnp.where(iota(v.shape, 1) % width == 0, 0.0, pltpu.roll(v, 1, 1))


def from_right(v, width):
    return jnp.where(iota(v.shape, 1) % width == width - 1, 0.0, pltpu.roll(v, LANES - 1, 1))


def halves(low, high):
    return pltpu.roll(jnp.where(iota(low.shape, 1) < LANES // 2, low, high), LANES // 2, 1)


def split(v):
    high = v.astype(BF16)
    return jnp.concatenate([high, (v - high.astype(F32)).astype(BF16)], 1)


def storage(block):
    return BF16 if block % 16 == 0 else F32


def flat(ref, s, r):
    if len(ref.shape) == 4:
        return ref[s, r]
    v = ref[:, s, r]
    return v.reshape(v.shape[0] * v.shape[1], LANES).astype(BF16)


class Dims:
    def __init__(self, nd, nc, skip, enc, dec, gate):
        self.nd, self.nc = nd, nc
        self.s, self.rows, self.cols = skip[1:]
        self.cs, self.ce, self.cd, self.g = skip[0], enc, dec, gate
        self.half, self.hcols = self.rows // 2, self.cols // 2
        self.fine_total = nd * self.s * self.rows * self.cols
        self.coarse_total = self.fine_total // 8
        self.enc_all = nc * enc
        self.skip_all = nc * skip[0]
        self.dec_all = nc * dec


GATHERS = ("pooled", "skip", "z1", "z2", "z3", "dz4", "du3", "du2", "du1")
CONVS = ("enc1", "enc2", "dec1", "dec2")


class Conv:
    def __init__(self, dm, o, c, blocks):
        self.o, self.c, self.blocks = o, c, blocks
        self.length = 27 * c
        self.chunks = -(-self.length // LANES)
        self.per = LANES // o
        self.tiles = -(-9 // self.per)
        self.wide = self.tiles * LANES
        self.kind = storage(min(size for size, _ in blocks))
        self.count = 3 * c // 16 * self.tiles
        self.share = -(-self.count // dm.nd)


def kernel(
    dm,
    skip_ref, cot_ref, w1, w2, w3, w4, gate_ref, vector_ref, en_ref, dn_ref,
    out_ref, sg_ref, g1, g2, g3, g4, ggate, gvector, gen, gdn,
    xp, xs, xh, xc, d1, xd, xz4, xz3, xz2, xz1,
    pz1, pz2, pz3, pu3, pu2, pu1, z1, z2, z3, z4, du_c, du_f, pre_ref, al_ref, pg_ref, ug_ref, dt, gg, cg,
    dzf, dzc, fs, fr, st, tt, norm_all, st_g, rows_ref, turned, acc, gate_all, gate_t, gate_own, gate_block,
    wt1, wt2, wt3, wt4, wf1, wf2, wf3, wf4, wx1, wx2, wx3u, wx3g, wx4, wb1, wb2, wb3, wb4,
    gt1, gt2, gt3, gt4, gr1, gr2, gr3, gr4, ga1, ga2, ga3, ga4,
    g_send, g_recv, t_send, t_recv, f_send, f_recv, w_send, w_recv, v_send, v_recv, c_send, c_recv, r_send, r_recv, a_send, a_recv,
):
    nd, nc, S, R, H = dm.nd, dm.nc, dm.s, dm.rows, dm.half
    W, V = dm.cols, dm.hcols
    Q = H // 2
    place = lax.axis_index("depth")
    me = lax.axis_index("chan")
    first, last = place == 0, place == nd - 1
    convs = dm.convs
    pending = []

    def peer_copy(src, dst, send, recv, depth, chan):
        return pltpu.make_async_remote_copy(
            src_ref=src, dst_ref=dst, send_sem=send, recv_sem=recv,
            device_id={"depth": depth, "chan": chan}, device_id_type=MESH,
        )

    def gather_parts(ref, which, pad, sides=(1, 0, 2)):
        n = ref.shape[1] - 2
        span = pl.ds(pad, ref.shape[2] - 2 * pad)
        k = GATHERS.index(which)
        other = me + 1 - 2 * lax.rem(me, 2)
        parts = []
        for side, own, theirs, size in ((1, 1, 1, n), (0, n, 0, 1), (2, 1, n + 1, 1)):
            step = 1 - side
            if side not in sides:
                continue
            can_send = (jnp.logical_not(last), None, jnp.logical_not(first))[side]
            can_recv = (jnp.logical_not(first), None, jnp.logical_not(last))[side]
            for t in range(nc // 2):
                to, source = lax.rem(me + 2 * t, nc), lax.rem(me + nc - 2 * t, nc)
                mate = lax.rem(other + nc - 2 * t, nc)
                i = side * (nc // 2) + t

                def copy(own, block, at, hop, depth, chan, size=size, i=i):
                    return peer_copy(
                        ref.at[block, pl.ds(own, size), span],
                        ref.at[block, pl.ds(at, size), span],
                        g_send.at[k, hop, i], g_recv.at[k, hop, i], depth, chan,
                    )

                mine = side == 1 and t == 0
                out = None if mine else functools.partial(copy, own, me, theirs, 0, place + step, to)
                back = None if mine else functools.partial(copy, theirs, source, theirs, 0, place, source)
                on = functools.partial(copy, theirs, source, theirs, 1, place, other)
                mates = functools.partial(copy, theirs, mate, theirs, 1, place, other)
                parts.append((can_send, can_recv, out, back, on, mates))
        return parts

    def drain():
        for cond, fn in pending:
            guarded(cond, fn)
        pending.clear()

    def guarded(cond, fn):
        if cond is None:
            fn()
        else:
            pl.when(cond)(fn)

    def gather_start(ref, which, pad):
        for can_send, can_recv, out, _, on, _ in gather_parts(ref, which, pad):
            if out is None:
                out = on
            guarded(can_send, lambda out=out: out().start())
            pending.append((can_send, lambda out=out: out().wait_send()))

    def gather_pass(*where):
        for _, can_recv, out, back, on, _ in gather_parts(*where):
            if out is not None:

                def relay(back=back, on=on):
                    back().wait_recv()
                    on().start()

                guarded(can_recv, relay)

    def gather_passed(*where):
        for _, can_recv, out, _, on, _ in gather_parts(*where):
            if out is not None:
                pending.append((can_recv, lambda on=on: on().wait_send()))

    def gather_wait(*where):
        for _, can_recv, _, _, _, mates in gather_parts(*where):
            guarded(can_recv, lambda mates=mates: mates().wait_recv())

    def sum_copy(ref, k, slot, t):
        return peer_copy(
            ref.at[slot, place], ref.at[slot, place], t_send.at[k, t], t_recv.at[k, t], lax.rem(place + t, nd), me
        )

    def sum_start(ref, k, slot, tile):
        ref[slot, place] = tile

        def send(t, _):
            sum_copy(ref, k, slot, t).start()
            return _

        def sent(t, _):
            sum_copy(ref, k, slot, t).wait_send()
            return _

        lax.fori_loop(1, nd, send, 0)
        pending.append((None, lambda: lax.fori_loop(1, nd, sent, 0)))

    def sum_finish(ref, k, slot):
        def receive(t, _):
            source = lax.rem(place + nd - t, nd)
            peer_copy(
                ref.at[slot, source], ref.at[slot, source], t_send.at[k, t], t_recv.at[k, t], source, me
            ).wait_recv()
            return _

        lax.fori_loop(1, nd, receive, 0)
        return jnp.sum(ref[slot], axis=0)

    def totals(k, slot, m):
        return columns_of(sum_finish(st, k, slot), m)

    def totals_start(k, slot):
        tt[slot, me] = sum_finish(st, k, slot)
        for t in range(1, nc):
            out = functools.partial(
                peer_copy, tt.at[slot, me], tt.at[slot, me], c_send.at[k, t], c_recv.at[k, t], place, lax.rem(me + t, nc)
            )
            out().start()
            pending.append((None, lambda out=out: out().wait_send()))

    def totals_wait(k, slot):
        for t in range(1, nc):
            source = lax.rem(me + nc - t, nc)
            theirs = tt.at[slot, source]
            peer_copy(theirs, theirs, c_send.at[k, t], c_recv.at[k, t], place, source).wait_recv()

    def columns_of(row, m):
        lane, channel = iota((m, LANES), 1), iota((m, LANES), 0)
        return tuple(
            jnp.sum(jnp.where(lane == channel + i * m, row, 0.0), axis=1, keepdims=True) for i in range(2)
        )

    def turn_in(w, cv):
        eye = (iota((LANES, LANES), 0) == iota((LANES, LANES), 1)).astype(BF16)

        def chunk(a):
            return dot_nt(eye, jnp.concatenate([a] * cv.per, 0).astype(BF16))

        full = cv.length // LANES

        def body(i, carry):
            at = pl.multiple_of(i * LANES, LANES)
            turned[pl.ds(at, LANES)] = chunk(w[:, pl.ds(at, LANES)])
            return carry

        lax.fori_loop(0, full, body, 0, unroll=4)
        if full < cv.chunks:
            a = w[:, full * LANES :]
            a = jnp.concatenate([a, jnp.zeros((cv.o, LANES - a.shape[1]), F32)], 1)
            turned[full * LANES : (full + 1) * LANES] = chunk(a)

    def prepare(k):
        cv, w, wt, wf = convs[k], (w1, w2, w3, w4)[k], (wt1, wt2, wt3, wt4)[k], (wf1, wf2, wf3, wf4)[k]
        turn_in(w, cv)
        group = iota((cv.c, LANES), 1) // cv.o
        for kz in range(3):
            for j in range(cv.tiles):
                tile = None
                for g in range(cv.per):
                    t = j * cv.per + g
                    if t < 9:
                        v = turned[pl.ds(9 * kz + t, cv.c, stride=27)]
                        tile = v if tile is None else jnp.where(group == g, v, tile)
                wt[kz, :, j * LANES : (j + 1) * LANES] = tile.astype(BF16).astype(wt.dtype)
        eye = (iota((LANES, LANES), 0) == iota((LANES, LANES), 1)).astype(BF16)
        for j in range(cv.tiles):
            v = jnp.concatenate([wt[kz, :, j * LANES : (j + 1) * LANES] for kz in range(3)], 0)
            size = min(LANES, 9 * cv.o - j * LANES)
            wf[j * LANES : j * LANES + size] = dot_nt(eye, v.astype(BF16))[0:size].astype(BF16)

    def weight_parts(k):
        cv, wt = convs[k], (wt1, wt2, wt3, wt4)[k]
        into = ((wx1,), (wx2,), (wx3u, wx3g), (wx4,))[k]
        parts = []
        for b, (size, start) in enumerate(cv.blocks):
            for t in range(1, nc):
                to, source = lax.rem(me + t, nc), lax.rem(me + nc - t, nc)
                at = start(to)
                sems = (w_send.at[k, b, t], w_recv.at[k, b, t])
                out = lambda b=b, at=at, size=size, to=to, sems=sems: peer_copy(
                    wt.at[:, pl.ds(at, size)], into[b].at[me], *sems, place, to
                )
                back = lambda b=b, source=source, sems=sems: peer_copy(
                    into[b].at[source], into[b].at[source], *sems, place, source
                )
                parts.append((out, back))
        return parts

    def weights_start(k):
        cv, wt = convs[k], (wt1, wt2, wt3, wt4)[k]
        into = ((wx1,), (wx2,), (wx3u, wx3g), (wx4,))[k]
        for b, (size, start) in enumerate(cv.blocks):
            into[b][me] = wt[:, pl.ds(start(me), size)]
        for out, _ in weight_parts(k):
            out().start()
            pending.append((None, lambda out=out: out().wait_send()))

    def weights_finish(k):
        cv = convs[k]
        into = ((wx1,), (wx2,), (wx3u, wx3g), (wx4,))[k]
        out = (wb1, wb2, wb3, wb4)[k]
        every = sum(size for size, _ in cv.blocks)
        offset = 0
        for _, back in weight_parts(k):
            back().wait_recv()
        for b, (size, _) in enumerate(cv.blocks):
            for t in range(9):
                pieces = [
                    into[b][j, 2 - kz, :, t * cv.o : (t + 1) * cv.o].astype(F32)
                    for kz in range(3)
                    for j in range(nc)
                ]
                at = (8 - t) * every + offset
                out[at : at + size] = jnp.concatenate(pieces, 1).astype(BF16)
            offset += size

    def reduce_copy(k, t):
        cv, gt, gr = convs[k], (gt1, gt2, gt3, gt4)[k], (gr1, gr2, gr3, gr4)[k]
        to = lax.rem(place + t, nd)
        return peer_copy(
            gt.at[pl.ds(to * cv.share, cv.share)], gr.at[place], r_send.at[k, t], r_recv.at[k, t], to, me
        )

    def reduce_start(k):
        cv, gt, gr = convs[k], (gt1, gt2, gt3, gt4)[k], (gr1, gr2, gr3, gr4)[k]

        def tile(i, carry):
            for j in range(cv.tiles):
                at = pl.multiple_of(i * 16, 16)
                gt[i * cv.tiles + j] = acc[pl.ds(at, 16), j * LANES : (j + 1) * LANES].astype(BF16)
            return carry

        lax.fori_loop(0, 3 * cv.c // 16, tile, 0, unroll=4)
        for i in range(cv.count, cv.share * nd):
            gt[i] = jnp.zeros((16, LANES), BF16)
        gr[place] = gt[pl.ds(place * cv.share, cv.share)]

        def send(t, _):
            reduce_copy(k, t).start()
            return _

        def sent(t, _):
            reduce_copy(k, t).wait_send()
            return _

        lax.fori_loop(1, nd, send, 0)
        pending.append((None, lambda: lax.fori_loop(1, nd, sent, 0)))

    def share_copy(k, t):
        cv, ga = convs[k], (ga1, ga2, ga3, ga4)[k]
        own = ga.at[pl.ds(place * cv.share, cv.share)]
        return peer_copy(own, own, a_send.at[k, t], a_recv.at[k, t], lax.rem(place + t, nd), me)

    def reduce_finish(k):
        cv, gr, ga = convs[k], (gr1, gr2, gr3, gr4)[k], (ga1, ga2, ga3, ga4)[k]

        def receive(t, _):
            source = lax.rem(place + nd - t, nd)
            peer_copy(gr.at[source], gr.at[source], r_send.at[k, t], r_recv.at[k, t], source, me).wait_recv()
            return _

        lax.fori_loop(1, nd, receive, 0)
        ga[pl.ds(place * cv.share, cv.share)] = jnp.sum(gr[...].astype(F32), axis=0).astype(BF16)

        def send(t, _):
            share_copy(k, t).start()
            return _

        def sent(t, _):
            share_copy(k, t).wait_send()
            return _

        lax.fori_loop(1, nd, send, 0)
        pending.append((None, lambda: lax.fori_loop(1, nd, sent, 0)))

    def gradient_out(k):
        cv, ga, out = convs[k], (ga1, ga2, ga3, ga4)[k], (g1, g2, g3, g4)[k]

        def receive(t, _):
            source = lax.rem(place + nd - t, nd)
            theirs = ga.at[pl.ds(source * cv.share, cv.share)]
            peer_copy(theirs, theirs, a_send.at[k, t], a_recv.at[k, t], source, me).wait_recv()
            return _

        lax.fori_loop(1, nd, receive, 0)
        group = iota((16, LANES), 1) // cv.o

        def scatter(i, carry):
            for kz in range(3):
                for j in range(cv.tiles):
                    v = ga[(kz * (cv.c // 16) + i) * cv.tiles + j].astype(F32)
                    for g in range(cv.per):
                        t = j * cv.per + g
                        if t < 9:
                            turned[pl.ds(9 * kz + t + i * (16 * 27), 16, stride=27)] = jnp.where(group == g, v, 0.0)
            return carry

        lax.fori_loop(0, cv.c // 16, scatter, 0, unroll=2)

        pick = (iota((cv.o, LANES), 1) % cv.o == iota((cv.o, LANES), 0)).astype(BF16)
        step = 8 * LANES
        for at in range(0, cv.length, step):
            size = min(step, cv.length - at)
            v = dot_nt(pick, turned[at : at + -(-size // LANES) * LANES].astype(BF16))
            out[:, at : at + size] = v[:, 0:size]

    def column(row):
        n = row.shape[1]
        eye = iota((n, n), 0) == iota((n, n), 1)
        return jnp.sum(jnp.where(eye, row, 0.0), axis=1, keepdims=True)

    def row_of(col):
        n = col.shape[0]
        eye = iota((n, n), 0) == iota((n, n), 1)
        return jnp.sum(jnp.where(eye, col, 0.0), axis=0, keepdims=True)

    def clear_edges(ref):
        if len(ref.shape) == 5:
            for j in range(nc):
                clear_edges(ref.at[j])
            return
        blank = jnp.zeros(ref.shape[2:], ref.dtype)
        for s in range(ref.shape[0]):
            ref[s, 0] = blank
            ref[s, ref.shape[1] - 1] = blank

    def clear_slice(ref, s):
        for j in range(nc):
            ref[j, s] = jnp.zeros(ref.shape[2:], ref.dtype)

    def clear_halos(ref):
        pl.when(first)(lambda: clear_slice(ref, 0))
        pl.when(last)(lambda: clear_slice(ref, ref.shape[1] - 1))

    def conv(ref, weight, slices, rows, m, n, width, emit, init, late=None):
        per = rows // n

        def body(i, carry):
            if late is not None:
                pl.when(i == (slices - 1) * per - 1)(late[0])
                pl.when(i == (slices - 1) * per)(late[1])
            d = i // per
            r0 = (i - d * per) * n
            x = jnp.concatenate(
                [
                    jnp.concatenate([flat(ref, d + kz, r0 + j) for j in range(n + 2)], 1)
                    for kz in range(3)
                ],
                0,
            )
            y = dot(weight[...], x)
            results = []
            for j in range(n):
                acc = []
                for kx in range(3):
                    terms = [
                        y[(3 * ky + kx) * m : (3 * ky + kx + 1) * m, (j + ky) * LANES : (j + ky + 1) * LANES]
                        for ky in range(3)
                    ]
                    acc.append(terms[0] + terms[1] + terms[2])
                results.append(from_left(acc[0], width) + acc[1] + from_right(acc[2], width))
            return emit(d, r0, results, carry)

        return lax.fori_loop(0, slices * per, body, init)

    def weight_grad(ref, dz, k, slices, rows, n):
        per = rows // n
        cv = convs[k]
        acc[0 : 3 * cv.c, 0 : cv.wide] = jnp.zeros((3 * cv.c, cv.wide), F32)

        def body(i, carry):
            d = i // per
            r0 = (i - d * per) * n
            x = jnp.concatenate(
                [
                    jnp.concatenate([flat(ref, d + kz, r0 + 1 + j) for j in range(n)], 1)
                    for kz in range(3)
                ],
                0,
            )
            y = jnp.concatenate(
                [
                    jnp.concatenate([dz[kx, d, r0 + j + 2 - ky] for j in range(n)], 1)
                    for ky in range(3)
                    for kx in range(3)
                ],
                0,
            ).astype(BF16)
            acc[0 : 3 * cv.c, 0 : 9 * cv.o] += dot_nt(x, y)
            return carry

        lax.fori_loop(0, slices * per, body, 0)

    def conv_coarse(ref, weight, m):
        x = jnp.concatenate(
            [jnp.concatenate([flat(ref, kz, i) for i in range(Q)], 1) for kz in range(3)], 0
        )
        y = dot(weight[...], x)
        blank = jnp.zeros((m, LANES), F32)

        def shifted(ky, i):
            if not 0 <= i < Q:
                return blank
            a, b, c = (
                y[(3 * ky + kx) * m : (3 * ky + kx + 1) * m, i * LANES : (i + 1) * LANES] for kx in range(3)
            )
            return from_left(a, V) + b + from_right(c, V)

        before = [shifted(0, i) for i in range(-1, Q)]
        after = [shifted(2, i) for i in range(Q + 1)]
        return [
            shifted(1, i) + halves(before[i + 1] + after[i + 1], before[i] + after[i]) for i in range(Q)
        ]

    def conv_stats_coarse(ref, weight, z, m):
        total = square = jnp.zeros((m, LANES), F32)
        for i, v in enumerate(conv_coarse(ref, weight, m)):
            z[i] = v
            total, square = total + v, square + v * v
        return total, square

    def weight_grad_coarse(ref, k):
        cv = convs[k]
        x = jnp.concatenate(
            [jnp.concatenate([flat(ref, kz, i) for i in range(Q)], 1) for kz in range(3)], 0
        )
        y = jnp.concatenate([jnp.concatenate([dzc[t, i] for i in range(Q)], 1) for t in range(9)], 0)
        acc[0 : 3 * cv.c, 0 : 9 * cv.o] = dot_nt(x, y.astype(BF16))

    def shifted_copies(z, given):
        mean, scale, level, slope = given
        rows = []
        for i in range(Q):
            v = scale * du_c[i] + level + slope * (z[i] - mean)
            rows.append(v.astype(BF16).astype(F32))
        blank = jnp.zeros_like(rows[0])
        rows = [blank] + rows + [blank]
        for i in range(Q):
            before, here, after = rows[i : i + 3]
            for ky, v in enumerate((halves(after, here), here, halves(here, before))):
                for kx, u in enumerate((from_right(v, V), v, from_left(v, V))):
                    dzc[3 * ky + kx, i] = u.astype(dzc.dtype)

    def conv_stats(ref, weight, z, slices, rows, m, n, width, late=None):
        def emit(d, r0, results, carry):
            total, square = carry
            for j, v in enumerate(results):
                z[d * rows + r0 + j] = v
                total, square = total + v, square + v * v
            return total, square

        blank = jnp.zeros((m, LANES), F32)
        return conv(ref, weight, slices, rows, m, n, width, emit, (blank, blank), late)

    def pack(a, b):
        m = a.shape[0]
        a = jnp.sum(a, axis=1, keepdims=True)
        b = jnp.sum(b, axis=1, keepdims=True)
        lane, channel = iota((m, LANES), 1), iota((m, LANES), 0)
        both = jnp.where(lane == channel, a, jnp.where(lane == channel + m, b, 0.0))
        return jnp.sum(both, axis=0, keepdims=True)

    def moments(total, count):
        mean = total[0] / count
        var = total[1] / count - mean * mean
        return mean, lax.rsqrt(var + EPS)

    def wide(column):
        return jnp.broadcast_to(column, (column.shape[0], LANES))

    def factors(stats, norm):
        mean, inv = stats
        gain, shift = norm
        return wide(mean), wide(gain * inv), wide(shift)

    def norm_rows(z, stats, norm, emit, n):
        mean, scale, shift = factors(stats, norm)

        def body(i, carry):
            for j in range(n):
                p = i * n + j
                u = (z[p] - mean) * scale + shift
                emit(p, u * jax.nn.sigmoid(u))
            return carry

        lax.fori_loop(0, z.shape[0] // n, body, 0)

    def norm_back_sums(z, keep_du, stats, norm, grad, n):
        mean, scale, shift = factors(stats, norm)
        inv = wide(stats[1])
        m = z.shape[1]

        def body(i, carry):
            a, b = carry
            for j in range(n):
                p = i * n + j
                centred = z[p] - mean
                u = centred * scale + shift
                sigma = jax.nn.sigmoid(u)
                v = grad(p) * sigma * (1.0 + u * (1.0 - sigma))
                keep_du(p, v)
                a, b = a + v, b + v * (centred * inv)
            return a, b

        blank = jnp.zeros((m, LANES), F32)
        return lax.fori_loop(0, z.shape[0] // n, body, (blank, blank))

    def back_factors(stats, norm, total, count):
        mean, inv = stats
        scale = norm[0] * inv
        return wide(mean), wide(scale), wide(-scale * total[0] / count), wide(-scale * inv * total[1] / count)

    def norm_back(z, du, given, x, rows, width, n):
        mean, scale, level, slope = given
        per = rows // n

        def body(i, carry):
            d = i // per
            r0 = (i - d * per) * n
            for j in range(n):
                r = r0 + j
                v = scale * du(d, r) + level + slope * (z(d, r) - mean)
                low = v.astype(BF16)
                if x is not None:
                    x[me, 1 + d, 1 + r] = low.astype(x.dtype)
                v = low.astype(F32)
                dzf[0, d, 1 + r] = from_right(v, width).astype(dzf.dtype)
                dzf[1, d, 1 + r] = low.astype(dzf.dtype)
                dzf[2, d, 1 + r] = from_left(v, width).astype(dzf.dtype)
            return carry

        lax.fori_loop(0, S * per, body, 0)

    def norm_cols(j, layer, m):
        return column(norm_all[j, 2 * layer : 2 * layer + 1, 0:m]), column(norm_all[j, 2 * layer + 1 : 2 * layer + 2, 0:m])

    def each_row(s0, s1, rows, n, fn):
        per = rows // n

        def body(i, carry):
            s = s0 + i // per
            r0 = (i - (i // per) * per) * n
            for q in range(n):
                fn(s, r0 + q)
            return carry

        lax.fori_loop(0, (s1 - s0) * per, body, 0)

    def norm_blocks(z, dst, pad, slot, layer, m, count, s0, s1, n):
        rows = z.shape[2] - 1
        for j in range(nc):
            mean, scale, shift = factors(moments(columns_of(tt[slot, j], m), count), norm_cols(j, layer, m))

            def one(s, r, j=j, mean=mean, scale=scale, shift=shift):
                centred = z[j, s, r].astype(F32) + (z[j, s, rows].astype(F32) - mean)
                u = centred * scale + shift
                dst[j, s, r + pad] = (u * jax.nn.sigmoid(u)).astype(BF16).astype(dst.dtype)

            each_row(s0, s1, rows, n, one)

    def back_blocks(z, du, dst, pad, slot, back_slot, layer, m, count, s0, s1, n):
        rows = z.shape[2] - 1
        for j in range(nc):
            stats = moments(columns_of(tt[slot, j], m), count)
            given = back_factors(stats, norm_cols(j, layer, m), columns_of(tt[back_slot, j], m), count)

            spread_by = wide(norm_cols(j, layer, m)[0] * stats[1] * stats[1])

            def one(s, r, j=j, given=given, spread_by=spread_by):
                mean, scale, level, slope = given
                if du.shape[2] > rows:
                    level = level + scale * du[j, s, rows].astype(F32)
                    slope = slope + spread_by * du[j, s, rows + 1].astype(F32)
                centred = z[j, s, r].astype(F32) + (z[j, s, rows].astype(F32) - mean)
                v = scale * du[j, s, r].astype(F32) + level + slope * centred
                dst[j, s, r + pad] = v.astype(BF16).astype(dst.dtype)

            each_row(s0, s1, rows, n, one)

    hc = iota((LANES, LANES), 0)
    fc = iota((LANES, LANES), 1)
    half = LANES // 2

    def up_table(coarse, fine):
        base = fine // 2
        other = jnp.clip(base + jnp.where(fine % 2 == 0, -1, 1), 0, V - 1)
        near = (coarse == base).astype(F32)
        far = (coarse == other).astype(F32)
        return (0.75 * near + 0.25 * far).astype(BF16)

    pool = jnp.concatenate([(hc // 2 == fc - at).astype(BF16) for at in (0, half)], 0)
    spread = jnp.concatenate([(hc - at == fc // 2).astype(BF16) for at in (0, half)], 1)
    up = jnp.concatenate([up_table(hc - at, fc) for at in (0, half)], 1)
    down = jnp.concatenate([up_table(fc - at, hc) for at in (0, 0, half, half)], 0)
    spread2 = jnp.concatenate([spread, spread], 0)

    def take_rows(ref):
        for c in range(dm.cs):
            rows_ref[c * S * R : (c + 1) * S * R] = ref[c].astype(F32).reshape(S * R, LANES)

    def row(p):
        return rows_ref[pl.ds(p, dm.cs, stride=S * R)]

    barrier = pltpu.get_barrier_semaphore()

    def greet(depth, chan):
        pl.semaphore_signal(barrier, inc=1, device_id={"depth": depth, "chan": chan}, device_id_type=MESH)

    for t in range(1, nc):
        greet(place, lax.rem(me + t, nc))

    def greet_slab(t, _):
        greet(lax.rem(place + t, nd), me)
        return _

    lax.fori_loop(1, nd, greet_slab, 0)
    for t in range(1, nc // 2):
        to = lax.rem(me + 2 * t, nc)
        pl.when(jnp.logical_not(first))(lambda to=to: greet(place - 1, to))
        pl.when(jnp.logical_not(last))(lambda to=to: greet(place + 1, to))
    clear_halos(xp)
    take_rows(skip_ref)

    def take_skip(i, carry):
        parts = []
        for s in range(S):
            v = [row(s * R + 4 * i + j).astype(BF16) for j in range(4)]
            for j in range(4):
                xs[me, 1 + s, 4 * i + j] = v[j].astype(xs.dtype)
            parts += [jnp.concatenate([v[j], v[2 + j]], 1) for j in range(2)]
        v = dot(jnp.concatenate(parts, 0), pool).reshape(2 * S, dm.cs, LANES)
        xp[me, 1, i] = (jnp.sum(v, axis=0) * 0.125).astype(BF16).astype(xp.dtype)
        return carry

    lax.fori_loop(0, Q, take_skip, 0, unroll=3)
    clear_halos(xs)
    beside = jnp.where(first, 0, 1) + jnp.where(last, 0, 1)
    pl.semaphore_wait(barrier, nc - 1 + nd - 1 + (nc // 2 - 1) * beside)
    gather_start(xp, "pooled", 0)
    gather_start(xs, "skip", 0)

    gq = dm.g // nc
    gate_all[me, :, 0 : gate_ref.shape[1]] = gate_ref[...]
    lane = iota((gq, LANES), 1)
    gate_all[me, :, 2 * LANES :] = jnp.where(
        lane == 0, column(vector_ref[0:1]), jnp.where(lane == 1, column(vector_ref[1:2]), 0.0)
    )
    for i, (ref, width) in enumerate(((en_ref, dm.ce), (dn_ref, dm.cd))):
        for layer in range(2):
            for part in range(2):
                at = 4 * i + 2 * layer + part
                norm_all[me, at : at + 1, 0:width] = ref[part, layer : layer + 1]

    def constants(i, t, source, to):
        ref = (norm_all, gate_all)[i]
        return peer_copy(ref.at[source], ref.at[source], v_send.at[i, t], v_recv.at[i, t], place, to)

    def constants_wait(i):
        for t in range(1, nc):
            source = lax.rem(me + nc - t, nc)
            constants(i, t, source, source).wait_recv()

    for i in range(2):
        for t in range(1, nc):
            out = functools.partial(constants, i, t, me, lax.rem(me + t, nc))
            out().start()
            pending.append((None, lambda out=out: out().wait_send()))

    prepare(0)
    for ref in (xd, d1, xz4, xz3):
        clear_edges(ref)
    clear_halos(xz4)
    for kx in range(3):
        for s in range(S):
            dzf[kx, s, 0] = jnp.zeros(dzf.shape[3:], dzf.dtype)
            dzf[kx, s, R + 1] = jnp.zeros(dzf.shape[3:], dzf.dtype)

    def norm_of(ref, layer):
        return column(ref[0, layer : layer + 1]), column(ref[1, layer : layer + 1])

    norm_e1, norm_e2 = norm_of(en_ref, 0), norm_of(en_ref, 1)
    norm_d1, norm_d2 = norm_of(dn_ref, 0), norm_of(dn_ref, 1)

    def send_z(z, total, ref, which, n):
        rows = ref.shape[2] - 1
        slabs = ref.shape[1] - 2
        level = wide(jnp.sum(total, axis=1, keepdims=True) / (slabs * rows * LANES)).astype(BF16)
        for d in range(slabs):
            ref[me, 1 + d, rows] = level.astype(ref.dtype)
        level = level.astype(F32)

        def store(s, r):
            ref[me, s, r] = (z[(s - 1) * rows + r] - level).astype(BF16).astype(ref.dtype)

        each_row(1, 1 + slabs, rows, n, store)
        gather_start(ref, which, 0)

    gather_pass(xp, "pooled", 0)
    gather_wait(xp, "pooled", 0)
    sums = conv_stats_coarse(xp, wf1, z1, dm.ce)
    sum_start(st, 0, 0, pack(*sums))
    send_z(z1, sums[0], pz1, "z1", Q)
    prepare(1)
    constants_wait(0)
    totals_start(0, 0)
    gather_pass(pz1, "z1", 0)
    totals_wait(0, 0)
    gather_wait(pz1, "z1", 0)
    norm_blocks(pz1, xh, 0, 0, 0, dm.ce, dm.coarse_total, 0, 3, Q)
    clear_halos(xh)
    sums = conv_stats_coarse(xh, wf2, z2, dm.ce)
    sum_start(st, 1, 1, pack(*sums))
    send_z(z2, sums[0], pz2, "z2", Q)
    gather_pass(xs, "skip", 0)
    totals_start(1, 1)
    gather_pass(pz2, "z2", 0)
    prepare(2)
    totals_wait(1, 1)
    gather_wait(pz2, "z2", 0)
    for k in (2, 1, 0):
        weights_start(k)
    norm_blocks(pz2, xc, 0, 1, 1, dm.ce, dm.coarse_total, 0, 3, Q)
    constants_wait(1)
    gate_full = gate_all[...].reshape(dm.g, 3 * LANES)
    wg = gate_full[:, 0 : dm.enc_all + dm.skip_all].astype(BF16)
    gbias = gate_full[:, 2 * LANES : 2 * LANES + 1]
    gout = gate_full[:, 2 * LANES + 1 : 2 * LANES + 2]
    gate_t[...] = jnp.transpose(gate_full[:, 0 : 2 * LANES])
    gate_own[...] = jnp.concatenate(
        [
            gate_t[pl.ds(pl.multiple_of(me * dm.ce, dm.ce), dm.ce)],
            gate_t[pl.ds(pl.multiple_of(dm.enc_all + me * dm.cs, dm.cs), dm.cs)],
        ],
        0,
    )

    def up_depth(i, carry):
        t = []
        for s in range(3):
            v = dot(flat(xc, s, i), up)
            t.append(jnp.stack([v[:, 0:LANES], v[:, LANES:]], 0))
        below = jnp.where(first, t[1], t[0])
        above = jnp.where(last, t[1], t[2])
        near = 0.75 * t[1]
        here = 0.25 * t[1]
        rows = pl.ds(i * 2, 2)
        dt[0, rows] = jnp.where(first, 0.0, 0.75 * below + here)
        dt[1, rows] = near + 0.25 * below
        dt[2, rows] = near + 0.25 * above
        dt[3, rows] = jnp.where(last, 0.0, 0.75 * above + here)
        return carry

    lax.fori_loop(0, Q, up_depth, 0)

    def up_rows(i, carry):
        before, after = jnp.maximum(i - 1, 0), jnp.minimum(i + 1, H - 1)
        for s in range(S + 2):
            v = 0.75 * dt[s, i]
            d1[s, 1 + 2 * i, 0 : dm.enc_all] = (v + 0.25 * dt[s, before]).astype(BF16)
            d1[s, 2 + 2 * i, 0 : dm.enc_all] = (v + 0.25 * dt[s, after]).astype(BF16)
        return carry

    lax.fori_loop(0, H, up_rows, 0)

    gather_wait(xs, "skip", 0)
    gate_n = 12

    def gate(i, carry):
        s = i // (R // gate_n)
        r0 = (i - s * (R // gate_n)) * gate_n
        skips = [flat(xs, s, r0 + j) for j in range(gate_n)]
        x = jnp.concatenate(
            [
                jnp.concatenate([d1[s, 1 + r0 + j, 0 : dm.enc_all] for j in range(gate_n)], 1),
                jnp.concatenate(skips, 1),
            ],
            0,
        )
        pre = dot(wg, x) + gbias
        act = pre * jax.nn.sigmoid(pre)
        alpha = jax.nn.sigmoid(jnp.sum(gout * act, axis=0, keepdims=True))
        for j in range(gate_n):
            lanes = slice(j * LANES, (j + 1) * LANES)
            d1[s, 1 + r0 + j, dm.enc_all :] = (alpha[:, lanes] * skips[j].astype(F32)).astype(BF16)
            pre_ref[s, r0 + j] = pre[:, lanes]
            al_ref[s, r0 + j] = alpha[:, lanes]
        return carry

    lax.fori_loop(0, (S + 2) * R // gate_n, gate, 0)

    sums = conv_stats(d1, wf3, z3, S, R, dm.cd, 12, W)
    sum_start(st, 4, 4, pack(*sums))
    send_z(z3, sums[0], pz3, "z3", R)
    prepare(3)
    weights_start(3)
    totals_start(4, 4)
    take_rows(cot_ref)
    drain()
    gather_pass(pz3, "z3", 0, (1, 0))
    totals_wait(4, 4)
    gather_wait(pz3, "z3", 0, (1, 0))

    def norm_slices(s0, s1):
        norm_blocks(pz3, xd, 1, 4, 2, dm.cd, dm.fine_total, s0, s1, R)

    norm_slices(0, S + 1)
    pl.when(first)(lambda: clear_slice(xd, 0))

    def last_hidden():
        gather_wait(pz3, "z3", 0, (2,))
        norm_slices(S + 1, S + 2)
        pl.when(last)(lambda: clear_slice(xd, S + 1))

    late = (lambda: gather_pass(pz3, "z3", 0, (2,)), last_hidden)
    sum_start(st, 5, 5, pack(*conv_stats(xd, wf4, z4, S, R, dm.cd, 12, W, late)))
    stats_d2 = moments(totals(5, 5, dm.cd), dm.fine_total)

    def keep_du(p, v):
        du_f[p] = v

    sum_start(st, 6, 6, pack(*norm_back_sums(z4, keep_du, stats_d2, norm_d2, row, R)))

    def keep_result(p, v):
        out_ref[pl.ds(pl.multiple_of(p * dm.cd, dm.cd), dm.cd)] = v

    norm_rows(z4, stats_d2, norm_d2, keep_result, R)
    total_d2 = totals(6, 6, dm.cd)
    given = back_factors(stats_d2, norm_d2, total_d2, dm.fine_total)
    norm_back(lambda d, r: z4[d * R + r], lambda d, r: du_f[d * R + r], given, xz4, R, W, 12)
    gather_start(xz4, "dz4", 1)
    weight_grad(xd, dzf, 3, S, R, 12)
    reduce_start(3)
    weights_finish(3)
    weights_finish(2)
    gather_pass(xz4, "dz4", 1, (1, 0))
    gather_wait(xz4, "dz4", 1, (1, 0))

    def keep_grad(d, r0, results, carry):
        for j, v in enumerate(results):
            gg[d * R + r0 + j] = v
        return carry

    late = (lambda: gather_pass(xz4, "dz4", 1, (2,)), lambda: gather_wait(xz4, "dz4", 1, (2,)))
    conv(xz4, wb4, S, R, dm.cd, 12, W, keep_grad, 0, late)
    stats_d1 = moments(columns_of(tt[4, me], dm.cd), dm.fine_total)

    sums = norm_back_sums(z3, keep_du, stats_d1, norm_d1, lambda p: gg[p], R)
    sum_start(st, 7, 7, pack(*sums))
    levels = [wide(jnp.sum(v, axis=1, keepdims=True) / (S * R * LANES)).astype(BF16) for v in sums]
    for d in range(S):
        for i in range(2):
            pu3[me, 1 + d, R + i] = levels[i].astype(pu3.dtype)
    own_level, own_slope = (v.astype(F32) for v in levels)
    own_slope = own_slope * wide(stats_d1[1])
    own_mean = wide(stats_d1[0])

    def send_du3(s, r):
        p = (s - 1) * R + r
        v = du_f[p] - own_level - own_slope * (z3[p] - own_mean)
        pu3[me, s, r] = v.astype(BF16).astype(pu3.dtype)

    each_row(1, 1 + S, R, R, send_du3)
    gather_start(pu3, "du3", 0)
    reduce_finish(3)
    totals_start(7, 7)
    total_d1 = columns_of(tt[7, me], dm.cd)
    given = back_factors(stats_d1, norm_d1, total_d1, dm.fine_total)
    norm_back(lambda d, r: z3[d * R + r], lambda d, r: du_f[d * R + r], given, None, R, W, 12)
    weight_grad(d1, dzf, 2, S, R, 12)
    gather_pass(pu3, "du3", 0, (1, 0))
    reduce_start(2)
    gradient_out(3)
    weights_finish(1)
    weights_finish(0)
    totals_wait(7, 7)
    gather_wait(pu3, "du3", 0, (1, 0))

    def back_slices(s0, s1):
        back_blocks(pz3, pu3, xz3, 1, 4, 7, 2, dm.cd, dm.fine_total, s0, s1, R)

    back_slices(0, S + 1)
    pl.when(first)(lambda: clear_slice(xz3, 0))

    def last_dz():
        gather_wait(pu3, "du3", 0, (2,))
        back_slices(S + 1, S + 2)
        pl.when(last)(lambda: clear_slice(xz3, S + 1))

    late = (lambda: gather_pass(pu3, "du3", 0, (2,)), last_dz)

    def gate_back(d, r0, results, carry):
        bias, psi = carry
        lows = []
        for j, both in enumerate(results):
            s, r = d + 1, r0 + j
            ug_ref[d * R + r] = both[0 : dm.ce]
            v = both[dm.ce :]
            grad = jnp.sum(v * flat(xs, s, r).astype(F32), axis=0, keepdims=True)
            alpha = al_ref[s, r]
            logit = grad * alpha * (1.0 - alpha)
            pre = pre_ref[s, r]
            sigma = jax.nn.sigmoid(pre)
            psi = psi + pre * sigma * logit
            low = (logit * gout * sigma * (1.0 + pre * (1.0 - sigma))).astype(BF16)
            bias = bias + low.astype(F32)
            pg_ref[d * R + r] = low
            lows.append(low)
            for t in range(nc):
                gg[t] = v[t * dm.cs : (t + 1) * dm.cs]
            sg_at = pl.ds(pl.multiple_of((d * R + r) * dm.cs, dm.cs), dm.cs)
            sg_ref[sg_at] = alpha * gg[me]
        back = dot(gate_own[...].astype(BF16), jnp.concatenate(lows, 1))
        for j in range(len(results)):
            lanes = slice(j * LANES, (j + 1) * LANES)
            ug_ref[d * R + r0 + j] += back[0 : dm.ce, lanes]
            sg_at = pl.ds(pl.multiple_of((d * R + r0 + j) * dm.cs, dm.cs), dm.cs)
            sg_ref[sg_at] += back[dm.ce :, lanes]
        return bias, psi

    blank = jnp.zeros((dm.g, LANES), F32)
    bias, psi = conv(xz3, wb3, S, R, dm.ce + dm.skip_all, 8, W, gate_back, (blank, blank), late)

    def down_rows(i, carry):
        terms = []
        for s in range(S):
            pair = []
            for j in range(2):
                r = i * 2 + j
                near = ug_ref[s * R + 2 * r] + ug_ref[s * R + 2 * r + 1]
                far = ug_ref[s * R + jnp.minimum(2 * r + 2, R - 1)] + ug_ref[s * R + jnp.maximum(2 * r - 1, 0)]
                pair.append(split(0.75 * near + 0.25 * far))
            terms.append(jnp.concatenate(pair, 1))
        v = dot(jnp.concatenate(terms, 0), down)
        even, odd = v[0 : dm.ce], v[dm.ce :]
        fs[0, i] = (0.25 * even).astype(BF16)
        fs[1, i] = (0.25 * odd).astype(BF16)
        cg[i] = 0.75 * (even + odd) + jnp.where(first, 0.25 * even, 0.0) + jnp.where(last, 0.25 * odd, 0.0)
        return carry

    lax.fori_loop(0, Q, down_rows, 0)

    def fold(side, step):
        return peer_copy(fs.at[side], fr.at[1 - side], f_send.at[side], f_recv.at[1 - side], place + step, me)

    pl.when(jnp.logical_not(first))(lambda: fold(0, -1).start())
    pl.when(jnp.logical_not(last))(lambda: fold(1, 1).start())
    pending.append((jnp.logical_not(first), lambda: fold(0, -1).wait_send()))
    pending.append((jnp.logical_not(last), lambda: fold(1, 1).wait_send()))
    columns = gate_ref.shape[1]
    acc[0 : dm.g, 0:columns] = jnp.zeros((dm.g, columns), F32)

    weight_n = 12

    def gate_weight(i, carry):
        d = i // (R // weight_n)
        r0 = (i - d * (R // weight_n)) * weight_n
        x = jnp.concatenate(
            [
                jnp.concatenate([d1[1 + d, 1 + r0 + j, 0 : dm.enc_all] for j in range(weight_n)], 1),
                jnp.concatenate([flat(xs, 1 + d, r0 + j) for j in range(weight_n)], 1),
            ],
            0,
        )
        y = jnp.concatenate([pg_ref[d * R + r0 + j] for j in range(weight_n)], 1)
        acc[0 : dm.g, 0:columns] += dot_nt(y, x)
        return carry

    lax.fori_loop(0, S * R // weight_n, gate_weight, 0)
    lane = iota((dm.g, LANES), 1)
    vectors = jnp.where(
        lane == 0,
        jnp.sum(bias, axis=1, keepdims=True),
        jnp.where(lane == 1, jnp.sum(psi, axis=1, keepdims=True), 0.0),
    )
    for j in range(nc):
        mine = slice(j * gq, (j + 1) * gq)
        gate_block[j, :, 0:columns] = acc[mine, 0:columns]
        gate_block[j, :, columns : 2 * LANES] = jnp.zeros((gq, 2 * LANES - columns), F32)
        gate_block[j, :, 2 * LANES :] = vectors[mine]
    sum_start(st_g, 8, 0, gate_block[me])
    reduce_finish(2)

    def fold_in(side):
        peer_copy(fs.at[side], fr.at[side], f_send.at[side], f_recv.at[side], place, me).wait_recv()
        cg[...] += fr[side].astype(F32)

    pl.when(jnp.logical_not(first))(lambda: fold_in(0))
    pl.when(jnp.logical_not(last))(lambda: fold_in(1))

    stats_e1 = moments(columns_of(tt[0, me], dm.ce), dm.coarse_total)
    stats_e2 = moments(columns_of(tt[1, me], dm.ce), dm.coarse_total)

    def keep_du_in(ref):
        def store(p, v):
            ref[me, 1, p] = v.astype(BF16).astype(ref.dtype)
            du_c[p] = v

        return store

    sums = norm_back_sums(z2, keep_du_in(pu2), stats_e2, norm_e2, lambda p: cg[p], Q)
    gather_start(pu2, "du2", 0)
    sum_start(st, 2, 2, pack(*sums))

    drain()
    totals_start(2, 2)
    total_e2 = columns_of(tt[2, me], dm.ce)
    gather_pass(pu2, "du2", 0)
    shifted_copies(z2, back_factors(stats_e2, norm_e2, total_e2, dm.coarse_total))
    weight_grad_coarse(xh, 1)
    reduce_start(1)
    gradient_out(2)
    totals_wait(2, 2)
    gather_wait(pu2, "du2", 0)
    back_blocks(pz2, pu2, xz2, 0, 1, 2, 1, dm.ce, dm.coarse_total, 0, 3, Q)
    clear_halos(xz2)
    for i, v in enumerate(conv_coarse(xz2, wb2, dm.ce)):
        cg[i] = v
    sums = norm_back_sums(z1, keep_du_in(pu1), stats_e1, norm_e1, lambda p: cg[p], Q)
    gather_start(pu1, "du1", 0)
    sum_start(st, 3, 3, pack(*sums))
    reduce_finish(1)
    totals_start(3, 3)
    total_e1 = columns_of(tt[3, me], dm.ce)
    gather_pass(pu1, "du1", 0)
    shifted_copies(z1, back_factors(stats_e1, norm_e1, total_e1, dm.coarse_total))
    weight_grad_coarse(xp, 0)
    reduce_start(0)
    drain()
    totals_wait(3, 3)
    gather_wait(pu1, "du1", 0)
    back_blocks(pz1, pu1, xz1, 0, 0, 3, 0, dm.ce, dm.coarse_total, 0, 3, Q)
    reduce_finish(0)
    clear_halos(xz1)
    for i, v in enumerate(conv_coarse(xz1, wb1, dm.cs)):
        v = dot(split(v), spread2) * 0.125
        for j in range(4):
            part = v[:, (j // 2) * LANES : (j // 2 + 1) * LANES]
            for s in range(S):
                at = (s * R + 4 * i + j) * dm.cs
                sg_ref[at : at + dm.cs] += part
    gradient_out(1)
    gate_total = sum_finish(st_g, 8, 0)
    ggate[...] = gate_total[:, 0:columns]
    gvector[0:1] = row_of(gate_total[:, 2 * LANES : 2 * LANES + 1])
    gvector[1:2] = row_of(gate_total[:, 2 * LANES + 1 : 2 * LANES + 2])
    for ref, both in ((gen, (total_e1, total_e2)), (gdn, (total_d1, total_d2))):
        for layer, total in enumerate(both):
            ref[0, layer : layer + 1] = row_of(total[1])
            ref[1, layer : layer + 1] = row_of(total[0])
    gradient_out(0)
    for ref, which, pad in (
        (xp, "pooled", 0), (xs, "skip", 0), (pz1, "z1", 0), (pz2, "z2", 0), (pz3, "z3", 0),
        (xz4, "dz4", 1), (pu3, "du3", 0), (pu2, "du2", 0), (pu1, "du1", 0),
    ):
        gather_passed(ref, which, pad)
    drain()


def adamw(weight, grad, moment, square, rate):
    new_moment = 0.9 * moment + 0.1 * grad
    new_square = 0.999 * square + 0.001 * grad * grad
    moment_hat = new_moment / (1.0 - 0.9**STEP)
    square_hat = new_square / (1.0 - 0.999**STEP)
    new_weight = weight - rate * (moment_hat / (jnp.sqrt(square_hat) + 1e-08) + 0.01 * weight)
    return (new_weight, new_moment, new_square)


RATES = (CONV_RATE, CONV_RATE, GATE_RATE, VECTOR_RATE, CONV_RATE, CONV_RATE, VECTOR_RATE, VECTOR_RATE)


def update_kernel(*refs):
    n = len(RATES)
    sources, targets = refs[: 2 + 4 * n], refs[2 + 4 * n : 4 + 7 * n]
    inside, outside = refs[4 + 7 * n : 6 + 11 * n], refs[6 + 11 * n : 8 + 14 * n]
    in_sem, out_sem = refs[8 + 14 * n :]
    order = (4, 1, 0, 5, 2, 3, 6, 7)

    def load(i):
        return pltpu.make_async_copy(sources[i], inside[i], in_sem.at[i])

    def store(i):
        return pltpu.make_async_copy(outside[i], targets[i], out_sem.at[i])

    for i in (1, 0):
        load(i).start()
    for k in order:
        for part in range(4):
            load(2 + part * n + k).start()
    for i in (1, 0):
        load(i).wait()
        chans, (slabs, rows) = outside[i].shape[0], outside[i].shape[1:3]
        for c in range(chans):
            v = inside[i][pl.ds(c, slabs * rows, stride=chans)]
            outside[i][c] = v.reshape(slabs, rows, LANES).astype(outside[i].dtype)
        store(i).start()
    for k in order:
        own = [2 + part * n + k for part in range(4)]
        for i in own:
            load(i).wait()
        rows = inside[own[0]].shape[0]
        step = 8 if rows % 8 == 0 and rows > 8 else rows
        for r in range(0, rows, step):
            at = slice(r, r + step)
            new = adamw(*(inside[i][at] for i in own), RATES[k])
            for part, value in enumerate(new):
                outside[2 + 3 * k + part][at] = value
        for part in range(3):
            store(2 + 3 * k + part).start()
    for i in range(len(targets)):
        store(i).wait()


def per_device(
    skip, cotangent, enc_conv1, enc_conv2, gate_proj, gate_vector, dec_conv1, dec_conv2, enc_norms, dec_norms, *states
):
    nd, nc = lax.axis_size("depth"), lax.axis_size("chan")
    dm = Dims(nd, nc, skip.shape, enc_conv1.shape[0], dec_conv1.shape[0], gate_proj.shape[0] * nc)
    S, R, H = dm.s, dm.rows, dm.half
    cin3 = dm.enc_all + dm.skip_all

    def block_of(size):
        return (size, lambda j: pl.multiple_of(j * size, size))

    dm.convs = convs = (
        Conv(dm, dm.ce, dm.skip_all, (block_of(dm.cs),)),
        Conv(dm, dm.ce, dm.enc_all, (block_of(dm.ce),)),
        Conv(dm, dm.cd, cin3, (block_of(dm.ce), (dm.skip_all, lambda j: dm.enc_all))),
        Conv(dm, dm.cd, dm.dec_all, (block_of(dm.cd),)),
    )
    params = (enc_conv1, enc_conv2, gate_proj, gate_vector, dec_conv1, dec_conv2, enc_norms, dec_norms)
    inputs = (
        skip, cotangent, enc_conv1, enc_conv2, dec_conv1, dec_conv2, gate_proj, gate_vector, enc_norms, dec_norms
    )
    shape = jax.ShapeDtypeStruct
    outs = (
        shape((S * R * dm.cd, LANES), F32),
        shape((S * R * dm.cs, LANES), F32),
        *(shape(a.shape, F32) for a in (enc_conv1, enc_conv2, dec_conv1, dec_conv2)),
        *(shape(a.shape, F32) for a in (gate_proj, gate_vector, enc_norms, dec_norms)),
    )

    def ext(slices, rows, block):
        return pltpu.VMEM((nc, slices, rows, block, LANES), storage(block))

    def exchange(cv):
        return [pltpu.VMEM((nc, 3, size, cv.wide), cv.kind) for size, _ in cv.blocks]

    def backward(cv):
        return [pltpu.VMEM((9 * sum(size for size, _ in cv.blocks), 3 * nc * cv.o), BF16)]

    gq = dm.g // nc
    Q = H // 2
    scratch = [
        ext(3, Q, dm.cs),
        ext(S + 2, R, dm.cs),
        ext(3, Q, dm.ce),
        ext(3, Q, dm.ce),
        pltpu.VMEM((S + 2, R + 2, cin3, LANES), BF16),
        ext(S + 2, R + 2, dm.cd),
        ext(S + 2, R + 2, dm.cd),
        ext(S + 2, R + 2, dm.cd),
        ext(3, Q, dm.ce),
        ext(3, Q, dm.ce),
        ext(3, Q + 1, dm.ce),
        ext(3, Q + 1, dm.ce),
        ext(S + 2, R + 1, dm.cd),
        ext(S + 2, R + 2, dm.cd),
        ext(3, Q, dm.ce),
        ext(3, Q, dm.ce),
        pltpu.VMEM((Q, dm.ce, LANES), F32),
        pltpu.VMEM((Q, dm.ce, LANES), F32),
        pltpu.VMEM((S * R, dm.cd, LANES), F32),
        pltpu.VMEM((S * R, dm.cd, LANES), F32),
        pltpu.VMEM((Q, dm.ce, LANES), F32),
        pltpu.VMEM((S * R, dm.cd, LANES), F32),
        pltpu.VMEM((S + 2, R, dm.g, LANES), F32),
        pltpu.VMEM((S + 2, R, 1, LANES), F32),
        pltpu.VMEM((S * R, dm.g, LANES), BF16),
        pltpu.VMEM((S * R, dm.ce, LANES), F32),
        pltpu.VMEM((S + 2, H, dm.enc_all, LANES), F32),
        pltpu.VMEM((S * R, dm.cd, LANES), F32),
        pltpu.VMEM((Q, dm.ce, LANES), F32),
        pltpu.VMEM((3, S, R + 2, dm.cd, LANES), storage(dm.cd)),
        pltpu.VMEM((9, Q, dm.ce, LANES), BF16),
        pltpu.VMEM((2, Q, dm.ce, LANES), BF16),
        pltpu.VMEM((2, Q, dm.ce, LANES), BF16),
        pltpu.VMEM((8, nd, 1, LANES), F32),
        pltpu.VMEM((8, nc, 1, LANES), F32),
        pltpu.VMEM((nc, 8, LANES), F32),
        pltpu.VMEM((1, nd, gq, 3 * LANES), F32),
        pltpu.VMEM((dm.cs * S * R, LANES), F32),
        pltpu.VMEM((max(cv.chunks for cv in convs) * LANES, LANES), F32),
        pltpu.VMEM((max(3 * cv.c for cv in convs), max(cv.wide for cv in convs)), F32),
        pltpu.VMEM((nc, gq, 3 * LANES), F32),
        pltpu.VMEM((2 * LANES, dm.g), F32),
        pltpu.VMEM((dm.ce + dm.cs, dm.g), F32),
        pltpu.VMEM((nc, gq, 3 * LANES), F32),
        *(pltpu.VMEM((3, cv.c, cv.wide), cv.kind) for cv in convs),
        *(pltpu.VMEM((9 * cv.o, 3 * cv.c), BF16) for cv in convs),
        *(ref for cv in convs for ref in exchange(cv)),
        *(ref for cv in convs for ref in backward(cv)),
        *(pltpu.VMEM((cv.share * nd, 16, LANES), BF16) for cv in convs),
        *(pltpu.VMEM((nd, cv.share, 16, LANES), BF16) for cv in convs),
        *(pltpu.VMEM((cv.share * nd, 16, LANES), BF16) for cv in convs),
        *[pltpu.SemaphoreType.DMA((len(GATHERS), 2, 3 * nc // 2))] * 2,
        *[pltpu.SemaphoreType.DMA((9, nd))] * 2,
        *[pltpu.SemaphoreType.DMA((2,))] * 2,
        *[pltpu.SemaphoreType.DMA((4, 2, nc))] * 2,
        *[pltpu.SemaphoreType.DMA((2, nc))] * 2,
        *[pltpu.SemaphoreType.DMA((8, nc))] * 2,
        *[pltpu.SemaphoreType.DMA((4, nd))] * 4,
    ]
    vmem = pl.BlockSpec(memory_space=pltpu.VMEM)
    out, sg, grad1, grad2, grad3, grad4, ggate, gvector, gen, gdn = pl.pallas_call(
        functools.partial(kernel, dm),
        out_shape=outs,
        in_specs=[vmem] * len(inputs),
        out_specs=[vmem] * len(outs),
        scratch_shapes=scratch,
        compiler_params=pltpu.CompilerParams(
            has_side_effects=True, collective_id=0, vmem_limit_bytes=60 * 1024 * 1024
        ),
        name="step",
    )(*inputs)
    grads = (grad1, grad2, ggate, gvector, grad3, grad4, gen, gdn)
    operands = (out, sg, *params, *grads, *states)
    updated = (
        shape(cotangent.shape, BF16),
        shape(skip.shape, F32),
        *(shape(p.shape, F32) for p in params for _ in range(3)),
    )
    anywhere = pl.BlockSpec(memory_space=pl.ANY)
    return pl.pallas_call(
        update_kernel,
        out_shape=updated,
        in_specs=[anywhere] * len(operands),
        out_specs=[anywhere] * len(updated),
        scratch_shapes=[
            *(pltpu.VMEM(a.shape, a.dtype) for a in operands),
            *(pltpu.VMEM(a.shape, a.dtype) for a in updated),
            pltpu.SemaphoreType.DMA((len(operands),)),
            pltpu.SemaphoreType.DMA((len(updated),)),
        ],
        compiler_params=pltpu.CompilerParams(vmem_limit_bytes=60 * 1024 * 1024),
        name="update",
    )(*operands)


def solution(mesh):
    volume = P("chan", "depth", None, None)
    row, column, norms = P("chan", None), P(None, "chan"), P(None, None, "chan")
    params = (row, row, row, column, row, row, norms, norms)
    return jax.shard_map(
        per_device,
        mesh=mesh,
        in_specs=(volume, volume) + params * 3,
        out_specs=(volume, volume) + tuple(spec for spec in params for _ in range(3)),
        check_vma=False,
    )
```

```python
import functools
import types

import jax
import jax.numpy as jnp
from jax import lax
from jax.experimental import pallas as pl
from jax.experimental.pallas import tpu as pltpu
from jax.sharding import PartitionSpec as P

STEP = 5
EPS = 1e-05
CONV_RATE = 0.03
GATE_RATE = 0.1
VECTOR_RATE = 0.5
LANES = 128
MESH = pl.DeviceIdType.MESH
F32 = jnp.float32
BF16 = jnp.bfloat16


def iota(shape, dim):
    return lax.broadcasted_iota(jnp.int32, shape, dim)


def dot(a, b):
    return jnp.dot(a, b, preferred_element_type=F32)


def dot_nt(a, b):
    return lax.dot_general(a, b, (((1,), (1,)), ((), ())), preferred_element_type=F32)


def from_left(v, width):
    return jnp.where(iota(v.shape, 1) % width == 0, 0.0, pltpu.roll(v, 1, 1))


def from_right(v, width):
    return jnp.where(iota(v.shape, 1) % width == width - 1, 0.0, pltpu.roll(v, LANES - 1, 1))


def halves(low, high):
    return pltpu.roll(jnp.where(iota(low.shape, 1) < LANES // 2, low, high), LANES // 2, 1)


def split(v):
    high = v.astype(BF16)
    return jnp.concatenate([high, (v - high.astype(F32)).astype(BF16)], 1)


def storage(block):
    return BF16 if block % 16 == 0 else F32


def flat(ref, s, r):
    if len(ref.shape) == 4:
        return ref[s, r]
    v = ref[:, s, r]
    return v.reshape(v.shape[0] * v.shape[1], LANES).astype(BF16)


class Dims:
    def __init__(self, nd, nc, skip, enc, dec, gate):
        self.nd, self.nc, self.nx = nd, nc, nc // 2
        self.s, self.rows, self.cols = skip[1:]
        self.cs, self.ce, self.cd, self.g = skip[0], enc, dec, gate
        self.half, self.hcols = self.rows // 2, self.cols // 2
        self.fine_total = nd * self.s * self.rows * self.cols
        self.coarse_total = self.fine_total // 8
        self.enc_all = nc * enc
        self.skip_all = nc * skip[0]
        self.dec_all = nc * dec
        self.rb = self.rows // self.nx
        self.ext = self.rb + 2
        self.cf = self.nx * dec


GATHERS = ("pooled", "skip", "hidden", "coarse", "dz2", "dz1")
FINE = ("hidden", "dz4", "dz3")


class Conv:
    def __init__(self, dm, o, c, blocks):
        self.o, self.c, self.blocks = o, c, blocks
        self.length = 27 * c
        self.chunks = -(-self.length // LANES)
        self.per = LANES // o
        self.tiles = -(-9 // self.per)
        self.wide = self.tiles * LANES
        self.kind = storage(min(size for size, _, _ in blocks))
        self.needed = sum(size for size, _, _ in blocks)
        self.count = 3 * c // 16 * self.tiles
        self.share = -(-self.count // dm.nd)
        self.taps = 9 * o
        self.stored = -(-self.taps // 16) * 16


def kernel(dm, names, *refs):
    k_ = types.SimpleNamespace(**dict(zip(names, refs)))
    nd, nc, nx, S, R, H = dm.nd, dm.nc, dm.nx, dm.s, dm.rows, dm.half
    W, V = dm.cols, dm.hcols
    Q, RB, E = H // 2, dm.rb, dm.ext
    place = lax.axis_index("depth")
    me = lax.axis_index("chan")
    x, core = lax.div(me, 2), lax.rem(me, 2)
    other = 1 - core
    mate = 2 * x + other
    row0, h0 = x * RB, x * (RB // 2)
    first, last = place == 0, place == nd - 1
    top, bottom = x == 0, x == nx - 1
    convs = dm.convs
    pending = []
    wt, wf, wx, wb = ([getattr(k_, f"{kind}{i}") for i in range(4)] for kind in ("wt", "wf", "wx", "wb"))
    gt, gr, ga = ([getattr(k_, f"{kind}{i}") for i in range(4)] for kind in ("gt", "gr", "ga"))
    weights = (k_.w0, k_.w1, k_.w2, k_.w3)
    grads = (k_.g0, k_.g1, k_.g2, k_.g3)
    turned, acc = k_.turned, k_.acc

    def no(cond):
        return jnp.logical_not(cond)

    def peer_copy(src, dst, send, recv, depth, chan):
        return pltpu.make_async_remote_copy(
            src_ref=src, dst_ref=dst, send_sem=send, recv_sem=recv,
            device_id={"depth": depth, "chan": chan}, device_id_type=MESH,
        )

    def guarded(cond, fn):
        if cond is None:
            fn()
        else:
            pl.when(cond)(fn)

    def drain():
        for cond, fn in pending:
            guarded(cond, fn)
        pending.clear()

    def launch(cond, copy):
        guarded(cond, lambda: copy().start())
        pending.append((cond, lambda: copy().wait_send()))

    def arrive(cond, copy):
        guarded(cond, lambda: copy().wait_recv())

    def gather_parts(ref, which, source_at=None):
        n = ref.shape[1] - 2
        k = GATHERS.index(which)
        parts = []
        for side, own, theirs, size in ((1, 1, 1, n), (0, n, 0, 1), (2, 1, n + 1, 1)):
            step = 1 - side
            can_send = (no(last), None, no(first))[side]
            can_recv = (no(first), None, no(last))[side]
            for t in range(nx):
                tox = lax.rem(x + t, nx)
                fromx = lax.rem(x + nx - t, nx)
                i = side * nx + t

                def copy(own, block, at, hop, depth, chan, src=None, size=size, i=i):
                    dst = ref.at[block, pl.ds(at, size)]
                    return peer_copy(
                        ref.at[block, pl.ds(own, size)] if src is None else src, dst,
                        k_.g_send.at[k, hop, i], k_.g_recv.at[k, hop, i], depth, chan,
                    )

                def out(copy=copy, own=own, theirs=theirs, step=step, tox=tox, size=size):
                    src = None if source_at is None else source_at(pl.ds(own - 1, size), tox)
                    return copy(own, me, theirs, 0, place + step, 2 * tox + core, src)

                source = 2 * fromx + core
                mine = side == 1 and t == 0
                back = functools.partial(copy, theirs, source, theirs, 0, place, source)
                on = functools.partial(copy, theirs, source, theirs, 1, place, mate)
                mates = functools.partial(copy, theirs, 2 * fromx + other, theirs, 1, place, mate)
                parts.append((can_send, can_recv, None if mine else out, back, on, mates))
        return parts

    def gather_start(ref, which, source_at=None):
        for can_send, _, out, _, on, _ in gather_parts(ref, which, source_at):
            launch(can_send, on if out is None else out)

    def gather_pass(ref, which):
        for _, can_recv, out, back, on, _ in gather_parts(ref, which):
            if out is not None:
                arrive(can_recv, back)
                launch(can_recv, on)

    def gather_wait(ref, which):
        for _, can_recv, _, _, _, mates in gather_parts(ref, which):
            arrive(can_recv, mates)

    def fine_parts(ref, which, sides):
        k = FINE.index(which)
        inner = pl.ds(1, RB)
        parts = []

        def piece(c, slices, rows, at_slices, at_rows, i, j, depth, chan):
            return peer_copy(
                ref.at[c, slices, rows], ref.at[c, at_slices, at_rows],
                k_.x_send.at[k, i], k_.x_recv.at[k, j], depth, chan,
            )

        def both(a, b):
            return b if a is None else jnp.logical_and(a, b)

        for side in sides:
            own, theirs = ((S, 1), (1, S), (1, 1))[side], ((0, 1), (1, S), (S + 1, 1))[side]
            own, theirs = pl.ds(*own), pl.ds(*theirs)
            step = 1 - side
            can_send = (no(last), None, no(first))[side]
            can_recv = (no(first), None, no(last))[side]
            if side == 1:
                parts.append((
                    "direct", None, None,
                    functools.partial(piece, core, own, inner, own, inner, 0, 0, place, mate),
                    functools.partial(piece, other, own, inner, own, inner, 0, 0, place, mate),
                ))
            else:
                i = 1 + side // 2
                parts.append((
                    "halo", can_send, can_recv,
                    functools.partial(piece, core, own, inner, theirs, inner, i, i, place + step, me),
                    functools.partial(piece, core, theirs, inner, theirs, inner, i, i, place, me),
                ))
                parts.append((
                    "relay", can_recv, can_recv,
                    functools.partial(piece, core, theirs, inner, theirs, inner, i + 2, i + 2, place, mate),
                    functools.partial(piece, other, theirs, inner, theirs, inner, i + 2, i + 2, place, mate),
                ))
            for up in range(2):
                row, at = pl.ds((1, RB)[up], 1), pl.ds((E - 1, 0)[up], 1)
                tox = x + (-1, 1)[up]
                sends = both(can_send, no((top, bottom)[up]))
                gets = both(can_recv, no((bottom, top)[up]))
                base = 5 + 4 * side + 2 * up
                for c in range(2):
                    parts.append((
                        "direct", sends, gets,
                        functools.partial(
                            piece, core, own, row, theirs, at, base + c, base + core, place + step, 2 * tox + c
                        ),
                        functools.partial(piece, c, theirs, at, theirs, at, base + c, base + c, place, mate),
                    ))
        return parts

    def fine_start(ref, which):
        parts = fine_parts(ref, which, (1, 0, 2))
        for kind in ("halo", "direct"):
            for name, sends, _, out, _ in parts:
                if name == kind:
                    launch(sends, out)

    def fine_pass(ref, which, sides):
        parts = fine_parts(ref, which, sides)
        for (name, _, gets, _, back), relay in zip(parts, parts[1:]):
            if name == "halo":
                arrive(gets, back)
                guarded(gets, lambda relay=relay: relay[3]().start())

    def fine_passed(ref, which):
        for name, sends, _, out, _ in fine_parts(ref, which, (0, 2)):
            if name == "relay":
                pending.append((sends, lambda out=out: out().wait_send()))

    def fine_wait(ref, which, sides):
        for name, _, gets, _, back in fine_parts(ref, which, sides):
            if name != "halo":
                arrive(gets, back)

    def natural(ref, s, r):
        v = ref[:, s, r]
        size = dm.cd
        return jnp.concatenate(
            [v[c, i * size : (i + 1) * size] for i in range(nx) for c in range(2)], 0
        ).astype(BF16)

    def slab_peer(i):
        return i, me

    def wide_peer(i):
        return lax.div(i, nx), 2 * lax.rem(i, nx) + core

    def sum_start(group, ref, k, slot, tile, source=None):
        n, own, peer, send, recv = group
        ref[slot, own] = tile

        def copy(t):
            depth, chan = peer(lax.rem(own + t, n))
            src = ref.at[slot, own] if source is None else source(depth, chan)
            return peer_copy(src, ref.at[slot, own], send.at[k, t], recv.at[k, t], depth, chan)

        def begin(t, _):
            copy(t).start()
            return _

        def sent(t, _):
            copy(t).wait_send()
            return _

        lax.fori_loop(1, n, begin, 0)
        pending.append((None, lambda: lax.fori_loop(1, n, sent, 0)))

    def sum_finish(group, ref, k, slot):
        n, own, peer, send, recv = group

        def receive(t, _):
            source = lax.rem(own + n - t, n)
            theirs = ref.at[slot, source]
            peer_copy(theirs, theirs, send.at[k, t], recv.at[k, t], *peer(source)).wait_recv()
            return _

        lax.fori_loop(1, n, receive, 0)
        return jnp.sum(ref[slot], axis=0)

    slabs = (nd, place, slab_peer, k_.t_send, k_.t_recv)
    everyone = (nd * nx, place * nx + x, wide_peer, k_.u_send, k_.u_recv)

    def columns_of(row, m):
        lane, channel = iota((m, LANES), 1), iota((m, LANES), 0)
        return tuple(
            jnp.sum(jnp.where(lane == channel + i * m, row, 0.0), axis=1, keepdims=True) for i in range(2)
        )

    def coarse_sums(slot, sums):
        sum_start(slabs, k_.st, slot, slot, pack(*sums))

    def coarse_totals(slot):
        return columns_of(sum_finish(slabs, k_.st, slot, slot), dm.ce)

    def fine_sums(slot, sums):
        sum_start(everyone, k_.su, slot, slot, pack(*sums))

    def fine_totals(slot):
        return columns_of(sum_finish(everyone, k_.su, slot, slot), dm.cf)

    def turn_in(w, cv):
        eye = (iota((LANES, LANES), 0) == iota((LANES, LANES), 1)).astype(BF16)

        def chunk(a):
            return dot_nt(eye, jnp.concatenate([a] * cv.per, 0).astype(BF16))

        full = cv.length // LANES

        def body(i, carry):
            at = pl.multiple_of(i * LANES, LANES)
            turned[pl.ds(at, LANES)] = chunk(w[:, pl.ds(at, LANES)])
            return carry

        lax.fori_loop(0, full, body, 0, unroll=4)
        if full < cv.chunks:
            a = w[:, full * LANES :]
            a = jnp.concatenate([a, jnp.zeros((cv.o, LANES - a.shape[1]), F32)], 1)
            turned[full * LANES : (full + 1) * LANES] = chunk(a)

    def prepare(k):
        cv, w, own = convs[k], weights[k], wt[k]
        out = wf[k] if k < 2 else wf[k].at[x]
        turn_in(w, cv)
        group = iota((cv.c, LANES), 1) // cv.o
        for kz in range(3):
            for j in range(cv.tiles):
                tile = None
                for g in range(cv.per):
                    t = j * cv.per + g
                    if t < 9:
                        v = turned[pl.ds(9 * kz + t, cv.c, stride=27)]
                        tile = v if tile is None else jnp.where(group == g, v, tile)
                own[kz, :, j * LANES : (j + 1) * LANES] = tile.astype(BF16).astype(own.dtype)
        eye = (iota((LANES, LANES), 0) == iota((LANES, LANES), 1)).astype(BF16)
        for j in range(cv.tiles):
            v = jnp.concatenate([own[kz, :, j * LANES : (j + 1) * LANES] for kz in range(3)], 0)
            size = min(LANES, 9 * cv.o - j * LANES)
            out[j * LANES : j * LANES + size] = dot_nt(eye, v.astype(BF16))[0:size].astype(BF16)

    def forward_copy(k, t):
        block = wf[k].at[x]
        return peer_copy(
            block, block, k_.p_send.at[k - 2, t], k_.p_recv.at[k - 2, t], place, 2 * lax.rem(x + t, nx) + core
        )

    def forward_start(k):
        for t in range(1, nx):
            launch(None, functools.partial(forward_copy, k, t))

    def forward_wait(k):
        for t in range(1, nx):
            fromx = lax.rem(x + nx - t, nx)
            block = wf[k].at[fromx]
            peer_copy(
                block, block, k_.p_send.at[k - 2, t], k_.p_recv.at[k - 2, t], place, 2 * fromx + core
            ).wait_recv()

    def forward_weight(k):
        return jnp.concatenate([wf[k][i, 0 : convs[k].taps] for i in range(nx)], 0)

    def weights_start(k):
        cv = convs[k]
        for b, (size, start, at) in enumerate(cv.blocks):
            wx[k][me, :, at : at + size] = wt[k][:, pl.ds(start(me), size)]
            for t in range(1, nc):
                to = lax.rem(me + t, nc)

                def copy(to=to, t=t, b=b, size=size, start=start, at=at):
                    return peer_copy(
                        wt[k].at[:, pl.ds(start(to), size)], wx[k].at[me, :, pl.ds(at, size)],
                        k_.w_send.at[k, b, t], k_.w_recv.at[k, b, t], place, to,
                    )

                launch(None, copy)

    def weights_finish(k):
        cv = convs[k]
        for b, (size, _, at) in enumerate(cv.blocks):
            for t in range(1, nc):
                source = lax.rem(me + nc - t, nc)
                theirs = wx[k].at[source, :, pl.ds(at, size)]
                peer_copy(theirs, theirs, k_.w_send.at[k, b, t], k_.w_recv.at[k, b, t], place, source).wait_recv()
        for t in range(9):
            pieces = [
                wx[k][j, 2 - kz, :, t * cv.o : (t + 1) * cv.o].astype(F32) for kz in range(3) for j in range(nc)
            ]
            wb[k][(8 - t) * cv.needed : (9 - t) * cv.needed] = jnp.concatenate(pieces, 1).astype(BF16)

    def tiles_of(k, part, put):
        cv = convs[k]

        def tile(i, carry):
            at = pl.multiple_of(i * 16, 16)
            for j in range(cv.tiles):
                put(i * cv.tiles + j, acc[part, pl.ds(at, 16), j * LANES : (j + 1) * LANES].astype(BF16))
            return carry

        lax.fori_loop(0, 3 * cv.c // 16, tile, 0, unroll=4)

    def cross_start(k):
        gs, gx = (k_.gs2, k_.gs3)[k - 2], (k_.gx2, k_.gx3)[k - 2]
        for part in range(nx):

            def put(i, v, part=part):
                gs[part, i] = v

            tiles_of(k, part, put)
        for t in range(1, nx):
            tox = lax.rem(x + t, nx)

            def copy(t=t, tox=tox):
                return peer_copy(
                    gs.at[tox], gx.at[x], k_.c_send.at[k - 2, t], k_.c_recv.at[k - 2, t], place, 2 * tox + core
                )

            launch(None, copy)

    def cross_finish(k):
        cv, gs, gx = convs[k], (k_.gs2, k_.gs3)[k - 2], (k_.gx2, k_.gx3)[k - 2]
        sources = [lax.rem(x + nx - t, nx) for t in range(1, nx)]
        for t, fromx in enumerate(sources, 1):
            theirs = gx.at[fromx]
            peer_copy(
                theirs, theirs, k_.c_send.at[k - 2, t], k_.c_recv.at[k - 2, t], place, 2 * fromx + core
            ).wait_recv()

        def add(i, carry):
            for j in range(cv.tiles):
                p = i * cv.tiles + j
                v = gs[x, p].astype(F32)
                for fromx in sources:
                    v += gx[fromx, p].astype(F32)
                gt[k][p] = v.astype(BF16)
            return carry

        lax.fori_loop(0, 3 * cv.c // 16, add, 0, unroll=4)
        reduce_send(k)

    def reduce_start(k):
        def put(i, v):
            gt[k][i] = v

        tiles_of(k, 0, put)
        reduce_send(k)

    def over_slabs(copy):
        def begin(t, _):
            copy(t).start()
            return _

        def sent(t, _):
            copy(t).wait_send()
            return _

        lax.fori_loop(1, nd, begin, 0)
        pending.append((None, lambda: lax.fori_loop(1, nd, sent, 0)))

    def from_slabs(ref_of, send, recv):
        def receive(t, _):
            source = lax.rem(place + nd - t, nd)
            theirs = ref_of(source)
            peer_copy(theirs, theirs, send.at[t], recv.at[t], source, me).wait_recv()
            return _

        lax.fori_loop(1, nd, receive, 0)

    def reduce_send(k):
        cv = convs[k]
        for i in range(cv.count, cv.share * nd):
            gt[k][i] = jnp.zeros((16, LANES), BF16)
        gr[k][place] = gt[k][pl.ds(place * cv.share, cv.share)]

        def copy(t):
            to = lax.rem(place + t, nd)
            return peer_copy(
                gt[k].at[pl.ds(to * cv.share, cv.share)], gr[k].at[place], k_.r_send.at[k, t], k_.r_recv.at[k, t], to, me
            )

        over_slabs(copy)

    def reduce_finish(k):
        cv = convs[k]
        from_slabs(lambda source: gr[k].at[source], k_.r_send.at[k], k_.r_recv.at[k])
        ga[k][pl.ds(place * cv.share, cv.share)] = jnp.sum(gr[k][...].astype(F32), axis=0).astype(BF16)

        def copy(t):
            own = ga[k].at[pl.ds(place * cv.share, cv.share)]
            return peer_copy(own, own, k_.a_send.at[k, t], k_.a_recv.at[k, t], lax.rem(place + t, nd), me)

        over_slabs(copy)

    def gradient_out(k):
        cv, out = convs[k], grads[k]
        from_slabs(
            lambda source: ga[k].at[pl.ds(source * cv.share, cv.share)], k_.a_send.at[k], k_.a_recv.at[k]
        )
        group = iota((16, LANES), 1) // cv.o

        def scatter(i, carry):
            for kz in range(3):
                for j in range(cv.tiles):
                    v = ga[k][(kz * (cv.c // 16) + i) * cv.tiles + j].astype(F32)
                    for g in range(cv.per):
                        t = j * cv.per + g
                        if t < 9:
                            turned[pl.ds(9 * kz + t + i * (16 * 27), 16, stride=27)] = jnp.where(group == g, v, 0.0)
            return carry

        lax.fori_loop(0, cv.c // 16, scatter, 0, unroll=2)

        pick = (iota((cv.o, LANES), 1) % cv.o == iota((cv.o, LANES), 0)).astype(BF16)
        step = 8 * LANES
        for at in range(0, cv.length, step):
            size = min(step, cv.length - at)
            v = dot_nt(pick, turned[at : at + -(-size // LANES) * LANES].astype(BF16))
            out[:, at : at + size] = v[:, 0:size]

    def column(row):
        n = row.shape[1]
        eye = iota((n, n), 0) == iota((n, n), 1)
        return jnp.sum(jnp.where(eye, row, 0.0), axis=1, keepdims=True)

    def row_of(col):
        n = col.shape[0]
        eye = iota((n, n), 0) == iota((n, n), 1)
        return jnp.sum(jnp.where(eye, col, 0.0), axis=0, keepdims=True)

    def clear_halos(ref):
        def clear(at):
            for j in range(ref.shape[0]):
                ref[j, at] = jnp.zeros(ref.shape[2:], ref.dtype)

        pl.when(first)(lambda: clear(0))
        pl.when(last)(lambda: clear(ref.shape[1] - 1))

    def clear_rows(ref):
        def clear(at):
            for c in range(2):
                for i in range(S + 2):
                    ref[c, i, at] = jnp.zeros(ref.shape[3:], ref.dtype)

        pl.when(top)(lambda: clear(0))
        pl.when(bottom)(lambda: clear(E - 1))

    def conv(row, weight, n, m, groups, emit, init, late=None):
        per = RB // n

        def body(i, carry):
            if late is not None:
                pl.when(i == (S - 1) * per - 1)(late[0])
                pl.when(i == (S - 1) * per)(late[1])
            d = lax.div(i, per)
            r0 = (i - d * per) * n
            v = jnp.concatenate(
                [jnp.concatenate([row(d + kz, r0 + j) for j in range(n + 2)], 1) for kz in range(3)], 0
            )
            y = dot(weight(), v)
            results = []
            for j in range(n):
                parts = []
                for g in range(groups):
                    a = []
                    for kx in range(3):
                        terms = [
                            y[
                                (9 * g + 3 * ky + kx) * m : (9 * g + 3 * ky + kx + 1) * m,
                                (j + ky) * LANES : (j + ky + 1) * LANES,
                            ]
                            for ky in range(3)
                        ]
                        a.append(terms[0] + terms[1] + terms[2])
                    parts.append(from_left(a[0], W) + a[1] + from_right(a[2], W))
                results.append(jnp.concatenate(parts, 0) if groups > 1 else parts[0])
            return emit(d, r0, results, carry)

        return lax.fori_loop(0, S * per, body, init)

    def conv_stats(row, weight, z, n, late=None):
        def emit(d, r0, results, carry):
            total, square = carry
            for j, v in enumerate(results):
                z[d * RB + r0 + j] = v
                total, square = total + v, square + v * v
            return total, square

        blank = jnp.zeros((dm.cf, LANES), F32)
        return conv(row, weight, n, dm.cd, nx, emit, (blank, blank), late)

    def weight_grad(row, k):
        cv = convs[k]
        dzf = k_.dzf
        n = E // 2
        acc[:, 0 : 3 * cv.c, 0 : cv.wide] = jnp.zeros((nx, 3 * cv.c, cv.wide), F32)

        def body(i, carry):
            d = lax.div(i, 2)
            r0 = (i - 2 * d) * n
            v = jnp.concatenate(
                [jnp.concatenate([row(d + kz, r0 + j) for j in range(n)], 1) for kz in range(3)], 0
            )
            for part in range(nx):
                y = jnp.concatenate(
                    [
                        jnp.concatenate(
                            [dzf[kx, d, r0 + j + 2 - ky, part * cv.o : (part + 1) * cv.o] for j in range(n)], 1
                        )
                        for ky in range(3)
                        for kx in range(3)
                    ],
                    0,
                ).astype(BF16)
                acc[part, 0 : 3 * cv.c, 0 : cv.taps] += dot_nt(v, y)
            return carry

        lax.fori_loop(0, S * 2, body, 0)

    def conv_coarse(ref, weight, m):
        v = jnp.concatenate(
            [jnp.concatenate([flat(ref, kz, i) for i in range(Q)], 1) for kz in range(3)], 0
        )
        y = dot(weight[...], v)
        blank = jnp.zeros((m, LANES), F32)

        def shifted(ky, i):
            if not 0 <= i < Q:
                return blank
            a, b, c = (
                y[(3 * ky + kx) * m : (3 * ky + kx + 1) * m, i * LANES : (i + 1) * LANES] for kx in range(3)
            )
            return from_left(a, V) + b + from_right(c, V)

        before = [shifted(0, i) for i in range(-1, Q)]
        after = [shifted(2, i) for i in range(Q + 1)]
        return [
            shifted(1, i) + halves(before[i + 1] + after[i + 1], before[i] + after[i]) for i in range(Q)
        ]

    def conv_stats_coarse(ref, weight, z, m):
        total = square = jnp.zeros((m, LANES), F32)
        for i, v in enumerate(conv_coarse(ref, weight, m)):
            z[i] = v
            total, square = total + v, square + v * v
        return total, square

    def weight_grad_coarse(ref, k):
        cv = convs[k]
        v = jnp.concatenate(
            [jnp.concatenate([flat(ref, kz, i) for i in range(Q)], 1) for kz in range(3)], 0
        )
        y = jnp.concatenate([jnp.concatenate([k_.dzc[t, i] for i in range(Q)], 1) for t in range(9)], 0)
        acc[0, 0 : 3 * cv.c, 0 : cv.taps] = dot_nt(v, y.astype(BF16))

    def pack(a, b):
        m = a.shape[0]
        a = jnp.sum(a, axis=1, keepdims=True)
        b = jnp.sum(b, axis=1, keepdims=True)
        lane, channel = iota((m, LANES), 1), iota((m, LANES), 0)
        both = jnp.where(lane == channel, a, jnp.where(lane == channel + m, b, 0.0))
        return jnp.sum(both, axis=0, keepdims=True)

    def moments(total, count):
        mean = total[0] / count
        var = total[1] / count - mean * mean
        return mean, lax.rsqrt(var + EPS)

    def wide(column):
        return jnp.broadcast_to(column, (column.shape[0], LANES))

    def factors(stats, norm):
        mean, inv = stats
        gain, shift = norm
        return wide(mean), wide(gain * inv), wide(shift)

    def norm_rows(z, stats, norm, emit, n):
        mean, scale, shift = factors(stats, norm)

        def body(i, carry):
            for j in range(n):
                p = i * n + j
                u = (z[p] - mean) * scale + shift
                emit(p, u * jax.nn.sigmoid(u))
            return carry

        lax.fori_loop(0, z.shape[0] // n, body, 0)

    def norm_back_sums(z, keep_du, stats, norm, grad, n):
        mean, scale, shift = factors(stats, norm)
        inv = wide(stats[1])
        m = z.shape[1]

        def body(i, carry):
            a, b = carry
            for j in range(n):
                p = i * n + j
                centred = z[p] - mean
                u = centred * scale + shift
                sigma = jax.nn.sigmoid(u)
                v = grad(p) * sigma * (1.0 + u * (1.0 - sigma))
                keep_du(p, v)
                a, b = a + v, b + v * (centred * inv)
            return a, b

        blank = jnp.zeros((m, LANES), F32)
        return lax.fori_loop(0, z.shape[0] // n, body, (blank, blank))

    def back_factors(stats, norm, total, count):
        mean, inv = stats
        scale = norm[0] * inv
        return wide(mean), wide(scale), wide(-scale * total[0] / count), wide(-scale * inv * total[1] / count)

    def norm_back_fine(z, given, ref):
        mean, scale, level, slope = given
        dzf = k_.dzf

        def body(d, carry):
            for r in range(RB):
                p = d * RB + r
                v = scale * k_.du_f[p] + level + slope * (z[p] - mean)
                low = v.astype(BF16)
                ref[core, 1 + d, 1 + r] = low.astype(ref.dtype)
                v = low.astype(F32)
                dzf[0, d, 2 + r] = from_right(v, W).astype(dzf.dtype)
                dzf[1, d, 2 + r] = low.astype(dzf.dtype)
                dzf[2, d, 2 + r] = from_left(v, W).astype(dzf.dtype)
            return carry

        lax.fori_loop(0, S, body, 0)

    def norm_back_coarse(z, given, ref):
        mean, scale, level, slope = given
        rows = []
        for i in range(Q):
            low = (scale * k_.du_c[i] + level + slope * (z[i] - mean)).astype(BF16)
            ref[me, 1, i] = low.astype(ref.dtype)
            rows.append(low.astype(F32))
        blank = jnp.zeros_like(rows[0])
        rows = [blank] + rows + [blank]
        for i in range(Q):
            before, here, after = rows[i : i + 3]
            for ky, v in enumerate((halves(after, here), here, halves(here, before))):
                for kx, u in enumerate((from_right(v, V), v, from_left(v, V))):
                    k_.dzc[3 * ky + kx, i] = u.astype(k_.dzc.dtype)

    def keep_du(ref):
        def store(p, v):
            ref[p] = v

        return store

    barrier = pltpu.get_barrier_semaphore()

    def greet(depth, chan):
        pl.semaphore_signal(barrier, inc=1, device_id={"depth": depth, "chan": chan}, device_id_type=MESH)

    def greet_core(t, _):
        greet(*wide_peer(lax.rem(place * nx + x + t, nd * nx)))
        return _

    lax.fori_loop(1, nd * nx, greet_core, 0)
    for t in range(nx):
        greet(place, 2 * lax.rem(x + t, nx) + other)
    for t in range(1, nx):
        to = 2 * lax.rem(x + t, nx) + other
        pl.when(no(first))(lambda to=to: greet(place - 1, to))
        pl.when(no(last))(lambda to=to: greet(place + 1, to))

    hc = iota((LANES, LANES), 0)
    fc = iota((LANES, LANES), 1)
    half = LANES // 2

    def up_table(coarse, fine):
        base = fine // 2
        beside = jnp.clip(base + jnp.where(fine % 2 == 0, -1, 1), 0, V - 1)
        near = (coarse == base).astype(F32)
        far = (coarse == beside).astype(F32)
        return (0.75 * near + 0.25 * far).astype(BF16)

    pool = jnp.concatenate([(hc // 2 == fc - at).astype(BF16) for at in (0, half)], 0)
    spread = jnp.concatenate([(hc - at == fc // 2).astype(BF16) for at in (0, half)], 1)
    up = jnp.concatenate([up_table(hc - at, fc) for at in (0, half)], 1)
    down = jnp.concatenate([up_table(fc, hc)] * 2, 0)
    spread2 = jnp.concatenate([spread, spread], 0)

    def take_rows(ref):
        for c in range(ref.shape[0]):
            k_.rows[c * S * R : (c + 1) * S * R] = ref[c].astype(F32).reshape(S * R, LANES)

    def row_of_all(p, chans):
        return k_.rows[pl.ds(p, chans, stride=S * R)]

    xp, xs, own_skip = k_.xp, k_.xs, k_.own_skip
    clear_halos(xp)
    take_rows(k_.skip)
    for i in range(S):
        for r in (0, R + 1):
            own_skip[i, r] = jnp.zeros((dm.cs, LANES), own_skip.dtype)

    def take_skip(i, carry):
        parts = []
        for d in range(S):
            v = [row_of_all(d * R + 4 * i + j, dm.cs).astype(BF16) for j in range(4)]
            for j in range(4):
                own_skip[d, 1 + 4 * i + j] = v[j].astype(own_skip.dtype)
            parts += [jnp.concatenate([v[j], v[2 + j]], 1) for j in range(2)]
        v = dot(jnp.concatenate(parts, 0), pool).reshape(2 * S, dm.cs, LANES)
        xp[me, 1, i] = (jnp.sum(v, axis=0) * 0.125).astype(BF16).astype(xp.dtype)
        return carry

    lax.fori_loop(0, Q, take_skip, 0, unroll=3)
    beside = jnp.where(first, 0, 1) + jnp.where(last, 0, 1)
    pl.semaphore_wait(barrier, nd * nx - 1 + nx + (nx - 1) * beside)
    gather_start(xp, "pooled")
    clear_halos(xs)
    xs[me, 1 : S + 1] = own_skip[:, pl.ds(row0, E)]
    gather_start(xs, "skip", lambda at, tox: own_skip.at[at, pl.ds(tox * RB, E)])

    gq = dm.g // nc
    columns = dm.enc_all + dm.skip_all
    gate_all, norm_all = k_.gate_all, k_.norm_all
    gate_all[me, :, 0:columns] = k_.gate[...]
    lane = iota((gq, LANES), 1)
    gate_all[me, :, 2 * LANES :] = jnp.where(
        lane == 0, column(k_.vector[0:1]), jnp.where(lane == 1, column(k_.vector[1:2]), 0.0)
    )
    for layer in range(2):
        for part in range(2):
            at = 2 * layer + part
            norm_all[me, at : at + 1, 0 : dm.cd] = k_.dn[part, layer : layer + 1]

    def constants(i, t, source, to):
        ref = (norm_all, gate_all)[i]
        return peer_copy(ref.at[source], ref.at[source], k_.v_send.at[i, t], k_.v_recv.at[i, t], place, to)

    for i in range(2):
        for t in range(1, nc):
            launch(None, functools.partial(constants, i, t, me, lax.rem(me + t, nc)))
    prepare(0)
    xd, xz4, xz3, d1 = k_.xd, k_.xz4, k_.xz3, k_.d1
    for ref in (xd, xz4, xz3):
        clear_rows(ref)
        clear_halos(ref)
    for ref in (k_.xh, k_.xz2, k_.xz1):
        clear_halos(ref)
    for i in range(S):
        for r in (0, 1, RB + 2, RB + 3):
            for kx in range(3):
                k_.dzf[kx, i, r] = jnp.zeros(k_.dzf.shape[3:], k_.dzf.dtype)
        for r in range(3):
            k_.ug[i, r] = jnp.zeros(k_.ug.shape[2:], F32)
            k_.ug[i, RB + 3 + r] = jnp.zeros(k_.ug.shape[2:], F32)
        for r in range(H + 2):
            k_.cb[i, r] = jnp.zeros(k_.cb.shape[2:], F32)

    def norm_of(layer):
        return column(k_.en[0, layer : layer + 1]), column(k_.en[1, layer : layer + 1])

    norm_e1, norm_e2 = norm_of(0), norm_of(1)

    gather_pass(xp, "pooled")
    gather_wait(xp, "pooled")
    coarse_sums(0, conv_stats_coarse(xp, wf[0], k_.z1, dm.ce))
    prepare(1)
    stats_e1 = moments(coarse_totals(0), dm.coarse_total)

    def keep_coarse(ref):
        def store(p, v):
            ref[me, 1, p] = v.astype(BF16).astype(ref.dtype)

        return store

    norm_rows(k_.z1, stats_e1, norm_e1, keep_coarse(k_.xh), Q)
    gather_start(k_.xh, "hidden")
    prepare(2)
    forward_start(2)
    gather_pass(k_.xh, "hidden")
    gather_pass(xs, "skip")
    gather_wait(k_.xh, "hidden")
    coarse_sums(1, conv_stats_coarse(k_.xh, wf[1], k_.z2, dm.ce))
    take_rows(k_.cot)

    def take_cot(i, carry):
        for d in range(S):
            for j in range(4):
                v = row_of_all(d * R + 4 * i + j, dm.cd).astype(BF16)
                k_.own_cot[d, 4 * i + j] = v.astype(k_.own_cot.dtype)
        return carry

    lax.fori_loop(0, Q, take_cot, 0)
    k_.cots[x] = k_.own_cot[:, pl.ds(row0, RB)]
    stats_e2 = moments(coarse_totals(1), dm.coarse_total)
    norm_rows(k_.z2, stats_e2, norm_e2, keep_coarse(k_.xc), Q)
    gather_start(k_.xc, "coarse")
    prepare(3)
    for t in range(1, nc):
        for i in range(2):
            source = lax.rem(me + nc - t, nc)
            constants(i, t, source, source).wait_recv()
    gate_full = gate_all[...].reshape(dm.g, 3 * LANES)
    wg = gate_full[:, 0:columns].astype(BF16)
    gbias = gate_full[:, 2 * LANES : 2 * LANES + 1]
    gout = gate_full[:, 2 * LANES + 1 : 2 * LANES + 2]
    k_.gate_t[...] = jnp.transpose(gate_full[:, 0 : 2 * LANES])
    own_rows = [k_.gate_t[pl.ds(pl.multiple_of((2 * i + core) * dm.ce, dm.ce), dm.ce)] for i in range(nx)]
    own_rows += [
        k_.gate_t[pl.ds(pl.multiple_of(dm.enc_all + (2 * i + core) * dm.cs, dm.cs), dm.cs)] for i in range(nx)
    ]
    k_.gate_own[...] = jnp.concatenate(own_rows, 0)

    def norm_fine(layer):
        return tuple(
            jnp.concatenate(
                [column(norm_all[2 * i + core, 2 * layer + part : 2 * layer + part + 1, 0 : dm.cd]) for i in range(nx)], 0
            )
            for part in range(2)
        )

    norm_d1, norm_d2 = norm_fine(0), norm_fine(1)
    gather_pass(k_.xc, "coarse")
    gather_wait(k_.xc, "coarse")
    forward_start(3)

    dt = k_.dt

    def up_depth(i, carry):
        t = []
        for j in range(3):
            v = dot(flat(k_.xc, j, i), up)
            t.append(jnp.stack([v[:, 0:LANES], v[:, LANES:]], 0))
        below = jnp.where(first, t[1], t[0])
        above = jnp.where(last, t[1], t[2])
        near = 0.75 * t[1]
        here = 0.25 * t[1]
        rows = pl.ds(i * 2, 2)
        dt[0, rows] = jnp.where(first, 0.0, 0.75 * below + here)
        dt[1, rows] = near + 0.25 * below
        dt[2, rows] = near + 0.25 * above
        dt[3, rows] = jnp.where(last, 0.0, 0.75 * above + here)
        return carry

    lax.fori_loop(0, Q, up_depth, 0)

    def up_rows(i, carry):
        here = h0 + i
        before, after = jnp.maximum(here - 1, 0), jnp.minimum(here + 1, H - 1)
        for j in range(S + 2):
            v = 0.75 * dt[j, here]
            d1[j, 1 + 2 * i, 0 : dm.enc_all] = (v + 0.25 * dt[j, before]).astype(BF16)
            d1[j, 2 + 2 * i, 0 : dm.enc_all] = (v + 0.25 * dt[j, after]).astype(BF16)
        return carry

    lax.fori_loop(0, RB // 2, up_rows, 0)
    for edge, at, near, far in (
        (top, 0, jnp.maximum(h0 - 1, 0), h0),
        (bottom, E - 1, jnp.minimum(h0 + RB // 2, H - 1), h0 + RB // 2 - 1),
    ):
        for j in range(S + 2):
            v = jnp.where(edge, 0.0, 0.75 * dt[j, near] + 0.25 * dt[j, far])
            d1[j, at, 0 : dm.enc_all] = v.astype(BF16)
    for t in range(1, nx):
        tox = lax.rem(x + t, nx)

        def send_cot(t=t, tox=tox):
            return peer_copy(
                k_.own_cot.at[:, pl.ds(tox * RB, RB)], k_.cots.at[x], k_.o_send.at[0, t], k_.o_recv.at[0, t],
                place, 2 * tox + core,
            )

        launch(None, send_cot)

    gather_wait(xs, "skip")
    gate_n = E // 2

    def gate(i, carry):
        j = lax.div(i, 2)
        r0 = (i - 2 * j) * gate_n
        skips = [flat(xs, j, r0 + q) for q in range(gate_n)]
        v = jnp.concatenate(
            [
                jnp.concatenate([d1[j, r0 + q, 0 : dm.enc_all] for q in range(gate_n)], 1),
                jnp.concatenate(skips, 1),
            ],
            0,
        )
        pre = dot(wg, v) + gbias
        act = pre * jax.nn.sigmoid(pre)
        alpha = jax.nn.sigmoid(jnp.sum(gout * act, axis=0, keepdims=True))
        for q in range(gate_n):
            lanes = slice(q * LANES, (q + 1) * LANES)
            d1[j, r0 + q, dm.enc_all :] = (alpha[:, lanes] * skips[q].astype(F32)).astype(BF16)
            k_.pre[j, r0 + q] = pre[:, lanes]
            k_.alpha[j, r0 + q] = alpha[:, lanes]
        return carry

    lax.fori_loop(0, (S + 2) * 2, gate, 0)
    for k in (3, 2, 1, 0):
        weights_start(k)

    n = min(6, RB)

    def row_d1(j, r):
        return d1[j, r]

    def row_xd(j, r):
        return natural(xd, j, r)

    forward_wait(2)
    fine_sums(0, conv_stats(row_d1, lambda: forward_weight(2), k_.z3, n))
    drain()
    forward_wait(3)
    stats_d1 = moments(fine_totals(0), dm.fine_total)

    def keep_dec(p, v):
        d = lax.div(p, RB)
        xd[core, 1 + d, 1 + p - d * RB] = v.astype(BF16).astype(xd.dtype)

    norm_rows(k_.z3, stats_d1, norm_d1, keep_dec, RB)
    fine_start(xd, "hidden")
    for t in range(1, nx):
        fromx = lax.rem(x + nx - t, nx)
        theirs = k_.cots.at[fromx]
        peer_copy(theirs, theirs, k_.o_send.at[0, t], k_.o_recv.at[0, t], place, 2 * fromx + core).wait_recv()
    fine_pass(xd, "hidden", (0,))
    weights_finish(3)
    fine_wait(xd, "hidden", (1, 0))
    late = (lambda: fine_pass(xd, "hidden", (2,)), lambda: fine_wait(xd, "hidden", (2,)))
    fine_sums(1, conv_stats(row_xd, lambda: forward_weight(3), k_.z4, n, late))
    fine_passed(xd, "hidden")
    stats_d2 = moments(fine_totals(1), dm.fine_total)

    def row_cot(p):
        d = lax.div(p, RB)
        return jnp.concatenate([k_.cots[i, d, p - d * RB] for i in range(nx)], 0).astype(F32)

    fine_sums(2, norm_back_sums(k_.z4, keep_du(k_.du_f), stats_d2, norm_d2, row_cot, RB))

    def keep_result(p, v):
        for i in range(nx):
            k_.ob[i, p] = v[i * dm.cd : (i + 1) * dm.cd].astype(BF16).astype(k_.ob.dtype)

    norm_rows(k_.z4, stats_d2, norm_d2, keep_result, RB)
    for t in range(1, nx):
        tox = lax.rem(x + t, nx)

        def send_result(t=t, tox=tox):
            return peer_copy(
                k_.ob.at[tox], k_.oi.at[x], k_.o_send.at[1, t], k_.o_recv.at[1, t], place, 2 * tox + core
            )

        launch(None, send_result)
    total_d2 = fine_totals(2)
    norm_back_fine(k_.z4, back_factors(stats_d2, norm_d2, total_d2, dm.fine_total), xz4)
    fine_start(xz4, "dz4")
    weight_grad(row_xd, 3)
    fine_pass(xz4, "dz4", (0,))
    cross_start(3)
    fine_wait(xz4, "dz4", (1, 0))

    def row_xz4(j, r):
        return natural(xz4, j, r)

    def keep_grad(d, r0, results, carry):
        for j, v in enumerate(results):
            k_.gg[d * RB + r0 + j] = v
        return carry

    late = (lambda: fine_pass(xz4, "dz4", (2,)), lambda: fine_wait(xz4, "dz4", (2,)))
    conv(row_xz4, lambda: wb[3][...], n, dm.cf, 1, keep_grad, 0, late)
    fine_passed(xz4, "dz4")
    fine_sums(3, norm_back_sums(k_.z3, keep_du(k_.du_f), stats_d1, norm_d1, lambda p: k_.gg[p], RB))
    cross_finish(3)
    total_d1 = fine_totals(3)
    norm_back_fine(k_.z3, back_factors(stats_d1, norm_d1, total_d1, dm.fine_total), xz3)
    fine_start(xz3, "dz3")
    weights_finish(2)
    weight_grad(row_d1, 2)
    fine_pass(xz3, "dz3", (0,))
    cross_start(2)
    fine_wait(xz3, "dz3", (1, 0))

    def row_xz3(j, r):
        return natural(xz3, j, r)

    ups = nx * dm.ce

    def gate_back(d, r0, results, carry):
        bias, psi = carry
        lows = []
        for j, both in enumerate(results):
            p = d * RB + r0 + j
            v = both[ups:]
            grad = jnp.sum(v * flat(xs, d + 1, r0 + 1 + j).astype(F32), axis=0, keepdims=True)
            alpha = k_.alpha[d + 1, r0 + 1 + j]
            logit = grad * alpha * (1.0 - alpha)
            pre = k_.pre[d + 1, r0 + 1 + j]
            sigma = jax.nn.sigmoid(pre)
            psi = psi + pre * sigma * logit
            low = (logit * gout * sigma * (1.0 + pre * (1.0 - sigma))).astype(BF16)
            bias = bias + low.astype(F32)
            k_.pg[p] = low
            lows.append(low)
            k_.ug[d, 3 + r0 + j] = both[0:ups]
            for i in range(nc):
                k_.gv[i] = v[i * dm.cs : (i + 1) * dm.cs]
            for i in range(nx):
                k_.sgp[i, p] = alpha * k_.gv[2 * i + core]
        back = dot(k_.gate_own[...].astype(BF16), jnp.concatenate(lows, 1))
        for j in range(len(results)):
            p = d * RB + r0 + j
            lanes = slice(j * LANES, (j + 1) * LANES)
            k_.ug[d, 3 + r0 + j] += back[0:ups, lanes]
            for i in range(nx):
                v = k_.sgp[i, p] + back[ups + i * dm.cs : ups + (i + 1) * dm.cs, lanes]
                k_.sgp[i, p] = v
                k_.sgb[i, p] = v.astype(BF16).astype(k_.sgb.dtype)
        return bias, psi

    blank = jnp.zeros((dm.g, LANES), F32)
    late = (lambda: fine_pass(xz3, "dz3", (2,)), lambda: fine_wait(xz3, "dz3", (2,)))
    bias, psi = conv(row_xz3, lambda: wb[2][...], n, ups + dm.skip_all, 1, gate_back, (blank, blank), late)
    fine_passed(xz3, "dz3")

    ug, cb, cg = k_.ug, k_.cb, k_.cg
    for q in range(RB // 2 + 2):
        terms = []
        for d in range(S):
            v = 0.75 * (ug[d, 2 * q + 1] + ug[d, 2 * q + 2]) + 0.25 * (ug[d, 2 * q + 3] + ug[d, 2 * q])
            if q == 1:
                v += jnp.where(top, 0.25 * ug[d, 3], 0.0)
            if q == RB // 2:
                v += jnp.where(bottom, 0.25 * ug[d, RB + 2], 0.0)
            terms.append(split(v))
        v = dot(jnp.concatenate(terms, 0), down)
        for d in range(S):
            cb[d, h0 + q] = v[d * ups : (d + 1) * ups]

    def to_slabs(i, carry):
        even, odd = (cb[d, 2 * i + 1] + pltpu.roll(cb[d, 2 * i + 2], half, 1) for d in range(S))
        middle = 0.75 * (even + odd) + jnp.where(first, 0.25 * even, 0.0) + jnp.where(last, 0.25 * odd, 0.0)
        for part, v in enumerate((0.25 * even, middle, 0.25 * odd)):
            for j in range(nx):
                block = v[j * dm.ce : (j + 1) * dm.ce]
                k_.fs[part, j, i] = block.astype(BF16).astype(k_.fs.dtype)
                if part == 1:
                    k_.fm[j, i] = block
        return carry

    lax.fori_loop(0, Q, to_slabs, 0)

    def fold_parts():
        for step in (-1, 1, 0):
            can_send = (no(first), None, no(last))[step + 1]
            can_recv = (no(last), None, no(first))[step + 1]
            for t in range(nx):
                if (step, t) != (0, 0):
                    tox, fromx = lax.rem(x + t, nx), lax.rem(x + nx - t, nx)
                    sems = (k_.f_send.at[step + 1, t], k_.f_recv.at[step + 1, t])
                    theirs = k_.fr.at[step + 1, fromx]
                    yield (
                        can_send, can_recv, fromx, step + 1,
                        functools.partial(
                            peer_copy, k_.fs.at[step + 1, tox], k_.fr.at[step + 1, x], *sems, place + step, 2 * tox + core
                        ),
                        functools.partial(peer_copy, theirs, theirs, *sems, place, 2 * fromx + core),
                    )

    for can_send, _, _, _, out, _ in fold_parts():
        launch(can_send, out)
    for t in range(1, nx):
        tox = lax.rem(x + t, nx)

        def send_skip(t=t, tox=tox):
            return peer_copy(
                k_.sgb.at[tox], k_.sgi.at[x], k_.o_send.at[2, t], k_.o_recv.at[2, t], place, 2 * tox + core
            )

        launch(None, send_skip)

    acc[0, 0 : dm.g, 0:columns] = jnp.zeros((dm.g, columns), F32)

    def gate_weight(d, carry):
        v = jnp.concatenate(
            [
                jnp.concatenate([d1[1 + d, 1 + j, 0 : dm.enc_all] for j in range(RB)], 1),
                jnp.concatenate([flat(xs, 1 + d, 1 + j) for j in range(RB)], 1),
            ],
            0,
        )
        y = jnp.concatenate([k_.pg[d * RB + j] for j in range(RB)], 1)
        acc[0, 0 : dm.g, 0:columns] += dot_nt(y, v)
        return carry

    lax.fori_loop(0, S, gate_weight, 0)
    lane = iota((dm.g, LANES), 1)
    vectors = jnp.where(
        lane == 0,
        jnp.sum(bias, axis=1, keepdims=True),
        jnp.where(lane == 1, jnp.sum(psi, axis=1, keepdims=True), 0.0),
    )
    gate_block = k_.gate_block
    for j in range(nc):
        mine = slice(j * gq, (j + 1) * gq)
        gate_block[j, :, 0:columns] = acc[0, mine, 0:columns]
        gate_block[j, :, columns : 2 * LANES] = jnp.zeros((gq, 2 * LANES - columns), F32)
        gate_block[j, :, 2 * LANES :] = vectors[mine]
    sum_start(everyone, k_.sv, 4, 0, gate_block[me], lambda depth, chan: gate_block.at[chan])
    cg[...] = k_.fm[x]
    for _, can_recv, fromx, part, _, back in fold_parts():

        def fold_in(back=back, part=part, fromx=fromx):
            back().wait_recv()
            cg[...] += k_.fr[part, fromx].astype(F32)

        guarded(can_recv, fold_in)

    coarse_sums(2, norm_back_sums(k_.z2, keep_du(k_.du_c), stats_e2, norm_e2, lambda p: cg[p], Q))
    cross_finish(2)
    weights_finish(1)
    total_e2 = coarse_totals(2)
    norm_back_coarse(k_.z2, back_factors(stats_e2, norm_e2, total_e2, dm.coarse_total), k_.xz2)
    gather_start(k_.xz2, "dz2")
    weight_grad_coarse(k_.xh, 1)
    reduce_finish(3)
    gather_pass(k_.xz2, "dz2")
    reduce_start(1)
    weights_finish(0)
    drain()
    gather_wait(k_.xz2, "dz2")
    for i, v in enumerate(conv_coarse(k_.xz2, wb[1], dm.ce)):
        cg[i] = v
    coarse_sums(3, norm_back_sums(k_.z1, keep_du(k_.du_c), stats_e1, norm_e1, lambda p: cg[p], Q))
    reduce_finish(2)
    total_e1 = coarse_totals(3)
    norm_back_coarse(k_.z1, back_factors(stats_e1, norm_e1, total_e1, dm.coarse_total), k_.xz1)
    gather_start(k_.xz1, "dz1")
    weight_grad_coarse(xp, 0)
    reduce_start(0)
    reduce_finish(1)
    gather_pass(k_.xz1, "dz1")
    gradient_out(3)

    def rows_out(ref, own, theirs, kind, size):
        def copy_rows(read, at):
            def body(d, carry):
                for r in range(RB):
                    p = (d * R + at * RB + r) * size
                    ref[pl.ds(pl.multiple_of(p, size), size)] = read(d * RB + r).astype(F32)
                return carry

            lax.fori_loop(0, S, body, 0)

        copy_rows(lambda p: own[x, p], x)
        for t in range(1, nx):
            fromx = lax.rem(x + nx - t, nx)
            block = theirs.at[fromx]
            peer_copy(block, block, k_.o_send.at[kind, t], k_.o_recv.at[kind, t], place, 2 * fromx + core).wait_recv()
            copy_rows(lambda p, fromx=fromx: theirs[fromx, p], fromx)

    rows_out(k_.out, k_.ob, k_.oi, 1, dm.cd)
    rows_out(k_.sg, k_.sgp, k_.sgi, 2, dm.cs)
    gather_wait(k_.xz1, "dz1")
    for i, v in enumerate(conv_coarse(k_.xz1, wb[0], dm.cs)):
        v = dot(split(v), spread2) * 0.125
        for j in range(4):
            part = v[:, (j // 2) * LANES : (j // 2 + 1) * LANES]
            for d in range(S):
                at = (d * R + 4 * i + j) * dm.cs
                k_.sg[at : at + dm.cs] += part
    reduce_finish(0)
    gradient_out(2)
    gradient_out(1)
    gate_total = sum_finish(everyone, k_.sv, 4, 0)
    k_.ggate[...] = gate_total[:, 0:columns]
    k_.gvector[0:1] = row_of(gate_total[:, 2 * LANES : 2 * LANES + 1])
    k_.gvector[1:2] = row_of(gate_total[:, 2 * LANES + 1 : 2 * LANES + 2])

    def own_part(col):
        parts = [jnp.where(x == i, col[i * dm.cd : (i + 1) * dm.cd], 0.0) for i in range(nx)]
        return functools.reduce(jnp.add, parts)

    for ref, both, pick in ((k_.gen, (total_e1, total_e2), lambda v: v), (k_.gdn, (total_d1, total_d2), own_part)):
        for layer, total in enumerate(both):
            ref[0, layer : layer + 1] = row_of(pick(total[1]))
            ref[1, layer : layer + 1] = row_of(pick(total[0]))
    gradient_out(0)
    drain()


def adamw(weight, grad, moment, square, rate):
    new_moment = 0.9 * moment + 0.1 * grad
    new_square = 0.999 * square + 0.001 * grad * grad
    moment_hat = new_moment / (1.0 - 0.9**STEP)
    square_hat = new_square / (1.0 - 0.999**STEP)
    new_weight = weight - rate * (moment_hat / (jnp.sqrt(square_hat) + 1e-08) + 0.01 * weight)
    return (new_weight, new_moment, new_square)


RATES = (CONV_RATE, CONV_RATE, GATE_RATE, VECTOR_RATE, CONV_RATE, CONV_RATE, VECTOR_RATE, VECTOR_RATE)


def update_kernel(*refs):
    n = len(RATES)
    sources, targets = refs[: 2 + 4 * n], refs[2 + 4 * n : 4 + 7 * n]
    inside, outside = refs[4 + 7 * n : 6 + 11 * n], refs[6 + 11 * n : 8 + 14 * n]
    in_sem, out_sem = refs[8 + 14 * n :]
    order = (4, 1, 0, 5, 2, 3, 6, 7)

    def load(i):
        return pltpu.make_async_copy(sources[i], inside[i], in_sem.at[i])

    def store(i):
        return pltpu.make_async_copy(outside[i], targets[i], out_sem.at[i])

    for i in (1, 0):
        load(i).start()
    for k in order:
        for part in range(4):
            load(2 + part * n + k).start()
    for i in (1, 0):
        load(i).wait()
        chans, (slabs, rows) = outside[i].shape[0], outside[i].shape[1:3]
        for c in range(chans):
            v = inside[i][pl.ds(c, slabs * rows, stride=chans)]
            outside[i][c] = v.reshape(slabs, rows, LANES).astype(outside[i].dtype)
        store(i).start()
    for k in order:
        own = [2 + part * n + k for part in range(4)]
        for i in own:
            load(i).wait()
        rows = inside[own[0]].shape[0]
        step = 8 if rows % 8 == 0 and rows > 8 else rows
        for r in range(0, rows, step):
            at = slice(r, r + step)
            new = adamw(*(inside[i][at] for i in own), RATES[k])
            for part, value in enumerate(new):
                outside[2 + 3 * k + part][at] = value
        for part in range(3):
            store(2 + 3 * k + part).start()
    for i in range(len(targets)):
        store(i).wait()


def per_device(
    skip, cotangent, enc_conv1, enc_conv2, gate_proj, gate_vector, dec_conv1, dec_conv2, enc_norms, dec_norms, *states
):
    nd, nc = lax.axis_size("depth"), lax.axis_size("chan")
    dm = Dims(nd, nc, skip.shape, enc_conv1.shape[0], dec_conv1.shape[0], gate_proj.shape[0] * nc)
    S, R, H, nx, RB, E = dm.s, dm.rows, dm.half, dm.nx, dm.rb, dm.ext
    Q = H // 2
    cin3 = dm.enc_all + dm.skip_all

    def own_block(size):
        return (size, lambda j: pl.multiple_of(j * size, size), 0)

    def core_blocks(size):
        return tuple(
            (size, lambda j, i=i: pl.multiple_of((2 * i + lax.rem(j, 2)) * size, size), i * size) for i in range(nx)
        )

    dm.convs = convs = (
        Conv(dm, dm.ce, dm.skip_all, (own_block(dm.cs),)),
        Conv(dm, dm.ce, dm.enc_all, (own_block(dm.ce),)),
        Conv(dm, dm.cd, cin3, core_blocks(dm.ce) + ((dm.skip_all, lambda j: dm.enc_all, nx * dm.ce),)),
        Conv(dm, dm.cd, dm.dec_all, core_blocks(dm.cd)),
    )
    params = (enc_conv1, enc_conv2, gate_proj, gate_vector, dec_conv1, dec_conv2, enc_norms, dec_norms)
    inputs = dict(
        skip=skip, cot=cotangent, w0=enc_conv1, w1=enc_conv2, w2=dec_conv1, w3=dec_conv2,
        gate=gate_proj, vector=gate_vector, en=enc_norms, dn=dec_norms,
    )
    shape = jax.ShapeDtypeStruct
    outs = dict(
        out=shape((S * R * dm.cd, LANES), F32),
        sg=shape((S * R * dm.cs, LANES), F32),
        **{f"g{i}": shape(a.shape, F32) for i, a in enumerate((enc_conv1, enc_conv2, dec_conv1, dec_conv2))},
        **{
            name: shape(a.shape, F32)
            for name, a in (("ggate", gate_proj), ("gvector", gate_vector), ("gen", enc_norms), ("gdn", dec_norms))
        },
    )
    gq = dm.g // nc

    def coarse(block):
        return pltpu.VMEM((nc, 3, Q, block, LANES), storage(block))

    def fine():
        return pltpu.VMEM((2, S + 2, E, dm.cf, LANES), storage(dm.cd))

    def f32(*dims):
        return pltpu.VMEM((*dims, LANES), F32)

    def tiles(*dims):
        return pltpu.VMEM((*dims, 16, LANES), BF16)

    def blocks(block, *dims):
        return pltpu.VMEM((*dims, block, LANES), storage(block))

    def sems(*dims):
        return pltpu.SemaphoreType.DMA(dims)

    scratch = dict(
        xp=coarse(dm.cs), xh=coarse(dm.ce), xc=coarse(dm.ce), xz2=coarse(dm.ce), xz1=coarse(dm.ce),
        own_skip=blocks(dm.cs, S, R + 2), xs=blocks(dm.cs, nc, S + 2, E),
        own_cot=blocks(dm.cd, S, R), cots=blocks(dm.cd, nx, S, RB),
        d1=pltpu.VMEM((S + 2, E, cin3, LANES), BF16), xd=fine(), xz4=fine(), xz3=fine(),
        z1=f32(Q, dm.ce), z2=f32(Q, dm.ce), z3=f32(S * RB, dm.cf), z4=f32(S * RB, dm.cf),
        du_c=f32(Q, dm.ce), du_f=f32(S * RB, dm.cf), gg=f32(S * RB, dm.cf), cg=f32(Q, dm.ce),
        pre=f32(S + 2, E, dm.g), alpha=f32(S + 2, E, 1), pg=pltpu.VMEM((S * RB, dm.g, LANES), BF16),
        ug=f32(S, RB + 6, nx * dm.ce), cb=f32(S, H + 2, nx * dm.ce), dt=f32(S + 2, H, dm.enc_all),
        gv=f32(nc, dm.cs), sgp=f32(nx, S * RB, dm.cs), sgb=blocks(dm.cs, nx, S * RB), sgi=blocks(dm.cs, nx, S * RB),
        ob=blocks(dm.cd, nx, S * RB), oi=blocks(dm.cd, nx, S * RB),
        dzf=pltpu.VMEM((3, S, RB + 4, dm.cf, LANES), storage(dm.cd)),
        dzc=pltpu.VMEM((9, Q, dm.ce, LANES), BF16),
        fs=blocks(dm.ce, 3, nx, Q), fr=blocks(dm.ce, 3, nx, Q), fm=f32(nx, Q, dm.ce),
        st=f32(4, nd, 1), su=f32(4, nd * nx, 1), sv=pltpu.VMEM((1, nd * nx, gq, 3 * LANES), F32),
        norm_all=f32(nc, 8), rows=f32(max(dm.cs, dm.cd) * S * R),
        turned=f32(max(cv.chunks for cv in convs) * LANES),
        acc=pltpu.VMEM((nx, max(3 * cv.c for cv in convs), max(cv.wide for cv in convs)), F32),
        gate_all=pltpu.VMEM((nc, gq, 3 * LANES), F32), gate_t=pltpu.VMEM((2 * LANES, dm.g), F32),
        gate_own=pltpu.VMEM((nx * (dm.ce + dm.cs), dm.g), F32), gate_block=pltpu.VMEM((nc, gq, 3 * LANES), F32),
        **{f"wt{i}": pltpu.VMEM((3, cv.c, cv.wide), cv.kind) for i, cv in enumerate(convs)},
        **{
            f"wf{i}": pltpu.VMEM((cv.taps, 3 * cv.c) if i < 2 else (nx, cv.stored, 3 * cv.c), BF16)
            for i, cv in enumerate(convs)
        },
        **{f"wx{i}": pltpu.VMEM((nc, 3, cv.needed, cv.wide), cv.kind) for i, cv in enumerate(convs)},
        **{f"wb{i}": pltpu.VMEM((9 * cv.needed, 3 * nc * cv.o), BF16) for i, cv in enumerate(convs)},
        **{f"gt{i}": tiles(cv.share * nd) for i, cv in enumerate(convs)},
        **{f"gr{i}": tiles(nd, cv.share) for i, cv in enumerate(convs)},
        **{f"ga{i}": tiles(cv.share * nd) for i, cv in enumerate(convs)},
        **{f"gs{i}": tiles(nx, convs[i].count) for i in (2, 3)},
        **{f"gx{i}": tiles(nx, convs[i].count) for i in (2, 3)},
        g_send=sems(len(GATHERS), 2, 3 * nx), g_recv=sems(len(GATHERS), 2, 3 * nx),
        x_send=sems(len(FINE), 17), x_recv=sems(len(FINE), 17),
        t_send=sems(4, nd), t_recv=sems(4, nd), u_send=sems(5, nd * nx), u_recv=sems(5, nd * nx),
        f_send=sems(3, nx), f_recv=sems(3, nx), w_send=sems(4, nx + 1, nc), w_recv=sems(4, nx + 1, nc),
        p_send=sems(2, nx), p_recv=sems(2, nx), c_send=sems(2, nx), c_recv=sems(2, nx),
        o_send=sems(3, nx), o_recv=sems(3, nx), v_send=sems(2, nc), v_recv=sems(2, nc),
        r_send=sems(4, nd), r_recv=sems(4, nd), a_send=sems(4, nd), a_recv=sems(4, nd),
    )
    vmem = pl.BlockSpec(memory_space=pltpu.VMEM)
    out, sg, grad1, grad2, grad3, grad4, ggate, gvector, gen, gdn = pl.pallas_call(
        functools.partial(kernel, dm, (*inputs, *outs, *scratch)),
        out_shape=tuple(outs.values()),
        in_specs=[vmem] * len(inputs),
        out_specs=[vmem] * len(outs),
        scratch_shapes=list(scratch.values()),
        compiler_params=pltpu.CompilerParams(
            has_side_effects=True, collective_id=0, vmem_limit_bytes=60 * 1024 * 1024
        ),
        name="step",
    )(*inputs.values())
    grads = (grad1, grad2, ggate, gvector, grad3, grad4, gen, gdn)
    operands = (out, sg, *params, *grads, *states)
    updated = (
        shape(cotangent.shape, BF16),
        shape(skip.shape, F32),
        *(shape(p.shape, F32) for p in params for _ in range(3)),
    )
    anywhere = pl.BlockSpec(memory_space=pl.ANY)
    return pl.pallas_call(
        update_kernel,
        out_shape=updated,
        in_specs=[anywhere] * len(operands),
        out_specs=[anywhere] * len(updated),
        scratch_shapes=[
            *(pltpu.VMEM(a.shape, a.dtype) for a in operands),
            *(pltpu.VMEM(a.shape, a.dtype) for a in updated),
            pltpu.SemaphoreType.DMA((len(operands),)),
            pltpu.SemaphoreType.DMA((len(updated),)),
        ],
        compiler_params=pltpu.CompilerParams(vmem_limit_bytes=60 * 1024 * 1024),
        name="update",
    )(*operands)


def solution(mesh):
    volume = P("chan", "depth", None, None)
    row, column, norms = P("chan", None), P(None, "chan"), P(None, None, "chan")
    params = (row, row, row, column, row, row, norms, norms)
    return jax.shard_map(
        per_device,
        mesh=mesh,
        in_specs=(volume, volume) + params * 3,
        out_specs=(volume, volume) + tuple(spec for spec in params for _ in range(3)),
        check_vma=False,
    )
```

```python
import functools
import types

import jax
import jax.numpy as jnp
from jax import lax
from jax.experimental import pallas as pl
from jax.experimental.pallas import tpu as pltpu
from jax.sharding import PartitionSpec as P

STEP = 5
EPS = 1e-05
CONV_RATE = 0.03
GATE_RATE = 0.1
VECTOR_RATE = 0.5
LANES = 128
MESH = pl.DeviceIdType.MESH
F32 = jnp.float32
BF16 = jnp.bfloat16


def iota(shape, dim):
    return lax.broadcasted_iota(jnp.int32, shape, dim)


def dot(a, b):
    return jnp.dot(a, b, preferred_element_type=F32)


def dot_nt(a, b):
    return lax.dot_general(a, b, (((1,), (1,)), ((), ())), preferred_element_type=F32)


def from_left(v, width):
    return jnp.where(iota(v.shape, 1) % width == 0, 0.0, pltpu.roll(v, 1, 1))


def from_right(v, width):
    return jnp.where(iota(v.shape, 1) % width == width - 1, 0.0, pltpu.roll(v, LANES - 1, 1))


def halves(low, high):
    return pltpu.roll(jnp.where(iota(low.shape, 1) < LANES // 2, low, high), LANES // 2, 1)


def split(v):
    high = v.astype(BF16)
    return jnp.concatenate([high, (v - high.astype(F32)).astype(BF16)], 1)


def storage(block):
    return BF16 if block % 16 == 0 else F32


def flat(ref, s, r):
    if len(ref.shape) == 4:
        return ref[s, r]
    v = ref[:, :, s, r]
    return jnp.concatenate([v[c, i] for i in range(v.shape[1]) for c in range(2)], 0).astype(BF16)


class Dims:
    def __init__(self, nd, nc, skip, enc, dec, gate):
        self.nd, self.nc, self.nx = nd, nc, nc // 2
        self.s, self.rows, self.cols = skip[1:]
        self.cs, self.ce, self.cd, self.g = skip[0], enc, dec, gate
        self.half, self.hcols = self.rows // 2, self.cols // 2
        self.fine_total = nd * self.s * self.rows * self.cols
        self.coarse_total = self.fine_total // 8
        self.enc_all = nc * enc
        self.skip_all = nc * skip[0]
        self.dec_all = nc * dec
        self.rb = self.rows // self.nx
        self.ext = self.rb + 2
        self.cf = self.nx * dec


GATHERS = ("pooled", "skip", "hidden", "coarse", "dz2", "dz1")
FINE = ("hidden", "dz4", "dz3")


class Conv:
    def __init__(self, dm, o, c, blocks):
        self.o, self.c, self.blocks = o, c, blocks
        self.length = 27 * c
        self.chunks = -(-self.length // LANES)
        self.per = LANES // o
        self.tiles = -(-9 // self.per)
        self.wide = self.tiles * LANES
        self.kind = storage(min(size for size, _, _ in blocks))
        self.needed = sum(size for size, _, _ in blocks)
        self.count = 3 * c // 16 * self.tiles
        self.share = -(-self.count // dm.nd)
        self.taps = 9 * o
        self.stored = -(-self.taps // 16) * 16


def kernel(dm, names, *refs):
    k_ = types.SimpleNamespace(**dict(zip(names, refs)))
    nd, nc, nx, S, R, H = dm.nd, dm.nc, dm.nx, dm.s, dm.rows, dm.half
    W, V = dm.cols, dm.hcols
    Q, RB, E = H // 2, dm.rb, dm.ext
    place = lax.axis_index("depth")
    me = lax.axis_index("chan")
    x, core = lax.div(me, 2), lax.rem(me, 2)
    other = 1 - core
    mate = 2 * x + other
    row0, h0 = x * RB, x * (RB // 2)
    first, last = place == 0, place == nd - 1
    top, bottom = x == 0, x == nx - 1
    convs = dm.convs
    pending = []
    wt, wf, wx, wb = ([getattr(k_, f"{kind}{i}") for i in range(4)] for kind in ("wt", "wf", "wx", "wb"))
    gt, gr, ga = ([getattr(k_, f"{kind}{i}") for i in range(4)] for kind in ("gt", "gr", "ga"))
    weights = (k_.w0, k_.w1, k_.w2, k_.w3)
    grads = (k_.g0, k_.g1, k_.g2, k_.g3)
    turned, acc = k_.turned, k_.acc

    def no(cond):
        return jnp.logical_not(cond)

    def peer_copy(src, dst, send, recv, depth, chan):
        return pltpu.make_async_remote_copy(
            src_ref=src, dst_ref=dst, send_sem=send, recv_sem=recv,
            device_id={"depth": depth, "chan": chan}, device_id_type=MESH,
        )

    def guarded(cond, fn):
        if cond is None:
            fn()
        else:
            pl.when(cond)(fn)

    def drain():
        for cond, fn in pending:
            guarded(cond, fn)
        pending.clear()

    def launch(cond, copy):
        guarded(cond, lambda: copy().start())
        pending.append((cond, lambda: copy().wait_send()))

    def arrive(cond, copy):
        guarded(cond, lambda: copy().wait_recv())

    def both(a, b):
        return b if a is None else a if b is None else jnp.logical_and(a, b)

    can_send = (no(last), None, no(first))
    can_recv = (no(first), None, no(last))

    def slices(side, n):
        return (pl.ds(n, 1), pl.ds(1, n), pl.ds(1, 1))[side], (pl.ds(0, 1), pl.ds(1, n), pl.ds(n + 1, 1))[side]

    def at_x(t):
        up, down = x + t, x - t
        return jnp.where(up >= nx, up - nx, up), jnp.where(down < 0, down + nx, down)


    def gather_start(ref, which, source_at=None):
        n = ref.shape[2] - 2
        k = GATHERS.index(which)
        for side in (0, 2, 1):
            own, theirs = slices(side, n)
            for t in range(nx):
                if side == 1 and t == 0:
                    continue
                tox = at_x(t)[0]

                def copy(side=side, t=t, own=own, theirs=theirs, tox=tox):
                    start = (n, 1, 1)[side] - 1
                    size = (1, n, 1)[side]
                    src = ref.at[core, x, own] if source_at is None else source_at(pl.ds(start, size), tox)
                    return peer_copy(
                        src, ref.at[core, x, theirs], k_.g_send.at[k, side, t], k_.g_recv.at[k, side],
                        place + 1 - side, 2 * tox + core,
                    )

                launch(can_send[side], copy)

    def handed(ref, k, c):
        return peer_copy(ref.at[c], ref.at[c], k_.h_send.at[k], k_.h_recv.at[k], place, mate)

    def gather_pass(ref, which):
        n = ref.shape[2] - 2
        k = GATHERS.index(which)
        for side in (1, 0, 2):
            theirs = slices(side, n)[1]
            if side != 1:
                got = ref.at[core, :, theirs]
            elif nx == 2:
                got = ref.at[core, 1 - x, theirs]
            else:
                got = ref.at[core, pl.ds(0, nx - 1), theirs]
            arrive(
                can_recv[side],
                lambda got=got, side=side: peer_copy(got, got, k_.g_send.at[k, side, 0], k_.g_recv.at[k, side], place, mate),
            )
        launch(None, lambda: handed(ref, k, core))

    def gather_wait(ref, which):
        handed(ref, GATHERS.index(which), other).wait_recv()

    def fine_parts(ref, which, side):
        k = FINE.index(which)
        own, theirs = slices(side, S)
        rows = [(None, None, pl.ds(1, RB), pl.ds(1, RB), x)] if side != 1 else []
        if nx > 1:
            rows.append((no(top), no(bottom), pl.ds(1, 1), pl.ds(E - 1, 1), x - 1))
            rows.append((no(bottom), no(top), pl.ds(RB, 1), pl.ds(0, 1), x + 1))
        parts = []
        for i, (sends, gets, row, at, tox) in enumerate(rows):
            sems = (k_.x_send.at[k, side, i], k_.x_recv.at[k, side, i])
            target = ref.at[core, theirs, at]
            parts.append((
                both(can_send[side], sends), both(can_recv[side], gets),
                functools.partial(
                    peer_copy, ref.at[core, own, row], target, *sems, place + 1 - side, 2 * tox + core
                ),
                functools.partial(peer_copy, target, target, *sems, place, mate),
            ))
        return parts

    def fine_start(ref, which):
        for side in (0, 2, 1):
            for sends, _, out, _ in fine_parts(ref, which, side):
                launch(sends, out)

    def fine_handed(ref, which, part, c):
        k = FINE.index(which)
        block = ref.at[c, (pl.ds(0, S + 1), pl.ds(S + 1, 1))[part]]
        return peer_copy(block, block, k_.y_send.at[k, part], k_.y_recv.at[k, part], place, mate)

    def fine_pass(ref, which, part):
        for side in ((1, 0), (2,))[part]:
            for _, gets, _, back in fine_parts(ref, which, side):
                arrive(gets, back)
        fine_handed(ref, which, part, core).start()

    def fine_passed(ref, which):
        for part in range(2):
            pending.append((None, lambda part=part: fine_handed(ref, which, part, core).wait_send()))

    def fine_wait(ref, which, part):
        fine_handed(ref, which, part, other).wait_recv()

    def natural(ref, s, r):
        v = ref[:, s, r]
        size = dm.cd
        return jnp.concatenate(
            [v[c, i * size : (i + 1) * size] for i in range(nx) for c in range(2)], 0
        ).astype(BF16)

    def in_turn(count, fn):
        if count <= 16:
            for i in range(count):
                fn(i)
        else:

            def body(i, carry):
                fn(i)
                return carry

            lax.fori_loop(0, count, body, 0)

    def slab_peers(i):
        to = place + 1 + i
        return jnp.where(to >= nd, to - nd, to), me

    def wide_peers(i):
        i = i + 1
        dt, xt = (i // nx, i % nx) if isinstance(i, int) else (lax.div(i, nx), lax.rem(i, nx))
        to, tox = place + dt, x + xt
        return jnp.where(to >= nd, to - nd, to), 2 * jnp.where(tox >= nx, tox - nx, tox) + core

    def exchange(n, peers, copy):
        in_turn(n - 1, lambda i: copy(*peers(i)).start())

    def sum_start(group, ref, k, slot, tile, source=None):
        n, own, peers, send, recv = group
        ref[slot, own] = tile

        def copy(depth, chan):
            src = ref.at[slot, own] if source is None else source(chan)
            return peer_copy(src, ref.at[slot, own], send.at[k], recv.at[k], depth, chan)

        exchange(n, peers, copy)
        pending.append((None, lambda: all_of(group, ref, k, slot).wait_send()))

    def all_of(group, ref, k, slot):
        n, _, _, send, recv = group
        every = ref.at[slot, pl.ds(0, n - 1)]
        return peer_copy(every, every, send.at[k], recv.at[k], place, mate)

    def sum_finish(group, ref, k, slot):
        all_of(group, ref, k, slot).wait_recv()
        return jnp.sum(ref[slot], axis=0)

    slabs = (nd, place, slab_peers, k_.t_send, k_.t_recv)
    everyone = (nd * nx, place * nx + x, wide_peers, k_.u_send, k_.u_recv)

    def columns_of(row, m):
        lane, channel = iota((m, LANES), 1), iota((m, LANES), 0)
        return tuple(
            jnp.sum(jnp.where(lane == channel + i * m, row, 0.0), axis=1, keepdims=True) for i in range(2)
        )

    def coarse_sums(slot, sums):
        sum_start(slabs, k_.st, slot, slot, pack(*sums))

    def coarse_totals(slot):
        return columns_of(sum_finish(slabs, k_.st, slot, slot), dm.ce)

    def fine_sums(slot, sums):
        sum_start(everyone, k_.su, slot, slot, pack(*sums))

    def fine_totals(slot):
        return columns_of(sum_finish(everyone, k_.su, slot, slot), dm.cf)

    def turn_in(w, cv):
        eye = (iota((LANES, LANES), 0) == iota((LANES, LANES), 1)).astype(BF16)

        def chunk(a):
            return dot_nt(eye, jnp.concatenate([a] * cv.per, 0).astype(BF16))

        full = cv.length // LANES

        def body(i, carry):
            at = pl.multiple_of(i * LANES, LANES)
            turned[pl.ds(at, LANES)] = chunk(w[:, pl.ds(at, LANES)])
            return carry

        lax.fori_loop(0, full, body, 0, unroll=4)
        if full < cv.chunks:
            a = w[:, full * LANES :]
            a = jnp.concatenate([a, jnp.zeros((cv.o, LANES - a.shape[1]), F32)], 1)
            turned[full * LANES : (full + 1) * LANES] = chunk(a)

    def prepare(k):
        cv, w, own = convs[k], weights[k], wt[k]
        out = wf[k] if k < 2 else wf[k].at[x]
        turn_in(w, cv)
        group = iota((cv.c, LANES), 1) // cv.o
        for kz in range(3):
            for j in range(cv.tiles):
                tile = None
                for g in range(cv.per):
                    t = j * cv.per + g
                    if t < 9:
                        v = turned[pl.ds(9 * kz + t, cv.c, stride=27)]
                        tile = v if tile is None else jnp.where(group == g, v, tile)
                own[kz, :, j * LANES : (j + 1) * LANES] = tile.astype(BF16).astype(own.dtype)
        eye = (iota((LANES, LANES), 0) == iota((LANES, LANES), 1)).astype(BF16)
        for j in range(cv.tiles):
            v = jnp.concatenate([own[kz, :, j * LANES : (j + 1) * LANES] for kz in range(3)], 0)
            size = min(LANES, 9 * cv.o - j * LANES)
            out[j * LANES : j * LANES + size] = dot_nt(eye, v.astype(BF16))[0:size].astype(BF16)

    def forward_copy(k, t):
        block = wf[k].at[x]
        return peer_copy(
            block, block, k_.p_send.at[k - 2, t], k_.p_recv.at[k - 2, t], place, 2 * lax.rem(x + t, nx) + core
        )

    def forward_start(k):
        for t in range(1, nx):
            launch(None, functools.partial(forward_copy, k, t))

    def forward_wait(k):
        for t in range(1, nx):
            fromx = lax.rem(x + nx - t, nx)
            block = wf[k].at[fromx]
            peer_copy(
                block, block, k_.p_send.at[k - 2, t], k_.p_recv.at[k - 2, t], place, 2 * fromx + core
            ).wait_recv()

    def forward_weight(k):
        return jnp.concatenate([wf[k][i, 0 : convs[k].taps] for i in range(nx)], 0)

    def weights_start(k):
        cv = convs[k]
        for b, (size, start, at) in enumerate(cv.blocks):
            wx[k][me, :, at : at + size] = wt[k][:, pl.ds(start(me), size)]
            for t in range(1, nc):
                to = lax.rem(me + t, nc)

                def copy(to=to, t=t, b=b, size=size, start=start, at=at):
                    return peer_copy(
                        wt[k].at[:, pl.ds(start(to), size)], wx[k].at[me, :, pl.ds(at, size)],
                        k_.w_send.at[k, b, t], k_.w_recv.at[k, b, t], place, to,
                    )

                launch(None, copy)

    def weights_finish(k):
        cv = convs[k]
        for b, (size, _, at) in enumerate(cv.blocks):
            for t in range(1, nc):
                source = lax.rem(me + nc - t, nc)
                theirs = wx[k].at[source, :, pl.ds(at, size)]
                peer_copy(theirs, theirs, k_.w_send.at[k, b, t], k_.w_recv.at[k, b, t], place, source).wait_recv()
        for t in range(9):
            pieces = [
                wx[k][j, 2 - kz, :, t * cv.o : (t + 1) * cv.o].astype(F32) for kz in range(3) for j in range(nc)
            ]
            wb[k][(8 - t) * cv.needed : (9 - t) * cv.needed] = jnp.concatenate(pieces, 1).astype(BF16)

    def tiles_of(k, part, put):
        cv = convs[k]

        def tile(i, carry):
            at = pl.multiple_of(i * 16, 16)
            for j in range(cv.tiles):
                put(i * cv.tiles + j, acc[part, pl.ds(at, 16), j * LANES : (j + 1) * LANES].astype(BF16))
            return carry

        lax.fori_loop(0, 3 * cv.c // 16, tile, 0, unroll=4)

    def cross_start(k):
        gs, gx = (k_.gs2, k_.gs3)[k - 2], (k_.gx2, k_.gx3)[k - 2]
        for part in range(nx):

            def put(i, v, part=part):
                gs[part, i] = v

            tiles_of(k, part, put)
        for t in range(1, nx):
            tox = lax.rem(x + t, nx)

            def copy(t=t, tox=tox):
                return peer_copy(
                    gs.at[tox], gx.at[x], k_.c_send.at[k - 2, t], k_.c_recv.at[k - 2, t], place, 2 * tox + core
                )

            launch(None, copy)

    def cross_finish(k):
        cv, gs, gx = convs[k], (k_.gs2, k_.gs3)[k - 2], (k_.gx2, k_.gx3)[k - 2]
        sources = [lax.rem(x + nx - t, nx) for t in range(1, nx)]
        for t, fromx in enumerate(sources, 1):
            theirs = gx.at[fromx]
            peer_copy(
                theirs, theirs, k_.c_send.at[k - 2, t], k_.c_recv.at[k - 2, t], place, 2 * fromx + core
            ).wait_recv()

        def add(i, carry):
            for j in range(cv.tiles):
                p = i * cv.tiles + j
                v = gs[x, p].astype(F32)
                for fromx in sources:
                    v += gx[fromx, p].astype(F32)
                gt[k][p] = v.astype(BF16)
            return carry

        lax.fori_loop(0, 3 * cv.c // 16, add, 0, unroll=4)
        reduce_send(k)

    def reduce_start(k):
        def put(i, v):
            gt[k][i] = v

        tiles_of(k, 0, put)
        reduce_send(k)

    def reduce_send(k):
        cv = convs[k]
        for i in range(cv.count, cv.share * nd):
            gt[k][i] = jnp.zeros((16, LANES), BF16)
        gr[k][place] = gt[k][pl.ds(place * cv.share, cv.share)]

        def copy(to, chan):
            return peer_copy(
                gt[k].at[pl.ds(to * cv.share, cv.share)], gr[k].at[place], k_.r_send.at[k], k_.r_recv.at[k], to, chan
            )

        exchange(nd, slab_peers, copy)
        pending.append((None, lambda: reduce_all(k).wait_send()))

    def reduce_all(k):
        every = gr[k].at[pl.ds(0, nd - 1)]
        return peer_copy(every, every, k_.r_send.at[k], k_.r_recv.at[k], place, mate)

    def share_all(k):
        every = ga[k].at[pl.ds(0, (nd - 1) * convs[k].share)]
        return peer_copy(every, every, k_.a_send.at[k], k_.a_recv.at[k], place, mate)

    def reduce_finish(k):
        cv = convs[k]
        reduce_all(k).wait_recv()
        own = pl.ds(place * cv.share, cv.share)
        ga[k][own] = jnp.sum(gr[k][...].astype(F32), axis=0).astype(BF16)

        def copy(to, chan):
            return peer_copy(ga[k].at[own], ga[k].at[own], k_.a_send.at[k], k_.a_recv.at[k], to, chan)

        exchange(nd, slab_peers, copy)
        pending.append((None, lambda: share_all(k).wait_send()))

    def gradient_out(k):
        cv, out = convs[k], grads[k]
        share_all(k).wait_recv()
        group = iota((16, LANES), 1) // cv.o

        def scatter(i, carry):
            for kz in range(3):
                for j in range(cv.tiles):
                    v = ga[k][(kz * (cv.c // 16) + i) * cv.tiles + j].astype(F32)
                    for g in range(cv.per):
                        t = j * cv.per + g
                        if t < 9:
                            turned[pl.ds(9 * kz + t + i * (16 * 27), 16, stride=27)] = jnp.where(group == g, v, 0.0)
            return carry

        lax.fori_loop(0, cv.c // 16, scatter, 0, unroll=2)

        pick = (iota((cv.o, LANES), 1) % cv.o == iota((cv.o, LANES), 0)).astype(BF16)
        step = 8 * LANES
        for at in range(0, cv.length, step):
            size = min(step, cv.length - at)
            v = dot_nt(pick, turned[at : at + -(-size // LANES) * LANES].astype(BF16))
            out[:, at : at + size] = v[:, 0:size]

    def column(row):
        n = row.shape[1]
        eye = iota((n, n), 0) == iota((n, n), 1)
        return jnp.sum(jnp.where(eye, row, 0.0), axis=1, keepdims=True)

    def row_of(col):
        n = col.shape[0]
        eye = iota((n, n), 0) == iota((n, n), 1)
        return jnp.sum(jnp.where(eye, col, 0.0), axis=0, keepdims=True)

    def clear_halos(ref):
        def clear(at):
            if len(ref.shape) == 5:
                ref[core, at] = jnp.zeros(ref.shape[2:], ref.dtype)
            else:
                for i in range(nx):
                    ref[core, i, at] = jnp.zeros(ref.shape[3:], ref.dtype)

        pl.when(first)(lambda: clear(0))
        pl.when(last)(lambda: clear(ref.shape[-4] - 1))

    def clear_rows(ref):
        def clear(at):
            for i in range(S + 2):
                ref[core, i, at] = jnp.zeros(ref.shape[3:], ref.dtype)

        pl.when(top)(lambda: clear(0))
        pl.when(bottom)(lambda: clear(E - 1))

    def conv(row, weight, n, m, groups, emit, init, late=None):
        per = RB // n

        def body(i, carry):
            if late is not None:
                pl.when(i == (S - 1) * per - 1)(late[0])
                pl.when(i == (S - 1) * per)(late[1])
            d = lax.div(i, per)
            r0 = (i - d * per) * n
            v = jnp.concatenate(
                [jnp.concatenate([row(d + kz, r0 + j) for j in range(n + 2)], 1) for kz in range(3)], 0
            )
            y = dot(weight(), v)
            results = []
            for j in range(n):
                parts = []
                for g in range(groups):
                    a = []
                    for kx in range(3):
                        terms = [
                            y[
                                (9 * g + 3 * ky + kx) * m : (9 * g + 3 * ky + kx + 1) * m,
                                (j + ky) * LANES : (j + ky + 1) * LANES,
                            ]
                            for ky in range(3)
                        ]
                        a.append(terms[0] + terms[1] + terms[2])
                    parts.append(from_left(a[0], W) + a[1] + from_right(a[2], W))
                results.append(jnp.concatenate(parts, 0) if groups > 1 else parts[0])
            return emit(d, r0, results, carry)

        return lax.fori_loop(0, S * per, body, init)

    def conv_stats(row, weight, z, n, late=None):
        def emit(d, r0, results, carry):
            total, square = carry
            for j, v in enumerate(results):
                z[d * RB + r0 + j] = v
                total, square = total + v, square + v * v
            return total, square

        blank = jnp.zeros((dm.cf, LANES), F32)
        return conv(row, weight, n, dm.cd, nx, emit, (blank, blank), late)

    def weight_grad(row, k):
        cv = convs[k]
        dzf = k_.dzf
        n = E // 2
        acc[:, 0 : 3 * cv.c, 0 : cv.wide] = jnp.zeros((nx, 3 * cv.c, cv.wide), F32)

        def body(i, carry):
            d = lax.div(i, 2)
            r0 = (i - 2 * d) * n
            v = jnp.concatenate(
                [jnp.concatenate([row(d + kz, r0 + j) for j in range(n)], 1) for kz in range(3)], 0
            )
            for part in range(nx):
                y = jnp.concatenate(
                    [
                        jnp.concatenate(
                            [dzf[kx, d, r0 + j + 2 - ky, part * cv.o : (part + 1) * cv.o] for j in range(n)], 1
                        )
                        for ky in range(3)
                        for kx in range(3)
                    ],
                    0,
                ).astype(BF16)
                acc[part, 0 : 3 * cv.c, 0 : cv.taps] += dot_nt(v, y)
            return carry

        lax.fori_loop(0, S * 2, body, 0)

    def conv_coarse(ref, weight, m):
        v = jnp.concatenate(
            [jnp.concatenate([flat(ref, kz, i) for i in range(Q)], 1) for kz in range(3)], 0
        )
        y = dot(weight[...], v)
        blank = jnp.zeros((m, LANES), F32)

        def shifted(ky, i):
            if not 0 <= i < Q:
                return blank
            a, b, c = (
                y[(3 * ky + kx) * m : (3 * ky + kx + 1) * m, i * LANES : (i + 1) * LANES] for kx in range(3)
            )
            return from_left(a, V) + b + from_right(c, V)

        before = [shifted(0, i) for i in range(-1, Q)]
        after = [shifted(2, i) for i in range(Q + 1)]
        return [
            shifted(1, i) + halves(before[i + 1] + after[i + 1], before[i] + after[i]) for i in range(Q)
        ]

    def conv_stats_coarse(ref, weight, z, m):
        total = square = jnp.zeros((m, LANES), F32)
        for i, v in enumerate(conv_coarse(ref, weight, m)):
            z[i] = v
            total, square = total + v, square + v * v
        return total, square

    def weight_grad_coarse(ref, k):
        cv = convs[k]
        v = jnp.concatenate(
            [jnp.concatenate([flat(ref, kz, i) for i in range(Q)], 1) for kz in range(3)], 0
        )
        y = jnp.concatenate([jnp.concatenate([k_.dzc[t, i] for i in range(Q)], 1) for t in range(9)], 0)
        acc[0, 0 : 3 * cv.c, 0 : cv.taps] = dot_nt(v, y.astype(BF16))

    def pack(a, b):
        m = a.shape[0]
        a = jnp.sum(a, axis=1, keepdims=True)
        b = jnp.sum(b, axis=1, keepdims=True)
        lane, channel = iota((m, LANES), 1), iota((m, LANES), 0)
        both = jnp.where(lane == channel, a, jnp.where(lane == channel + m, b, 0.0))
        return jnp.sum(both, axis=0, keepdims=True)

    def moments(total, count):
        mean = total[0] / count
        var = total[1] / count - mean * mean
        return mean, lax.rsqrt(var + EPS)

    def wide(column):
        return jnp.broadcast_to(column, (column.shape[0], LANES))

    def factors(stats, norm):
        mean, inv = stats
        gain, shift = norm
        return wide(mean), wide(gain * inv), wide(shift)

    def norm_rows(z, stats, norm, emit, n):
        mean, scale, shift = factors(stats, norm)

        def body(i, carry):
            for j in range(n):
                p = i * n + j
                u = (z[p] - mean) * scale + shift
                emit(p, u * jax.nn.sigmoid(u))
            return carry

        lax.fori_loop(0, z.shape[0] // n, body, 0)

    def norm_back_sums(z, keep_du, stats, norm, grad, n):
        mean, scale, shift = factors(stats, norm)
        inv = wide(stats[1])
        m = z.shape[1]

        def body(i, carry):
            a, b = carry
            for j in range(n):
                p = i * n + j
                centred = z[p] - mean
                u = centred * scale + shift
                sigma = jax.nn.sigmoid(u)
                v = grad(p) * sigma * (1.0 + u * (1.0 - sigma))
                keep_du(p, v)
                a, b = a + v, b + v * (centred * inv)
            return a, b

        blank = jnp.zeros((m, LANES), F32)
        return lax.fori_loop(0, z.shape[0] // n, body, (blank, blank))

    def back_factors(stats, norm, total, count):
        mean, inv = stats
        scale = norm[0] * inv
        return wide(mean), wide(scale), wide(-scale * total[0] / count), wide(-scale * inv * total[1] / count)

    def norm_back_fine(z, given, ref):
        mean, scale, level, slope = given
        dzf = k_.dzf

        def body(d, carry):
            for r in range(RB):
                p = d * RB + r
                v = scale * k_.du_f[p] + level + slope * (z[p] - mean)
                low = v.astype(BF16)
                ref[core, 1 + d, 1 + r] = low.astype(ref.dtype)
                v = low.astype(F32)
                dzf[0, d, 2 + r] = from_right(v, W).astype(dzf.dtype)
                dzf[1, d, 2 + r] = low.astype(dzf.dtype)
                dzf[2, d, 2 + r] = from_left(v, W).astype(dzf.dtype)
            return carry

        lax.fori_loop(0, S, body, 0)

    def norm_back_coarse(z, given, ref):
        mean, scale, level, slope = given
        rows = []
        for i in range(Q):
            low = (scale * k_.du_c[i] + level + slope * (z[i] - mean)).astype(BF16)
            ref[core, x, 1, i] = low.astype(ref.dtype)
            rows.append(low.astype(F32))
        blank = jnp.zeros_like(rows[0])
        rows = [blank] + rows + [blank]
        for i in range(Q):
            before, here, after = rows[i : i + 3]
            for ky, v in enumerate((halves(after, here), here, halves(here, before))):
                for kx, u in enumerate((from_right(v, V), v, from_left(v, V))):
                    k_.dzc[3 * ky + kx, i] = u.astype(k_.dzc.dtype)

    def keep_du(ref):
        def store(p, v):
            ref[p] = v

        return store

    barrier = pltpu.get_barrier_semaphore()

    def greet(depth, chan):
        pl.semaphore_signal(barrier, inc=1, device_id={"depth": depth, "chan": chan}, device_id_type=MESH)

    exchange(nd * nx, wide_peers, lambda depth, chan: types.SimpleNamespace(start=lambda: greet(depth, chan)))
    for t in range(nx):
        greet(place, 2 * at_x(t)[0] + other)

    hc = iota((LANES, LANES), 0)
    fc = iota((LANES, LANES), 1)
    half = LANES // 2

    def up_table(coarse, fine):
        base = fine // 2
        beside = jnp.clip(base + jnp.where(fine % 2 == 0, -1, 1), 0, V - 1)
        near = (coarse == base).astype(F32)
        far = (coarse == beside).astype(F32)
        return (0.75 * near + 0.25 * far).astype(BF16)

    pool = jnp.concatenate([(hc // 2 == fc - at).astype(BF16) for at in (0, half)], 0)
    spread = jnp.concatenate([(hc - at == fc // 2).astype(BF16) for at in (0, half)], 1)
    up = jnp.concatenate([up_table(hc - at, fc) for at in (0, half)], 1)
    down = jnp.concatenate([up_table(fc, hc)] * 2, 0)
    spread2 = jnp.concatenate([spread, spread], 0)

    def take_rows(ref):
        for c in range(ref.shape[0]):
            k_.rows[c * S * R : (c + 1) * S * R] = ref[c].astype(F32).reshape(S * R, LANES)

    def row_of_all(p, chans):
        return k_.rows[pl.ds(p, chans, stride=S * R)]

    xp, xs, own_skip = k_.xp, k_.xs, k_.own_skip
    clear_halos(xp)
    take_rows(k_.skip)
    for i in range(S):
        for r in (0, R + 1):
            own_skip[i, r] = jnp.zeros((dm.cs, LANES), own_skip.dtype)

    def take_skip(i, carry):
        parts = []
        for d in range(S):
            v = [row_of_all(d * R + 4 * i + j, dm.cs).astype(BF16) for j in range(4)]
            for j in range(4):
                own_skip[d, 1 + 4 * i + j] = v[j].astype(own_skip.dtype)
            parts += [jnp.concatenate([v[j], v[2 + j]], 1) for j in range(2)]
        v = dot(jnp.concatenate(parts, 0), pool).reshape(2 * S, dm.cs, LANES)
        xp[core, x, 1, i] = (jnp.sum(v, axis=0) * 0.125).astype(BF16).astype(xp.dtype)
        return carry

    lax.fori_loop(0, Q, take_skip, 0, unroll=3)
    pl.semaphore_wait(barrier, nd * nx - 1 + nx)
    gather_start(xp, "pooled")
    clear_halos(xs)
    xs[core, x, 1 : S + 1] = own_skip[:, pl.ds(row0, E)]
    gather_start(xs, "skip", lambda at, tox: own_skip.at[at, pl.ds(tox * RB, E)])

    gq = dm.g // nc
    columns = dm.enc_all + dm.skip_all
    gate_all, norm_all = k_.gate_all, k_.norm_all
    gate_all[me, :, 0:columns] = k_.gate[...]
    lane = iota((gq, LANES), 1)
    gate_all[me, :, 2 * LANES :] = jnp.where(
        lane == 0, column(k_.vector[0:1]), jnp.where(lane == 1, column(k_.vector[1:2]), 0.0)
    )
    for layer in range(2):
        for part in range(2):
            at = 2 * layer + part
            norm_all[me, at : at + 1, 0 : dm.cd] = k_.dn[part, layer : layer + 1]

    def constants(i, t, source, to):
        ref = (norm_all, gate_all)[i]
        return peer_copy(ref.at[source], ref.at[source], k_.v_send.at[i, t], k_.v_recv.at[i, t], place, to)

    for i in range(2):
        for t in range(1, nc):
            launch(None, functools.partial(constants, i, t, me, lax.rem(me + t, nc)))
    prepare(0)
    xd, xz4, xz3, d1 = k_.xd, k_.xz4, k_.xz3, k_.d1
    for ref in (xd, xz4, xz3):
        clear_rows(ref)
        clear_halos(ref)
    for ref in (k_.xh, k_.xz2, k_.xz1):
        clear_halos(ref)
    for i in range(S):
        for r in (0, 1, RB + 2, RB + 3):
            for kx in range(3):
                k_.dzf[kx, i, r] = jnp.zeros(k_.dzf.shape[3:], k_.dzf.dtype)
        for r in range(3):
            k_.ug[i, r] = jnp.zeros(k_.ug.shape[2:], F32)
            k_.ug[i, RB + 3 + r] = jnp.zeros(k_.ug.shape[2:], F32)
        for r in range(H + 2):
            k_.cb[i, r] = jnp.zeros(k_.cb.shape[2:], F32)

    def norm_of(layer):
        return column(k_.en[0, layer : layer + 1]), column(k_.en[1, layer : layer + 1])

    norm_e1, norm_e2 = norm_of(0), norm_of(1)

    gather_pass(xp, "pooled")
    gather_wait(xp, "pooled")
    coarse_sums(0, conv_stats_coarse(xp, wf[0], k_.z1, dm.ce))
    prepare(1)
    stats_e1 = moments(coarse_totals(0), dm.coarse_total)

    def keep_coarse(ref):
        def store(p, v):
            ref[core, x, 1, p] = v.astype(BF16).astype(ref.dtype)

        return store

    norm_rows(k_.z1, stats_e1, norm_e1, keep_coarse(k_.xh), Q)
    gather_start(k_.xh, "hidden")
    prepare(2)
    forward_start(2)
    gather_pass(k_.xh, "hidden")
    gather_pass(xs, "skip")
    gather_wait(k_.xh, "hidden")
    coarse_sums(1, conv_stats_coarse(k_.xh, wf[1], k_.z2, dm.ce))
    take_rows(k_.cot)

    def take_cot(i, carry):
        for d in range(S):
            for j in range(4):
                v = row_of_all(d * R + 4 * i + j, dm.cd).astype(BF16)
                k_.own_cot[d, 4 * i + j] = v.astype(k_.own_cot.dtype)
        return carry

    lax.fori_loop(0, Q, take_cot, 0)
    k_.cots[x] = k_.own_cot[:, pl.ds(row0, RB)]
    stats_e2 = moments(coarse_totals(1), dm.coarse_total)
    norm_rows(k_.z2, stats_e2, norm_e2, keep_coarse(k_.xc), Q)
    gather_start(k_.xc, "coarse")
    prepare(3)
    for t in range(1, nc):
        for i in range(2):
            source = lax.rem(me + nc - t, nc)
            constants(i, t, source, source).wait_recv()
    gate_full = gate_all[...].reshape(dm.g, 3 * LANES)
    wg = gate_full[:, 0:columns].astype(BF16)
    gbias = gate_full[:, 2 * LANES : 2 * LANES + 1]
    gout = gate_full[:, 2 * LANES + 1 : 2 * LANES + 2]
    k_.gate_t[...] = jnp.transpose(gate_full[:, 0 : 2 * LANES])
    own_rows = [k_.gate_t[pl.ds(pl.multiple_of((2 * i + core) * dm.ce, dm.ce), dm.ce)] for i in range(nx)]
    own_rows += [
        k_.gate_t[pl.ds(pl.multiple_of(dm.enc_all + (2 * i + core) * dm.cs, dm.cs), dm.cs)] for i in range(nx)
    ]
    k_.gate_own[...] = jnp.concatenate(own_rows, 0)

    def norm_fine(layer):
        return tuple(
            jnp.concatenate(
                [column(norm_all[2 * i + core, 2 * layer + part : 2 * layer + part + 1, 0 : dm.cd]) for i in range(nx)], 0
            )
            for part in range(2)
        )

    norm_d1, norm_d2 = norm_fine(0), norm_fine(1)
    gather_pass(k_.xc, "coarse")
    gather_wait(k_.xc, "coarse")
    forward_start(3)

    dt = k_.dt

    def up_depth(i, carry):
        t = []
        for j in range(3):
            v = dot(flat(k_.xc, j, i), up)
            t.append(jnp.stack([v[:, 0:LANES], v[:, LANES:]], 0))
        below = jnp.where(first, t[1], t[0])
        above = jnp.where(last, t[1], t[2])
        near = 0.75 * t[1]
        here = 0.25 * t[1]
        rows = pl.ds(i * 2, 2)
        dt[0, rows] = jnp.where(first, 0.0, 0.75 * below + here)
        dt[1, rows] = near + 0.25 * below
        dt[2, rows] = near + 0.25 * above
        dt[3, rows] = jnp.where(last, 0.0, 0.75 * above + here)
        return carry

    lax.fori_loop(0, Q, up_depth, 0)

    def up_rows(i, carry):
        here = h0 + i
        before, after = jnp.maximum(here - 1, 0), jnp.minimum(here + 1, H - 1)
        for j in range(S + 2):
            v = 0.75 * dt[j, here]
            d1[j, 1 + 2 * i, 0 : dm.enc_all] = (v + 0.25 * dt[j, before]).astype(BF16)
            d1[j, 2 + 2 * i, 0 : dm.enc_all] = (v + 0.25 * dt[j, after]).astype(BF16)
        return carry

    lax.fori_loop(0, RB // 2, up_rows, 0)
    for edge, at, near, far in (
        (top, 0, jnp.maximum(h0 - 1, 0), h0),
        (bottom, E - 1, jnp.minimum(h0 + RB // 2, H - 1), h0 + RB // 2 - 1),
    ):
        for j in range(S + 2):
            v = jnp.where(edge, 0.0, 0.75 * dt[j, near] + 0.25 * dt[j, far])
            d1[j, at, 0 : dm.enc_all] = v.astype(BF16)
    for t in range(1, nx):
        tox = lax.rem(x + t, nx)

        def send_cot(t=t, tox=tox):
            return peer_copy(
                k_.own_cot.at[:, pl.ds(tox * RB, RB)], k_.cots.at[x], k_.o_send.at[0, t], k_.o_recv.at[0, t],
                place, 2 * tox + core,
            )

        launch(None, send_cot)

    gather_wait(xs, "skip")
    gate_n = E // 2

    def gate(i, carry):
        j = lax.div(i, 2)
        r0 = (i - 2 * j) * gate_n
        skips = [flat(xs, j, r0 + q) for q in range(gate_n)]
        v = jnp.concatenate(
            [
                jnp.concatenate([d1[j, r0 + q, 0 : dm.enc_all] for q in range(gate_n)], 1),
                jnp.concatenate(skips, 1),
            ],
            0,
        )
        pre = dot(wg, v) + gbias
        act = pre * jax.nn.sigmoid(pre)
        alpha = jax.nn.sigmoid(jnp.sum(gout * act, axis=0, keepdims=True))
        for q in range(gate_n):
            lanes = slice(q * LANES, (q + 1) * LANES)
            d1[j, r0 + q, dm.enc_all :] = (alpha[:, lanes] * skips[q].astype(F32)).astype(BF16)
            k_.pre[j, r0 + q] = pre[:, lanes]
            k_.alpha[j, r0 + q] = alpha[:, lanes]
        return carry

    lax.fori_loop(0, (S + 2) * 2, gate, 0)
    for k in (3, 2, 1, 0):
        weights_start(k)

    n = min(6, RB)

    def row_d1(j, r):
        return d1[j, r]

    def row_xd(j, r):
        return natural(xd, j, r)

    forward_wait(2)
    fine_sums(0, conv_stats(row_d1, lambda: forward_weight(2), k_.z3, n))
    drain()
    forward_wait(3)
    stats_d1 = moments(fine_totals(0), dm.fine_total)

    def keep_dec(p, v):
        d = lax.div(p, RB)
        xd[core, 1 + d, 1 + p - d * RB] = v.astype(BF16).astype(xd.dtype)

    norm_rows(k_.z3, stats_d1, norm_d1, keep_dec, RB)
    fine_start(xd, "hidden")
    for t in range(1, nx):
        fromx = lax.rem(x + nx - t, nx)
        theirs = k_.cots.at[fromx]
        peer_copy(theirs, theirs, k_.o_send.at[0, t], k_.o_recv.at[0, t], place, 2 * fromx + core).wait_recv()
    fine_pass(xd, "hidden", 0)
    weights_finish(3)
    fine_wait(xd, "hidden", 0)
    late = (lambda: fine_pass(xd, "hidden", 1), lambda: fine_wait(xd, "hidden", 1))
    fine_sums(1, conv_stats(row_xd, lambda: forward_weight(3), k_.z4, n, late))
    fine_passed(xd, "hidden")
    stats_d2 = moments(fine_totals(1), dm.fine_total)

    def row_cot(p):
        d = lax.div(p, RB)
        return jnp.concatenate([k_.cots[i, d, p - d * RB] for i in range(nx)], 0).astype(F32)

    fine_sums(2, norm_back_sums(k_.z4, keep_du(k_.du_f), stats_d2, norm_d2, row_cot, RB))

    def keep_result(p, v):
        for i in range(nx):
            k_.ob[i, p] = v[i * dm.cd : (i + 1) * dm.cd].astype(BF16).astype(k_.ob.dtype)

    norm_rows(k_.z4, stats_d2, norm_d2, keep_result, RB)
    for t in range(1, nx):
        tox = lax.rem(x + t, nx)

        def send_result(t=t, tox=tox):
            return peer_copy(
                k_.ob.at[tox], k_.oi.at[x], k_.o_send.at[1, t], k_.o_recv.at[1, t], place, 2 * tox + core
            )

        launch(None, send_result)
    total_d2 = fine_totals(2)
    norm_back_fine(k_.z4, back_factors(stats_d2, norm_d2, total_d2, dm.fine_total), xz4)
    fine_start(xz4, "dz4")
    weight_grad(row_xd, 3)
    fine_pass(xz4, "dz4", 0)
    cross_start(3)
    fine_wait(xz4, "dz4", 0)

    def row_xz4(j, r):
        return natural(xz4, j, r)

    def keep_grad(d, r0, results, carry):
        for j, v in enumerate(results):
            k_.gg[d * RB + r0 + j] = v
        return carry

    late = (lambda: fine_pass(xz4, "dz4", 1), lambda: fine_wait(xz4, "dz4", 1))
    conv(row_xz4, lambda: wb[3][...], n, dm.cf, 1, keep_grad, 0, late)
    fine_passed(xz4, "dz4")
    fine_sums(3, norm_back_sums(k_.z3, keep_du(k_.du_f), stats_d1, norm_d1, lambda p: k_.gg[p], RB))
    cross_finish(3)
    total_d1 = fine_totals(3)
    norm_back_fine(k_.z3, back_factors(stats_d1, norm_d1, total_d1, dm.fine_total), xz3)
    fine_start(xz3, "dz3")
    weights_finish(2)
    weight_grad(row_d1, 2)
    fine_pass(xz3, "dz3", 0)
    cross_start(2)
    fine_wait(xz3, "dz3", 0)

    def row_xz3(j, r):
        return natural(xz3, j, r)

    ups = nx * dm.ce

    def gate_back(d, r0, results, carry):
        bias, psi = carry
        lows = []
        for j, both in enumerate(results):
            p = d * RB + r0 + j
            v = both[ups:]
            grad = jnp.sum(v * flat(xs, d + 1, r0 + 1 + j).astype(F32), axis=0, keepdims=True)
            alpha = k_.alpha[d + 1, r0 + 1 + j]
            logit = grad * alpha * (1.0 - alpha)
            pre = k_.pre[d + 1, r0 + 1 + j]
            sigma = jax.nn.sigmoid(pre)
            psi = psi + pre * sigma * logit
            low = (logit * gout * sigma * (1.0 + pre * (1.0 - sigma))).astype(BF16)
            bias = bias + low.astype(F32)
            k_.pg[p] = low
            lows.append(low)
            k_.ug[d, 3 + r0 + j] = both[0:ups]
            for i in range(nc):
                k_.gv[i] = v[i * dm.cs : (i + 1) * dm.cs]
            for i in range(nx):
                k_.sgp[i, p] = alpha * k_.gv[2 * i + core]
        back = dot(k_.gate_own[...].astype(BF16), jnp.concatenate(lows, 1))
        for j in range(len(results)):
            p = d * RB + r0 + j
            lanes = slice(j * LANES, (j + 1) * LANES)
            k_.ug[d, 3 + r0 + j] += back[0:ups, lanes]
            for i in range(nx):
                v = k_.sgp[i, p] + back[ups + i * dm.cs : ups + (i + 1) * dm.cs, lanes]
                k_.sgp[i, p] = v
                k_.sgb[i, p] = v.astype(BF16).astype(k_.sgb.dtype)
        return bias, psi

    blank = jnp.zeros((dm.g, LANES), F32)
    late = (lambda: fine_pass(xz3, "dz3", 1), lambda: fine_wait(xz3, "dz3", 1))
    bias, psi = conv(row_xz3, lambda: wb[2][...], n, ups + dm.skip_all, 1, gate_back, (blank, blank), late)
    fine_passed(xz3, "dz3")

    ug, cb, cg = k_.ug, k_.cb, k_.cg
    for q in range(RB // 2 + 2):
        terms = []
        for d in range(S):
            v = 0.75 * (ug[d, 2 * q + 1] + ug[d, 2 * q + 2]) + 0.25 * (ug[d, 2 * q + 3] + ug[d, 2 * q])
            if q == 1:
                v += jnp.where(top, 0.25 * ug[d, 3], 0.0)
            if q == RB // 2:
                v += jnp.where(bottom, 0.25 * ug[d, RB + 2], 0.0)
            terms.append(split(v))
        v = dot(jnp.concatenate(terms, 0), down)
        for d in range(S):
            cb[d, h0 + q] = v[d * ups : (d + 1) * ups]

    def to_slabs(i, carry):
        even, odd = (cb[d, 2 * i + 1] + pltpu.roll(cb[d, 2 * i + 2], half, 1) for d in range(S))
        middle = 0.75 * (even + odd) + jnp.where(first, 0.25 * even, 0.0) + jnp.where(last, 0.25 * odd, 0.0)
        for part, v in enumerate((0.25 * even, middle, 0.25 * odd)):
            for j in range(nx):
                block = v[j * dm.ce : (j + 1) * dm.ce]
                k_.fs[part, j, i] = block.astype(BF16).astype(k_.fs.dtype)
                if part == 1:
                    k_.fm[j, i] = block
        return carry

    lax.fori_loop(0, Q, to_slabs, 0)

    def fold_parts():
        for step in (-1, 1, 0):
            sends = (no(first), None, no(last))[step + 1]
            gets = (no(last), None, no(first))[step + 1]
            for t in range(nx):
                if (step, t) != (0, 0):
                    tox, fromx = lax.rem(x + t, nx), lax.rem(x + nx - t, nx)
                    sems = (k_.f_send.at[step + 1, t], k_.f_recv.at[step + 1, t])
                    theirs = k_.fr.at[step + 1, fromx]
                    yield (
                        sends, gets, fromx, step + 1,
                        functools.partial(
                            peer_copy, k_.fs.at[step + 1, tox], k_.fr.at[step + 1, x], *sems, place + step, 2 * tox + core
                        ),
                        functools.partial(peer_copy, theirs, theirs, *sems, place, 2 * fromx + core),
                    )

    for sends, _, _, _, out, _ in fold_parts():
        launch(sends, out)
    for t in range(1, nx):
        tox = lax.rem(x + t, nx)

        def send_skip(t=t, tox=tox):
            return peer_copy(
                k_.sgb.at[tox], k_.sgi.at[x], k_.o_send.at[2, t], k_.o_recv.at[2, t], place, 2 * tox + core
            )

        launch(None, send_skip)

    acc[0, 0 : dm.g, 0:columns] = jnp.zeros((dm.g, columns), F32)

    def gate_weight(d, carry):
        v = jnp.concatenate(
            [
                jnp.concatenate([d1[1 + d, 1 + j, 0 : dm.enc_all] for j in range(RB)], 1),
                jnp.concatenate([flat(xs, 1 + d, 1 + j) for j in range(RB)], 1),
            ],
            0,
        )
        y = jnp.concatenate([k_.pg[d * RB + j] for j in range(RB)], 1)
        acc[0, 0 : dm.g, 0:columns] += dot_nt(y, v)
        return carry

    lax.fori_loop(0, S, gate_weight, 0)
    lane = iota((dm.g, LANES), 1)
    vectors = jnp.where(
        lane == 0,
        jnp.sum(bias, axis=1, keepdims=True),
        jnp.where(lane == 1, jnp.sum(psi, axis=1, keepdims=True), 0.0),
    )
    gate_block = k_.gate_block
    for j in range(nc):
        mine = slice(j * gq, (j + 1) * gq)
        gate_block[j, :, 0:columns] = acc[0, mine, 0:columns]
        gate_block[j, :, columns : 2 * LANES] = jnp.zeros((gq, 2 * LANES - columns), F32)
        gate_block[j, :, 2 * LANES :] = vectors[mine]
    sum_start(everyone, k_.sv, 4, 0, gate_block[me], lambda chan: gate_block.at[chan])
    cg[...] = k_.fm[x]
    for _, gets, fromx, part, _, back in fold_parts():

        def fold_in(back=back, part=part, fromx=fromx):
            back().wait_recv()
            cg[...] += k_.fr[part, fromx].astype(F32)

        guarded(gets, fold_in)

    coarse_sums(2, norm_back_sums(k_.z2, keep_du(k_.du_c), stats_e2, norm_e2, lambda p: cg[p], Q))
    cross_finish(2)
    weights_finish(1)
    total_e2 = coarse_totals(2)
    norm_back_coarse(k_.z2, back_factors(stats_e2, norm_e2, total_e2, dm.coarse_total), k_.xz2)
    gather_start(k_.xz2, "dz2")
    weight_grad_coarse(k_.xh, 1)
    reduce_finish(3)
    gather_pass(k_.xz2, "dz2")
    reduce_start(1)
    weights_finish(0)
    drain()
    gather_wait(k_.xz2, "dz2")
    for i, v in enumerate(conv_coarse(k_.xz2, wb[1], dm.ce)):
        cg[i] = v
    coarse_sums(3, norm_back_sums(k_.z1, keep_du(k_.du_c), stats_e1, norm_e1, lambda p: cg[p], Q))
    reduce_finish(2)
    total_e1 = coarse_totals(3)
    norm_back_coarse(k_.z1, back_factors(stats_e1, norm_e1, total_e1, dm.coarse_total), k_.xz1)
    gather_start(k_.xz1, "dz1")
    weight_grad_coarse(xp, 0)
    reduce_start(0)
    reduce_finish(1)
    gather_pass(k_.xz1, "dz1")
    gradient_out(3)

    def rows_out(ref, own, theirs, kind, size):
        def copy_rows(read, at):
            def body(d, carry):
                for r in range(RB):
                    p = (d * R + at * RB + r) * size
                    ref[pl.ds(pl.multiple_of(p, size), size)] = read(d * RB + r).astype(F32)
                return carry

            lax.fori_loop(0, S, body, 0)

        copy_rows(lambda p: own[x, p], x)
        for t in range(1, nx):
            fromx = lax.rem(x + nx - t, nx)
            block = theirs.at[fromx]
            peer_copy(block, block, k_.o_send.at[kind, t], k_.o_recv.at[kind, t], place, 2 * fromx + core).wait_recv()
            copy_rows(lambda p, fromx=fromx: theirs[fromx, p], fromx)

    rows_out(k_.out, k_.ob, k_.oi, 1, dm.cd)
    rows_out(k_.sg, k_.sgp, k_.sgi, 2, dm.cs)
    gather_wait(k_.xz1, "dz1")
    for i, v in enumerate(conv_coarse(k_.xz1, wb[0], dm.cs)):
        v = dot(split(v), spread2) * 0.125
        for j in range(4):
            part = v[:, (j // 2) * LANES : (j // 2 + 1) * LANES]
            for d in range(S):
                at = (d * R + 4 * i + j) * dm.cs
                k_.sg[at : at + dm.cs] += part
    reduce_finish(0)
    gradient_out(2)
    gradient_out(1)
    gate_total = sum_finish(everyone, k_.sv, 4, 0)
    k_.ggate[...] = gate_total[:, 0:columns]
    k_.gvector[0:1] = row_of(gate_total[:, 2 * LANES : 2 * LANES + 1])
    k_.gvector[1:2] = row_of(gate_total[:, 2 * LANES + 1 : 2 * LANES + 2])

    def own_part(col):
        parts = [jnp.where(x == i, col[i * dm.cd : (i + 1) * dm.cd], 0.0) for i in range(nx)]
        return functools.reduce(jnp.add, parts)

    for ref, pair, pick in ((k_.gen, (total_e1, total_e2), lambda v: v), (k_.gdn, (total_d1, total_d2), own_part)):
        for layer, total in enumerate(pair):
            ref[0, layer : layer + 1] = row_of(pick(total[1]))
            ref[1, layer : layer + 1] = row_of(pick(total[0]))
    gradient_out(0)
    drain()


def adamw(weight, grad, moment, square, rate):
    new_moment = 0.9 * moment + 0.1 * grad
    new_square = 0.999 * square + 0.001 * grad * grad
    moment_hat = new_moment / (1.0 - 0.9**STEP)
    square_hat = new_square / (1.0 - 0.999**STEP)
    new_weight = weight - rate * (moment_hat / (jnp.sqrt(square_hat) + 1e-08) + 0.01 * weight)
    return (new_weight, new_moment, new_square)


RATES = (CONV_RATE, CONV_RATE, GATE_RATE, VECTOR_RATE, CONV_RATE, CONV_RATE, VECTOR_RATE, VECTOR_RATE)


def update_kernel(*refs):
    n = len(RATES)
    sources, targets = refs[: 2 + 4 * n], refs[2 + 4 * n : 4 + 7 * n]
    inside, outside = refs[4 + 7 * n : 6 + 11 * n], refs[6 + 11 * n : 8 + 14 * n]
    in_sem, out_sem = refs[8 + 14 * n :]
    order = (4, 1, 0, 5, 2, 3, 6, 7)

    def load(i):
        return pltpu.make_async_copy(sources[i], inside[i], in_sem.at[i])

    def store(i):
        return pltpu.make_async_copy(outside[i], targets[i], out_sem.at[i])

    for i in (1, 0):
        load(i).start()
    for k in order:
        for part in range(4):
            load(2 + part * n + k).start()
    for i in (1, 0):
        load(i).wait()
        chans, (slabs, rows) = outside[i].shape[0], outside[i].shape[1:3]
        for c in range(chans):
            v = inside[i][pl.ds(c, slabs * rows, stride=chans)]
            outside[i][c] = v.reshape(slabs, rows, LANES).astype(outside[i].dtype)
        store(i).start()
    for k in order:
        own = [2 + part * n + k for part in range(4)]
        for i in own:
            load(i).wait()
        rows = inside[own[0]].shape[0]
        step = 8 if rows % 8 == 0 and rows > 8 else rows
        for r in range(0, rows, step):
            at = slice(r, r + step)
            new = adamw(*(inside[i][at] for i in own), RATES[k])
            for part, value in enumerate(new):
                outside[2 + 3 * k + part][at] = value
        for part in range(3):
            store(2 + 3 * k + part).start()
    for i in range(len(targets)):
        store(i).wait()


def per_device(
    skip, cotangent, enc_conv1, enc_conv2, gate_proj, gate_vector, dec_conv1, dec_conv2, enc_norms, dec_norms, *states
):
    nd, nc = lax.axis_size("depth"), lax.axis_size("chan")
    dm = Dims(nd, nc, skip.shape, enc_conv1.shape[0], dec_conv1.shape[0], gate_proj.shape[0] * nc)
    S, R, H, nx, RB, E = dm.s, dm.rows, dm.half, dm.nx, dm.rb, dm.ext
    Q = H // 2
    cin3 = dm.enc_all + dm.skip_all

    def own_block(size):
        return (size, lambda j: pl.multiple_of(j * size, size), 0)

    def core_blocks(size):
        return tuple(
            (size, lambda j, i=i: pl.multiple_of((2 * i + lax.rem(j, 2)) * size, size), i * size) for i in range(nx)
        )

    dm.convs = convs = (
        Conv(dm, dm.ce, dm.skip_all, (own_block(dm.cs),)),
        Conv(dm, dm.ce, dm.enc_all, (own_block(dm.ce),)),
        Conv(dm, dm.cd, cin3, core_blocks(dm.ce) + ((dm.skip_all, lambda j: dm.enc_all, nx * dm.ce),)),
        Conv(dm, dm.cd, dm.dec_all, core_blocks(dm.cd)),
    )
    params = (enc_conv1, enc_conv2, gate_proj, gate_vector, dec_conv1, dec_conv2, enc_norms, dec_norms)
    inputs = dict(
        skip=skip, cot=cotangent, w0=enc_conv1, w1=enc_conv2, w2=dec_conv1, w3=dec_conv2,
        gate=gate_proj, vector=gate_vector, en=enc_norms, dn=dec_norms,
    )
    shape = jax.ShapeDtypeStruct
    outs = dict(
        out=shape((S * R * dm.cd, LANES), F32),
        sg=shape((S * R * dm.cs, LANES), F32),
        **{f"g{i}": shape(a.shape, F32) for i, a in enumerate((enc_conv1, enc_conv2, dec_conv1, dec_conv2))},
        **{
            name: shape(a.shape, F32)
            for name, a in (("ggate", gate_proj), ("gvector", gate_vector), ("gen", enc_norms), ("gdn", dec_norms))
        },
    )
    gq = dm.g // nc

    def coarse(block):
        return pltpu.VMEM((2, nx, 3, Q, block, LANES), storage(block))

    def fine():
        return pltpu.VMEM((2, S + 2, E, dm.cf, LANES), storage(dm.cd))

    def f32(*dims):
        return pltpu.VMEM((*dims, LANES), F32)

    def tiles(*dims):
        return pltpu.VMEM((*dims, 16, LANES), BF16)

    def blocks(block, *dims):
        return pltpu.VMEM((*dims, block, LANES), storage(block))

    def sems(*dims):
        return pltpu.SemaphoreType.DMA(dims)

    scratch = dict(
        xp=coarse(dm.cs), xh=coarse(dm.ce), xc=coarse(dm.ce), xz2=coarse(dm.ce), xz1=coarse(dm.ce),
        own_skip=blocks(dm.cs, S, R + 2), xs=blocks(dm.cs, 2, nx, S + 2, E),
        own_cot=blocks(dm.cd, S, R), cots=blocks(dm.cd, nx, S, RB),
        d1=pltpu.VMEM((S + 2, E, cin3, LANES), BF16), xd=fine(), xz4=fine(), xz3=fine(),
        z1=f32(Q, dm.ce), z2=f32(Q, dm.ce), z3=f32(S * RB, dm.cf), z4=f32(S * RB, dm.cf),
        du_c=f32(Q, dm.ce), du_f=f32(S * RB, dm.cf), gg=f32(S * RB, dm.cf), cg=f32(Q, dm.ce),
        pre=f32(S + 2, E, dm.g), alpha=f32(S + 2, E, 1), pg=pltpu.VMEM((S * RB, dm.g, LANES), BF16),
        ug=f32(S, RB + 6, nx * dm.ce), cb=f32(S, H + 2, nx * dm.ce), dt=f32(S + 2, H, dm.enc_all),
        gv=f32(nc, dm.cs), sgp=f32(nx, S * RB, dm.cs), sgb=blocks(dm.cs, nx, S * RB), sgi=blocks(dm.cs, nx, S * RB),
        ob=blocks(dm.cd, nx, S * RB), oi=blocks(dm.cd, nx, S * RB),
        dzf=pltpu.VMEM((3, S, RB + 4, dm.cf, LANES), storage(dm.cd)),
        dzc=pltpu.VMEM((9, Q, dm.ce, LANES), BF16),
        fs=blocks(dm.ce, 3, nx, Q), fr=blocks(dm.ce, 3, nx, Q), fm=f32(nx, Q, dm.ce),
        st=f32(4, nd, 1), su=f32(4, nd * nx, 1), sv=pltpu.VMEM((1, nd * nx, gq, 3 * LANES), F32),
        norm_all=f32(nc, 8), rows=f32(max(dm.cs, dm.cd) * S * R),
        turned=f32(max(cv.chunks for cv in convs) * LANES),
        acc=pltpu.VMEM((nx, max(3 * cv.c for cv in convs), max(cv.wide for cv in convs)), F32),
        gate_all=pltpu.VMEM((nc, gq, 3 * LANES), F32), gate_t=pltpu.VMEM((2 * LANES, dm.g), F32),
        gate_own=pltpu.VMEM((nx * (dm.ce + dm.cs), dm.g), F32), gate_block=pltpu.VMEM((nc, gq, 3 * LANES), F32),
        **{f"wt{i}": pltpu.VMEM((3, cv.c, cv.wide), cv.kind) for i, cv in enumerate(convs)},
        **{
            f"wf{i}": pltpu.VMEM((cv.taps, 3 * cv.c) if i < 2 else (nx, cv.stored, 3 * cv.c), BF16)
            for i, cv in enumerate(convs)
        },
        **{f"wx{i}": pltpu.VMEM((nc, 3, cv.needed, cv.wide), cv.kind) for i, cv in enumerate(convs)},
        **{f"wb{i}": pltpu.VMEM((9 * cv.needed, 3 * nc * cv.o), BF16) for i, cv in enumerate(convs)},
        **{f"gt{i}": tiles(cv.share * nd) for i, cv in enumerate(convs)},
        **{f"gr{i}": tiles(nd, cv.share) for i, cv in enumerate(convs)},
        **{f"ga{i}": tiles(cv.share * nd) for i, cv in enumerate(convs)},
        **{f"gs{i}": tiles(nx, convs[i].count) for i in (2, 3)},
        **{f"gx{i}": tiles(nx, convs[i].count) for i in (2, 3)},
        g_send=sems(len(GATHERS), 3, nx), g_recv=sems(len(GATHERS), 3),
        h_send=sems(len(GATHERS)), h_recv=sems(len(GATHERS)),
        x_send=sems(len(FINE), 3, 3), x_recv=sems(len(FINE), 3, 3), y_send=sems(len(FINE), 2), y_recv=sems(len(FINE), 2),
        t_send=sems(4), t_recv=sems(4), u_send=sems(5), u_recv=sems(5),
        f_send=sems(3, nx), f_recv=sems(3, nx), w_send=sems(4, nx + 1, nc), w_recv=sems(4, nx + 1, nc),
        p_send=sems(2, nx), p_recv=sems(2, nx), c_send=sems(2, nx), c_recv=sems(2, nx),
        o_send=sems(3, nx), o_recv=sems(3, nx), v_send=sems(2, nc), v_recv=sems(2, nc),
        r_send=sems(4), r_recv=sems(4), a_send=sems(4), a_recv=sems(4),
    )
    vmem = pl.BlockSpec(memory_space=pltpu.VMEM)
    out, sg, grad1, grad2, grad3, grad4, ggate, gvector, gen, gdn = pl.pallas_call(
        functools.partial(kernel, dm, (*inputs, *outs, *scratch)),
        out_shape=tuple(outs.values()),
        in_specs=[vmem] * len(inputs),
        out_specs=[vmem] * len(outs),
        scratch_shapes=list(scratch.values()),
        compiler_params=pltpu.CompilerParams(
            has_side_effects=True, collective_id=0, vmem_limit_bytes=60 * 1024 * 1024
        ),
        name="step",
    )(*inputs.values())
    grads = (grad1, grad2, ggate, gvector, grad3, grad4, gen, gdn)
    operands = (out, sg, *params, *grads, *states)
    updated = (
        shape(cotangent.shape, BF16),
        shape(skip.shape, F32),
        *(shape(p.shape, F32) for p in params for _ in range(3)),
    )
    anywhere = pl.BlockSpec(memory_space=pl.ANY)
    return pl.pallas_call(
        update_kernel,
        out_shape=updated,
        in_specs=[anywhere] * len(operands),
        out_specs=[anywhere] * len(updated),
        scratch_shapes=[
            *(pltpu.VMEM(a.shape, a.dtype) for a in operands),
            *(pltpu.VMEM(a.shape, a.dtype) for a in updated),
            pltpu.SemaphoreType.DMA((len(operands),)),
            pltpu.SemaphoreType.DMA((len(updated),)),
        ],
        compiler_params=pltpu.CompilerParams(vmem_limit_bytes=60 * 1024 * 1024),
        name="update",
    )(*operands)


def solution(mesh):
    volume = P("chan", "depth", None, None)
    row, column, norms = P("chan", None), P(None, "chan"), P(None, None, "chan")
    params = (row, row, row, column, row, row, norms, norms)
    return jax.shard_map(
        per_device,
        mesh=mesh,
        in_specs=(volume, volume) + params * 3,
        out_specs=(volume, volume) + tuple(spec for spec in params for _ in range(3)),
        check_vma=False,
    )
```

```python
import functools
import types

import jax
import jax.numpy as jnp
from jax import lax
from jax.experimental import pallas as pl
from jax.experimental.pallas import tpu as pltpu
from jax.sharding import PartitionSpec as P

STEP = 5
EPS = 1e-05
CONV_RATE = 0.03
GATE_RATE = 0.1
VECTOR_RATE = 0.5
LANES = 128
MESH = pl.DeviceIdType.MESH
F32 = jnp.float32
BF16 = jnp.bfloat16


def iota(shape, dim):
    return lax.broadcasted_iota(jnp.int32, shape, dim)


def dot(a, b):
    return jnp.dot(a, b, preferred_element_type=F32)


def dot_nt(a, b):
    return lax.dot_general(a, b, (((1,), (1,)), ((), ())), preferred_element_type=F32)


def from_left(v, width):
    return jnp.where(iota(v.shape, 1) % width == 0, 0.0, pltpu.roll(v, 1, 1))


def from_right(v, width):
    return jnp.where(iota(v.shape, 1) % width == width - 1, 0.0, pltpu.roll(v, LANES - 1, 1))


def halves(low, high):
    return pltpu.roll(jnp.where(iota(low.shape, 1) < LANES // 2, low, high), LANES // 2, 1)


def split(v):
    high = v.astype(BF16)
    return jnp.concatenate([high, (v - high.astype(F32)).astype(BF16)], 1)


def storage(block):
    return BF16 if block % 16 == 0 else F32


def flat(ref, s, r):
    if len(ref.shape) == 4:
        return ref[s, r]
    v = ref[:, :, s, r]
    return jnp.concatenate([v[c, i] for i in range(v.shape[1]) for c in range(2)], 0).astype(BF16)


class Dims:
    def __init__(self, nd, nc, skip, enc, dec, gate):
        self.nd, self.nc, self.nx = nd, nc, nc // 2
        self.s, self.rows, self.cols = skip[1:]
        self.cs, self.ce, self.cd, self.g = skip[0], enc, dec, gate
        self.half, self.hcols = self.rows // 2, self.cols // 2
        self.fine_total = nd * self.s * self.rows * self.cols
        self.coarse_total = self.fine_total // 8
        self.enc_all = nc * enc
        self.skip_all = nc * skip[0]
        self.dec_all = nc * dec
        self.rb = self.rows // self.nx
        self.ext = self.rb + 2
        self.cf = self.nx * dec


GATHERS = ("pooled", "skip", "hidden", "coarse", "dz2", "dz1")
FINE = ("hidden", "dz4", "dz3")


class Conv:
    def __init__(self, dm, o, c, blocks):
        self.o, self.c, self.blocks = o, c, blocks
        self.length = 27 * c
        self.chunks = -(-self.length // LANES)
        self.per = LANES // o
        self.tiles = -(-9 // self.per)
        self.wide = self.tiles * LANES
        self.kind = storage(min(size for size, _, _ in blocks))
        self.needed = sum(size for size, _, _ in blocks)
        self.count = 3 * c // 16 * self.tiles
        self.share = -(-self.count // dm.nd)
        self.taps = 9 * o
        self.stored = -(-3 * o // 16) * 16


def kernel(dm, names, *refs):
    k_ = types.SimpleNamespace(**dict(zip(names, refs)))
    nd, nc, nx, S, R, H = dm.nd, dm.nc, dm.nx, dm.s, dm.rows, dm.half
    W, V = dm.cols, dm.hcols
    Q, RB, E = H // 2, dm.rb, dm.ext
    place = lax.axis_index("depth")
    me = lax.axis_index("chan")
    x, core = lax.div(me, 2), lax.rem(me, 2)
    other = 1 - core
    mate = 2 * x + other
    row0, h0 = x * RB, x * (RB // 2)
    first, last = place == 0, place == nd - 1
    top, bottom = x == 0, x == nx - 1
    convs = dm.convs
    pending = []
    wt, wf, wx, wb = ([getattr(k_, f"{kind}{i}") for i in range(4)] for kind in ("wt", "wf", "wx", "wb"))
    gt, gr, ga = ([getattr(k_, f"{kind}{i}") for i in range(4)] for kind in ("gt", "gr", "ga"))
    weights = (k_.w0, k_.w1, k_.w2, k_.w3)
    grads = (k_.g0, k_.g1, k_.g2, k_.g3)
    turned, acc = k_.turned, k_.acc

    def no(cond):
        return jnp.logical_not(cond)

    def peer_copy(src, dst, send, recv, depth, chan):
        return pltpu.make_async_remote_copy(
            src_ref=src, dst_ref=dst, send_sem=send, recv_sem=recv,
            device_id={"depth": depth, "chan": chan}, device_id_type=MESH,
        )

    def guarded(cond, fn):
        if cond is None:
            fn()
        else:
            pl.when(cond)(fn)

    def drain():
        for cond, fn in pending:
            guarded(cond, fn)
        pending.clear()

    def launch(cond, copy):
        guarded(cond, lambda: copy().start())
        pending.append((cond, lambda: copy().wait_send()))

    def arrive(cond, copy):
        guarded(cond, lambda: copy().wait_recv())

    def both(a, b):
        return b if a is None else a if b is None else jnp.logical_and(a, b)

    can_send = (no(last), None, no(first))
    can_recv = (no(first), None, no(last))

    def slices(side, n):
        return (pl.ds(n, 1), pl.ds(1, n), pl.ds(1, 1))[side], (pl.ds(0, 1), pl.ds(1, n), pl.ds(n + 1, 1))[side]

    def at_x(t):
        up, down = x + t, x - t
        return jnp.where(up >= nx, up - nx, up), jnp.where(down < 0, down + nx, down)


    def gather_start(ref, which, source_at=None):
        n = ref.shape[2] - 2
        k = GATHERS.index(which)
        for side in (0, 2, 1):
            own, theirs = slices(side, n)
            for t in range(nx):
                if side == 1 and t == 0:
                    continue
                tox = at_x(t)[0]

                def copy(side=side, t=t, own=own, theirs=theirs, tox=tox):
                    start = (n, 1, 1)[side] - 1
                    size = (1, n, 1)[side]
                    src = ref.at[core, x, own] if source_at is None else source_at(pl.ds(start, size), tox)
                    return peer_copy(
                        src, ref.at[core, x, theirs], k_.g_send.at[k, side, t], k_.g_recv.at[k, side],
                        place + 1 - side, 2 * tox + core,
                    )

                launch(can_send[side], copy)

    def handed(ref, k, c):
        return peer_copy(ref.at[c], ref.at[c], k_.h_send.at[k], k_.h_recv.at[k], place, mate)

    def gather_pass(ref, which):
        n = ref.shape[2] - 2
        k = GATHERS.index(which)
        for side in (1, 0, 2):
            theirs = slices(side, n)[1]
            if side != 1:
                got = ref.at[core, :, theirs]
            elif nx == 2:
                got = ref.at[core, 1 - x, theirs]
            else:
                got = ref.at[core, pl.ds(0, nx - 1), theirs]
            arrive(
                can_recv[side],
                lambda got=got, side=side: peer_copy(got, got, k_.g_send.at[k, side, 0], k_.g_recv.at[k, side], place, mate),
            )
        launch(None, lambda: handed(ref, k, core))

    def gather_wait(ref, which):
        handed(ref, GATHERS.index(which), other).wait_recv()

    def fine_parts(ref, which, side):
        k = FINE.index(which)
        own, theirs = slices(side, S)
        rows = [(None, None, pl.ds(1, RB), pl.ds(1, RB), x)] if side != 1 else []
        if nx > 1:
            rows.append((no(top), no(bottom), pl.ds(1, 1), pl.ds(E - 1, 1), x - 1))
            rows.append((no(bottom), no(top), pl.ds(RB, 1), pl.ds(0, 1), x + 1))
        parts = []
        for i, (sends, gets, row, at, tox) in enumerate(rows):
            sems = (k_.x_send.at[k, side, i], k_.x_recv.at[k, side, i])
            target = ref.at[core, theirs, at]
            parts.append((
                both(can_send[side], sends), both(can_recv[side], gets),
                functools.partial(
                    peer_copy, ref.at[core, own, row], target, *sems, place + 1 - side, 2 * tox + core
                ),
                functools.partial(peer_copy, target, target, *sems, place, mate),
            ))
        return parts

    def fine_start(ref, which):
        for side in (0, 2, 1):
            for sends, _, out, _ in fine_parts(ref, which, side):
                launch(sends, out)

    def fine_handed(ref, which, c):
        k = FINE.index(which)
        return peer_copy(ref.at[c], ref.at[c], k_.y_send.at[k], k_.y_recv.at[k], place, mate)

    def fine_pass(ref, which):
        for side in (1, 0, 2):
            for _, gets, _, back in fine_parts(ref, which, side):
                arrive(gets, back)
        launch(None, lambda: fine_handed(ref, which, core))

    def fine_wait(ref, which):
        fine_handed(ref, which, other).wait_recv()

    def natural(ref, s, r):
        v = ref[:, s, r]
        size = dm.cd
        return jnp.concatenate(
            [v[c, i * size : (i + 1) * size] for i in range(nx) for c in range(2)], 0
        ).astype(BF16)

    def in_turn(count, fn):
        if count <= 16:
            for i in range(count):
                fn(i)
        else:

            def body(i, carry):
                fn(i)
                return carry

            lax.fori_loop(0, count, body, 0)

    def slab_peers(i):
        to = place + 1 + i
        return jnp.where(to >= nd, to - nd, to), me

    def wide_peers(i):
        i = i + 1
        dt, xt = (i // nx, i % nx) if isinstance(i, int) else (lax.div(i, nx), lax.rem(i, nx))
        to, tox = place + dt, x + xt
        return jnp.where(to >= nd, to - nd, to), 2 * jnp.where(tox >= nx, tox - nx, tox) + core

    def exchange(n, peers, copy):
        in_turn(n - 1, lambda i: copy(*peers(i)).start())

    def sum_start(group, ref, k, slot, tile, source=None):
        n, own, peers, send, recv = group
        ref[slot, own] = tile

        def copy(depth, chan):
            src = ref.at[slot, own] if source is None else source(chan)
            return peer_copy(src, ref.at[slot, own], send.at[k], recv.at[k], depth, chan)

        exchange(n, peers, copy)
        pending.append((None, lambda: all_of(group, ref, k, slot).wait_send()))

    def all_of(group, ref, k, slot):
        n, _, _, send, recv = group
        every = ref.at[slot, pl.ds(0, n - 1)]
        return peer_copy(every, every, send.at[k], recv.at[k], place, mate)

    def sum_finish(group, ref, k, slot):
        all_of(group, ref, k, slot).wait_recv()
        return jnp.sum(ref[slot], axis=0)

    slabs = (nd, place, slab_peers, k_.t_send, k_.t_recv)
    everyone = (nd * nx, place * nx + x, wide_peers, k_.u_send, k_.u_recv)

    def columns_of(row, m):
        lane, channel = iota((m, LANES), 1), iota((m, LANES), 0)
        return tuple(
            jnp.sum(jnp.where(lane == channel + i * m, row, 0.0), axis=1, keepdims=True) for i in range(2)
        )

    def coarse_sums(slot, sums):
        sum_start(slabs, k_.st, slot, slot, pack(*sums))

    def coarse_totals(slot):
        return columns_of(sum_finish(slabs, k_.st, slot, slot), dm.ce)

    def fine_sums(slot, sums):
        sum_start(everyone, k_.su, slot, slot, pack(*sums))

    def fine_totals(slot):
        return columns_of(sum_finish(everyone, k_.su, slot, slot), dm.cf)

    def turn_in(w, cv):
        eye = (iota((LANES, LANES), 0) == iota((LANES, LANES), 1)).astype(BF16)

        def chunk(a):
            return dot_nt(eye, jnp.concatenate([a] * cv.per, 0).astype(BF16))

        full = cv.length // LANES

        def body(i, carry):
            at = pl.multiple_of(i * LANES, LANES)
            turned[pl.ds(at, LANES)] = chunk(w[:, pl.ds(at, LANES)])
            return carry

        lax.fori_loop(0, full, body, 0, unroll=4)
        if full < cv.chunks:
            a = w[:, full * LANES :]
            a = jnp.concatenate([a, jnp.zeros((cv.o, LANES - a.shape[1]), F32)], 1)
            turned[full * LANES : (full + 1) * LANES] = chunk(a)

    def prepare(k):
        cv, w, own = convs[k], weights[k], wt[k]
        out = wf[k] if k < 2 else wf[k].at[x]
        turn_in(w, cv)
        group = iota((cv.c, LANES), 1) // cv.o
        for kz in range(3):
            for j in range(cv.tiles):
                tile = None
                for g in range(cv.per):
                    t = j * cv.per + g
                    if t < 9:
                        v = turned[pl.ds(9 * kz + t, cv.c, stride=27)]
                        tile = v if tile is None else jnp.where(group == g, v, tile)
                own[kz, :, j * LANES : (j + 1) * LANES] = tile.astype(BF16).astype(own.dtype)
        eye = (iota((LANES, LANES), 0) == iota((LANES, LANES), 1)).astype(BF16)
        for j in range(cv.tiles):
            v = jnp.concatenate([own[kz, :, j * LANES : (j + 1) * LANES] for kz in range(3)], 0)
            size = min(LANES, cv.taps - j * LANES)
            v = dot_nt(eye, v.astype(BF16))[0:size]
            if k < 2:
                out[j * LANES : j * LANES + size] = v.astype(BF16)
            else:
                k_.flip[j * LANES : j * LANES + size, 0 : 3 * cv.c] = v
        if k >= 2:
            rows = 3 * cv.o
            out[0:rows] = jnp.concatenate(
                [
                    k_.flip[ky * rows : (ky + 1) * rows, kz * cv.c : (kz + 1) * cv.c]
                    for kz in range(3)
                    for ky in range(3)
                ],
                1,
            ).astype(BF16)

    def forward_copy(k, t):
        block = wf[k].at[x]
        return peer_copy(
            block, block, k_.p_send.at[k - 2, t], k_.p_recv.at[k - 2, t], place, 2 * lax.rem(x + t, nx) + core
        )

    def forward_start(k):
        for t in range(1, nx):
            launch(None, functools.partial(forward_copy, k, t))

    def forward_wait(k):
        for t in range(1, nx):
            fromx = lax.rem(x + nx - t, nx)
            block = wf[k].at[fromx]
            peer_copy(
                block, block, k_.p_send.at[k - 2, t], k_.p_recv.at[k - 2, t], place, 2 * fromx + core
            ).wait_recv()

    def forward_weight(k):
        return jnp.concatenate([wf[k][i, 0 : 3 * convs[k].o] for i in range(nx)], 0)

    def weights_start(k):
        cv = convs[k]
        for b, (size, start, at) in enumerate(cv.blocks):
            wx[k][me, :, at : at + size] = wt[k][:, pl.ds(start(me), size)]
            for t in range(1, nc):
                to = lax.rem(me + t, nc)

                def copy(to=to, t=t, b=b, size=size, start=start, at=at):
                    return peer_copy(
                        wt[k].at[:, pl.ds(start(to), size)], wx[k].at[me, :, pl.ds(at, size)],
                        k_.w_send.at[k, b, t], k_.w_recv.at[k, b, t], place, to,
                    )

                launch(None, copy)

    def weights_finish(k):
        cv = convs[k]
        for b, (size, _, at) in enumerate(cv.blocks):
            for t in range(1, nc):
                source = lax.rem(me + nc - t, nc)
                theirs = wx[k].at[source, :, pl.ds(at, size)]
                peer_copy(theirs, theirs, k_.w_send.at[k, b, t], k_.w_recv.at[k, b, t], place, source).wait_recv()

        def pieces(kz, t):
            return [wx[k][j, 2 - kz, :, t * cv.o : (t + 1) * cv.o].astype(F32) for j in range(nc)]

        for i in range(9 if k < 2 else 3):
            if k < 2:
                found = [v for kz in range(3) for v in pieces(kz, 8 - i)]
            else:
                found = [v for kz in range(3) for ky in range(3) for v in pieces(kz, 3 * (2 - ky) + 2 - i)]
            wb[k][i * cv.needed : (i + 1) * cv.needed] = jnp.concatenate(found, 1).astype(BF16)

    def tiles_of(k, part, put):
        cv = convs[k]

        def tile(i, carry):
            at = pl.multiple_of(i * 16, 16)
            for j in range(cv.tiles):
                put(i * cv.tiles + j, acc[part, pl.ds(at, 16), j * LANES : (j + 1) * LANES].astype(BF16))
            return carry

        lax.fori_loop(0, 3 * cv.c // 16, tile, 0, unroll=4)

    def cross_start(k):
        gs, gx = (k_.gs2, k_.gs3)[k - 2], (k_.gx2, k_.gx3)[k - 2]
        for part in range(nx):

            def put(i, v, part=part):
                gs[part, i] = v

            tiles_of(k, part, put)
        for t in range(1, nx):
            tox = lax.rem(x + t, nx)

            def copy(t=t, tox=tox):
                return peer_copy(
                    gs.at[tox], gx.at[x], k_.c_send.at[k - 2, t], k_.c_recv.at[k - 2, t], place, 2 * tox + core
                )

            launch(None, copy)

    def cross_finish(k):
        cv, gs, gx = convs[k], (k_.gs2, k_.gs3)[k - 2], (k_.gx2, k_.gx3)[k - 2]
        sources = [lax.rem(x + nx - t, nx) for t in range(1, nx)]
        for t, fromx in enumerate(sources, 1):
            theirs = gx.at[fromx]
            peer_copy(
                theirs, theirs, k_.c_send.at[k - 2, t], k_.c_recv.at[k - 2, t], place, 2 * fromx + core
            ).wait_recv()

        def add(i, carry):
            for j in range(cv.tiles):
                p = i * cv.tiles + j
                v = gs[x, p].astype(F32)
                for fromx in sources:
                    v += gx[fromx, p].astype(F32)
                gt[k][p] = v.astype(BF16)
            return carry

        lax.fori_loop(0, 3 * cv.c // 16, add, 0, unroll=4)
        reduce_send(k)

    def reduce_start(k):
        def put(i, v):
            gt[k][i] = v

        tiles_of(k, 0, put)
        reduce_send(k)

    def reduce_send(k):
        cv = convs[k]
        for i in range(cv.count, cv.share * nd):
            gt[k][i] = jnp.zeros((16, LANES), BF16)
        gr[k][place] = gt[k][pl.ds(place * cv.share, cv.share)]

        def copy(to, chan):
            return peer_copy(
                gt[k].at[pl.ds(to * cv.share, cv.share)], gr[k].at[place], k_.r_send.at[k], k_.r_recv.at[k], to, chan
            )

        exchange(nd, slab_peers, copy)
        pending.append((None, lambda: reduce_all(k).wait_send()))

    def reduce_all(k):
        every = gr[k].at[pl.ds(0, nd - 1)]
        return peer_copy(every, every, k_.r_send.at[k], k_.r_recv.at[k], place, mate)

    def share_all(k):
        every = ga[k].at[pl.ds(0, (nd - 1) * convs[k].share)]
        return peer_copy(every, every, k_.a_send.at[k], k_.a_recv.at[k], place, mate)

    def reduce_finish(k):
        cv = convs[k]
        reduce_all(k).wait_recv()
        own = pl.ds(place * cv.share, cv.share)
        ga[k][own] = jnp.sum(gr[k][...].astype(F32), axis=0).astype(BF16)

        def copy(to, chan):
            return peer_copy(ga[k].at[own], ga[k].at[own], k_.a_send.at[k], k_.a_recv.at[k], to, chan)

        exchange(nd, slab_peers, copy)
        pending.append((None, lambda: share_all(k).wait_send()))

    def gradient_out(k):
        cv, out = convs[k], grads[k]
        share_all(k).wait_recv()
        group = iota((16, LANES), 1) // cv.o

        def scatter(i, carry):
            for kz in range(3):
                for j in range(cv.tiles):
                    v = ga[k][(kz * (cv.c // 16) + i) * cv.tiles + j].astype(F32)
                    for g in range(cv.per):
                        t = j * cv.per + g
                        if t < 9:
                            turned[pl.ds(9 * kz + t + i * (16 * 27), 16, stride=27)] = jnp.where(group == g, v, 0.0)
            return carry

        lax.fori_loop(0, cv.c // 16, scatter, 0, unroll=2)

        pick = (iota((cv.o, LANES), 1) % cv.o == iota((cv.o, LANES), 0)).astype(BF16)
        step = 8 * LANES
        for at in range(0, cv.length, step):
            size = min(step, cv.length - at)
            v = dot_nt(pick, turned[at : at + -(-size // LANES) * LANES].astype(BF16))
            out[:, at : at + size] = v[:, 0:size]

    def column(row):
        n = row.shape[1]
        eye = iota((n, n), 0) == iota((n, n), 1)
        return jnp.sum(jnp.where(eye, row, 0.0), axis=1, keepdims=True)

    def row_of(col):
        n = col.shape[0]
        eye = iota((n, n), 0) == iota((n, n), 1)
        return jnp.sum(jnp.where(eye, col, 0.0), axis=0, keepdims=True)

    def clear_halos(ref):
        def clear(at):
            if len(ref.shape) == 5:
                ref[core, at] = jnp.zeros(ref.shape[2:], ref.dtype)
            else:
                for i in range(nx):
                    ref[core, i, at] = jnp.zeros(ref.shape[3:], ref.dtype)

        pl.when(first)(lambda: clear(0))
        pl.when(last)(lambda: clear(ref.shape[-4] - 1))

    def clear_rows(ref):
        def clear(at):
            for i in range(S + 2):
                ref[core, i, at] = jnp.zeros(ref.shape[3:], ref.dtype)

        pl.when(top)(lambda: clear(0))
        pl.when(bottom)(lambda: clear(E - 1))

    def conv(row, weight, m, groups, emit, init):
        def body(d, carry):
            v = jnp.concatenate(
                [
                    jnp.concatenate([row(d + kz, ky + j) for j in range(RB)], 1)
                    for kz in range(3)
                    for ky in range(3)
                ],
                0,
            )
            y = dot(weight, v)
            results = []
            for j in range(RB):
                lanes = slice(j * LANES, (j + 1) * LANES)
                parts = []
                for g in range(groups):
                    a = [y[(3 * g + kx) * m : (3 * g + kx + 1) * m, lanes] for kx in range(3)]
                    parts.append(from_left(a[0], W) + a[1] + from_right(a[2], W))
                results.append(jnp.concatenate(parts, 0) if groups > 1 else parts[0])
            return emit(d, results, carry)

        return lax.fori_loop(0, S, body, init)

    def conv_stats(row, weight, z):
        def emit(d, results, carry):
            total, square = carry
            for j, v in enumerate(results):
                z[d * RB + j] = v
                total, square = total + v, square + v * v
            return total, square

        blank = jnp.zeros((dm.cf, LANES), F32)
        return conv(row, weight, dm.cd, nx, emit, (blank, blank))

    def weight_grad(row, k):
        cv = convs[k]
        dzf = k_.dzf
        n = E // 2
        acc[:, 0 : 3 * cv.c, 0 : cv.wide] = jnp.zeros((nx, 3 * cv.c, cv.wide), F32)

        def body(i, carry):
            d = lax.div(i, 2)
            r0 = (i - 2 * d) * n
            v = jnp.concatenate(
                [jnp.concatenate([row(d + kz, r0 + j) for j in range(n)], 1) for kz in range(3)], 0
            )
            for part in range(nx):
                y = jnp.concatenate(
                    [
                        jnp.concatenate(
                            [dzf[kx, d, r0 + j + 2 - ky, part * cv.o : (part + 1) * cv.o] for j in range(n)], 1
                        )
                        for ky in range(3)
                        for kx in range(3)
                    ],
                    0,
                ).astype(BF16)
                acc[part, 0 : 3 * cv.c, 0 : cv.taps] += dot_nt(v, y)
            return carry

        lax.fori_loop(0, S * 2, body, 0)

    def conv_coarse(ref, weight, m):
        v = jnp.concatenate(
            [jnp.concatenate([flat(ref, kz, i) for i in range(Q)], 1) for kz in range(3)], 0
        )
        y = dot(weight[...], v)
        blank = jnp.zeros((m, LANES), F32)

        def shifted(ky, i):
            if not 0 <= i < Q:
                return blank
            a, b, c = (
                y[(3 * ky + kx) * m : (3 * ky + kx + 1) * m, i * LANES : (i + 1) * LANES] for kx in range(3)
            )
            return from_left(a, V) + b + from_right(c, V)

        before = [shifted(0, i) for i in range(-1, Q)]
        after = [shifted(2, i) for i in range(Q + 1)]
        return [
            shifted(1, i) + halves(before[i + 1] + after[i + 1], before[i] + after[i]) for i in range(Q)
        ]

    def conv_stats_coarse(ref, weight, z, m):
        total = square = jnp.zeros((m, LANES), F32)
        for i, v in enumerate(conv_coarse(ref, weight, m)):
            z[i] = v
            total, square = total + v, square + v * v
        return total, square

    def weight_grad_coarse(ref, k):
        cv = convs[k]
        v = jnp.concatenate(
            [jnp.concatenate([flat(ref, kz, i) for i in range(Q)], 1) for kz in range(3)], 0
        )
        y = jnp.concatenate([jnp.concatenate([k_.dzc[t, i] for i in range(Q)], 1) for t in range(9)], 0)
        acc[0, 0 : 3 * cv.c, 0 : cv.taps] = dot_nt(v, y.astype(BF16))

    def pack(a, b):
        m = a.shape[0]
        a = jnp.sum(a, axis=1, keepdims=True)
        b = jnp.sum(b, axis=1, keepdims=True)
        lane, channel = iota((m, LANES), 1), iota((m, LANES), 0)
        both = jnp.where(lane == channel, a, jnp.where(lane == channel + m, b, 0.0))
        return jnp.sum(both, axis=0, keepdims=True)

    def moments(total, count):
        mean = total[0] / count
        var = total[1] / count - mean * mean
        return mean, lax.rsqrt(var + EPS)

    def wide(column):
        return jnp.broadcast_to(column, (column.shape[0], LANES))

    def factors(stats, norm):
        mean, inv = stats
        gain, shift = norm
        return wide(mean), wide(gain * inv), wide(shift)

    def norm_rows(z, stats, norm, emit, n):
        mean, scale, shift = factors(stats, norm)

        def body(i, carry):
            for j in range(n):
                p = i * n + j
                u = (z[p] - mean) * scale + shift
                emit(p, u * jax.nn.sigmoid(u))
            return carry

        lax.fori_loop(0, z.shape[0] // n, body, 0)

    def norm_back_sums(z, keep_du, stats, norm, grad, n):
        mean, scale, shift = factors(stats, norm)
        inv = wide(stats[1])
        m = z.shape[1]

        def body(i, carry):
            a, b = carry
            for j in range(n):
                p = i * n + j
                centred = z[p] - mean
                u = centred * scale + shift
                sigma = jax.nn.sigmoid(u)
                v = grad(p) * sigma * (1.0 + u * (1.0 - sigma))
                keep_du(p, v)
                a, b = a + v, b + v * (centred * inv)
            return a, b

        blank = jnp.zeros((m, LANES), F32)
        return lax.fori_loop(0, z.shape[0] // n, body, (blank, blank))

    def back_factors(stats, norm, total, count):
        mean, inv = stats
        scale = norm[0] * inv
        return wide(mean), wide(scale), wide(-scale * total[0] / count), wide(-scale * inv * total[1] / count)

    def norm_back_fine(z, given, ref):
        mean, scale, level, slope = given
        dzf = k_.dzf

        def body(d, carry):
            for r in range(RB):
                p = d * RB + r
                v = scale * k_.du_f[p] + level + slope * (z[p] - mean)
                low = v.astype(BF16)
                ref[core, 1 + d, 1 + r] = low.astype(ref.dtype)
                v = low.astype(F32)
                dzf[0, d, 2 + r] = from_right(v, W).astype(dzf.dtype)
                dzf[1, d, 2 + r] = low.astype(dzf.dtype)
                dzf[2, d, 2 + r] = from_left(v, W).astype(dzf.dtype)
            return carry

        lax.fori_loop(0, S, body, 0)

    def norm_back_coarse(z, given, ref):
        mean, scale, level, slope = given
        rows = []
        for i in range(Q):
            low = (scale * k_.du_c[i] + level + slope * (z[i] - mean)).astype(BF16)
            ref[core, x, 1, i] = low.astype(ref.dtype)
            rows.append(low.astype(F32))
        blank = jnp.zeros_like(rows[0])
        rows = [blank] + rows + [blank]
        for i in range(Q):
            before, here, after = rows[i : i + 3]
            for ky, v in enumerate((halves(after, here), here, halves(here, before))):
                for kx, u in enumerate((from_right(v, V), v, from_left(v, V))):
                    k_.dzc[3 * ky + kx, i] = u.astype(k_.dzc.dtype)

    def keep_du(ref):
        def store(p, v):
            ref[p] = v

        return store

    barrier = pltpu.get_barrier_semaphore()

    def greet(depth, chan):
        pl.semaphore_signal(barrier, inc=1, device_id={"depth": depth, "chan": chan}, device_id_type=MESH)

    exchange(nd * nx, wide_peers, lambda depth, chan: types.SimpleNamespace(start=lambda: greet(depth, chan)))
    for t in range(nx):
        greet(place, 2 * at_x(t)[0] + other)

    hc = iota((LANES, LANES), 0)
    fc = iota((LANES, LANES), 1)
    half = LANES // 2

    def up_table(coarse, fine):
        base = fine // 2
        beside = jnp.clip(base + jnp.where(fine % 2 == 0, -1, 1), 0, V - 1)
        near = (coarse == base).astype(F32)
        far = (coarse == beside).astype(F32)
        return (0.75 * near + 0.25 * far).astype(BF16)

    pool = jnp.concatenate([(hc // 2 == fc - at).astype(BF16) for at in (0, half)], 0)
    spread = jnp.concatenate([(hc - at == fc // 2).astype(BF16) for at in (0, half)], 1)
    up = jnp.concatenate([up_table(hc - at, fc) for at in (0, half)], 1)
    down = jnp.concatenate([up_table(fc, hc)] * 2, 0)
    spread2 = jnp.concatenate([spread, spread], 0)

    def take_rows(ref):
        for c in range(ref.shape[0]):
            k_.rows[c * S * R : (c + 1) * S * R] = ref[c].astype(F32).reshape(S * R, LANES)

    def row_of_all(p, chans):
        return k_.rows[pl.ds(p, chans, stride=S * R)]

    xp, xs, own_skip = k_.xp, k_.xs, k_.own_skip
    clear_halos(xp)
    take_rows(k_.skip)
    for i in range(S):
        for r in (0, R + 1):
            own_skip[i, r] = jnp.zeros((dm.cs, LANES), own_skip.dtype)

    def take_skip(i, carry):
        parts = []
        for d in range(S):
            v = [row_of_all(d * R + 4 * i + j, dm.cs).astype(BF16) for j in range(4)]
            for j in range(4):
                own_skip[d, 1 + 4 * i + j] = v[j].astype(own_skip.dtype)
            parts += [jnp.concatenate([v[j], v[2 + j]], 1) for j in range(2)]
        v = dot(jnp.concatenate(parts, 0), pool).reshape(2 * S, dm.cs, LANES)
        xp[core, x, 1, i] = (jnp.sum(v, axis=0) * 0.125).astype(BF16).astype(xp.dtype)
        return carry

    lax.fori_loop(0, Q, take_skip, 0, unroll=3)
    pl.semaphore_wait(barrier, nd * nx - 1 + nx)
    gather_start(xp, "pooled")
    clear_halos(xs)
    xs[core, x, 1 : S + 1] = own_skip[:, pl.ds(row0, E)]
    gather_start(xs, "skip", lambda at, tox: own_skip.at[at, pl.ds(tox * RB, E)])

    gq = dm.g // nc
    columns = dm.enc_all + dm.skip_all
    gate_all, norm_all = k_.gate_all, k_.norm_all
    gate_all[me, :, 0:columns] = k_.gate[...]
    lane = iota((gq, LANES), 1)
    gate_all[me, :, 2 * LANES :] = jnp.where(
        lane == 0, column(k_.vector[0:1]), jnp.where(lane == 1, column(k_.vector[1:2]), 0.0)
    )
    for layer in range(2):
        for part in range(2):
            at = 2 * layer + part
            norm_all[me, at : at + 1, 0 : dm.cd] = k_.dn[part, layer : layer + 1]

    def constants(i, t, source, to):
        ref = (norm_all, gate_all)[i]
        return peer_copy(ref.at[source], ref.at[source], k_.v_send.at[i, t], k_.v_recv.at[i, t], place, to)

    for i in range(2):
        for t in range(1, nc):
            launch(None, functools.partial(constants, i, t, me, lax.rem(me + t, nc)))
    prepare(0)
    xd, xz4, xz3, d1 = k_.xd, k_.xz4, k_.xz3, k_.d1
    for ref in (xd, xz4, xz3):
        clear_rows(ref)
        clear_halos(ref)
    for ref in (k_.xh, k_.xz2, k_.xz1):
        clear_halos(ref)
    for i in range(S):
        for r in (0, 1, RB + 2, RB + 3):
            for kx in range(3):
                k_.dzf[kx, i, r] = jnp.zeros(k_.dzf.shape[3:], k_.dzf.dtype)
        for r in range(3):
            k_.ug[i, r] = jnp.zeros(k_.ug.shape[2:], F32)
            k_.ug[i, RB + 3 + r] = jnp.zeros(k_.ug.shape[2:], F32)
        for r in range(H + 2):
            k_.cb[i, r] = jnp.zeros(k_.cb.shape[2:], F32)

    def norm_of(layer):
        return column(k_.en[0, layer : layer + 1]), column(k_.en[1, layer : layer + 1])

    norm_e1, norm_e2 = norm_of(0), norm_of(1)

    gather_pass(xp, "pooled")
    gather_wait(xp, "pooled")
    coarse_sums(0, conv_stats_coarse(xp, wf[0], k_.z1, dm.ce))
    prepare(1)
    stats_e1 = moments(coarse_totals(0), dm.coarse_total)

    def keep_coarse(ref):
        def store(p, v):
            ref[core, x, 1, p] = v.astype(BF16).astype(ref.dtype)

        return store

    norm_rows(k_.z1, stats_e1, norm_e1, keep_coarse(k_.xh), Q)
    gather_start(k_.xh, "hidden")
    prepare(2)
    forward_start(2)
    gather_pass(k_.xh, "hidden")
    gather_pass(xs, "skip")
    gather_wait(k_.xh, "hidden")
    coarse_sums(1, conv_stats_coarse(k_.xh, wf[1], k_.z2, dm.ce))
    take_rows(k_.cot)

    def take_cot(i, carry):
        for d in range(S):
            for j in range(4):
                v = row_of_all(d * R + 4 * i + j, dm.cd).astype(BF16)
                k_.own_cot[d, 4 * i + j] = v.astype(k_.own_cot.dtype)
        return carry

    lax.fori_loop(0, Q, take_cot, 0)
    k_.cots[x] = k_.own_cot[:, pl.ds(row0, RB)]
    stats_e2 = moments(coarse_totals(1), dm.coarse_total)
    norm_rows(k_.z2, stats_e2, norm_e2, keep_coarse(k_.xc), Q)
    gather_start(k_.xc, "coarse")
    prepare(3)
    for t in range(1, nc):
        for i in range(2):
            source = lax.rem(me + nc - t, nc)
            constants(i, t, source, source).wait_recv()
    gate_full = gate_all[...].reshape(dm.g, 3 * LANES)
    wg = gate_full[:, 0:columns].astype(BF16)
    gbias = gate_full[:, 2 * LANES : 2 * LANES + 1]
    gout = gate_full[:, 2 * LANES + 1 : 2 * LANES + 2]
    k_.gate_t[...] = jnp.transpose(gate_full[:, 0 : 2 * LANES])
    own_rows = [k_.gate_t[pl.ds(pl.multiple_of((2 * i + core) * dm.ce, dm.ce), dm.ce)] for i in range(nx)]
    own_rows += [
        k_.gate_t[pl.ds(pl.multiple_of(dm.enc_all + (2 * i + core) * dm.cs, dm.cs), dm.cs)] for i in range(nx)
    ]
    k_.gate_own[...] = jnp.concatenate(own_rows, 0)

    def norm_fine(layer):
        return tuple(
            jnp.concatenate(
                [column(norm_all[2 * i + core, 2 * layer + part : 2 * layer + part + 1, 0 : dm.cd]) for i in range(nx)], 0
            )
            for part in range(2)
        )

    norm_d1, norm_d2 = norm_fine(0), norm_fine(1)
    gather_pass(k_.xc, "coarse")
    gather_wait(k_.xc, "coarse")
    forward_start(3)

    dt = k_.dt

    def up_depth(i, carry):
        t = []
        for j in range(3):
            v = dot(flat(k_.xc, j, i), up)
            t.append(jnp.stack([v[:, 0:LANES], v[:, LANES:]], 0))
        below = jnp.where(first, t[1], t[0])
        above = jnp.where(last, t[1], t[2])
        near = 0.75 * t[1]
        here = 0.25 * t[1]
        rows = pl.ds(i * 2, 2)
        dt[0, rows] = jnp.where(first, 0.0, 0.75 * below + here)
        dt[1, rows] = near + 0.25 * below
        dt[2, rows] = near + 0.25 * above
        dt[3, rows] = jnp.where(last, 0.0, 0.75 * above + here)
        return carry

    lax.fori_loop(0, Q, up_depth, 0)

    def up_rows(i, carry):
        here = h0 + i
        before, after = jnp.maximum(here - 1, 0), jnp.minimum(here + 1, H - 1)
        for j in range(S + 2):
            v = 0.75 * dt[j, here]
            d1[j, 1 + 2 * i, 0 : dm.enc_all] = (v + 0.25 * dt[j, before]).astype(BF16)
            d1[j, 2 + 2 * i, 0 : dm.enc_all] = (v + 0.25 * dt[j, after]).astype(BF16)
        return carry

    lax.fori_loop(0, RB // 2, up_rows, 0)
    for edge, at, near, far in (
        (top, 0, jnp.maximum(h0 - 1, 0), h0),
        (bottom, E - 1, jnp.minimum(h0 + RB // 2, H - 1), h0 + RB // 2 - 1),
    ):
        for j in range(S + 2):
            v = jnp.where(edge, 0.0, 0.75 * dt[j, near] + 0.25 * dt[j, far])
            d1[j, at, 0 : dm.enc_all] = v.astype(BF16)
    for t in range(1, nx):
        tox = lax.rem(x + t, nx)

        def send_cot(t=t, tox=tox):
            return peer_copy(
                k_.own_cot.at[:, pl.ds(tox * RB, RB)], k_.cots.at[x], k_.o_send.at[0, t], k_.o_recv.at[0, t],
                place, 2 * tox + core,
            )

        launch(None, send_cot)

    gather_wait(xs, "skip")
    gate_n = E // 2

    def gate(i, carry):
        j = lax.div(i, 2)
        r0 = (i - 2 * j) * gate_n
        skips = [flat(xs, j, r0 + q) for q in range(gate_n)]
        v = jnp.concatenate(
            [
                jnp.concatenate([d1[j, r0 + q, 0 : dm.enc_all] for q in range(gate_n)], 1),
                jnp.concatenate(skips, 1),
            ],
            0,
        )
        pre = dot(wg, v) + gbias
        act = pre * jax.nn.sigmoid(pre)
        alpha = jax.nn.sigmoid(jnp.sum(gout * act, axis=0, keepdims=True))
        for q in range(gate_n):
            lanes = slice(q * LANES, (q + 1) * LANES)
            d1[j, r0 + q, dm.enc_all :] = (alpha[:, lanes] * skips[q].astype(F32)).astype(BF16)
            k_.pre[j, r0 + q] = pre[:, lanes]
            k_.alpha[j, r0 + q] = alpha[:, lanes]
        return carry

    lax.fori_loop(0, (S + 2) * 2, gate, 0)
    for k in (3, 2, 1, 0):
        weights_start(k)

    def row_d1(j, r):
        return d1[j, r]

    def row_xd(j, r):
        return natural(xd, j, r)

    forward_wait(2)
    fine_sums(0, conv_stats(row_d1, forward_weight(2), k_.z3))
    drain()
    forward_wait(3)
    stats_d1 = moments(fine_totals(0), dm.fine_total)

    def keep_dec(p, v):
        d = lax.div(p, RB)
        xd[core, 1 + d, 1 + p - d * RB] = v.astype(BF16).astype(xd.dtype)

    norm_rows(k_.z3, stats_d1, norm_d1, keep_dec, RB)
    fine_start(xd, "hidden")
    for t in range(1, nx):
        fromx = lax.rem(x + nx - t, nx)
        theirs = k_.cots.at[fromx]
        peer_copy(theirs, theirs, k_.o_send.at[0, t], k_.o_recv.at[0, t], place, 2 * fromx + core).wait_recv()
    fine_pass(xd, "hidden")
    weights_finish(3)
    fine_wait(xd, "hidden")
    fine_sums(1, conv_stats(row_xd, forward_weight(3), k_.z4))
    stats_d2 = moments(fine_totals(1), dm.fine_total)

    def row_cot(p):
        d = lax.div(p, RB)
        return jnp.concatenate([k_.cots[i, d, p - d * RB] for i in range(nx)], 0).astype(F32)

    fine_sums(2, norm_back_sums(k_.z4, keep_du(k_.du_f), stats_d2, norm_d2, row_cot, RB))

    def keep_result(p, v):
        for i in range(nx):
            k_.ob[i, p] = v[i * dm.cd : (i + 1) * dm.cd].astype(BF16).astype(k_.ob.dtype)

    norm_rows(k_.z4, stats_d2, norm_d2, keep_result, RB)
    for t in range(1, nx):
        tox = lax.rem(x + t, nx)

        def send_result(t=t, tox=tox):
            return peer_copy(
                k_.ob.at[tox], k_.oi.at[x], k_.o_send.at[1, t], k_.o_recv.at[1, t], place, 2 * tox + core
            )

        launch(None, send_result)
    total_d2 = fine_totals(2)
    norm_back_fine(k_.z4, back_factors(stats_d2, norm_d2, total_d2, dm.fine_total), xz4)
    fine_start(xz4, "dz4")
    weight_grad(row_xd, 3)
    fine_pass(xz4, "dz4")
    cross_start(3)
    fine_wait(xz4, "dz4")

    def row_xz4(j, r):
        return natural(xz4, j, r)

    def keep_grad(d, results, carry):
        for j, v in enumerate(results):
            k_.gg[d * RB + j] = v
        return carry

    conv(row_xz4, wb[3][...], dm.cf, 1, keep_grad, 0)
    fine_sums(3, norm_back_sums(k_.z3, keep_du(k_.du_f), stats_d1, norm_d1, lambda p: k_.gg[p], RB))
    cross_finish(3)
    total_d1 = fine_totals(3)
    norm_back_fine(k_.z3, back_factors(stats_d1, norm_d1, total_d1, dm.fine_total), xz3)
    fine_start(xz3, "dz3")
    weights_finish(2)
    weight_grad(row_d1, 2)
    fine_pass(xz3, "dz3")
    cross_start(2)
    fine_wait(xz3, "dz3")

    def row_xz3(j, r):
        return natural(xz3, j, r)

    ups = nx * dm.ce

    def gate_back(d, results, carry):
        bias, psi = carry
        lows = []
        for j, both in enumerate(results):
            p = d * RB + j
            v = both[ups:]
            grad = jnp.sum(v * flat(xs, d + 1, 1 + j).astype(F32), axis=0, keepdims=True)
            alpha = k_.alpha[d + 1, 1 + j]
            logit = grad * alpha * (1.0 - alpha)
            pre = k_.pre[d + 1, 1 + j]
            sigma = jax.nn.sigmoid(pre)
            psi = psi + pre * sigma * logit
            low = (logit * gout * sigma * (1.0 + pre * (1.0 - sigma))).astype(BF16)
            bias = bias + low.astype(F32)
            k_.pg[p] = low
            lows.append(low)
            k_.ug[d, 3 + j] = both[0:ups]
            for i in range(nc):
                k_.gv[i] = v[i * dm.cs : (i + 1) * dm.cs]
            for i in range(nx):
                k_.sgp[i, p] = alpha * k_.gv[2 * i + core]
        back = dot(k_.gate_own[...].astype(BF16), jnp.concatenate(lows, 1))
        for j in range(len(results)):
            p = d * RB + j
            lanes = slice(j * LANES, (j + 1) * LANES)
            k_.ug[d, 3 + j] += back[0:ups, lanes]
            for i in range(nx):
                v = k_.sgp[i, p] + back[ups + i * dm.cs : ups + (i + 1) * dm.cs, lanes]
                k_.sgp[i, p] = v
                k_.sgb[i, p] = v.astype(BF16).astype(k_.sgb.dtype)
        return bias, psi

    blank = jnp.zeros((dm.g, LANES), F32)
    bias, psi = conv(row_xz3, wb[2][...], ups + dm.skip_all, 1, gate_back, (blank, blank))

    ug, cb, cg = k_.ug, k_.cb, k_.cg
    for q in range(RB // 2 + 2):
        terms = []
        for d in range(S):
            v = 0.75 * (ug[d, 2 * q + 1] + ug[d, 2 * q + 2]) + 0.25 * (ug[d, 2 * q + 3] + ug[d, 2 * q])
            if q == 1:
                v += jnp.where(top, 0.25 * ug[d, 3], 0.0)
            if q == RB // 2:
                v += jnp.where(bottom, 0.25 * ug[d, RB + 2], 0.0)
            terms.append(split(v))
        v = dot(jnp.concatenate(terms, 0), down)
        for d in range(S):
            cb[d, h0 + q] = v[d * ups : (d + 1) * ups]

    def to_slabs(i, carry):
        even, odd = (cb[d, 2 * i + 1] + pltpu.roll(cb[d, 2 * i + 2], half, 1) for d in range(S))
        middle = 0.75 * (even + odd) + jnp.where(first, 0.25 * even, 0.0) + jnp.where(last, 0.25 * odd, 0.0)
        for part, v in enumerate((0.25 * even, middle, 0.25 * odd)):
            for j in range(nx):
                block = v[j * dm.ce : (j + 1) * dm.ce]
                k_.fs[part, j, i] = block.astype(BF16).astype(k_.fs.dtype)
                if part == 1:
                    k_.fm[j, i] = block
        return carry

    lax.fori_loop(0, Q, to_slabs, 0)

    def fold_parts():
        for step in (-1, 1, 0):
            sends = (no(first), None, no(last))[step + 1]
            gets = (no(last), None, no(first))[step + 1]
            for t in range(nx):
                if (step, t) != (0, 0):
                    tox, fromx = lax.rem(x + t, nx), lax.rem(x + nx - t, nx)
                    sems = (k_.f_send.at[step + 1, t], k_.f_recv.at[step + 1, t])
                    theirs = k_.fr.at[step + 1, fromx]
                    yield (
                        sends, gets, fromx, step + 1,
                        functools.partial(
                            peer_copy, k_.fs.at[step + 1, tox], k_.fr.at[step + 1, x], *sems, place + step, 2 * tox + core
                        ),
                        functools.partial(peer_copy, theirs, theirs, *sems, place, 2 * fromx + core),
                    )

    for sends, _, _, _, out, _ in fold_parts():
        launch(sends, out)
    for t in range(1, nx):
        tox = lax.rem(x + t, nx)

        def send_skip(t=t, tox=tox):
            return peer_copy(
                k_.sgb.at[tox], k_.sgi.at[x], k_.o_send.at[2, t], k_.o_recv.at[2, t], place, 2 * tox + core
            )

        launch(None, send_skip)

    acc[0, 0 : dm.g, 0:columns] = jnp.zeros((dm.g, columns), F32)

    def gate_weight(d, carry):
        v = jnp.concatenate(
            [
                jnp.concatenate([d1[1 + d, 1 + j, 0 : dm.enc_all] for j in range(RB)], 1),
                jnp.concatenate([flat(xs, 1 + d, 1 + j) for j in range(RB)], 1),
            ],
            0,
        )
        y = jnp.concatenate([k_.pg[d * RB + j] for j in range(RB)], 1)
        acc[0, 0 : dm.g, 0:columns] += dot_nt(y, v)
        return carry

    lax.fori_loop(0, S, gate_weight, 0)
    lane = iota((dm.g, LANES), 1)
    vectors = jnp.where(
        lane == 0,
        jnp.sum(bias, axis=1, keepdims=True),
        jnp.where(lane == 1, jnp.sum(psi, axis=1, keepdims=True), 0.0),
    )
    gate_block = k_.gate_block
    for j in range(nc):
        mine = slice(j * gq, (j + 1) * gq)
        gate_block[j, :, 0:columns] = acc[0, mine, 0:columns]
        gate_block[j, :, columns : 2 * LANES] = jnp.zeros((gq, 2 * LANES - columns), F32)
        gate_block[j, :, 2 * LANES :] = vectors[mine]
    sum_start(everyone, k_.sv, 4, 0, gate_block[me], lambda chan: gate_block.at[chan])
    cg[...] = k_.fm[x]
    for _, gets, fromx, part, _, back in fold_parts():

        def fold_in(back=back, part=part, fromx=fromx):
            back().wait_recv()
            cg[...] += k_.fr[part, fromx].astype(F32)

        guarded(gets, fold_in)

    coarse_sums(2, norm_back_sums(k_.z2, keep_du(k_.du_c), stats_e2, norm_e2, lambda p: cg[p], Q))
    cross_finish(2)
    weights_finish(1)
    total_e2 = coarse_totals(2)
    norm_back_coarse(k_.z2, back_factors(stats_e2, norm_e2, total_e2, dm.coarse_total), k_.xz2)
    gather_start(k_.xz2, "dz2")
    weight_grad_coarse(k_.xh, 1)
    reduce_finish(3)
    gather_pass(k_.xz2, "dz2")
    reduce_start(1)
    weights_finish(0)
    drain()
    gather_wait(k_.xz2, "dz2")
    for i, v in enumerate(conv_coarse(k_.xz2, wb[1], dm.ce)):
        cg[i] = v
    coarse_sums(3, norm_back_sums(k_.z1, keep_du(k_.du_c), stats_e1, norm_e1, lambda p: cg[p], Q))
    reduce_finish(2)
    total_e1 = coarse_totals(3)
    norm_back_coarse(k_.z1, back_factors(stats_e1, norm_e1, total_e1, dm.coarse_total), k_.xz1)
    gather_start(k_.xz1, "dz1")
    weight_grad_coarse(xp, 0)
    reduce_start(0)
    reduce_finish(1)
    gather_pass(k_.xz1, "dz1")
    gradient_out(3)

    def rows_out(ref, own, theirs, kind, size):
        def copy_rows(read, at):
            def body(d, carry):
                for r in range(RB):
                    p = (d * R + at * RB + r) * size
                    ref[pl.ds(pl.multiple_of(p, size), size)] = read(d * RB + r).astype(F32)
                return carry

            lax.fori_loop(0, S, body, 0)

        copy_rows(lambda p: own[x, p], x)
        for t in range(1, nx):
            fromx = lax.rem(x + nx - t, nx)
            block = theirs.at[fromx]
            peer_copy(block, block, k_.o_send.at[kind, t], k_.o_recv.at[kind, t], place, 2 * fromx + core).wait_recv()
            copy_rows(lambda p, fromx=fromx: theirs[fromx, p], fromx)

    rows_out(k_.out, k_.ob, k_.oi, 1, dm.cd)
    rows_out(k_.sg, k_.sgp, k_.sgi, 2, dm.cs)
    gather_wait(k_.xz1, "dz1")
    for i, v in enumerate(conv_coarse(k_.xz1, wb[0], dm.cs)):
        v = dot(split(v), spread2) * 0.125
        for j in range(4):
            part = v[:, (j // 2) * LANES : (j // 2 + 1) * LANES]
            for d in range(S):
                at = (d * R + 4 * i + j) * dm.cs
                k_.sg[at : at + dm.cs] += part
    reduce_finish(0)
    gradient_out(2)
    gradient_out(1)
    gate_total = sum_finish(everyone, k_.sv, 4, 0)
    k_.ggate[...] = gate_total[:, 0:columns]
    k_.gvector[0:1] = row_of(gate_total[:, 2 * LANES : 2 * LANES + 1])
    k_.gvector[1:2] = row_of(gate_total[:, 2 * LANES + 1 : 2 * LANES + 2])

    def own_part(col):
        parts = [jnp.where(x == i, col[i * dm.cd : (i + 1) * dm.cd], 0.0) for i in range(nx)]
        return functools.reduce(jnp.add, parts)

    for ref, pair, pick in ((k_.gen, (total_e1, total_e2), lambda v: v), (k_.gdn, (total_d1, total_d2), own_part)):
        for layer, total in enumerate(pair):
            ref[0, layer : layer + 1] = row_of(pick(total[1]))
            ref[1, layer : layer + 1] = row_of(pick(total[0]))
    gradient_out(0)
    drain()


def adamw(weight, grad, moment, square, rate):
    new_moment = 0.9 * moment + 0.1 * grad
    new_square = 0.999 * square + 0.001 * grad * grad
    moment_hat = new_moment / (1.0 - 0.9**STEP)
    square_hat = new_square / (1.0 - 0.999**STEP)
    new_weight = weight - rate * (moment_hat / (jnp.sqrt(square_hat) + 1e-08) + 0.01 * weight)
    return (new_weight, new_moment, new_square)


RATES = (CONV_RATE, CONV_RATE, GATE_RATE, VECTOR_RATE, CONV_RATE, CONV_RATE, VECTOR_RATE, VECTOR_RATE)


def update_kernel(*refs):
    n = len(RATES)
    sources, targets = refs[: 2 + 4 * n], refs[2 + 4 * n : 4 + 7 * n]
    inside, outside = refs[4 + 7 * n : 6 + 11 * n], refs[6 + 11 * n : 8 + 14 * n]
    in_sem, out_sem = refs[8 + 14 * n :]
    order = (4, 1, 0, 5, 2, 3, 6, 7)

    def load(i):
        return pltpu.make_async_copy(sources[i], inside[i], in_sem.at[i])

    def store(i):
        return pltpu.make_async_copy(outside[i], targets[i], out_sem.at[i])

    for i in (1, 0):
        load(i).start()
    for k in order:
        for part in range(4):
            load(2 + part * n + k).start()
    for i in (1, 0):
        load(i).wait()
        chans, (slabs, rows) = outside[i].shape[0], outside[i].shape[1:3]
        for c in range(chans):
            v = inside[i][pl.ds(c, slabs * rows, stride=chans)]
            outside[i][c] = v.reshape(slabs, rows, LANES).astype(outside[i].dtype)
        store(i).start()
    for k in order:
        own = [2 + part * n + k for part in range(4)]
        for i in own:
            load(i).wait()
        rows = inside[own[0]].shape[0]
        step = 8 if rows % 8 == 0 and rows > 8 else rows
        for r in range(0, rows, step):
            at = slice(r, r + step)
            new = adamw(*(inside[i][at] for i in own), RATES[k])
            for part, value in enumerate(new):
                outside[2 + 3 * k + part][at] = value
        for part in range(3):
            store(2 + 3 * k + part).start()
    for i in range(len(targets)):
        store(i).wait()


def per_device(
    skip, cotangent, enc_conv1, enc_conv2, gate_proj, gate_vector, dec_conv1, dec_conv2, enc_norms, dec_norms, *states
):
    nd, nc = lax.axis_size("depth"), lax.axis_size("chan")
    dm = Dims(nd, nc, skip.shape, enc_conv1.shape[0], dec_conv1.shape[0], gate_proj.shape[0] * nc)
    S, R, H, nx, RB, E = dm.s, dm.rows, dm.half, dm.nx, dm.rb, dm.ext
    Q = H // 2
    cin3 = dm.enc_all + dm.skip_all

    def own_block(size):
        return (size, lambda j: pl.multiple_of(j * size, size), 0)

    def core_blocks(size):
        return tuple(
            (size, lambda j, i=i: pl.multiple_of((2 * i + lax.rem(j, 2)) * size, size), i * size) for i in range(nx)
        )

    dm.convs = convs = (
        Conv(dm, dm.ce, dm.skip_all, (own_block(dm.cs),)),
        Conv(dm, dm.ce, dm.enc_all, (own_block(dm.ce),)),
        Conv(dm, dm.cd, cin3, core_blocks(dm.ce) + ((dm.skip_all, lambda j: dm.enc_all, nx * dm.ce),)),
        Conv(dm, dm.cd, dm.dec_all, core_blocks(dm.cd)),
    )
    params = (enc_conv1, enc_conv2, gate_proj, gate_vector, dec_conv1, dec_conv2, enc_norms, dec_norms)
    inputs = dict(
        skip=skip, cot=cotangent, w0=enc_conv1, w1=enc_conv2, w2=dec_conv1, w3=dec_conv2,
        gate=gate_proj, vector=gate_vector, en=enc_norms, dn=dec_norms,
    )
    shape = jax.ShapeDtypeStruct
    outs = dict(
        out=shape((S * R * dm.cd, LANES), F32),
        sg=shape((S * R * dm.cs, LANES), F32),
        **{f"g{i}": shape(a.shape, F32) for i, a in enumerate((enc_conv1, enc_conv2, dec_conv1, dec_conv2))},
        **{
            name: shape(a.shape, F32)
            for name, a in (("ggate", gate_proj), ("gvector", gate_vector), ("gen", enc_norms), ("gdn", dec_norms))
        },
    )
    gq = dm.g // nc

    def coarse(block):
        return pltpu.VMEM((2, nx, 3, Q, block, LANES), storage(block))

    def fine():
        return pltpu.VMEM((2, S + 2, E, dm.cf, LANES), storage(dm.cd))

    def f32(*dims):
        return pltpu.VMEM((*dims, LANES), F32)

    def tiles(*dims):
        return pltpu.VMEM((*dims, 16, LANES), BF16)

    def blocks(block, *dims):
        return pltpu.VMEM((*dims, block, LANES), storage(block))

    def sems(*dims):
        return pltpu.SemaphoreType.DMA(dims)

    scratch = dict(
        xp=coarse(dm.cs), xh=coarse(dm.ce), xc=coarse(dm.ce), xz2=coarse(dm.ce), xz1=coarse(dm.ce),
        own_skip=blocks(dm.cs, S, R + 2), xs=blocks(dm.cs, 2, nx, S + 2, E),
        own_cot=blocks(dm.cd, S, R), cots=blocks(dm.cd, nx, S, RB),
        d1=pltpu.VMEM((S + 2, E, cin3, LANES), BF16), xd=fine(), xz4=fine(), xz3=fine(),
        z1=f32(Q, dm.ce), z2=f32(Q, dm.ce), z3=f32(S * RB, dm.cf), z4=f32(S * RB, dm.cf),
        du_c=f32(Q, dm.ce), du_f=f32(S * RB, dm.cf), gg=f32(S * RB, dm.cf), cg=f32(Q, dm.ce),
        pre=f32(S + 2, E, dm.g), alpha=f32(S + 2, E, 1), pg=pltpu.VMEM((S * RB, dm.g, LANES), BF16),
        ug=f32(S, RB + 6, nx * dm.ce), cb=f32(S, H + 2, nx * dm.ce), dt=f32(S + 2, H, dm.enc_all),
        gv=f32(nc, dm.cs), sgp=f32(nx, S * RB, dm.cs), sgb=blocks(dm.cs, nx, S * RB), sgi=blocks(dm.cs, nx, S * RB),
        ob=blocks(dm.cd, nx, S * RB), oi=blocks(dm.cd, nx, S * RB),
        dzf=pltpu.VMEM((3, S, RB + 4, dm.cf, LANES), storage(dm.cd)),
        dzc=pltpu.VMEM((9, Q, dm.ce, LANES), BF16),
        fs=blocks(dm.ce, 3, nx, Q), fr=blocks(dm.ce, 3, nx, Q), fm=f32(nx, Q, dm.ce),
        st=f32(4, nd, 1), su=f32(4, nd * nx, 1), sv=pltpu.VMEM((1, nd * nx, gq, 3 * LANES), F32),
        norm_all=f32(nc, 8), rows=f32(max(dm.cs, dm.cd) * S * R),
        turned=f32(max(cv.chunks for cv in convs) * LANES),
        acc=pltpu.VMEM((nx, max(3 * cv.c for cv in convs), max(cv.wide for cv in convs)), F32),
        gate_all=pltpu.VMEM((nc, gq, 3 * LANES), F32), gate_t=pltpu.VMEM((2 * LANES, dm.g), F32),
        gate_own=pltpu.VMEM((nx * (dm.ce + dm.cs), dm.g), F32), gate_block=pltpu.VMEM((nc, gq, 3 * LANES), F32),
        **{f"wt{i}": pltpu.VMEM((3, cv.c, cv.wide), cv.kind) for i, cv in enumerate(convs)},
        **{
            f"wf{i}": pltpu.VMEM((cv.taps, 3 * cv.c) if i < 2 else (nx, cv.stored, 9 * cv.c), BF16)
            for i, cv in enumerate(convs)
        },
        **{f"wx{i}": pltpu.VMEM((nc, 3, cv.needed, cv.wide), cv.kind) for i, cv in enumerate(convs)},
        **{
            f"wb{i}": pltpu.VMEM((9 * cv.needed, 3 * nc * cv.o) if i < 2 else (3 * cv.needed, 9 * nc * cv.o), BF16)
            for i, cv in enumerate(convs)
        },
        flip=pltpu.VMEM((max(cv.tiles for cv in convs[2:]) * LANES, max(3 * cv.c for cv in convs[2:])), F32),
        **{f"gt{i}": tiles(cv.share * nd) for i, cv in enumerate(convs)},
        **{f"gr{i}": tiles(nd, cv.share) for i, cv in enumerate(convs)},
        **{f"ga{i}": tiles(cv.share * nd) for i, cv in enumerate(convs)},
        **{f"gs{i}": tiles(nx, convs[i].count) for i in (2, 3)},
        **{f"gx{i}": tiles(nx, convs[i].count) for i in (2, 3)},
        g_send=sems(len(GATHERS), 3, nx), g_recv=sems(len(GATHERS), 3),
        h_send=sems(len(GATHERS)), h_recv=sems(len(GATHERS)),
        x_send=sems(len(FINE), 3, 3), x_recv=sems(len(FINE), 3, 3), y_send=sems(len(FINE)), y_recv=sems(len(FINE)),
        t_send=sems(4), t_recv=sems(4), u_send=sems(5), u_recv=sems(5),
        f_send=sems(3, nx), f_recv=sems(3, nx), w_send=sems(4, nx + 1, nc), w_recv=sems(4, nx + 1, nc),
        p_send=sems(2, nx), p_recv=sems(2, nx), c_send=sems(2, nx), c_recv=sems(2, nx),
        o_send=sems(3, nx), o_recv=sems(3, nx), v_send=sems(2, nc), v_recv=sems(2, nc),
        r_send=sems(4), r_recv=sems(4), a_send=sems(4), a_recv=sems(4),
    )
    vmem = pl.BlockSpec(memory_space=pltpu.VMEM)
    out, sg, grad1, grad2, grad3, grad4, ggate, gvector, gen, gdn = pl.pallas_call(
        functools.partial(kernel, dm, (*inputs, *outs, *scratch)),
        out_shape=tuple(outs.values()),
        in_specs=[vmem] * len(inputs),
        out_specs=[vmem] * len(outs),
        scratch_shapes=list(scratch.values()),
        compiler_params=pltpu.CompilerParams(
            has_side_effects=True, collective_id=0, vmem_limit_bytes=60 * 1024 * 1024
        ),
        name="step",
    )(*inputs.values())
    grads = (grad1, grad2, ggate, gvector, grad3, grad4, gen, gdn)
    operands = (out, sg, *params, *grads, *states)
    updated = (
        shape(cotangent.shape, BF16),
        shape(skip.shape, F32),
        *(shape(p.shape, F32) for p in params for _ in range(3)),
    )
    anywhere = pl.BlockSpec(memory_space=pl.ANY)
    return pl.pallas_call(
        update_kernel,
        out_shape=updated,
        in_specs=[anywhere] * len(operands),
        out_specs=[anywhere] * len(updated),
        scratch_shapes=[
            *(pltpu.VMEM(a.shape, a.dtype) for a in operands),
            *(pltpu.VMEM(a.shape, a.dtype) for a in updated),
            pltpu.SemaphoreType.DMA((len(operands),)),
            pltpu.SemaphoreType.DMA((len(updated),)),
        ],
        compiler_params=pltpu.CompilerParams(vmem_limit_bytes=60 * 1024 * 1024),
        name="update",
    )(*operands)


def solution(mesh):
    volume = P("chan", "depth", None, None)
    row, column, norms = P("chan", None), P(None, "chan"), P(None, None, "chan")
    params = (row, row, row, column, row, row, norms, norms)
    return jax.shard_map(
        per_device,
        mesh=mesh,
        in_specs=(volume, volume) + params * 3,
        out_specs=(volume, volume) + tuple(spec for spec in params for _ in range(3)),
        check_vma=False,
    )
```

```python
import functools
import types

import jax
import jax.numpy as jnp
from jax import lax
from jax.experimental import pallas as pl
from jax.experimental.pallas import tpu as pltpu
from jax.sharding import PartitionSpec as P

STEP = 5
EPS = 1e-05
CONV_RATE = 0.03
GATE_RATE = 0.1
VECTOR_RATE = 0.5
LANES = 128
MESH = pl.DeviceIdType.MESH
F32 = jnp.float32
BF16 = jnp.bfloat16


def iota(shape, dim):
    return lax.broadcasted_iota(jnp.int32, shape, dim)


def dot(a, b):
    return jnp.dot(a, b, preferred_element_type=F32)


def dot_nt(a, b):
    return lax.dot_general(a, b, (((1,), (1,)), ((), ())), preferred_element_type=F32)


def from_left(v, width):
    return jnp.where(iota(v.shape, 1) % width == 0, 0.0, pltpu.roll(v, 1, 1))


def from_right(v, width):
    return jnp.where(iota(v.shape, 1) % width == width - 1, 0.0, pltpu.roll(v, LANES - 1, 1))


def halves(low, high):
    return pltpu.roll(jnp.where(iota(low.shape, 1) < LANES // 2, low, high), LANES // 2, 1)


def split(v):
    high = v.astype(BF16)
    return jnp.concatenate([high, (v - high.astype(F32)).astype(BF16)], 1)


def storage(block):
    return BF16 if block % 16 == 0 else F32


def flat(ref, s, r):
    if len(ref.shape) == 4:
        return ref[s, r]
    v = ref[:, :, s, r]
    return jnp.concatenate([v[c, i] for i in range(v.shape[1]) for c in range(2)], 0).astype(BF16)


class Dims:
    def __init__(self, nd, nc, skip, enc, dec, gate):
        self.nd, self.nc, self.nx = nd, nc, nc // 2
        self.s, self.rows, self.cols = skip[1:]
        self.cs, self.ce, self.cd, self.g = skip[0], enc, dec, gate
        self.half, self.hcols = self.rows // 2, self.cols // 2
        self.fine_total = nd * self.s * self.rows * self.cols
        self.coarse_total = self.fine_total // 8
        self.enc_all = nc * enc
        self.skip_all = nc * skip[0]
        self.dec_all = nc * dec
        self.rb = self.rows // self.nx
        self.ext = self.rb + 2
        self.cf = self.nx * dec


GATHERS = ("pooled", "skip", "hidden", "coarse", "dz2", "dz1")
FINE = ("hidden", "dz4", "dz3")


class Conv:
    def __init__(self, dm, o, c, blocks):
        self.o, self.c, self.blocks = o, c, blocks
        self.length = 27 * c
        self.chunks = -(-self.length // LANES)
        self.per = LANES // o
        self.tiles = -(-9 // self.per)
        self.wide = self.tiles * LANES
        self.kind = storage(min(size for size, _, _ in blocks))
        self.needed = sum(size for size, _, _ in blocks)
        self.count = 3 * c // 16 * self.tiles
        self.share = -(-self.count // dm.nd)
        self.taps = 9 * o
        self.stored = -(-3 * o // 16) * 16


def kernel(dm, names, *refs):
    k_ = types.SimpleNamespace(**dict(zip(names, refs)))
    nd, nc, nx, S, R, H = dm.nd, dm.nc, dm.nx, dm.s, dm.rows, dm.half
    W, V = dm.cols, dm.hcols
    Q, RB, E = H // 2, dm.rb, dm.ext
    place = lax.axis_index("depth")
    me = lax.axis_index("chan")
    x, core = lax.div(me, 2), lax.rem(me, 2)
    other = 1 - core
    mate = 2 * x + other
    row0, h0 = x * RB, x * (RB // 2)
    first, last = place == 0, place == nd - 1
    top, bottom = x == 0, x == nx - 1
    convs = dm.convs
    pending = []
    wt, wf, wx, wb = ([getattr(k_, f"{kind}{i}") for i in range(4)] for kind in ("wt", "wf", "wx", "wb"))
    gt, gr, ga = ([getattr(k_, f"{kind}{i}") for i in range(4)] for kind in ("gt", "gr", "ga"))
    weights = (k_.w0, k_.w1, k_.w2, k_.w3)
    grads = (k_.g0, k_.g1, k_.g2, k_.g3)
    turned, acc = k_.turned, k_.acc

    def no(cond):
        return jnp.logical_not(cond)

    def peer_copy(src, dst, send, recv, depth, chan):
        return pltpu.make_async_remote_copy(
            src_ref=src, dst_ref=dst, send_sem=send, recv_sem=recv,
            device_id={"depth": depth, "chan": chan}, device_id_type=MESH,
        )

    def guarded(cond, fn):
        if cond is None:
            fn()
        else:
            pl.when(cond)(fn)

    def drain():
        for cond, fn in pending:
            guarded(cond, fn)
        pending.clear()

    def launch(cond, copy):
        guarded(cond, lambda: copy().start())
        pending.append((cond, lambda: copy().wait_send()))

    def arrive(cond, copy):
        guarded(cond, lambda: copy().wait_recv())

    def both(a, b):
        return b if a is None else a if b is None else jnp.logical_and(a, b)

    can_send = (no(last), None, no(first))
    can_recv = (no(first), None, no(last))

    def slices(side, n):
        return (pl.ds(n, 1), pl.ds(1, n), pl.ds(1, 1))[side], (pl.ds(0, 1), pl.ds(1, n), pl.ds(n + 1, 1))[side]

    def at_x(t):
        up, down = x + t, x - t
        return jnp.where(up >= nx, up - nx, up), jnp.where(down < 0, down + nx, down)


    def gather_start(ref, which, source_at=None):
        n = ref.shape[2] - 2
        k = GATHERS.index(which)
        for side in (0, 2, 1):
            own, theirs = slices(side, n)
            for t in range(nx):
                if side == 1 and t == 0:
                    continue
                tox = at_x(t)[0]

                def copy(side=side, t=t, own=own, theirs=theirs, tox=tox):
                    start = (n, 1, 1)[side] - 1
                    size = (1, n, 1)[side]
                    src = ref.at[core, x, own] if source_at is None else source_at(pl.ds(start, size), tox)
                    return peer_copy(
                        src, ref.at[core, x, theirs], k_.g_send.at[k, side, t], k_.g_recv.at[k, side],
                        place + 1 - side, 2 * tox + core,
                    )

                launch(can_send[side], copy)
        gather_own(ref, which)

    def handed(ref, k, piece, i):
        return peer_copy(piece, piece, k_.h_send.at[k, i], k_.h_recv.at[k], place, mate)

    def gather_own(ref, which):
        k = GATHERS.index(which)
        launch(None, lambda: handed(ref, k, ref.at[core, x, pl.ds(1, ref.shape[2] - 2)], 0))

    def gather_pass(ref, which):
        n = ref.shape[2] - 2
        k = GATHERS.index(which)
        for side in (1, 0, 2):
            theirs = slices(side, n)[1]
            if side != 1:
                pieces = [ref.at[core, :, theirs]]
            else:
                pieces = [ref.at[core, at_x(t)[1], theirs] for t in range(1, nx)]
            for i, got in enumerate(pieces):
                arrive(
                    can_recv[side],
                    lambda got=got, side=side: peer_copy(
                        got, got, k_.g_send.at[k, side, 0], k_.g_recv.at[k, side], place, mate
                    ),
                )
                launch(None, lambda got=got, i=i, side=side: handed(ref, k, got, 1 + (side // 2 if side != 1 else 2 + i)))

    def gather_wait(ref, which):
        handed(ref, GATHERS.index(which), ref.at[other], 0).wait_recv()

    def fine_parts(ref, which, side):
        k = FINE.index(which)
        own, theirs = slices(side, S)
        inner = pl.ds(1, RB)
        rows = [(None, None, inner, inner, x, core, core)] if side != 1 else [(None, None, inner, inner, x, other, other)]
        if nx > 1:
            for c in range(2):
                rows.append((no(top), no(bottom), pl.ds(1, 1), pl.ds(E - 1, 1), x - 1, c, c))
                rows.append((no(bottom), no(top), pl.ds(RB, 1), pl.ds(0, 1), x + 1, c, c))
        parts = []
        for i, (sends, gets, row, at, tox, to, source) in enumerate(rows):
            target = ref.at[core, theirs, at]
            theirs_ = ref.at[source, theirs, at]
            up = (i - 1) % 2
            arrived = 0 if i == 0 else 1 + up * 2 + core
            expected = 0 if i == 0 else 1 + up * 2 + source
            send = k_.x_send.at[k, side, i]
            parts.append((
                both(can_send[side], sends), both(can_recv[side], gets),
                functools.partial(
                    peer_copy, ref.at[core, own, row], target, send, k_.x_recv.at[k, side, arrived],
                    place + 1 - side, 2 * tox + to,
                ),
                functools.partial(peer_copy, theirs_, theirs_, send, k_.x_recv.at[k, side, expected], place, mate),
            ))
        return parts

    def fine_start(ref, which):
        for side in (0, 2, 1):
            for sends, _, out, _ in fine_parts(ref, which, side):
                launch(sends, out)

    def fine_halo(ref, which, side, c):
        k = FINE.index(which)
        block = ref.at[c, slices(side, S)[1], pl.ds(1, RB)]
        return peer_copy(block, block, k_.y_send.at[k, side], k_.y_recv.at[k, side], place, mate)

    def fine_pass(ref, which):
        for side in (0, 2):
            _, gets, _, back = fine_parts(ref, which, side)[0]
            arrive(gets, back)
            launch(gets, functools.partial(fine_halo, ref, which, side, core))

    def fine_wait(ref, which):
        for side in (1, 0, 2):
            for _, gets, _, back in fine_parts(ref, which, side)[side != 1 :]:
                arrive(gets, back)
            if side != 1:
                arrive(can_recv[side], functools.partial(fine_halo, ref, which, side, other))

    def natural(ref, s, r):
        v = ref[:, s, r]
        size = dm.cd
        return jnp.concatenate(
            [v[c, i * size : (i + 1) * size] for i in range(nx) for c in range(2)], 0
        ).astype(BF16)

    def in_turn(count, fn):
        if count <= 16:
            for i in range(count):
                fn(i)
        else:

            def body(i, carry):
                fn(i)
                return carry

            lax.fori_loop(0, count, body, 0)

    def slab_peers(i):
        to = place + 1 + i
        return jnp.where(to >= nd, to - nd, to), me

    def wide_peers(i):
        i = i + 1
        dt, xt = (i // nx, i % nx) if isinstance(i, int) else (lax.div(i, nx), lax.rem(i, nx))
        to, tox = place + dt, x + xt
        return jnp.where(to >= nd, to - nd, to), 2 * jnp.where(tox >= nx, tox - nx, tox) + core

    def exchange(n, peers, copy):
        in_turn(n - 1, lambda i: copy(*peers(i)).start())

    def sum_start(group, ref, k, slot, tile, source=None):
        n, own, peers, send, recv = group
        ref[slot, own] = tile

        def copy(depth, chan):
            src = ref.at[slot, own] if source is None else source(chan)
            return peer_copy(src, ref.at[slot, own], send.at[k], recv.at[k], depth, chan)

        exchange(n, peers, copy)
        pending.append((None, lambda: all_of(group, ref, k, slot).wait_send()))

    def all_of(group, ref, k, slot):
        n, _, _, send, recv = group
        every = ref.at[slot, pl.ds(0, n - 1)]
        return peer_copy(every, every, send.at[k], recv.at[k], place, mate)

    def sum_finish(group, ref, k, slot):
        all_of(group, ref, k, slot).wait_recv()
        return jnp.sum(ref[slot], axis=0)

    slabs = (nd, place, slab_peers, k_.t_send, k_.t_recv)
    everyone = (nd * nx, place * nx + x, wide_peers, k_.u_send, k_.u_recv)

    def columns_of(row, m):
        lane, channel = iota((m, LANES), 1), iota((m, LANES), 0)
        return tuple(
            jnp.sum(jnp.where(lane == channel + i * m, row, 0.0), axis=1, keepdims=True) for i in range(2)
        )

    def coarse_sums(slot, sums):
        sum_start(slabs, k_.st, slot, slot, pack(*sums))

    def coarse_totals(slot):
        return columns_of(sum_finish(slabs, k_.st, slot, slot), dm.ce)

    def fine_sums(slot, sums):
        sum_start(everyone, k_.su, slot, slot, pack(*sums))

    def fine_totals(slot):
        return columns_of(sum_finish(everyone, k_.su, slot, slot), dm.cf)

    def turn_in(w, cv):
        eye = (iota((LANES, LANES), 0) == iota((LANES, LANES), 1)).astype(BF16)

        def chunk(a):
            return dot_nt(eye, jnp.concatenate([a] * cv.per, 0).astype(BF16))

        full = cv.length // LANES

        def body(i, carry):
            at = pl.multiple_of(i * LANES, LANES)
            turned[pl.ds(at, LANES)] = chunk(w[:, pl.ds(at, LANES)])
            return carry

        lax.fori_loop(0, full, body, 0, unroll=4)
        if full < cv.chunks:
            a = w[:, full * LANES :]
            a = jnp.concatenate([a, jnp.zeros((cv.o, LANES - a.shape[1]), F32)], 1)
            turned[full * LANES : (full + 1) * LANES] = chunk(a)

    def prepare(k):
        cv, w, own = convs[k], weights[k], wt[k]
        out = wf[k] if k < 2 else wf[k].at[x]
        turn_in(w, cv)
        group = iota((cv.c, LANES), 1) // cv.o
        for kz in range(3):
            for j in range(cv.tiles):
                tile = None
                for g in range(cv.per):
                    t = j * cv.per + g
                    if t < 9:
                        v = turned[pl.ds(9 * kz + t, cv.c, stride=27)]
                        tile = v if tile is None else jnp.where(group == g, v, tile)
                own[kz, :, j * LANES : (j + 1) * LANES] = tile.astype(BF16).astype(own.dtype)
        eye = (iota((LANES, LANES), 0) == iota((LANES, LANES), 1)).astype(BF16)
        for j in range(cv.tiles):
            v = jnp.concatenate([own[kz, :, j * LANES : (j + 1) * LANES] for kz in range(3)], 0)
            size = min(LANES, cv.taps - j * LANES)
            v = dot_nt(eye, v.astype(BF16))[0:size]
            if k < 2:
                out[j * LANES : j * LANES + size] = v.astype(BF16)
            else:
                k_.flip[j * LANES : j * LANES + size, 0 : 3 * cv.c] = v
        if k >= 2:
            rows = 3 * cv.o
            out[0:rows] = jnp.concatenate(
                [
                    k_.flip[ky * rows : (ky + 1) * rows, kz * cv.c : (kz + 1) * cv.c]
                    for kz in range(3)
                    for ky in range(3)
                ],
                1,
            ).astype(BF16)

    def forward_copy(k, t):
        block = wf[k].at[x]
        return peer_copy(
            block, block, k_.p_send.at[k - 2, t], k_.p_recv.at[k - 2, t], place, 2 * lax.rem(x + t, nx) + core
        )

    def forward_start(k):
        for t in range(1, nx):
            launch(None, functools.partial(forward_copy, k, t))

    def forward_wait(k):
        for t in range(1, nx):
            fromx = lax.rem(x + nx - t, nx)
            block = wf[k].at[fromx]
            peer_copy(
                block, block, k_.p_send.at[k - 2, t], k_.p_recv.at[k - 2, t], place, 2 * fromx + core
            ).wait_recv()

    def forward_weight(k):
        return jnp.concatenate([wf[k][i, 0 : 3 * convs[k].o] for i in range(nx)], 0)

    def weights_start(k):
        cv = convs[k]
        for b, (size, start, at) in enumerate(cv.blocks):
            wx[k][me, :, at : at + size] = wt[k][:, pl.ds(start(me), size)]
            for t in range(1, nc):
                to = lax.rem(me + t, nc)

                def copy(to=to, t=t, b=b, size=size, start=start, at=at):
                    return peer_copy(
                        wt[k].at[:, pl.ds(start(to), size)], wx[k].at[me, :, pl.ds(at, size)],
                        k_.w_send.at[k, b, t], k_.w_recv.at[k, b, t], place, to,
                    )

                launch(None, copy)

    def weights_finish(k):
        cv = convs[k]
        for b, (size, _, at) in enumerate(cv.blocks):
            for t in range(1, nc):
                source = lax.rem(me + nc - t, nc)
                theirs = wx[k].at[source, :, pl.ds(at, size)]
                peer_copy(theirs, theirs, k_.w_send.at[k, b, t], k_.w_recv.at[k, b, t], place, source).wait_recv()

        def pieces(kz, t):
            return [wx[k][j, 2 - kz, :, t * cv.o : (t + 1) * cv.o].astype(F32) for j in range(nc)]

        for i in range(9 if k < 2 else 3):
            if k < 2:
                found = [v for kz in range(3) for v in pieces(kz, 8 - i)]
            else:
                found = [v for kz in range(3) for ky in range(3) for v in pieces(kz, 3 * (2 - ky) + 2 - i)]
            wb[k][i * cv.needed : (i + 1) * cv.needed] = jnp.concatenate(found, 1).astype(BF16)

    def tiles_of(k, part, put):
        cv = convs[k]

        def tile(i, carry):
            at = pl.multiple_of(i * 16, 16)
            for j in range(cv.tiles):
                put(i * cv.tiles + j, acc[part, pl.ds(at, 16), j * LANES : (j + 1) * LANES].astype(BF16))
            return carry

        lax.fori_loop(0, 3 * cv.c // 16, tile, 0, unroll=4)

    def cross_start(k):
        gs, gx = (k_.gs2, k_.gs3)[k - 2], (k_.gx2, k_.gx3)[k - 2]
        for part in range(nx):

            def put(i, v, part=part):
                gs[part, i] = v

            tiles_of(k, part, put)
        for t in range(1, nx):
            tox = lax.rem(x + t, nx)

            def copy(t=t, tox=tox):
                return peer_copy(
                    gs.at[tox], gx.at[x], k_.c_send.at[k - 2, t], k_.c_recv.at[k - 2, t], place, 2 * tox + core
                )

            launch(None, copy)

    def cross_finish(k):
        cv, gs, gx = convs[k], (k_.gs2, k_.gs3)[k - 2], (k_.gx2, k_.gx3)[k - 2]
        sources = [lax.rem(x + nx - t, nx) for t in range(1, nx)]
        for t, fromx in enumerate(sources, 1):
            theirs = gx.at[fromx]
            peer_copy(
                theirs, theirs, k_.c_send.at[k - 2, t], k_.c_recv.at[k - 2, t], place, 2 * fromx + core
            ).wait_recv()

        def add(i, carry):
            for j in range(cv.tiles):
                p = i * cv.tiles + j
                v = gs[x, p].astype(F32)
                for fromx in sources:
                    v += gx[fromx, p].astype(F32)
                gt[k][p] = v.astype(BF16)
            return carry

        lax.fori_loop(0, 3 * cv.c // 16, add, 0, unroll=4)
        reduce_send(k)

    def reduce_start(k):
        def put(i, v):
            gt[k][i] = v

        tiles_of(k, 0, put)
        reduce_send(k)

    def reduce_send(k):
        cv = convs[k]
        for i in range(cv.count, cv.share * nd):
            gt[k][i] = jnp.zeros((16, LANES), BF16)
        gr[k][place] = gt[k][pl.ds(place * cv.share, cv.share)]

        def copy(to, chan):
            return peer_copy(
                gt[k].at[pl.ds(to * cv.share, cv.share)], gr[k].at[place], k_.r_send.at[k], k_.r_recv.at[k], to, chan
            )

        exchange(nd, slab_peers, copy)
        pending.append((None, lambda: reduce_all(k).wait_send()))

    def reduce_all(k):
        every = gr[k].at[pl.ds(0, nd - 1)]
        return peer_copy(every, every, k_.r_send.at[k], k_.r_recv.at[k], place, mate)

    def share_all(k):
        every = ga[k].at[pl.ds(0, (nd - 1) * convs[k].share)]
        return peer_copy(every, every, k_.a_send.at[k], k_.a_recv.at[k], place, mate)

    def reduce_finish(k):
        cv = convs[k]
        reduce_all(k).wait_recv()
        own = pl.ds(place * cv.share, cv.share)
        ga[k][own] = jnp.sum(gr[k][...].astype(F32), axis=0).astype(BF16)

        def copy(to, chan):
            return peer_copy(ga[k].at[own], ga[k].at[own], k_.a_send.at[k], k_.a_recv.at[k], to, chan)

        exchange(nd, slab_peers, copy)
        pending.append((None, lambda: share_all(k).wait_send()))

    def gradient_out(k):
        cv, out = convs[k], grads[k]
        share_all(k).wait_recv()
        group = iota((16, LANES), 1) // cv.o

        def scatter(i, carry):
            for kz in range(3):
                for j in range(cv.tiles):
                    v = ga[k][(kz * (cv.c // 16) + i) * cv.tiles + j].astype(F32)
                    for g in range(cv.per):
                        t = j * cv.per + g
                        if t < 9:
                            turned[pl.ds(9 * kz + t + i * (16 * 27), 16, stride=27)] = jnp.where(group == g, v, 0.0)
            return carry

        lax.fori_loop(0, cv.c // 16, scatter, 0, unroll=2)

        pick = (iota((cv.o, LANES), 1) % cv.o == iota((cv.o, LANES), 0)).astype(BF16)
        step = 8 * LANES
        for at in range(0, cv.length, step):
            size = min(step, cv.length - at)
            v = dot_nt(pick, turned[at : at + -(-size // LANES) * LANES].astype(BF16))
            out[:, at : at + size] = v[:, 0:size]

    def column(row):
        n = row.shape[1]
        eye = iota((n, n), 0) == iota((n, n), 1)
        return jnp.sum(jnp.where(eye, row, 0.0), axis=1, keepdims=True)

    def row_of(col):
        n = col.shape[0]
        eye = iota((n, n), 0) == iota((n, n), 1)
        return jnp.sum(jnp.where(eye, col, 0.0), axis=0, keepdims=True)

    def clear_halos(ref):
        def clear(at):
            if len(ref.shape) == 5:
                for c in range(2):
                    ref[c, at] = jnp.zeros(ref.shape[2:], ref.dtype)
            else:
                for i in range(nx):
                    ref[core, i, at] = jnp.zeros(ref.shape[3:], ref.dtype)

        pl.when(first)(lambda: clear(0))
        pl.when(last)(lambda: clear(ref.shape[-4] - 1))

    def clear_rows(ref):
        def clear(at):
            for c in range(2):
                for i in range(S + 2):
                    ref[c, i, at] = jnp.zeros(ref.shape[3:], ref.dtype)

        pl.when(top)(lambda: clear(0))
        pl.when(bottom)(lambda: clear(E - 1))

    def conv(row, weight, m, groups, emit, init):
        def body(d, carry):
            v = jnp.concatenate(
                [
                    jnp.concatenate([row(d + kz, ky + j) for j in range(RB)], 1)
                    for kz in range(3)
                    for ky in range(3)
                ],
                0,
            )
            y = dot(weight, v)
            results = []
            for j in range(RB):
                lanes = slice(j * LANES, (j + 1) * LANES)
                parts = []
                for g in range(groups):
                    a = [y[(3 * g + kx) * m : (3 * g + kx + 1) * m, lanes] for kx in range(3)]
                    parts.append(from_left(a[0], W) + a[1] + from_right(a[2], W))
                results.append(jnp.concatenate(parts, 0) if groups > 1 else parts[0])
            return emit(d, results, carry)

        return lax.fori_loop(0, S, body, init)

    def conv_stats(row, weight, z):
        def emit(d, results, carry):
            total, square = carry
            for j, v in enumerate(results):
                z[d * RB + j] = v
                total, square = total + v, square + v * v
            return total, square

        blank = jnp.zeros((dm.cf, LANES), F32)
        return conv(row, weight, dm.cd, nx, emit, (blank, blank))

    def weight_grad(row, k):
        cv = convs[k]
        dzf = k_.dzf
        n = E // 2
        acc[:, 0 : 3 * cv.c, 0 : cv.wide] = jnp.zeros((nx, 3 * cv.c, cv.wide), F32)

        def body(i, carry):
            d = lax.div(i, 2)
            r0 = (i - 2 * d) * n
            v = jnp.concatenate(
                [jnp.concatenate([row(d + kz, r0 + j) for j in range(n)], 1) for kz in range(3)], 0
            )
            for part in range(nx):
                y = jnp.concatenate(
                    [
                        jnp.concatenate(
                            [dzf[kx, d, r0 + j + 2 - ky, part * cv.o : (part + 1) * cv.o] for j in range(n)], 1
                        )
                        for ky in range(3)
                        for kx in range(3)
                    ],
                    0,
                ).astype(BF16)
                acc[part, 0 : 3 * cv.c, 0 : cv.taps] += dot_nt(v, y)
            return carry

        lax.fori_loop(0, S * 2, body, 0)

    def conv_coarse(ref, weight, m):
        v = jnp.concatenate(
            [jnp.concatenate([flat(ref, kz, i) for i in range(Q)], 1) for kz in range(3)], 0
        )
        y = dot(weight[...], v)
        blank = jnp.zeros((m, LANES), F32)

        def shifted(ky, i):
            if not 0 <= i < Q:
                return blank
            a, b, c = (
                y[(3 * ky + kx) * m : (3 * ky + kx + 1) * m, i * LANES : (i + 1) * LANES] for kx in range(3)
            )
            return from_left(a, V) + b + from_right(c, V)

        before = [shifted(0, i) for i in range(-1, Q)]
        after = [shifted(2, i) for i in range(Q + 1)]
        return [
            shifted(1, i) + halves(before[i + 1] + after[i + 1], before[i] + after[i]) for i in range(Q)
        ]

    def conv_stats_coarse(ref, weight, z, m):
        total = square = jnp.zeros((m, LANES), F32)
        for i, v in enumerate(conv_coarse(ref, weight, m)):
            z[i] = v
            total, square = total + v, square + v * v
        return total, square

    def weight_grad_coarse(ref, k):
        cv = convs[k]
        v = jnp.concatenate(
            [jnp.concatenate([flat(ref, kz, i) for i in range(Q)], 1) for kz in range(3)], 0
        )
        y = jnp.concatenate([jnp.concatenate([k_.dzc[t, i] for i in range(Q)], 1) for t in range(9)], 0)
        acc[0, 0 : 3 * cv.c, 0 : cv.taps] = dot_nt(v, y.astype(BF16))

    def pack(a, b):
        m = a.shape[0]
        a = jnp.sum(a, axis=1, keepdims=True)
        b = jnp.sum(b, axis=1, keepdims=True)
        lane, channel = iota((m, LANES), 1), iota((m, LANES), 0)
        both = jnp.where(lane == channel, a, jnp.where(lane == channel + m, b, 0.0))
        return jnp.sum(both, axis=0, keepdims=True)

    def moments(total, count):
        mean = total[0] / count
        var = total[1] / count - mean * mean
        return mean, lax.rsqrt(var + EPS)

    def wide(column):
        return jnp.broadcast_to(column, (column.shape[0], LANES))

    def factors(stats, norm):
        mean, inv = stats
        gain, shift = norm
        return wide(mean), wide(gain * inv), wide(shift)

    def norm_rows(z, stats, norm, emit, n):
        mean, scale, shift = factors(stats, norm)

        def body(i, carry):
            for j in range(n):
                p = i * n + j
                u = (z[p] - mean) * scale + shift
                emit(p, u * jax.nn.sigmoid(u))
            return carry

        lax.fori_loop(0, z.shape[0] // n, body, 0)

    def norm_back_sums(z, keep_du, stats, norm, grad, n):
        mean, scale, shift = factors(stats, norm)
        inv = wide(stats[1])
        m = z.shape[1]

        def body(i, carry):
            a, b = carry
            for j in range(n):
                p = i * n + j
                centred = z[p] - mean
                u = centred * scale + shift
                sigma = jax.nn.sigmoid(u)
                v = grad(p) * sigma * (1.0 + u * (1.0 - sigma))
                keep_du(p, v)
                a, b = a + v, b + v * (centred * inv)
            return a, b

        blank = jnp.zeros((m, LANES), F32)
        return lax.fori_loop(0, z.shape[0] // n, body, (blank, blank))

    def back_factors(stats, norm, total, count):
        mean, inv = stats
        scale = norm[0] * inv
        return wide(mean), wide(scale), wide(-scale * total[0] / count), wide(-scale * inv * total[1] / count)

    def norm_back_fine(z, given, ref):
        mean, scale, level, slope = given
        dzf = k_.dzf

        def body(d, carry):
            for r in range(RB):
                p = d * RB + r
                v = scale * k_.du_f[p] + level + slope * (z[p] - mean)
                low = v.astype(BF16)
                ref[core, 1 + d, 1 + r] = low.astype(ref.dtype)
                v = low.astype(F32)
                dzf[0, d, 2 + r] = from_right(v, W).astype(dzf.dtype)
                dzf[1, d, 2 + r] = low.astype(dzf.dtype)
                dzf[2, d, 2 + r] = from_left(v, W).astype(dzf.dtype)
            return carry

        lax.fori_loop(0, S, body, 0)

    def norm_back_coarse(z, given, ref):
        mean, scale, level, slope = given
        rows = []
        for i in range(Q):
            low = (scale * k_.du_c[i] + level + slope * (z[i] - mean)).astype(BF16)
            ref[core, x, 1, i] = low.astype(ref.dtype)
            rows.append(low.astype(F32))
        blank = jnp.zeros_like(rows[0])
        rows = [blank] + rows + [blank]
        for i in range(Q):
            before, here, after = rows[i : i + 3]
            for ky, v in enumerate((halves(after, here), here, halves(here, before))):
                for kx, u in enumerate((from_right(v, V), v, from_left(v, V))):
                    k_.dzc[3 * ky + kx, i] = u.astype(k_.dzc.dtype)

    def keep_du(ref):
        def store(p, v):
            ref[p] = v

        return store

    barrier = pltpu.get_barrier_semaphore()

    def greet(depth, chan):
        pl.semaphore_signal(barrier, inc=1, device_id={"depth": depth, "chan": chan}, device_id_type=MESH)

    exchange(nd * nx, wide_peers, lambda depth, chan: types.SimpleNamespace(start=lambda: greet(depth, chan)))
    for t in range(nx):
        to = 2 * at_x(t)[0] + other
        greet(place, to)
        if t > 0:
            pl.when(no(first))(lambda to=to: greet(place - 1, to))
            pl.when(no(last))(lambda to=to: greet(place + 1, to))

    hc = iota((LANES, LANES), 0)
    fc = iota((LANES, LANES), 1)
    half = LANES // 2

    def up_table(coarse, fine):
        base = fine // 2
        beside = jnp.clip(base + jnp.where(fine % 2 == 0, -1, 1), 0, V - 1)
        near = (coarse == base).astype(F32)
        far = (coarse == beside).astype(F32)
        return (0.75 * near + 0.25 * far).astype(BF16)

    pool = jnp.concatenate([(hc // 2 == fc - at).astype(BF16) for at in (0, half)], 0)
    spread = jnp.concatenate([(hc - at == fc // 2).astype(BF16) for at in (0, half)], 1)
    up = jnp.concatenate([up_table(hc - at, fc) for at in (0, half)], 1)
    down = jnp.concatenate([up_table(fc, hc)] * 2, 0)
    spread2 = jnp.concatenate([spread, spread], 0)

    def take_rows(ref):
        for c in range(ref.shape[0]):
            k_.rows[c * S * R : (c + 1) * S * R] = ref[c].astype(F32).reshape(S * R, LANES)

    def row_of_all(p, chans):
        return k_.rows[pl.ds(p, chans, stride=S * R)]

    xp, xs, own_skip = k_.xp, k_.xs, k_.own_skip
    clear_halos(xp)
    take_rows(k_.skip)
    for i in range(S):
        for r in (0, R + 1):
            own_skip[i, r] = jnp.zeros((dm.cs, LANES), own_skip.dtype)

    def take_skip(i, carry):
        parts = []
        for d in range(S):
            v = [row_of_all(d * R + 4 * i + j, dm.cs).astype(BF16) for j in range(4)]
            for j in range(4):
                own_skip[d, 1 + 4 * i + j] = v[j].astype(own_skip.dtype)
            parts += [jnp.concatenate([v[j], v[2 + j]], 1) for j in range(2)]
        v = dot(jnp.concatenate(parts, 0), pool).reshape(2 * S, dm.cs, LANES)
        xp[core, x, 1, i] = (jnp.sum(v, axis=0) * 0.125).astype(BF16).astype(xp.dtype)
        return carry

    lax.fori_loop(0, Q, take_skip, 0, unroll=3)
    beside = jnp.where(first, 0, 1) + jnp.where(last, 0, 1)
    pl.semaphore_wait(barrier, nd * nx - 1 + nx + (nx - 1) * beside)
    gather_start(xp, "pooled")
    clear_halos(xs)
    xs[core, x, 1 : S + 1] = own_skip[:, pl.ds(row0, E)]
    gather_start(xs, "skip", lambda at, tox: own_skip.at[at, pl.ds(tox * RB, E)])

    gq = dm.g // nc
    columns = dm.enc_all + dm.skip_all
    gate_all, norm_all = k_.gate_all, k_.norm_all
    gate_all[me, :, 0:columns] = k_.gate[...]
    lane = iota((gq, LANES), 1)
    gate_all[me, :, 2 * LANES :] = jnp.where(
        lane == 0, column(k_.vector[0:1]), jnp.where(lane == 1, column(k_.vector[1:2]), 0.0)
    )
    for layer in range(2):
        for part in range(2):
            at = 2 * layer + part
            norm_all[me, at : at + 1, 0 : dm.cd] = k_.dn[part, layer : layer + 1]

    def constants(i, t, source, to):
        ref = (norm_all, gate_all)[i]
        return peer_copy(ref.at[source], ref.at[source], k_.v_send.at[i, t], k_.v_recv.at[i, t], place, to)

    for i in range(2):
        for t in range(1, nc):
            launch(None, functools.partial(constants, i, t, me, lax.rem(me + t, nc)))
    prepare(0)
    xd, xz4, xz3, d1 = k_.xd, k_.xz4, k_.xz3, k_.d1
    for ref in (xd, xz4, xz3):
        clear_rows(ref)
        clear_halos(ref)
    for ref in (k_.xh, k_.xz2, k_.xz1):
        clear_halos(ref)
    for i in range(S):
        for r in (0, 1, RB + 2, RB + 3):
            for kx in range(3):
                k_.dzf[kx, i, r] = jnp.zeros(k_.dzf.shape[3:], k_.dzf.dtype)
        for r in range(3):
            k_.ug[i, r] = jnp.zeros(k_.ug.shape[2:], F32)
            k_.ug[i, RB + 3 + r] = jnp.zeros(k_.ug.shape[2:], F32)
        for r in range(H + 2):
            k_.cb[i, r] = jnp.zeros(k_.cb.shape[2:], F32)

    def norm_of(layer):
        return column(k_.en[0, layer : layer + 1]), column(k_.en[1, layer : layer + 1])

    norm_e1, norm_e2 = norm_of(0), norm_of(1)

    gather_pass(xp, "pooled")
    gather_wait(xp, "pooled")
    coarse_sums(0, conv_stats_coarse(xp, wf[0], k_.z1, dm.ce))
    prepare(1)
    stats_e1 = moments(coarse_totals(0), dm.coarse_total)

    def keep_coarse(ref):
        def store(p, v):
            ref[core, x, 1, p] = v.astype(BF16).astype(ref.dtype)

        return store

    norm_rows(k_.z1, stats_e1, norm_e1, keep_coarse(k_.xh), Q)
    gather_start(k_.xh, "hidden")
    prepare(2)
    forward_start(2)
    gather_pass(k_.xh, "hidden")
    gather_pass(xs, "skip")
    gather_wait(k_.xh, "hidden")
    coarse_sums(1, conv_stats_coarse(k_.xh, wf[1], k_.z2, dm.ce))
    take_rows(k_.cot)

    def take_cot(i, carry):
        for d in range(S):
            for j in range(4):
                v = row_of_all(d * R + 4 * i + j, dm.cd).astype(BF16)
                k_.own_cot[d, 4 * i + j] = v.astype(k_.own_cot.dtype)
        return carry

    lax.fori_loop(0, Q, take_cot, 0)
    k_.cots[x] = k_.own_cot[:, pl.ds(row0, RB)]
    stats_e2 = moments(coarse_totals(1), dm.coarse_total)
    norm_rows(k_.z2, stats_e2, norm_e2, keep_coarse(k_.xc), Q)
    gather_start(k_.xc, "coarse")
    prepare(3)
    for t in range(1, nc):
        for i in range(2):
            source = lax.rem(me + nc - t, nc)
            constants(i, t, source, source).wait_recv()
    gate_full = gate_all[...].reshape(dm.g, 3 * LANES)
    wg = gate_full[:, 0:columns].astype(BF16)
    gbias = gate_full[:, 2 * LANES : 2 * LANES + 1]
    gout = gate_full[:, 2 * LANES + 1 : 2 * LANES + 2]
    k_.gate_t[...] = jnp.transpose(gate_full[:, 0 : 2 * LANES])
    own_rows = [k_.gate_t[pl.ds(pl.multiple_of((2 * i + core) * dm.ce, dm.ce), dm.ce)] for i in range(nx)]
    own_rows += [
        k_.gate_t[pl.ds(pl.multiple_of(dm.enc_all + (2 * i + core) * dm.cs, dm.cs), dm.cs)] for i in range(nx)
    ]
    k_.gate_own[...] = jnp.concatenate(own_rows, 0)

    def norm_fine(layer):
        return tuple(
            jnp.concatenate(
                [column(norm_all[2 * i + core, 2 * layer + part : 2 * layer + part + 1, 0 : dm.cd]) for i in range(nx)], 0
            )
            for part in range(2)
        )

    norm_d1, norm_d2 = norm_fine(0), norm_fine(1)
    gather_pass(k_.xc, "coarse")
    gather_wait(k_.xc, "coarse")
    forward_start(3)

    dt = k_.dt

    def up_depth(i, carry):
        t = []
        for j in range(3):
            v = dot(flat(k_.xc, j, i), up)
            t.append(jnp.stack([v[:, 0:LANES], v[:, LANES:]], 0))
        below = jnp.where(first, t[1], t[0])
        above = jnp.where(last, t[1], t[2])
        near = 0.75 * t[1]
        here = 0.25 * t[1]
        rows = pl.ds(i * 2, 2)
        dt[0, rows] = jnp.where(first, 0.0, 0.75 * below + here)
        dt[1, rows] = near + 0.25 * below
        dt[2, rows] = near + 0.25 * above
        dt[3, rows] = jnp.where(last, 0.0, 0.75 * above + here)
        return carry

    lax.fori_loop(0, Q, up_depth, 0)

    def up_rows(i, carry):
        here = h0 + i
        before, after = jnp.maximum(here - 1, 0), jnp.minimum(here + 1, H - 1)
        for j in range(S + 2):
            v = 0.75 * dt[j, here]
            d1[j, 1 + 2 * i, 0 : dm.enc_all] = (v + 0.25 * dt[j, before]).astype(BF16)
            d1[j, 2 + 2 * i, 0 : dm.enc_all] = (v + 0.25 * dt[j, after]).astype(BF16)
        return carry

    lax.fori_loop(0, RB // 2, up_rows, 0)
    for edge, at, near, far in (
        (top, 0, jnp.maximum(h0 - 1, 0), h0),
        (bottom, E - 1, jnp.minimum(h0 + RB // 2, H - 1), h0 + RB // 2 - 1),
    ):
        for j in range(S + 2):
            v = jnp.where(edge, 0.0, 0.75 * dt[j, near] + 0.25 * dt[j, far])
            d1[j, at, 0 : dm.enc_all] = v.astype(BF16)
    for t in range(1, nx):
        tox = lax.rem(x + t, nx)

        def send_cot(t=t, tox=tox):
            return peer_copy(
                k_.own_cot.at[:, pl.ds(tox * RB, RB)], k_.cots.at[x], k_.o_send.at[0, t], k_.o_recv.at[0, t],
                place, 2 * tox + core,
            )

        launch(None, send_cot)

    gather_wait(xs, "skip")
    gate_n = E // 2

    def gate(i, carry):
        j = lax.div(i, 2)
        r0 = (i - 2 * j) * gate_n
        skips = [flat(xs, j, r0 + q) for q in range(gate_n)]
        v = jnp.concatenate(
            [
                jnp.concatenate([d1[j, r0 + q, 0 : dm.enc_all] for q in range(gate_n)], 1),
                jnp.concatenate(skips, 1),
            ],
            0,
        )
        pre = dot(wg, v) + gbias
        act = pre * jax.nn.sigmoid(pre)
        alpha = jax.nn.sigmoid(jnp.sum(gout * act, axis=0, keepdims=True))
        for q in range(gate_n):
            lanes = slice(q * LANES, (q + 1) * LANES)
            d1[j, r0 + q, dm.enc_all :] = (alpha[:, lanes] * skips[q].astype(F32)).astype(BF16)
            k_.pre[j, r0 + q] = pre[:, lanes]
            k_.alpha[j, r0 + q] = alpha[:, lanes]
        return carry

    lax.fori_loop(0, (S + 2) * 2, gate, 0)
    for k in (3, 2, 1, 0):
        weights_start(k)

    def row_d1(j, r):
        return d1[j, r]

    def row_xd(j, r):
        return natural(xd, j, r)

    forward_wait(2)
    fine_sums(0, conv_stats(row_d1, forward_weight(2), k_.z3))
    drain()
    forward_wait(3)
    stats_d1 = moments(fine_totals(0), dm.fine_total)

    def keep_dec(p, v):
        d = lax.div(p, RB)
        xd[core, 1 + d, 1 + p - d * RB] = v.astype(BF16).astype(xd.dtype)

    norm_rows(k_.z3, stats_d1, norm_d1, keep_dec, RB)
    fine_start(xd, "hidden")
    for t in range(1, nx):
        fromx = lax.rem(x + nx - t, nx)
        theirs = k_.cots.at[fromx]
        peer_copy(theirs, theirs, k_.o_send.at[0, t], k_.o_recv.at[0, t], place, 2 * fromx + core).wait_recv()
    fine_pass(xd, "hidden")
    weights_finish(3)
    fine_wait(xd, "hidden")
    fine_sums(1, conv_stats(row_xd, forward_weight(3), k_.z4))
    stats_d2 = moments(fine_totals(1), dm.fine_total)

    def row_cot(p):
        d = lax.div(p, RB)
        return jnp.concatenate([k_.cots[i, d, p - d * RB] for i in range(nx)], 0).astype(F32)

    fine_sums(2, norm_back_sums(k_.z4, keep_du(k_.du_f), stats_d2, norm_d2, row_cot, RB))

    def keep_result(p, v):
        for i in range(nx):
            k_.ob[i, p] = v[i * dm.cd : (i + 1) * dm.cd].astype(BF16).astype(k_.ob.dtype)

    norm_rows(k_.z4, stats_d2, norm_d2, keep_result, RB)
    for t in range(1, nx):
        tox = lax.rem(x + t, nx)

        def send_result(t=t, tox=tox):
            return peer_copy(
                k_.ob.at[tox], k_.oi.at[x], k_.o_send.at[1, t], k_.o_recv.at[1, t], place, 2 * tox + core
            )

        launch(None, send_result)
    total_d2 = fine_totals(2)
    norm_back_fine(k_.z4, back_factors(stats_d2, norm_d2, total_d2, dm.fine_total), xz4)
    fine_start(xz4, "dz4")
    weight_grad(row_xd, 3)
    fine_pass(xz4, "dz4")
    cross_start(3)
    fine_wait(xz4, "dz4")

    def row_xz4(j, r):
        return natural(xz4, j, r)

    def keep_grad(d, results, carry):
        for j, v in enumerate(results):
            k_.gg[d * RB + j] = v
        return carry

    conv(row_xz4, wb[3][...], dm.cf, 1, keep_grad, 0)
    fine_sums(3, norm_back_sums(k_.z3, keep_du(k_.du_f), stats_d1, norm_d1, lambda p: k_.gg[p], RB))
    cross_finish(3)
    total_d1 = fine_totals(3)
    norm_back_fine(k_.z3, back_factors(stats_d1, norm_d1, total_d1, dm.fine_total), xz3)
    fine_start(xz3, "dz3")
    weights_finish(2)
    weight_grad(row_d1, 2)
    fine_pass(xz3, "dz3")
    cross_start(2)
    fine_wait(xz3, "dz3")

    def row_xz3(j, r):
        return natural(xz3, j, r)

    ups = nx * dm.ce

    def gate_back(d, results, carry):
        bias, psi = carry
        lows = []
        for j, both in enumerate(results):
            p = d * RB + j
            v = both[ups:]
            grad = jnp.sum(v * flat(xs, d + 1, 1 + j).astype(F32), axis=0, keepdims=True)
            alpha = k_.alpha[d + 1, 1 + j]
            logit = grad * alpha * (1.0 - alpha)
            pre = k_.pre[d + 1, 1 + j]
            sigma = jax.nn.sigmoid(pre)
            psi = psi + pre * sigma * logit
            low = (logit * gout * sigma * (1.0 + pre * (1.0 - sigma))).astype(BF16)
            bias = bias + low.astype(F32)
            k_.pg[p] = low
            lows.append(low)
            k_.ug[d, 3 + j] = both[0:ups]
            for i in range(nc):
                k_.gv[i] = v[i * dm.cs : (i + 1) * dm.cs]
            for i in range(nx):
                k_.sgp[i, p] = alpha * k_.gv[2 * i + core]
        back = dot(k_.gate_own[...].astype(BF16), jnp.concatenate(lows, 1))
        for j in range(len(results)):
            p = d * RB + j
            lanes = slice(j * LANES, (j + 1) * LANES)
            k_.ug[d, 3 + j] += back[0:ups, lanes]
            for i in range(nx):
                v = k_.sgp[i, p] + back[ups + i * dm.cs : ups + (i + 1) * dm.cs, lanes]
                k_.sgp[i, p] = v
                k_.sgb[i, p] = v.astype(BF16).astype(k_.sgb.dtype)
        return bias, psi

    blank = jnp.zeros((dm.g, LANES), F32)
    bias, psi = conv(row_xz3, wb[2][...], ups + dm.skip_all, 1, gate_back, (blank, blank))

    ug, cb, cg = k_.ug, k_.cb, k_.cg
    for q in range(RB // 2 + 2):
        terms = []
        for d in range(S):
            v = 0.75 * (ug[d, 2 * q + 1] + ug[d, 2 * q + 2]) + 0.25 * (ug[d, 2 * q + 3] + ug[d, 2 * q])
            if q == 1:
                v += jnp.where(top, 0.25 * ug[d, 3], 0.0)
            if q == RB // 2:
                v += jnp.where(bottom, 0.25 * ug[d, RB + 2], 0.0)
            terms.append(split(v))
        v = dot(jnp.concatenate(terms, 0), down)
        for d in range(S):
            cb[d, h0 + q] = v[d * ups : (d + 1) * ups]

    def to_slabs(i, carry):
        even, odd = (cb[d, 2 * i + 1] + pltpu.roll(cb[d, 2 * i + 2], half, 1) for d in range(S))
        middle = 0.75 * (even + odd) + jnp.where(first, 0.25 * even, 0.0) + jnp.where(last, 0.25 * odd, 0.0)
        for part, v in enumerate((0.25 * even, middle, 0.25 * odd)):
            for j in range(nx):
                block = v[j * dm.ce : (j + 1) * dm.ce]
                k_.fs[part, j, i] = block.astype(BF16).astype(k_.fs.dtype)
                if part == 1:
                    k_.fm[j, i] = block
        return carry

    lax.fori_loop(0, Q, to_slabs, 0)

    def fold_parts():
        for step in (-1, 1, 0):
            sends = (no(first), None, no(last))[step + 1]
            gets = (no(last), None, no(first))[step + 1]
            for t in range(nx):
                if (step, t) != (0, 0):
                    tox, fromx = lax.rem(x + t, nx), lax.rem(x + nx - t, nx)
                    sems = (k_.f_send.at[step + 1, t], k_.f_recv.at[step + 1, t])
                    theirs = k_.fr.at[step + 1, fromx]
                    yield (
                        sends, gets, fromx, step + 1,
                        functools.partial(
                            peer_copy, k_.fs.at[step + 1, tox], k_.fr.at[step + 1, x], *sems, place + step, 2 * tox + core
                        ),
                        functools.partial(peer_copy, theirs, theirs, *sems, place, 2 * fromx + core),
                    )

    for sends, _, _, _, out, _ in fold_parts():
        launch(sends, out)
    for t in range(1, nx):
        tox = lax.rem(x + t, nx)

        def send_skip(t=t, tox=tox):
            return peer_copy(
                k_.sgb.at[tox], k_.sgi.at[x], k_.o_send.at[2, t], k_.o_recv.at[2, t], place, 2 * tox + core
            )

        launch(None, send_skip)

    acc[0, 0 : dm.g, 0:columns] = jnp.zeros((dm.g, columns), F32)

    def gate_weight(d, carry):
        v = jnp.concatenate(
            [
                jnp.concatenate([d1[1 + d, 1 + j, 0 : dm.enc_all] for j in range(RB)], 1),
                jnp.concatenate([flat(xs, 1 + d, 1 + j) for j in range(RB)], 1),
            ],
            0,
        )
        y = jnp.concatenate([k_.pg[d * RB + j] for j in range(RB)], 1)
        acc[0, 0 : dm.g, 0:columns] += dot_nt(y, v)
        return carry

    lax.fori_loop(0, S, gate_weight, 0)
    lane = iota((dm.g, LANES), 1)
    vectors = jnp.where(
        lane == 0,
        jnp.sum(bias, axis=1, keepdims=True),
        jnp.where(lane == 1, jnp.sum(psi, axis=1, keepdims=True), 0.0),
    )
    gate_block = k_.gate_block
    for j in range(nc):
        mine = slice(j * gq, (j + 1) * gq)
        gate_block[j, :, 0:columns] = acc[0, mine, 0:columns]
        gate_block[j, :, columns : 2 * LANES] = jnp.zeros((gq, 2 * LANES - columns), F32)
        gate_block[j, :, 2 * LANES :] = vectors[mine]
    sum_start(everyone, k_.sv, 4, 0, gate_block[me], lambda chan: gate_block.at[chan])
    cg[...] = k_.fm[x]
    for _, gets, fromx, part, _, back in fold_parts():

        def fold_in(back=back, part=part, fromx=fromx):
            back().wait_recv()
            cg[...] += k_.fr[part, fromx].astype(F32)

        guarded(gets, fold_in)

    coarse_sums(2, norm_back_sums(k_.z2, keep_du(k_.du_c), stats_e2, norm_e2, lambda p: cg[p], Q))
    cross_finish(2)
    weights_finish(1)
    total_e2 = coarse_totals(2)
    norm_back_coarse(k_.z2, back_factors(stats_e2, norm_e2, total_e2, dm.coarse_total), k_.xz2)
    gather_start(k_.xz2, "dz2")
    weight_grad_coarse(k_.xh, 1)
    reduce_finish(3)
    gather_pass(k_.xz2, "dz2")
    reduce_start(1)
    weights_finish(0)
    drain()
    gather_wait(k_.xz2, "dz2")
    for i, v in enumerate(conv_coarse(k_.xz2, wb[1], dm.ce)):
        cg[i] = v
    coarse_sums(3, norm_back_sums(k_.z1, keep_du(k_.du_c), stats_e1, norm_e1, lambda p: cg[p], Q))
    reduce_finish(2)
    total_e1 = coarse_totals(3)
    norm_back_coarse(k_.z1, back_factors(stats_e1, norm_e1, total_e1, dm.coarse_total), k_.xz1)
    gather_start(k_.xz1, "dz1")
    weight_grad_coarse(xp, 0)
    reduce_start(0)
    reduce_finish(1)
    gather_pass(k_.xz1, "dz1")
    gradient_out(3)

    def rows_out(ref, own, theirs, kind, size):
        def copy_rows(read, at):
            def body(d, carry):
                for r in range(RB):
                    p = (d * R + at * RB + r) * size
                    ref[pl.ds(pl.multiple_of(p, size), size)] = read(d * RB + r).astype(F32)
                return carry

            lax.fori_loop(0, S, body, 0)

        copy_rows(lambda p: own[x, p], x)
        for t in range(1, nx):
            fromx = lax.rem(x + nx - t, nx)
            block = theirs.at[fromx]
            peer_copy(block, block, k_.o_send.at[kind, t], k_.o_recv.at[kind, t], place, 2 * fromx + core).wait_recv()
            copy_rows(lambda p, fromx=fromx: theirs[fromx, p], fromx)

    rows_out(k_.out, k_.ob, k_.oi, 1, dm.cd)
    rows_out(k_.sg, k_.sgp, k_.sgi, 2, dm.cs)
    gather_wait(k_.xz1, "dz1")
    for i, v in enumerate(conv_coarse(k_.xz1, wb[0], dm.cs)):
        v = dot(split(v), spread2) * 0.125
        for j in range(4):
            part = v[:, (j // 2) * LANES : (j // 2 + 1) * LANES]
            for d in range(S):
                at = (d * R + 4 * i + j) * dm.cs
                k_.sg[at : at + dm.cs] += part
    reduce_finish(0)
    gradient_out(2)
    gradient_out(1)
    gate_total = sum_finish(everyone, k_.sv, 4, 0)
    k_.ggate[...] = gate_total[:, 0:columns]
    k_.gvector[0:1] = row_of(gate_total[:, 2 * LANES : 2 * LANES + 1])
    k_.gvector[1:2] = row_of(gate_total[:, 2 * LANES + 1 : 2 * LANES + 2])

    def own_part(col):
        parts = [jnp.where(x == i, col[i * dm.cd : (i + 1) * dm.cd], 0.0) for i in range(nx)]
        return functools.reduce(jnp.add, parts)

    for ref, pair, pick in ((k_.gen, (total_e1, total_e2), lambda v: v), (k_.gdn, (total_d1, total_d2), own_part)):
        for layer, total in enumerate(pair):
            ref[0, layer : layer + 1] = row_of(pick(total[1]))
            ref[1, layer : layer + 1] = row_of(pick(total[0]))
    gradient_out(0)
    drain()


def adamw(weight, grad, moment, square, rate):
    new_moment = 0.9 * moment + 0.1 * grad
    new_square = 0.999 * square + 0.001 * grad * grad
    moment_hat = new_moment / (1.0 - 0.9**STEP)
    square_hat = new_square / (1.0 - 0.999**STEP)
    new_weight = weight - rate * (moment_hat / (jnp.sqrt(square_hat) + 1e-08) + 0.01 * weight)
    return (new_weight, new_moment, new_square)


RATES = (CONV_RATE, CONV_RATE, GATE_RATE, VECTOR_RATE, CONV_RATE, CONV_RATE, VECTOR_RATE, VECTOR_RATE)


def update_kernel(*refs):
    n = len(RATES)
    sources, targets = refs[: 2 + 4 * n], refs[2 + 4 * n : 4 + 7 * n]
    inside, outside = refs[4 + 7 * n : 6 + 11 * n], refs[6 + 11 * n : 8 + 14 * n]
    in_sem, out_sem = refs[8 + 14 * n :]
    order = (4, 1, 0, 5, 2, 3, 6, 7)

    def load(i):
        return pltpu.make_async_copy(sources[i], inside[i], in_sem.at[i])

    def store(i):
        return pltpu.make_async_copy(outside[i], targets[i], out_sem.at[i])

    for i in (1, 0):
        load(i).start()
    for k in order:
        for part in range(4):
            load(2 + part * n + k).start()
    for i in (1, 0):
        load(i).wait()
        chans, (slabs, rows) = outside[i].shape[0], outside[i].shape[1:3]
        for c in range(chans):
            v = inside[i][pl.ds(c, slabs * rows, stride=chans)]
            outside[i][c] = v.reshape(slabs, rows, LANES).astype(outside[i].dtype)
        store(i).start()
    for k in order:
        own = [2 + part * n + k for part in range(4)]
        for i in own:
            load(i).wait()
        rows = inside[own[0]].shape[0]
        step = 8 if rows % 8 == 0 and rows > 8 else rows
        for r in range(0, rows, step):
            at = slice(r, r + step)
            new = adamw(*(inside[i][at] for i in own), RATES[k])
            for part, value in enumerate(new):
                outside[2 + 3 * k + part][at] = value
        for part in range(3):
            store(2 + 3 * k + part).start()
    for i in range(len(targets)):
        store(i).wait()


def per_device(
    skip, cotangent, enc_conv1, enc_conv2, gate_proj, gate_vector, dec_conv1, dec_conv2, enc_norms, dec_norms, *states
):
    nd, nc = lax.axis_size("depth"), lax.axis_size("chan")
    dm = Dims(nd, nc, skip.shape, enc_conv1.shape[0], dec_conv1.shape[0], gate_proj.shape[0] * nc)
    S, R, H, nx, RB, E = dm.s, dm.rows, dm.half, dm.nx, dm.rb, dm.ext
    Q = H // 2
    cin3 = dm.enc_all + dm.skip_all

    def own_block(size):
        return (size, lambda j: pl.multiple_of(j * size, size), 0)

    def core_blocks(size):
        return tuple(
            (size, lambda j, i=i: pl.multiple_of((2 * i + lax.rem(j, 2)) * size, size), i * size) for i in range(nx)
        )

    dm.convs = convs = (
        Conv(dm, dm.ce, dm.skip_all, (own_block(dm.cs),)),
        Conv(dm, dm.ce, dm.enc_all, (own_block(dm.ce),)),
        Conv(dm, dm.cd, cin3, core_blocks(dm.ce) + ((dm.skip_all, lambda j: dm.enc_all, nx * dm.ce),)),
        Conv(dm, dm.cd, dm.dec_all, core_blocks(dm.cd)),
    )
    params = (enc_conv1, enc_conv2, gate_proj, gate_vector, dec_conv1, dec_conv2, enc_norms, dec_norms)
    inputs = dict(
        skip=skip, cot=cotangent, w0=enc_conv1, w1=enc_conv2, w2=dec_conv1, w3=dec_conv2,
        gate=gate_proj, vector=gate_vector, en=enc_norms, dn=dec_norms,
    )
    shape = jax.ShapeDtypeStruct
    outs = dict(
        out=shape((S * R * dm.cd, LANES), F32),
        sg=shape((S * R * dm.cs, LANES), F32),
        **{f"g{i}": shape(a.shape, F32) for i, a in enumerate((enc_conv1, enc_conv2, dec_conv1, dec_conv2))},
        **{
            name: shape(a.shape, F32)
            for name, a in (("ggate", gate_proj), ("gvector", gate_vector), ("gen", enc_norms), ("gdn", dec_norms))
        },
    )
    gq = dm.g // nc

    def coarse(block):
        return pltpu.VMEM((2, nx, 3, Q, block, LANES), storage(block))

    def fine():
        return pltpu.VMEM((2, S + 2, E, dm.cf, LANES), storage(dm.cd))

    def f32(*dims):
        return pltpu.VMEM((*dims, LANES), F32)

    def tiles(*dims):
        return pltpu.VMEM((*dims, 16, LANES), BF16)

    def blocks(block, *dims):
        return pltpu.VMEM((*dims, block, LANES), storage(block))

    def sems(*dims):
        return pltpu.SemaphoreType.DMA(dims)

    scratch = dict(
        xp=coarse(dm.cs), xh=coarse(dm.ce), xc=coarse(dm.ce), xz2=coarse(dm.ce), xz1=coarse(dm.ce),
        own_skip=blocks(dm.cs, S, R + 2), xs=blocks(dm.cs, 2, nx, S + 2, E),
        own_cot=blocks(dm.cd, S, R), cots=blocks(dm.cd, nx, S, RB),
        d1=pltpu.VMEM((S + 2, E, cin3, LANES), BF16), xd=fine(), xz4=fine(), xz3=fine(),
        z1=f32(Q, dm.ce), z2=f32(Q, dm.ce), z3=f32(S * RB, dm.cf), z4=f32(S * RB, dm.cf),
        du_c=f32(Q, dm.ce), du_f=f32(S * RB, dm.cf), gg=f32(S * RB, dm.cf), cg=f32(Q, dm.ce),
        pre=f32(S + 2, E, dm.g), alpha=f32(S + 2, E, 1), pg=pltpu.VMEM((S * RB, dm.g, LANES), BF16),
        ug=f32(S, RB + 6, nx * dm.ce), cb=f32(S, H + 2, nx * dm.ce), dt=f32(S + 2, H, dm.enc_all),
        gv=f32(nc, dm.cs), sgp=f32(nx, S * RB, dm.cs), sgb=blocks(dm.cs, nx, S * RB), sgi=blocks(dm.cs, nx, S * RB),
        ob=blocks(dm.cd, nx, S * RB), oi=blocks(dm.cd, nx, S * RB),
        dzf=pltpu.VMEM((3, S, RB + 4, dm.cf, LANES), storage(dm.cd)),
        dzc=pltpu.VMEM((9, Q, dm.ce, LANES), BF16),
        fs=blocks(dm.ce, 3, nx, Q), fr=blocks(dm.ce, 3, nx, Q), fm=f32(nx, Q, dm.ce),
        st=f32(4, nd, 1), su=f32(4, nd * nx, 1), sv=pltpu.VMEM((1, nd * nx, gq, 3 * LANES), F32),
        norm_all=f32(nc, 8), rows=f32(max(dm.cs, dm.cd) * S * R),
        turned=f32(max(cv.chunks for cv in convs) * LANES),
        acc=pltpu.VMEM((nx, max(3 * cv.c for cv in convs), max(cv.wide for cv in convs)), F32),
        gate_all=pltpu.VMEM((nc, gq, 3 * LANES), F32), gate_t=pltpu.VMEM((2 * LANES, dm.g), F32),
        gate_own=pltpu.VMEM((nx * (dm.ce + dm.cs), dm.g), F32), gate_block=pltpu.VMEM((nc, gq, 3 * LANES), F32),
        **{f"wt{i}": pltpu.VMEM((3, cv.c, cv.wide), cv.kind) for i, cv in enumerate(convs)},
        **{
            f"wf{i}": pltpu.VMEM((cv.taps, 3 * cv.c) if i < 2 else (nx, cv.stored, 9 * cv.c), BF16)
            for i, cv in enumerate(convs)
        },
        **{f"wx{i}": pltpu.VMEM((nc, 3, cv.needed, cv.wide), cv.kind) for i, cv in enumerate(convs)},
        **{
            f"wb{i}": pltpu.VMEM((9 * cv.needed, 3 * nc * cv.o) if i < 2 else (3 * cv.needed, 9 * nc * cv.o), BF16)
            for i, cv in enumerate(convs)
        },
        flip=pltpu.VMEM((max(cv.tiles for cv in convs[2:]) * LANES, max(3 * cv.c for cv in convs[2:])), F32),
        **{f"gt{i}": tiles(cv.share * nd) for i, cv in enumerate(convs)},
        **{f"gr{i}": tiles(nd, cv.share) for i, cv in enumerate(convs)},
        **{f"ga{i}": tiles(cv.share * nd) for i, cv in enumerate(convs)},
        **{f"gs{i}": tiles(nx, convs[i].count) for i in (2, 3)},
        **{f"gx{i}": tiles(nx, convs[i].count) for i in (2, 3)},
        g_send=sems(len(GATHERS), 3, nx), g_recv=sems(len(GATHERS), 3),
        h_send=sems(len(GATHERS), 2 + nx), h_recv=sems(len(GATHERS)),
        x_send=sems(len(FINE), 3, 5), x_recv=sems(len(FINE), 3, 5),
        y_send=sems(len(FINE), 3), y_recv=sems(len(FINE), 3),
        t_send=sems(4), t_recv=sems(4), u_send=sems(5), u_recv=sems(5),
        f_send=sems(3, nx), f_recv=sems(3, nx), w_send=sems(4, nx + 1, nc), w_recv=sems(4, nx + 1, nc),
        p_send=sems(2, nx), p_recv=sems(2, nx), c_send=sems(2, nx), c_recv=sems(2, nx),
        o_send=sems(3, nx), o_recv=sems(3, nx), v_send=sems(2, nc), v_recv=sems(2, nc),
        r_send=sems(4), r_recv=sems(4), a_send=sems(4), a_recv=sems(4),
    )
    vmem = pl.BlockSpec(memory_space=pltpu.VMEM)
    out, sg, grad1, grad2, grad3, grad4, ggate, gvector, gen, gdn = pl.pallas_call(
        functools.partial(kernel, dm, (*inputs, *outs, *scratch)),
        out_shape=tuple(outs.values()),
        in_specs=[vmem] * len(inputs),
        out_specs=[vmem] * len(outs),
        scratch_shapes=list(scratch.values()),
        compiler_params=pltpu.CompilerParams(
            has_side_effects=True, collective_id=0, vmem_limit_bytes=60 * 1024 * 1024
        ),
        name="step",
    )(*inputs.values())
    grads = (grad1, grad2, ggate, gvector, grad3, grad4, gen, gdn)
    operands = (out, sg, *params, *grads, *states)
    updated = (
        shape(cotangent.shape, BF16),
        shape(skip.shape, F32),
        *(shape(p.shape, F32) for p in params for _ in range(3)),
    )
    anywhere = pl.BlockSpec(memory_space=pl.ANY)
    return pl.pallas_call(
        update_kernel,
        out_shape=updated,
        in_specs=[anywhere] * len(operands),
        out_specs=[anywhere] * len(updated),
        scratch_shapes=[
            *(pltpu.VMEM(a.shape, a.dtype) for a in operands),
            *(pltpu.VMEM(a.shape, a.dtype) for a in updated),
            pltpu.SemaphoreType.DMA((len(operands),)),
            pltpu.SemaphoreType.DMA((len(updated),)),
        ],
        compiler_params=pltpu.CompilerParams(vmem_limit_bytes=60 * 1024 * 1024),
        name="update",
    )(*operands)


def solution(mesh):
    volume = P("chan", "depth", None, None)
    row, column, norms = P("chan", None), P(None, "chan"), P(None, None, "chan")
    params = (row, row, row, column, row, row, norms, norms)
    return jax.shard_map(
        per_device,
        mesh=mesh,
        in_specs=(volume, volume) + params * 3,
        out_specs=(volume, volume) + tuple(spec for spec in params for _ in range(3)),
        check_vma=False,
    )
```

```python
import functools
import types

import jax
import jax.numpy as jnp
from jax import lax
from jax.experimental import pallas as pl
from jax.experimental.pallas import tpu as pltpu
from jax.sharding import PartitionSpec as P

STEP = 5
EPS = 1e-05
CONV_RATE = 0.03
GATE_RATE = 0.1
VECTOR_RATE = 0.5
LANES = 128
MESH = pl.DeviceIdType.MESH
F32 = jnp.float32
BF16 = jnp.bfloat16


def iota(shape, dim):
    return lax.broadcasted_iota(jnp.int32, shape, dim)


def dot(a, b):
    return jnp.dot(a, b, preferred_element_type=F32)


def dot_nt(a, b):
    return lax.dot_general(a, b, (((1,), (1,)), ((), ())), preferred_element_type=F32)


def dot_tn(a, b):
    return lax.dot_general(a, b, (((0,), (0,)), ((), ())), preferred_element_type=F32)


def from_left(v, width):
    return jnp.where(iota(v.shape, 1) % width == 0, 0.0, pltpu.roll(v, 1, 1))


def from_right(v, width):
    return jnp.where(iota(v.shape, 1) % width == width - 1, 0.0, pltpu.roll(v, LANES - 1, 1))


def halves(low, high):
    return pltpu.roll(jnp.where(iota(low.shape, 1) < LANES // 2, low, high), LANES // 2, 1)


def split(v):
    high = v.astype(BF16)
    return jnp.concatenate([high, (v - high.astype(F32)).astype(BF16)], 1)


def storage(block):
    return BF16 if block % 16 == 0 else F32


def flat(ref, s, r):
    if len(ref.shape) == 4:
        return ref[s, r]
    v = ref[:, :, s, r]
    return jnp.concatenate([v[c, i] for i in range(v.shape[1]) for c in range(2)], 0).astype(BF16)


class Dims:
    def __init__(self, nd, nc, skip, enc, dec, gate):
        self.nd, self.nc, self.nx = nd, nc, nc // 2
        self.s, self.rows, self.cols = skip[1:]
        self.cs, self.ce, self.cd, self.g = skip[0], enc, dec, gate
        self.half, self.hcols = self.rows // 2, self.cols // 2
        self.fine_total = nd * self.s * self.rows * self.cols
        self.coarse_total = self.fine_total // 8
        self.enc_all = nc * enc
        self.skip_all = nc * skip[0]
        self.dec_all = nc * dec
        self.rb = self.rows // self.nx
        self.ext = self.rb + 2
        self.cf = self.nx * dec


GATHERS = ("pooled", "skip", "hidden", "coarse", "dz2", "dz1")
FINE = ("hidden", "dz4", "dz3")


class Conv:
    def __init__(self, dm, o, c, blocks):
        self.o, self.c, self.blocks = o, c, blocks
        self.length = 27 * c
        self.chunks = -(-self.length // LANES)
        self.per = LANES // o
        self.tiles = -(-9 // self.per)
        self.wide = self.tiles * LANES
        self.kind = storage(min(size for size, _, _ in blocks))
        self.needed = sum(size for size, _, _ in blocks)
        self.count = 3 * c // 16 * 3
        self.share = -(-self.count // dm.nd)
        self.taps = 9 * o
        self.stored = -(-3 * o // 16) * 16


def kernel(dm, names, *refs):
    k_ = types.SimpleNamespace(**dict(zip(names, refs)))
    nd, nc, nx, S, R, H = dm.nd, dm.nc, dm.nx, dm.s, dm.rows, dm.half
    W, V = dm.cols, dm.hcols
    Q, RB, E = H // 2, dm.rb, dm.ext
    place = lax.axis_index("depth")
    me = lax.axis_index("chan")
    x, core = lax.div(me, 2), lax.rem(me, 2)
    other = 1 - core
    mate = 2 * x + other
    row0, h0 = x * RB, x * (RB // 2)
    first, last = place == 0, place == nd - 1
    top, bottom = x == 0, x == nx - 1
    convs = dm.convs
    pending = []
    wt, wf, wx, wb = ([getattr(k_, f"{kind}{i}") for i in range(4)] for kind in ("wt", "wf", "wx", "wb"))
    gt, gr, ga = ([getattr(k_, f"{kind}{i}") for i in range(4)] for kind in ("gt", "gr", "ga"))
    weights = (k_.w0, k_.w1, k_.w2, k_.w3)
    grads = (k_.g0, k_.g1, k_.g2, k_.g3)
    turned, acc = k_.turned, k_.acc

    def no(cond):
        return jnp.logical_not(cond)

    def peer_copy(src, dst, send, recv, depth, chan):
        return pltpu.make_async_remote_copy(
            src_ref=src, dst_ref=dst, send_sem=send, recv_sem=recv,
            device_id={"depth": depth, "chan": chan}, device_id_type=MESH,
        )

    def guarded(cond, fn):
        if cond is None:
            fn()
        else:
            pl.when(cond)(fn)

    def drain():
        for cond, fn in pending:
            guarded(cond, fn)
        pending.clear()

    def launch(cond, copy):
        guarded(cond, lambda: copy().start())
        pending.append((cond, lambda: copy().wait_send()))

    def arrive(cond, copy):
        guarded(cond, lambda: copy().wait_recv())

    def both(a, b):
        return b if a is None else a if b is None else jnp.logical_and(a, b)

    can_send = (no(last), None, no(first))
    can_recv = (no(first), None, no(last))

    def slices(side, n):
        return (pl.ds(n, 1), pl.ds(1, n), pl.ds(1, 1))[side], (pl.ds(0, 1), pl.ds(1, n), pl.ds(n + 1, 1))[side]

    def at_x(t):
        up, down = x + t, x - t
        return jnp.where(up >= nx, up - nx, up), jnp.where(down < 0, down + nx, down)


    def gather_start(ref, which, source_at=None):
        n = ref.shape[2] - 2
        k = GATHERS.index(which)
        for side in (0, 2, 1):
            own, theirs = slices(side, n)
            for t in range(nx):
                if side == 1 and t == 0:
                    continue
                tox = at_x(t)[0]

                def copy(side=side, t=t, own=own, theirs=theirs, tox=tox):
                    start = (n, 1, 1)[side] - 1
                    size = (1, n, 1)[side]
                    src = ref.at[core, x, own] if source_at is None else source_at(pl.ds(start, size), tox)
                    return peer_copy(
                        src, ref.at[core, x, theirs], k_.g_send.at[k, side, t], k_.g_recv.at[k, side],
                        place + 1 - side, 2 * tox + core,
                    )

                launch(can_send[side], copy)
        gather_own(ref, which)

    def handed(ref, k, piece, i):
        return peer_copy(piece, piece, k_.h_send.at[k, i], k_.h_recv.at[k], place, mate)

    def gather_own(ref, which):
        k = GATHERS.index(which)
        launch(None, lambda: handed(ref, k, ref.at[core, x, pl.ds(1, ref.shape[2] - 2)], 0))

    def gather_pass(ref, which):
        n = ref.shape[2] - 2
        k = GATHERS.index(which)
        for side in (1, 0, 2):
            theirs = slices(side, n)[1]
            if side != 1:
                pieces = [ref.at[core, :, theirs]]
            else:
                pieces = [ref.at[core, at_x(t)[1], theirs] for t in range(1, nx)]
            for i, got in enumerate(pieces):
                arrive(
                    can_recv[side],
                    lambda got=got, side=side: peer_copy(
                        got, got, k_.g_send.at[k, side, 0], k_.g_recv.at[k, side], place, mate
                    ),
                )
                launch(None, lambda got=got, i=i, side=side: handed(ref, k, got, 1 + (side // 2 if side != 1 else 2 + i)))

    def gather_wait(ref, which):
        handed(ref, GATHERS.index(which), ref.at[other], 0).wait_recv()

    def fine_parts(ref, which, side):
        k = FINE.index(which)
        own, theirs = slices(side, S)
        inner = pl.ds(1, RB)
        rows = [(None, None, inner, inner, x, core, core)] if side != 1 else [(None, None, inner, inner, x, other, other)]
        if nx > 1:
            for c in range(2):
                rows.append((no(top), no(bottom), pl.ds(1, 1), pl.ds(E - 1, 1), x - 1, c, c))
                rows.append((no(bottom), no(top), pl.ds(RB, 1), pl.ds(0, 1), x + 1, c, c))
        parts = []
        for i, (sends, gets, row, at, tox, to, source) in enumerate(rows):
            target = ref.at[core, theirs, at]
            theirs_ = ref.at[source, theirs, at]
            up = (i - 1) % 2
            arrived = 0 if i == 0 else 1 + up * 2 + core
            expected = 0 if i == 0 else 1 + up * 2 + source
            send = k_.x_send.at[k, side, i]
            parts.append((
                both(can_send[side], sends), both(can_recv[side], gets),
                functools.partial(
                    peer_copy, ref.at[core, own, row], target, send, k_.x_recv.at[k, side, arrived],
                    place + 1 - side, 2 * tox + to,
                ),
                functools.partial(peer_copy, theirs_, theirs_, send, k_.x_recv.at[k, side, expected], place, mate),
            ))
        return parts

    def fine_start(ref, which):
        for side in (0, 2, 1):
            for sends, _, out, _ in fine_parts(ref, which, side):
                launch(sends, out)

    def fine_halo(ref, which, side, c):
        k = FINE.index(which)
        block = ref.at[c, slices(side, S)[1], pl.ds(1, RB)]
        return peer_copy(block, block, k_.y_send.at[k, side], k_.y_recv.at[k, side], place, mate)

    def fine_pass(ref, which):
        for side in (0, 2):
            _, gets, _, back = fine_parts(ref, which, side)[0]
            arrive(gets, back)
            launch(gets, functools.partial(fine_halo, ref, which, side, core))

    def fine_wait(ref, which):
        for side in (1, 0, 2):
            for _, gets, _, back in fine_parts(ref, which, side)[side != 1 :]:
                arrive(gets, back)
            if side != 1:
                arrive(can_recv[side], functools.partial(fine_halo, ref, which, side, other))

    def natural(ref, s, r):
        v = ref[:, s, r]
        size = dm.cd
        return jnp.concatenate(
            [v[c, i * size : (i + 1) * size] for i in range(nx) for c in range(2)], 0
        ).astype(BF16)

    def in_turn(count, fn):
        if count <= 16:
            for i in range(count):
                fn(i)
        else:

            def body(i, carry):
                fn(i)
                return carry

            lax.fori_loop(0, count, body, 0)

    def slab_peers(i):
        to = place + 1 + i
        return jnp.where(to >= nd, to - nd, to), me

    def wide_peers(i):
        i = i + 1
        dt, xt = (i // nx, i % nx) if isinstance(i, int) else (lax.div(i, nx), lax.rem(i, nx))
        to, tox = place + dt, x + xt
        return jnp.where(to >= nd, to - nd, to), 2 * jnp.where(tox >= nx, tox - nx, tox) + core

    def exchange(n, peers, copy):
        in_turn(n - 1, lambda i: copy(*peers(i)).start())

    def sum_start(group, ref, k, slot, tile, source=None):
        n, own, peers, send, recv = group
        ref[slot, own] = tile

        def copy(depth, chan):
            src = ref.at[slot, own] if source is None else source(chan)
            return peer_copy(src, ref.at[slot, own], send.at[k], recv.at[k], depth, chan)

        exchange(n, peers, copy)
        pending.append((None, lambda: all_of(group, ref, k, slot).wait_send()))

    def all_of(group, ref, k, slot):
        n, _, _, send, recv = group
        every = ref.at[slot, pl.ds(0, n - 1)]
        return peer_copy(every, every, send.at[k], recv.at[k], place, mate)

    def sum_finish(group, ref, k, slot):
        all_of(group, ref, k, slot).wait_recv()
        return jnp.sum(ref[slot], axis=0)

    slabs = (nd, place, slab_peers, k_.t_send, k_.t_recv)
    everyone = (nd * nx, place * nx + x, wide_peers, k_.u_send, k_.u_recv)

    def columns_of(row, m):
        lane, channel = iota((m, LANES), 1), iota((m, LANES), 0)
        return tuple(
            jnp.sum(jnp.where(lane == channel + i * m, row, 0.0), axis=1, keepdims=True) for i in range(2)
        )

    def coarse_sums(slot, sums):
        sum_start(slabs, k_.st, slot, slot, pack(*sums))

    def coarse_totals(slot):
        return columns_of(sum_finish(slabs, k_.st, slot, slot), dm.ce)

    def fine_sums(slot, sums):
        sum_start(everyone, k_.su, slot, slot, pack(*sums))

    def fine_totals(slot):
        return columns_of(sum_finish(everyone, k_.su, slot, slot), dm.cf)

    def prepare(k):
        cv, w, own = convs[k], weights[k], wt[k]
        out = wf[k] if k < 2 else wf[k].at[x]
        repeat = (iota((cv.o, LANES), 1) % cv.o == iota((cv.o, LANES), 0)).astype(BF16)
        step = 8 * LANES
        for at in range(0, cv.length, step):
            end = min(at + step, cv.length)
            turned[at:end] = dot_tn(w[:, at:end].astype(BF16), repeat)
        group = iota((cv.c, LANES), 1) // cv.o
        for kz in range(3):
            for j in range(cv.tiles):
                tile = None
                for g in range(cv.per):
                    u = j * cv.per + g
                    if u < 9:
                        kx, ky = u // 3, u % 3
                        v = turned[pl.ds(9 * kz + 3 * ky + kx, cv.c, stride=27)]
                        tile = v if tile is None else jnp.where(group == g, v, tile)
                own[kz, :, j * LANES : (j + 1) * LANES] = tile.astype(BF16).astype(own.dtype)
        eye = (iota((LANES, LANES), 0) == iota((LANES, LANES), 1)).astype(BF16)
        for j in range(cv.tiles):
            v = jnp.concatenate([own[kz, :, j * LANES : (j + 1) * LANES] for kz in range(3)], 0)
            size = min(LANES, cv.taps - j * LANES)
            v = dot_nt(eye, v.astype(BF16))[0:size]
            if k < 2:
                out[j * LANES : j * LANES + size] = v.astype(BF16)
            else:
                k_.flip[j * LANES : j * LANES + size, 0 : 3 * cv.c] = v
        if k >= 2:
            out[0 : 3 * cv.o] = jnp.concatenate(
                [
                    jnp.concatenate(
                        [
                            k_.flip[(3 * kx + ky) * cv.o : (3 * kx + ky + 1) * cv.o, kz * cv.c : (kz + 1) * cv.c]
                            for kx in range(3)
                        ],
                        0,
                    )
                    for kz in range(3)
                    for ky in range(3)
                ],
                1,
            ).astype(BF16)

    def forward_copy(k, t):
        block = wf[k].at[x]
        return peer_copy(
            block, block, k_.p_send.at[k - 2, t], k_.p_recv.at[k - 2, t], place, 2 * lax.rem(x + t, nx) + core
        )

    def forward_start(k):
        for t in range(1, nx):
            launch(None, functools.partial(forward_copy, k, t))

    def forward_wait(k):
        for t in range(1, nx):
            fromx = lax.rem(x + nx - t, nx)
            block = wf[k].at[fromx]
            peer_copy(
                block, block, k_.p_send.at[k - 2, t], k_.p_recv.at[k - 2, t], place, 2 * fromx + core
            ).wait_recv()

    def forward_weight(k):
        return jnp.concatenate([wf[k][i, 0 : 3 * convs[k].o] for i in range(nx)], 0)

    def weights_start(k):
        cv = convs[k]
        for b, (size, start, at) in enumerate(cv.blocks):
            wx[k][me, :, at : at + size] = wt[k][:, pl.ds(start(me), size)]
            for t in range(1, nc):
                to = lax.rem(me + t, nc)

                def copy(to=to, t=t, b=b, size=size, start=start, at=at):
                    return peer_copy(
                        wt[k].at[:, pl.ds(start(to), size)], wx[k].at[me, :, pl.ds(at, size)],
                        k_.w_send.at[k, b, t], k_.w_recv.at[k, b, t], place, to,
                    )

                launch(None, copy)

    def weights_finish(k):
        cv = convs[k]
        for b, (size, _, at) in enumerate(cv.blocks):
            for t in range(1, nc):
                source = lax.rem(me + nc - t, nc)
                theirs = wx[k].at[source, :, pl.ds(at, size)]
                peer_copy(theirs, theirs, k_.w_send.at[k, b, t], k_.w_recv.at[k, b, t], place, source).wait_recv()

        parts = 9 if k < 2 else 3
        lanes = cv.taps // parts
        for i in range(parts):
            at = (parts - 1 - i) * lanes
            found = [wx[k][j, 2 - kz, :, at : at + lanes].astype(F32) for kz in range(3) for j in range(nc)]
            wb[k][i * cv.needed : (i + 1) * cv.needed] = jnp.concatenate(found, 1).astype(BF16)

    def tiles_of(k, put):
        def tile(i, carry):
            at = pl.multiple_of(i * 16, 16)
            for j in range(3):
                put(3 * i + j, acc[pl.ds(at, 16), j * LANES : (j + 1) * LANES].astype(BF16))
            return carry

        lax.fori_loop(0, convs[k].c // 16 * 3, tile, 0, unroll=4)

    def cross_start(k):
        gs, gx = (k_.gs2, k_.gs3)[k - 2], (k_.gx2, k_.gx3)[k - 2]

        def put(i, v):
            gs[i] = v

        tiles_of(k, put)
        for t in range(1, nx):

            def copy(t=t):
                return peer_copy(
                    gs, gx.at[x], k_.c_send.at[k - 2, t], k_.c_recv.at[k - 2, t], place, 2 * at_x(t)[0] + core
                )

            launch(None, copy)

    def cross_finish(k):
        cv, gs, gx = convs[k], (k_.gs2, k_.gs3)[k - 2], (k_.gx2, k_.gx3)[k - 2]
        sources = [at_x(t)[1] for t in range(1, nx)]
        for t, fromx in enumerate(sources, 1):
            theirs = gx.at[fromx]
            peer_copy(
                theirs, theirs, k_.c_send.at[k - 2, t], k_.c_recv.at[k - 2, t], place, 2 * fromx + core
            ).wait_recv()

        def add(i, carry):
            for j in range(9):
                p = 9 * i + j
                v = gs[p].astype(F32)
                for fromx in sources:
                    v += gx[fromx, p].astype(F32)
                gt[k][p] = v.astype(BF16)
            return carry

        lax.fori_loop(0, cv.count // 9, add, 0, unroll=2)
        reduce_send(k)

    def reduce_start(k):
        def put(i, v):
            gt[k][i] = v

        tiles_of(k, put)
        reduce_send(k)

    def reduce_send(k):
        cv = convs[k]
        for i in range(cv.count, cv.share * nd):
            gt[k][i] = jnp.zeros((16, LANES), BF16)
        gr[k][place] = gt[k][pl.ds(place * cv.share, cv.share)]

        def copy(to, chan):
            return peer_copy(
                gt[k].at[pl.ds(to * cv.share, cv.share)], gr[k].at[place], k_.r_send.at[k], k_.r_recv.at[k], to, chan
            )

        exchange(nd, slab_peers, copy)
        pending.append((None, lambda: reduce_all(k).wait_send()))

    def reduce_all(k):
        every = gr[k].at[pl.ds(0, nd - 1)]
        return peer_copy(every, every, k_.r_send.at[k], k_.r_recv.at[k], place, mate)

    def share_all(k):
        every = ga[k].at[pl.ds(0, (nd - 1) * convs[k].share)]
        return peer_copy(every, every, k_.a_send.at[k], k_.a_recv.at[k], place, mate)

    def reduce_finish(k):
        cv = convs[k]
        reduce_all(k).wait_recv()
        own = pl.ds(place * cv.share, cv.share)
        ga[k][own] = jnp.sum(gr[k][...].astype(F32), axis=0).astype(BF16)

        def copy(to, chan):
            return peer_copy(ga[k].at[own], ga[k].at[own], k_.a_send.at[k], k_.a_recv.at[k], to, chan)

        exchange(nd, slab_peers, copy)
        pending.append((None, lambda: share_all(k).wait_send()))

    def gradient_out(k):
        cv, out = convs[k], grads[k]
        share_all(k).wait_recv()
        group = iota((16, LANES), 1) // cv.o - (3 * x if k >= 2 else 0)

        def scatter(i, carry):
            for kz in range(3):
                for ky in range(3):
                    v = ga[k][(kz * (cv.c // 16) + i) * 3 + ky].astype(F32)
                    for kx in range(3):
                        at = 9 * kz + 3 * ky + kx + i * (16 * 27)
                        turned[pl.ds(at, 16, stride=27)] = jnp.where(group == kx, v, 0.0)
            return carry

        lax.fori_loop(0, cv.c // 16, scatter, 0, unroll=2)

        pick = (iota((cv.o, LANES), 1) % cv.o == iota((cv.o, LANES), 0)).astype(BF16)
        step = 8 * LANES
        for at in range(0, cv.length, step):
            size = min(step, cv.length - at)
            v = dot_nt(pick, turned[at : at + -(-size // LANES) * LANES].astype(BF16))
            out[:, at : at + size] = v[:, 0:size]

    def column(row):
        n = row.shape[1]
        eye = iota((n, n), 0) == iota((n, n), 1)
        return jnp.sum(jnp.where(eye, row, 0.0), axis=1, keepdims=True)

    def row_of(col):
        n = col.shape[0]
        eye = iota((n, n), 0) == iota((n, n), 1)
        return jnp.sum(jnp.where(eye, col, 0.0), axis=0, keepdims=True)

    def clear_halos(ref):
        def clear(at):
            if len(ref.shape) == 5:
                for c in range(2):
                    ref[c, at] = jnp.zeros(ref.shape[2:], ref.dtype)
            else:
                for i in range(nx):
                    ref[core, i, at] = jnp.zeros(ref.shape[3:], ref.dtype)

        pl.when(first)(lambda: clear(0))
        pl.when(last)(lambda: clear(ref.shape[-4] - 1))

    def clear_rows(ref):
        def clear(at):
            for c in range(2):
                for i in range(S + 2):
                    ref[c, i, at] = jnp.zeros(ref.shape[3:], ref.dtype)

        pl.when(top)(lambda: clear(0))
        pl.when(bottom)(lambda: clear(E - 1))

    def conv(operand, weight, m, groups, emit, init):
        def body(d, carry):
            v = operand(d)
            y = dot(weight, v)
            results = []
            for j in range(RB):
                lanes = slice(j * LANES, (j + 1) * LANES)
                parts = []
                for g in range(groups):
                    a = [y[(3 * g + kx) * m : (3 * g + kx + 1) * m, lanes] for kx in range(3)]
                    parts.append(from_left(a[0], W) + a[1] + from_right(a[2], W))
                results.append(jnp.concatenate(parts, 0) if groups > 1 else parts[0])
            return emit(d, results, carry)

        return lax.fori_loop(0, S, body, init)

    def rows_of(row):
        return lambda d: jnp.concatenate(
            [jnp.concatenate([row(d + kz, ky + j) for j in range(RB)], 1) for kz in range(3) for ky in range(3)], 0
        )

    def blocks_of(ref):
        size = dm.cd
        return lambda d: jnp.concatenate(
            [
                jnp.concatenate([ref[c, d + kz, 2 - ky + j, i * size : (i + 1) * size] for j in range(RB)], 1)
                for kz in range(3)
                for i in range(nx)
                for c in range(2)
                for ky in range(3)
            ],
            0,
        ).astype(BF16)

    def conv_stats(row, weight, z):
        def emit(d, results, carry):
            total, square = carry
            for j, v in enumerate(results):
                z[d * RB + j] = v
                total, square = total + v, square + v * v
            return total, square

        blank = jnp.zeros((dm.cf, LANES), F32)
        return conv(rows_of(row), weight, dm.cd, nx, emit, (blank, blank))

    def weight_grad(row, k):
        cv = convs[k]

        def part(d):
            v = jnp.concatenate([jnp.concatenate([row(d + kz, j) for j in range(E)], 1) for kz in range(3)], 0)
            y = jnp.concatenate(
                [k_.dzt[d, (2 - ky) * LANES : (2 - ky + E) * LANES] for ky in range(3)], 1
            )
            return dot(v, y)

        acc[0 : 3 * cv.c] = part(0)

        def more(d, carry):
            acc[0 : 3 * cv.c] += part(d)
            return carry

        lax.fori_loop(1, S, more, 0)

    def conv_coarse(ref, weight, m):
        v = jnp.concatenate(
            [jnp.concatenate([flat(ref, kz, i) for i in range(Q)], 1) for kz in range(3)], 0
        )
        y = dot(weight[...], v)
        blank = jnp.zeros((m, LANES), F32)

        def shifted(ky, i):
            if not 0 <= i < Q:
                return blank
            a, b, c = (
                y[(3 * kx + ky) * m : (3 * kx + ky + 1) * m, i * LANES : (i + 1) * LANES] for kx in range(3)
            )
            return from_left(a, V) + b + from_right(c, V)

        before = [shifted(0, i) for i in range(-1, Q)]
        after = [shifted(2, i) for i in range(Q + 1)]
        return [
            shifted(1, i) + halves(before[i + 1] + after[i + 1], before[i] + after[i]) for i in range(Q)
        ]

    def conv_stats_coarse(ref, weight, z, m):
        total = square = jnp.zeros((m, LANES), F32)
        for i, v in enumerate(conv_coarse(ref, weight, m)):
            z[i] = v
            total, square = total + v, square + v * v
        return total, square

    def weight_grad_coarse(ref, k):
        cv = convs[k]
        v = jnp.concatenate(
            [jnp.concatenate([flat(ref, kz, i) for i in range(Q)], 1) for kz in range(3)], 0
        )
        y = jnp.concatenate([k_.dzct[(2 - ky) * V : (2 - ky) * V + Q * LANES] for ky in range(3)], 1)
        acc[0 : 3 * cv.c] = dot(v, y)

    def pack(a, b):
        m = a.shape[0]
        a = jnp.sum(a, axis=1, keepdims=True)
        b = jnp.sum(b, axis=1, keepdims=True)
        lane, channel = iota((m, LANES), 1), iota((m, LANES), 0)
        both = jnp.where(lane == channel, a, jnp.where(lane == channel + m, b, 0.0))
        return jnp.sum(both, axis=0, keepdims=True)

    def moments(total, count):
        mean = total[0] / count
        var = total[1] / count - mean * mean
        return mean, lax.rsqrt(var + EPS)

    def wide(column):
        return jnp.broadcast_to(column, (column.shape[0], LANES))

    def factors(stats, norm):
        mean, inv = stats
        gain, shift = norm
        return wide(mean), wide(gain * inv), wide(shift)

    def norm_rows(z, stats, norm, emit, n):
        mean, scale, shift = factors(stats, norm)

        def body(i, carry):
            for j in range(n):
                p = i * n + j
                u = (z[p] - mean) * scale + shift
                emit(p, u * jax.nn.sigmoid(u))
            return carry

        lax.fori_loop(0, z.shape[0] // n, body, 0)

    def norm_back_sums(z, keep_du, stats, norm, grad, n):
        mean, scale, shift = factors(stats, norm)
        inv = wide(stats[1])
        m = z.shape[1]

        def body(i, carry):
            a, b = carry
            for j in range(n):
                p = i * n + j
                centred = z[p] - mean
                u = centred * scale + shift
                sigma = jax.nn.sigmoid(u)
                v = grad(p) * sigma * (1.0 + u * (1.0 - sigma))
                keep_du(p, v)
                a, b = a + v, b + v * (centred * inv)
            return a, b

        blank = jnp.zeros((m, LANES), F32)
        return lax.fori_loop(0, z.shape[0] // n, body, (blank, blank))

    def back_factors(stats, norm, total, count):
        mean, inv = stats
        scale = norm[0] * inv
        return wide(mean), wide(scale), wide(-scale * total[0] / count), wide(-scale * inv * total[1] / count)

    def columns_first(copies, groups):
        size = copies[0].shape[0] // groups
        rows = [v[g * size : (g + 1) * size] for g in range(groups) for v in copies]
        used = 3 * groups * size
        if used < LANES:
            rows.append(jnp.zeros((LANES - used, LANES), F32))
        return jnp.transpose(jnp.concatenate(rows, 0)).astype(BF16)

    def norm_back_fine(z, given, ref):
        mean, scale, level, slope = given

        def body(i, carry):
            for j in range(2):
                p = 2 * i + j
                d = lax.div(p, RB)
                r = p - d * RB
                v = scale * k_.du_f[p] + level + slope * (z[p] - mean)
                low = v.astype(BF16)
                ref[core, 1 + d, 1 + r] = low.astype(ref.dtype)
                v = low.astype(F32)
                at = pl.ds(pl.multiple_of((2 + r) * LANES, LANES), LANES)
                k_.dzt[d, at] = columns_first((from_right(v, W), v, from_left(v, W)), nx)
            return carry

        lax.fori_loop(0, S * RB // 2, body, 0)

    def norm_back_coarse(z, given, ref):
        mean, scale, level, slope = given
        for i in range(Q):
            low = (scale * k_.du_c[i] + level + slope * (z[i] - mean)).astype(BF16)
            ref[core, x, 1, i] = low.astype(ref.dtype)
            v = low.astype(F32)
            k_.dzct[V + i * LANES : V + (i + 1) * LANES] = columns_first((from_right(v, V), v, from_left(v, V)), 1)

    def keep_du(ref):
        def store(p, v):
            ref[p] = v

        return store

    barrier = pltpu.get_barrier_semaphore()

    def greet(depth, chan):
        pl.semaphore_signal(barrier, inc=1, device_id={"depth": depth, "chan": chan}, device_id_type=MESH)

    exchange(nd * nx, wide_peers, lambda depth, chan: types.SimpleNamespace(start=lambda: greet(depth, chan)))
    for t in range(nx):
        to = 2 * at_x(t)[0] + other
        greet(place, to)
        if t > 0:
            pl.when(no(first))(lambda to=to: greet(place - 1, to))
            pl.when(no(last))(lambda to=to: greet(place + 1, to))

    hc = iota((LANES, LANES), 0)
    fc = iota((LANES, LANES), 1)
    half = LANES // 2

    def up_table(coarse, fine):
        base = fine // 2
        beside = jnp.clip(base + jnp.where(fine % 2 == 0, -1, 1), 0, V - 1)
        near = (coarse == base).astype(F32)
        far = (coarse == beside).astype(F32)
        return (0.75 * near + 0.25 * far).astype(BF16)

    pool = jnp.concatenate([(hc // 2 == fc - at).astype(BF16) for at in (0, half)], 0)
    spread = jnp.concatenate([(hc - at == fc // 2).astype(BF16) for at in (0, half)], 1)
    up = jnp.concatenate([up_table(hc - at, fc) for at in (0, half)], 1)
    down = jnp.concatenate([up_table(fc, hc)] * 2, 0)
    spread2 = jnp.concatenate([spread, spread], 0)

    def take_rows(ref):
        for c in range(ref.shape[0]):
            k_.rows[c * S * R : (c + 1) * S * R] = ref[c].astype(F32).reshape(S * R, LANES)

    def row_of_all(p, chans):
        return k_.rows[pl.ds(p, chans, stride=S * R)]

    xp, xs, own_skip = k_.xp, k_.xs, k_.own_skip
    clear_halos(xp)
    take_rows(k_.skip)
    for i in range(S):
        for r in (0, R + 1):
            own_skip[i, r] = jnp.zeros((dm.cs, LANES), own_skip.dtype)

    def take_skip(i, carry):
        parts = []
        for d in range(S):
            v = [row_of_all(d * R + 4 * i + j, dm.cs).astype(BF16) for j in range(4)]
            for j in range(4):
                own_skip[d, 1 + 4 * i + j] = v[j].astype(own_skip.dtype)
            parts += [jnp.concatenate([v[j], v[2 + j]], 1) for j in range(2)]
        v = dot(jnp.concatenate(parts, 0), pool).reshape(2 * S, dm.cs, LANES)
        xp[core, x, 1, i] = (jnp.sum(v, axis=0) * 0.125).astype(BF16).astype(xp.dtype)
        return carry

    lax.fori_loop(0, Q, take_skip, 0, unroll=3)
    beside = jnp.where(first, 0, 1) + jnp.where(last, 0, 1)
    pl.semaphore_wait(barrier, nd * nx - 1 + nx + (nx - 1) * beside)
    gather_start(xp, "pooled")
    clear_halos(xs)
    xs[core, x, 1 : S + 1] = own_skip[:, pl.ds(row0, E)]
    gather_start(xs, "skip", lambda at, tox: own_skip.at[at, pl.ds(tox * RB, E)])

    gq = dm.g // nc
    columns = dm.enc_all + dm.skip_all
    gate_all, norm_all = k_.gate_all, k_.norm_all
    gate_all[me, :, 0:columns] = k_.gate[...]
    lane = iota((gq, LANES), 1)
    gate_all[me, :, 2 * LANES :] = jnp.where(
        lane == 0, column(k_.vector[0:1]), jnp.where(lane == 1, column(k_.vector[1:2]), 0.0)
    )
    for layer in range(2):
        for part in range(2):
            at = 2 * layer + part
            norm_all[me, at : at + 1, 0 : dm.cd] = k_.dn[part, layer : layer + 1]

    def constants(i, t, source, to):
        ref = (norm_all, gate_all)[i]
        return peer_copy(ref.at[source], ref.at[source], k_.v_send.at[i, t], k_.v_recv.at[i, t], place, to)

    for i in range(2):
        for t in range(1, nc):
            launch(None, functools.partial(constants, i, t, me, lax.rem(me + t, nc)))
    prepare(0)
    xd, xz4, xz3, d1 = k_.xd, k_.xz4, k_.xz3, k_.d1
    for ref in (xd, xz4, xz3):
        clear_rows(ref)
        clear_halos(ref)
    for ref in (k_.xh, k_.xz2, k_.xz1):
        clear_halos(ref)
    for i in range(S):
        for at in (0, (RB + 2) * LANES):
            k_.dzt[i, at : at + 2 * LANES] = jnp.zeros((2 * LANES, LANES), BF16)
        for r in range(3):
            k_.ug[i, r] = jnp.zeros(k_.ug.shape[2:], F32)
            k_.ug[i, RB + 3 + r] = jnp.zeros(k_.ug.shape[2:], F32)
        for r in range(H + 2):
            k_.cb[i, r] = jnp.zeros(k_.cb.shape[2:], F32)

    for at in (0, V + Q * LANES):
        k_.dzct[at : at + V] = jnp.zeros((V, LANES), BF16)

    def norm_of(layer):
        return column(k_.en[0, layer : layer + 1]), column(k_.en[1, layer : layer + 1])

    norm_e1, norm_e2 = norm_of(0), norm_of(1)

    gather_pass(xp, "pooled")
    gather_wait(xp, "pooled")
    coarse_sums(0, conv_stats_coarse(xp, wf[0], k_.z1, dm.ce))
    prepare(1)
    stats_e1 = moments(coarse_totals(0), dm.coarse_total)

    def keep_coarse(ref):
        def store(p, v):
            ref[core, x, 1, p] = v.astype(BF16).astype(ref.dtype)

        return store

    norm_rows(k_.z1, stats_e1, norm_e1, keep_coarse(k_.xh), Q)
    gather_start(k_.xh, "hidden")
    prepare(2)
    forward_start(2)
    gather_pass(k_.xh, "hidden")
    gather_pass(xs, "skip")
    gather_wait(k_.xh, "hidden")
    coarse_sums(1, conv_stats_coarse(k_.xh, wf[1], k_.z2, dm.ce))
    take_rows(k_.cot)

    def take_cot(i, carry):
        for d in range(S):
            for j in range(4):
                v = row_of_all(d * R + 4 * i + j, dm.cd).astype(BF16)
                k_.own_cot[d, 4 * i + j] = v.astype(k_.own_cot.dtype)
        return carry

    lax.fori_loop(0, Q, take_cot, 0)
    k_.cots[x] = k_.own_cot[:, pl.ds(row0, RB)]
    stats_e2 = moments(coarse_totals(1), dm.coarse_total)
    norm_rows(k_.z2, stats_e2, norm_e2, keep_coarse(k_.xc), Q)
    gather_start(k_.xc, "coarse")
    prepare(3)
    for t in range(1, nc):
        for i in range(2):
            source = lax.rem(me + nc - t, nc)
            constants(i, t, source, source).wait_recv()
    gate_full = gate_all[...].reshape(dm.g, 3 * LANES)
    wg = gate_full[:, 0:columns].astype(BF16)
    gbias = gate_full[:, 2 * LANES : 2 * LANES + 1]
    gout = gate_full[:, 2 * LANES + 1 : 2 * LANES + 2]
    k_.gate_t[...] = jnp.transpose(gate_full[:, 0 : 2 * LANES])
    own_rows = [k_.gate_t[pl.ds(pl.multiple_of((2 * i + core) * dm.ce, dm.ce), dm.ce)] for i in range(nx)]
    own_rows += [
        k_.gate_t[pl.ds(pl.multiple_of(dm.enc_all + (2 * i + core) * dm.cs, dm.cs), dm.cs)] for i in range(nx)
    ]
    k_.gate_own[...] = jnp.concatenate(own_rows, 0)

    def norm_fine(layer):
        return tuple(
            jnp.concatenate(
                [column(norm_all[2 * i + core, 2 * layer + part : 2 * layer + part + 1, 0 : dm.cd]) for i in range(nx)], 0
            )
            for part in range(2)
        )

    norm_d1, norm_d2 = norm_fine(0), norm_fine(1)
    gather_pass(k_.xc, "coarse")
    gather_wait(k_.xc, "coarse")
    forward_start(3)

    dt = k_.dt

    def up_depth(i, carry):
        t = []
        for j in range(3):
            v = dot(flat(k_.xc, j, i), up)
            t.append(jnp.stack([v[:, 0:LANES], v[:, LANES:]], 0))
        below = jnp.where(first, t[1], t[0])
        above = jnp.where(last, t[1], t[2])
        near = 0.75 * t[1]
        here = 0.25 * t[1]
        rows = pl.ds(i * 2, 2)
        dt[0, rows] = jnp.where(first, 0.0, 0.75 * below + here)
        dt[1, rows] = near + 0.25 * below
        dt[2, rows] = near + 0.25 * above
        dt[3, rows] = jnp.where(last, 0.0, 0.75 * above + here)
        return carry

    lax.fori_loop(0, Q, up_depth, 0)

    def up_rows(i, carry):
        here = h0 + i
        before, after = jnp.maximum(here - 1, 0), jnp.minimum(here + 1, H - 1)
        for j in range(S + 2):
            v = 0.75 * dt[j, here]
            d1[j, 1 + 2 * i, 0 : dm.enc_all] = (v + 0.25 * dt[j, before]).astype(BF16)
            d1[j, 2 + 2 * i, 0 : dm.enc_all] = (v + 0.25 * dt[j, after]).astype(BF16)
        return carry

    lax.fori_loop(0, RB // 2, up_rows, 0)
    for edge, at, near, far in (
        (top, 0, jnp.maximum(h0 - 1, 0), h0),
        (bottom, E - 1, jnp.minimum(h0 + RB // 2, H - 1), h0 + RB // 2 - 1),
    ):
        for j in range(S + 2):
            v = jnp.where(edge, 0.0, 0.75 * dt[j, near] + 0.25 * dt[j, far])
            d1[j, at, 0 : dm.enc_all] = v.astype(BF16)
    for t in range(1, nx):
        tox = lax.rem(x + t, nx)

        def send_cot(t=t, tox=tox):
            return peer_copy(
                k_.own_cot.at[:, pl.ds(tox * RB, RB)], k_.cots.at[x], k_.o_send.at[0, t], k_.o_recv.at[0, t],
                place, 2 * tox + core,
            )

        launch(None, send_cot)

    gather_wait(xs, "skip")
    gate_n = E // 2

    def gate(i, carry):
        j = lax.div(i, 2)
        r0 = (i - 2 * j) * gate_n
        skips = [flat(xs, j, r0 + q) for q in range(gate_n)]
        v = jnp.concatenate(
            [
                jnp.concatenate([d1[j, r0 + q, 0 : dm.enc_all] for q in range(gate_n)], 1),
                jnp.concatenate(skips, 1),
            ],
            0,
        )
        pre = dot(wg, v) + gbias
        act = pre * jax.nn.sigmoid(pre)
        alpha = jax.nn.sigmoid(jnp.sum(gout * act, axis=0, keepdims=True))
        for q in range(gate_n):
            lanes = slice(q * LANES, (q + 1) * LANES)
            d1[j, r0 + q, dm.enc_all :] = (alpha[:, lanes] * skips[q].astype(F32)).astype(BF16)
            k_.pre[j, r0 + q] = pre[:, lanes]
            k_.alpha[j, r0 + q] = alpha[:, lanes]
        return carry

    lax.fori_loop(0, (S + 2) * 2, gate, 0)
    for k in (3, 2, 1, 0):
        weights_start(k)

    def row_d1(j, r):
        return d1[j, r]

    def row_xd(j, r):
        return natural(xd, j, r)

    forward_wait(2)
    fine_sums(0, conv_stats(row_d1, forward_weight(2), k_.z3))
    drain()
    forward_wait(3)
    stats_d1 = moments(fine_totals(0), dm.fine_total)

    def keep_dec(p, v):
        d = lax.div(p, RB)
        xd[core, 1 + d, 1 + p - d * RB] = v.astype(BF16).astype(xd.dtype)

    norm_rows(k_.z3, stats_d1, norm_d1, keep_dec, RB)
    fine_start(xd, "hidden")
    for t in range(1, nx):
        fromx = lax.rem(x + nx - t, nx)
        theirs = k_.cots.at[fromx]
        peer_copy(theirs, theirs, k_.o_send.at[0, t], k_.o_recv.at[0, t], place, 2 * fromx + core).wait_recv()
    fine_pass(xd, "hidden")
    weights_finish(3)
    fine_wait(xd, "hidden")
    fine_sums(1, conv_stats(row_xd, forward_weight(3), k_.z4))
    stats_d2 = moments(fine_totals(1), dm.fine_total)

    def row_cot(p):
        d = lax.div(p, RB)
        return jnp.concatenate([k_.cots[i, d, p - d * RB] for i in range(nx)], 0).astype(F32)

    fine_sums(2, norm_back_sums(k_.z4, keep_du(k_.du_f), stats_d2, norm_d2, row_cot, RB))

    def keep_result(p, v):
        for i in range(nx):
            k_.ob[i, p] = v[i * dm.cd : (i + 1) * dm.cd].astype(BF16).astype(k_.ob.dtype)

    norm_rows(k_.z4, stats_d2, norm_d2, keep_result, RB)
    for t in range(1, nx):
        tox = lax.rem(x + t, nx)

        def send_result(t=t, tox=tox):
            return peer_copy(
                k_.ob.at[tox], k_.oi.at[x], k_.o_send.at[1, t], k_.o_recv.at[1, t], place, 2 * tox + core
            )

        launch(None, send_result)
    total_d2 = fine_totals(2)
    norm_back_fine(k_.z4, back_factors(stats_d2, norm_d2, total_d2, dm.fine_total), xz4)
    fine_start(xz4, "dz4")
    weight_grad(row_xd, 3)
    fine_pass(xz4, "dz4")
    cross_start(3)
    fine_wait(xz4, "dz4")

    def keep_grad(d, results, carry):
        for j, v in enumerate(results):
            k_.gg[d * RB + j] = v
        return carry

    conv(blocks_of(xz4), wb[3][...], dm.cf, 1, keep_grad, 0)
    fine_sums(3, norm_back_sums(k_.z3, keep_du(k_.du_f), stats_d1, norm_d1, lambda p: k_.gg[p], RB))
    cross_finish(3)
    total_d1 = fine_totals(3)
    norm_back_fine(k_.z3, back_factors(stats_d1, norm_d1, total_d1, dm.fine_total), xz3)
    fine_start(xz3, "dz3")
    weights_finish(2)
    weight_grad(row_d1, 2)
    fine_pass(xz3, "dz3")
    cross_start(2)
    fine_wait(xz3, "dz3")

    ups = nx * dm.ce

    def gate_back(d, results, carry):
        bias, psi = carry
        lows = []
        for j, both in enumerate(results):
            p = d * RB + j
            v = both[ups:]
            grad = jnp.sum(v * flat(xs, d + 1, 1 + j).astype(F32), axis=0, keepdims=True)
            alpha = k_.alpha[d + 1, 1 + j]
            logit = grad * alpha * (1.0 - alpha)
            pre = k_.pre[d + 1, 1 + j]
            sigma = jax.nn.sigmoid(pre)
            psi = psi + pre * sigma * logit
            low = (logit * gout * sigma * (1.0 + pre * (1.0 - sigma))).astype(BF16)
            bias = bias + low.astype(F32)
            k_.pg[p] = low
            lows.append(low)
            k_.ug[d, 3 + j] = both[0:ups]
            for i in range(nc):
                k_.gv[i] = v[i * dm.cs : (i + 1) * dm.cs]
            for i in range(nx):
                k_.sgp[i, p] = alpha * k_.gv[2 * i + core]
        back = dot(k_.gate_own[...].astype(BF16), jnp.concatenate(lows, 1))
        for j in range(len(results)):
            p = d * RB + j
            lanes = slice(j * LANES, (j + 1) * LANES)
            k_.ug[d, 3 + j] += back[0:ups, lanes]
            for i in range(nx):
                v = k_.sgp[i, p] + back[ups + i * dm.cs : ups + (i + 1) * dm.cs, lanes]
                k_.sgp[i, p] = v
                k_.sgb[i, p] = v.astype(BF16).astype(k_.sgb.dtype)
        return bias, psi

    blank = jnp.zeros((dm.g, LANES), F32)
    bias, psi = conv(blocks_of(xz3), wb[2][...], ups + dm.skip_all, 1, gate_back, (blank, blank))

    ug, cb, cg = k_.ug, k_.cb, k_.cg
    for q in range(RB // 2 + 2):
        terms = []
        for d in range(S):
            v = 0.75 * (ug[d, 2 * q + 1] + ug[d, 2 * q + 2]) + 0.25 * (ug[d, 2 * q + 3] + ug[d, 2 * q])
            if q == 1:
                v += jnp.where(top, 0.25 * ug[d, 3], 0.0)
            if q == RB // 2:
                v += jnp.where(bottom, 0.25 * ug[d, RB + 2], 0.0)
            terms.append(split(v))
        v = dot(jnp.concatenate(terms, 0), down)
        for d in range(S):
            cb[d, h0 + q] = v[d * ups : (d + 1) * ups]

    def to_slabs(i, carry):
        even, odd = (cb[d, 2 * i + 1] + pltpu.roll(cb[d, 2 * i + 2], half, 1) for d in range(S))
        middle = 0.75 * (even + odd) + jnp.where(first, 0.25 * even, 0.0) + jnp.where(last, 0.25 * odd, 0.0)
        for part, v in enumerate((0.25 * even, middle, 0.25 * odd)):
            for j in range(nx):
                block = v[j * dm.ce : (j + 1) * dm.ce]
                k_.fs[part, j, i] = block.astype(BF16).astype(k_.fs.dtype)
                if part == 1:
                    k_.fm[j, i] = block
        return carry

    lax.fori_loop(0, Q, to_slabs, 0)

    def fold_parts():
        for step in (-1, 1, 0):
            sends = (no(first), None, no(last))[step + 1]
            gets = (no(last), None, no(first))[step + 1]
            for t in range(nx):
                if (step, t) != (0, 0):
                    tox, fromx = lax.rem(x + t, nx), lax.rem(x + nx - t, nx)
                    sems = (k_.f_send.at[step + 1, t], k_.f_recv.at[step + 1, t])
                    theirs = k_.fr.at[step + 1, fromx]
                    yield (
                        sends, gets, fromx, step + 1,
                        functools.partial(
                            peer_copy, k_.fs.at[step + 1, tox], k_.fr.at[step + 1, x], *sems, place + step, 2 * tox + core
                        ),
                        functools.partial(peer_copy, theirs, theirs, *sems, place, 2 * fromx + core),
                    )

    for sends, _, _, _, out, _ in fold_parts():
        launch(sends, out)
    for t in range(1, nx):
        tox = lax.rem(x + t, nx)

        def send_skip(t=t, tox=tox):
            return peer_copy(
                k_.sgb.at[tox], k_.sgi.at[x], k_.o_send.at[2, t], k_.o_recv.at[2, t], place, 2 * tox + core
            )

        launch(None, send_skip)

    k_.gw[...] = jnp.zeros(k_.gw.shape, F32)

    def gate_weight(d, carry):
        v = jnp.concatenate(
            [
                jnp.concatenate([d1[1 + d, 1 + j, 0 : dm.enc_all] for j in range(RB)], 1),
                jnp.concatenate([flat(xs, 1 + d, 1 + j) for j in range(RB)], 1),
            ],
            0,
        )
        y = jnp.concatenate([k_.pg[d * RB + j] for j in range(RB)], 1)
        k_.gw[0:columns, 0 : dm.g] += dot_nt(v, y)
        return carry

    lax.fori_loop(0, S, gate_weight, 0)
    gate_grad = jnp.transpose(k_.gw[...])
    lane = iota((dm.g, LANES), 1)
    vectors = jnp.where(
        lane == 0,
        jnp.sum(bias, axis=1, keepdims=True),
        jnp.where(lane == 1, jnp.sum(psi, axis=1, keepdims=True), 0.0),
    )
    gate_block = k_.gate_block
    for j in range(nc):
        mine = slice(j * gq, (j + 1) * gq)
        gate_block[j, :, 0 : 2 * LANES] = gate_grad[mine]
        gate_block[j, :, 2 * LANES :] = vectors[mine]
    sum_start(everyone, k_.sv, 4, 0, gate_block[me], lambda chan: gate_block.at[chan])
    cg[...] = k_.fm[x]
    for _, gets, fromx, part, _, back in fold_parts():

        def fold_in(back=back, part=part, fromx=fromx):
            back().wait_recv()
            cg[...] += k_.fr[part, fromx].astype(F32)

        guarded(gets, fold_in)

    coarse_sums(2, norm_back_sums(k_.z2, keep_du(k_.du_c), stats_e2, norm_e2, lambda p: cg[p], Q))
    cross_finish(2)
    weights_finish(1)
    total_e2 = coarse_totals(2)
    norm_back_coarse(k_.z2, back_factors(stats_e2, norm_e2, total_e2, dm.coarse_total), k_.xz2)
    gather_start(k_.xz2, "dz2")
    weight_grad_coarse(k_.xh, 1)
    reduce_finish(3)
    gather_pass(k_.xz2, "dz2")
    reduce_start(1)
    weights_finish(0)
    drain()
    gather_wait(k_.xz2, "dz2")
    for i, v in enumerate(conv_coarse(k_.xz2, wb[1], dm.ce)):
        cg[i] = v
    coarse_sums(3, norm_back_sums(k_.z1, keep_du(k_.du_c), stats_e1, norm_e1, lambda p: cg[p], Q))
    reduce_finish(2)
    total_e1 = coarse_totals(3)
    norm_back_coarse(k_.z1, back_factors(stats_e1, norm_e1, total_e1, dm.coarse_total), k_.xz1)
    gather_start(k_.xz1, "dz1")
    weight_grad_coarse(xp, 0)
    reduce_start(0)
    reduce_finish(1)
    gather_pass(k_.xz1, "dz1")
    gradient_out(3)

    def rows_out(ref, own, theirs, kind, size):
        def copy_rows(read, at):
            def body(d, carry):
                for r in range(RB):
                    p = (d * R + at * RB + r) * size
                    ref[pl.ds(pl.multiple_of(p, size), size)] = read(d * RB + r).astype(F32)
                return carry

            lax.fori_loop(0, S, body, 0)

        copy_rows(lambda p: own[x, p], x)
        for t in range(1, nx):
            fromx = lax.rem(x + nx - t, nx)
            block = theirs.at[fromx]
            peer_copy(block, block, k_.o_send.at[kind, t], k_.o_recv.at[kind, t], place, 2 * fromx + core).wait_recv()
            copy_rows(lambda p, fromx=fromx: theirs[fromx, p], fromx)

    rows_out(k_.out, k_.ob, k_.oi, 1, dm.cd)
    rows_out(k_.sg, k_.sgp, k_.sgi, 2, dm.cs)
    gather_wait(k_.xz1, "dz1")
    for i, v in enumerate(conv_coarse(k_.xz1, wb[0], dm.cs)):
        v = dot(split(v), spread2) * 0.125
        for j in range(4):
            part = v[:, (j // 2) * LANES : (j // 2 + 1) * LANES]
            for d in range(S):
                at = (d * R + 4 * i + j) * dm.cs
                k_.sg[at : at + dm.cs] += part
    reduce_finish(0)
    gradient_out(2)
    gradient_out(1)
    gate_total = sum_finish(everyone, k_.sv, 4, 0)
    k_.ggate[...] = gate_total[:, 0:columns]
    k_.gvector[0:1] = row_of(gate_total[:, 2 * LANES : 2 * LANES + 1])
    k_.gvector[1:2] = row_of(gate_total[:, 2 * LANES + 1 : 2 * LANES + 2])

    def own_part(col):
        parts = [jnp.where(x == i, col[i * dm.cd : (i + 1) * dm.cd], 0.0) for i in range(nx)]
        return functools.reduce(jnp.add, parts)

    for ref, pair, pick in ((k_.gen, (total_e1, total_e2), lambda v: v), (k_.gdn, (total_d1, total_d2), own_part)):
        for layer, total in enumerate(pair):
            ref[0, layer : layer + 1] = row_of(pick(total[1]))
            ref[1, layer : layer + 1] = row_of(pick(total[0]))
    gradient_out(0)
    drain()


def adamw(weight, grad, moment, square, rate):
    new_moment = 0.9 * moment + 0.1 * grad
    new_square = 0.999 * square + 0.001 * grad * grad
    moment_hat = new_moment / (1.0 - 0.9**STEP)
    square_hat = new_square / (1.0 - 0.999**STEP)
    new_weight = weight - rate * (moment_hat / (jnp.sqrt(square_hat) + 1e-08) + 0.01 * weight)
    return (new_weight, new_moment, new_square)


RATES = (CONV_RATE, CONV_RATE, GATE_RATE, VECTOR_RATE, CONV_RATE, CONV_RATE, VECTOR_RATE, VECTOR_RATE)


def update_kernel(*refs):
    n = len(RATES)
    sources, targets = refs[: 2 + 4 * n], refs[2 + 4 * n : 4 + 7 * n]
    inside, outside = refs[4 + 7 * n : 6 + 11 * n], refs[6 + 11 * n : 8 + 14 * n]
    in_sem, out_sem = refs[8 + 14 * n :]
    order = (4, 1, 0, 5, 2, 3, 6, 7)

    def load(i):
        return pltpu.make_async_copy(sources[i], inside[i], in_sem.at[i])

    def store(i):
        return pltpu.make_async_copy(outside[i], targets[i], out_sem.at[i])

    for i in (1, 0):
        load(i).start()
    for k in order:
        for part in range(4):
            load(2 + part * n + k).start()
    for i in (1, 0):
        load(i).wait()
        chans, (slabs, rows) = outside[i].shape[0], outside[i].shape[1:3]
        for c in range(chans):
            v = inside[i][pl.ds(c, slabs * rows, stride=chans)]
            outside[i][c] = v.reshape(slabs, rows, LANES).astype(outside[i].dtype)
        store(i).start()
    for k in order:
        own = [2 + part * n + k for part in range(4)]
        for i in own:
            load(i).wait()
        rows = inside[own[0]].shape[0]
        step = 8 if rows % 8 == 0 and rows > 8 else rows
        for r in range(0, rows, step):
            at = slice(r, r + step)
            new = adamw(*(inside[i][at] for i in own), RATES[k])
            for part, value in enumerate(new):
                outside[2 + 3 * k + part][at] = value
        for part in range(3):
            store(2 + 3 * k + part).start()
    for i in range(len(targets)):
        store(i).wait()


def per_device(
    skip, cotangent, enc_conv1, enc_conv2, gate_proj, gate_vector, dec_conv1, dec_conv2, enc_norms, dec_norms, *states
):
    nd, nc = lax.axis_size("depth"), lax.axis_size("chan")
    dm = Dims(nd, nc, skip.shape, enc_conv1.shape[0], dec_conv1.shape[0], gate_proj.shape[0] * nc)
    S, R, H, nx, RB, E = dm.s, dm.rows, dm.half, dm.nx, dm.rb, dm.ext
    Q = H // 2
    cin3 = dm.enc_all + dm.skip_all

    def own_block(size):
        return (size, lambda j: pl.multiple_of(j * size, size), 0)

    def core_blocks(size):
        return tuple(
            (size, lambda j, i=i: pl.multiple_of((2 * i + lax.rem(j, 2)) * size, size), i * size) for i in range(nx)
        )

    dm.convs = convs = (
        Conv(dm, dm.ce, dm.skip_all, (own_block(dm.cs),)),
        Conv(dm, dm.ce, dm.enc_all, (own_block(dm.ce),)),
        Conv(dm, dm.cd, cin3, core_blocks(dm.ce) + ((dm.skip_all, lambda j: dm.enc_all, nx * dm.ce),)),
        Conv(dm, dm.cd, dm.dec_all, core_blocks(dm.cd)),
    )
    params = (enc_conv1, enc_conv2, gate_proj, gate_vector, dec_conv1, dec_conv2, enc_norms, dec_norms)
    inputs = dict(
        skip=skip, cot=cotangent, w0=enc_conv1, w1=enc_conv2, w2=dec_conv1, w3=dec_conv2,
        gate=gate_proj, vector=gate_vector, en=enc_norms, dn=dec_norms,
    )
    shape = jax.ShapeDtypeStruct
    outs = dict(
        out=shape((S * R * dm.cd, LANES), F32),
        sg=shape((S * R * dm.cs, LANES), F32),
        **{f"g{i}": shape(a.shape, F32) for i, a in enumerate((enc_conv1, enc_conv2, dec_conv1, dec_conv2))},
        **{
            name: shape(a.shape, F32)
            for name, a in (("ggate", gate_proj), ("gvector", gate_vector), ("gen", enc_norms), ("gdn", dec_norms))
        },
    )
    gq = dm.g // nc

    def coarse(block):
        return pltpu.VMEM((2, nx, 3, Q, block, LANES), storage(block))

    def fine():
        return pltpu.VMEM((2, S + 2, E, dm.cf, LANES), storage(dm.cd))

    def f32(*dims):
        return pltpu.VMEM((*dims, LANES), F32)

    def tiles(*dims):
        return pltpu.VMEM((*dims, 16, LANES), BF16)

    def blocks(block, *dims):
        return pltpu.VMEM((*dims, block, LANES), storage(block))

    def sems(*dims):
        return pltpu.SemaphoreType.DMA(dims)

    scratch = dict(
        xp=coarse(dm.cs), xh=coarse(dm.ce), xc=coarse(dm.ce), xz2=coarse(dm.ce), xz1=coarse(dm.ce),
        own_skip=blocks(dm.cs, S, R + 2), xs=blocks(dm.cs, 2, nx, S + 2, E),
        own_cot=blocks(dm.cd, S, R), cots=blocks(dm.cd, nx, S, RB),
        d1=pltpu.VMEM((S + 2, E, cin3, LANES), BF16), xd=fine(), xz4=fine(), xz3=fine(),
        z1=f32(Q, dm.ce), z2=f32(Q, dm.ce), z3=f32(S * RB, dm.cf), z4=f32(S * RB, dm.cf),
        du_c=f32(Q, dm.ce), du_f=f32(S * RB, dm.cf), gg=f32(S * RB, dm.cf), cg=f32(Q, dm.ce),
        pre=f32(S + 2, E, dm.g), alpha=f32(S + 2, E, 1), pg=pltpu.VMEM((S * RB, dm.g, LANES), BF16),
        ug=f32(S, RB + 6, nx * dm.ce), cb=f32(S, H + 2, nx * dm.ce), dt=f32(S + 2, H, dm.enc_all),
        gv=f32(nc, dm.cs), sgp=f32(nx, S * RB, dm.cs), sgb=blocks(dm.cs, nx, S * RB), sgi=blocks(dm.cs, nx, S * RB),
        ob=blocks(dm.cd, nx, S * RB), oi=blocks(dm.cd, nx, S * RB),
        dzt=pltpu.VMEM((S, (RB + 4) * LANES, LANES), BF16), dzct=pltpu.VMEM((Q * LANES + 2 * dm.hcols, LANES), BF16),
        gw=f32(2 * LANES),
        fs=blocks(dm.ce, 3, nx, Q), fr=blocks(dm.ce, 3, nx, Q), fm=f32(nx, Q, dm.ce),
        st=f32(4, nd, 1), su=f32(4, nd * nx, 1), sv=pltpu.VMEM((1, nd * nx, gq, 3 * LANES), F32),
        norm_all=f32(nc, 8), rows=f32(max(dm.cs, dm.cd) * S * R),
        turned=f32(max(cv.chunks for cv in convs) * LANES),
        acc=pltpu.VMEM((max(3 * cv.c for cv in convs), 3 * LANES), F32),
        gate_all=pltpu.VMEM((nc, gq, 3 * LANES), F32), gate_t=pltpu.VMEM((2 * LANES, dm.g), F32),
        gate_own=pltpu.VMEM((nx * (dm.ce + dm.cs), dm.g), F32), gate_block=pltpu.VMEM((nc, gq, 3 * LANES), F32),
        **{f"wt{i}": pltpu.VMEM((3, cv.c, cv.wide), cv.kind) for i, cv in enumerate(convs)},
        **{
            f"wf{i}": pltpu.VMEM((cv.taps, 3 * cv.c) if i < 2 else (nx, cv.stored, 9 * cv.c), BF16)
            for i, cv in enumerate(convs)
        },
        **{f"wx{i}": pltpu.VMEM((nc, 3, cv.needed, cv.wide), cv.kind) for i, cv in enumerate(convs)},
        **{
            f"wb{i}": pltpu.VMEM((9 * cv.needed, 3 * nc * cv.o) if i < 2 else (3 * cv.needed, 9 * nc * cv.o), BF16)
            for i, cv in enumerate(convs)
        },
        flip=pltpu.VMEM((max(cv.tiles for cv in convs[2:]) * LANES, max(3 * cv.c for cv in convs[2:])), F32),
        **{f"gt{i}": tiles(cv.share * nd) for i, cv in enumerate(convs)},
        **{f"gr{i}": tiles(nd, cv.share) for i, cv in enumerate(convs)},
        **{f"ga{i}": tiles(cv.share * nd) for i, cv in enumerate(convs)},
        **{f"gs{i}": tiles(convs[i].count) for i in (2, 3)},
        **{f"gx{i}": tiles(nx, convs[i].count) for i in (2, 3)},
        g_send=sems(len(GATHERS), 3, nx), g_recv=sems(len(GATHERS), 3),
        h_send=sems(len(GATHERS), 2 + nx), h_recv=sems(len(GATHERS)),
        x_send=sems(len(FINE), 3, 5), x_recv=sems(len(FINE), 3, 5),
        y_send=sems(len(FINE), 3), y_recv=sems(len(FINE), 3),
        t_send=sems(4), t_recv=sems(4), u_send=sems(5), u_recv=sems(5),
        f_send=sems(3, nx), f_recv=sems(3, nx), w_send=sems(4, nx + 1, nc), w_recv=sems(4, nx + 1, nc),
        p_send=sems(2, nx), p_recv=sems(2, nx), c_send=sems(2, nx), c_recv=sems(2, nx),
        o_send=sems(3, nx), o_recv=sems(3, nx), v_send=sems(2, nc), v_recv=sems(2, nc),
        r_send=sems(4), r_recv=sems(4), a_send=sems(4), a_recv=sems(4),
    )
    vmem = pl.BlockSpec(memory_space=pltpu.VMEM)
    out, sg, grad1, grad2, grad3, grad4, ggate, gvector, gen, gdn = pl.pallas_call(
        functools.partial(kernel, dm, (*inputs, *outs, *scratch)),
        out_shape=tuple(outs.values()),
        in_specs=[vmem] * len(inputs),
        out_specs=[vmem] * len(outs),
        scratch_shapes=list(scratch.values()),
        compiler_params=pltpu.CompilerParams(
            has_side_effects=True, collective_id=0, vmem_limit_bytes=60 * 1024 * 1024
        ),
        name="step",
    )(*inputs.values())
    grads = (grad1, grad2, ggate, gvector, grad3, grad4, gen, gdn)
    operands = (out, sg, *params, *grads, *states)
    updated = (
        shape(cotangent.shape, BF16),
        shape(skip.shape, F32),
        *(shape(p.shape, F32) for p in params for _ in range(3)),
    )
    anywhere = pl.BlockSpec(memory_space=pl.ANY)
    return pl.pallas_call(
        update_kernel,
        out_shape=updated,
        in_specs=[anywhere] * len(operands),
        out_specs=[anywhere] * len(updated),
        scratch_shapes=[
            *(pltpu.VMEM(a.shape, a.dtype) for a in operands),
            *(pltpu.VMEM(a.shape, a.dtype) for a in updated),
            pltpu.SemaphoreType.DMA((len(operands),)),
            pltpu.SemaphoreType.DMA((len(updated),)),
        ],
        compiler_params=pltpu.CompilerParams(vmem_limit_bytes=60 * 1024 * 1024),
        name="update",
    )(*operands)


def solution(mesh):
    volume = P("chan", "depth", None, None)
    row, column, norms = P("chan", None), P(None, "chan"), P(None, None, "chan")
    params = (row, row, row, column, row, row, norms, norms)
    return jax.shard_map(
        per_device,
        mesh=mesh,
        in_specs=(volume, volume) + params * 3,
        out_specs=(volume, volume) + tuple(spec for spec in params for _ in range(3)),
        check_vma=False,
    )
```

```python
import functools
import types

import jax
import jax.numpy as jnp
from jax import lax
from jax.experimental import pallas as pl
from jax.experimental.pallas import tpu as pltpu
from jax.sharding import PartitionSpec as P

STEP = 5
EPS = 1e-05
CONV_RATE = 0.03
GATE_RATE = 0.1
VECTOR_RATE = 0.5
LANES = 128
MESH = pl.DeviceIdType.MESH
F32 = jnp.float32
BF16 = jnp.bfloat16


def iota(shape, dim):
    return lax.broadcasted_iota(jnp.int32, shape, dim)


def dot(a, b):
    return jnp.dot(a, b, preferred_element_type=F32)


def dot_nt(a, b):
    return lax.dot_general(a, b, (((1,), (1,)), ((), ())), preferred_element_type=F32)


def dot_tn(a, b):
    return lax.dot_general(a, b, (((0,), (0,)), ((), ())), preferred_element_type=F32)


def from_left(v, width):
    return jnp.where(iota(v.shape, 1) % width == 0, 0.0, pltpu.roll(v, 1, 1))


def from_right(v, width):
    return jnp.where(iota(v.shape, 1) % width == width - 1, 0.0, pltpu.roll(v, LANES - 1, 1))


def halves(low, high):
    return pltpu.roll(jnp.where(iota(low.shape, 1) < LANES // 2, low, high), LANES // 2, 1)


def split(v):
    high = v.astype(BF16)
    return jnp.concatenate([high, (v - high.astype(F32)).astype(BF16)], 1)


def storage(block):
    return BF16 if block % 16 == 0 else F32


def flat(ref, s, r):
    if len(ref.shape) == 4:
        return ref[s, r]
    v = ref[:, :, s, r]
    return jnp.concatenate([v[c, i] for i in range(v.shape[1]) for c in range(2)], 0).astype(BF16)


class Dims:
    def __init__(self, nd, nc, skip, enc, dec, gate):
        self.nd, self.nc, self.nx = nd, nc, nc // 2
        self.s, self.rows, self.cols = skip[1:]
        self.cs, self.ce, self.cd, self.g = skip[0], enc, dec, gate
        self.half, self.hcols = self.rows // 2, self.cols // 2
        self.fine_total = nd * self.s * self.rows * self.cols
        self.coarse_total = self.fine_total // 8
        self.enc_all = nc * enc
        self.skip_all = nc * skip[0]
        self.dec_all = nc * dec
        self.rb = self.rows // self.nx
        self.ext = self.rb + 2
        self.cf = self.nx * dec


GATHERS = ("pooled", "skip", "hidden", "coarse", "dz2", "dz1")
FINE = ("hidden", "dz4", "dz3")


class Conv:
    def __init__(self, dm, o, c, blocks):
        self.o, self.c, self.blocks = o, c, blocks
        self.length = 27 * c
        self.chunks = -(-self.length // LANES)
        self.per = LANES // o
        self.tiles = -(-9 // self.per)
        self.wide = self.tiles * LANES
        self.kind = storage(min(size for size, _, _ in blocks))
        self.needed = sum(size for size, _, _ in blocks)
        self.count = 3 * c // 16 * 3
        self.share = -(-self.count // dm.nd)
        self.taps = 9 * o
        self.stored = -(-3 * o // 16) * 16


def kernel(dm, names, *refs):
    k_ = types.SimpleNamespace(**dict(zip(names, refs)))
    nd, nc, nx, S, R, H = dm.nd, dm.nc, dm.nx, dm.s, dm.rows, dm.half
    W, V = dm.cols, dm.hcols
    Q, RB, E = H // 2, dm.rb, dm.ext
    place = lax.axis_index("depth")
    me = lax.axis_index("chan")
    x, core = lax.div(me, 2), lax.rem(me, 2)
    other = 1 - core
    mate = 2 * x + other
    row0, h0 = x * RB, x * (RB // 2)
    first, last = place == 0, place == nd - 1
    top, bottom = x == 0, x == nx - 1
    convs = dm.convs
    pending = []
    wt, wf, wx, wb = ([getattr(k_, f"{kind}{i}") for i in range(4)] for kind in ("wt", "wf", "wx", "wb"))
    gt, gr, ga = ([getattr(k_, f"{kind}{i}") for i in range(4)] for kind in ("gt", "gr", "ga"))
    weights = (k_.w0, k_.w1, k_.w2, k_.w3)
    grads = (k_.g0, k_.g1, k_.g2, k_.g3)
    turned, acc = k_.turned, k_.acc

    def no(cond):
        return jnp.logical_not(cond)

    def peer_copy(src, dst, send, recv, depth, chan):
        return pltpu.make_async_remote_copy(
            src_ref=src, dst_ref=dst, send_sem=send, recv_sem=recv,
            device_id={"depth": depth, "chan": chan}, device_id_type=MESH,
        )

    def guarded(cond, fn):
        if cond is None:
            fn()
        else:
            pl.when(cond)(fn)

    def drain():
        for cond, fn in pending:
            guarded(cond, fn)
        pending.clear()

    def launch(cond, copy):
        guarded(cond, lambda: copy().start())
        pending.append((cond, lambda: copy().wait_send()))

    def arrive(cond, copy):
        guarded(cond, lambda: copy().wait_recv())

    def both(a, b):
        return b if a is None else a if b is None else jnp.logical_and(a, b)

    can_send = (no(last), None, no(first))
    can_recv = (no(first), None, no(last))

    def slices(side, n):
        return (pl.ds(n, 1), pl.ds(1, n), pl.ds(1, 1))[side], (pl.ds(0, 1), pl.ds(1, n), pl.ds(n + 1, 1))[side]

    def at_x(t):
        up, down = x + t, x - t
        return jnp.where(up >= nx, up - nx, up), jnp.where(down < 0, down + nx, down)


    def gather_start(ref, which, source_at=None):
        n = ref.shape[2] - 2
        k = GATHERS.index(which)
        for side in (0, 2, 1):
            own, theirs = slices(side, n)
            for t in range(nx):
                if side == 1 and t == 0:
                    continue
                tox = at_x(t)[0]

                def copy(side=side, t=t, own=own, theirs=theirs, tox=tox):
                    start = (n, 1, 1)[side] - 1
                    size = (1, n, 1)[side]
                    src = ref.at[core, x, own] if source_at is None else source_at(pl.ds(start, size), tox)
                    return peer_copy(
                        src, ref.at[core, x, theirs], k_.g_send.at[k, side, t], k_.g_recv.at[k, side],
                        place + 1 - side, 2 * tox + core,
                    )

                launch(can_send[side], copy)
        gather_own(ref, which)

    def handed(ref, k, piece, i):
        return peer_copy(piece, piece, k_.h_send.at[k, i], k_.h_recv.at[k], place, mate)

    def gather_own(ref, which):
        k = GATHERS.index(which)
        launch(None, lambda: handed(ref, k, ref.at[core, x, pl.ds(1, ref.shape[2] - 2)], 0))

    def gather_pass(ref, which):
        n = ref.shape[2] - 2
        k = GATHERS.index(which)
        for side in (1, 0, 2):
            theirs = slices(side, n)[1]
            if side != 1:
                pieces = [ref.at[core, :, theirs]]
            else:
                pieces = [ref.at[core, at_x(t)[1], theirs] for t in range(1, nx)]
            for i, got in enumerate(pieces):
                arrive(
                    can_recv[side],
                    lambda got=got, side=side: peer_copy(
                        got, got, k_.g_send.at[k, side, 0], k_.g_recv.at[k, side], place, mate
                    ),
                )
                launch(None, lambda got=got, i=i, side=side: handed(ref, k, got, 1 + (side // 2 if side != 1 else 2 + i)))

    def gather_wait(ref, which):
        handed(ref, GATHERS.index(which), ref.at[other], 0).wait_recv()

    def fine_parts(ref, which, side):
        k = FINE.index(which)
        own, theirs = slices(side, S)
        inner = pl.ds(1, RB)
        rows = [(None, None, inner, inner, x, core, core)] if side != 1 else [(None, None, inner, inner, x, other, other)]
        if nx > 1:
            for c in range(2):
                rows.append((no(top), no(bottom), pl.ds(1, 1), pl.ds(E - 1, 1), x - 1, c, c))
                rows.append((no(bottom), no(top), pl.ds(RB, 1), pl.ds(0, 1), x + 1, c, c))
        parts = []
        for i, (sends, gets, row, at, tox, to, source) in enumerate(rows):
            target = ref.at[core, theirs, at]
            theirs_ = ref.at[source, theirs, at]
            up = (i - 1) % 2
            arrived = 0 if i == 0 else 1 + up * 2 + core
            expected = 0 if i == 0 else 1 + up * 2 + source
            send = k_.x_send.at[k, side, i]
            parts.append((
                both(can_send[side], sends), both(can_recv[side], gets),
                functools.partial(
                    peer_copy, ref.at[core, own, row], target, send, k_.x_recv.at[k, side, arrived],
                    place + 1 - side, 2 * tox + to,
                ),
                functools.partial(peer_copy, theirs_, theirs_, send, k_.x_recv.at[k, side, expected], place, mate),
            ))
        return parts

    def fine_start(ref, which):
        for side in (0, 2, 1):
            for sends, _, out, _ in fine_parts(ref, which, side):
                launch(sends, out)

    def fine_halo(ref, which, side, c):
        k = FINE.index(which)
        block = ref.at[c, slices(side, S)[1], pl.ds(1, RB)]
        return peer_copy(block, block, k_.y_send.at[k, side], k_.y_recv.at[k, side], place, mate)

    def fine_pass(ref, which):
        for side in (0, 2):
            _, gets, _, back = fine_parts(ref, which, side)[0]
            arrive(gets, back)
            launch(gets, functools.partial(fine_halo, ref, which, side, core))

    def fine_wait(ref, which):
        for side in (1, 0, 2):
            for _, gets, _, back in fine_parts(ref, which, side)[side != 1 :]:
                arrive(gets, back)
            if side != 1:
                arrive(can_recv[side], functools.partial(fine_halo, ref, which, side, other))

    def natural(ref, s, r):
        v = ref[:, s, r]
        size = dm.cd
        return jnp.concatenate(
            [v[c, i * size : (i + 1) * size] for i in range(nx) for c in range(2)], 0
        ).astype(BF16)

    def in_turn(count, fn):
        if count <= 16:
            for i in range(count):
                fn(i)
        else:

            def body(i, carry):
                fn(i)
                return carry

            lax.fori_loop(0, count, body, 0)

    def slab_peers(i):
        to = place + 1 + i
        return jnp.where(to >= nd, to - nd, to), me

    def wide_peers(i):
        i = i + 1
        dt, xt = (i // nx, i % nx) if isinstance(i, int) else (lax.div(i, nx), lax.rem(i, nx))
        to, tox = place + dt, x + xt
        return jnp.where(to >= nd, to - nd, to), 2 * jnp.where(tox >= nx, tox - nx, tox) + core

    def exchange(n, peers, copy):
        in_turn(n - 1, lambda i: copy(*peers(i)).start())

    def sum_start(group, ref, k, slot, tile, source=None):
        n, own, peers, send, recv = group
        ref[slot, own] = tile

        def copy(depth, chan):
            src = ref.at[slot, own] if source is None else source(chan)
            return peer_copy(src, ref.at[slot, own], send.at[k], recv.at[k], depth, chan)

        exchange(n, peers, copy)
        pending.append((None, lambda: all_of(group, ref, k, slot).wait_send()))

    def all_of(group, ref, k, slot):
        n, _, _, send, recv = group
        every = ref.at[slot, pl.ds(0, n - 1)]
        return peer_copy(every, every, send.at[k], recv.at[k], place, mate)

    def sum_finish(group, ref, k, slot):
        all_of(group, ref, k, slot).wait_recv()
        return jnp.sum(ref[slot], axis=0)

    slabs = (nd, place, slab_peers, k_.t_send, k_.t_recv)
    everyone = (nd * nx, place * nx + x, wide_peers, k_.u_send, k_.u_recv)

    def columns_of(row, m):
        lane, channel = iota((m, LANES), 1), iota((m, LANES), 0)
        return tuple(
            jnp.sum(jnp.where(lane == channel + i * m, row, 0.0), axis=1, keepdims=True) for i in range(2)
        )

    def coarse_sums(slot, sums):
        sum_start(slabs, k_.st, slot, slot, pack(*sums))

    def coarse_totals(slot):
        return columns_of(sum_finish(slabs, k_.st, slot, slot), dm.ce)

    def fine_sums(slot, sums):
        sum_start(everyone, k_.su, slot, slot, pack(*sums))

    def fine_totals(slot):
        return columns_of(sum_finish(everyone, k_.su, slot, slot), dm.cf)

    def prepare(k):
        cv, w, own = convs[k], weights[k], wt[k]
        out = wf[k] if k < 2 else wf[k].at[x]
        eye = (iota((LANES, LANES), 0) == iota((LANES, LANES), 1)).astype(BF16)

        def chunk(a):
            return dot_nt(eye, jnp.concatenate([a] * cv.per, 0).astype(BF16))

        full = cv.length // LANES

        def body(i, carry):
            at = pl.multiple_of(i * LANES, LANES)
            turned[pl.ds(at, LANES)] = chunk(w[:, pl.ds(at, LANES)])
            return carry

        lax.fori_loop(0, full, body, 0, unroll=4)
        if full < cv.chunks:
            a = w[:, full * LANES :]
            a = jnp.concatenate([a, jnp.zeros((cv.o, LANES - a.shape[1]), F32)], 1)
            turned[full * LANES : (full + 1) * LANES] = chunk(a)
        group = iota((cv.c, LANES), 1) // cv.o
        for kz in range(3):
            for j in range(cv.tiles):
                tile = None
                for g in range(cv.per):
                    u = j * cv.per + g
                    if u < 9:
                        kx, ky = u // 3, u % 3
                        v = turned[pl.ds(9 * kz + 3 * ky + kx, cv.c, stride=27)]
                        tile = v if tile is None else jnp.where(group == g, v, tile)
                own[kz, :, j * LANES : (j + 1) * LANES] = tile.astype(BF16).astype(own.dtype)
        for j in range(cv.tiles):
            v = jnp.concatenate([own[kz, :, j * LANES : (j + 1) * LANES] for kz in range(3)], 0)
            size = min(LANES, cv.taps - j * LANES)
            v = dot_nt(eye, v.astype(BF16))[0:size]
            if k < 2:
                out[j * LANES : j * LANES + size] = v.astype(BF16)
            else:
                k_.flip[j * LANES : j * LANES + size, 0 : 3 * cv.c] = v
        if k >= 2:
            out[0 : 3 * cv.o] = jnp.concatenate(
                [
                    jnp.concatenate(
                        [
                            k_.flip[(3 * kx + ky) * cv.o : (3 * kx + ky + 1) * cv.o, kz * cv.c : (kz + 1) * cv.c]
                            for kx in range(3)
                        ],
                        0,
                    )
                    for kz in range(3)
                    for ky in range(3)
                ],
                1,
            ).astype(BF16)

    def forward_copy(k, t):
        block = wf[k].at[x]
        return peer_copy(
            block, block, k_.p_send.at[k - 2, t], k_.p_recv.at[k - 2, t], place, 2 * lax.rem(x + t, nx) + core
        )

    def forward_start(k):
        for t in range(1, nx):
            launch(None, functools.partial(forward_copy, k, t))

    def forward_wait(k):
        for t in range(1, nx):
            fromx = lax.rem(x + nx - t, nx)
            block = wf[k].at[fromx]
            peer_copy(
                block, block, k_.p_send.at[k - 2, t], k_.p_recv.at[k - 2, t], place, 2 * fromx + core
            ).wait_recv()

    def forward_weight(k):
        return jnp.concatenate([wf[k][i, 0 : 3 * convs[k].o] for i in range(nx)], 0)

    def weights_start(k):
        cv = convs[k]
        for b, (size, start, at) in enumerate(cv.blocks):
            wx[k][me, :, at : at + size] = wt[k][:, pl.ds(start(me), size)]
            for t in range(1, nc):
                to = lax.rem(me + t, nc)

                def copy(to=to, t=t, b=b, size=size, start=start, at=at):
                    return peer_copy(
                        wt[k].at[:, pl.ds(start(to), size)], wx[k].at[me, :, pl.ds(at, size)],
                        k_.w_send.at[k, b, t], k_.w_recv.at[k, b, t], place, to,
                    )

                launch(None, copy)

    def weights_finish(k):
        cv = convs[k]
        for b, (size, _, at) in enumerate(cv.blocks):
            for t in range(1, nc):
                source = lax.rem(me + nc - t, nc)
                theirs = wx[k].at[source, :, pl.ds(at, size)]
                peer_copy(theirs, theirs, k_.w_send.at[k, b, t], k_.w_recv.at[k, b, t], place, source).wait_recv()

        parts = 9 if k < 2 else 3
        lanes = cv.taps // parts
        for i in range(parts):
            at = (parts - 1 - i) * lanes
            found = [wx[k][j, 2 - kz, :, at : at + lanes].astype(F32) for kz in range(3) for j in range(nc)]
            wb[k][i * cv.needed : (i + 1) * cv.needed] = jnp.concatenate(found, 1).astype(BF16)

    def tiles_of(k, put):
        def tile(i, carry):
            at = pl.multiple_of(i * 16, 16)
            for j in range(3):
                put(3 * i + j, acc[pl.ds(at, 16), j * LANES : (j + 1) * LANES].astype(BF16))
            return carry

        lax.fori_loop(0, convs[k].c // 16 * 3, tile, 0, unroll=4)

    def cross_start(k):
        gs, gx = (k_.gs2, k_.gs3)[k - 2], (k_.gx2, k_.gx3)[k - 2]

        def put(i, v):
            gs[i] = v

        tiles_of(k, put)
        for t in range(1, nx):

            def copy(t=t):
                return peer_copy(
                    gs, gx.at[x], k_.c_send.at[k - 2, t], k_.c_recv.at[k - 2, t], place, 2 * at_x(t)[0] + core
                )

            launch(None, copy)

    def cross_finish(k):
        cv, gs, gx = convs[k], (k_.gs2, k_.gs3)[k - 2], (k_.gx2, k_.gx3)[k - 2]
        sources = [at_x(t)[1] for t in range(1, nx)]
        for t, fromx in enumerate(sources, 1):
            theirs = gx.at[fromx]
            peer_copy(
                theirs, theirs, k_.c_send.at[k - 2, t], k_.c_recv.at[k - 2, t], place, 2 * fromx + core
            ).wait_recv()

        def add(i, carry):
            for j in range(9):
                p = 9 * i + j
                v = gs[p].astype(F32)
                for fromx in sources:
                    v += gx[fromx, p].astype(F32)
                gt[k][p] = v.astype(BF16)
            return carry

        lax.fori_loop(0, cv.count // 9, add, 0, unroll=2)
        reduce_send(k)

    def reduce_start(k):
        def put(i, v):
            gt[k][i] = v

        tiles_of(k, put)
        reduce_send(k)

    def reduce_send(k):
        cv = convs[k]
        for i in range(cv.count, cv.share * nd):
            gt[k][i] = jnp.zeros((16, LANES), BF16)
        gr[k][place] = gt[k][pl.ds(place * cv.share, cv.share)]

        def copy(to, chan):
            return peer_copy(
                gt[k].at[pl.ds(to * cv.share, cv.share)], gr[k].at[place], k_.r_send.at[k], k_.r_recv.at[k], to, chan
            )

        exchange(nd, slab_peers, copy)
        pending.append((None, lambda: reduce_all(k).wait_send()))

    def reduce_all(k):
        every = gr[k].at[pl.ds(0, nd - 1)]
        return peer_copy(every, every, k_.r_send.at[k], k_.r_recv.at[k], place, mate)

    def share_all(k):
        every = ga[k].at[pl.ds(0, (nd - 1) * convs[k].share)]
        return peer_copy(every, every, k_.a_send.at[k], k_.a_recv.at[k], place, mate)

    def reduce_finish(k):
        cv = convs[k]
        reduce_all(k).wait_recv()
        own = pl.ds(place * cv.share, cv.share)
        ga[k][own] = jnp.sum(gr[k][...].astype(F32), axis=0).astype(BF16)

        def copy(to, chan):
            return peer_copy(ga[k].at[own], ga[k].at[own], k_.a_send.at[k], k_.a_recv.at[k], to, chan)

        exchange(nd, slab_peers, copy)
        pending.append((None, lambda: share_all(k).wait_send()))

    def gradient_out(k):
        cv, out = convs[k], grads[k]
        share_all(k).wait_recv()
        group = iota((16, LANES), 1) // cv.o - (3 * x if k >= 2 else 0)

        def scatter(i, carry):
            for kz in range(3):
                for ky in range(3):
                    v = ga[k][(kz * (cv.c // 16) + i) * 3 + ky].astype(F32)
                    for kx in range(3):
                        at = 9 * kz + 3 * ky + kx + i * (16 * 27)
                        turned[pl.ds(at, 16, stride=27)] = jnp.where(group == kx, v, 0.0)
            return carry

        lax.fori_loop(0, cv.c // 16, scatter, 0, unroll=2)

        pick = (iota((cv.o, LANES), 1) % cv.o == iota((cv.o, LANES), 0)).astype(BF16)
        step = 8 * LANES
        for at in range(0, cv.length, step):
            size = min(step, cv.length - at)
            v = dot_nt(pick, turned[at : at + -(-size // LANES) * LANES].astype(BF16))
            out[:, at : at + size] = v[:, 0:size]

    def column(row):
        n = row.shape[1]
        eye = iota((n, n), 0) == iota((n, n), 1)
        return jnp.sum(jnp.where(eye, row, 0.0), axis=1, keepdims=True)

    def row_of(col):
        n = col.shape[0]
        eye = iota((n, n), 0) == iota((n, n), 1)
        return jnp.sum(jnp.where(eye, col, 0.0), axis=0, keepdims=True)

    def clear_halos(ref):
        def clear(at):
            if len(ref.shape) == 5:
                for c in range(2):
                    ref[c, at] = jnp.zeros(ref.shape[2:], ref.dtype)
            else:
                for i in range(nx):
                    ref[core, i, at] = jnp.zeros(ref.shape[3:], ref.dtype)

        pl.when(first)(lambda: clear(0))
        pl.when(last)(lambda: clear(ref.shape[-4] - 1))

    def clear_rows(ref):
        def clear(at):
            for c in range(2):
                for i in range(S + 2):
                    ref[c, i, at] = jnp.zeros(ref.shape[3:], ref.dtype)

        pl.when(top)(lambda: clear(0))
        pl.when(bottom)(lambda: clear(E - 1))

    def conv(operand, weight, m, groups, emit, init):
        def body(d, carry):
            v = operand(d)
            y = dot(weight, v)
            results = []
            for j in range(RB):
                lanes = slice(j * LANES, (j + 1) * LANES)
                parts = []
                for g in range(groups):
                    a = [y[(3 * g + kx) * m : (3 * g + kx + 1) * m, lanes] for kx in range(3)]
                    parts.append(from_left(a[0], W) + a[1] + from_right(a[2], W))
                results.append(jnp.concatenate(parts, 0) if groups > 1 else parts[0])
            return emit(d, results, carry)

        return lax.fori_loop(0, S, body, init)

    def rows_of(row):
        return lambda d: jnp.concatenate(
            [jnp.concatenate([row(d + kz, ky + j) for j in range(RB)], 1) for kz in range(3) for ky in range(3)], 0
        )

    def blocks_of(ref):
        size = dm.cd
        return lambda d: jnp.concatenate(
            [
                jnp.concatenate([ref[c, d + kz, 2 - ky + j, i * size : (i + 1) * size] for j in range(RB)], 1)
                for kz in range(3)
                for i in range(nx)
                for c in range(2)
                for ky in range(3)
            ],
            0,
        ).astype(BF16)

    def conv_stats(row, weight, z):
        def emit(d, results, carry):
            total, square = carry
            for j, v in enumerate(results):
                z[d * RB + j] = v
                total, square = total + v, square + v * v
            return total, square

        blank = jnp.zeros((dm.cf, LANES), F32)
        return conv(rows_of(row), weight, dm.cd, nx, emit, (blank, blank))

    def weight_grad(row, k):
        cv = convs[k]

        def part(d):
            v = jnp.concatenate([jnp.concatenate([row(d + kz, j) for j in range(E)], 1) for kz in range(3)], 0)
            y = jnp.concatenate(
                [k_.dzt[d, (2 - ky) * LANES : (2 - ky + E) * LANES] for ky in range(3)], 1
            )
            return dot(v, y)

        acc[0 : 3 * cv.c] = part(0)

        def more(d, carry):
            acc[0 : 3 * cv.c] += part(d)
            return carry

        lax.fori_loop(1, S, more, 0)

    def conv_coarse(ref, weight, m):
        v = jnp.concatenate(
            [jnp.concatenate([flat(ref, kz, i) for i in range(Q)], 1) for kz in range(3)], 0
        )
        y = dot(weight[...], v)
        blank = jnp.zeros((m, LANES), F32)

        def shifted(ky, i):
            if not 0 <= i < Q:
                return blank
            a, b, c = (
                y[(3 * kx + ky) * m : (3 * kx + ky + 1) * m, i * LANES : (i + 1) * LANES] for kx in range(3)
            )
            return from_left(a, V) + b + from_right(c, V)

        before = [shifted(0, i) for i in range(-1, Q)]
        after = [shifted(2, i) for i in range(Q + 1)]
        return [
            shifted(1, i) + halves(before[i + 1] + after[i + 1], before[i] + after[i]) for i in range(Q)
        ]

    def conv_stats_coarse(ref, weight, z, m):
        total = square = jnp.zeros((m, LANES), F32)
        for i, v in enumerate(conv_coarse(ref, weight, m)):
            z[i] = v
            total, square = total + v, square + v * v
        return total, square

    def weight_grad_coarse(ref, k):
        cv = convs[k]
        v = jnp.concatenate(
            [jnp.concatenate([flat(ref, kz, i) for i in range(Q)], 1) for kz in range(3)], 0
        )
        y = jnp.concatenate([k_.dzct[(2 - ky) * V : (2 - ky) * V + Q * LANES] for ky in range(3)], 1)
        acc[0 : 3 * cv.c] = dot(v, y)

    def pack(a, b):
        m = a.shape[0]
        a = jnp.sum(a, axis=1, keepdims=True)
        b = jnp.sum(b, axis=1, keepdims=True)
        lane, channel = iota((m, LANES), 1), iota((m, LANES), 0)
        both = jnp.where(lane == channel, a, jnp.where(lane == channel + m, b, 0.0))
        return jnp.sum(both, axis=0, keepdims=True)

    def moments(total, count):
        mean = total[0] / count
        var = total[1] / count - mean * mean
        return mean, lax.rsqrt(var + EPS)

    def wide(column):
        return jnp.broadcast_to(column, (column.shape[0], LANES))

    def factors(stats, norm):
        mean, inv = stats
        gain, shift = norm
        return wide(mean), wide(gain * inv), wide(shift)

    def norm_rows(z, stats, norm, emit, n):
        mean, scale, shift = factors(stats, norm)

        def body(i, carry):
            for j in range(n):
                p = i * n + j
                u = (z[p] - mean) * scale + shift
                emit(p, u * jax.nn.sigmoid(u))
            return carry

        lax.fori_loop(0, z.shape[0] // n, body, 0)

    def norm_back_sums(z, keep_du, stats, norm, grad, n):
        mean, scale, shift = factors(stats, norm)
        inv = wide(stats[1])
        m = z.shape[1]

        def body(i, carry):
            a, b = carry
            for j in range(n):
                p = i * n + j
                centred = z[p] - mean
                u = centred * scale + shift
                sigma = jax.nn.sigmoid(u)
                v = grad(p) * sigma * (1.0 + u * (1.0 - sigma))
                keep_du(p, v)
                a, b = a + v, b + v * (centred * inv)
            return a, b

        blank = jnp.zeros((m, LANES), F32)
        return lax.fori_loop(0, z.shape[0] // n, body, (blank, blank))

    def back_factors(stats, norm, total, count):
        mean, inv = stats
        scale = norm[0] * inv
        return wide(mean), wide(scale), wide(-scale * total[0] / count), wide(-scale * inv * total[1] / count)

    def columns_first(copies, groups):
        size = copies[0].shape[0] // groups
        rows = [v[g * size : (g + 1) * size] for g in range(groups) for v in copies]
        used = 3 * groups * size
        if used < LANES:
            rows.append(jnp.zeros((LANES - used, LANES), F32))
        return jnp.transpose(jnp.concatenate(rows, 0)).astype(BF16)

    def norm_back_fine(z, given, ref):
        mean, scale, level, slope = given

        def body(d, carry):
            for r in range(RB):
                p = d * RB + r
                v = scale * k_.du_f[p] + level + slope * (z[p] - mean)
                ref[core, 1 + d, 1 + r] = v.astype(BF16).astype(ref.dtype)
            return carry

        lax.fori_loop(0, S, body, 0)

    def turn_fine(ref):
        n = 4 if RB % 4 == 0 else 2

        def body(i, carry):
            d = lax.div(i, RB // n)
            r0 = (i - d * (RB // n)) * n
            for j in range(n):
                v = ref[core, 1 + d, 1 + r0 + j].astype(F32)
                at = pl.ds(pl.multiple_of((2 + r0 + j) * LANES, LANES), LANES)
                k_.dzt[d, at] = columns_first((from_right(v, W), v, from_left(v, W)), nx)
            return carry

        lax.fori_loop(0, S * RB // n, body, 0)

    def norm_back_coarse(z, given, ref):
        mean, scale, level, slope = given
        for i in range(Q):
            v = scale * k_.du_c[i] + level + slope * (z[i] - mean)
            ref[core, x, 1, i] = v.astype(BF16).astype(ref.dtype)

    def turn_coarse(ref):
        for i in range(Q):
            v = ref[core, x, 1, i].astype(F32)
            k_.dzct[V + i * LANES : V + (i + 1) * LANES] = columns_first((from_right(v, V), v, from_left(v, V)), 1)

    def keep_du(ref):
        def store(p, v):
            ref[p] = v

        return store

    barrier = pltpu.get_barrier_semaphore()

    def greet(depth, chan):
        pl.semaphore_signal(barrier, inc=1, device_id={"depth": depth, "chan": chan}, device_id_type=MESH)

    exchange(nd * nx, wide_peers, lambda depth, chan: types.SimpleNamespace(start=lambda: greet(depth, chan)))
    for t in range(nx):
        to = 2 * at_x(t)[0] + other
        greet(place, to)
        if t > 0:
            pl.when(no(first))(lambda to=to: greet(place - 1, to))
            pl.when(no(last))(lambda to=to: greet(place + 1, to))

    hc = iota((LANES, LANES), 0)
    fc = iota((LANES, LANES), 1)
    half = LANES // 2

    def up_table(coarse, fine):
        base = fine // 2
        beside = jnp.clip(base + jnp.where(fine % 2 == 0, -1, 1), 0, V - 1)
        near = (coarse == base).astype(F32)
        far = (coarse == beside).astype(F32)
        return (0.75 * near + 0.25 * far).astype(BF16)

    pool = jnp.concatenate([(hc // 2 == fc - at).astype(BF16) for at in (0, half)], 0)
    spread = jnp.concatenate([(hc - at == fc // 2).astype(BF16) for at in (0, half)], 1)
    up = jnp.concatenate([up_table(hc - at, fc) for at in (0, half)], 1)
    down = jnp.concatenate([up_table(fc, hc)] * 2, 0)
    spread2 = jnp.concatenate([spread, spread], 0)

    def take_rows(ref):
        for c in range(ref.shape[0]):
            k_.rows[c * S * R : (c + 1) * S * R] = ref[c].astype(F32).reshape(S * R, LANES)

    def row_of_all(p, chans):
        return k_.rows[pl.ds(p, chans, stride=S * R)]

    xp, xs, own_skip = k_.xp, k_.xs, k_.own_skip
    clear_halos(xp)
    take_rows(k_.skip)
    for i in range(S):
        for r in (0, R + 1):
            own_skip[i, r] = jnp.zeros((dm.cs, LANES), own_skip.dtype)

    def take_skip(i, carry):
        parts = []
        for d in range(S):
            v = [row_of_all(d * R + 4 * i + j, dm.cs).astype(BF16) for j in range(4)]
            for j in range(4):
                own_skip[d, 1 + 4 * i + j] = v[j].astype(own_skip.dtype)
            parts += [jnp.concatenate([v[j], v[2 + j]], 1) for j in range(2)]
        v = dot(jnp.concatenate(parts, 0), pool).reshape(2 * S, dm.cs, LANES)
        xp[core, x, 1, i] = (jnp.sum(v, axis=0) * 0.125).astype(BF16).astype(xp.dtype)
        return carry

    lax.fori_loop(0, Q, take_skip, 0, unroll=3)
    beside = jnp.where(first, 0, 1) + jnp.where(last, 0, 1)
    pl.semaphore_wait(barrier, nd * nx - 1 + nx + (nx - 1) * beside)
    gather_start(xp, "pooled")
    clear_halos(xs)
    xs[core, x, 1 : S + 1] = own_skip[:, pl.ds(row0, E)]
    gather_start(xs, "skip", lambda at, tox: own_skip.at[at, pl.ds(tox * RB, E)])

    gq = dm.g // nc
    columns = dm.enc_all + dm.skip_all
    gate_all, norm_all = k_.gate_all, k_.norm_all
    gate_all[me, :, 0:columns] = k_.gate[...]
    lane = iota((gq, LANES), 1)
    gate_all[me, :, 2 * LANES :] = jnp.where(
        lane == 0, column(k_.vector[0:1]), jnp.where(lane == 1, column(k_.vector[1:2]), 0.0)
    )
    for layer in range(2):
        for part in range(2):
            at = 2 * layer + part
            norm_all[me, at : at + 1, 0 : dm.cd] = k_.dn[part, layer : layer + 1]

    def constants(i, t, source, to):
        ref = (norm_all, gate_all)[i]
        return peer_copy(ref.at[source], ref.at[source], k_.v_send.at[i, t], k_.v_recv.at[i, t], place, to)

    for i in range(2):
        for t in range(1, nc):
            launch(None, functools.partial(constants, i, t, me, lax.rem(me + t, nc)))
    prepare(0)
    xd, xz4, xz3, d1 = k_.xd, k_.xz4, k_.xz3, k_.d1
    for ref in (xd, xz4, xz3):
        clear_rows(ref)
        clear_halos(ref)
    for ref in (k_.xh, k_.xz2, k_.xz1):
        clear_halos(ref)
    for i in range(S):
        for at in (0, (RB + 2) * LANES):
            k_.dzt[i, at : at + 2 * LANES] = jnp.zeros((2 * LANES, LANES), BF16)
        for r in range(3):
            k_.ug[i, r] = jnp.zeros(k_.ug.shape[2:], F32)
            k_.ug[i, RB + 3 + r] = jnp.zeros(k_.ug.shape[2:], F32)
        for r in range(H + 2):
            k_.cb[i, r] = jnp.zeros(k_.cb.shape[2:], F32)

    for at in (0, V + Q * LANES):
        k_.dzct[at : at + V] = jnp.zeros((V, LANES), BF16)

    def norm_of(layer):
        return column(k_.en[0, layer : layer + 1]), column(k_.en[1, layer : layer + 1])

    norm_e1, norm_e2 = norm_of(0), norm_of(1)

    gather_pass(xp, "pooled")
    gather_wait(xp, "pooled")
    coarse_sums(0, conv_stats_coarse(xp, wf[0], k_.z1, dm.ce))
    prepare(1)
    stats_e1 = moments(coarse_totals(0), dm.coarse_total)

    def keep_coarse(ref):
        def store(p, v):
            ref[core, x, 1, p] = v.astype(BF16).astype(ref.dtype)

        return store

    norm_rows(k_.z1, stats_e1, norm_e1, keep_coarse(k_.xh), Q)
    gather_start(k_.xh, "hidden")
    prepare(2)
    forward_start(2)
    gather_pass(k_.xh, "hidden")
    gather_pass(xs, "skip")
    gather_wait(k_.xh, "hidden")
    coarse_sums(1, conv_stats_coarse(k_.xh, wf[1], k_.z2, dm.ce))
    take_rows(k_.cot)

    def take_cot(i, carry):
        for d in range(S):
            for j in range(4):
                v = row_of_all(d * R + 4 * i + j, dm.cd).astype(BF16)
                k_.own_cot[d, 4 * i + j] = v.astype(k_.own_cot.dtype)
        return carry

    lax.fori_loop(0, Q, take_cot, 0)
    k_.cots[x] = k_.own_cot[:, pl.ds(row0, RB)]
    stats_e2 = moments(coarse_totals(1), dm.coarse_total)
    norm_rows(k_.z2, stats_e2, norm_e2, keep_coarse(k_.xc), Q)
    gather_start(k_.xc, "coarse")
    prepare(3)
    for t in range(1, nc):
        for i in range(2):
            source = lax.rem(me + nc - t, nc)
            constants(i, t, source, source).wait_recv()
    gate_full = gate_all[...].reshape(dm.g, 3 * LANES)
    wg = gate_full[:, 0:columns].astype(BF16)
    gbias = gate_full[:, 2 * LANES : 2 * LANES + 1]
    gout = gate_full[:, 2 * LANES + 1 : 2 * LANES + 2]
    k_.gate_t[...] = jnp.transpose(gate_full[:, 0 : 2 * LANES])
    own_rows = [k_.gate_t[pl.ds(pl.multiple_of((2 * i + core) * dm.ce, dm.ce), dm.ce)] for i in range(nx)]
    own_rows += [
        k_.gate_t[pl.ds(pl.multiple_of(dm.enc_all + (2 * i + core) * dm.cs, dm.cs), dm.cs)] for i in range(nx)
    ]
    k_.gate_own[...] = jnp.concatenate(own_rows, 0)

    def norm_fine(layer):
        return tuple(
            jnp.concatenate(
                [column(norm_all[2 * i + core, 2 * layer + part : 2 * layer + part + 1, 0 : dm.cd]) for i in range(nx)], 0
            )
            for part in range(2)
        )

    norm_d1, norm_d2 = norm_fine(0), norm_fine(1)
    gather_pass(k_.xc, "coarse")
    gather_wait(k_.xc, "coarse")
    forward_start(3)

    dt = k_.dt

    def up_depth(i, carry):
        t = []
        for j in range(3):
            v = dot(flat(k_.xc, j, i), up)
            t.append(jnp.stack([v[:, 0:LANES], v[:, LANES:]], 0))
        below = jnp.where(first, t[1], t[0])
        above = jnp.where(last, t[1], t[2])
        near = 0.75 * t[1]
        here = 0.25 * t[1]
        rows = pl.ds(i * 2, 2)
        dt[0, rows] = jnp.where(first, 0.0, 0.75 * below + here)
        dt[1, rows] = near + 0.25 * below
        dt[2, rows] = near + 0.25 * above
        dt[3, rows] = jnp.where(last, 0.0, 0.75 * above + here)
        return carry

    lax.fori_loop(0, Q, up_depth, 0)

    def up_rows(i, carry):
        here = h0 + i
        before, after = jnp.maximum(here - 1, 0), jnp.minimum(here + 1, H - 1)
        for j in range(S + 2):
            v = 0.75 * dt[j, here]
            d1[j, 1 + 2 * i, 0 : dm.enc_all] = (v + 0.25 * dt[j, before]).astype(BF16)
            d1[j, 2 + 2 * i, 0 : dm.enc_all] = (v + 0.25 * dt[j, after]).astype(BF16)
        return carry

    lax.fori_loop(0, RB // 2, up_rows, 0)
    for edge, at, near, far in (
        (top, 0, jnp.maximum(h0 - 1, 0), h0),
        (bottom, E - 1, jnp.minimum(h0 + RB // 2, H - 1), h0 + RB // 2 - 1),
    ):
        for j in range(S + 2):
            v = jnp.where(edge, 0.0, 0.75 * dt[j, near] + 0.25 * dt[j, far])
            d1[j, at, 0 : dm.enc_all] = v.astype(BF16)
    for t in range(1, nx):
        tox = lax.rem(x + t, nx)

        def send_cot(t=t, tox=tox):
            return peer_copy(
                k_.own_cot.at[:, pl.ds(tox * RB, RB)], k_.cots.at[x], k_.o_send.at[0, t], k_.o_recv.at[0, t],
                place, 2 * tox + core,
            )

        launch(None, send_cot)

    gather_wait(xs, "skip")
    gate_n = E // 2

    def gate(i, carry):
        j = lax.div(i, 2)
        r0 = (i - 2 * j) * gate_n
        skips = [flat(xs, j, r0 + q) for q in range(gate_n)]
        v = jnp.concatenate(
            [
                jnp.concatenate([d1[j, r0 + q, 0 : dm.enc_all] for q in range(gate_n)], 1),
                jnp.concatenate(skips, 1),
            ],
            0,
        )
        pre = dot(wg, v) + gbias
        act = pre * jax.nn.sigmoid(pre)
        alpha = jax.nn.sigmoid(jnp.sum(gout * act, axis=0, keepdims=True))
        for q in range(gate_n):
            lanes = slice(q * LANES, (q + 1) * LANES)
            d1[j, r0 + q, dm.enc_all :] = (alpha[:, lanes] * skips[q].astype(F32)).astype(BF16)
            k_.pre[j, r0 + q] = pre[:, lanes]
            k_.alpha[j, r0 + q] = alpha[:, lanes]
        return carry

    lax.fori_loop(0, (S + 2) * 2, gate, 0)
    for k in (3, 2, 1, 0):
        weights_start(k)

    def row_d1(j, r):
        return d1[j, r]

    def row_xd(j, r):
        return natural(xd, j, r)

    forward_wait(2)
    fine_sums(0, conv_stats(row_d1, forward_weight(2), k_.z3))
    drain()
    forward_wait(3)
    stats_d1 = moments(fine_totals(0), dm.fine_total)

    def keep_dec(p, v):
        d = lax.div(p, RB)
        xd[core, 1 + d, 1 + p - d * RB] = v.astype(BF16).astype(xd.dtype)

    norm_rows(k_.z3, stats_d1, norm_d1, keep_dec, RB)
    fine_start(xd, "hidden")
    for t in range(1, nx):
        fromx = lax.rem(x + nx - t, nx)
        theirs = k_.cots.at[fromx]
        peer_copy(theirs, theirs, k_.o_send.at[0, t], k_.o_recv.at[0, t], place, 2 * fromx + core).wait_recv()
    fine_pass(xd, "hidden")
    weights_finish(3)
    fine_wait(xd, "hidden")
    fine_sums(1, conv_stats(row_xd, forward_weight(3), k_.z4))
    stats_d2 = moments(fine_totals(1), dm.fine_total)

    def row_cot(p):
        d = lax.div(p, RB)
        return jnp.concatenate([k_.cots[i, d, p - d * RB] for i in range(nx)], 0).astype(F32)

    fine_sums(2, norm_back_sums(k_.z4, keep_du(k_.du_f), stats_d2, norm_d2, row_cot, RB))

    def keep_result(p, v):
        for i in range(nx):
            k_.ob[i, p] = v[i * dm.cd : (i + 1) * dm.cd].astype(BF16).astype(k_.ob.dtype)

    norm_rows(k_.z4, stats_d2, norm_d2, keep_result, RB)
    for t in range(1, nx):
        tox = lax.rem(x + t, nx)

        def send_result(t=t, tox=tox):
            return peer_copy(
                k_.ob.at[tox], k_.oi.at[x], k_.o_send.at[1, t], k_.o_recv.at[1, t], place, 2 * tox + core
            )

        launch(None, send_result)
    total_d2 = fine_totals(2)
    norm_back_fine(k_.z4, back_factors(stats_d2, norm_d2, total_d2, dm.fine_total), xz4)
    fine_start(xz4, "dz4")
    turn_fine(xz4)
    weight_grad(row_xd, 3)
    fine_pass(xz4, "dz4")
    cross_start(3)
    fine_wait(xz4, "dz4")

    def keep_grad(d, results, carry):
        for j, v in enumerate(results):
            k_.gg[d * RB + j] = v
        return carry

    conv(blocks_of(xz4), wb[3][...], dm.cf, 1, keep_grad, 0)
    fine_sums(3, norm_back_sums(k_.z3, keep_du(k_.du_f), stats_d1, norm_d1, lambda p: k_.gg[p], RB))
    cross_finish(3)
    total_d1 = fine_totals(3)
    norm_back_fine(k_.z3, back_factors(stats_d1, norm_d1, total_d1, dm.fine_total), xz3)
    fine_start(xz3, "dz3")
    turn_fine(xz3)
    weights_finish(2)
    weight_grad(row_d1, 2)
    fine_pass(xz3, "dz3")
    cross_start(2)
    fine_wait(xz3, "dz3")

    ups = nx * dm.ce

    def gate_back(d, results, carry):
        bias, psi = carry
        lows = []
        for j, both in enumerate(results):
            p = d * RB + j
            v = both[ups:]
            grad = jnp.sum(v * flat(xs, d + 1, 1 + j).astype(F32), axis=0, keepdims=True)
            alpha = k_.alpha[d + 1, 1 + j]
            logit = grad * alpha * (1.0 - alpha)
            pre = k_.pre[d + 1, 1 + j]
            sigma = jax.nn.sigmoid(pre)
            psi = psi + pre * sigma * logit
            low = (logit * gout * sigma * (1.0 + pre * (1.0 - sigma))).astype(BF16)
            bias = bias + low.astype(F32)
            k_.pg[p] = low
            lows.append(low)
            k_.ug[d, 3 + j] = both[0:ups]
            for i in range(nc):
                k_.gv[i] = v[i * dm.cs : (i + 1) * dm.cs]
            for i in range(nx):
                k_.sgp[i, p] = alpha * k_.gv[2 * i + core]
        back = dot(k_.gate_own[...].astype(BF16), jnp.concatenate(lows, 1))
        for j in range(len(results)):
            p = d * RB + j
            lanes = slice(j * LANES, (j + 1) * LANES)
            k_.ug[d, 3 + j] += back[0:ups, lanes]
            for i in range(nx):
                v = k_.sgp[i, p] + back[ups + i * dm.cs : ups + (i + 1) * dm.cs, lanes]
                k_.sgp[i, p] = v
                k_.sgb[i, p] = v.astype(BF16).astype(k_.sgb.dtype)
        return bias, psi

    blank = jnp.zeros((dm.g, LANES), F32)
    bias, psi = conv(blocks_of(xz3), wb[2][...], ups + dm.skip_all, 1, gate_back, (blank, blank))

    ug, cb, cg = k_.ug, k_.cb, k_.cg
    for q in range(RB // 2 + 2):
        terms = []
        for d in range(S):
            v = 0.75 * (ug[d, 2 * q + 1] + ug[d, 2 * q + 2]) + 0.25 * (ug[d, 2 * q + 3] + ug[d, 2 * q])
            if q == 1:
                v += jnp.where(top, 0.25 * ug[d, 3], 0.0)
            if q == RB // 2:
                v += jnp.where(bottom, 0.25 * ug[d, RB + 2], 0.0)
            terms.append(split(v))
        v = dot(jnp.concatenate(terms, 0), down)
        for d in range(S):
            cb[d, h0 + q] = v[d * ups : (d + 1) * ups]

    def to_slabs(i, carry):
        even, odd = (cb[d, 2 * i + 1] + pltpu.roll(cb[d, 2 * i + 2], half, 1) for d in range(S))
        middle = 0.75 * (even + odd) + jnp.where(first, 0.25 * even, 0.0) + jnp.where(last, 0.25 * odd, 0.0)
        for part, v in enumerate((0.25 * even, middle, 0.25 * odd)):
            for j in range(nx):
                block = v[j * dm.ce : (j + 1) * dm.ce]
                k_.fs[part, j, i] = block.astype(BF16).astype(k_.fs.dtype)
                if part == 1:
                    k_.fm[j, i] = block
        return carry

    lax.fori_loop(0, Q, to_slabs, 0)

    def fold_parts():
        for step in (-1, 1, 0):
            sends = (no(first), None, no(last))[step + 1]
            gets = (no(last), None, no(first))[step + 1]
            for t in range(nx):
                if (step, t) != (0, 0):
                    tox, fromx = lax.rem(x + t, nx), lax.rem(x + nx - t, nx)
                    sems = (k_.f_send.at[step + 1, t], k_.f_recv.at[step + 1, t])
                    theirs = k_.fr.at[step + 1, fromx]
                    yield (
                        sends, gets, fromx, step + 1,
                        functools.partial(
                            peer_copy, k_.fs.at[step + 1, tox], k_.fr.at[step + 1, x], *sems, place + step, 2 * tox + core
                        ),
                        functools.partial(peer_copy, theirs, theirs, *sems, place, 2 * fromx + core),
                    )

    for sends, _, _, _, out, _ in fold_parts():
        launch(sends, out)
    for t in range(1, nx):
        tox = lax.rem(x + t, nx)

        def send_skip(t=t, tox=tox):
            return peer_copy(
                k_.sgb.at[tox], k_.sgi.at[x], k_.o_send.at[2, t], k_.o_recv.at[2, t], place, 2 * tox + core
            )

        launch(None, send_skip)

    k_.gw[...] = jnp.zeros(k_.gw.shape, F32)

    def gate_weight(d, carry):
        v = jnp.concatenate(
            [
                jnp.concatenate([d1[1 + d, 1 + j, 0 : dm.enc_all] for j in range(RB)], 1),
                jnp.concatenate([flat(xs, 1 + d, 1 + j) for j in range(RB)], 1),
            ],
            0,
        )
        y = jnp.concatenate([k_.pg[d * RB + j] for j in range(RB)], 1)
        k_.gw[0:columns, 0 : dm.g] += dot_nt(v, y)
        return carry

    lax.fori_loop(0, S, gate_weight, 0)
    gate_grad = jnp.transpose(k_.gw[...])
    lane = iota((dm.g, LANES), 1)
    vectors = jnp.where(
        lane == 0,
        jnp.sum(bias, axis=1, keepdims=True),
        jnp.where(lane == 1, jnp.sum(psi, axis=1, keepdims=True), 0.0),
    )
    gate_block = k_.gate_block
    for j in range(nc):
        mine = slice(j * gq, (j + 1) * gq)
        gate_block[j, :, 0 : 2 * LANES] = gate_grad[mine]
        gate_block[j, :, 2 * LANES :] = vectors[mine]
    sum_start(everyone, k_.sv, 4, 0, gate_block[me], lambda chan: gate_block.at[chan])
    cg[...] = k_.fm[x]
    for _, gets, fromx, part, _, back in fold_parts():

        def fold_in(back=back, part=part, fromx=fromx):
            back().wait_recv()
            cg[...] += k_.fr[part, fromx].astype(F32)

        guarded(gets, fold_in)

    coarse_sums(2, norm_back_sums(k_.z2, keep_du(k_.du_c), stats_e2, norm_e2, lambda p: cg[p], Q))
    cross_finish(2)
    weights_finish(1)
    total_e2 = coarse_totals(2)
    norm_back_coarse(k_.z2, back_factors(stats_e2, norm_e2, total_e2, dm.coarse_total), k_.xz2)
    gather_start(k_.xz2, "dz2")
    turn_coarse(k_.xz2)
    weight_grad_coarse(k_.xh, 1)
    reduce_finish(3)
    gather_pass(k_.xz2, "dz2")
    reduce_start(1)
    weights_finish(0)
    drain()
    gather_wait(k_.xz2, "dz2")
    for i, v in enumerate(conv_coarse(k_.xz2, wb[1], dm.ce)):
        cg[i] = v
    coarse_sums(3, norm_back_sums(k_.z1, keep_du(k_.du_c), stats_e1, norm_e1, lambda p: cg[p], Q))
    reduce_finish(2)
    total_e1 = coarse_totals(3)
    norm_back_coarse(k_.z1, back_factors(stats_e1, norm_e1, total_e1, dm.coarse_total), k_.xz1)
    gather_start(k_.xz1, "dz1")
    turn_coarse(k_.xz1)
    weight_grad_coarse(xp, 0)
    reduce_start(0)
    reduce_finish(1)
    gather_pass(k_.xz1, "dz1")
    gradient_out(3)

    def rows_out(ref, own, theirs, kind, size):
        def copy_rows(read, at):
            def body(d, carry):
                for r in range(RB):
                    p = (d * R + at * RB + r) * size
                    ref[pl.ds(pl.multiple_of(p, size), size)] = read(d * RB + r).astype(F32)
                return carry

            lax.fori_loop(0, S, body, 0)

        copy_rows(lambda p: own[x, p], x)
        for t in range(1, nx):
            fromx = lax.rem(x + nx - t, nx)
            block = theirs.at[fromx]
            peer_copy(block, block, k_.o_send.at[kind, t], k_.o_recv.at[kind, t], place, 2 * fromx + core).wait_recv()
            copy_rows(lambda p, fromx=fromx: theirs[fromx, p], fromx)

    rows_out(k_.out, k_.ob, k_.oi, 1, dm.cd)
    rows_out(k_.sg, k_.sgp, k_.sgi, 2, dm.cs)
    gather_wait(k_.xz1, "dz1")
    for i, v in enumerate(conv_coarse(k_.xz1, wb[0], dm.cs)):
        v = dot(split(v), spread2) * 0.125
        for j in range(4):
            part = v[:, (j // 2) * LANES : (j // 2 + 1) * LANES]
            for d in range(S):
                at = (d * R + 4 * i + j) * dm.cs
                k_.sg[at : at + dm.cs] += part
    reduce_finish(0)
    gradient_out(2)
    gradient_out(1)
    gate_total = sum_finish(everyone, k_.sv, 4, 0)
    k_.ggate[...] = gate_total[:, 0:columns]
    k_.gvector[0:1] = row_of(gate_total[:, 2 * LANES : 2 * LANES + 1])
    k_.gvector[1:2] = row_of(gate_total[:, 2 * LANES + 1 : 2 * LANES + 2])

    def own_part(col):
        parts = [jnp.where(x == i, col[i * dm.cd : (i + 1) * dm.cd], 0.0) for i in range(nx)]
        return functools.reduce(jnp.add, parts)

    for ref, pair, pick in ((k_.gen, (total_e1, total_e2), lambda v: v), (k_.gdn, (total_d1, total_d2), own_part)):
        for layer, total in enumerate(pair):
            ref[0, layer : layer + 1] = row_of(pick(total[1]))
            ref[1, layer : layer + 1] = row_of(pick(total[0]))
    gradient_out(0)
    drain()


def adamw(weight, grad, moment, square, rate):
    new_moment = 0.9 * moment + 0.1 * grad
    new_square = 0.999 * square + 0.001 * grad * grad
    moment_hat = new_moment / (1.0 - 0.9**STEP)
    square_hat = new_square / (1.0 - 0.999**STEP)
    new_weight = weight - rate * (moment_hat / (jnp.sqrt(square_hat) + 1e-08) + 0.01 * weight)
    return (new_weight, new_moment, new_square)


RATES = (CONV_RATE, CONV_RATE, GATE_RATE, VECTOR_RATE, CONV_RATE, CONV_RATE, VECTOR_RATE, VECTOR_RATE)


def update_kernel(*refs):
    n = len(RATES)
    sources, targets = refs[: 2 + 4 * n], refs[2 + 4 * n : 4 + 7 * n]
    inside, outside = refs[4 + 7 * n : 6 + 11 * n], refs[6 + 11 * n : 8 + 14 * n]
    in_sem, out_sem = refs[8 + 14 * n :]
    order = (4, 1, 0, 5, 2, 3, 6, 7)

    def load(i):
        return pltpu.make_async_copy(sources[i], inside[i], in_sem.at[i])

    def store(i):
        return pltpu.make_async_copy(outside[i], targets[i], out_sem.at[i])

    for i in (1, 0):
        load(i).start()
    for k in order:
        for part in range(4):
            load(2 + part * n + k).start()
    for i in (1, 0):
        load(i).wait()
        chans, (slabs, rows) = outside[i].shape[0], outside[i].shape[1:3]
        for c in range(chans):
            v = inside[i][pl.ds(c, slabs * rows, stride=chans)]
            outside[i][c] = v.reshape(slabs, rows, LANES).astype(outside[i].dtype)
        store(i).start()
    for k in order:
        own = [2 + part * n + k for part in range(4)]
        for i in own:
            load(i).wait()
        rows = inside[own[0]].shape[0]
        step = 8 if rows % 8 == 0 and rows > 8 else rows
        for r in range(0, rows, step):
            at = slice(r, r + step)
            new = adamw(*(inside[i][at] for i in own), RATES[k])
            for part, value in enumerate(new):
                outside[2 + 3 * k + part][at] = value
        for part in range(3):
            store(2 + 3 * k + part).start()
    for i in range(len(targets)):
        store(i).wait()


def per_device(
    skip, cotangent, enc_conv1, enc_conv2, gate_proj, gate_vector, dec_conv1, dec_conv2, enc_norms, dec_norms, *states
):
    nd, nc = lax.axis_size("depth"), lax.axis_size("chan")
    dm = Dims(nd, nc, skip.shape, enc_conv1.shape[0], dec_conv1.shape[0], gate_proj.shape[0] * nc)
    S, R, H, nx, RB, E = dm.s, dm.rows, dm.half, dm.nx, dm.rb, dm.ext
    Q = H // 2
    cin3 = dm.enc_all + dm.skip_all

    def own_block(size):
        return (size, lambda j: pl.multiple_of(j * size, size), 0)

    def core_blocks(size):
        return tuple(
            (size, lambda j, i=i: pl.multiple_of((2 * i + lax.rem(j, 2)) * size, size), i * size) for i in range(nx)
        )

    dm.convs = convs = (
        Conv(dm, dm.ce, dm.skip_all, (own_block(dm.cs),)),
        Conv(dm, dm.ce, dm.enc_all, (own_block(dm.ce),)),
        Conv(dm, dm.cd, cin3, core_blocks(dm.ce) + ((dm.skip_all, lambda j: dm.enc_all, nx * dm.ce),)),
        Conv(dm, dm.cd, dm.dec_all, core_blocks(dm.cd)),
    )
    params = (enc_conv1, enc_conv2, gate_proj, gate_vector, dec_conv1, dec_conv2, enc_norms, dec_norms)
    inputs = dict(
        skip=skip, cot=cotangent, w0=enc_conv1, w1=enc_conv2, w2=dec_conv1, w3=dec_conv2,
        gate=gate_proj, vector=gate_vector, en=enc_norms, dn=dec_norms,
    )
    shape = jax.ShapeDtypeStruct
    outs = dict(
        out=shape((S * R * dm.cd, LANES), F32),
        sg=shape((S * R * dm.cs, LANES), F32),
        **{f"g{i}": shape(a.shape, F32) for i, a in enumerate((enc_conv1, enc_conv2, dec_conv1, dec_conv2))},
        **{
            name: shape(a.shape, F32)
            for name, a in (("ggate", gate_proj), ("gvector", gate_vector), ("gen", enc_norms), ("gdn", dec_norms))
        },
    )
    gq = dm.g // nc

    def coarse(block):
        return pltpu.VMEM((2, nx, 3, Q, block, LANES), storage(block))

    def fine():
        return pltpu.VMEM((2, S + 2, E, dm.cf, LANES), storage(dm.cd))

    def f32(*dims):
        return pltpu.VMEM((*dims, LANES), F32)

    def tiles(*dims):
        return pltpu.VMEM((*dims, 16, LANES), BF16)

    def blocks(block, *dims):
        return pltpu.VMEM((*dims, block, LANES), storage(block))

    def sems(*dims):
        return pltpu.SemaphoreType.DMA(dims)

    scratch = dict(
        xp=coarse(dm.cs), xh=coarse(dm.ce), xc=coarse(dm.ce), xz2=coarse(dm.ce), xz1=coarse(dm.ce),
        own_skip=blocks(dm.cs, S, R + 2), xs=blocks(dm.cs, 2, nx, S + 2, E),
        own_cot=blocks(dm.cd, S, R), cots=blocks(dm.cd, nx, S, RB),
        d1=pltpu.VMEM((S + 2, E, cin3, LANES), BF16), xd=fine(), xz4=fine(), xz3=fine(),
        z1=f32(Q, dm.ce), z2=f32(Q, dm.ce), z3=f32(S * RB, dm.cf), z4=f32(S * RB, dm.cf),
        du_c=f32(Q, dm.ce), du_f=f32(S * RB, dm.cf), gg=f32(S * RB, dm.cf), cg=f32(Q, dm.ce),
        pre=f32(S + 2, E, dm.g), alpha=f32(S + 2, E, 1), pg=pltpu.VMEM((S * RB, dm.g, LANES), BF16),
        ug=f32(S, RB + 6, nx * dm.ce), cb=f32(S, H + 2, nx * dm.ce), dt=f32(S + 2, H, dm.enc_all),
        gv=f32(nc, dm.cs), sgp=f32(nx, S * RB, dm.cs), sgb=blocks(dm.cs, nx, S * RB), sgi=blocks(dm.cs, nx, S * RB),
        ob=blocks(dm.cd, nx, S * RB), oi=blocks(dm.cd, nx, S * RB),
        dzt=pltpu.VMEM((S, (RB + 4) * LANES, LANES), BF16), dzct=pltpu.VMEM((Q * LANES + 2 * dm.hcols, LANES), BF16),
        gw=f32(2 * LANES),
        fs=blocks(dm.ce, 3, nx, Q), fr=blocks(dm.ce, 3, nx, Q), fm=f32(nx, Q, dm.ce),
        st=f32(4, nd, 1), su=f32(4, nd * nx, 1), sv=pltpu.VMEM((1, nd * nx, gq, 3 * LANES), F32),
        norm_all=f32(nc, 8), rows=f32(max(dm.cs, dm.cd) * S * R),
        turned=f32(max(cv.chunks for cv in convs) * LANES),
        acc=pltpu.VMEM((max(3 * cv.c for cv in convs), 3 * LANES), F32),
        gate_all=pltpu.VMEM((nc, gq, 3 * LANES), F32), gate_t=pltpu.VMEM((2 * LANES, dm.g), F32),
        gate_own=pltpu.VMEM((nx * (dm.ce + dm.cs), dm.g), F32), gate_block=pltpu.VMEM((nc, gq, 3 * LANES), F32),
        **{f"wt{i}": pltpu.VMEM((3, cv.c, cv.wide), cv.kind) for i, cv in enumerate(convs)},
        **{
            f"wf{i}": pltpu.VMEM((cv.taps, 3 * cv.c) if i < 2 else (nx, cv.stored, 9 * cv.c), BF16)
            for i, cv in enumerate(convs)
        },
        **{f"wx{i}": pltpu.VMEM((nc, 3, cv.needed, cv.wide), cv.kind) for i, cv in enumerate(convs)},
        **{
            f"wb{i}": pltpu.VMEM((9 * cv.needed, 3 * nc * cv.o) if i < 2 else (3 * cv.needed, 9 * nc * cv.o), BF16)
            for i, cv in enumerate(convs)
        },
        flip=pltpu.VMEM((max(cv.tiles for cv in convs[2:]) * LANES, max(3 * cv.c for cv in convs[2:])), F32),
        **{f"gt{i}": tiles(cv.share * nd) for i, cv in enumerate(convs)},
        **{f"gr{i}": tiles(nd, cv.share) for i, cv in enumerate(convs)},
        **{f"ga{i}": tiles(cv.share * nd) for i, cv in enumerate(convs)},
        **{f"gs{i}": tiles(convs[i].count) for i in (2, 3)},
        **{f"gx{i}": tiles(nx, convs[i].count) for i in (2, 3)},
        g_send=sems(len(GATHERS), 3, nx), g_recv=sems(len(GATHERS), 3),
        h_send=sems(len(GATHERS), 2 + nx), h_recv=sems(len(GATHERS)),
        x_send=sems(len(FINE), 3, 5), x_recv=sems(len(FINE), 3, 5),
        y_send=sems(len(FINE), 3), y_recv=sems(len(FINE), 3),
        t_send=sems(4), t_recv=sems(4), u_send=sems(5), u_recv=sems(5),
        f_send=sems(3, nx), f_recv=sems(3, nx), w_send=sems(4, nx + 1, nc), w_recv=sems(4, nx + 1, nc),
        p_send=sems(2, nx), p_recv=sems(2, nx), c_send=sems(2, nx), c_recv=sems(2, nx),
        o_send=sems(3, nx), o_recv=sems(3, nx), v_send=sems(2, nc), v_recv=sems(2, nc),
        r_send=sems(4), r_recv=sems(4), a_send=sems(4), a_recv=sems(4),
    )
    vmem = pl.BlockSpec(memory_space=pltpu.VMEM)
    out, sg, grad1, grad2, grad3, grad4, ggate, gvector, gen, gdn = pl.pallas_call(
        functools.partial(kernel, dm, (*inputs, *outs, *scratch)),
        out_shape=tuple(outs.values()),
        in_specs=[vmem] * len(inputs),
        out_specs=[vmem] * len(outs),
        scratch_shapes=list(scratch.values()),
        compiler_params=pltpu.CompilerParams(
            has_side_effects=True, collective_id=0, vmem_limit_bytes=60 * 1024 * 1024
        ),
        name="step",
    )(*inputs.values())
    grads = (grad1, grad2, ggate, gvector, grad3, grad4, gen, gdn)
    operands = (out, sg, *params, *grads, *states)
    updated = (
        shape(cotangent.shape, BF16),
        shape(skip.shape, F32),
        *(shape(p.shape, F32) for p in params for _ in range(3)),
    )
    anywhere = pl.BlockSpec(memory_space=pl.ANY)
    return pl.pallas_call(
        update_kernel,
        out_shape=updated,
        in_specs=[anywhere] * len(operands),
        out_specs=[anywhere] * len(updated),
        scratch_shapes=[
            *(pltpu.VMEM(a.shape, a.dtype) for a in operands),
            *(pltpu.VMEM(a.shape, a.dtype) for a in updated),
            pltpu.SemaphoreType.DMA((len(operands),)),
            pltpu.SemaphoreType.DMA((len(updated),)),
        ],
        compiler_params=pltpu.CompilerParams(vmem_limit_bytes=60 * 1024 * 1024),
        name="update",
    )(*operands)


def solution(mesh):
    volume = P("chan", "depth", None, None)
    row, column, norms = P("chan", None), P(None, "chan"), P(None, None, "chan")
    params = (row, row, row, column, row, row, norms, norms)
    return jax.shard_map(
        per_device,
        mesh=mesh,
        in_specs=(volume, volume) + params * 3,
        out_specs=(volume, volume) + tuple(spec for spec in params for _ in range(3)),
        check_vma=False,
    )
```

```python
import functools
import types

import jax
import jax.numpy as jnp
from jax import lax
from jax.experimental import pallas as pl
from jax.experimental.pallas import tpu as pltpu
from jax.sharding import PartitionSpec as P

STEP = 5
EPS = 1e-05
CONV_RATE = 0.03
GATE_RATE = 0.1
VECTOR_RATE = 0.5
LANES = 128
MESH = pl.DeviceIdType.MESH
F32 = jnp.float32
BF16 = jnp.bfloat16


def iota(shape, dim):
    return lax.broadcasted_iota(jnp.int32, shape, dim)


def dot(a, b):
    return jnp.dot(a, b, preferred_element_type=F32)


def dot_nt(a, b):
    return lax.dot_general(a, b, (((1,), (1,)), ((), ())), preferred_element_type=F32)


def dot_tn(a, b):
    return lax.dot_general(a, b, (((0,), (0,)), ((), ())), preferred_element_type=F32)


def from_left(v, width):
    return jnp.where(iota(v.shape, 1) % width == 0, 0.0, pltpu.roll(v, 1, 1))


def from_right(v, width):
    return jnp.where(iota(v.shape, 1) % width == width - 1, 0.0, pltpu.roll(v, LANES - 1, 1))


def halves(low, high):
    return pltpu.roll(jnp.where(iota(low.shape, 1) < LANES // 2, low, high), LANES // 2, 1)


def split(v):
    high = v.astype(BF16)
    return jnp.concatenate([high, (v - high.astype(F32)).astype(BF16)], 1)


def storage(block):
    return BF16 if block % 16 == 0 else F32


def flat(ref, s, r):
    if len(ref.shape) == 4:
        return ref[s, r]
    v = ref[:, :, s, r]
    return jnp.concatenate([v[c, i] for i in range(v.shape[1]) for c in range(2)], 0).astype(BF16)


class Dims:
    def __init__(self, nd, nc, skip, enc, dec, gate):
        self.nd, self.nc, self.nx = nd, nc, nc // 2
        self.s, self.rows, self.cols = skip[1:]
        self.cs, self.ce, self.cd, self.g = skip[0], enc, dec, gate
        self.half, self.hcols = self.rows // 2, self.cols // 2
        self.fine_total = nd * self.s * self.rows * self.cols
        self.coarse_total = self.fine_total // 8
        self.enc_all = nc * enc
        self.skip_all = nc * skip[0]
        self.dec_all = nc * dec
        self.rb = self.rows // self.nx
        self.ext = self.rb + 2
        self.cf = self.nx * dec


GATHERS = ("pooled", "skip", "hidden", "coarse", "dz2", "dz1")
FINE = ("hidden", "dz4", "dz3")


class Conv:
    def __init__(self, dm, o, c, blocks):
        self.o, self.c, self.blocks = o, c, blocks
        self.length = 27 * c
        self.chunks = -(-self.length // LANES)
        self.per = LANES // o
        self.tiles = -(-9 // self.per)
        self.wide = self.tiles * LANES
        self.kind = storage(min(size for size, _, _ in blocks))
        self.needed = sum(size for size, _, _ in blocks)
        self.full = max(1, 9 // self.per)
        self.left = max(0, 9 - self.full * self.per)
        self.group = 3 * self.full + (self.left > 0)
        self.count = c // 16 * self.group
        self.share = -(-self.count // dm.nd)
        self.taps = 9 * o
        self.stored = -(-3 * o // 16) * 16


def kernel(dm, names, *refs):
    k_ = types.SimpleNamespace(**dict(zip(names, refs)))
    nd, nc, nx, S, R, H = dm.nd, dm.nc, dm.nx, dm.s, dm.rows, dm.half
    W, V = dm.cols, dm.hcols
    Q, RB, E = H // 2, dm.rb, dm.ext
    place = lax.axis_index("depth")
    me = lax.axis_index("chan")
    x, core = lax.div(me, 2), lax.rem(me, 2)
    other = 1 - core
    mate = 2 * x + other
    row0, h0 = x * RB, x * (RB // 2)
    first, last = place == 0, place == nd - 1
    top, bottom = x == 0, x == nx - 1
    convs = dm.convs
    pending = []
    wt, wf, wx, wb = ([getattr(k_, f"{kind}{i}") for i in range(4)] for kind in ("wt", "wf", "wx", "wb"))
    gt, gr, ga = ([getattr(k_, f"{kind}{i}") for i in range(4)] for kind in ("gt", "gr", "ga"))
    weights = (k_.w0, k_.w1, k_.w2, k_.w3)
    grads = (k_.g0, k_.g1, k_.g2, k_.g3)
    turned, acc = k_.turned, k_.acc

    def no(cond):
        return jnp.logical_not(cond)

    def peer_copy(src, dst, send, recv, depth, chan):
        return pltpu.make_async_remote_copy(
            src_ref=src, dst_ref=dst, send_sem=send, recv_sem=recv,
            device_id={"depth": depth, "chan": chan}, device_id_type=MESH,
        )

    def guarded(cond, fn):
        if cond is None:
            fn()
        else:
            pl.when(cond)(fn)

    def drain():
        for cond, fn in pending:
            guarded(cond, fn)
        pending.clear()

    def launch(cond, copy):
        guarded(cond, lambda: copy().start())
        pending.append((cond, lambda: copy().wait_send()))

    def arrive(cond, copy):
        guarded(cond, lambda: copy().wait_recv())

    def both(a, b):
        return b if a is None else a if b is None else jnp.logical_and(a, b)

    can_send = (no(last), None, no(first))
    can_recv = (no(first), None, no(last))

    def slices(side, n):
        return (pl.ds(n, 1), pl.ds(1, n), pl.ds(1, 1))[side], (pl.ds(0, 1), pl.ds(1, n), pl.ds(n + 1, 1))[side]

    def at_x(t):
        up, down = x + t, x - t
        return jnp.where(up >= nx, up - nx, up), jnp.where(down < 0, down + nx, down)


    def gather_start(ref, which, source_at=None):
        n = ref.shape[2] - 2
        k = GATHERS.index(which)
        for side in (0, 2, 1):
            own, theirs = slices(side, n)
            for t in range(nx):
                if side == 1 and t == 0:
                    continue
                tox = at_x(t)[0]

                def copy(side=side, t=t, own=own, theirs=theirs, tox=tox):
                    start = (n, 1, 1)[side] - 1
                    size = (1, n, 1)[side]
                    src = ref.at[core, x, own] if source_at is None else source_at(pl.ds(start, size), tox)
                    return peer_copy(
                        src, ref.at[core, x, theirs], k_.g_send.at[k, side, t], k_.g_recv.at[k, side],
                        place + 1 - side, 2 * tox + core,
                    )

                launch(can_send[side], copy)
        gather_own(ref, which)

    def handed(ref, k, piece, i):
        return peer_copy(piece, piece, k_.h_send.at[k, i], k_.h_recv.at[k], place, mate)

    def gather_own(ref, which):
        k = GATHERS.index(which)
        launch(None, lambda: handed(ref, k, ref.at[core, x, pl.ds(1, ref.shape[2] - 2)], 0))

    def gather_pass(ref, which):
        n = ref.shape[2] - 2
        k = GATHERS.index(which)
        for side in (1, 0, 2):
            theirs = slices(side, n)[1]
            if side != 1:
                pieces = [ref.at[core, :, theirs]]
            else:
                pieces = [ref.at[core, at_x(t)[1], theirs] for t in range(1, nx)]
            for i, got in enumerate(pieces):
                arrive(
                    can_recv[side],
                    lambda got=got, side=side: peer_copy(
                        got, got, k_.g_send.at[k, side, 0], k_.g_recv.at[k, side], place, mate
                    ),
                )
                launch(None, lambda got=got, i=i, side=side: handed(ref, k, got, 1 + (side // 2 if side != 1 else 2 + i)))

    def gather_wait(ref, which):
        handed(ref, GATHERS.index(which), ref.at[other], 0).wait_recv()

    def fine_parts(ref, which, side):
        k = FINE.index(which)
        own, theirs = slices(side, S)
        inner = pl.ds(1, RB)
        rows = [(None, None, inner, inner, x, core, core)] if side != 1 else [(None, None, inner, inner, x, other, other)]
        if nx > 1:
            for c in range(2):
                rows.append((no(top), no(bottom), pl.ds(1, 1), pl.ds(E - 1, 1), x - 1, c, c))
                rows.append((no(bottom), no(top), pl.ds(RB, 1), pl.ds(0, 1), x + 1, c, c))
        parts = []
        for i, (sends, gets, row, at, tox, to, source) in enumerate(rows):
            target = ref.at[core, theirs, at]
            theirs_ = ref.at[source, theirs, at]
            up = (i - 1) % 2
            arrived = 0 if i == 0 else 1 + up * 2 + core
            expected = 0 if i == 0 else 1 + up * 2 + source
            send = k_.x_send.at[k, side, i]
            parts.append((
                both(can_send[side], sends), both(can_recv[side], gets),
                functools.partial(
                    peer_copy, ref.at[core, own, row], target, send, k_.x_recv.at[k, side, arrived],
                    place + 1 - side, 2 * tox + to,
                ),
                functools.partial(peer_copy, theirs_, theirs_, send, k_.x_recv.at[k, side, expected], place, mate),
            ))
        return parts

    def fine_start(ref, which):
        for side in (0, 2, 1):
            for sends, _, out, _ in fine_parts(ref, which, side):
                launch(sends, out)

    def fine_halo(ref, which, side, c):
        k = FINE.index(which)
        block = ref.at[c, slices(side, S)[1], pl.ds(1, RB)]
        return peer_copy(block, block, k_.y_send.at[k, side], k_.y_recv.at[k, side], place, mate)

    def fine_pass(ref, which):
        for side in (0, 2):
            _, gets, _, back = fine_parts(ref, which, side)[0]
            arrive(gets, back)
            launch(gets, functools.partial(fine_halo, ref, which, side, core))

    def fine_wait(ref, which):
        for side in (1, 0, 2):
            for _, gets, _, back in fine_parts(ref, which, side)[side != 1 :]:
                arrive(gets, back)
            if side != 1:
                arrive(can_recv[side], functools.partial(fine_halo, ref, which, side, other))

    def natural(ref, s, r):
        v = ref[:, s, r]
        size = dm.cd
        return jnp.concatenate(
            [v[c, i * size : (i + 1) * size] for i in range(nx) for c in range(2)], 0
        ).astype(BF16)

    def in_turn(count, fn):
        if count <= 16:
            for i in range(count):
                fn(i)
        else:

            def body(i, carry):
                fn(i)
                return carry

            lax.fori_loop(0, count, body, 0)

    def slab_peers(i):
        to = place + 1 + i
        return jnp.where(to >= nd, to - nd, to), me

    def wide_peers(i):
        i = i + 1
        dt, xt = (i // nx, i % nx) if isinstance(i, int) else (lax.div(i, nx), lax.rem(i, nx))
        to, tox = place + dt, x + xt
        return jnp.where(to >= nd, to - nd, to), 2 * jnp.where(tox >= nx, tox - nx, tox) + core

    def exchange(n, peers, copy):
        in_turn(n - 1, lambda i: copy(*peers(i)).start())

    def sum_start(group, ref, k, slot, tile, source=None):
        n, own, peers, send, recv = group
        ref[slot, own] = tile

        def copy(depth, chan):
            src = ref.at[slot, own] if source is None else source(chan)
            return peer_copy(src, ref.at[slot, own], send.at[k], recv.at[k], depth, chan)

        exchange(n, peers, copy)
        pending.append((None, lambda: all_of(group, ref, k, slot).wait_send()))

    def all_of(group, ref, k, slot):
        n, _, _, send, recv = group
        every = ref.at[slot, pl.ds(0, n - 1)]
        return peer_copy(every, every, send.at[k], recv.at[k], place, mate)

    def sum_finish(group, ref, k, slot):
        all_of(group, ref, k, slot).wait_recv()
        return jnp.sum(ref[slot], axis=0)

    slabs = (nd, place, slab_peers, k_.t_send, k_.t_recv)
    everyone = (nd * nx, place * nx + x, wide_peers, k_.u_send, k_.u_recv)

    def columns_of(row, m):
        lane, channel = iota((m, LANES), 1), iota((m, LANES), 0)
        return tuple(
            jnp.sum(jnp.where(lane == channel + i * m, row, 0.0), axis=1, keepdims=True) for i in range(2)
        )

    def coarse_sums(slot, sums):
        sum_start(slabs, k_.st, slot, slot, pack(*sums))

    def coarse_totals(slot):
        return columns_of(sum_finish(slabs, k_.st, slot, slot), dm.ce)

    def fine_sums(slot, sums):
        sum_start(everyone, k_.su, slot, slot, pack(*sums))

    def fine_totals(slot):
        return columns_of(sum_finish(everyone, k_.su, slot, slot), dm.cf)

    def prepare(k):
        cv, w, own = convs[k], weights[k], wt[k]
        out = wf[k] if k < 2 else wf[k].at[x]
        eye = (iota((LANES, LANES), 0) == iota((LANES, LANES), 1)).astype(BF16)

        def chunk(a):
            return dot_nt(eye, jnp.concatenate([a] * cv.per, 0).astype(BF16))

        full = cv.length // LANES

        def body(i, carry):
            at = pl.multiple_of(i * LANES, LANES)
            turned[pl.ds(at, LANES)] = chunk(w[:, pl.ds(at, LANES)])
            return carry

        lax.fori_loop(0, full, body, 0, unroll=4)
        if full < cv.chunks:
            a = w[:, full * LANES :]
            a = jnp.concatenate([a, jnp.zeros((cv.o, LANES - a.shape[1]), F32)], 1)
            turned[full * LANES : (full + 1) * LANES] = chunk(a)
        group = iota((cv.c, LANES), 1) // cv.o
        for kz in range(3):
            for j in range(cv.tiles):
                tile = None
                for g in range(cv.per):
                    u = j * cv.per + g
                    if u < 9:
                        kx, ky = u // 3, u % 3
                        v = turned[pl.ds(9 * kz + 3 * ky + kx, cv.c, stride=27)]
                        tile = v if tile is None else jnp.where(group == g, v, tile)
                own[kz, :, j * LANES : (j + 1) * LANES] = tile.astype(BF16).astype(own.dtype)
        for j in range(cv.tiles):
            v = jnp.concatenate([own[kz, :, j * LANES : (j + 1) * LANES] for kz in range(3)], 0)
            size = min(LANES, cv.taps - j * LANES)
            v = dot_nt(eye, v.astype(BF16))[0:size]
            if k < 2:
                out[j * LANES : j * LANES + size] = v.astype(BF16)
            else:
                k_.flip[j * LANES : j * LANES + size, 0 : 3 * cv.c] = v
        if k >= 2:
            out[0 : 3 * cv.o] = jnp.concatenate(
                [
                    jnp.concatenate(
                        [
                            k_.flip[(3 * kx + ky) * cv.o : (3 * kx + ky + 1) * cv.o, kz * cv.c : (kz + 1) * cv.c]
                            for kx in range(3)
                        ],
                        0,
                    )
                    for kz in range(3)
                    for ky in range(3)
                ],
                1,
            ).astype(BF16)

    def forward_copy(k, t):
        block = wf[k].at[x]
        return peer_copy(
            block, block, k_.p_send.at[k - 2, t], k_.p_recv.at[k - 2, t], place, 2 * lax.rem(x + t, nx) + core
        )

    def forward_start(k):
        for t in range(1, nx):
            launch(None, functools.partial(forward_copy, k, t))

    def forward_wait(k):
        for t in range(1, nx):
            fromx = lax.rem(x + nx - t, nx)
            block = wf[k].at[fromx]
            peer_copy(
                block, block, k_.p_send.at[k - 2, t], k_.p_recv.at[k - 2, t], place, 2 * fromx + core
            ).wait_recv()

    def forward_weight(k):
        return jnp.concatenate([wf[k][i, 0 : 3 * convs[k].o] for i in range(nx)], 0)

    def weights_start(k):
        cv = convs[k]
        for b, (size, start, at) in enumerate(cv.blocks):
            wx[k][me, :, at : at + size] = wt[k][:, pl.ds(start(me), size)]
            for t in range(1, nc):
                to = lax.rem(me + t, nc)

                def copy(to=to, t=t, b=b, size=size, start=start, at=at):
                    return peer_copy(
                        wt[k].at[:, pl.ds(start(to), size)], wx[k].at[me, :, pl.ds(at, size)],
                        k_.w_send.at[k, b, t], k_.w_recv.at[k, b, t], place, to,
                    )

                launch(None, copy)

    def weights_finish(k):
        cv = convs[k]
        for b, (size, _, at) in enumerate(cv.blocks):
            for t in range(1, nc):
                source = lax.rem(me + nc - t, nc)
                theirs = wx[k].at[source, :, pl.ds(at, size)]
                peer_copy(theirs, theirs, k_.w_send.at[k, b, t], k_.w_recv.at[k, b, t], place, source).wait_recv()

        parts = 9 if k < 2 else 3
        lanes = cv.taps // parts
        for i in range(parts):
            at = (parts - 1 - i) * lanes
            found = [wx[k][j, 2 - kz, :, at : at + lanes].astype(F32) for kz in range(3) for j in range(nc)]
            wb[k][i * cv.needed : (i + 1) * cv.needed] = jnp.concatenate(found, 1).astype(BF16)

    def tiles_of(k, part, put):
        cv, dense = convs[k], k_.dense
        rows, size = 3 * cv.c, 3 * cv.o
        for ky in range(3):
            at = ky * LANES + part * size
            dense[0:rows, ky * size : (ky + 1) * size] = acc[0:rows, at : at + size]

        def tile(i, carry):
            left = []
            for kz in range(3):
                at = pl.ds(pl.multiple_of(kz * cv.c + i * 16, 16), 16)
                for j in range(cv.full):
                    put(i * cv.group + kz * cv.full + j, dense[at, j * LANES : (j + 1) * LANES].astype(BF16))
                left.append(dense[at, cv.full * LANES : cv.full * LANES + cv.left * cv.o])
            if cv.left:
                used = 3 * cv.left * cv.o
                v = jnp.concatenate(left + [jnp.zeros((16, LANES - used), F32)], 1)
                put(i * cv.group + 3 * cv.full, v.astype(BF16))
            return carry

        lax.fori_loop(0, cv.c // 16, tile, 0, unroll=2)

    def cross_start(k):
        gs, gx = (k_.gs2, k_.gs3)[k - 2], (k_.gx2, k_.gx3)[k - 2]

        for part in range(nx):

            def put(i, v, part=part):
                gs[part, i] = v

            tiles_of(k, part, put)
        for t in range(1, nx):

            def copy(t=t):
                tox = at_x(t)[0]
                return peer_copy(
                    gs.at[tox], gx.at[x], k_.c_send.at[k - 2, t], k_.c_recv.at[k - 2, t], place, 2 * tox + core
                )

            launch(None, copy)

    def cross_finish(k):
        cv, gs, gx = convs[k], (k_.gs2, k_.gs3)[k - 2], (k_.gx2, k_.gx3)[k - 2]
        sources = [at_x(t)[1] for t in range(1, nx)]
        for t, fromx in enumerate(sources, 1):
            theirs = gx.at[fromx]
            peer_copy(
                theirs, theirs, k_.c_send.at[k - 2, t], k_.c_recv.at[k - 2, t], place, 2 * fromx + core
            ).wait_recv()

        def add(i, carry):
            for j in range(cv.group):
                p = cv.group * i + j
                v = gs[x, p].astype(F32)
                for fromx in sources:
                    v += gx[fromx, p].astype(F32)
                gt[k][p] = v.astype(BF16)
            return carry

        lax.fori_loop(0, cv.c // 16, add, 0, unroll=2)
        reduce_send(k)

    def reduce_start(k):
        def put(i, v):
            gt[k][i] = v

        tiles_of(k, 0, put)
        reduce_send(k)

    def reduce_send(k):
        cv = convs[k]
        for i in range(cv.count, cv.share * nd):
            gt[k][i] = jnp.zeros((16, LANES), BF16)
        gr[k][place] = gt[k][pl.ds(place * cv.share, cv.share)]

        def copy(to, chan):
            return peer_copy(
                gt[k].at[pl.ds(to * cv.share, cv.share)], gr[k].at[place], k_.r_send.at[k], k_.r_recv.at[k], to, chan
            )

        exchange(nd, slab_peers, copy)
        pending.append((None, lambda: reduce_all(k).wait_send()))

    def reduce_all(k):
        every = gr[k].at[pl.ds(0, nd - 1)]
        return peer_copy(every, every, k_.r_send.at[k], k_.r_recv.at[k], place, mate)

    def share_all(k):
        every = ga[k].at[pl.ds(0, (nd - 1) * convs[k].share)]
        return peer_copy(every, every, k_.a_send.at[k], k_.a_recv.at[k], place, mate)

    def reduce_finish(k):
        cv = convs[k]
        reduce_all(k).wait_recv()
        own = pl.ds(place * cv.share, cv.share)
        ga[k][own] = jnp.sum(gr[k][...].astype(F32), axis=0).astype(BF16)

        def copy(to, chan):
            return peer_copy(ga[k].at[own], ga[k].at[own], k_.a_send.at[k], k_.a_recv.at[k], to, chan)

        exchange(nd, slab_peers, copy)
        pending.append((None, lambda: share_all(k).wait_send()))

    def gradient_out(k):
        cv, out = convs[k], grads[k]
        share_all(k).wait_recv()
        group = iota((16, LANES), 1) // cv.o

        def scatter(i, carry):
            def put(v, g, kz, t):
                turned[pl.ds(9 * kz + t + i * (16 * 27), 16, stride=27)] = jnp.where(group == g, v, 0.0)

            for kz in range(3):
                for j in range(cv.full):
                    v = ga[k][i * cv.group + kz * cv.full + j].astype(F32)
                    for g in range(min(cv.per, 9)):
                        put(v, g, kz, j * cv.per + g)
            if cv.left:
                v = ga[k][i * cv.group + 3 * cv.full].astype(F32)
                for kz in range(3):
                    for g in range(cv.left):
                        put(v, kz * cv.left + g, kz, cv.full * cv.per + g)
            return carry

        lax.fori_loop(0, cv.c // 16, scatter, 0, unroll=2)

        pick = (iota((cv.o, LANES), 1) % cv.o == iota((cv.o, LANES), 0)).astype(BF16)
        step = 8 * LANES
        for at in range(0, cv.length, step):
            size = min(step, cv.length - at)
            v = dot_nt(pick, turned[at : at + -(-size // LANES) * LANES].astype(BF16))
            out[:, at : at + size] = v[:, 0:size]

    def column(row):
        n = row.shape[1]
        eye = iota((n, n), 0) == iota((n, n), 1)
        return jnp.sum(jnp.where(eye, row, 0.0), axis=1, keepdims=True)

    def row_of(col):
        n = col.shape[0]
        eye = iota((n, n), 0) == iota((n, n), 1)
        return jnp.sum(jnp.where(eye, col, 0.0), axis=0, keepdims=True)

    def clear_halos(ref):
        def clear(at):
            if len(ref.shape) == 5:
                for c in range(2):
                    ref[c, at] = jnp.zeros(ref.shape[2:], ref.dtype)
            else:
                for i in range(nx):
                    ref[core, i, at] = jnp.zeros(ref.shape[3:], ref.dtype)

        pl.when(first)(lambda: clear(0))
        pl.when(last)(lambda: clear(ref.shape[-4] - 1))

    def clear_rows(ref):
        def clear(at):
            for c in range(2):
                for i in range(S + 2):
                    ref[c, i, at] = jnp.zeros(ref.shape[3:], ref.dtype)

        pl.when(top)(lambda: clear(0))
        pl.when(bottom)(lambda: clear(E - 1))

    def conv(operand, weight, m, groups, emit, init):
        def body(d, carry):
            v = operand(d)
            y = dot(weight, v)
            results = []
            for j in range(RB):
                lanes = slice(j * LANES, (j + 1) * LANES)
                parts = []
                for g in range(groups):
                    a = [y[(3 * g + kx) * m : (3 * g + kx + 1) * m, lanes] for kx in range(3)]
                    parts.append(from_left(a[0], W) + a[1] + from_right(a[2], W))
                results.append(jnp.concatenate(parts, 0) if groups > 1 else parts[0])
            return emit(d, results, carry)

        return lax.fori_loop(0, S, body, init)

    def rows_of(row):
        return lambda d: jnp.concatenate(
            [jnp.concatenate([row(d + kz, ky + j) for j in range(RB)], 1) for kz in range(3) for ky in range(3)], 0
        )

    def blocks_of(ref):
        size = dm.cd
        return lambda d: jnp.concatenate(
            [
                jnp.concatenate([ref[c, d + kz, 2 - ky + j, i * size : (i + 1) * size] for j in range(RB)], 1)
                for kz in range(3)
                for i in range(nx)
                for c in range(2)
                for ky in range(3)
            ],
            0,
        ).astype(BF16)

    def conv_stats(row, weight, z):
        def emit(d, results, carry):
            total, square = carry
            for j, v in enumerate(results):
                z[d * RB + j] = v
                total, square = total + v, square + v * v
            return total, square

        blank = jnp.zeros((dm.cf, LANES), F32)
        return conv(rows_of(row), weight, dm.cd, nx, emit, (blank, blank))

    def weight_grad(row, k):
        cv = convs[k]

        def part(d):
            v = jnp.concatenate([jnp.concatenate([row(d + kz, j) for j in range(E)], 1) for kz in range(3)], 0)
            y = jnp.concatenate(
                [k_.dzt[d, (2 - ky) * LANES : (2 - ky + E) * LANES] for ky in range(3)], 1
            )
            return dot(v, y)

        acc[0 : 3 * cv.c] = part(0)

        def more(d, carry):
            acc[0 : 3 * cv.c] += part(d)
            return carry

        lax.fori_loop(1, S, more, 0)

    def conv_coarse(ref, weight, m):
        v = jnp.concatenate(
            [jnp.concatenate([flat(ref, kz, i) for i in range(Q)], 1) for kz in range(3)], 0
        )
        y = dot(weight[...], v)
        blank = jnp.zeros((m, LANES), F32)

        def shifted(ky, i):
            if not 0 <= i < Q:
                return blank
            a, b, c = (
                y[(3 * kx + ky) * m : (3 * kx + ky + 1) * m, i * LANES : (i + 1) * LANES] for kx in range(3)
            )
            return from_left(a, V) + b + from_right(c, V)

        before = [shifted(0, i) for i in range(-1, Q)]
        after = [shifted(2, i) for i in range(Q + 1)]
        return [
            shifted(1, i) + halves(before[i + 1] + after[i + 1], before[i] + after[i]) for i in range(Q)
        ]

    def conv_stats_coarse(ref, weight, z, m):
        total = square = jnp.zeros((m, LANES), F32)
        for i, v in enumerate(conv_coarse(ref, weight, m)):
            z[i] = v
            total, square = total + v, square + v * v
        return total, square

    def weight_grad_coarse(ref, k):
        cv = convs[k]
        v = jnp.concatenate(
            [jnp.concatenate([flat(ref, kz, i) for i in range(Q)], 1) for kz in range(3)], 0
        )
        y = jnp.concatenate([k_.dzct[(2 - ky) * V : (2 - ky) * V + Q * LANES] for ky in range(3)], 1)
        acc[0 : 3 * cv.c] = dot(v, y)

    def pack(a, b):
        m = a.shape[0]
        a = jnp.sum(a, axis=1, keepdims=True)
        b = jnp.sum(b, axis=1, keepdims=True)
        lane, channel = iota((m, LANES), 1), iota((m, LANES), 0)
        both = jnp.where(lane == channel, a, jnp.where(lane == channel + m, b, 0.0))
        return jnp.sum(both, axis=0, keepdims=True)

    def moments(total, count):
        mean = total[0] / count
        var = total[1] / count - mean * mean
        return mean, lax.rsqrt(var + EPS)

    def wide(column):
        return jnp.broadcast_to(column, (column.shape[0], LANES))

    def factors(stats, norm):
        mean, inv = stats
        gain, shift = norm
        return wide(mean), wide(gain * inv), wide(shift)

    def norm_rows(z, stats, norm, emit, n):
        mean, scale, shift = factors(stats, norm)

        def body(i, carry):
            for j in range(n):
                p = i * n + j
                u = (z[p] - mean) * scale + shift
                emit(p, u * jax.nn.sigmoid(u))
            return carry

        lax.fori_loop(0, z.shape[0] // n, body, 0)

    def norm_back_sums(z, keep_du, stats, norm, grad, n):
        mean, scale, shift = factors(stats, norm)
        inv = wide(stats[1])
        m = z.shape[1]

        def body(i, carry):
            a, b = carry
            for j in range(n):
                p = i * n + j
                centred = z[p] - mean
                u = centred * scale + shift
                sigma = jax.nn.sigmoid(u)
                v = grad(p) * sigma * (1.0 + u * (1.0 - sigma))
                keep_du(p, v)
                a, b = a + v, b + v * (centred * inv)
            return a, b

        blank = jnp.zeros((m, LANES), F32)
        return lax.fori_loop(0, z.shape[0] // n, body, (blank, blank))

    def back_factors(stats, norm, total, count):
        mean, inv = stats
        scale = norm[0] * inv
        return wide(mean), wide(scale), wide(-scale * total[0] / count), wide(-scale * inv * total[1] / count)

    def columns_first(copies, groups):
        size = copies[0].shape[0] // groups
        rows = [v[g * size : (g + 1) * size] for g in range(groups) for v in copies]
        used = 3 * groups * size
        if used < LANES:
            rows.append(jnp.zeros((LANES - used, LANES), F32))
        return jnp.transpose(jnp.concatenate(rows, 0)).astype(BF16)

    def norm_back_fine(z, given, ref):
        mean, scale, level, slope = given

        def body(d, carry):
            for r in range(RB):
                p = d * RB + r
                v = scale * k_.du_f[p] + level + slope * (z[p] - mean)
                ref[core, 1 + d, 1 + r] = v.astype(BF16).astype(ref.dtype)
            return carry

        lax.fori_loop(0, S, body, 0)

    def turn_fine(ref):
        n = 4 if RB % 4 == 0 else 2

        def body(i, carry):
            d = lax.div(i, RB // n)
            r0 = (i - d * (RB // n)) * n
            for j in range(n):
                v = ref[core, 1 + d, 1 + r0 + j].astype(F32)
                at = pl.ds(pl.multiple_of((2 + r0 + j) * LANES, LANES), LANES)
                k_.dzt[d, at] = columns_first((from_right(v, W), v, from_left(v, W)), nx)
            return carry

        lax.fori_loop(0, S * RB // n, body, 0)

    def norm_back_coarse(z, given, ref):
        mean, scale, level, slope = given
        for i in range(Q):
            v = scale * k_.du_c[i] + level + slope * (z[i] - mean)
            ref[core, x, 1, i] = v.astype(BF16).astype(ref.dtype)

    def turn_coarse(ref):
        for i in range(Q):
            v = ref[core, x, 1, i].astype(F32)
            k_.dzct[V + i * LANES : V + (i + 1) * LANES] = columns_first((from_right(v, V), v, from_left(v, V)), 1)

    def keep_du(ref):
        def store(p, v):
            ref[p] = v

        return store

    barrier = pltpu.get_barrier_semaphore()

    def greet(depth, chan):
        pl.semaphore_signal(barrier, inc=1, device_id={"depth": depth, "chan": chan}, device_id_type=MESH)

    exchange(nd * nx, wide_peers, lambda depth, chan: types.SimpleNamespace(start=lambda: greet(depth, chan)))
    for t in range(nx):
        to = 2 * at_x(t)[0] + other
        greet(place, to)
        if t > 0:
            pl.when(no(first))(lambda to=to: greet(place - 1, to))
            pl.when(no(last))(lambda to=to: greet(place + 1, to))

    hc = iota((LANES, LANES), 0)
    fc = iota((LANES, LANES), 1)
    half = LANES // 2

    def up_table(coarse, fine):
        base = fine // 2
        beside = jnp.clip(base + jnp.where(fine % 2 == 0, -1, 1), 0, V - 1)
        near = (coarse == base).astype(F32)
        far = (coarse == beside).astype(F32)
        return (0.75 * near + 0.25 * far).astype(BF16)

    pool = jnp.concatenate([(hc // 2 == fc - at).astype(BF16) for at in (0, half)], 0)
    spread = jnp.concatenate([(hc - at == fc // 2).astype(BF16) for at in (0, half)], 1)
    up = jnp.concatenate([up_table(hc - at, fc) for at in (0, half)], 1)
    down = jnp.concatenate([up_table(fc, hc)] * 2, 0)
    spread2 = jnp.concatenate([spread, spread], 0)

    def take_rows(ref):
        for c in range(ref.shape[0]):
            k_.rows[c * S * R : (c + 1) * S * R] = ref[c].astype(F32).reshape(S * R, LANES)

    def row_of_all(p, chans):
        return k_.rows[pl.ds(p, chans, stride=S * R)]

    xp, xs, own_skip = k_.xp, k_.xs, k_.own_skip
    clear_halos(xp)
    take_rows(k_.skip)
    for i in range(S):
        for r in (0, R + 1):
            own_skip[i, r] = jnp.zeros((dm.cs, LANES), own_skip.dtype)

    def take_skip(i, carry):
        parts = []
        for d in range(S):
            v = [row_of_all(d * R + 4 * i + j, dm.cs).astype(BF16) for j in range(4)]
            for j in range(4):
                own_skip[d, 1 + 4 * i + j] = v[j].astype(own_skip.dtype)
            parts += [jnp.concatenate([v[j], v[2 + j]], 1) for j in range(2)]
        v = dot(jnp.concatenate(parts, 0), pool).reshape(2 * S, dm.cs, LANES)
        xp[core, x, 1, i] = (jnp.sum(v, axis=0) * 0.125).astype(BF16).astype(xp.dtype)
        return carry

    lax.fori_loop(0, Q, take_skip, 0, unroll=3)
    beside = jnp.where(first, 0, 1) + jnp.where(last, 0, 1)
    pl.semaphore_wait(barrier, nd * nx - 1 + nx + (nx - 1) * beside)
    gather_start(xp, "pooled")
    clear_halos(xs)
    xs[core, x, 1 : S + 1] = own_skip[:, pl.ds(row0, E)]
    gather_start(xs, "skip", lambda at, tox: own_skip.at[at, pl.ds(tox * RB, E)])

    gq = dm.g // nc
    columns = dm.enc_all + dm.skip_all
    gate_all, norm_all = k_.gate_all, k_.norm_all
    gate_all[me, :, 0:columns] = k_.gate[...]
    lane = iota((gq, LANES), 1)
    gate_all[me, :, 2 * LANES :] = jnp.where(
        lane == 0, column(k_.vector[0:1]), jnp.where(lane == 1, column(k_.vector[1:2]), 0.0)
    )
    for layer in range(2):
        for part in range(2):
            at = 2 * layer + part
            norm_all[me, at : at + 1, 0 : dm.cd] = k_.dn[part, layer : layer + 1]

    def constants(i, t, source, to):
        ref = (norm_all, gate_all)[i]
        return peer_copy(ref.at[source], ref.at[source], k_.v_send.at[i, t], k_.v_recv.at[i, t], place, to)

    for i in range(2):
        for t in range(1, nc):
            launch(None, functools.partial(constants, i, t, me, lax.rem(me + t, nc)))
    prepare(0)
    xd, xz4, xz3, d1 = k_.xd, k_.xz4, k_.xz3, k_.d1
    for ref in (xd, xz4, xz3):
        clear_rows(ref)
        clear_halos(ref)
    for ref in (k_.xh, k_.xz2, k_.xz1):
        clear_halos(ref)
    for i in range(S):
        for at in (0, (RB + 2) * LANES):
            k_.dzt[i, at : at + 2 * LANES] = jnp.zeros((2 * LANES, LANES), BF16)
        for r in range(3):
            k_.ug[i, r] = jnp.zeros(k_.ug.shape[2:], F32)
            k_.ug[i, RB + 3 + r] = jnp.zeros(k_.ug.shape[2:], F32)
        for r in range(H + 2):
            k_.cb[i, r] = jnp.zeros(k_.cb.shape[2:], F32)

    for at in (0, V + Q * LANES):
        k_.dzct[at : at + V] = jnp.zeros((V, LANES), BF16)

    def norm_of(layer):
        return column(k_.en[0, layer : layer + 1]), column(k_.en[1, layer : layer + 1])

    norm_e1, norm_e2 = norm_of(0), norm_of(1)

    gather_pass(xp, "pooled")
    gather_wait(xp, "pooled")
    coarse_sums(0, conv_stats_coarse(xp, wf[0], k_.z1, dm.ce))
    prepare(1)
    stats_e1 = moments(coarse_totals(0), dm.coarse_total)

    def keep_coarse(ref):
        def store(p, v):
            ref[core, x, 1, p] = v.astype(BF16).astype(ref.dtype)

        return store

    norm_rows(k_.z1, stats_e1, norm_e1, keep_coarse(k_.xh), Q)
    gather_start(k_.xh, "hidden")
    prepare(2)
    forward_start(2)
    gather_pass(k_.xh, "hidden")
    gather_pass(xs, "skip")
    gather_wait(k_.xh, "hidden")
    coarse_sums(1, conv_stats_coarse(k_.xh, wf[1], k_.z2, dm.ce))
    take_rows(k_.cot)

    def take_cot(i, carry):
        for d in range(S):
            for j in range(4):
                v = row_of_all(d * R + 4 * i + j, dm.cd).astype(BF16)
                k_.own_cot[d, 4 * i + j] = v.astype(k_.own_cot.dtype)
        return carry

    lax.fori_loop(0, Q, take_cot, 0)
    k_.cots[x] = k_.own_cot[:, pl.ds(row0, RB)]
    stats_e2 = moments(coarse_totals(1), dm.coarse_total)
    norm_rows(k_.z2, stats_e2, norm_e2, keep_coarse(k_.xc), Q)
    gather_start(k_.xc, "coarse")
    prepare(3)
    for t in range(1, nc):
        for i in range(2):
            source = lax.rem(me + nc - t, nc)
            constants(i, t, source, source).wait_recv()
    gate_full = gate_all[...].reshape(dm.g, 3 * LANES)
    wg = gate_full[:, 0:columns].astype(BF16)
    gbias = gate_full[:, 2 * LANES : 2 * LANES + 1]
    gout = gate_full[:, 2 * LANES + 1 : 2 * LANES + 2]
    k_.gate_t[...] = jnp.transpose(gate_full[:, 0 : 2 * LANES])
    own_rows = [k_.gate_t[pl.ds(pl.multiple_of((2 * i + core) * dm.ce, dm.ce), dm.ce)] for i in range(nx)]
    own_rows += [
        k_.gate_t[pl.ds(pl.multiple_of(dm.enc_all + (2 * i + core) * dm.cs, dm.cs), dm.cs)] for i in range(nx)
    ]
    k_.gate_own[...] = jnp.concatenate(own_rows, 0)

    def norm_fine(layer):
        return tuple(
            jnp.concatenate(
                [column(norm_all[2 * i + core, 2 * layer + part : 2 * layer + part + 1, 0 : dm.cd]) for i in range(nx)], 0
            )
            for part in range(2)
        )

    norm_d1, norm_d2 = norm_fine(0), norm_fine(1)
    gather_pass(k_.xc, "coarse")
    gather_wait(k_.xc, "coarse")
    forward_start(3)

    dt = k_.dt

    def up_depth(i, carry):
        t = []
        for j in range(3):
            v = dot(flat(k_.xc, j, i), up)
            t.append(jnp.stack([v[:, 0:LANES], v[:, LANES:]], 0))
        below = jnp.where(first, t[1], t[0])
        above = jnp.where(last, t[1], t[2])
        near = 0.75 * t[1]
        here = 0.25 * t[1]
        rows = pl.ds(i * 2, 2)
        dt[0, rows] = jnp.where(first, 0.0, 0.75 * below + here)
        dt[1, rows] = near + 0.25 * below
        dt[2, rows] = near + 0.25 * above
        dt[3, rows] = jnp.where(last, 0.0, 0.75 * above + here)
        return carry

    lax.fori_loop(0, Q, up_depth, 0)

    def up_rows(i, carry):
        here = h0 + i
        before, after = jnp.maximum(here - 1, 0), jnp.minimum(here + 1, H - 1)
        for j in range(S + 2):
            v = 0.75 * dt[j, here]
            d1[j, 1 + 2 * i, 0 : dm.enc_all] = (v + 0.25 * dt[j, before]).astype(BF16)
            d1[j, 2 + 2 * i, 0 : dm.enc_all] = (v + 0.25 * dt[j, after]).astype(BF16)
        return carry

    lax.fori_loop(0, RB // 2, up_rows, 0)
    for edge, at, near, far in (
        (top, 0, jnp.maximum(h0 - 1, 0), h0),
        (bottom, E - 1, jnp.minimum(h0 + RB // 2, H - 1), h0 + RB // 2 - 1),
    ):
        for j in range(S + 2):
            v = jnp.where(edge, 0.0, 0.75 * dt[j, near] + 0.25 * dt[j, far])
            d1[j, at, 0 : dm.enc_all] = v.astype(BF16)
    for t in range(1, nx):
        tox = lax.rem(x + t, nx)

        def send_cot(t=t, tox=tox):
            return peer_copy(
                k_.own_cot.at[:, pl.ds(tox * RB, RB)], k_.cots.at[x], k_.o_send.at[0, t], k_.o_recv.at[0, t],
                place, 2 * tox + core,
            )

        launch(None, send_cot)

    gather_wait(xs, "skip")
    gate_n = E // 2

    def gate(i, carry):
        j = lax.div(i, 2)
        r0 = (i - 2 * j) * gate_n
        skips = [flat(xs, j, r0 + q) for q in range(gate_n)]
        v = jnp.concatenate(
            [
                jnp.concatenate([d1[j, r0 + q, 0 : dm.enc_all] for q in range(gate_n)], 1),
                jnp.concatenate(skips, 1),
            ],
            0,
        )
        pre = dot(wg, v) + gbias
        act = pre * jax.nn.sigmoid(pre)
        alpha = jax.nn.sigmoid(jnp.sum(gout * act, axis=0, keepdims=True))
        for q in range(gate_n):
            lanes = slice(q * LANES, (q + 1) * LANES)
            d1[j, r0 + q, dm.enc_all :] = (alpha[:, lanes] * skips[q].astype(F32)).astype(BF16)
            k_.pre[j, r0 + q] = pre[:, lanes]
            k_.alpha[j, r0 + q] = alpha[:, lanes]
        return carry

    lax.fori_loop(0, (S + 2) * 2, gate, 0)
    for k in (3, 2, 1, 0):
        weights_start(k)

    def row_d1(j, r):
        return d1[j, r]

    def row_xd(j, r):
        return natural(xd, j, r)

    forward_wait(2)
    fine_sums(0, conv_stats(row_d1, forward_weight(2), k_.z3))
    drain()
    forward_wait(3)
    stats_d1 = moments(fine_totals(0), dm.fine_total)

    def keep_dec(p, v):
        d = lax.div(p, RB)
        xd[core, 1 + d, 1 + p - d * RB] = v.astype(BF16).astype(xd.dtype)

    norm_rows(k_.z3, stats_d1, norm_d1, keep_dec, RB)
    fine_start(xd, "hidden")
    for t in range(1, nx):
        fromx = lax.rem(x + nx - t, nx)
        theirs = k_.cots.at[fromx]
        peer_copy(theirs, theirs, k_.o_send.at[0, t], k_.o_recv.at[0, t], place, 2 * fromx + core).wait_recv()
    fine_pass(xd, "hidden")
    weights_finish(3)
    fine_wait(xd, "hidden")
    fine_sums(1, conv_stats(row_xd, forward_weight(3), k_.z4))
    stats_d2 = moments(fine_totals(1), dm.fine_total)

    def row_cot(p):
        d = lax.div(p, RB)
        return jnp.concatenate([k_.cots[i, d, p - d * RB] for i in range(nx)], 0).astype(F32)

    fine_sums(2, norm_back_sums(k_.z4, keep_du(k_.du_f), stats_d2, norm_d2, row_cot, RB))

    def keep_result(p, v):
        for i in range(nx):
            k_.ob[i, p] = v[i * dm.cd : (i + 1) * dm.cd].astype(BF16).astype(k_.ob.dtype)

    norm_rows(k_.z4, stats_d2, norm_d2, keep_result, RB)
    for t in range(1, nx):
        tox = lax.rem(x + t, nx)

        def send_result(t=t, tox=tox):
            return peer_copy(
                k_.ob.at[tox], k_.oi.at[x], k_.o_send.at[1, t], k_.o_recv.at[1, t], place, 2 * tox + core
            )

        launch(None, send_result)
    total_d2 = fine_totals(2)
    norm_back_fine(k_.z4, back_factors(stats_d2, norm_d2, total_d2, dm.fine_total), xz4)
    fine_start(xz4, "dz4")
    turn_fine(xz4)
    weight_grad(row_xd, 3)
    fine_pass(xz4, "dz4")
    cross_start(3)
    fine_wait(xz4, "dz4")

    def keep_grad(d, results, carry):
        for j, v in enumerate(results):
            k_.gg[d * RB + j] = v
        return carry

    conv(blocks_of(xz4), wb[3][...], dm.cf, 1, keep_grad, 0)
    fine_sums(3, norm_back_sums(k_.z3, keep_du(k_.du_f), stats_d1, norm_d1, lambda p: k_.gg[p], RB))
    cross_finish(3)
    total_d1 = fine_totals(3)
    norm_back_fine(k_.z3, back_factors(stats_d1, norm_d1, total_d1, dm.fine_total), xz3)
    fine_start(xz3, "dz3")
    turn_fine(xz3)
    weights_finish(2)
    weight_grad(row_d1, 2)
    fine_pass(xz3, "dz3")
    cross_start(2)
    fine_wait(xz3, "dz3")

    ups = nx * dm.ce

    def gate_back(d, results, carry):
        bias, psi = carry
        lows = []
        for j, both in enumerate(results):
            p = d * RB + j
            v = both[ups:]
            grad = jnp.sum(v * flat(xs, d + 1, 1 + j).astype(F32), axis=0, keepdims=True)
            alpha = k_.alpha[d + 1, 1 + j]
            logit = grad * alpha * (1.0 - alpha)
            pre = k_.pre[d + 1, 1 + j]
            sigma = jax.nn.sigmoid(pre)
            psi = psi + pre * sigma * logit
            low = (logit * gout * sigma * (1.0 + pre * (1.0 - sigma))).astype(BF16)
            bias = bias + low.astype(F32)
            k_.pg[p] = low
            lows.append(low)
            k_.ug[d, 3 + j] = both[0:ups]
            for i in range(nc):
                k_.gv[i] = v[i * dm.cs : (i + 1) * dm.cs]
            for i in range(nx):
                k_.sgp[i, p] = alpha * k_.gv[2 * i + core]
        back = dot(k_.gate_own[...].astype(BF16), jnp.concatenate(lows, 1))
        for j in range(len(results)):
            p = d * RB + j
            lanes = slice(j * LANES, (j + 1) * LANES)
            k_.ug[d, 3 + j] += back[0:ups, lanes]
            for i in range(nx):
                v = k_.sgp[i, p] + back[ups + i * dm.cs : ups + (i + 1) * dm.cs, lanes]
                k_.sgp[i, p] = v
                k_.sgb[i, p] = v.astype(BF16).astype(k_.sgb.dtype)
        return bias, psi

    blank = jnp.zeros((dm.g, LANES), F32)
    bias, psi = conv(blocks_of(xz3), wb[2][...], ups + dm.skip_all, 1, gate_back, (blank, blank))

    ug, cb, cg = k_.ug, k_.cb, k_.cg
    for q in range(RB // 2 + 2):
        terms = []
        for d in range(S):
            v = 0.75 * (ug[d, 2 * q + 1] + ug[d, 2 * q + 2]) + 0.25 * (ug[d, 2 * q + 3] + ug[d, 2 * q])
            if q == 1:
                v += jnp.where(top, 0.25 * ug[d, 3], 0.0)
            if q == RB // 2:
                v += jnp.where(bottom, 0.25 * ug[d, RB + 2], 0.0)
            terms.append(split(v))
        v = dot(jnp.concatenate(terms, 0), down)
        for d in range(S):
            cb[d, h0 + q] = v[d * ups : (d + 1) * ups]

    def to_slabs(i, carry):
        even, odd = (cb[d, 2 * i + 1] + pltpu.roll(cb[d, 2 * i + 2], half, 1) for d in range(S))
        middle = 0.75 * (even + odd) + jnp.where(first, 0.25 * even, 0.0) + jnp.where(last, 0.25 * odd, 0.0)
        for part, v in enumerate((0.25 * even, middle, 0.25 * odd)):
            for j in range(nx):
                block = v[j * dm.ce : (j + 1) * dm.ce]
                k_.fs[part, j, i] = block.astype(BF16).astype(k_.fs.dtype)
                if part == 1:
                    k_.fm[j, i] = block
        return carry

    lax.fori_loop(0, Q, to_slabs, 0)

    def fold_parts():
        for step in (-1, 1, 0):
            sends = (no(first), None, no(last))[step + 1]
            gets = (no(last), None, no(first))[step + 1]
            for t in range(nx):
                if (step, t) != (0, 0):
                    tox, fromx = lax.rem(x + t, nx), lax.rem(x + nx - t, nx)
                    sems = (k_.f_send.at[step + 1, t], k_.f_recv.at[step + 1, t])
                    theirs = k_.fr.at[step + 1, fromx]
                    yield (
                        sends, gets, fromx, step + 1,
                        functools.partial(
                            peer_copy, k_.fs.at[step + 1, tox], k_.fr.at[step + 1, x], *sems, place + step, 2 * tox + core
                        ),
                        functools.partial(peer_copy, theirs, theirs, *sems, place, 2 * fromx + core),
                    )

    for sends, _, _, _, out, _ in fold_parts():
        launch(sends, out)
    for t in range(1, nx):
        tox = lax.rem(x + t, nx)

        def send_skip(t=t, tox=tox):
            return peer_copy(
                k_.sgb.at[tox], k_.sgi.at[x], k_.o_send.at[2, t], k_.o_recv.at[2, t], place, 2 * tox + core
            )

        launch(None, send_skip)

    reduce_finish(3)
    cross_finish(2)

    k_.gw[...] = jnp.zeros(k_.gw.shape, F32)

    def gate_weight(d, carry):
        v = jnp.concatenate(
            [
                jnp.concatenate([d1[1 + d, 1 + j, 0 : dm.enc_all] for j in range(RB)], 1),
                jnp.concatenate([flat(xs, 1 + d, 1 + j) for j in range(RB)], 1),
            ],
            0,
        )
        y = jnp.concatenate([k_.pg[d * RB + j] for j in range(RB)], 1)
        k_.gw[0:columns, 0 : dm.g] += dot_nt(v, y)
        return carry

    lax.fori_loop(0, S, gate_weight, 0)
    gate_grad = jnp.transpose(k_.gw[...])
    lane = iota((dm.g, LANES), 1)
    vectors = jnp.where(
        lane == 0,
        jnp.sum(bias, axis=1, keepdims=True),
        jnp.where(lane == 1, jnp.sum(psi, axis=1, keepdims=True), 0.0),
    )
    gate_block = k_.gate_block
    for j in range(nc):
        mine = slice(j * gq, (j + 1) * gq)
        gate_block[j, :, 0 : 2 * LANES] = gate_grad[mine]
        gate_block[j, :, 2 * LANES :] = vectors[mine]
    sum_start(everyone, k_.sv, 4, 0, gate_block[me], lambda chan: gate_block.at[chan])
    cg[...] = k_.fm[x]
    for _, gets, fromx, part, _, back in fold_parts():

        def fold_in(back=back, part=part, fromx=fromx):
            back().wait_recv()
            cg[...] += k_.fr[part, fromx].astype(F32)

        guarded(gets, fold_in)

    coarse_sums(2, norm_back_sums(k_.z2, keep_du(k_.du_c), stats_e2, norm_e2, lambda p: cg[p], Q))
    weights_finish(1)
    total_e2 = coarse_totals(2)
    norm_back_coarse(k_.z2, back_factors(stats_e2, norm_e2, total_e2, dm.coarse_total), k_.xz2)
    gather_start(k_.xz2, "dz2")
    turn_coarse(k_.xz2)
    weight_grad_coarse(k_.xh, 1)
    gather_pass(k_.xz2, "dz2")
    reduce_start(1)
    weights_finish(0)
    reduce_finish(2)
    drain()
    gather_wait(k_.xz2, "dz2")
    for i, v in enumerate(conv_coarse(k_.xz2, wb[1], dm.ce)):
        cg[i] = v
    coarse_sums(3, norm_back_sums(k_.z1, keep_du(k_.du_c), stats_e1, norm_e1, lambda p: cg[p], Q))
    gradient_out(3)
    total_e1 = coarse_totals(3)
    norm_back_coarse(k_.z1, back_factors(stats_e1, norm_e1, total_e1, dm.coarse_total), k_.xz1)
    gather_start(k_.xz1, "dz1")
    turn_coarse(k_.xz1)
    weight_grad_coarse(xp, 0)
    reduce_start(0)
    reduce_finish(1)
    gather_pass(k_.xz1, "dz1")
    gradient_out(2)

    def rows_out(ref, own, theirs, kind, size):
        def copy_rows(read, at):
            def body(d, carry):
                for r in range(RB):
                    p = (d * R + at * RB + r) * size
                    ref[pl.ds(pl.multiple_of(p, size), size)] = read(d * RB + r).astype(F32)
                return carry

            lax.fori_loop(0, S, body, 0)

        copy_rows(lambda p: own[x, p], x)
        for t in range(1, nx):
            fromx = lax.rem(x + nx - t, nx)
            block = theirs.at[fromx]
            peer_copy(block, block, k_.o_send.at[kind, t], k_.o_recv.at[kind, t], place, 2 * fromx + core).wait_recv()
            copy_rows(lambda p, fromx=fromx: theirs[fromx, p], fromx)

    rows_out(k_.out, k_.ob, k_.oi, 1, dm.cd)
    rows_out(k_.sg, k_.sgp, k_.sgi, 2, dm.cs)
    reduce_finish(0)
    gather_wait(k_.xz1, "dz1")
    for i, v in enumerate(conv_coarse(k_.xz1, wb[0], dm.cs)):
        v = dot(split(v), spread2) * 0.125
        for j in range(4):
            part = v[:, (j // 2) * LANES : (j // 2 + 1) * LANES]
            for d in range(S):
                at = (d * R + 4 * i + j) * dm.cs
                k_.sg[at : at + dm.cs] += part
    gradient_out(1)
    gate_total = sum_finish(everyone, k_.sv, 4, 0)
    k_.ggate[...] = gate_total[:, 0:columns]
    k_.gvector[0:1] = row_of(gate_total[:, 2 * LANES : 2 * LANES + 1])
    k_.gvector[1:2] = row_of(gate_total[:, 2 * LANES + 1 : 2 * LANES + 2])

    def own_part(col):
        parts = [jnp.where(x == i, col[i * dm.cd : (i + 1) * dm.cd], 0.0) for i in range(nx)]
        return functools.reduce(jnp.add, parts)

    for ref, pair, pick in ((k_.gen, (total_e1, total_e2), lambda v: v), (k_.gdn, (total_d1, total_d2), own_part)):
        for layer, total in enumerate(pair):
            ref[0, layer : layer + 1] = row_of(pick(total[1]))
            ref[1, layer : layer + 1] = row_of(pick(total[0]))
    gradient_out(0)
    drain()


def adamw(weight, grad, moment, square, rate):
    new_moment = 0.9 * moment + 0.1 * grad
    new_square = 0.999 * square + 0.001 * grad * grad
    moment_hat = new_moment / (1.0 - 0.9**STEP)
    square_hat = new_square / (1.0 - 0.999**STEP)
    new_weight = weight - rate * (moment_hat / (jnp.sqrt(square_hat) + 1e-08) + 0.01 * weight)
    return (new_weight, new_moment, new_square)


RATES = (CONV_RATE, CONV_RATE, GATE_RATE, VECTOR_RATE, CONV_RATE, CONV_RATE, VECTOR_RATE, VECTOR_RATE)


def update_kernel(*refs):
    n = len(RATES)
    sources, targets = refs[: 2 + 4 * n], refs[2 + 4 * n : 4 + 7 * n]
    inside, outside = refs[4 + 7 * n : 6 + 11 * n], refs[6 + 11 * n : 8 + 14 * n]
    in_sem, out_sem = refs[8 + 14 * n :]
    order = (4, 1, 0, 5, 2, 3, 6, 7)

    def load(i):
        return pltpu.make_async_copy(sources[i], inside[i], in_sem.at[i])

    def store(i):
        return pltpu.make_async_copy(outside[i], targets[i], out_sem.at[i])

    for i in (1, 0):
        load(i).start()
    for k in order:
        for part in range(4):
            load(2 + part * n + k).start()
    for i in (1, 0):
        load(i).wait()
        chans, (slabs, rows) = outside[i].shape[0], outside[i].shape[1:3]
        for c in range(chans):
            v = inside[i][pl.ds(c, slabs * rows, stride=chans)]
            outside[i][c] = v.reshape(slabs, rows, LANES).astype(outside[i].dtype)
        store(i).start()
    for k in order:
        own = [2 + part * n + k for part in range(4)]
        for i in own:
            load(i).wait()
        rows = inside[own[0]].shape[0]
        step = 8 if rows % 8 == 0 and rows > 8 else rows
        for r in range(0, rows, step):
            at = slice(r, r + step)
            new = adamw(*(inside[i][at] for i in own), RATES[k])
            for part, value in enumerate(new):
                outside[2 + 3 * k + part][at] = value
        for part in range(3):
            store(2 + 3 * k + part).start()
    for i in range(len(targets)):
        store(i).wait()


def per_device(
    skip, cotangent, enc_conv1, enc_conv2, gate_proj, gate_vector, dec_conv1, dec_conv2, enc_norms, dec_norms, *states
):
    nd, nc = lax.axis_size("depth"), lax.axis_size("chan")
    dm = Dims(nd, nc, skip.shape, enc_conv1.shape[0], dec_conv1.shape[0], gate_proj.shape[0] * nc)
    S, R, H, nx, RB, E = dm.s, dm.rows, dm.half, dm.nx, dm.rb, dm.ext
    Q = H // 2
    cin3 = dm.enc_all + dm.skip_all

    def own_block(size):
        return (size, lambda j: pl.multiple_of(j * size, size), 0)

    def core_blocks(size):
        return tuple(
            (size, lambda j, i=i: pl.multiple_of((2 * i + lax.rem(j, 2)) * size, size), i * size) for i in range(nx)
        )

    dm.convs = convs = (
        Conv(dm, dm.ce, dm.skip_all, (own_block(dm.cs),)),
        Conv(dm, dm.ce, dm.enc_all, (own_block(dm.ce),)),
        Conv(dm, dm.cd, cin3, core_blocks(dm.ce) + ((dm.skip_all, lambda j: dm.enc_all, nx * dm.ce),)),
        Conv(dm, dm.cd, dm.dec_all, core_blocks(dm.cd)),
    )
    params = (enc_conv1, enc_conv2, gate_proj, gate_vector, dec_conv1, dec_conv2, enc_norms, dec_norms)
    inputs = dict(
        skip=skip, cot=cotangent, w0=enc_conv1, w1=enc_conv2, w2=dec_conv1, w3=dec_conv2,
        gate=gate_proj, vector=gate_vector, en=enc_norms, dn=dec_norms,
    )
    shape = jax.ShapeDtypeStruct
    outs = dict(
        out=shape((S * R * dm.cd, LANES), F32),
        sg=shape((S * R * dm.cs, LANES), F32),
        **{f"g{i}": shape(a.shape, F32) for i, a in enumerate((enc_conv1, enc_conv2, dec_conv1, dec_conv2))},
        **{
            name: shape(a.shape, F32)
            for name, a in (("ggate", gate_proj), ("gvector", gate_vector), ("gen", enc_norms), ("gdn", dec_norms))
        },
    )
    gq = dm.g // nc

    def coarse(block):
        return pltpu.VMEM((2, nx, 3, Q, block, LANES), storage(block))

    def fine():
        return pltpu.VMEM((2, S + 2, E, dm.cf, LANES), storage(dm.cd))

    def f32(*dims):
        return pltpu.VMEM((*dims, LANES), F32)

    def tiles(*dims):
        return pltpu.VMEM((*dims, 16, LANES), BF16)

    def blocks(block, *dims):
        return pltpu.VMEM((*dims, block, LANES), storage(block))

    def sems(*dims):
        return pltpu.SemaphoreType.DMA(dims)

    scratch = dict(
        xp=coarse(dm.cs), xh=coarse(dm.ce), xc=coarse(dm.ce), xz2=coarse(dm.ce), xz1=coarse(dm.ce),
        own_skip=blocks(dm.cs, S, R + 2), xs=blocks(dm.cs, 2, nx, S + 2, E),
        own_cot=blocks(dm.cd, S, R), cots=blocks(dm.cd, nx, S, RB),
        d1=pltpu.VMEM((S + 2, E, cin3, LANES), BF16), xd=fine(), xz4=fine(), xz3=fine(),
        z1=f32(Q, dm.ce), z2=f32(Q, dm.ce), z3=f32(S * RB, dm.cf), z4=f32(S * RB, dm.cf),
        du_c=f32(Q, dm.ce), du_f=f32(S * RB, dm.cf), gg=f32(S * RB, dm.cf), cg=f32(Q, dm.ce),
        pre=f32(S + 2, E, dm.g), alpha=f32(S + 2, E, 1), pg=pltpu.VMEM((S * RB, dm.g, LANES), BF16),
        ug=f32(S, RB + 6, nx * dm.ce), cb=f32(S, H + 2, nx * dm.ce), dt=f32(S + 2, H, dm.enc_all),
        gv=f32(nc, dm.cs), sgp=f32(nx, S * RB, dm.cs), sgb=blocks(dm.cs, nx, S * RB), sgi=blocks(dm.cs, nx, S * RB),
        ob=blocks(dm.cd, nx, S * RB), oi=blocks(dm.cd, nx, S * RB),
        dzt=pltpu.VMEM((S, (RB + 4) * LANES, LANES), BF16), dzct=pltpu.VMEM((Q * LANES + 2 * dm.hcols, LANES), BF16),
        gw=f32(2 * LANES), dense=pltpu.VMEM((max(3 * cv.c for cv in convs), 3 * LANES), F32),
        fs=blocks(dm.ce, 3, nx, Q), fr=blocks(dm.ce, 3, nx, Q), fm=f32(nx, Q, dm.ce),
        st=f32(4, nd, 1), su=f32(4, nd * nx, 1), sv=pltpu.VMEM((1, nd * nx, gq, 3 * LANES), F32),
        norm_all=f32(nc, 8), rows=f32(max(dm.cs, dm.cd) * S * R),
        turned=f32(max(cv.chunks for cv in convs) * LANES),
        acc=pltpu.VMEM((max(3 * cv.c for cv in convs), 3 * LANES), F32),
        gate_all=pltpu.VMEM((nc, gq, 3 * LANES), F32), gate_t=pltpu.VMEM((2 * LANES, dm.g), F32),
        gate_own=pltpu.VMEM((nx * (dm.ce + dm.cs), dm.g), F32), gate_block=pltpu.VMEM((nc, gq, 3 * LANES), F32),
        **{f"wt{i}": pltpu.VMEM((3, cv.c, cv.wide), cv.kind) for i, cv in enumerate(convs)},
        **{
            f"wf{i}": pltpu.VMEM((cv.taps, 3 * cv.c) if i < 2 else (nx, cv.stored, 9 * cv.c), BF16)
            for i, cv in enumerate(convs)
        },
        **{f"wx{i}": pltpu.VMEM((nc, 3, cv.needed, cv.wide), cv.kind) for i, cv in enumerate(convs)},
        **{
            f"wb{i}": pltpu.VMEM((9 * cv.needed, 3 * nc * cv.o) if i < 2 else (3 * cv.needed, 9 * nc * cv.o), BF16)
            for i, cv in enumerate(convs)
        },
        flip=pltpu.VMEM((max(cv.tiles for cv in convs[2:]) * LANES, max(3 * cv.c for cv in convs[2:])), F32),
        **{f"gt{i}": tiles(cv.share * nd) for i, cv in enumerate(convs)},
        **{f"gr{i}": tiles(nd, cv.share) for i, cv in enumerate(convs)},
        **{f"ga{i}": tiles(cv.share * nd) for i, cv in enumerate(convs)},
        **{f"gs{i}": tiles(nx, convs[i].count) for i in (2, 3)},
        **{f"gx{i}": tiles(nx, convs[i].count) for i in (2, 3)},
        g_send=sems(len(GATHERS), 3, nx), g_recv=sems(len(GATHERS), 3),
        h_send=sems(len(GATHERS), 2 + nx), h_recv=sems(len(GATHERS)),
        x_send=sems(len(FINE), 3, 5), x_recv=sems(len(FINE), 3, 5),
        y_send=sems(len(FINE), 3), y_recv=sems(len(FINE), 3),
        t_send=sems(4), t_recv=sems(4), u_send=sems(5), u_recv=sems(5),
        f_send=sems(3, nx), f_recv=sems(3, nx), w_send=sems(4, nx + 1, nc), w_recv=sems(4, nx + 1, nc),
        p_send=sems(2, nx), p_recv=sems(2, nx), c_send=sems(2, nx), c_recv=sems(2, nx),
        o_send=sems(3, nx), o_recv=sems(3, nx), v_send=sems(2, nc), v_recv=sems(2, nc),
        r_send=sems(4), r_recv=sems(4), a_send=sems(4), a_recv=sems(4),
    )
    vmem = pl.BlockSpec(memory_space=pltpu.VMEM)
    out, sg, grad1, grad2, grad3, grad4, ggate, gvector, gen, gdn = pl.pallas_call(
        functools.partial(kernel, dm, (*inputs, *outs, *scratch)),
        out_shape=tuple(outs.values()),
        in_specs=[vmem] * len(inputs),
        out_specs=[vmem] * len(outs),
        scratch_shapes=list(scratch.values()),
        compiler_params=pltpu.CompilerParams(
            has_side_effects=True, collective_id=0, vmem_limit_bytes=60 * 1024 * 1024
        ),
        name="step",
    )(*inputs.values())
    grads = (grad1, grad2, ggate, gvector, grad3, grad4, gen, gdn)
    operands = (out, sg, *params, *grads, *states)
    updated = (
        shape(cotangent.shape, BF16),
        shape(skip.shape, F32),
        *(shape(p.shape, F32) for p in params for _ in range(3)),
    )
    anywhere = pl.BlockSpec(memory_space=pl.ANY)
    return pl.pallas_call(
        update_kernel,
        out_shape=updated,
        in_specs=[anywhere] * len(operands),
        out_specs=[anywhere] * len(updated),
        scratch_shapes=[
            *(pltpu.VMEM(a.shape, a.dtype) for a in operands),
            *(pltpu.VMEM(a.shape, a.dtype) for a in updated),
            pltpu.SemaphoreType.DMA((len(operands),)),
            pltpu.SemaphoreType.DMA((len(updated),)),
        ],
        compiler_params=pltpu.CompilerParams(vmem_limit_bytes=60 * 1024 * 1024),
        name="update",
    )(*operands)


def solution(mesh):
    volume = P("chan", "depth", None, None)
    row, column, norms = P("chan", None), P(None, "chan"), P(None, None, "chan")
    params = (row, row, row, column, row, row, norms, norms)
    return jax.shard_map(
        per_device,
        mesh=mesh,
        in_specs=(volume, volume) + params * 3,
        out_specs=(volume, volume) + tuple(spec for spec in params for _ in range(3)),
        check_vma=False,
    )
```

```python
import functools
import types

import jax
import jax.numpy as jnp
from jax import lax
from jax.experimental import pallas as pl
from jax.experimental.pallas import tpu as pltpu
from jax.sharding import PartitionSpec as P

STEP = 5
EPS = 1e-05
CONV_RATE = 0.03
GATE_RATE = 0.1
VECTOR_RATE = 0.5
LANES = 128
MESH = pl.DeviceIdType.MESH
F32 = jnp.float32
BF16 = jnp.bfloat16


def iota(shape, dim):
    return lax.broadcasted_iota(jnp.int32, shape, dim)


def dot(a, b):
    return jnp.dot(a, b, preferred_element_type=F32)


def dot_nt(a, b):
    return lax.dot_general(a, b, (((1,), (1,)), ((), ())), preferred_element_type=F32)


def dot_tn(a, b):
    return lax.dot_general(a, b, (((0,), (0,)), ((), ())), preferred_element_type=F32)


def from_left(v, width):
    return jnp.where(iota(v.shape, 1) % width == 0, 0.0, pltpu.roll(v, 1, 1))


def from_right(v, width):
    return jnp.where(iota(v.shape, 1) % width == width - 1, 0.0, pltpu.roll(v, LANES - 1, 1))


def halves(low, high):
    return pltpu.roll(jnp.where(iota(low.shape, 1) < LANES // 2, low, high), LANES // 2, 1)


def split(v):
    high = v.astype(BF16)
    return jnp.concatenate([high, (v - high.astype(F32)).astype(BF16)], 1)


def storage(block):
    return BF16 if block % 16 == 0 else F32


def flat(ref, s, r):
    if len(ref.shape) == 4:
        return ref[s, r]
    v = ref[:, :, s, r]
    return jnp.concatenate([v[c, i] for i in range(v.shape[1]) for c in range(2)], 0).astype(BF16)


class Dims:
    def __init__(self, nd, nc, skip, enc, dec, gate):
        self.nd, self.nc, self.nx = nd, nc, nc // 2
        self.s, self.rows, self.cols = skip[1:]
        self.cs, self.ce, self.cd, self.g = skip[0], enc, dec, gate
        self.half, self.hcols = self.rows // 2, self.cols // 2
        self.fine_total = nd * self.s * self.rows * self.cols
        self.coarse_total = self.fine_total // 8
        self.enc_all = nc * enc
        self.skip_all = nc * skip[0]
        self.dec_all = nc * dec
        self.rb = self.rows // self.nx
        self.ext = self.rb + 2
        self.cf = self.nx * dec


GATHERS = ("pooled", "skip", "hidden", "coarse", "dz2", "dz1")
FINE = ("hidden", "dz4", "dz3")


class Conv:
    def __init__(self, dm, o, c, blocks):
        self.o, self.c, self.blocks = o, c, blocks
        self.length = 27 * c
        self.chunks = -(-self.length // LANES)
        self.per = LANES // o
        self.tiles = -(-9 // self.per)
        self.wide = self.tiles * LANES
        self.kind = storage(min(size for size, _, _ in blocks))
        self.needed = sum(size for size, _, _ in blocks)
        self.full = max(1, 9 // self.per)
        self.left = max(0, 9 - self.full * self.per)
        self.group = 3 * self.full + (self.left > 0)
        self.count = c // 16 * self.group
        self.share = -(-self.count // dm.nd)
        self.taps = 9 * o
        self.stored = -(-3 * o // 16) * 16


def kernel(dm, names, *refs):
    k_ = types.SimpleNamespace(**dict(zip(names, refs)))
    nd, nc, nx, S, R, H = dm.nd, dm.nc, dm.nx, dm.s, dm.rows, dm.half
    W, V = dm.cols, dm.hcols
    Q, RB, E = H // 2, dm.rb, dm.ext
    place = lax.axis_index("depth")
    me = lax.axis_index("chan")
    x, core = lax.div(me, 2), lax.rem(me, 2)
    other = 1 - core
    mate = 2 * x + other
    row0, h0 = x * RB, x * (RB // 2)
    first, last = place == 0, place == nd - 1
    top, bottom = x == 0, x == nx - 1
    convs = dm.convs
    pending = []
    wt, wf, wx, wb = ([getattr(k_, f"{kind}{i}") for i in range(4)] for kind in ("wt", "wf", "wx", "wb"))
    gp = (k_.gp1, k_.gp2, k_.gp3)
    gt, gr, ga = ([getattr(k_, f"{kind}{i}") for i in range(4)] for kind in ("gt", "gr", "ga"))
    weights = (k_.w0, k_.w1, k_.w2, k_.w3)
    grads = (k_.g0, k_.g1, k_.g2, k_.g3)
    turned, acc = k_.turned, k_.acc

    def no(cond):
        return jnp.logical_not(cond)

    def peer_copy(src, dst, send, recv, depth, chan):
        return pltpu.make_async_remote_copy(
            src_ref=src, dst_ref=dst, send_sem=send, recv_sem=recv,
            device_id={"depth": depth, "chan": chan}, device_id_type=MESH,
        )

    def guarded(cond, fn):
        if cond is None:
            fn()
        else:
            pl.when(cond)(fn)

    def drain():
        for cond, fn in pending:
            guarded(cond, fn)
        pending.clear()

    def launch(cond, copy):
        guarded(cond, lambda: copy().start())
        pending.append((cond, lambda: copy().wait_send()))

    def arrive(cond, copy):
        guarded(cond, lambda: copy().wait_recv())

    def both(a, b):
        return b if a is None else a if b is None else jnp.logical_and(a, b)

    can_send = (no(last), None, no(first))
    can_recv = (no(first), None, no(last))

    def slices(side, n):
        return (pl.ds(n, 1), pl.ds(1, n), pl.ds(1, 1))[side], (pl.ds(0, 1), pl.ds(1, n), pl.ds(n + 1, 1))[side]

    def at_x(t):
        up, down = x + t, x - t
        return jnp.where(up >= nx, up - nx, up), jnp.where(down < 0, down + nx, down)


    def gather_start(ref, which, source_at=None):
        n = ref.shape[2] - 2
        k = GATHERS.index(which)
        for side in (0, 2, 1):
            own, theirs = slices(side, n)
            for t in range(nx):
                if side == 1 and t == 0:
                    continue
                tox = at_x(t)[0]

                def copy(side=side, t=t, own=own, theirs=theirs, tox=tox):
                    start = (n, 1, 1)[side] - 1
                    size = (1, n, 1)[side]
                    src = ref.at[core, x, own] if source_at is None else source_at(pl.ds(start, size), tox)
                    return peer_copy(
                        src, ref.at[core, x, theirs], k_.g_send.at[k, side, t], k_.g_recv.at[k, side],
                        place + 1 - side, 2 * tox + core,
                    )

                launch(can_send[side], copy)
        gather_own(ref, which)

    def handed(ref, k, piece, i):
        return peer_copy(piece, piece, k_.h_send.at[k, i], k_.h_recv.at[k], place, mate)

    def gather_own(ref, which):
        k = GATHERS.index(which)
        launch(None, lambda: handed(ref, k, ref.at[core, x, pl.ds(1, ref.shape[2] - 2)], 0))

    def gather_pass(ref, which):
        n = ref.shape[2] - 2
        k = GATHERS.index(which)
        for side in (1, 0, 2):
            theirs = slices(side, n)[1]
            if side != 1:
                pieces = [ref.at[core, :, theirs]]
            else:
                pieces = [ref.at[core, at_x(t)[1], theirs] for t in range(1, nx)]
            for i, got in enumerate(pieces):
                arrive(
                    can_recv[side],
                    lambda got=got, side=side: peer_copy(
                        got, got, k_.g_send.at[k, side, 0], k_.g_recv.at[k, side], place, mate
                    ),
                )
                launch(None, lambda got=got, i=i, side=side: handed(ref, k, got, 1 + (side // 2 if side != 1 else 2 + i)))

    def gather_wait(ref, which):
        handed(ref, GATHERS.index(which), ref.at[other], 0).wait_recv()

    def fine_parts(ref, which, side):
        k = FINE.index(which)
        own, theirs = slices(side, S)
        inner = pl.ds(1, RB)
        rows = [(None, None, inner, inner, x, core, core)] if side != 1 else [(None, None, inner, inner, x, other, other)]
        if nx > 1:
            for c in range(2):
                rows.append((no(top), no(bottom), pl.ds(1, 1), pl.ds(E - 1, 1), x - 1, c, c))
                rows.append((no(bottom), no(top), pl.ds(RB, 1), pl.ds(0, 1), x + 1, c, c))
        parts = []
        for i, (sends, gets, row, at, tox, to, source) in enumerate(rows):
            target = ref.at[core, theirs, at]
            theirs_ = ref.at[source, theirs, at]
            up = (i - 1) % 2
            arrived = 0 if i == 0 else 1 + up * 2 + core
            expected = 0 if i == 0 else 1 + up * 2 + source
            send = k_.x_send.at[k, side, i]
            parts.append((
                both(can_send[side], sends), both(can_recv[side], gets),
                functools.partial(
                    peer_copy, ref.at[core, own, row], target, send, k_.x_recv.at[k, side, arrived],
                    place + 1 - side, 2 * tox + to,
                ),
                functools.partial(peer_copy, theirs_, theirs_, send, k_.x_recv.at[k, side, expected], place, mate),
            ))
        return parts

    def fine_start(ref, which):
        for side in (0, 2, 1):
            for sends, _, out, _ in fine_parts(ref, which, side):
                launch(sends, out)

    def fine_halo(ref, which, side, c):
        k = FINE.index(which)
        block = ref.at[c, slices(side, S)[1], pl.ds(1, RB)]
        return peer_copy(block, block, k_.y_send.at[k, side], k_.y_recv.at[k, side], place, mate)

    def fine_pass(ref, which):
        for side in (0, 2):
            _, gets, _, back = fine_parts(ref, which, side)[0]
            arrive(gets, back)
            launch(gets, functools.partial(fine_halo, ref, which, side, core))

    def fine_wait(ref, which):
        for side in (1, 0, 2):
            for _, gets, _, back in fine_parts(ref, which, side)[side != 1 :]:
                arrive(gets, back)
            if side != 1:
                arrive(can_recv[side], functools.partial(fine_halo, ref, which, side, other))

    def natural(ref, s, r):
        v = ref[:, s, r]
        size = dm.cd
        return jnp.concatenate(
            [v[c, i * size : (i + 1) * size] for i in range(nx) for c in range(2)], 0
        ).astype(BF16)

    def in_turn(count, fn):
        if count <= 16:
            for i in range(count):
                fn(i)
        else:

            def body(i, carry):
                fn(i)
                return carry

            lax.fori_loop(0, count, body, 0)

    def slab_peers(i):
        to = place + 1 + i
        return jnp.where(to >= nd, to - nd, to), me

    def wide_peers(i):
        i = i + 1
        dt, xt = (i // nx, i % nx) if isinstance(i, int) else (lax.div(i, nx), lax.rem(i, nx))
        to, tox = place + dt, x + xt
        return jnp.where(to >= nd, to - nd, to), 2 * jnp.where(tox >= nx, tox - nx, tox) + core

    def exchange(n, peers, copy):
        in_turn(n - 1, lambda i: copy(*peers(i)).start())

    def sum_start(group, ref, k, slot, tile, source=None):
        n, own, peers, send, recv = group
        ref[slot, own] = tile

        def copy(depth, chan):
            src = ref.at[slot, own] if source is None else source(chan)
            return peer_copy(src, ref.at[slot, own], send.at[k], recv.at[k], depth, chan)

        exchange(n, peers, copy)
        pending.append((None, lambda: all_of(group, ref, k, slot).wait_send()))

    def all_of(group, ref, k, slot):
        n, _, _, send, recv = group
        every = ref.at[slot, pl.ds(0, n - 1)]
        return peer_copy(every, every, send.at[k], recv.at[k], place, mate)

    def sum_finish(group, ref, k, slot):
        all_of(group, ref, k, slot).wait_recv()
        return jnp.sum(ref[slot], axis=0)

    slabs = (nd, place, slab_peers, k_.t_send, k_.t_recv)
    everyone = (nd * nx, place * nx + x, wide_peers, k_.u_send, k_.u_recv)

    def columns_of(row, m):
        lane, channel = iota((m, LANES), 1), iota((m, LANES), 0)
        return tuple(
            jnp.sum(jnp.where(lane == channel + i * m, row, 0.0), axis=1, keepdims=True) for i in range(2)
        )

    def coarse_sums(slot, sums):
        sum_start(slabs, k_.st, slot, slot, pack(*sums))

    def coarse_totals(slot):
        return columns_of(sum_finish(slabs, k_.st, slot, slot), dm.ce)

    def fine_sums(slot, sums):
        sum_start(everyone, k_.su, slot, slot, pack(*sums))

    def fine_totals(slot):
        return columns_of(sum_finish(everyone, k_.su, slot, slot), dm.cf)

    def prepare(k):
        cv, w, own = convs[k], weights[k], wt[k]
        out = wf[k] if k < 2 else wf[k].at[x]
        eye = (iota((LANES, LANES), 0) == iota((LANES, LANES), 1)).astype(BF16)

        def chunk(a):
            return dot_nt(eye, jnp.concatenate([a] * cv.per, 0).astype(BF16))

        full = cv.length // LANES

        def body(i, carry):
            at = pl.multiple_of(i * LANES, LANES)
            turned[pl.ds(at, LANES)] = chunk(w[:, pl.ds(at, LANES)])
            return carry

        lax.fori_loop(0, full, body, 0, unroll=4)
        if full < cv.chunks:
            a = w[:, full * LANES :]
            a = jnp.concatenate([a, jnp.zeros((cv.o, LANES - a.shape[1]), F32)], 1)
            turned[full * LANES : (full + 1) * LANES] = chunk(a)
        group = iota((cv.c, LANES), 1) // cv.o
        for kz in range(3):
            for j in range(cv.tiles):
                tile = None
                for g in range(cv.per):
                    u = j * cv.per + g
                    if u < 9:
                        kx, ky = u // 3, u % 3
                        v = turned[pl.ds(9 * kz + 3 * ky + kx, cv.c, stride=27)]
                        tile = v if tile is None else jnp.where(group == g, v, tile)
                own[kz, :, j * LANES : (j + 1) * LANES] = tile.astype(BF16).astype(own.dtype)
        for j in range(cv.tiles):
            v = jnp.concatenate([own[kz, :, j * LANES : (j + 1) * LANES] for kz in range(3)], 0)
            size = min(LANES, cv.taps - j * LANES)
            v = dot_nt(eye, v.astype(BF16))[0:size]
            if k < 2:
                out[j * LANES : j * LANES + size] = v.astype(BF16)
            else:
                k_.flip[j * LANES : j * LANES + size, 0 : 3 * cv.c] = v
        if k >= 2:
            out[0 : 3 * cv.o] = jnp.concatenate(
                [
                    jnp.concatenate(
                        [
                            k_.flip[(3 * kx + ky) * cv.o : (3 * kx + ky + 1) * cv.o, kz * cv.c : (kz + 1) * cv.c]
                            for kx in range(3)
                        ],
                        0,
                    )
                    for kz in range(3)
                    for ky in range(3)
                ],
                1,
            ).astype(BF16)

    def forward_copy(k, t):
        block = wf[k].at[x]
        return peer_copy(
            block, block, k_.p_send.at[k - 2, t], k_.p_recv.at[k - 2, t], place, 2 * lax.rem(x + t, nx) + core
        )

    def forward_start(k):
        for t in range(1, nx):
            launch(None, functools.partial(forward_copy, k, t))

    def forward_wait(k):
        for t in range(1, nx):
            fromx = lax.rem(x + nx - t, nx)
            block = wf[k].at[fromx]
            peer_copy(
                block, block, k_.p_send.at[k - 2, t], k_.p_recv.at[k - 2, t], place, 2 * fromx + core
            ).wait_recv()

    def forward_weight(k):
        return jnp.concatenate([wf[k][i, 0 : 3 * convs[k].o] for i in range(nx)], 0)

    def weights_start(k):
        cv = convs[k]
        for b, (size, start, at) in enumerate(cv.blocks):
            wx[k][me, :, at : at + size] = wt[k][:, pl.ds(start(me), size)]
            for t in range(1, nc):
                to = lax.rem(me + t, nc)

                def copy(to=to, t=t, b=b, size=size, start=start, at=at):
                    return peer_copy(
                        wt[k].at[:, pl.ds(start(to), size)], wx[k].at[me, :, pl.ds(at, size)],
                        k_.w_send.at[k, b, t], k_.w_recv.at[k, b, t], place, to,
                    )

                launch(None, copy)

    def weights_finish(k):
        cv = convs[k]
        for b, (size, _, at) in enumerate(cv.blocks):
            for t in range(1, nc):
                source = lax.rem(me + nc - t, nc)
                theirs = wx[k].at[source, :, pl.ds(at, size)]
                peer_copy(theirs, theirs, k_.w_send.at[k, b, t], k_.w_recv.at[k, b, t], place, source).wait_recv()

        parts = 9 if k < 2 else 3
        lanes = cv.taps // parts
        for i in range(parts):
            at = (parts - 1 - i) * lanes
            found = [wx[k][j, 2 - kz, :, at : at + lanes].astype(F32) for kz in range(3) for j in range(nc)]
            wb[k][i * cv.needed : (i + 1) * cv.needed] = jnp.concatenate(found, 1).astype(BF16)

    def tiles_of(k, part, put):
        cv, dense = convs[k], k_.dense
        rows, size = 3 * cv.c, 3 * cv.o
        for ky in range(3):
            at = ky * LANES + part * size
            dense[0:rows, ky * size : (ky + 1) * size] = acc[0:rows, at : at + size]

        def tile(i, carry):
            left = []
            for kz in range(3):
                at = pl.ds(pl.multiple_of(kz * cv.c + i * 16, 16), 16)
                for j in range(cv.full):
                    put(i * cv.group + kz * cv.full + j, dense[at, j * LANES : (j + 1) * LANES].astype(BF16))
                left.append(dense[at, cv.full * LANES : cv.full * LANES + cv.left * cv.o])
            if cv.left:
                used = 3 * cv.left * cv.o
                v = jnp.concatenate(left + [jnp.zeros((16, LANES - used), F32)], 1)
                put(i * cv.group + 3 * cv.full, v.astype(BF16))
            return carry

        lax.fori_loop(0, cv.c // 16, tile, 0, unroll=2)

    def cross_start(k):
        gs, gx = (k_.gs2, k_.gs3)[k - 2], (k_.gx2, k_.gx3)[k - 2]

        for part in range(nx):

            def put(i, v, part=part):
                gs[part, i] = v

            tiles_of(k, part, put)
        for t in range(1, nx):

            def copy(t=t):
                tox = at_x(t)[0]
                return peer_copy(
                    gs.at[tox], gx.at[x], k_.c_send.at[k - 2, t], k_.c_recv.at[k - 2, t], place, 2 * tox + core
                )

            launch(None, copy)

    def cross_finish(k):
        cv, gs, gx = convs[k], (k_.gs2, k_.gs3)[k - 2], (k_.gx2, k_.gx3)[k - 2]
        sources = [at_x(t)[1] for t in range(1, nx)]
        for t, fromx in enumerate(sources, 1):
            theirs = gx.at[fromx]
            peer_copy(
                theirs, theirs, k_.c_send.at[k - 2, t], k_.c_recv.at[k - 2, t], place, 2 * fromx + core
            ).wait_recv()

        def add(i, carry):
            for j in range(cv.group):
                p = cv.group * i + j
                v = gs[x, p].astype(F32)
                for fromx in sources:
                    v += gx[fromx, p].astype(F32)
                gt[k][p] = v.astype(BF16)
            return carry

        lax.fori_loop(0, cv.c // 16, add, 0, unroll=2)
        reduce_send(k)

    def reduce_start(k):
        def put(i, v):
            gt[k][i] = v

        tiles_of(k, 0, put)
        reduce_send(k)

    nh = nd // 2
    par, rank = lax.rem(place, 2), lax.div(place, 2)
    partner = place + 1 - 2 * par

    def rank_peers(i):
        to = rank + 1 + i
        return 2 * jnp.where(to >= nh, to - nh, to) + par, me

    def half_of(k, which):
        size = nh * convs[k].share
        return pl.ds(which * size, size)

    def share_of(k, owner):
        size = convs[k].share
        if k == 0:
            return pl.ds(owner * size, size)
        return pl.ds((lax.rem(owner, 2) * nh + lax.div(owner, 2)) * size, size)

    def level(k):
        return (nd, slab_peers, place) if k == 0 else (nh, rank_peers, rank)

    def pair_copy(src, dst, k, i):
        return peer_copy(src, dst, k_.q_send.at[k, i], k_.q_recv.at[k, i], partner, me)

    def reduce_send(k):
        cv = convs[k]
        for i in range(cv.count, cv.share * nd):
            gt[k][i] = jnp.zeros((16, LANES), BF16)
        if k == 0:
            spread_shares(k)
        else:
            launch(None, lambda: pair_copy(gt[k].at[half_of(k, 1 - par)], gp[k - 1], k, 0))

    def pair_finish(k):
        pair_copy(gp[k - 1], gp[k - 1], k, 0).wait_recv()
        own = half_of(k, par)
        gt[k][own] = (gt[k][own].astype(F32) + gp[k - 1][...].astype(F32)).astype(BF16)
        spread_shares(k)

    def spread_shares(k):
        n, peers, own = level(k)
        gr[k][own] = gt[k][share_of(k, place)]

        def copy(to, chan):
            return peer_copy(gt[k].at[share_of(k, to)], gr[k].at[own], k_.r_send.at[k], k_.r_recv.at[k], to, chan)

        exchange(n, peers, copy)
        pending.append((None, lambda: reduce_all(k).wait_send()))

    def reduce_all(k):
        every = gr[k].at[pl.ds(0, level(k)[0] - 1)]
        return peer_copy(every, every, k_.r_send.at[k], k_.r_recv.at[k], place, mate)

    def share_all(k):
        every = ga[k].at[pl.ds(0, (level(k)[0] - 1) * convs[k].share)]
        return peer_copy(every, every, k_.a_send.at[k], k_.a_recv.at[k], place, mate)

    def reduce_finish(k):
        reduce_all(k).wait_recv()
        own = share_of(k, place)
        ga[k][own] = jnp.sum(gr[k][...].astype(F32), axis=0).astype(BF16)

        def copy(to, chan):
            return peer_copy(ga[k].at[own], ga[k].at[own], k_.a_send.at[k], k_.a_recv.at[k], to, chan)

        n, peers, _ = level(k)
        exchange(n, peers, copy)
        pending.append((None, lambda: share_all(k).wait_send()))

    def share_pass(k):
        share_all(k).wait_recv()
        own = ga[k].at[half_of(k, par)]
        launch(None, lambda: pair_copy(own, own, k, 1))

    def gradient_out(k):
        cv, out = convs[k], grads[k]
        if k == 0:
            share_all(k).wait_recv()
        else:
            theirs = ga[k].at[half_of(k, 1 - par)]
            pair_copy(theirs, theirs, k, 1).wait_recv()
        group = iota((16, LANES), 1) // cv.o

        def scatter(i, carry):
            def put(v, g, kz, t):
                turned[pl.ds(9 * kz + t + i * (16 * 27), 16, stride=27)] = jnp.where(group == g, v, 0.0)

            for kz in range(3):
                for j in range(cv.full):
                    v = ga[k][i * cv.group + kz * cv.full + j].astype(F32)
                    for g in range(min(cv.per, 9)):
                        put(v, g, kz, j * cv.per + g)
            if cv.left:
                v = ga[k][i * cv.group + 3 * cv.full].astype(F32)
                for kz in range(3):
                    for g in range(cv.left):
                        put(v, kz * cv.left + g, kz, cv.full * cv.per + g)
            return carry

        lax.fori_loop(0, cv.c // 16, scatter, 0, unroll=2)

        pick = (iota((cv.o, LANES), 1) % cv.o == iota((cv.o, LANES), 0)).astype(BF16)
        step = 8 * LANES
        for at in range(0, cv.length, step):
            size = min(step, cv.length - at)
            v = dot_nt(pick, turned[at : at + -(-size // LANES) * LANES].astype(BF16))
            out[:, at : at + size] = v[:, 0:size]

    def column(row):
        n = row.shape[1]
        eye = iota((n, n), 0) == iota((n, n), 1)
        return jnp.sum(jnp.where(eye, row, 0.0), axis=1, keepdims=True)

    def row_of(col):
        n = col.shape[0]
        eye = iota((n, n), 0) == iota((n, n), 1)
        return jnp.sum(jnp.where(eye, col, 0.0), axis=0, keepdims=True)

    def clear_halos(ref):
        def clear(at):
            if len(ref.shape) == 5:
                for c in range(2):
                    ref[c, at] = jnp.zeros(ref.shape[2:], ref.dtype)
            else:
                for i in range(nx):
                    ref[core, i, at] = jnp.zeros(ref.shape[3:], ref.dtype)

        pl.when(first)(lambda: clear(0))
        pl.when(last)(lambda: clear(ref.shape[-4] - 1))

    def clear_rows(ref):
        def clear(at):
            for c in range(2):
                for i in range(S + 2):
                    ref[c, i, at] = jnp.zeros(ref.shape[3:], ref.dtype)

        pl.when(top)(lambda: clear(0))
        pl.when(bottom)(lambda: clear(E - 1))

    def conv(operand, weight, m, groups, emit, init):
        def body(d, carry):
            v = operand(d)
            y = dot(weight, v)
            results = []
            for j in range(RB):
                lanes = slice(j * LANES, (j + 1) * LANES)
                parts = []
                for g in range(groups):
                    a = [y[(3 * g + kx) * m : (3 * g + kx + 1) * m, lanes] for kx in range(3)]
                    parts.append(from_left(a[0], W) + a[1] + from_right(a[2], W))
                results.append(jnp.concatenate(parts, 0) if groups > 1 else parts[0])
            return emit(d, results, carry)

        return lax.fori_loop(0, S, body, init)

    def rows_of(row):
        return lambda d: jnp.concatenate(
            [jnp.concatenate([row(d + kz, ky + j) for j in range(RB)], 1) for kz in range(3) for ky in range(3)], 0
        )

    def blocks_of(ref):
        size = dm.cd
        return lambda d: jnp.concatenate(
            [
                jnp.concatenate([ref[c, d + kz, 2 - ky + j, i * size : (i + 1) * size] for j in range(RB)], 1)
                for kz in range(3)
                for i in range(nx)
                for c in range(2)
                for ky in range(3)
            ],
            0,
        ).astype(BF16)

    def conv_stats(row, weight, z):
        def emit(d, results, carry):
            total, square = carry
            for j, v in enumerate(results):
                z[d * RB + j] = v
                total, square = total + v, square + v * v
            return total, square

        blank = jnp.zeros((dm.cf, LANES), F32)
        return conv(rows_of(row), weight, dm.cd, nx, emit, (blank, blank))

    def weight_grad(row, k):
        cv = convs[k]

        def part(d):
            v = jnp.concatenate([jnp.concatenate([row(d + kz, j) for j in range(E)], 1) for kz in range(3)], 0)
            y = jnp.concatenate(
                [k_.dzt[d, (2 - ky) * LANES : (2 - ky + E) * LANES] for ky in range(3)], 1
            )
            return dot(v, y)

        acc[0 : 3 * cv.c] = part(0)

        def more(d, carry):
            acc[0 : 3 * cv.c] += part(d)
            return carry

        lax.fori_loop(1, S, more, 0)

    def conv_coarse(ref, weight, m):
        v = jnp.concatenate(
            [jnp.concatenate([flat(ref, kz, i) for i in range(Q)], 1) for kz in range(3)], 0
        )
        y = dot(weight[...], v)
        blank = jnp.zeros((m, LANES), F32)

        def shifted(ky, i):
            if not 0 <= i < Q:
                return blank
            a, b, c = (
                y[(3 * kx + ky) * m : (3 * kx + ky + 1) * m, i * LANES : (i + 1) * LANES] for kx in range(3)
            )
            return from_left(a, V) + b + from_right(c, V)

        before = [shifted(0, i) for i in range(-1, Q)]
        after = [shifted(2, i) for i in range(Q + 1)]
        return [
            shifted(1, i) + halves(before[i + 1] + after[i + 1], before[i] + after[i]) for i in range(Q)
        ]

    def conv_stats_coarse(ref, weight, z, m):
        total = square = jnp.zeros((m, LANES), F32)
        for i, v in enumerate(conv_coarse(ref, weight, m)):
            z[i] = v
            total, square = total + v, square + v * v
        return total, square

    def weight_grad_coarse(ref, k):
        cv = convs[k]
        v = jnp.concatenate(
            [jnp.concatenate([flat(ref, kz, i) for i in range(Q)], 1) for kz in range(3)], 0
        )
        y = jnp.concatenate([k_.dzct[(2 - ky) * V : (2 - ky) * V + Q * LANES] for ky in range(3)], 1)
        acc[0 : 3 * cv.c] = dot(v, y)

    def pack(a, b):
        m = a.shape[0]
        a = jnp.sum(a, axis=1, keepdims=True)
        b = jnp.sum(b, axis=1, keepdims=True)
        lane, channel = iota((m, LANES), 1), iota((m, LANES), 0)
        both = jnp.where(lane == channel, a, jnp.where(lane == channel + m, b, 0.0))
        return jnp.sum(both, axis=0, keepdims=True)

    def moments(total, count):
        mean = total[0] / count
        var = total[1] / count - mean * mean
        return mean, lax.rsqrt(var + EPS)

    def wide(column):
        return jnp.broadcast_to(column, (column.shape[0], LANES))

    def factors(stats, norm):
        mean, inv = stats
        gain, shift = norm
        return wide(mean), wide(gain * inv), wide(shift)

    def norm_rows(z, stats, norm, emit, n):
        mean, scale, shift = factors(stats, norm)

        def body(i, carry):
            for j in range(n):
                p = i * n + j
                u = (z[p] - mean) * scale + shift
                emit(p, u * jax.nn.sigmoid(u))
            return carry

        lax.fori_loop(0, z.shape[0] // n, body, 0)

    def norm_back_sums(z, keep_du, stats, norm, grad, n):
        mean, scale, shift = factors(stats, norm)
        inv = wide(stats[1])
        m = z.shape[1]

        def body(i, carry):
            a, b = carry
            for j in range(n):
                p = i * n + j
                centred = z[p] - mean
                u = centred * scale + shift
                sigma = jax.nn.sigmoid(u)
                v = grad(p) * sigma * (1.0 + u * (1.0 - sigma))
                keep_du(p, v)
                a, b = a + v, b + v * (centred * inv)
            return a, b

        blank = jnp.zeros((m, LANES), F32)
        return lax.fori_loop(0, z.shape[0] // n, body, (blank, blank))

    def back_factors(stats, norm, total, count):
        mean, inv = stats
        scale = norm[0] * inv
        return wide(mean), wide(scale), wide(-scale * total[0] / count), wide(-scale * inv * total[1] / count)

    def columns_first(copies, groups):
        size = copies[0].shape[0] // groups
        rows = [v[g * size : (g + 1) * size] for g in range(groups) for v in copies]
        used = 3 * groups * size
        if used < LANES:
            rows.append(jnp.zeros((LANES - used, LANES), F32))
        return jnp.transpose(jnp.concatenate(rows, 0)).astype(BF16)

    def norm_back_fine(z, given, ref):
        mean, scale, level, slope = given

        def body(d, carry):
            for r in range(RB):
                p = d * RB + r
                v = scale * k_.du_f[p] + level + slope * (z[p] - mean)
                ref[core, 1 + d, 1 + r] = v.astype(BF16).astype(ref.dtype)
            return carry

        lax.fori_loop(0, S, body, 0)

    def turn_fine(ref):
        n = 4 if RB % 4 == 0 else 2

        def body(i, carry):
            d = lax.div(i, RB // n)
            r0 = (i - d * (RB // n)) * n
            for j in range(n):
                v = ref[core, 1 + d, 1 + r0 + j].astype(F32)
                at = pl.ds(pl.multiple_of((2 + r0 + j) * LANES, LANES), LANES)
                k_.dzt[d, at] = columns_first((from_right(v, W), v, from_left(v, W)), nx)
            return carry

        lax.fori_loop(0, S * RB // n, body, 0)

    def norm_back_coarse(z, given, ref):
        mean, scale, level, slope = given
        for i in range(Q):
            v = scale * k_.du_c[i] + level + slope * (z[i] - mean)
            ref[core, x, 1, i] = v.astype(BF16).astype(ref.dtype)

    def turn_coarse(ref):
        for i in range(Q):
            v = ref[core, x, 1, i].astype(F32)
            k_.dzct[V + i * LANES : V + (i + 1) * LANES] = columns_first((from_right(v, V), v, from_left(v, V)), 1)

    def keep_du(ref):
        def store(p, v):
            ref[p] = v

        return store

    barrier = pltpu.get_barrier_semaphore()

    def greet(depth, chan):
        pl.semaphore_signal(barrier, inc=1, device_id={"depth": depth, "chan": chan}, device_id_type=MESH)

    exchange(nd * nx, wide_peers, lambda depth, chan: types.SimpleNamespace(start=lambda: greet(depth, chan)))
    for t in range(nx):
        to = 2 * at_x(t)[0] + other
        greet(place, to)
        if t > 0:
            pl.when(no(first))(lambda to=to: greet(place - 1, to))
            pl.when(no(last))(lambda to=to: greet(place + 1, to))

    hc = iota((LANES, LANES), 0)
    fc = iota((LANES, LANES), 1)
    half = LANES // 2

    def up_table(coarse, fine):
        base = fine // 2
        beside = jnp.clip(base + jnp.where(fine % 2 == 0, -1, 1), 0, V - 1)
        near = (coarse == base).astype(F32)
        far = (coarse == beside).astype(F32)
        return (0.75 * near + 0.25 * far).astype(BF16)

    pool = jnp.concatenate([(hc // 2 == fc - at).astype(BF16) for at in (0, half)], 0)
    spread = jnp.concatenate([(hc - at == fc // 2).astype(BF16) for at in (0, half)], 1)
    up = jnp.concatenate([up_table(hc - at, fc) for at in (0, half)], 1)
    down = jnp.concatenate([up_table(fc, hc)] * 2, 0)
    spread2 = jnp.concatenate([spread, spread], 0)

    def take_rows(ref):
        for c in range(ref.shape[0]):
            k_.rows[c * S * R : (c + 1) * S * R] = ref[c].astype(F32).reshape(S * R, LANES)

    def row_of_all(p, chans):
        return k_.rows[pl.ds(p, chans, stride=S * R)]

    xp, xs, own_skip = k_.xp, k_.xs, k_.own_skip
    clear_halos(xp)
    take_rows(k_.skip)
    for i in range(S):
        for r in (0, R + 1):
            own_skip[i, r] = jnp.zeros((dm.cs, LANES), own_skip.dtype)

    def take_skip(i, carry):
        parts = []
        for d in range(S):
            v = [row_of_all(d * R + 4 * i + j, dm.cs).astype(BF16) for j in range(4)]
            for j in range(4):
                own_skip[d, 1 + 4 * i + j] = v[j].astype(own_skip.dtype)
            parts += [jnp.concatenate([v[j], v[2 + j]], 1) for j in range(2)]
        v = dot(jnp.concatenate(parts, 0), pool).reshape(2 * S, dm.cs, LANES)
        xp[core, x, 1, i] = (jnp.sum(v, axis=0) * 0.125).astype(BF16).astype(xp.dtype)
        return carry

    lax.fori_loop(0, Q, take_skip, 0, unroll=3)
    beside = jnp.where(first, 0, 1) + jnp.where(last, 0, 1)
    pl.semaphore_wait(barrier, nd * nx - 1 + nx + (nx - 1) * beside)
    gather_start(xp, "pooled")
    clear_halos(xs)
    xs[core, x, 1 : S + 1] = own_skip[:, pl.ds(row0, E)]
    gather_start(xs, "skip", lambda at, tox: own_skip.at[at, pl.ds(tox * RB, E)])

    gq = dm.g // nc
    columns = dm.enc_all + dm.skip_all
    gate_all, norm_all = k_.gate_all, k_.norm_all
    gate_all[me, :, 0:columns] = k_.gate[...]
    lane = iota((gq, LANES), 1)
    gate_all[me, :, 2 * LANES :] = jnp.where(
        lane == 0, column(k_.vector[0:1]), jnp.where(lane == 1, column(k_.vector[1:2]), 0.0)
    )
    for layer in range(2):
        for part in range(2):
            at = 2 * layer + part
            norm_all[me, at : at + 1, 0 : dm.cd] = k_.dn[part, layer : layer + 1]

    def constants(i, t, source, to):
        ref = (norm_all, gate_all)[i]
        return peer_copy(ref.at[source], ref.at[source], k_.v_send.at[i, t], k_.v_recv.at[i, t], place, to)

    for i in range(2):
        for t in range(1, nc):
            launch(None, functools.partial(constants, i, t, me, lax.rem(me + t, nc)))
    prepare(0)
    xd, xz4, xz3, d1 = k_.xd, k_.xz4, k_.xz3, k_.d1
    for ref in (xd, xz4, xz3):
        clear_rows(ref)
        clear_halos(ref)
    for ref in (k_.xh, k_.xz2, k_.xz1):
        clear_halos(ref)
    for i in range(S):
        for at in (0, (RB + 2) * LANES):
            k_.dzt[i, at : at + 2 * LANES] = jnp.zeros((2 * LANES, LANES), BF16)
        for r in range(3):
            k_.ug[i, r] = jnp.zeros(k_.ug.shape[2:], F32)
            k_.ug[i, RB + 3 + r] = jnp.zeros(k_.ug.shape[2:], F32)
        for r in range(H + 2):
            k_.cb[i, r] = jnp.zeros(k_.cb.shape[2:], F32)

    for at in (0, V + Q * LANES):
        k_.dzct[at : at + V] = jnp.zeros((V, LANES), BF16)

    def norm_of(layer):
        return column(k_.en[0, layer : layer + 1]), column(k_.en[1, layer : layer + 1])

    norm_e1, norm_e2 = norm_of(0), norm_of(1)

    gather_pass(xp, "pooled")
    gather_wait(xp, "pooled")
    coarse_sums(0, conv_stats_coarse(xp, wf[0], k_.z1, dm.ce))
    prepare(1)
    stats_e1 = moments(coarse_totals(0), dm.coarse_total)

    def keep_coarse(ref):
        def store(p, v):
            ref[core, x, 1, p] = v.astype(BF16).astype(ref.dtype)

        return store

    norm_rows(k_.z1, stats_e1, norm_e1, keep_coarse(k_.xh), Q)
    gather_start(k_.xh, "hidden")
    prepare(2)
    forward_start(2)
    gather_pass(k_.xh, "hidden")
    gather_pass(xs, "skip")
    gather_wait(k_.xh, "hidden")
    coarse_sums(1, conv_stats_coarse(k_.xh, wf[1], k_.z2, dm.ce))
    take_rows(k_.cot)

    def take_cot(i, carry):
        for d in range(S):
            for j in range(4):
                v = row_of_all(d * R + 4 * i + j, dm.cd).astype(BF16)
                k_.own_cot[d, 4 * i + j] = v.astype(k_.own_cot.dtype)
        return carry

    lax.fori_loop(0, Q, take_cot, 0)
    k_.cots[x] = k_.own_cot[:, pl.ds(row0, RB)]
    stats_e2 = moments(coarse_totals(1), dm.coarse_total)
    norm_rows(k_.z2, stats_e2, norm_e2, keep_coarse(k_.xc), Q)
    gather_start(k_.xc, "coarse")
    prepare(3)
    for t in range(1, nc):
        for i in range(2):
            source = lax.rem(me + nc - t, nc)
            constants(i, t, source, source).wait_recv()
    gate_full = gate_all[...].reshape(dm.g, 3 * LANES)
    wg = gate_full[:, 0:columns].astype(BF16)
    gbias = gate_full[:, 2 * LANES : 2 * LANES + 1]
    gout = gate_full[:, 2 * LANES + 1 : 2 * LANES + 2]
    k_.gate_t[...] = jnp.transpose(gate_full[:, 0 : 2 * LANES])
    own_rows = [k_.gate_t[pl.ds(pl.multiple_of((2 * i + core) * dm.ce, dm.ce), dm.ce)] for i in range(nx)]
    own_rows += [
        k_.gate_t[pl.ds(pl.multiple_of(dm.enc_all + (2 * i + core) * dm.cs, dm.cs), dm.cs)] for i in range(nx)
    ]
    k_.gate_own[...] = jnp.concatenate(own_rows, 0)

    def norm_fine(layer):
        return tuple(
            jnp.concatenate(
                [column(norm_all[2 * i + core, 2 * layer + part : 2 * layer + part + 1, 0 : dm.cd]) for i in range(nx)], 0
            )
            for part in range(2)
        )

    norm_d1, norm_d2 = norm_fine(0), norm_fine(1)
    gather_pass(k_.xc, "coarse")
    gather_wait(k_.xc, "coarse")
    forward_start(3)

    dt = k_.dt

    def up_depth(i, carry):
        t = []
        for j in range(3):
            v = dot(flat(k_.xc, j, i), up)
            t.append(jnp.stack([v[:, 0:LANES], v[:, LANES:]], 0))
        below = jnp.where(first, t[1], t[0])
        above = jnp.where(last, t[1], t[2])
        near = 0.75 * t[1]
        here = 0.25 * t[1]
        rows = pl.ds(i * 2, 2)
        dt[0, rows] = jnp.where(first, 0.0, 0.75 * below + here)
        dt[1, rows] = near + 0.25 * below
        dt[2, rows] = near + 0.25 * above
        dt[3, rows] = jnp.where(last, 0.0, 0.75 * above + here)
        return carry

    lax.fori_loop(0, Q, up_depth, 0)

    def up_rows(i, carry):
        here = h0 + i
        before, after = jnp.maximum(here - 1, 0), jnp.minimum(here + 1, H - 1)
        for j in range(S + 2):
            v = 0.75 * dt[j, here]
            d1[j, 1 + 2 * i, 0 : dm.enc_all] = (v + 0.25 * dt[j, before]).astype(BF16)
            d1[j, 2 + 2 * i, 0 : dm.enc_all] = (v + 0.25 * dt[j, after]).astype(BF16)
        return carry

    lax.fori_loop(0, RB // 2, up_rows, 0)
    for edge, at, near, far in (
        (top, 0, jnp.maximum(h0 - 1, 0), h0),
        (bottom, E - 1, jnp.minimum(h0 + RB // 2, H - 1), h0 + RB // 2 - 1),
    ):
        for j in range(S + 2):
            v = jnp.where(edge, 0.0, 0.75 * dt[j, near] + 0.25 * dt[j, far])
            d1[j, at, 0 : dm.enc_all] = v.astype(BF16)
    for t in range(1, nx):
        tox = lax.rem(x + t, nx)

        def send_cot(t=t, tox=tox):
            return peer_copy(
                k_.own_cot.at[:, pl.ds(tox * RB, RB)], k_.cots.at[x], k_.o_send.at[0, t], k_.o_recv.at[0, t],
                place, 2 * tox + core,
            )

        launch(None, send_cot)

    gather_wait(xs, "skip")
    gate_n = E // 2

    def gate(i, carry):
        j = lax.div(i, 2)
        r0 = (i - 2 * j) * gate_n
        skips = [flat(xs, j, r0 + q) for q in range(gate_n)]
        v = jnp.concatenate(
            [
                jnp.concatenate([d1[j, r0 + q, 0 : dm.enc_all] for q in range(gate_n)], 1),
                jnp.concatenate(skips, 1),
            ],
            0,
        )
        pre = dot(wg, v) + gbias
        act = pre * jax.nn.sigmoid(pre)
        alpha = jax.nn.sigmoid(jnp.sum(gout * act, axis=0, keepdims=True))
        for q in range(gate_n):
            lanes = slice(q * LANES, (q + 1) * LANES)
            d1[j, r0 + q, dm.enc_all :] = (alpha[:, lanes] * skips[q].astype(F32)).astype(BF16)
            k_.pre[j, r0 + q] = pre[:, lanes]
            k_.alpha[j, r0 + q] = alpha[:, lanes]
        return carry

    lax.fori_loop(0, (S + 2) * 2, gate, 0)
    for k in (3, 2, 1, 0):
        weights_start(k)

    def row_d1(j, r):
        return d1[j, r]

    def row_xd(j, r):
        return natural(xd, j, r)

    forward_wait(2)
    fine_sums(0, conv_stats(row_d1, forward_weight(2), k_.z3))
    drain()
    forward_wait(3)
    stats_d1 = moments(fine_totals(0), dm.fine_total)

    def keep_dec(p, v):
        d = lax.div(p, RB)
        xd[core, 1 + d, 1 + p - d * RB] = v.astype(BF16).astype(xd.dtype)

    norm_rows(k_.z3, stats_d1, norm_d1, keep_dec, RB)
    fine_start(xd, "hidden")
    for t in range(1, nx):
        fromx = lax.rem(x + nx - t, nx)
        theirs = k_.cots.at[fromx]
        peer_copy(theirs, theirs, k_.o_send.at[0, t], k_.o_recv.at[0, t], place, 2 * fromx + core).wait_recv()
    fine_pass(xd, "hidden")
    weights_finish(3)
    fine_wait(xd, "hidden")
    fine_sums(1, conv_stats(row_xd, forward_weight(3), k_.z4))
    stats_d2 = moments(fine_totals(1), dm.fine_total)

    def row_cot(p):
        d = lax.div(p, RB)
        return jnp.concatenate([k_.cots[i, d, p - d * RB] for i in range(nx)], 0).astype(F32)

    fine_sums(2, norm_back_sums(k_.z4, keep_du(k_.du_f), stats_d2, norm_d2, row_cot, RB))

    def keep_result(p, v):
        for i in range(nx):
            k_.ob[i, p] = v[i * dm.cd : (i + 1) * dm.cd].astype(BF16).astype(k_.ob.dtype)

    norm_rows(k_.z4, stats_d2, norm_d2, keep_result, RB)
    for t in range(1, nx):
        tox = lax.rem(x + t, nx)

        def send_result(t=t, tox=tox):
            return peer_copy(
                k_.ob.at[tox], k_.oi.at[x], k_.o_send.at[1, t], k_.o_recv.at[1, t], place, 2 * tox + core
            )

        launch(None, send_result)
    total_d2 = fine_totals(2)
    norm_back_fine(k_.z4, back_factors(stats_d2, norm_d2, total_d2, dm.fine_total), xz4)
    fine_start(xz4, "dz4")
    turn_fine(xz4)
    weight_grad(row_xd, 3)
    fine_pass(xz4, "dz4")
    cross_start(3)
    fine_wait(xz4, "dz4")

    def keep_grad(d, results, carry):
        for j, v in enumerate(results):
            k_.gg[d * RB + j] = v
        return carry

    conv(blocks_of(xz4), wb[3][...], dm.cf, 1, keep_grad, 0)
    fine_sums(3, norm_back_sums(k_.z3, keep_du(k_.du_f), stats_d1, norm_d1, lambda p: k_.gg[p], RB))
    cross_finish(3)
    total_d1 = fine_totals(3)
    norm_back_fine(k_.z3, back_factors(stats_d1, norm_d1, total_d1, dm.fine_total), xz3)
    fine_start(xz3, "dz3")
    turn_fine(xz3)
    weights_finish(2)
    weight_grad(row_d1, 2)
    fine_pass(xz3, "dz3")
    cross_start(2)
    pair_finish(3)
    fine_wait(xz3, "dz3")

    ups = nx * dm.ce

    def gate_back(d, results, carry):
        bias, psi = carry
        lows = []
        for j, both in enumerate(results):
            p = d * RB + j
            v = both[ups:]
            grad = jnp.sum(v * flat(xs, d + 1, 1 + j).astype(F32), axis=0, keepdims=True)
            alpha = k_.alpha[d + 1, 1 + j]
            logit = grad * alpha * (1.0 - alpha)
            pre = k_.pre[d + 1, 1 + j]
            sigma = jax.nn.sigmoid(pre)
            psi = psi + pre * sigma * logit
            low = (logit * gout * sigma * (1.0 + pre * (1.0 - sigma))).astype(BF16)
            bias = bias + low.astype(F32)
            k_.pg[p] = low
            lows.append(low)
            k_.ug[d, 3 + j] = both[0:ups]
            for i in range(nc):
                k_.gv[i] = v[i * dm.cs : (i + 1) * dm.cs]
            for i in range(nx):
                k_.sgp[i, p] = alpha * k_.gv[2 * i + core]
        back = dot(k_.gate_own[...].astype(BF16), jnp.concatenate(lows, 1))
        for j in range(len(results)):
            p = d * RB + j
            lanes = slice(j * LANES, (j + 1) * LANES)
            k_.ug[d, 3 + j] += back[0:ups, lanes]
            for i in range(nx):
                v = k_.sgp[i, p] + back[ups + i * dm.cs : ups + (i + 1) * dm.cs, lanes]
                k_.sgp[i, p] = v
                k_.sgb[i, p] = v.astype(BF16).astype(k_.sgb.dtype)
        return bias, psi

    blank = jnp.zeros((dm.g, LANES), F32)
    bias, psi = conv(blocks_of(xz3), wb[2][...], ups + dm.skip_all, 1, gate_back, (blank, blank))

    ug, cb, cg = k_.ug, k_.cb, k_.cg
    for q in range(RB // 2 + 2):
        terms = []
        for d in range(S):
            v = 0.75 * (ug[d, 2 * q + 1] + ug[d, 2 * q + 2]) + 0.25 * (ug[d, 2 * q + 3] + ug[d, 2 * q])
            if q == 1:
                v += jnp.where(top, 0.25 * ug[d, 3], 0.0)
            if q == RB // 2:
                v += jnp.where(bottom, 0.25 * ug[d, RB + 2], 0.0)
            terms.append(split(v))
        v = dot(jnp.concatenate(terms, 0), down)
        for d in range(S):
            cb[d, h0 + q] = v[d * ups : (d + 1) * ups]

    def to_slabs(i, carry):
        even, odd = (cb[d, 2 * i + 1] + pltpu.roll(cb[d, 2 * i + 2], half, 1) for d in range(S))
        middle = 0.75 * (even + odd) + jnp.where(first, 0.25 * even, 0.0) + jnp.where(last, 0.25 * odd, 0.0)
        for part, v in enumerate((0.25 * even, middle, 0.25 * odd)):
            for j in range(nx):
                block = v[j * dm.ce : (j + 1) * dm.ce]
                k_.fs[part, j, i] = block.astype(BF16).astype(k_.fs.dtype)
                if part == 1:
                    k_.fm[j, i] = block
        return carry

    lax.fori_loop(0, Q, to_slabs, 0)

    def fold_parts():
        for step in (-1, 1, 0):
            sends = (no(first), None, no(last))[step + 1]
            gets = (no(last), None, no(first))[step + 1]
            for t in range(nx):
                if (step, t) != (0, 0):
                    tox, fromx = lax.rem(x + t, nx), lax.rem(x + nx - t, nx)
                    sems = (k_.f_send.at[step + 1, t], k_.f_recv.at[step + 1, t])
                    theirs = k_.fr.at[step + 1, fromx]
                    yield (
                        sends, gets, fromx, step + 1,
                        functools.partial(
                            peer_copy, k_.fs.at[step + 1, tox], k_.fr.at[step + 1, x], *sems, place + step, 2 * tox + core
                        ),
                        functools.partial(peer_copy, theirs, theirs, *sems, place, 2 * fromx + core),
                    )

    for sends, _, _, _, out, _ in fold_parts():
        launch(sends, out)
    for t in range(1, nx):
        tox = lax.rem(x + t, nx)

        def send_skip(t=t, tox=tox):
            return peer_copy(
                k_.sgb.at[tox], k_.sgi.at[x], k_.o_send.at[2, t], k_.o_recv.at[2, t], place, 2 * tox + core
            )

        launch(None, send_skip)

    reduce_finish(3)
    cross_finish(2)

    k_.gw[...] = jnp.zeros(k_.gw.shape, F32)

    def gate_weight(d, carry):
        v = jnp.concatenate(
            [
                jnp.concatenate([d1[1 + d, 1 + j, 0 : dm.enc_all] for j in range(RB)], 1),
                jnp.concatenate([flat(xs, 1 + d, 1 + j) for j in range(RB)], 1),
            ],
            0,
        )
        y = jnp.concatenate([k_.pg[d * RB + j] for j in range(RB)], 1)
        k_.gw[0:columns, 0 : dm.g] += dot_nt(v, y)
        return carry

    lax.fori_loop(0, S, gate_weight, 0)
    gate_grad = jnp.transpose(k_.gw[...])
    lane = iota((dm.g, LANES), 1)
    vectors = jnp.where(
        lane == 0,
        jnp.sum(bias, axis=1, keepdims=True),
        jnp.where(lane == 1, jnp.sum(psi, axis=1, keepdims=True), 0.0),
    )
    gate_block = k_.gate_block
    for j in range(nc):
        mine = slice(j * gq, (j + 1) * gq)
        gate_block[j, :, 0 : 2 * LANES] = gate_grad[mine]
        gate_block[j, :, 2 * LANES :] = vectors[mine]
    sum_start(everyone, k_.sv, 4, 0, gate_block[me], lambda chan: gate_block.at[chan])
    cg[...] = k_.fm[x]
    for _, gets, fromx, part, _, back in fold_parts():

        def fold_in(back=back, part=part, fromx=fromx):
            back().wait_recv()
            cg[...] += k_.fr[part, fromx].astype(F32)

        guarded(gets, fold_in)

    coarse_sums(2, norm_back_sums(k_.z2, keep_du(k_.du_c), stats_e2, norm_e2, lambda p: cg[p], Q))
    pair_finish(2)
    share_pass(3)
    weights_finish(1)
    total_e2 = coarse_totals(2)
    norm_back_coarse(k_.z2, back_factors(stats_e2, norm_e2, total_e2, dm.coarse_total), k_.xz2)
    gather_start(k_.xz2, "dz2")
    turn_coarse(k_.xz2)
    weight_grad_coarse(k_.xh, 1)
    gather_pass(k_.xz2, "dz2")
    reduce_start(1)
    weights_finish(0)
    reduce_finish(2)
    drain()
    gather_wait(k_.xz2, "dz2")
    for i, v in enumerate(conv_coarse(k_.xz2, wb[1], dm.ce)):
        cg[i] = v
    coarse_sums(3, norm_back_sums(k_.z1, keep_du(k_.du_c), stats_e1, norm_e1, lambda p: cg[p], Q))
    pair_finish(1)
    share_pass(2)
    gradient_out(3)
    total_e1 = coarse_totals(3)
    norm_back_coarse(k_.z1, back_factors(stats_e1, norm_e1, total_e1, dm.coarse_total), k_.xz1)
    gather_start(k_.xz1, "dz1")
    turn_coarse(k_.xz1)
    weight_grad_coarse(xp, 0)
    reduce_start(0)
    reduce_finish(1)
    gather_pass(k_.xz1, "dz1")
    gradient_out(2)

    def rows_out(ref, own, theirs, kind, size):
        def copy_rows(read, at):
            def body(d, carry):
                for r in range(RB):
                    p = (d * R + at * RB + r) * size
                    ref[pl.ds(pl.multiple_of(p, size), size)] = read(d * RB + r).astype(F32)
                return carry

            lax.fori_loop(0, S, body, 0)

        copy_rows(lambda p: own[x, p], x)
        for t in range(1, nx):
            fromx = lax.rem(x + nx - t, nx)
            block = theirs.at[fromx]
            peer_copy(block, block, k_.o_send.at[kind, t], k_.o_recv.at[kind, t], place, 2 * fromx + core).wait_recv()
            copy_rows(lambda p, fromx=fromx: theirs[fromx, p], fromx)

    share_pass(1)
    rows_out(k_.out, k_.ob, k_.oi, 1, dm.cd)
    rows_out(k_.sg, k_.sgp, k_.sgi, 2, dm.cs)
    reduce_finish(0)
    gather_wait(k_.xz1, "dz1")
    for i, v in enumerate(conv_coarse(k_.xz1, wb[0], dm.cs)):
        v = dot(split(v), spread2) * 0.125
        for j in range(4):
            part = v[:, (j // 2) * LANES : (j // 2 + 1) * LANES]
            for d in range(S):
                at = (d * R + 4 * i + j) * dm.cs
                k_.sg[at : at + dm.cs] += part
    gradient_out(1)
    gate_total = sum_finish(everyone, k_.sv, 4, 0)
    k_.ggate[...] = gate_total[:, 0:columns]
    k_.gvector[0:1] = row_of(gate_total[:, 2 * LANES : 2 * LANES + 1])
    k_.gvector[1:2] = row_of(gate_total[:, 2 * LANES + 1 : 2 * LANES + 2])

    def own_part(col):
        parts = [jnp.where(x == i, col[i * dm.cd : (i + 1) * dm.cd], 0.0) for i in range(nx)]
        return functools.reduce(jnp.add, parts)

    for ref, pair, pick in ((k_.gen, (total_e1, total_e2), lambda v: v), (k_.gdn, (total_d1, total_d2), own_part)):
        for layer, total in enumerate(pair):
            ref[0, layer : layer + 1] = row_of(pick(total[1]))
            ref[1, layer : layer + 1] = row_of(pick(total[0]))
    gradient_out(0)
    drain()


def adamw(weight, grad, moment, square, rate):
    new_moment = 0.9 * moment + 0.1 * grad
    new_square = 0.999 * square + 0.001 * grad * grad
    moment_hat = new_moment / (1.0 - 0.9**STEP)
    square_hat = new_square / (1.0 - 0.999**STEP)
    new_weight = weight - rate * (moment_hat / (jnp.sqrt(square_hat) + 1e-08) + 0.01 * weight)
    return (new_weight, new_moment, new_square)


RATES = (CONV_RATE, CONV_RATE, GATE_RATE, VECTOR_RATE, CONV_RATE, CONV_RATE, VECTOR_RATE, VECTOR_RATE)


def update_kernel(*refs):
    n = len(RATES)
    sources, targets = refs[: 2 + 4 * n], refs[2 + 4 * n : 4 + 7 * n]
    inside, outside = refs[4 + 7 * n : 6 + 11 * n], refs[6 + 11 * n : 8 + 14 * n]
    in_sem, out_sem = refs[8 + 14 * n :]
    order = (4, 1, 0, 5, 2, 3, 6, 7)

    def load(i):
        return pltpu.make_async_copy(sources[i], inside[i], in_sem.at[i])

    def store(i):
        return pltpu.make_async_copy(outside[i], targets[i], out_sem.at[i])

    for i in (1, 0):
        load(i).start()
    for k in order:
        for part in range(4):
            load(2 + part * n + k).start()
    for i in (1, 0):
        load(i).wait()
        chans, (slabs, rows) = outside[i].shape[0], outside[i].shape[1:3]
        for c in range(chans):
            v = inside[i][pl.ds(c, slabs * rows, stride=chans)]
            outside[i][c] = v.reshape(slabs, rows, LANES).astype(outside[i].dtype)
        store(i).start()
    for k in order:
        own = [2 + part * n + k for part in range(4)]
        for i in own:
            load(i).wait()
        rows = inside[own[0]].shape[0]
        step = 8 if rows % 8 == 0 and rows > 8 else rows
        for r in range(0, rows, step):
            at = slice(r, r + step)
            new = adamw(*(inside[i][at] for i in own), RATES[k])
            for part, value in enumerate(new):
                outside[2 + 3 * k + part][at] = value
        for part in range(3):
            store(2 + 3 * k + part).start()
    for i in range(len(targets)):
        store(i).wait()


def per_device(
    skip, cotangent, enc_conv1, enc_conv2, gate_proj, gate_vector, dec_conv1, dec_conv2, enc_norms, dec_norms, *states
):
    nd, nc = lax.axis_size("depth"), lax.axis_size("chan")
    dm = Dims(nd, nc, skip.shape, enc_conv1.shape[0], dec_conv1.shape[0], gate_proj.shape[0] * nc)
    S, R, H, nx, RB, E = dm.s, dm.rows, dm.half, dm.nx, dm.rb, dm.ext
    Q = H // 2
    cin3 = dm.enc_all + dm.skip_all

    def own_block(size):
        return (size, lambda j: pl.multiple_of(j * size, size), 0)

    def core_blocks(size):
        return tuple(
            (size, lambda j, i=i: pl.multiple_of((2 * i + lax.rem(j, 2)) * size, size), i * size) for i in range(nx)
        )

    dm.convs = convs = (
        Conv(dm, dm.ce, dm.skip_all, (own_block(dm.cs),)),
        Conv(dm, dm.ce, dm.enc_all, (own_block(dm.ce),)),
        Conv(dm, dm.cd, cin3, core_blocks(dm.ce) + ((dm.skip_all, lambda j: dm.enc_all, nx * dm.ce),)),
        Conv(dm, dm.cd, dm.dec_all, core_blocks(dm.cd)),
    )
    params = (enc_conv1, enc_conv2, gate_proj, gate_vector, dec_conv1, dec_conv2, enc_norms, dec_norms)
    inputs = dict(
        skip=skip, cot=cotangent, w0=enc_conv1, w1=enc_conv2, w2=dec_conv1, w3=dec_conv2,
        gate=gate_proj, vector=gate_vector, en=enc_norms, dn=dec_norms,
    )
    shape = jax.ShapeDtypeStruct
    outs = dict(
        out=shape((S * R * dm.cd, LANES), F32),
        sg=shape((S * R * dm.cs, LANES), F32),
        **{f"g{i}": shape(a.shape, F32) for i, a in enumerate((enc_conv1, enc_conv2, dec_conv1, dec_conv2))},
        **{
            name: shape(a.shape, F32)
            for name, a in (("ggate", gate_proj), ("gvector", gate_vector), ("gen", enc_norms), ("gdn", dec_norms))
        },
    )
    gq = dm.g // nc

    def coarse(block):
        return pltpu.VMEM((2, nx, 3, Q, block, LANES), storage(block))

    def fine():
        return pltpu.VMEM((2, S + 2, E, dm.cf, LANES), storage(dm.cd))

    def f32(*dims):
        return pltpu.VMEM((*dims, LANES), F32)

    def tiles(*dims):
        return pltpu.VMEM((*dims, 16, LANES), BF16)

    def blocks(block, *dims):
        return pltpu.VMEM((*dims, block, LANES), storage(block))

    def sems(*dims):
        return pltpu.SemaphoreType.DMA(dims)

    scratch = dict(
        xp=coarse(dm.cs), xh=coarse(dm.ce), xc=coarse(dm.ce), xz2=coarse(dm.ce), xz1=coarse(dm.ce),
        own_skip=blocks(dm.cs, S, R + 2), xs=blocks(dm.cs, 2, nx, S + 2, E),
        own_cot=blocks(dm.cd, S, R), cots=blocks(dm.cd, nx, S, RB),
        d1=pltpu.VMEM((S + 2, E, cin3, LANES), BF16), xd=fine(), xz4=fine(), xz3=fine(),
        z1=f32(Q, dm.ce), z2=f32(Q, dm.ce), z3=f32(S * RB, dm.cf), z4=f32(S * RB, dm.cf),
        du_c=f32(Q, dm.ce), du_f=f32(S * RB, dm.cf), gg=f32(S * RB, dm.cf), cg=f32(Q, dm.ce),
        pre=f32(S + 2, E, dm.g), alpha=f32(S + 2, E, 1), pg=pltpu.VMEM((S * RB, dm.g, LANES), BF16),
        ug=f32(S, RB + 6, nx * dm.ce), cb=f32(S, H + 2, nx * dm.ce), dt=f32(S + 2, H, dm.enc_all),
        gv=f32(nc, dm.cs), sgp=f32(nx, S * RB, dm.cs), sgb=blocks(dm.cs, nx, S * RB), sgi=blocks(dm.cs, nx, S * RB),
        ob=blocks(dm.cd, nx, S * RB), oi=blocks(dm.cd, nx, S * RB),
        dzt=pltpu.VMEM((S, (RB + 4) * LANES, LANES), BF16), dzct=pltpu.VMEM((Q * LANES + 2 * dm.hcols, LANES), BF16),
        gw=f32(2 * LANES), dense=pltpu.VMEM((max(3 * cv.c for cv in convs), 3 * LANES), F32),
        fs=blocks(dm.ce, 3, nx, Q), fr=blocks(dm.ce, 3, nx, Q), fm=f32(nx, Q, dm.ce),
        st=f32(4, nd, 1), su=f32(4, nd * nx, 1), sv=pltpu.VMEM((1, nd * nx, gq, 3 * LANES), F32),
        norm_all=f32(nc, 8), rows=f32(max(dm.cs, dm.cd) * S * R),
        turned=f32(max(cv.chunks for cv in convs) * LANES),
        acc=pltpu.VMEM((max(3 * cv.c for cv in convs), 3 * LANES), F32),
        gate_all=pltpu.VMEM((nc, gq, 3 * LANES), F32), gate_t=pltpu.VMEM((2 * LANES, dm.g), F32),
        gate_own=pltpu.VMEM((nx * (dm.ce + dm.cs), dm.g), F32), gate_block=pltpu.VMEM((nc, gq, 3 * LANES), F32),
        **{f"wt{i}": pltpu.VMEM((3, cv.c, cv.wide), cv.kind) for i, cv in enumerate(convs)},
        **{
            f"wf{i}": pltpu.VMEM((cv.taps, 3 * cv.c) if i < 2 else (nx, cv.stored, 9 * cv.c), BF16)
            for i, cv in enumerate(convs)
        },
        **{f"wx{i}": pltpu.VMEM((nc, 3, cv.needed, cv.wide), cv.kind) for i, cv in enumerate(convs)},
        **{
            f"wb{i}": pltpu.VMEM((9 * cv.needed, 3 * nc * cv.o) if i < 2 else (3 * cv.needed, 9 * nc * cv.o), BF16)
            for i, cv in enumerate(convs)
        },
        flip=pltpu.VMEM((max(cv.tiles for cv in convs[2:]) * LANES, max(3 * cv.c for cv in convs[2:])), F32),
        **{f"gt{i}": tiles(cv.share * nd) for i, cv in enumerate(convs)},
        **{f"gr{i}": tiles(nd if i == 0 else nd // 2, cv.share) for i, cv in enumerate(convs)},
        **{f"gp{i}": tiles(nd // 2 * cv.share) for i, cv in enumerate(convs) if i > 0},
        **{f"ga{i}": tiles(cv.share * nd) for i, cv in enumerate(convs)},
        **{f"gs{i}": tiles(nx, convs[i].count) for i in (2, 3)},
        **{f"gx{i}": tiles(nx, convs[i].count) for i in (2, 3)},
        g_send=sems(len(GATHERS), 3, nx), g_recv=sems(len(GATHERS), 3),
        h_send=sems(len(GATHERS), 2 + nx), h_recv=sems(len(GATHERS)),
        x_send=sems(len(FINE), 3, 5), x_recv=sems(len(FINE), 3, 5),
        y_send=sems(len(FINE), 3), y_recv=sems(len(FINE), 3),
        t_send=sems(4), t_recv=sems(4), u_send=sems(5), u_recv=sems(5),
        f_send=sems(3, nx), f_recv=sems(3, nx), w_send=sems(4, nx + 1, nc), w_recv=sems(4, nx + 1, nc),
        p_send=sems(2, nx), p_recv=sems(2, nx), c_send=sems(2, nx), c_recv=sems(2, nx),
        o_send=sems(3, nx), o_recv=sems(3, nx), v_send=sems(2, nc), v_recv=sems(2, nc),
        r_send=sems(4), r_recv=sems(4), a_send=sems(4), a_recv=sems(4), q_send=sems(4, 2), q_recv=sems(4, 2),
    )
    vmem = pl.BlockSpec(memory_space=pltpu.VMEM)
    out, sg, grad1, grad2, grad3, grad4, ggate, gvector, gen, gdn = pl.pallas_call(
        functools.partial(kernel, dm, (*inputs, *outs, *scratch)),
        out_shape=tuple(outs.values()),
        in_specs=[vmem] * len(inputs),
        out_specs=[vmem] * len(outs),
        scratch_shapes=list(scratch.values()),
        compiler_params=pltpu.CompilerParams(
            has_side_effects=True, collective_id=0, vmem_limit_bytes=60 * 1024 * 1024
        ),
        name="step",
    )(*inputs.values())
    grads = (grad1, grad2, ggate, gvector, grad3, grad4, gen, gdn)
    operands = (out, sg, *params, *grads, *states)
    updated = (
        shape(cotangent.shape, BF16),
        shape(skip.shape, F32),
        *(shape(p.shape, F32) for p in params for _ in range(3)),
    )
    anywhere = pl.BlockSpec(memory_space=pl.ANY)
    return pl.pallas_call(
        update_kernel,
        out_shape=updated,
        in_specs=[anywhere] * len(operands),
        out_specs=[anywhere] * len(updated),
        scratch_shapes=[
            *(pltpu.VMEM(a.shape, a.dtype) for a in operands),
            *(pltpu.VMEM(a.shape, a.dtype) for a in updated),
            pltpu.SemaphoreType.DMA((len(operands),)),
            pltpu.SemaphoreType.DMA((len(updated),)),
        ],
        compiler_params=pltpu.CompilerParams(vmem_limit_bytes=60 * 1024 * 1024),
        name="update",
    )(*operands)


def solution(mesh):
    volume = P("chan", "depth", None, None)
    row, column, norms = P("chan", None), P(None, "chan"), P(None, None, "chan")
    params = (row, row, row, column, row, row, norms, norms)
    return jax.shard_map(
        per_device,
        mesh=mesh,
        in_specs=(volume, volume) + params * 3,
        out_specs=(volume, volume) + tuple(spec for spec in params for _ in range(3)),
        check_vma=False,
    )
```

```python
import functools
import types

import jax
import jax.numpy as jnp
from jax import lax
from jax.experimental import pallas as pl
from jax.experimental.pallas import tpu as pltpu
from jax.sharding import PartitionSpec as P

STEP = 5
EPS = 1e-05
CONV_RATE = 0.03
GATE_RATE = 0.1
VECTOR_RATE = 0.5
LANES = 128
MESH = pl.DeviceIdType.MESH
F32 = jnp.float32
BF16 = jnp.bfloat16


def iota(shape, dim):
    return lax.broadcasted_iota(jnp.int32, shape, dim)


def dot(a, b):
    return jnp.dot(a, b, preferred_element_type=F32)


def dot_nt(a, b):
    return lax.dot_general(a, b, (((1,), (1,)), ((), ())), preferred_element_type=F32)


def dot_tn(a, b):
    return lax.dot_general(a, b, (((0,), (0,)), ((), ())), preferred_element_type=F32)


def from_left(v, width):
    return jnp.where(iota(v.shape, 1) % width == 0, 0.0, pltpu.roll(v, 1, 1))


def from_right(v, width):
    return jnp.where(iota(v.shape, 1) % width == width - 1, 0.0, pltpu.roll(v, LANES - 1, 1))


def halves(low, high):
    return pltpu.roll(jnp.where(iota(low.shape, 1) < LANES // 2, low, high), LANES // 2, 1)


def split(v):
    high = v.astype(BF16)
    return jnp.concatenate([high, (v - high.astype(F32)).astype(BF16)], 1)


def storage(block):
    return BF16 if block % 16 == 0 else F32


def flat(ref, s, r):
    if len(ref.shape) == 4:
        return ref[s, r]
    v = ref[:, :, s, r]
    return jnp.concatenate([v[c, i] for i in range(v.shape[1]) for c in range(2)], 0).astype(BF16)


class Dims:
    def __init__(self, nd, nc, skip, enc, dec, gate):
        self.nd, self.nc, self.nx = nd, nc, nc // 2
        self.s, self.rows, self.cols = skip[1:]
        self.cs, self.ce, self.cd, self.g = skip[0], enc, dec, gate
        self.half, self.hcols = self.rows // 2, self.cols // 2
        self.fine_total = nd * self.s * self.rows * self.cols
        self.coarse_total = self.fine_total // 8
        self.enc_all = nc * enc
        self.skip_all = nc * skip[0]
        self.dec_all = nc * dec
        self.rb = self.rows // self.nx
        self.ext = self.rb + 2
        self.cf = self.nx * dec


GATHERS = ("pooled", "skip", "hidden", "coarse", "dz2", "dz1")
FINE = ("hidden", "dz4", "dz3")


class Conv:
    def __init__(self, dm, o, c, blocks):
        self.o, self.c, self.blocks = o, c, blocks
        self.length = 27 * c
        self.chunks = -(-self.length // LANES)
        self.per = LANES // o
        self.tiles = -(-9 // self.per)
        self.wide = self.tiles * LANES
        self.kind = storage(min(size for size, _, _ in blocks))
        self.needed = sum(size for size, _, _ in blocks)
        self.full = max(1, 9 // self.per)
        self.left = max(0, 9 - self.full * self.per)
        self.group = 3 * self.full + (self.left > 0)
        self.count = c // 16 * self.group
        self.share = -(-self.count // dm.nd)
        self.taps = 9 * o
        self.stored = -(-3 * o // 16) * 16


def kernel(dm, names, *refs):
    k_ = types.SimpleNamespace(**dict(zip(names, refs)))
    nd, nc, nx, S, R, H = dm.nd, dm.nc, dm.nx, dm.s, dm.rows, dm.half
    W, V = dm.cols, dm.hcols
    Q, RB, E = H // 2, dm.rb, dm.ext
    place = lax.axis_index("depth")
    me = lax.axis_index("chan")
    x, core = lax.div(me, 2), lax.rem(me, 2)
    other = 1 - core
    mate = 2 * x + other
    row0, h0 = x * RB, x * (RB // 2)
    first, last = place == 0, place == nd - 1
    top, bottom = x == 0, x == nx - 1
    convs = dm.convs
    pending = []
    wt, wf, wx, wb = ([getattr(k_, f"{kind}{i}") for i in range(4)] for kind in ("wt", "wf", "wx", "wb"))
    gp = (k_.gp1, k_.gp2, k_.gp3)
    gt, gr, ga = ([getattr(k_, f"{kind}{i}") for i in range(4)] for kind in ("gt", "gr", "ga"))
    weights = (k_.w0, k_.w1, k_.w2, k_.w3)
    grads = (k_.g0, k_.g1, k_.g2, k_.g3)
    turned, acc = k_.turned, k_.acc

    def no(cond):
        return jnp.logical_not(cond)

    def peer_copy(src, dst, send, recv, depth, chan):
        return pltpu.make_async_remote_copy(
            src_ref=src, dst_ref=dst, send_sem=send, recv_sem=recv,
            device_id={"depth": depth, "chan": chan}, device_id_type=MESH,
        )

    def guarded(cond, fn):
        if cond is None:
            fn()
        else:
            pl.when(cond)(fn)

    def drain():
        for cond, fn in pending:
            guarded(cond, fn)
        pending.clear()

    def launch(cond, copy):
        guarded(cond, lambda: copy().start())
        pending.append((cond, lambda: copy().wait_send()))

    def arrive(cond, copy):
        guarded(cond, lambda: copy().wait_recv())

    def both(a, b):
        return b if a is None else a if b is None else jnp.logical_and(a, b)

    can_send = (no(last), None, no(first))
    can_recv = (no(first), None, no(last))

    def slices(side, n):
        return (pl.ds(n, 1), pl.ds(1, n), pl.ds(1, 1))[side], (pl.ds(0, 1), pl.ds(1, n), pl.ds(n + 1, 1))[side]

    def at_x(t):
        up, down = x + t, x - t
        return jnp.where(up >= nx, up - nx, up), jnp.where(down < 0, down + nx, down)


    def gather_start(ref, which, source_at=None):
        n = ref.shape[2] - 2
        k = GATHERS.index(which)
        for side in (0, 2, 1):
            own, theirs = slices(side, n)
            for t in range(nx):
                if side == 1 and t == 0:
                    continue
                tox = at_x(t)[0]

                def copy(side=side, t=t, own=own, theirs=theirs, tox=tox):
                    start = (n, 1, 1)[side] - 1
                    size = (1, n, 1)[side]
                    src = ref.at[core, x, own] if source_at is None else source_at(pl.ds(start, size), tox)
                    return peer_copy(
                        src, ref.at[core, x, theirs], k_.g_send.at[k, side, t], k_.g_recv.at[k, side],
                        place + 1 - side, 2 * tox + core,
                    )

                launch(can_send[side], copy)
        gather_own(ref, which)

    def handed(ref, k, piece, i):
        return peer_copy(piece, piece, k_.h_send.at[k, i], k_.h_recv.at[k], place, mate)

    def gather_own(ref, which):
        k = GATHERS.index(which)
        launch(None, lambda: handed(ref, k, ref.at[core, x, pl.ds(1, ref.shape[2] - 2)], 0))

    def gather_pass(ref, which):
        n = ref.shape[2] - 2
        k = GATHERS.index(which)
        for side in (1, 0, 2):
            theirs = slices(side, n)[1]
            if side != 1:
                pieces = [ref.at[core, :, theirs]]
            else:
                pieces = [ref.at[core, at_x(t)[1], theirs] for t in range(1, nx)]
            for i, got in enumerate(pieces):
                arrive(
                    can_recv[side],
                    lambda got=got, side=side: peer_copy(
                        got, got, k_.g_send.at[k, side, 0], k_.g_recv.at[k, side], place, mate
                    ),
                )
                launch(None, lambda got=got, i=i, side=side: handed(ref, k, got, 1 + (side // 2 if side != 1 else 2 + i)))

    def gather_wait(ref, which):
        handed(ref, GATHERS.index(which), ref.at[other], 0).wait_recv()

    def fine_parts(ref, which, side):
        k = FINE.index(which)
        own, theirs = slices(side, S)
        inner = pl.ds(1, RB)
        rows = [(None, None, inner, inner, x, core, core)] if side != 1 else [(None, None, inner, inner, x, other, other)]
        if nx > 1:
            for c in range(2):
                rows.append((no(top), no(bottom), pl.ds(1, 1), pl.ds(E - 1, 1), x - 1, c, c))
                rows.append((no(bottom), no(top), pl.ds(RB, 1), pl.ds(0, 1), x + 1, c, c))
        parts = []
        for i, (sends, gets, row, at, tox, to, source) in enumerate(rows):
            target = ref.at[core, theirs, at]
            theirs_ = ref.at[source, theirs, at]
            up = (i - 1) % 2
            arrived = 0 if i == 0 else 1 + up * 2 + core
            expected = 0 if i == 0 else 1 + up * 2 + source
            send = k_.x_send.at[k, side, i]
            parts.append((
                both(can_send[side], sends), both(can_recv[side], gets),
                functools.partial(
                    peer_copy, ref.at[core, own, row], target, send, k_.x_recv.at[k, side, arrived],
                    place + 1 - side, 2 * tox + to,
                ),
                functools.partial(peer_copy, theirs_, theirs_, send, k_.x_recv.at[k, side, expected], place, mate),
            ))
        return parts

    def fine_start(ref, which):
        for side in (0, 2, 1):
            for sends, _, out, _ in fine_parts(ref, which, side):
                launch(sends, out)

    def fine_halo(ref, which, side, c):
        k = FINE.index(which)
        block = ref.at[c, slices(side, S)[1], pl.ds(1, RB)]
        return peer_copy(block, block, k_.y_send.at[k, side], k_.y_recv.at[k, side], place, mate)

    def fine_pass(ref, which):
        for side in (0, 2):
            _, gets, _, back = fine_parts(ref, which, side)[0]
            arrive(gets, back)
            launch(gets, functools.partial(fine_halo, ref, which, side, core))

    def fine_wait(ref, which):
        for side in (1, 0, 2):
            for _, gets, _, back in fine_parts(ref, which, side)[side != 1 :]:
                arrive(gets, back)
            if side != 1:
                arrive(can_recv[side], functools.partial(fine_halo, ref, which, side, other))

    def natural(ref, s, r):
        v = ref[:, s, r]
        size = dm.cd
        return jnp.concatenate(
            [v[c, i * size : (i + 1) * size] for i in range(nx) for c in range(2)], 0
        ).astype(BF16)

    def in_turn(count, fn):
        if count <= 16:
            for i in range(count):
                fn(i)
        else:

            def body(i, carry):
                fn(i)
                return carry

            lax.fori_loop(0, count, body, 0)

    def slab_peers(i):
        to = place + 1 + i
        return jnp.where(to >= nd, to - nd, to), me

    def wide_peers(i):
        i = i + 1
        dt, xt = (i // nx, i % nx) if isinstance(i, int) else (lax.div(i, nx), lax.rem(i, nx))
        to, tox = place + dt, x + xt
        return jnp.where(to >= nd, to - nd, to), 2 * jnp.where(tox >= nx, tox - nx, tox) + core

    def exchange(n, peers, copy):
        in_turn(n - 1, lambda i: copy(*peers(i)).start())

    def sum_start(group, ref, k, slot, tile, source=None):
        n, own, peers, send, recv = group
        ref[slot, own] = tile

        def copy(depth, chan):
            src = ref.at[slot, own] if source is None else source(chan)
            return peer_copy(src, ref.at[slot, own], send.at[k], recv.at[k], depth, chan)

        exchange(n, peers, copy)
        pending.append((None, lambda: all_of(group, ref, k, slot).wait_send()))

    def all_of(group, ref, k, slot):
        n, _, _, send, recv = group
        every = ref.at[slot, pl.ds(0, n - 1)]
        return peer_copy(every, every, send.at[k], recv.at[k], place, mate)

    def sum_finish(group, ref, k, slot):
        all_of(group, ref, k, slot).wait_recv()
        return jnp.sum(ref[slot], axis=0)

    slabs = (nd, place, slab_peers, k_.t_send, k_.t_recv)
    everyone = (nd * nx, place * nx + x, wide_peers, k_.u_send, k_.u_recv)

    def columns_of(row, m):
        lane, channel = iota((m, LANES), 1), iota((m, LANES), 0)
        return tuple(
            jnp.sum(jnp.where(lane == channel + i * m, row, 0.0), axis=1, keepdims=True) for i in range(2)
        )

    def coarse_sums(slot, sums):
        sum_start(slabs, k_.st, slot, slot, pack(*sums))

    def coarse_totals(slot):
        return columns_of(sum_finish(slabs, k_.st, slot, slot), dm.ce)

    def fine_sums(slot, sums):
        sum_start(everyone, k_.su, slot, slot, pack(*sums))

    def fine_totals(slot):
        return columns_of(sum_finish(everyone, k_.su, slot, slot), dm.cf)

    def prepare(k):
        cv, w, own = convs[k], weights[k], wt[k]
        out = wf[k] if k < 2 else wf[k].at[x]
        eye = (iota((LANES, LANES), 0) == iota((LANES, LANES), 1)).astype(BF16)

        def chunk(a):
            return dot_nt(eye, jnp.concatenate([a] * cv.per, 0).astype(BF16))

        full = cv.length // LANES

        def body(i, carry):
            at = pl.multiple_of(i * LANES, LANES)
            turned[pl.ds(at, LANES)] = chunk(w[:, pl.ds(at, LANES)])
            return carry

        lax.fori_loop(0, full, body, 0, unroll=4)
        if full < cv.chunks:
            a = w[:, full * LANES :]
            a = jnp.concatenate([a, jnp.zeros((cv.o, LANES - a.shape[1]), F32)], 1)
            turned[full * LANES : (full + 1) * LANES] = chunk(a)
        group = iota((cv.c, LANES), 1) // cv.o
        for kz in range(3):
            for j in range(cv.tiles):
                tile = None
                for g in range(cv.per):
                    u = j * cv.per + g
                    if u < 9:
                        kx, ky = u // 3, u % 3
                        v = turned[pl.ds(9 * kz + 3 * ky + kx, cv.c, stride=27)]
                        tile = v if tile is None else jnp.where(group == g, v, tile)
                own[kz, :, j * LANES : (j + 1) * LANES] = tile.astype(BF16).astype(own.dtype)
        for j in range(cv.tiles):
            v = jnp.concatenate([own[kz, :, j * LANES : (j + 1) * LANES] for kz in range(3)], 0)
            size = min(LANES, cv.taps - j * LANES)
            v = dot_nt(eye, v.astype(BF16))[0:size]
            if k < 2:
                out[j * LANES : j * LANES + size] = v.astype(BF16)
            else:
                k_.flip[j * LANES : j * LANES + size, 0 : 3 * cv.c] = v
        if k >= 2:
            out[0 : 3 * cv.o] = jnp.concatenate(
                [
                    jnp.concatenate(
                        [
                            k_.flip[(3 * kx + ky) * cv.o : (3 * kx + ky + 1) * cv.o, kz * cv.c : (kz + 1) * cv.c]
                            for kx in range(3)
                        ],
                        0,
                    )
                    for kz in range(3)
                    for ky in range(3)
                ],
                1,
            ).astype(BF16)

    def forward_copy(k, t):
        block = wf[k].at[x]
        return peer_copy(
            block, block, k_.p_send.at[k - 2, t], k_.p_recv.at[k - 2, t], place, 2 * lax.rem(x + t, nx) + core
        )

    def forward_start(k):
        for t in range(1, nx):
            launch(None, functools.partial(forward_copy, k, t))

    def forward_wait(k):
        for t in range(1, nx):
            fromx = lax.rem(x + nx - t, nx)
            block = wf[k].at[fromx]
            peer_copy(
                block, block, k_.p_send.at[k - 2, t], k_.p_recv.at[k - 2, t], place, 2 * fromx + core
            ).wait_recv()

    def forward_weight(k):
        return jnp.concatenate([wf[k][i, 0 : 3 * convs[k].o] for i in range(nx)], 0)

    def weights_start(k):
        cv = convs[k]
        for b, (size, start, at) in enumerate(cv.blocks):
            wx[k][me, :, at : at + size] = wt[k][:, pl.ds(start(me), size)]
            for t in range(1, nc):
                to = lax.rem(me + t, nc)

                def copy(to=to, t=t, b=b, size=size, start=start, at=at):
                    return peer_copy(
                        wt[k].at[:, pl.ds(start(to), size)], wx[k].at[me, :, pl.ds(at, size)],
                        k_.w_send.at[k, b, t], k_.w_recv.at[k, b, t], place, to,
                    )

                launch(None, copy)

    def weights_finish(k):
        cv = convs[k]
        for b, (size, _, at) in enumerate(cv.blocks):
            for t in range(1, nc):
                source = lax.rem(me + nc - t, nc)
                theirs = wx[k].at[source, :, pl.ds(at, size)]
                peer_copy(theirs, theirs, k_.w_send.at[k, b, t], k_.w_recv.at[k, b, t], place, source).wait_recv()

        parts = 9 if k < 2 else 3
        lanes = cv.taps // parts
        for i in range(parts):
            at = (parts - 1 - i) * lanes
            found = [wx[k][j, 2 - kz, :, at : at + lanes].astype(F32) for kz in range(3) for j in range(nc)]
            wb[k][i * cv.needed : (i + 1) * cv.needed] = jnp.concatenate(found, 1).astype(BF16)

    def tiles_of(k, part, put):
        cv, dense = convs[k], k_.dense
        rows, size = 3 * cv.c, 3 * cv.o
        for ky in range(3):
            at = ky * LANES + part * size
            dense[0:rows, ky * size : (ky + 1) * size] = acc[0:rows, at : at + size]

        def tile(i, carry):
            left = []
            for kz in range(3):
                at = pl.ds(pl.multiple_of(kz * cv.c + i * 16, 16), 16)
                for j in range(cv.full):
                    put(i * cv.group + kz * cv.full + j, dense[at, j * LANES : (j + 1) * LANES].astype(BF16))
                left.append(dense[at, cv.full * LANES : cv.full * LANES + cv.left * cv.o])
            if cv.left:
                used = 3 * cv.left * cv.o
                v = jnp.concatenate(left + [jnp.zeros((16, LANES - used), F32)], 1)
                put(i * cv.group + 3 * cv.full, v.astype(BF16))
            return carry

        lax.fori_loop(0, cv.c // 16, tile, 0, unroll=2)

    def cross_start(k):
        gs, gx = (k_.gs2, k_.gs3)[k - 2], (k_.gx2, k_.gx3)[k - 2]

        for part in range(nx):

            def put(i, v, part=part):
                gs[part, i] = v

            tiles_of(k, part, put)
        for t in range(1, nx):

            def copy(t=t):
                tox = at_x(t)[0]
                return peer_copy(
                    gs.at[tox], gx.at[x], k_.c_send.at[k - 2, t], k_.c_recv.at[k - 2, t], place, 2 * tox + core
                )

            launch(None, copy)

    def cross_finish(k):
        cv, gs, gx = convs[k], (k_.gs2, k_.gs3)[k - 2], (k_.gx2, k_.gx3)[k - 2]
        sources = [at_x(t)[1] for t in range(1, nx)]
        for t, fromx in enumerate(sources, 1):
            theirs = gx.at[fromx]
            peer_copy(
                theirs, theirs, k_.c_send.at[k - 2, t], k_.c_recv.at[k - 2, t], place, 2 * fromx + core
            ).wait_recv()

        def add(i, carry):
            for j in range(cv.group):
                p = cv.group * i + j
                v = gs[x, p].astype(F32)
                for fromx in sources:
                    v += gx[fromx, p].astype(F32)
                gt[k][p] = v.astype(BF16)
            return carry

        lax.fori_loop(0, cv.c // 16, add, 0, unroll=2)
        reduce_send(k)

    def reduce_start(k):
        def put(i, v):
            gt[k][i] = v

        tiles_of(k, 0, put)
        reduce_send(k)

    nh = nd // 2
    par, rank = lax.rem(place, 2), lax.div(place, 2)
    partner = place + 1 - 2 * par

    def rank_peers(i):
        to = rank + 1 + i
        return 2 * jnp.where(to >= nh, to - nh, to) + par, me

    def half_of(k, which):
        size = nh * convs[k].share
        return pl.ds(which * size, size)

    def share_of(k, owner):
        size = convs[k].share
        if k == 0:
            return pl.ds(owner * size, size)
        return pl.ds((lax.rem(owner, 2) * nh + lax.div(owner, 2)) * size, size)

    def level(k):
        return (nd, slab_peers, place) if k == 0 else (nh, rank_peers, rank)

    def pair_copy(src, dst, k, i):
        return peer_copy(src, dst, k_.q_send.at[k, i], k_.q_recv.at[k, i], partner, me)

    def reduce_send(k):
        cv = convs[k]
        for i in range(cv.count, cv.share * nd):
            gt[k][i] = jnp.zeros((16, LANES), BF16)
        if k == 0:
            spread_shares(k)
        else:
            launch(None, lambda: pair_copy(gt[k].at[half_of(k, 1 - par)], gp[k - 1], k, 0))

    def pair_finish(k):
        pair_copy(gp[k - 1], gp[k - 1], k, 0).wait_recv()
        own = half_of(k, par)
        gt[k][own] = (gt[k][own].astype(F32) + gp[k - 1][...].astype(F32)).astype(BF16)
        spread_shares(k)

    def spread_shares(k):
        n, peers, own = level(k)
        gr[k][own] = gt[k][share_of(k, place)]

        def copy(to, chan):
            return peer_copy(gt[k].at[share_of(k, to)], gr[k].at[own], k_.r_send.at[k], k_.r_recv.at[k], to, chan)

        exchange(n, peers, copy)
        pending.append((None, lambda: reduce_all(k).wait_send()))

    def reduce_all(k):
        every = gr[k].at[pl.ds(0, level(k)[0] - 1)]
        return peer_copy(every, every, k_.r_send.at[k], k_.r_recv.at[k], place, mate)

    def share_all(k):
        every = ga[k].at[pl.ds(0, (level(k)[0] - 1) * convs[k].share)]
        return peer_copy(every, every, k_.a_send.at[k], k_.a_recv.at[k], place, mate)

    def reduce_finish(k):
        reduce_all(k).wait_recv()
        own = share_of(k, place)
        ga[k][own] = jnp.sum(gr[k][...].astype(F32), axis=0).astype(BF16)

        def copy(to, chan):
            return peer_copy(ga[k].at[own], ga[k].at[own], k_.a_send.at[k], k_.a_recv.at[k], to, chan)

        n, peers, _ = level(k)
        exchange(n, peers, copy)
        pending.append((None, lambda: share_all(k).wait_send()))

    def share_pass(k):
        share_all(k).wait_recv()
        own = ga[k].at[half_of(k, par)]
        launch(None, lambda: pair_copy(own, own, k, 1))

    def gradient_out(k):
        cv, out = convs[k], grads[k]
        if k == 0:
            share_all(k).wait_recv()
        else:
            theirs = ga[k].at[half_of(k, 1 - par)]
            pair_copy(theirs, theirs, k, 1).wait_recv()
        group = iota((16, LANES), 1) // cv.o

        def scatter(i, carry):
            def put(v, g, kz, t):
                turned[pl.ds(9 * kz + t + i * (16 * 27), 16, stride=27)] = jnp.where(group == g, v, 0.0)

            for kz in range(3):
                for j in range(cv.full):
                    v = ga[k][i * cv.group + kz * cv.full + j].astype(F32)
                    for g in range(min(cv.per, 9)):
                        put(v, g, kz, j * cv.per + g)
            if cv.left:
                v = ga[k][i * cv.group + 3 * cv.full].astype(F32)
                for kz in range(3):
                    for g in range(cv.left):
                        put(v, kz * cv.left + g, kz, cv.full * cv.per + g)
            return carry

        lax.fori_loop(0, cv.c // 16, scatter, 0, unroll=2)

        pick = (iota((cv.o, LANES), 1) % cv.o == iota((cv.o, LANES), 0)).astype(BF16)
        step = 8 * LANES
        for at in range(0, cv.length, step):
            size = min(step, cv.length - at)
            v = dot_nt(pick, turned[at : at + -(-size // LANES) * LANES].astype(BF16))
            out[:, at : at + size] = v[:, 0:size]

    def column(row):
        n = row.shape[1]
        eye = iota((n, n), 0) == iota((n, n), 1)
        return jnp.sum(jnp.where(eye, row, 0.0), axis=1, keepdims=True)

    def row_of(col):
        n = col.shape[0]
        eye = iota((n, n), 0) == iota((n, n), 1)
        return jnp.sum(jnp.where(eye, col, 0.0), axis=0, keepdims=True)

    def clear_halos(ref):
        def clear(at):
            if len(ref.shape) == 5:
                for c in range(2):
                    ref[c, at] = jnp.zeros(ref.shape[2:], ref.dtype)
            else:
                for i in range(nx):
                    ref[core, i, at] = jnp.zeros(ref.shape[3:], ref.dtype)

        pl.when(first)(lambda: clear(0))
        pl.when(last)(lambda: clear(ref.shape[-4] - 1))

    def clear_rows(ref):
        def clear(at):
            for c in range(2):
                for i in range(S + 2):
                    ref[c, i, at] = jnp.zeros(ref.shape[3:], ref.dtype)

        pl.when(top)(lambda: clear(0))
        pl.when(bottom)(lambda: clear(E - 1))

    def conv(operand, weight, m, groups, emit, init):
        def body(d, carry):
            v = operand(d)
            y = dot(weight, v)
            results = []
            for j in range(RB):
                lanes = slice(j * LANES, (j + 1) * LANES)
                parts = []
                for g in range(groups):
                    a = [y[(3 * g + kx) * m : (3 * g + kx + 1) * m, lanes] for kx in range(3)]
                    parts.append(from_left(a[0], W) + a[1] + from_right(a[2], W))
                results.append(jnp.concatenate(parts, 0) if groups > 1 else parts[0])
            return emit(d, results, carry)

        return lax.fori_loop(0, S, body, init)

    def rows_of(row):
        return lambda d: jnp.concatenate(
            [jnp.concatenate([row(d + kz, ky + j) for j in range(RB)], 1) for kz in range(3) for ky in range(3)], 0
        )

    def blocks_of(ref):
        size = dm.cd
        return lambda d: jnp.concatenate(
            [
                jnp.concatenate([ref[c, d + kz, 2 - ky + j, i * size : (i + 1) * size] for j in range(RB)], 1)
                for kz in range(3)
                for i in range(nx)
                for c in range(2)
                for ky in range(3)
            ],
            0,
        ).astype(BF16)

    def conv_stats(row, weight, z):
        def emit(d, results, carry):
            total, square = carry
            for j, v in enumerate(results):
                z[d * RB + j] = v
                total, square = total + v, square + v * v
            return total, square

        blank = jnp.zeros((dm.cf, LANES), F32)
        return conv(rows_of(row), weight, dm.cd, nx, emit, (blank, blank))

    def weight_grad(row, k):
        cv = convs[k]

        def part(d):
            v = jnp.concatenate([jnp.concatenate([row(d + kz, j) for j in range(E)], 1) for kz in range(3)], 0)
            y = jnp.concatenate(
                [k_.dzt[d, (2 - ky) * LANES : (2 - ky + E) * LANES] for ky in range(3)], 1
            )
            return dot(v, y)

        acc[0 : 3 * cv.c] = part(0)

        def more(d, carry):
            acc[0 : 3 * cv.c] += part(d)
            return carry

        lax.fori_loop(1, S, more, 0)

    def conv_coarse(ref, weight, m):
        v = jnp.concatenate(
            [jnp.concatenate([flat(ref, kz, i) for i in range(Q)], 1) for kz in range(3)], 0
        )
        y = dot(weight[...], v)
        blank = jnp.zeros((m, LANES), F32)

        def shifted(ky, i):
            if not 0 <= i < Q:
                return blank
            a, b, c = (
                y[(3 * kx + ky) * m : (3 * kx + ky + 1) * m, i * LANES : (i + 1) * LANES] for kx in range(3)
            )
            return from_left(a, V) + b + from_right(c, V)

        before = [shifted(0, i) for i in range(-1, Q)]
        after = [shifted(2, i) for i in range(Q + 1)]
        return [
            shifted(1, i) + halves(before[i + 1] + after[i + 1], before[i] + after[i]) for i in range(Q)
        ]

    def conv_stats_coarse(ref, weight, z, m):
        total = square = jnp.zeros((m, LANES), F32)
        for i, v in enumerate(conv_coarse(ref, weight, m)):
            z[i] = v
            total, square = total + v, square + v * v
        return total, square

    def weight_grad_coarse(ref, k):
        cv = convs[k]
        v = jnp.concatenate(
            [jnp.concatenate([flat(ref, kz, i) for i in range(Q)], 1) for kz in range(3)], 0
        )
        y = jnp.concatenate([k_.dzct[(2 - ky) * V : (2 - ky) * V + Q * LANES] for ky in range(3)], 1)
        acc[0 : 3 * cv.c] = dot(v, y)

    def pack(a, b):
        m = a.shape[0]
        a = jnp.sum(a, axis=1, keepdims=True)
        b = jnp.sum(b, axis=1, keepdims=True)
        lane, channel = iota((m, LANES), 1), iota((m, LANES), 0)
        both = jnp.where(lane == channel, a, jnp.where(lane == channel + m, b, 0.0))
        return jnp.sum(both, axis=0, keepdims=True)

    def moments(total, count):
        mean = total[0] / count
        var = total[1] / count - mean * mean
        return mean, lax.rsqrt(var + EPS)

    def wide(column):
        return jnp.broadcast_to(column, (column.shape[0], LANES))

    def factors(stats, norm):
        mean, inv = stats
        gain, shift = norm
        return wide(mean), wide(gain * inv), wide(shift)

    def norm_rows(z, stats, norm, emit, n):
        mean, scale, shift = factors(stats, norm)

        def body(i, carry):
            for j in range(n):
                p = i * n + j
                u = (z[p] - mean) * scale + shift
                emit(p, u * jax.nn.sigmoid(u))
            return carry

        lax.fori_loop(0, z.shape[0] // n, body, 0)

    def norm_back_sums(z, keep_du, stats, norm, grad, n):
        mean, scale, shift = factors(stats, norm)
        inv = wide(stats[1])
        m = z.shape[1]

        def body(i, carry):
            a, b = carry
            for j in range(n):
                p = i * n + j
                centred = z[p] - mean
                u = centred * scale + shift
                sigma = jax.nn.sigmoid(u)
                v = grad(p) * sigma * (1.0 + u * (1.0 - sigma))
                keep_du(p, v)
                a, b = a + v, b + v * (centred * inv)
            return a, b

        blank = jnp.zeros((m, LANES), F32)
        return lax.fori_loop(0, z.shape[0] // n, body, (blank, blank))

    def back_factors(stats, norm, total, count):
        mean, inv = stats
        scale = norm[0] * inv
        return wide(mean), wide(scale), wide(-scale * total[0] / count), wide(-scale * inv * total[1] / count)

    def columns_first(copies, groups):
        size = copies[0].shape[0] // groups
        rows = [v[g * size : (g + 1) * size] for g in range(groups) for v in copies]
        used = 3 * groups * size
        if used < LANES:
            rows.append(jnp.zeros((LANES - used, LANES), F32))
        return jnp.transpose(jnp.concatenate(rows, 0)).astype(BF16)

    def norm_back_fine(z, given, ref):
        mean, scale, level, slope = given

        def body(d, carry):
            for r in range(RB):
                p = d * RB + r
                v = scale * k_.du_f[p] + level + slope * (z[p] - mean)
                ref[core, 1 + d, 1 + r] = v.astype(BF16).astype(ref.dtype)
            return carry

        lax.fori_loop(0, S, body, 0)

    def turn_fine(ref):
        n = 4 if RB % 4 == 0 else 2

        def body(i, carry):
            d = lax.div(i, RB // n)
            r0 = (i - d * (RB // n)) * n
            for j in range(n):
                v = ref[core, 1 + d, 1 + r0 + j].astype(F32)
                at = pl.ds(pl.multiple_of((2 + r0 + j) * LANES, LANES), LANES)
                k_.dzt[d, at] = columns_first((from_right(v, W), v, from_left(v, W)), nx)
            return carry

        lax.fori_loop(0, S * RB // n, body, 0)

    def norm_back_coarse(z, given, ref):
        mean, scale, level, slope = given
        for i in range(Q):
            v = scale * k_.du_c[i] + level + slope * (z[i] - mean)
            ref[core, x, 1, i] = v.astype(BF16).astype(ref.dtype)

    def turn_coarse(ref):
        for i in range(Q):
            v = ref[core, x, 1, i].astype(F32)
            k_.dzct[V + i * LANES : V + (i + 1) * LANES] = columns_first((from_right(v, V), v, from_left(v, V)), 1)

    def keep_du(ref):
        def store(p, v):
            ref[p] = v

        return store

    barrier = pltpu.get_barrier_semaphore()

    def greet(depth, chan):
        pl.semaphore_signal(barrier, inc=1, device_id={"depth": depth, "chan": chan}, device_id_type=MESH)

    exchange(nd * nx, wide_peers, lambda depth, chan: types.SimpleNamespace(start=lambda: greet(depth, chan)))
    for t in range(nx):
        to = 2 * at_x(t)[0] + other
        greet(place, to)
        if t > 0:
            pl.when(no(first))(lambda to=to: greet(place - 1, to))
            pl.when(no(last))(lambda to=to: greet(place + 1, to))

    hc = iota((LANES, LANES), 0)
    fc = iota((LANES, LANES), 1)
    half = LANES // 2

    def up_table(coarse, fine):
        base = fine // 2
        beside = jnp.clip(base + jnp.where(fine % 2 == 0, -1, 1), 0, V - 1)
        near = (coarse == base).astype(F32)
        far = (coarse == beside).astype(F32)
        return (0.75 * near + 0.25 * far).astype(BF16)

    pool = jnp.concatenate([(hc // 2 == fc - at).astype(BF16) for at in (0, half)], 0)
    spread = jnp.concatenate([(hc - at == fc // 2).astype(BF16) for at in (0, half)], 1)
    up = jnp.concatenate([up_table(hc - at, fc) for at in (0, half)], 1)
    down = jnp.concatenate([up_table(fc, hc)] * 2, 0)
    spread2 = jnp.concatenate([spread, spread], 0)

    def take_rows(ref):
        for c in range(ref.shape[0]):
            k_.rows[c * S * R : (c + 1) * S * R] = ref[c].astype(F32).reshape(S * R, LANES)

    def row_of_all(p, chans):
        return k_.rows[pl.ds(p, chans, stride=S * R)]

    xp, xs, own_skip = k_.xp, k_.xs, k_.own_skip
    clear_halos(xp)
    take_rows(k_.skip)
    for i in range(S):
        for r in (0, R + 1):
            own_skip[i, r] = jnp.zeros((dm.cs, LANES), own_skip.dtype)

    def take_skip(i, carry):
        parts = []
        for d in range(S):
            v = [row_of_all(d * R + 4 * i + j, dm.cs).astype(BF16) for j in range(4)]
            for j in range(4):
                own_skip[d, 1 + 4 * i + j] = v[j].astype(own_skip.dtype)
            parts += [jnp.concatenate([v[j], v[2 + j]], 1) for j in range(2)]
        v = dot(jnp.concatenate(parts, 0), pool).reshape(2 * S, dm.cs, LANES)
        xp[core, x, 1, i] = (jnp.sum(v, axis=0) * 0.125).astype(BF16).astype(xp.dtype)
        return carry

    lax.fori_loop(0, Q, take_skip, 0, unroll=3)
    beside = jnp.where(first, 0, 1) + jnp.where(last, 0, 1)
    pl.semaphore_wait(barrier, nd * nx - 1 + nx + (nx - 1) * beside)
    gather_start(xp, "pooled")
    clear_halos(xs)
    xs[core, x, 1 : S + 1] = own_skip[:, pl.ds(row0, E)]
    gather_start(xs, "skip", lambda at, tox: own_skip.at[at, pl.ds(tox * RB, E)])

    gq = dm.g // nc
    columns = dm.enc_all + dm.skip_all
    gate_all, norm_all = k_.gate_all, k_.norm_all
    gate_all[me, :, 0:columns] = k_.gate[...]
    lane = iota((gq, LANES), 1)
    gate_all[me, :, 2 * LANES :] = jnp.where(
        lane == 0, column(k_.vector[0:1]), jnp.where(lane == 1, column(k_.vector[1:2]), 0.0)
    )
    for layer in range(2):
        for part in range(2):
            at = 2 * layer + part
            norm_all[me, at : at + 1, 0 : dm.cd] = k_.dn[part, layer : layer + 1]

    def constants(i, t, source, to):
        ref = (norm_all, gate_all)[i]
        return peer_copy(ref.at[source], ref.at[source], k_.v_send.at[i, t], k_.v_recv.at[i, t], place, to)

    for i in range(2):
        for t in range(1, nc):
            launch(None, functools.partial(constants, i, t, me, lax.rem(me + t, nc)))
    prepare(0)
    xd, xz4, xz3, d1 = k_.xd, k_.xz4, k_.xz3, k_.d1
    for ref in (xd, xz4, xz3):
        clear_rows(ref)
        clear_halos(ref)
    for ref in (k_.xh, k_.xz2, k_.xz1):
        clear_halos(ref)
    for i in range(S):
        for at in (0, (RB + 2) * LANES):
            k_.dzt[i, at : at + 2 * LANES] = jnp.zeros((2 * LANES, LANES), BF16)
        for r in range(3):
            k_.ug[i, r] = jnp.zeros(k_.ug.shape[2:], F32)
            k_.ug[i, RB + 3 + r] = jnp.zeros(k_.ug.shape[2:], F32)
        for r in range(H + 2):
            k_.cb[i, r] = jnp.zeros(k_.cb.shape[2:], F32)

    for at in (0, V + Q * LANES):
        k_.dzct[at : at + V] = jnp.zeros((V, LANES), BF16)

    def norm_of(layer):
        return column(k_.en[0, layer : layer + 1]), column(k_.en[1, layer : layer + 1])

    norm_e1, norm_e2 = norm_of(0), norm_of(1)

    gather_pass(xp, "pooled")
    gather_wait(xp, "pooled")
    coarse_sums(0, conv_stats_coarse(xp, wf[0], k_.z1, dm.ce))
    prepare(1)
    stats_e1 = moments(coarse_totals(0), dm.coarse_total)

    def keep_coarse(ref):
        def store(p, v):
            ref[core, x, 1, p] = v.astype(BF16).astype(ref.dtype)

        return store

    norm_rows(k_.z1, stats_e1, norm_e1, keep_coarse(k_.xh), Q)
    gather_start(k_.xh, "hidden")
    prepare(2)
    forward_start(2)
    gather_pass(k_.xh, "hidden")
    gather_pass(xs, "skip")
    gather_wait(k_.xh, "hidden")
    coarse_sums(1, conv_stats_coarse(k_.xh, wf[1], k_.z2, dm.ce))
    take_rows(k_.cot)

    def take_cot(i, carry):
        for d in range(S):
            for j in range(4):
                v = row_of_all(d * R + 4 * i + j, dm.cd).astype(BF16)
                k_.own_cot[d, 4 * i + j] = v.astype(k_.own_cot.dtype)
        return carry

    lax.fori_loop(0, Q, take_cot, 0)
    k_.cots[x] = k_.own_cot[:, pl.ds(row0, RB)]
    stats_e2 = moments(coarse_totals(1), dm.coarse_total)
    norm_rows(k_.z2, stats_e2, norm_e2, keep_coarse(k_.xc), Q)
    gather_start(k_.xc, "coarse")
    prepare(3)
    for t in range(1, nc):
        for i in range(2):
            source = lax.rem(me + nc - t, nc)
            constants(i, t, source, source).wait_recv()
    gate_full = gate_all[...].reshape(dm.g, 3 * LANES)
    wg = gate_full[:, 0:columns].astype(BF16)
    gbias = gate_full[:, 2 * LANES : 2 * LANES + 1]
    gout = gate_full[:, 2 * LANES + 1 : 2 * LANES + 2]
    k_.gate_t[...] = jnp.transpose(gate_full[:, 0 : 2 * LANES])
    own_rows = [k_.gate_t[pl.ds(pl.multiple_of((2 * i + core) * dm.ce, dm.ce), dm.ce)] for i in range(nx)]
    own_rows += [
        k_.gate_t[pl.ds(pl.multiple_of(dm.enc_all + (2 * i + core) * dm.cs, dm.cs), dm.cs)] for i in range(nx)
    ]
    k_.gate_own[...] = jnp.concatenate(own_rows, 0)

    def norm_fine(layer):
        return tuple(
            jnp.concatenate(
                [column(norm_all[2 * i + core, 2 * layer + part : 2 * layer + part + 1, 0 : dm.cd]) for i in range(nx)], 0
            )
            for part in range(2)
        )

    norm_d1, norm_d2 = norm_fine(0), norm_fine(1)
    gather_pass(k_.xc, "coarse")
    gather_wait(k_.xc, "coarse")
    forward_start(3)

    dt = k_.dt

    def up_depth(i, carry):
        t = []
        for j in range(3):
            v = dot(flat(k_.xc, j, i), up)
            t.append(jnp.stack([v[:, 0:LANES], v[:, LANES:]], 0))
        below = jnp.where(first, t[1], t[0])
        above = jnp.where(last, t[1], t[2])
        near = 0.75 * t[1]
        here = 0.25 * t[1]
        rows = pl.ds(i * 2, 2)
        dt[0, rows] = jnp.where(first, 0.0, 0.75 * below + here)
        dt[1, rows] = near + 0.25 * below
        dt[2, rows] = near + 0.25 * above
        dt[3, rows] = jnp.where(last, 0.0, 0.75 * above + here)
        return carry

    lax.fori_loop(0, Q, up_depth, 0)

    def up_rows(i, carry):
        here = h0 + i
        before, after = jnp.maximum(here - 1, 0), jnp.minimum(here + 1, H - 1)
        for j in range(S + 2):
            v = 0.75 * dt[j, here]
            d1[j, 1 + 2 * i, 0 : dm.enc_all] = (v + 0.25 * dt[j, before]).astype(BF16)
            d1[j, 2 + 2 * i, 0 : dm.enc_all] = (v + 0.25 * dt[j, after]).astype(BF16)
        return carry

    lax.fori_loop(0, RB // 2, up_rows, 0)
    for edge, at, near, far in (
        (top, 0, jnp.maximum(h0 - 1, 0), h0),
        (bottom, E - 1, jnp.minimum(h0 + RB // 2, H - 1), h0 + RB // 2 - 1),
    ):
        for j in range(S + 2):
            v = jnp.where(edge, 0.0, 0.75 * dt[j, near] + 0.25 * dt[j, far])
            d1[j, at, 0 : dm.enc_all] = v.astype(BF16)
    for t in range(1, nx):
        tox = lax.rem(x + t, nx)

        def send_cot(t=t, tox=tox):
            return peer_copy(
                k_.own_cot.at[:, pl.ds(tox * RB, RB)], k_.cots.at[x], k_.o_send.at[0, t], k_.o_recv.at[0, t],
                place, 2 * tox + core,
            )

        launch(None, send_cot)

    gather_wait(xs, "skip")
    gate_n = E // 2

    def gate(i, carry):
        j = lax.div(i, 2)
        r0 = (i - 2 * j) * gate_n
        skips = [flat(xs, j, r0 + q) for q in range(gate_n)]
        v = jnp.concatenate(
            [
                jnp.concatenate([d1[j, r0 + q, 0 : dm.enc_all] for q in range(gate_n)], 1),
                jnp.concatenate(skips, 1),
            ],
            0,
        )
        pre = dot(wg, v) + gbias
        act = pre * jax.nn.sigmoid(pre)
        alpha = jax.nn.sigmoid(jnp.sum(gout * act, axis=0, keepdims=True))
        for q in range(gate_n):
            lanes = slice(q * LANES, (q + 1) * LANES)
            d1[j, r0 + q, dm.enc_all :] = (alpha[:, lanes] * skips[q].astype(F32)).astype(BF16)
            k_.pre[j, r0 + q] = pre[:, lanes]
            k_.alpha[j, r0 + q] = alpha[:, lanes]
        return carry

    lax.fori_loop(0, (S + 2) * 2, gate, 0)
    def row_d1(j, r):
        return d1[j, r]

    def row_xd(j, r):
        return natural(xd, j, r)

    forward_wait(2)
    fine_sums(0, conv_stats(row_d1, forward_weight(2), k_.z3))
    forward_wait(3)
    stats_d1 = moments(fine_totals(0), dm.fine_total)

    def keep_dec(p, v):
        d = lax.div(p, RB)
        xd[core, 1 + d, 1 + p - d * RB] = v.astype(BF16).astype(xd.dtype)

    norm_rows(k_.z3, stats_d1, norm_d1, keep_dec, RB)
    fine_start(xd, "hidden")
    weights_start(3)
    weights_start(2)
    for t in range(1, nx):
        fromx = lax.rem(x + nx - t, nx)
        theirs = k_.cots.at[fromx]
        peer_copy(theirs, theirs, k_.o_send.at[0, t], k_.o_recv.at[0, t], place, 2 * fromx + core).wait_recv()
    fine_pass(xd, "hidden")
    fine_wait(xd, "hidden")
    fine_sums(1, conv_stats(row_xd, forward_weight(3), k_.z4))
    stats_d2 = moments(fine_totals(1), dm.fine_total)

    def row_cot(p):
        d = lax.div(p, RB)
        return jnp.concatenate([k_.cots[i, d, p - d * RB] for i in range(nx)], 0).astype(F32)

    fine_sums(2, norm_back_sums(k_.z4, keep_du(k_.du_f), stats_d2, norm_d2, row_cot, RB))

    def keep_result(p, v):
        for i in range(nx):
            k_.ob[i, p] = v[i * dm.cd : (i + 1) * dm.cd].astype(BF16).astype(k_.ob.dtype)

    norm_rows(k_.z4, stats_d2, norm_d2, keep_result, RB)
    for t in range(1, nx):
        tox = lax.rem(x + t, nx)

        def send_result(t=t, tox=tox):
            return peer_copy(
                k_.ob.at[tox], k_.oi.at[x], k_.o_send.at[1, t], k_.o_recv.at[1, t], place, 2 * tox + core
            )

        launch(None, send_result)
    total_d2 = fine_totals(2)
    norm_back_fine(k_.z4, back_factors(stats_d2, norm_d2, total_d2, dm.fine_total), xz4)
    fine_start(xz4, "dz4")
    weights_start(1)
    weights_start(0)
    turn_fine(xz4)
    weight_grad(row_xd, 3)
    fine_pass(xz4, "dz4")
    cross_start(3)
    weights_finish(3)
    fine_wait(xz4, "dz4")

    def keep_grad(d, results, carry):
        for j, v in enumerate(results):
            k_.gg[d * RB + j] = v
        return carry

    conv(blocks_of(xz4), wb[3][...], dm.cf, 1, keep_grad, 0)
    fine_sums(3, norm_back_sums(k_.z3, keep_du(k_.du_f), stats_d1, norm_d1, lambda p: k_.gg[p], RB))
    cross_finish(3)
    total_d1 = fine_totals(3)
    norm_back_fine(k_.z3, back_factors(stats_d1, norm_d1, total_d1, dm.fine_total), xz3)
    fine_start(xz3, "dz3")
    turn_fine(xz3)
    weights_finish(2)
    weight_grad(row_d1, 2)
    fine_pass(xz3, "dz3")
    cross_start(2)
    pair_finish(3)
    fine_wait(xz3, "dz3")

    ups = nx * dm.ce

    def gate_back(d, results, carry):
        bias, psi = carry
        lows = []
        for j, both in enumerate(results):
            p = d * RB + j
            v = both[ups:]
            grad = jnp.sum(v * flat(xs, d + 1, 1 + j).astype(F32), axis=0, keepdims=True)
            alpha = k_.alpha[d + 1, 1 + j]
            logit = grad * alpha * (1.0 - alpha)
            pre = k_.pre[d + 1, 1 + j]
            sigma = jax.nn.sigmoid(pre)
            psi = psi + pre * sigma * logit
            low = (logit * gout * sigma * (1.0 + pre * (1.0 - sigma))).astype(BF16)
            bias = bias + low.astype(F32)
            k_.pg[p] = low
            lows.append(low)
            k_.ug[d, 3 + j] = both[0:ups]
            for i in range(nc):
                k_.gv[i] = v[i * dm.cs : (i + 1) * dm.cs]
            for i in range(nx):
                k_.sgp[i, p] = alpha * k_.gv[2 * i + core]
        back = dot(k_.gate_own[...].astype(BF16), jnp.concatenate(lows, 1))
        for j in range(len(results)):
            p = d * RB + j
            lanes = slice(j * LANES, (j + 1) * LANES)
            k_.ug[d, 3 + j] += back[0:ups, lanes]
            for i in range(nx):
                v = k_.sgp[i, p] + back[ups + i * dm.cs : ups + (i + 1) * dm.cs, lanes]
                k_.sgp[i, p] = v
                k_.sgb[i, p] = v.astype(BF16).astype(k_.sgb.dtype)
        return bias, psi

    blank = jnp.zeros((dm.g, LANES), F32)
    bias, psi = conv(blocks_of(xz3), wb[2][...], ups + dm.skip_all, 1, gate_back, (blank, blank))

    ug, cb, cg = k_.ug, k_.cb, k_.cg
    for q in range(RB // 2 + 2):
        terms = []
        for d in range(S):
            v = 0.75 * (ug[d, 2 * q + 1] + ug[d, 2 * q + 2]) + 0.25 * (ug[d, 2 * q + 3] + ug[d, 2 * q])
            if q == 1:
                v += jnp.where(top, 0.25 * ug[d, 3], 0.0)
            if q == RB // 2:
                v += jnp.where(bottom, 0.25 * ug[d, RB + 2], 0.0)
            terms.append(split(v))
        v = dot(jnp.concatenate(terms, 0), down)
        for d in range(S):
            cb[d, h0 + q] = v[d * ups : (d + 1) * ups]

    def to_slabs(i, carry):
        even, odd = (cb[d, 2 * i + 1] + pltpu.roll(cb[d, 2 * i + 2], half, 1) for d in range(S))
        middle = 0.75 * (even + odd) + jnp.where(first, 0.25 * even, 0.0) + jnp.where(last, 0.25 * odd, 0.0)
        for part, v in enumerate((0.25 * even, middle, 0.25 * odd)):
            for j in range(nx):
                block = v[j * dm.ce : (j + 1) * dm.ce]
                k_.fs[part, j, i] = block.astype(BF16).astype(k_.fs.dtype)
                if part == 1:
                    k_.fm[j, i] = block
        return carry

    lax.fori_loop(0, Q, to_slabs, 0)

    def fold_parts():
        for step in (-1, 1, 0):
            sends = (no(first), None, no(last))[step + 1]
            gets = (no(last), None, no(first))[step + 1]
            for t in range(nx):
                if (step, t) != (0, 0):
                    tox, fromx = lax.rem(x + t, nx), lax.rem(x + nx - t, nx)
                    sems = (k_.f_send.at[step + 1, t], k_.f_recv.at[step + 1, t])
                    theirs = k_.fr.at[step + 1, fromx]
                    yield (
                        sends, gets, fromx, step + 1,
                        functools.partial(
                            peer_copy, k_.fs.at[step + 1, tox], k_.fr.at[step + 1, x], *sems, place + step, 2 * tox + core
                        ),
                        functools.partial(peer_copy, theirs, theirs, *sems, place, 2 * fromx + core),
                    )

    for sends, _, _, _, out, _ in fold_parts():
        launch(sends, out)
    for t in range(1, nx):
        tox = lax.rem(x + t, nx)

        def send_skip(t=t, tox=tox):
            return peer_copy(
                k_.sgb.at[tox], k_.sgi.at[x], k_.o_send.at[2, t], k_.o_recv.at[2, t], place, 2 * tox + core
            )

        launch(None, send_skip)

    reduce_finish(3)
    cross_finish(2)

    k_.gw[...] = jnp.zeros(k_.gw.shape, F32)

    def gate_weight(d, carry):
        v = jnp.concatenate(
            [
                jnp.concatenate([d1[1 + d, 1 + j, 0 : dm.enc_all] for j in range(RB)], 1),
                jnp.concatenate([flat(xs, 1 + d, 1 + j) for j in range(RB)], 1),
            ],
            0,
        )
        y = jnp.concatenate([k_.pg[d * RB + j] for j in range(RB)], 1)
        k_.gw[0:columns, 0 : dm.g] += dot_nt(v, y)
        return carry

    lax.fori_loop(0, S, gate_weight, 0)
    gate_grad = jnp.transpose(k_.gw[...])
    lane = iota((dm.g, LANES), 1)
    vectors = jnp.where(
        lane == 0,
        jnp.sum(bias, axis=1, keepdims=True),
        jnp.where(lane == 1, jnp.sum(psi, axis=1, keepdims=True), 0.0),
    )
    gate_block = k_.gate_block
    for j in range(nc):
        mine = slice(j * gq, (j + 1) * gq)
        gate_block[j, :, 0 : 2 * LANES] = gate_grad[mine]
        gate_block[j, :, 2 * LANES :] = vectors[mine]
    sum_start(everyone, k_.sv, 4, 0, gate_block[me], lambda chan: gate_block.at[chan])
    cg[...] = k_.fm[x]
    for _, gets, fromx, part, _, back in fold_parts():

        def fold_in(back=back, part=part, fromx=fromx):
            back().wait_recv()
            cg[...] += k_.fr[part, fromx].astype(F32)

        guarded(gets, fold_in)

    coarse_sums(2, norm_back_sums(k_.z2, keep_du(k_.du_c), stats_e2, norm_e2, lambda p: cg[p], Q))
    pair_finish(2)
    share_pass(3)
    weights_finish(1)
    total_e2 = coarse_totals(2)
    norm_back_coarse(k_.z2, back_factors(stats_e2, norm_e2, total_e2, dm.coarse_total), k_.xz2)
    gather_start(k_.xz2, "dz2")
    turn_coarse(k_.xz2)
    weight_grad_coarse(k_.xh, 1)
    gather_pass(k_.xz2, "dz2")
    reduce_start(1)
    weights_finish(0)
    reduce_finish(2)
    gather_wait(k_.xz2, "dz2")
    for i, v in enumerate(conv_coarse(k_.xz2, wb[1], dm.ce)):
        cg[i] = v
    coarse_sums(3, norm_back_sums(k_.z1, keep_du(k_.du_c), stats_e1, norm_e1, lambda p: cg[p], Q))
    pair_finish(1)
    share_pass(2)
    gradient_out(3)
    total_e1 = coarse_totals(3)
    norm_back_coarse(k_.z1, back_factors(stats_e1, norm_e1, total_e1, dm.coarse_total), k_.xz1)
    gather_start(k_.xz1, "dz1")
    turn_coarse(k_.xz1)
    weight_grad_coarse(xp, 0)
    reduce_start(0)
    reduce_finish(1)
    gather_pass(k_.xz1, "dz1")
    gradient_out(2)

    def rows_out(ref, own, theirs, kind, size):
        def copy_rows(read, at):
            def body(d, carry):
                for r in range(RB):
                    p = (d * R + at * RB + r) * size
                    ref[pl.ds(pl.multiple_of(p, size), size)] = read(d * RB + r).astype(F32)
                return carry

            lax.fori_loop(0, S, body, 0)

        copy_rows(lambda p: own[x, p], x)
        for t in range(1, nx):
            fromx = lax.rem(x + nx - t, nx)
            block = theirs.at[fromx]
            peer_copy(block, block, k_.o_send.at[kind, t], k_.o_recv.at[kind, t], place, 2 * fromx + core).wait_recv()
            copy_rows(lambda p, fromx=fromx: theirs[fromx, p], fromx)

    share_pass(1)
    rows_out(k_.out, k_.ob, k_.oi, 1, dm.cd)
    rows_out(k_.sg, k_.sgp, k_.sgi, 2, dm.cs)
    reduce_finish(0)
    gather_wait(k_.xz1, "dz1")
    for i, v in enumerate(conv_coarse(k_.xz1, wb[0], dm.cs)):
        v = dot(split(v), spread2) * 0.125
        for j in range(4):
            part = v[:, (j // 2) * LANES : (j // 2 + 1) * LANES]
            for d in range(S):
                at = (d * R + 4 * i + j) * dm.cs
                k_.sg[at : at + dm.cs] += part
    gradient_out(1)
    gate_total = sum_finish(everyone, k_.sv, 4, 0)
    k_.ggate[...] = gate_total[:, 0:columns]
    k_.gvector[0:1] = row_of(gate_total[:, 2 * LANES : 2 * LANES + 1])
    k_.gvector[1:2] = row_of(gate_total[:, 2 * LANES + 1 : 2 * LANES + 2])

    def own_part(col):
        parts = [jnp.where(x == i, col[i * dm.cd : (i + 1) * dm.cd], 0.0) for i in range(nx)]
        return functools.reduce(jnp.add, parts)

    for ref, pair, pick in ((k_.gen, (total_e1, total_e2), lambda v: v), (k_.gdn, (total_d1, total_d2), own_part)):
        for layer, total in enumerate(pair):
            ref[0, layer : layer + 1] = row_of(pick(total[1]))
            ref[1, layer : layer + 1] = row_of(pick(total[0]))
    gradient_out(0)
    drain()


def adamw(weight, grad, moment, square, rate):
    new_moment = 0.9 * moment + 0.1 * grad
    new_square = 0.999 * square + 0.001 * grad * grad
    moment_hat = new_moment / (1.0 - 0.9**STEP)
    square_hat = new_square / (1.0 - 0.999**STEP)
    new_weight = weight - rate * (moment_hat / (jnp.sqrt(square_hat) + 1e-08) + 0.01 * weight)
    return (new_weight, new_moment, new_square)


RATES = (CONV_RATE, CONV_RATE, GATE_RATE, VECTOR_RATE, CONV_RATE, CONV_RATE, VECTOR_RATE, VECTOR_RATE)


def update_kernel(*refs):
    n = len(RATES)
    sources, targets = refs[: 2 + 4 * n], refs[2 + 4 * n : 4 + 7 * n]
    inside, outside = refs[4 + 7 * n : 6 + 11 * n], refs[6 + 11 * n : 8 + 14 * n]
    in_sem, out_sem = refs[8 + 14 * n :]
    order = (4, 1, 0, 5, 2, 3, 6, 7)

    def load(i):
        return pltpu.make_async_copy(sources[i], inside[i], in_sem.at[i])

    def store(i):
        return pltpu.make_async_copy(outside[i], targets[i], out_sem.at[i])

    for i in (1, 0):
        load(i).start()
    for k in order:
        for part in range(4):
            load(2 + part * n + k).start()
    for i in (1, 0):
        load(i).wait()
        chans, (slabs, rows) = outside[i].shape[0], outside[i].shape[1:3]
        for c in range(chans):
            v = inside[i][pl.ds(c, slabs * rows, stride=chans)]
            outside[i][c] = v.reshape(slabs, rows, LANES).astype(outside[i].dtype)
        store(i).start()
    for k in order:
        own = [2 + part * n + k for part in range(4)]
        for i in own:
            load(i).wait()
        rows = inside[own[0]].shape[0]
        step = 8 if rows % 8 == 0 and rows > 8 else rows
        for r in range(0, rows, step):
            at = slice(r, r + step)
            new = adamw(*(inside[i][at] for i in own), RATES[k])
            for part, value in enumerate(new):
                outside[2 + 3 * k + part][at] = value
        for part in range(3):
            store(2 + 3 * k + part).start()
    for i in range(len(targets)):
        store(i).wait()


def per_device(
    skip, cotangent, enc_conv1, enc_conv2, gate_proj, gate_vector, dec_conv1, dec_conv2, enc_norms, dec_norms, *states
):
    nd, nc = lax.axis_size("depth"), lax.axis_size("chan")
    dm = Dims(nd, nc, skip.shape, enc_conv1.shape[0], dec_conv1.shape[0], gate_proj.shape[0] * nc)
    S, R, H, nx, RB, E = dm.s, dm.rows, dm.half, dm.nx, dm.rb, dm.ext
    Q = H // 2
    cin3 = dm.enc_all + dm.skip_all

    def own_block(size):
        return (size, lambda j: pl.multiple_of(j * size, size), 0)

    def core_blocks(size):
        return tuple(
            (size, lambda j, i=i: pl.multiple_of((2 * i + lax.rem(j, 2)) * size, size), i * size) for i in range(nx)
        )

    dm.convs = convs = (
        Conv(dm, dm.ce, dm.skip_all, (own_block(dm.cs),)),
        Conv(dm, dm.ce, dm.enc_all, (own_block(dm.ce),)),
        Conv(dm, dm.cd, cin3, core_blocks(dm.ce) + ((dm.skip_all, lambda j: dm.enc_all, nx * dm.ce),)),
        Conv(dm, dm.cd, dm.dec_all, core_blocks(dm.cd)),
    )
    params = (enc_conv1, enc_conv2, gate_proj, gate_vector, dec_conv1, dec_conv2, enc_norms, dec_norms)
    inputs = dict(
        skip=skip, cot=cotangent, w0=enc_conv1, w1=enc_conv2, w2=dec_conv1, w3=dec_conv2,
        gate=gate_proj, vector=gate_vector, en=enc_norms, dn=dec_norms,
    )
    shape = jax.ShapeDtypeStruct
    outs = dict(
        out=shape((S * R * dm.cd, LANES), F32),
        sg=shape((S * R * dm.cs, LANES), F32),
        **{f"g{i}": shape(a.shape, F32) for i, a in enumerate((enc_conv1, enc_conv2, dec_conv1, dec_conv2))},
        **{
            name: shape(a.shape, F32)
            for name, a in (("ggate", gate_proj), ("gvector", gate_vector), ("gen", enc_norms), ("gdn", dec_norms))
        },
    )
    gq = dm.g // nc

    def coarse(block):
        return pltpu.VMEM((2, nx, 3, Q, block, LANES), storage(block))

    def fine():
        return pltpu.VMEM((2, S + 2, E, dm.cf, LANES), storage(dm.cd))

    def f32(*dims):
        return pltpu.VMEM((*dims, LANES), F32)

    def tiles(*dims):
        return pltpu.VMEM((*dims, 16, LANES), BF16)

    def blocks(block, *dims):
        return pltpu.VMEM((*dims, block, LANES), storage(block))

    def sems(*dims):
        return pltpu.SemaphoreType.DMA(dims)

    scratch = dict(
        xp=coarse(dm.cs), xh=coarse(dm.ce), xc=coarse(dm.ce), xz2=coarse(dm.ce), xz1=coarse(dm.ce),
        own_skip=blocks(dm.cs, S, R + 2), xs=blocks(dm.cs, 2, nx, S + 2, E),
        own_cot=blocks(dm.cd, S, R), cots=blocks(dm.cd, nx, S, RB),
        d1=pltpu.VMEM((S + 2, E, cin3, LANES), BF16), xd=fine(), xz4=fine(), xz3=fine(),
        z1=f32(Q, dm.ce), z2=f32(Q, dm.ce), z3=f32(S * RB, dm.cf), z4=f32(S * RB, dm.cf),
        du_c=f32(Q, dm.ce), du_f=f32(S * RB, dm.cf), gg=f32(S * RB, dm.cf), cg=f32(Q, dm.ce),
        pre=f32(S + 2, E, dm.g), alpha=f32(S + 2, E, 1), pg=pltpu.VMEM((S * RB, dm.g, LANES), BF16),
        ug=f32(S, RB + 6, nx * dm.ce), cb=f32(S, H + 2, nx * dm.ce), dt=f32(S + 2, H, dm.enc_all),
        gv=f32(nc, dm.cs), sgp=f32(nx, S * RB, dm.cs), sgb=blocks(dm.cs, nx, S * RB), sgi=blocks(dm.cs, nx, S * RB),
        ob=blocks(dm.cd, nx, S * RB), oi=blocks(dm.cd, nx, S * RB),
        dzt=pltpu.VMEM((S, (RB + 4) * LANES, LANES), BF16), dzct=pltpu.VMEM((Q * LANES + 2 * dm.hcols, LANES), BF16),
        gw=f32(2 * LANES), dense=pltpu.VMEM((max(3 * cv.c for cv in convs), 3 * LANES), F32),
        fs=blocks(dm.ce, 3, nx, Q), fr=blocks(dm.ce, 3, nx, Q), fm=f32(nx, Q, dm.ce),
        st=f32(4, nd, 1), su=f32(4, nd * nx, 1), sv=pltpu.VMEM((1, nd * nx, gq, 3 * LANES), F32),
        norm_all=f32(nc, 8), rows=f32(max(dm.cs, dm.cd) * S * R),
        turned=f32(max(cv.chunks for cv in convs) * LANES),
        acc=pltpu.VMEM((max(3 * cv.c for cv in convs), 3 * LANES), F32),
        gate_all=pltpu.VMEM((nc, gq, 3 * LANES), F32), gate_t=pltpu.VMEM((2 * LANES, dm.g), F32),
        gate_own=pltpu.VMEM((nx * (dm.ce + dm.cs), dm.g), F32), gate_block=pltpu.VMEM((nc, gq, 3 * LANES), F32),
        **{f"wt{i}": pltpu.VMEM((3, cv.c, cv.wide), cv.kind) for i, cv in enumerate(convs)},
        **{
            f"wf{i}": pltpu.VMEM((cv.taps, 3 * cv.c) if i < 2 else (nx, cv.stored, 9 * cv.c), BF16)
            for i, cv in enumerate(convs)
        },
        **{f"wx{i}": pltpu.VMEM((nc, 3, cv.needed, cv.wide), cv.kind) for i, cv in enumerate(convs)},
        **{
            f"wb{i}": pltpu.VMEM((9 * cv.needed, 3 * nc * cv.o) if i < 2 else (3 * cv.needed, 9 * nc * cv.o), BF16)
            for i, cv in enumerate(convs)
        },
        flip=pltpu.VMEM((max(cv.tiles for cv in convs[2:]) * LANES, max(3 * cv.c for cv in convs[2:])), F32),
        **{f"gt{i}": tiles(cv.share * nd) for i, cv in enumerate(convs)},
        **{f"gr{i}": tiles(nd if i == 0 else nd // 2, cv.share) for i, cv in enumerate(convs)},
        **{f"gp{i}": tiles(nd // 2 * cv.share) for i, cv in enumerate(convs) if i > 0},
        **{f"ga{i}": tiles(cv.share * nd) for i, cv in enumerate(convs)},
        **{f"gs{i}": tiles(nx, convs[i].count) for i in (2, 3)},
        **{f"gx{i}": tiles(nx, convs[i].count) for i in (2, 3)},
        g_send=sems(len(GATHERS), 3, nx), g_recv=sems(len(GATHERS), 3),
        h_send=sems(len(GATHERS), 2 + nx), h_recv=sems(len(GATHERS)),
        x_send=sems(len(FINE), 3, 5), x_recv=sems(len(FINE), 3, 5),
        y_send=sems(len(FINE), 3), y_recv=sems(len(FINE), 3),
        t_send=sems(4), t_recv=sems(4), u_send=sems(5), u_recv=sems(5),
        f_send=sems(3, nx), f_recv=sems(3, nx), w_send=sems(4, nx + 1, nc), w_recv=sems(4, nx + 1, nc),
        p_send=sems(2, nx), p_recv=sems(2, nx), c_send=sems(2, nx), c_recv=sems(2, nx),
        o_send=sems(3, nx), o_recv=sems(3, nx), v_send=sems(2, nc), v_recv=sems(2, nc),
        r_send=sems(4), r_recv=sems(4), a_send=sems(4), a_recv=sems(4), q_send=sems(4, 2), q_recv=sems(4, 2),
    )
    vmem = pl.BlockSpec(memory_space=pltpu.VMEM)
    out, sg, grad1, grad2, grad3, grad4, ggate, gvector, gen, gdn = pl.pallas_call(
        functools.partial(kernel, dm, (*inputs, *outs, *scratch)),
        out_shape=tuple(outs.values()),
        in_specs=[vmem] * len(inputs),
        out_specs=[vmem] * len(outs),
        scratch_shapes=list(scratch.values()),
        compiler_params=pltpu.CompilerParams(
            has_side_effects=True, collective_id=0, vmem_limit_bytes=60 * 1024 * 1024
        ),
        name="step",
    )(*inputs.values())
    grads = (grad1, grad2, ggate, gvector, grad3, grad4, gen, gdn)
    operands = (out, sg, *params, *grads, *states)
    updated = (
        shape(cotangent.shape, BF16),
        shape(skip.shape, F32),
        *(shape(p.shape, F32) for p in params for _ in range(3)),
    )
    anywhere = pl.BlockSpec(memory_space=pl.ANY)
    return pl.pallas_call(
        update_kernel,
        out_shape=updated,
        in_specs=[anywhere] * len(operands),
        out_specs=[anywhere] * len(updated),
        scratch_shapes=[
            *(pltpu.VMEM(a.shape, a.dtype) for a in operands),
            *(pltpu.VMEM(a.shape, a.dtype) for a in updated),
            pltpu.SemaphoreType.DMA((len(operands),)),
            pltpu.SemaphoreType.DMA((len(updated),)),
        ],
        compiler_params=pltpu.CompilerParams(vmem_limit_bytes=60 * 1024 * 1024),
        name="update",
    )(*operands)


def solution(mesh):
    volume = P("chan", "depth", None, None)
    row, column, norms = P("chan", None), P(None, "chan"), P(None, None, "chan")
    params = (row, row, row, column, row, row, norms, norms)
    return jax.shard_map(
        per_device,
        mesh=mesh,
        in_specs=(volume, volume) + params * 3,
        out_specs=(volume, volume) + tuple(spec for spec in params for _ in range(3)),
        check_vma=False,
    )
```

```python
import functools
import types

import jax
import jax.numpy as jnp
from jax import lax
from jax.experimental import pallas as pl
from jax.experimental.pallas import tpu as pltpu
from jax.sharding import PartitionSpec as P

STEP = 5
EPS = 1e-05
CONV_RATE = 0.03
GATE_RATE = 0.1
VECTOR_RATE = 0.5
LANES = 128
MESH = pl.DeviceIdType.MESH
F32 = jnp.float32
BF16 = jnp.bfloat16


def iota(shape, dim):
    return lax.broadcasted_iota(jnp.int32, shape, dim)


def dot(a, b):
    return jnp.dot(a, b, preferred_element_type=F32)


def dot_nt(a, b):
    return lax.dot_general(a, b, (((1,), (1,)), ((), ())), preferred_element_type=F32)


def dot_tn(a, b):
    return lax.dot_general(a, b, (((0,), (0,)), ((), ())), preferred_element_type=F32)


def from_left(v, width):
    return jnp.where(iota(v.shape, 1) % width == 0, 0.0, pltpu.roll(v, 1, 1))


def from_right(v, width):
    return jnp.where(iota(v.shape, 1) % width == width - 1, 0.0, pltpu.roll(v, LANES - 1, 1))


def halves(low, high):
    return pltpu.roll(jnp.where(iota(low.shape, 1) < LANES // 2, low, high), LANES // 2, 1)


def split(v):
    high = v.astype(BF16)
    return jnp.concatenate([high, (v - high.astype(F32)).astype(BF16)], 1)


def storage(block):
    return BF16 if block % 16 == 0 else F32


def flat(ref, s, r):
    if len(ref.shape) == 4:
        return ref[s, r]
    v = ref[:, :, s, r]
    return jnp.concatenate([v[c, i] for i in range(v.shape[1]) for c in range(2)], 0).astype(BF16)


class Dims:
    def __init__(self, nd, nc, skip, enc, dec, gate):
        self.nd, self.nc, self.nx = nd, nc, nc // 2
        self.s, self.rows, self.cols = skip[1:]
        self.cs, self.ce, self.cd, self.g = skip[0], enc, dec, gate
        self.half, self.hcols = self.rows // 2, self.cols // 2
        self.fine_total = nd * self.s * self.rows * self.cols
        self.coarse_total = self.fine_total // 8
        self.enc_all = nc * enc
        self.skip_all = nc * skip[0]
        self.dec_all = nc * dec
        self.rb = self.rows // self.nx
        self.ext = self.rb + 2
        self.cf = self.nx * dec


GATHERS = ("pooled", "skip", "hidden", "coarse", "dz2", "dz1")
FINE = ("hidden", "dz4", "dz3")


class Conv:
    def __init__(self, dm, o, c, blocks):
        self.o, self.c, self.blocks = o, c, blocks
        self.length = 27 * c
        self.chunks = -(-self.length // LANES)
        self.per = LANES // o
        self.tiles = -(-9 // self.per)
        self.wide = self.tiles * LANES
        self.kind = storage(min(size for size, _, _ in blocks))
        self.needed = sum(size for size, _, _ in blocks)
        self.full = max(1, 9 // self.per)
        self.left = max(0, 9 - self.full * self.per)
        self.group = 3 * self.full + (self.left > 0)
        self.count = c // 16 * self.group
        self.share = -(-self.count // dm.nd)
        self.taps = 9 * o
        self.stored = -(-3 * o // 16) * 16


def kernel(dm, names, *refs):
    k_ = types.SimpleNamespace(**dict(zip(names, refs)))
    nd, nc, nx, S, R, H = dm.nd, dm.nc, dm.nx, dm.s, dm.rows, dm.half
    W, V = dm.cols, dm.hcols
    Q, RB, E = H // 2, dm.rb, dm.ext
    place = lax.axis_index("depth")
    me = lax.axis_index("chan")
    x, core = lax.div(me, 2), lax.rem(me, 2)
    other = 1 - core
    mate = 2 * x + other
    row0, h0 = x * RB, x * (RB // 2)
    first, last = place == 0, place == nd - 1
    top, bottom = x == 0, x == nx - 1
    convs = dm.convs
    pending = []
    wt, wf, wx, wb = ([getattr(k_, f"{kind}{i}") for i in range(4)] for kind in ("wt", "wf", "wx", "wb"))
    gp = (k_.gp1, k_.gp2, k_.gp3)
    gt, gr, ga = ([getattr(k_, f"{kind}{i}") for i in range(4)] for kind in ("gt", "gr", "ga"))
    weights = (k_.w0, k_.w1, k_.w2, k_.w3)
    grads = (k_.g0, k_.g1, k_.g2, k_.g3)
    turned, acc = k_.turned, k_.acc

    def no(cond):
        return jnp.logical_not(cond)

    def peer_copy(src, dst, send, recv, depth, chan):
        return pltpu.make_async_remote_copy(
            src_ref=src, dst_ref=dst, send_sem=send, recv_sem=recv,
            device_id={"depth": depth, "chan": chan}, device_id_type=MESH,
        )

    def guarded(cond, fn):
        if cond is None:
            fn()
        else:
            pl.when(cond)(fn)

    def drain():
        for cond, fn in pending:
            guarded(cond, fn)
        pending.clear()

    def launch(cond, copy):
        guarded(cond, lambda: copy().start())
        pending.append((cond, lambda: copy().wait_send()))

    def arrive(cond, copy):
        guarded(cond, lambda: copy().wait_recv())

    def both(a, b):
        return b if a is None else a if b is None else jnp.logical_and(a, b)

    can_send = (no(last), None, no(first))
    can_recv = (no(first), None, no(last))

    def slices(side, n):
        return (pl.ds(n, 1), pl.ds(1, n), pl.ds(1, 1))[side], (pl.ds(0, 1), pl.ds(1, n), pl.ds(n + 1, 1))[side]

    def at_x(t):
        up, down = x + t, x - t
        return jnp.where(up >= nx, up - nx, up), jnp.where(down < 0, down + nx, down)


    def gather_start(ref, which, source_at=None):
        n = ref.shape[2] - 2
        k = GATHERS.index(which)
        for side in (0, 2, 1):
            own, theirs = slices(side, n)
            for t in range(nx):
                if side == 1 and t == 0:
                    continue
                tox = at_x(t)[0]

                def copy(side=side, t=t, own=own, theirs=theirs, tox=tox):
                    start = (n, 1, 1)[side] - 1
                    size = (1, n, 1)[side]
                    src = ref.at[core, x, own] if source_at is None else source_at(pl.ds(start, size), tox)
                    return peer_copy(
                        src, ref.at[core, x, theirs], k_.g_send.at[k, side, t], k_.g_recv.at[k, side],
                        place + 1 - side, 2 * tox + core,
                    )

                launch(can_send[side], copy)
        gather_own(ref, which)

    def handed(ref, k, piece, i):
        return peer_copy(piece, piece, k_.h_send.at[k, i], k_.h_recv.at[k], place, mate)

    def gather_own(ref, which):
        k = GATHERS.index(which)
        launch(None, lambda: handed(ref, k, ref.at[core, x, pl.ds(1, ref.shape[2] - 2)], 0))

    def gather_pass(ref, which):
        n = ref.shape[2] - 2
        k = GATHERS.index(which)
        for side in (1, 0, 2):
            theirs = slices(side, n)[1]
            if side != 1:
                pieces = [ref.at[core, :, theirs]]
            else:
                pieces = [ref.at[core, at_x(t)[1], theirs] for t in range(1, nx)]
            for i, got in enumerate(pieces):
                arrive(
                    can_recv[side],
                    lambda got=got, side=side: peer_copy(
                        got, got, k_.g_send.at[k, side, 0], k_.g_recv.at[k, side], place, mate
                    ),
                )
                launch(None, lambda got=got, i=i, side=side: handed(ref, k, got, 1 + (side // 2 if side != 1 else 2 + i)))

    def gather_wait(ref, which):
        handed(ref, GATHERS.index(which), ref.at[other], 0).wait_recv()

    def fine_parts(ref, which, side):
        k = FINE.index(which)
        own, theirs = slices(side, S)
        inner = pl.ds(1, RB)
        rows = [(None, None, inner, inner, x, core, core)] if side != 1 else [(None, None, inner, inner, x, other, other)]
        if nx > 1:
            for c in range(2):
                rows.append((no(top), no(bottom), pl.ds(1, 1), pl.ds(E - 1, 1), x - 1, c, c))
                rows.append((no(bottom), no(top), pl.ds(RB, 1), pl.ds(0, 1), x + 1, c, c))
        parts = []
        for i, (sends, gets, row, at, tox, to, source) in enumerate(rows):
            target = ref.at[core, theirs, at]
            theirs_ = ref.at[source, theirs, at]
            up = (i - 1) % 2
            arrived = 0 if i == 0 else 1 + up * 2 + core
            expected = 0 if i == 0 else 1 + up * 2 + source
            send = k_.x_send.at[k, side, i]
            parts.append((
                both(can_send[side], sends), both(can_recv[side], gets),
                functools.partial(
                    peer_copy, ref.at[core, own, row], target, send, k_.x_recv.at[k, side, arrived],
                    place + 1 - side, 2 * tox + to,
                ),
                functools.partial(peer_copy, theirs_, theirs_, send, k_.x_recv.at[k, side, expected], place, mate),
            ))
        return parts

    def fine_start(ref, which):
        for side in (0, 2, 1):
            for sends, _, out, _ in fine_parts(ref, which, side):
                launch(sends, out)

    def fine_halo(ref, which, side, c):
        k = FINE.index(which)
        block = ref.at[c, slices(side, S)[1], pl.ds(1, RB)]
        return peer_copy(block, block, k_.y_send.at[k, side], k_.y_recv.at[k, side], place, mate)

    def fine_pass(ref, which):
        for side in (0, 2):
            _, gets, _, back = fine_parts(ref, which, side)[0]
            arrive(gets, back)
            launch(gets, functools.partial(fine_halo, ref, which, side, core))

    def fine_wait(ref, which):
        for side in (1, 0, 2):
            for _, gets, _, back in fine_parts(ref, which, side)[side != 1 :]:
                arrive(gets, back)
            if side != 1:
                arrive(can_recv[side], functools.partial(fine_halo, ref, which, side, other))

    def natural(ref, s, r):
        v = ref[:, s, r]
        size = dm.cd
        return jnp.concatenate(
            [v[c, i * size : (i + 1) * size] for i in range(nx) for c in range(2)], 0
        ).astype(BF16)

    def in_turn(count, fn):
        if count <= 16:
            for i in range(count):
                fn(i)
        else:

            def body(i, carry):
                fn(i)
                return carry

            lax.fori_loop(0, count, body, 0)

    def slab_peers(i):
        to = place + 1 + i
        return jnp.where(to >= nd, to - nd, to), me

    def wide_peers(i):
        i = i + 1
        dt, xt = (i // nx, i % nx) if isinstance(i, int) else (lax.div(i, nx), lax.rem(i, nx))
        to, tox = place + dt, x + xt
        return jnp.where(to >= nd, to - nd, to), 2 * jnp.where(tox >= nx, tox - nx, tox) + core

    def exchange(n, peers, copy):
        in_turn(n - 1, lambda i: copy(*peers(i)).start())

    def sum_start(group, ref, k, slot, tile, source=None):
        n, own, peers, send, recv = group
        ref[slot, own] = tile

        def copy(depth, chan):
            src = ref.at[slot, own] if source is None else source(chan)
            return peer_copy(src, ref.at[slot, own], send.at[k], recv.at[k], depth, chan)

        exchange(n, peers, copy)
        pending.append((None, lambda: all_of(group, ref, k, slot).wait_send()))

    def all_of(group, ref, k, slot):
        n, _, _, send, recv = group
        every = ref.at[slot, pl.ds(0, n - 1)]
        return peer_copy(every, every, send.at[k], recv.at[k], place, mate)

    def sum_finish(group, ref, k, slot):
        all_of(group, ref, k, slot).wait_recv()
        return jnp.sum(ref[slot], axis=0)

    slabs = (nd, place, slab_peers, k_.t_send, k_.t_recv)
    everyone = (nd * nx, place * nx + x, wide_peers, k_.u_send, k_.u_recv)

    def columns_of(row, m):
        lane, channel = iota((m, LANES), 1), iota((m, LANES), 0)
        return tuple(
            jnp.sum(jnp.where(lane == channel + i * m, row, 0.0), axis=1, keepdims=True) for i in range(2)
        )

    def coarse_sums(slot, sums):
        sum_start(slabs, k_.st, slot, slot, pack(*sums))

    def coarse_totals(slot):
        return columns_of(sum_finish(slabs, k_.st, slot, slot), dm.ce)

    def fine_sums(slot, sums):
        sum_start(everyone, k_.su, slot, slot, pack(*sums))

    def fine_totals(slot):
        return columns_of(sum_finish(everyone, k_.su, slot, slot), dm.cf)

    def prepare(k):
        cv, w, own = convs[k], weights[k], wt[k]
        out = wf[k] if k < 2 else wf[k].at[x]
        eye = (iota((LANES, LANES), 0) == iota((LANES, LANES), 1)).astype(BF16)

        def chunk(a):
            return dot_nt(eye, jnp.concatenate([a] * cv.per, 0).astype(BF16))

        full = cv.length // LANES

        def body(i, carry):
            at = pl.multiple_of(i * LANES, LANES)
            turned[pl.ds(at, LANES)] = chunk(w[:, pl.ds(at, LANES)])
            return carry

        lax.fori_loop(0, full, body, 0, unroll=4)
        if full < cv.chunks:
            a = w[:, full * LANES :]
            a = jnp.concatenate([a, jnp.zeros((cv.o, LANES - a.shape[1]), F32)], 1)
            turned[full * LANES : (full + 1) * LANES] = chunk(a)
        group = iota((cv.c, LANES), 1) // cv.o
        for kz in range(3):
            for j in range(cv.tiles):
                tile = None
                for g in range(cv.per):
                    u = j * cv.per + g
                    if u < 9:
                        kx, ky = u // 3, u % 3
                        v = turned[pl.ds(9 * kz + 3 * ky + kx, cv.c, stride=27)]
                        tile = v if tile is None else jnp.where(group == g, v, tile)
                own[kz, :, j * LANES : (j + 1) * LANES] = tile.astype(BF16).astype(own.dtype)
        for j in range(cv.tiles):
            v = jnp.concatenate([own[kz, :, j * LANES : (j + 1) * LANES] for kz in range(3)], 0)
            size = min(LANES, cv.taps - j * LANES)
            v = dot_nt(eye, v.astype(BF16))[0:size]
            if k < 2:
                out[j * LANES : j * LANES + size] = v.astype(BF16)
            else:
                k_.flip[j * LANES : j * LANES + size, 0 : 3 * cv.c] = v
        if k >= 2:
            out[0 : 3 * cv.o] = jnp.concatenate(
                [
                    jnp.concatenate(
                        [
                            k_.flip[(3 * kx + ky) * cv.o : (3 * kx + ky + 1) * cv.o, kz * cv.c : (kz + 1) * cv.c]
                            for kx in range(3)
                        ],
                        0,
                    )
                    for kz in range(3)
                    for ky in range(3)
                ],
                1,
            ).astype(BF16)

    def forward_copy(k, t):
        block = wf[k].at[x]
        return peer_copy(
            block, block, k_.p_send.at[k - 2, t], k_.p_recv.at[k - 2, t], place, 2 * lax.rem(x + t, nx) + core
        )

    def forward_start(k):
        for t in range(1, nx):
            launch(None, functools.partial(forward_copy, k, t))

    def forward_wait(k):
        for t in range(1, nx):
            fromx = lax.rem(x + nx - t, nx)
            block = wf[k].at[fromx]
            peer_copy(
                block, block, k_.p_send.at[k - 2, t], k_.p_recv.at[k - 2, t], place, 2 * fromx + core
            ).wait_recv()

    def forward_weight(k):
        return jnp.concatenate([wf[k][i, 0 : 3 * convs[k].o] for i in range(nx)], 0)

    def weights_start(k):
        cv = convs[k]
        for b, (size, start, at) in enumerate(cv.blocks):
            wx[k][me, :, at : at + size] = wt[k][:, pl.ds(start(me), size)]
            for t in range(1, nc):
                to = lax.rem(me + t, nc)

                def copy(to=to, t=t, b=b, size=size, start=start, at=at):
                    return peer_copy(
                        wt[k].at[:, pl.ds(start(to), size)], wx[k].at[me, :, pl.ds(at, size)],
                        k_.w_send.at[k, b, t], k_.w_recv.at[k, b, t], place, to,
                    )

                launch(None, copy)

    def weights_finish(k):
        cv = convs[k]
        for b, (size, _, at) in enumerate(cv.blocks):
            for t in range(1, nc):
                source = lax.rem(me + nc - t, nc)
                theirs = wx[k].at[source, :, pl.ds(at, size)]
                peer_copy(theirs, theirs, k_.w_send.at[k, b, t], k_.w_recv.at[k, b, t], place, source).wait_recv()

        parts = 9 if k < 2 else 3
        lanes = cv.taps // parts
        for i in range(parts):
            at = (parts - 1 - i) * lanes
            found = [wx[k][j, 2 - kz, :, at : at + lanes].astype(F32) for kz in range(3) for j in range(nc)]
            wb[k][i * cv.needed : (i + 1) * cv.needed] = jnp.concatenate(found, 1).astype(BF16)

    def tiles_of(k, part, put):
        cv, dense = convs[k], k_.dense
        rows, size = 3 * cv.c, 3 * cv.o
        for ky in range(3):
            at = ky * LANES + part * size
            dense[0:rows, ky * size : (ky + 1) * size] = acc[0:rows, at : at + size]

        def tile(i, carry):
            left = []
            for kz in range(3):
                at = pl.ds(pl.multiple_of(kz * cv.c + i * 16, 16), 16)
                for j in range(cv.full):
                    put(i * cv.group + kz * cv.full + j, dense[at, j * LANES : (j + 1) * LANES].astype(BF16))
                left.append(dense[at, cv.full * LANES : cv.full * LANES + cv.left * cv.o])
            if cv.left:
                used = 3 * cv.left * cv.o
                v = jnp.concatenate(left + [jnp.zeros((16, LANES - used), F32)], 1)
                put(i * cv.group + 3 * cv.full, v.astype(BF16))
            return carry

        lax.fori_loop(0, cv.c // 16, tile, 0, unroll=2)

    def cross_start(k):
        gs, gx = (k_.gs2, k_.gs3)[k - 2], (k_.gx2, k_.gx3)[k - 2]

        for part in range(nx):

            def put(i, v, part=part):
                gs[part, i] = v

            tiles_of(k, part, put)
        for t in range(1, nx):

            def copy(t=t):
                tox = at_x(t)[0]
                return peer_copy(
                    gs.at[tox], gx.at[x], k_.c_send.at[k - 2, t], k_.c_recv.at[k - 2, t], place, 2 * tox + core
                )

            launch(None, copy)

    def cross_finish(k):
        cv, gs, gx = convs[k], (k_.gs2, k_.gs3)[k - 2], (k_.gx2, k_.gx3)[k - 2]
        sources = [at_x(t)[1] for t in range(1, nx)]
        for t, fromx in enumerate(sources, 1):
            theirs = gx.at[fromx]
            peer_copy(
                theirs, theirs, k_.c_send.at[k - 2, t], k_.c_recv.at[k - 2, t], place, 2 * fromx + core
            ).wait_recv()

        def add(i, carry):
            for j in range(cv.group):
                p = cv.group * i + j
                v = gs[x, p].astype(F32)
                for fromx in sources:
                    v += gx[fromx, p].astype(F32)
                gt[k][p] = v.astype(BF16)
            return carry

        lax.fori_loop(0, cv.c // 16, add, 0, unroll=2)
        reduce_send(k)

    def reduce_start(k):
        def put(i, v):
            gt[k][i] = v

        tiles_of(k, 0, put)
        reduce_send(k)

    nh = nd // 2
    par, rank = lax.rem(place, 2), lax.div(place, 2)
    partner = place + 1 - 2 * par

    def rank_peers(i):
        to = rank + 1 + i
        return 2 * jnp.where(to >= nh, to - nh, to) + par, me

    def half_of(k, which):
        size = nh * convs[k].share
        return pl.ds(which * size, size)

    def share_of(k, owner):
        size = convs[k].share
        if k == 0:
            return pl.ds(owner * size, size)
        return pl.ds((lax.rem(owner, 2) * nh + lax.div(owner, 2)) * size, size)

    def level(k):
        return (nd, slab_peers, place) if k == 0 else (nh, rank_peers, rank)

    def pair_copy(src, dst, k, i):
        return peer_copy(src, dst, k_.q_send.at[k, i], k_.q_recv.at[k, i], partner, me)

    def reduce_send(k):
        cv = convs[k]
        for i in range(cv.count, cv.share * nd):
            gt[k][i] = jnp.zeros((16, LANES), BF16)
        if k == 0:
            spread_shares(k)
        else:
            launch(None, lambda: pair_copy(gt[k].at[half_of(k, 1 - par)], gp[k - 1], k, 0))

    def pair_finish(k):
        pair_copy(gp[k - 1], gp[k - 1], k, 0).wait_recv()
        own = half_of(k, par)
        gt[k][own] = (gt[k][own].astype(F32) + gp[k - 1][...].astype(F32)).astype(BF16)
        spread_shares(k)

    def spread_shares(k):
        n, peers, own = level(k)
        gr[k][own] = gt[k][share_of(k, place)]

        def copy(to, chan):
            return peer_copy(gt[k].at[share_of(k, to)], gr[k].at[own], k_.r_send.at[k], k_.r_recv.at[k], to, chan)

        exchange(n, peers, copy)
        pending.append((None, lambda: reduce_all(k).wait_send()))

    def reduce_all(k):
        every = gr[k].at[pl.ds(0, level(k)[0] - 1)]
        return peer_copy(every, every, k_.r_send.at[k], k_.r_recv.at[k], place, mate)

    def share_all(k):
        every = ga[k].at[pl.ds(0, (level(k)[0] - 1) * convs[k].share)]
        return peer_copy(every, every, k_.a_send.at[k], k_.a_recv.at[k], place, mate)

    def reduce_finish(k):
        reduce_all(k).wait_recv()
        own = share_of(k, place)
        ga[k][own] = jnp.sum(gr[k][...].astype(F32), axis=0).astype(BF16)

        def copy(to, chan):
            return peer_copy(ga[k].at[own], ga[k].at[own], k_.a_send.at[k], k_.a_recv.at[k], to, chan)

        n, peers, _ = level(k)
        exchange(n, peers, copy)
        pending.append((None, lambda: share_all(k).wait_send()))

    def share_pass(k):
        share_all(k).wait_recv()
        own = ga[k].at[half_of(k, par)]
        launch(None, lambda: pair_copy(own, own, k, 1))

    def gradient_out(k):
        cv, out = convs[k], grads[k]
        if k == 0:
            share_all(k).wait_recv()
        else:
            theirs = ga[k].at[half_of(k, 1 - par)]
            pair_copy(theirs, theirs, k, 1).wait_recv()
        group = iota((16, LANES), 1) // cv.o

        def scatter(i, carry):
            def put(v, g, kz, t):
                turned[pl.ds(9 * kz + t + i * (16 * 27), 16, stride=27)] = jnp.where(group == g, v, 0.0)

            for kz in range(3):
                for j in range(cv.full):
                    v = ga[k][i * cv.group + kz * cv.full + j].astype(F32)
                    for g in range(min(cv.per, 9)):
                        put(v, g, kz, j * cv.per + g)
            if cv.left:
                v = ga[k][i * cv.group + 3 * cv.full].astype(F32)
                for kz in range(3):
                    for g in range(cv.left):
                        put(v, kz * cv.left + g, kz, cv.full * cv.per + g)
            return carry

        lax.fori_loop(0, cv.c // 16, scatter, 0, unroll=2)

        pick = (iota((cv.o, LANES), 1) % cv.o == iota((cv.o, LANES), 0)).astype(BF16)
        step = 8 * LANES
        for at in range(0, cv.length, step):
            size = min(step, cv.length - at)
            v = dot_nt(pick, turned[at : at + -(-size // LANES) * LANES].astype(BF16))
            out[:, at : at + size] = v[:, 0:size]

    def column(row):
        n = row.shape[1]
        eye = iota((n, n), 0) == iota((n, n), 1)
        return jnp.sum(jnp.where(eye, row, 0.0), axis=1, keepdims=True)

    def row_of(col):
        n = col.shape[0]
        eye = iota((n, n), 0) == iota((n, n), 1)
        return jnp.sum(jnp.where(eye, col, 0.0), axis=0, keepdims=True)

    def clear_halos(ref):
        def clear(at):
            if len(ref.shape) == 5:
                for c in range(2):
                    ref[c, at] = jnp.zeros(ref.shape[2:], ref.dtype)
            else:
                for i in range(nx):
                    ref[core, i, at] = jnp.zeros(ref.shape[3:], ref.dtype)

        pl.when(first)(lambda: clear(0))
        pl.when(last)(lambda: clear(ref.shape[-4] - 1))

    def clear_rows(ref):
        def clear(at):
            for c in range(2):
                for i in range(S + 2):
                    ref[c, i, at] = jnp.zeros(ref.shape[3:], ref.dtype)

        pl.when(top)(lambda: clear(0))
        pl.when(bottom)(lambda: clear(E - 1))

    def conv(operand, weight, m, groups, emit, init):
        def body(d, carry):
            v = operand(d)
            y = dot(weight, v)
            results = []
            for j in range(RB):
                lanes = slice(j * LANES, (j + 1) * LANES)
                parts = []
                for g in range(groups):
                    a = [y[(3 * g + kx) * m : (3 * g + kx + 1) * m, lanes] for kx in range(3)]
                    parts.append(from_left(a[0], W) + a[1] + from_right(a[2], W))
                results.append(jnp.concatenate(parts, 0) if groups > 1 else parts[0])
            return emit(d, results, carry)

        return lax.fori_loop(0, S, body, init)

    def rows_of(row):
        return lambda d: jnp.concatenate(
            [jnp.concatenate([row(d + kz, ky + j) for j in range(RB)], 1) for kz in range(3) for ky in range(3)], 0
        )

    def blocks_of(ref):
        size = dm.cd
        return lambda d: jnp.concatenate(
            [
                jnp.concatenate([ref[c, d + kz, 2 - ky + j, i * size : (i + 1) * size] for j in range(RB)], 1)
                for kz in range(3)
                for i in range(nx)
                for c in range(2)
                for ky in range(3)
            ],
            0,
        ).astype(BF16)

    def conv_stats(row, weight, z):
        def emit(d, results, carry):
            total, square = carry
            for j, v in enumerate(results):
                z[d * RB + j] = v
                total, square = total + v, square + v * v
            return total, square

        blank = jnp.zeros((dm.cf, LANES), F32)
        return conv(rows_of(row), weight, dm.cd, nx, emit, (blank, blank))

    def weight_grad(row, k):
        cv = convs[k]

        def part(d):
            v = jnp.concatenate([jnp.concatenate([row(d + kz, j) for j in range(E)], 1) for kz in range(3)], 0)
            y = jnp.concatenate(
                [k_.dzt[d, (2 - ky) * LANES : (2 - ky + E) * LANES] for ky in range(3)], 1
            )
            return dot(v, y)

        acc[0 : 3 * cv.c] = part(0)

        def more(d, carry):
            acc[0 : 3 * cv.c] += part(d)
            return carry

        lax.fori_loop(1, S, more, 0)

    def conv_coarse(ref, weight, m):
        v = jnp.concatenate(
            [jnp.concatenate([flat(ref, kz, i) for i in range(Q)], 1) for kz in range(3)], 0
        )
        y = dot(weight[...], v)
        blank = jnp.zeros((m, LANES), F32)

        def shifted(ky, i):
            if not 0 <= i < Q:
                return blank
            a, b, c = (
                y[(3 * kx + ky) * m : (3 * kx + ky + 1) * m, i * LANES : (i + 1) * LANES] for kx in range(3)
            )
            return from_left(a, V) + b + from_right(c, V)

        before = [shifted(0, i) for i in range(-1, Q)]
        after = [shifted(2, i) for i in range(Q + 1)]
        return [
            shifted(1, i) + halves(before[i + 1] + after[i + 1], before[i] + after[i]) for i in range(Q)
        ]

    def conv_stats_coarse(ref, weight, z, m):
        total = square = jnp.zeros((m, LANES), F32)
        for i, v in enumerate(conv_coarse(ref, weight, m)):
            z[i] = v
            total, square = total + v, square + v * v
        return total, square

    def weight_grad_coarse(ref, k):
        cv = convs[k]
        v = jnp.concatenate(
            [jnp.concatenate([flat(ref, kz, i) for i in range(Q)], 1) for kz in range(3)], 0
        )
        y = jnp.concatenate([k_.dzct[(2 - ky) * V : (2 - ky) * V + Q * LANES] for ky in range(3)], 1)
        acc[0 : 3 * cv.c] = dot(v, y)

    def pack(a, b):
        m = a.shape[0]
        a = jnp.sum(a, axis=1, keepdims=True)
        b = jnp.sum(b, axis=1, keepdims=True)
        lane, channel = iota((m, LANES), 1), iota((m, LANES), 0)
        both = jnp.where(lane == channel, a, jnp.where(lane == channel + m, b, 0.0))
        return jnp.sum(both, axis=0, keepdims=True)

    def moments(total, count):
        mean = total[0] / count
        var = total[1] / count - mean * mean
        return mean, lax.rsqrt(var + EPS)

    def wide(column):
        return jnp.broadcast_to(column, (column.shape[0], LANES))

    def factors(stats, norm):
        mean, inv = stats
        gain, shift = norm
        return wide(mean), wide(gain * inv), wide(shift)

    def norm_rows(z, stats, norm, emit, n):
        mean, scale, shift = factors(stats, norm)

        def body(i, carry):
            for j in range(n):
                p = i * n + j
                u = (z[p] - mean) * scale + shift
                emit(p, u * jax.nn.sigmoid(u))
            return carry

        lax.fori_loop(0, z.shape[0] // n, body, 0)

    def norm_back_sums(z, keep_du, stats, norm, grad, n):
        mean, scale, shift = factors(stats, norm)
        inv = wide(stats[1])
        m = z.shape[1]

        def body(i, carry):
            a, b = carry
            for j in range(n):
                p = i * n + j
                centred = z[p] - mean
                u = centred * scale + shift
                sigma = jax.nn.sigmoid(u)
                v = grad(p) * sigma * (1.0 + u * (1.0 - sigma))
                keep_du(p, v)
                a, b = a + v, b + v * (centred * inv)
            return a, b

        blank = jnp.zeros((m, LANES), F32)
        return lax.fori_loop(0, z.shape[0] // n, body, (blank, blank))

    def back_factors(stats, norm, total, count):
        mean, inv = stats
        scale = norm[0] * inv
        return wide(mean), wide(scale), wide(-scale * total[0] / count), wide(-scale * inv * total[1] / count)

    def columns_first(copies, groups):
        size = copies[0].shape[0] // groups
        rows = [v[g * size : (g + 1) * size] for g in range(groups) for v in copies]
        used = 3 * groups * size
        if used < LANES:
            rows.append(jnp.zeros((LANES - used, LANES), F32))
        return jnp.transpose(jnp.concatenate(rows, 0)).astype(BF16)

    def norm_back_fine(z, given, ref):
        mean, scale, level, slope = given

        def body(d, carry):
            for r in range(RB):
                p = d * RB + r
                v = scale * k_.du_f[p] + level + slope * (z[p] - mean)
                ref[core, 1 + d, 1 + r] = v.astype(BF16).astype(ref.dtype)
            return carry

        lax.fori_loop(0, S, body, 0)

    def turn_fine(ref):
        n = 4 if RB % 4 == 0 else 2

        def body(i, carry):
            d = lax.div(i, RB // n)
            r0 = (i - d * (RB // n)) * n
            for j in range(n):
                v = ref[core, 1 + d, 1 + r0 + j].astype(F32)
                at = pl.ds(pl.multiple_of((2 + r0 + j) * LANES, LANES), LANES)
                k_.dzt[d, at] = columns_first((from_right(v, W), v, from_left(v, W)), nx)
            return carry

        lax.fori_loop(0, S * RB // n, body, 0)

    def norm_back_coarse(z, given, ref):
        mean, scale, level, slope = given
        for i in range(Q):
            v = scale * k_.du_c[i] + level + slope * (z[i] - mean)
            ref[core, x, 1, i] = v.astype(BF16).astype(ref.dtype)

    def turn_coarse(ref):
        for i in range(Q):
            v = ref[core, x, 1, i].astype(F32)
            k_.dzct[V + i * LANES : V + (i + 1) * LANES] = columns_first((from_right(v, V), v, from_left(v, V)), 1)

    def keep_du(ref):
        def store(p, v):
            ref[p] = v

        return store

    barrier = pltpu.get_barrier_semaphore()

    def greet(depth, chan):
        pl.semaphore_signal(barrier, inc=1, device_id={"depth": depth, "chan": chan}, device_id_type=MESH)

    exchange(nd * nx, wide_peers, lambda depth, chan: types.SimpleNamespace(start=lambda: greet(depth, chan)))
    for t in range(nx):
        to = 2 * at_x(t)[0] + other
        greet(place, to)
        if t > 0:
            pl.when(no(first))(lambda to=to: greet(place - 1, to))
            pl.when(no(last))(lambda to=to: greet(place + 1, to))

    hc = iota((LANES, LANES), 0)
    fc = iota((LANES, LANES), 1)
    half = LANES // 2

    def up_table(coarse, fine):
        base = fine // 2
        beside = jnp.clip(base + jnp.where(fine % 2 == 0, -1, 1), 0, V - 1)
        near = (coarse == base).astype(F32)
        far = (coarse == beside).astype(F32)
        return (0.75 * near + 0.25 * far).astype(BF16)

    pool = jnp.concatenate([(hc // 2 == fc - at).astype(BF16) for at in (0, half)], 0)
    spread = jnp.concatenate([(hc - at == fc // 2).astype(BF16) for at in (0, half)], 1)
    up = jnp.concatenate([up_table(hc - at, fc) for at in (0, half)], 1)
    down = jnp.concatenate([up_table(fc, hc)] * 2, 0)
    spread2 = jnp.concatenate([spread, spread], 0)

    def take_rows(ref):
        for c in range(ref.shape[0]):
            k_.rows[c * S * R : (c + 1) * S * R] = ref[c].astype(F32).reshape(S * R, LANES)

    def row_of_all(p, chans):
        return k_.rows[pl.ds(p, chans, stride=S * R)]

    xp, xs, own_skip = k_.xp, k_.xs, k_.own_skip
    clear_halos(xp)
    take_rows(k_.skip)
    for i in range(S):
        for r in (0, R + 1):
            own_skip[i, r] = jnp.zeros((dm.cs, LANES), own_skip.dtype)

    def take_skip(i, carry):
        parts = []
        for d in range(S):
            v = [row_of_all(d * R + 4 * i + j, dm.cs).astype(BF16) for j in range(4)]
            for j in range(4):
                own_skip[d, 1 + 4 * i + j] = v[j].astype(own_skip.dtype)
            parts += [jnp.concatenate([v[j], v[2 + j]], 1) for j in range(2)]
        v = dot(jnp.concatenate(parts, 0), pool).reshape(2 * S, dm.cs, LANES)
        xp[core, x, 1, i] = (jnp.sum(v, axis=0) * 0.125).astype(BF16).astype(xp.dtype)
        return carry

    lax.fori_loop(0, Q, take_skip, 0, unroll=3)
    beside = jnp.where(first, 0, 1) + jnp.where(last, 0, 1)
    pl.semaphore_wait(barrier, nd * nx - 1 + nx + (nx - 1) * beside)
    gather_start(xp, "pooled")
    clear_halos(xs)
    xs[core, x, 1 : S + 1] = own_skip[:, pl.ds(row0, E)]
    gather_start(xs, "skip", lambda at, tox: own_skip.at[at, pl.ds(tox * RB, E)])

    gq = dm.g // nc
    columns = dm.enc_all + dm.skip_all
    gate_all, norm_all = k_.gate_all, k_.norm_all
    gate_all[me, :, 0:columns] = k_.gate[...]
    lane = iota((gq, LANES), 1)
    gate_all[me, :, 2 * LANES :] = jnp.where(
        lane == 0, column(k_.vector[0:1]), jnp.where(lane == 1, column(k_.vector[1:2]), 0.0)
    )
    for layer in range(2):
        for part in range(2):
            at = 2 * layer + part
            norm_all[me, at : at + 1, 0 : dm.cd] = k_.dn[part, layer : layer + 1]

    def constants(i, t, source, to):
        ref = (norm_all, gate_all)[i]
        return peer_copy(ref.at[source], ref.at[source], k_.v_send.at[i, t], k_.v_recv.at[i, t], place, to)

    for i in range(2):
        for t in range(1, nc):
            launch(None, functools.partial(constants, i, t, me, lax.rem(me + t, nc)))
    prepare(0)
    xd, xz4, xz3, d1 = k_.xd, k_.xz4, k_.xz3, k_.d1
    for ref in (xd, xz4, xz3):
        clear_rows(ref)
        clear_halos(ref)
    for ref in (k_.xh, k_.xz2, k_.xz1):
        clear_halos(ref)
    for i in range(S):
        for at in (0, (RB + 2) * LANES):
            k_.dzt[i, at : at + 2 * LANES] = jnp.zeros((2 * LANES, LANES), BF16)
        for r in range(3):
            k_.ug[i, r] = jnp.zeros(k_.ug.shape[2:], F32)
            k_.ug[i, RB + 3 + r] = jnp.zeros(k_.ug.shape[2:], F32)
        for r in range(H + 2):
            k_.cb[i, r] = jnp.zeros(k_.cb.shape[2:], F32)

    for at in (0, V + Q * LANES):
        k_.dzct[at : at + V] = jnp.zeros((V, LANES), BF16)

    def norm_of(layer):
        return column(k_.en[0, layer : layer + 1]), column(k_.en[1, layer : layer + 1])

    norm_e1, norm_e2 = norm_of(0), norm_of(1)

    gather_pass(xp, "pooled")
    gather_wait(xp, "pooled")
    coarse_sums(0, conv_stats_coarse(xp, wf[0], k_.z1, dm.ce))
    prepare(1)
    stats_e1 = moments(coarse_totals(0), dm.coarse_total)

    def keep_coarse(ref):
        def store(p, v):
            ref[core, x, 1, p] = v.astype(BF16).astype(ref.dtype)

        return store

    norm_rows(k_.z1, stats_e1, norm_e1, keep_coarse(k_.xh), Q)
    gather_start(k_.xh, "hidden")
    prepare(2)
    forward_start(2)
    gather_pass(k_.xh, "hidden")
    gather_pass(xs, "skip")
    gather_wait(k_.xh, "hidden")
    coarse_sums(1, conv_stats_coarse(k_.xh, wf[1], k_.z2, dm.ce))
    take_rows(k_.cot)

    def take_cot(i, carry):
        for d in range(S):
            for j in range(4):
                v = row_of_all(d * R + 4 * i + j, dm.cd).astype(BF16)
                k_.own_cot[d, 4 * i + j] = v.astype(k_.own_cot.dtype)
        return carry

    lax.fori_loop(0, Q, take_cot, 0)
    k_.cots[x] = k_.own_cot[:, pl.ds(row0, RB)]
    stats_e2 = moments(coarse_totals(1), dm.coarse_total)
    norm_rows(k_.z2, stats_e2, norm_e2, keep_coarse(k_.xc), Q)
    gather_start(k_.xc, "coarse")
    prepare(3)
    for t in range(1, nc):
        for i in range(2):
            source = lax.rem(me + nc - t, nc)
            constants(i, t, source, source).wait_recv()
    gate_full = gate_all[...].reshape(dm.g, 3 * LANES)
    wg = gate_full[:, 0:columns].astype(BF16)
    gbias = gate_full[:, 2 * LANES : 2 * LANES + 1]
    gout = gate_full[:, 2 * LANES + 1 : 2 * LANES + 2]
    k_.gate_t[...] = jnp.transpose(gate_full[:, 0 : 2 * LANES])
    own_rows = [k_.gate_t[pl.ds(pl.multiple_of((2 * i + core) * dm.ce, dm.ce), dm.ce)] for i in range(nx)]
    own_rows += [
        k_.gate_t[pl.ds(pl.multiple_of(dm.enc_all + (2 * i + core) * dm.cs, dm.cs), dm.cs)] for i in range(nx)
    ]
    k_.gate_own[...] = jnp.concatenate(own_rows, 0)

    def norm_fine(layer):
        return tuple(
            jnp.concatenate(
                [column(norm_all[2 * i + core, 2 * layer + part : 2 * layer + part + 1, 0 : dm.cd]) for i in range(nx)], 0
            )
            for part in range(2)
        )

    norm_d1, norm_d2 = norm_fine(0), norm_fine(1)
    gather_pass(k_.xc, "coarse")
    gather_wait(k_.xc, "coarse")
    forward_start(3)

    dt = k_.dt

    def up_depth(i, carry):
        t = []
        for j in range(3):
            v = dot(flat(k_.xc, j, i), up)
            t.append(jnp.stack([v[:, 0:LANES], v[:, LANES:]], 0))
        below = jnp.where(first, t[1], t[0])
        above = jnp.where(last, t[1], t[2])
        near = 0.75 * t[1]
        here = 0.25 * t[1]
        rows = pl.ds(i * 2, 2)
        dt[0, rows] = jnp.where(first, 0.0, 0.75 * below + here)
        dt[1, rows] = near + 0.25 * below
        dt[2, rows] = near + 0.25 * above
        dt[3, rows] = jnp.where(last, 0.0, 0.75 * above + here)
        return carry

    lax.fori_loop(0, Q, up_depth, 0)

    def up_rows(i, carry):
        here = h0 + i
        before, after = jnp.maximum(here - 1, 0), jnp.minimum(here + 1, H - 1)
        for j in range(S + 2):
            v = 0.75 * dt[j, here]
            d1[j, 1 + 2 * i, 0 : dm.enc_all] = (v + 0.25 * dt[j, before]).astype(BF16)
            d1[j, 2 + 2 * i, 0 : dm.enc_all] = (v + 0.25 * dt[j, after]).astype(BF16)
        return carry

    lax.fori_loop(0, RB // 2, up_rows, 0)
    for edge, at, near, far in (
        (top, 0, jnp.maximum(h0 - 1, 0), h0),
        (bottom, E - 1, jnp.minimum(h0 + RB // 2, H - 1), h0 + RB // 2 - 1),
    ):
        for j in range(S + 2):
            v = jnp.where(edge, 0.0, 0.75 * dt[j, near] + 0.25 * dt[j, far])
            d1[j, at, 0 : dm.enc_all] = v.astype(BF16)
    for t in range(1, nx):
        tox = lax.rem(x + t, nx)

        def send_cot(t=t, tox=tox):
            return peer_copy(
                k_.own_cot.at[:, pl.ds(tox * RB, RB)], k_.cots.at[x], k_.o_send.at[0, t], k_.o_recv.at[0, t],
                place, 2 * tox + core,
            )

        launch(None, send_cot)

    gather_wait(xs, "skip")
    gate_n = E // 2

    def gate(i, carry):
        j = lax.div(i, 2)
        r0 = (i - 2 * j) * gate_n
        skips = [flat(xs, j, r0 + q) for q in range(gate_n)]
        v = jnp.concatenate(
            [
                jnp.concatenate([d1[j, r0 + q, 0 : dm.enc_all] for q in range(gate_n)], 1),
                jnp.concatenate(skips, 1),
            ],
            0,
        )
        pre = dot(wg, v) + gbias
        act = pre * jax.nn.sigmoid(pre)
        alpha = jax.nn.sigmoid(jnp.sum(gout * act, axis=0, keepdims=True))
        for q in range(gate_n):
            lanes = slice(q * LANES, (q + 1) * LANES)
            d1[j, r0 + q, dm.enc_all :] = (alpha[:, lanes] * skips[q].astype(F32)).astype(BF16)
            k_.pre[j, r0 + q] = pre[:, lanes]
            k_.alpha[j, r0 + q] = alpha[:, lanes]
        return carry

    lax.fori_loop(0, (S + 2) * 2, gate, 0)
    def row_d1(j, r):
        return d1[j, r]

    def row_xd(j, r):
        return natural(xd, j, r)

    forward_wait(2)
    fine_sums(0, conv_stats(row_d1, forward_weight(2), k_.z3))
    forward_wait(3)
    stats_d1 = moments(fine_totals(0), dm.fine_total)

    def keep_dec(p, v):
        d = lax.div(p, RB)
        xd[core, 1 + d, 1 + p - d * RB] = v.astype(BF16).astype(xd.dtype)

    norm_rows(k_.z3, stats_d1, norm_d1, keep_dec, RB)
    fine_start(xd, "hidden")
    weights_start(3)
    weights_start(2)
    for t in range(1, nx):
        fromx = lax.rem(x + nx - t, nx)
        theirs = k_.cots.at[fromx]
        peer_copy(theirs, theirs, k_.o_send.at[0, t], k_.o_recv.at[0, t], place, 2 * fromx + core).wait_recv()
    fine_pass(xd, "hidden")
    fine_wait(xd, "hidden")
    fine_sums(1, conv_stats(row_xd, forward_weight(3), k_.z4))
    stats_d2 = moments(fine_totals(1), dm.fine_total)

    def rows_out(ref, own, theirs, kind, size):
        def copy_rows(read, at):
            def body(d, carry):
                for r in range(RB):
                    p = (d * R + at * RB + r) * size
                    ref[pl.ds(pl.multiple_of(p, size), size)] = read(d * RB + r).astype(F32)
                return carry

            lax.fori_loop(0, S, body, 0)

        copy_rows(lambda p: own[x, p], x)
        for t in range(1, nx):
            fromx = lax.rem(x + nx - t, nx)
            block = theirs.at[fromx]
            peer_copy(block, block, k_.o_send.at[kind, t], k_.o_recv.at[kind, t], place, 2 * fromx + core).wait_recv()
            copy_rows(lambda p, fromx=fromx: theirs[fromx, p], fromx)

    def row_cot(p):
        d = lax.div(p, RB)
        return jnp.concatenate([k_.cots[i, d, p - d * RB] for i in range(nx)], 0).astype(F32)

    fine_sums(2, norm_back_sums(k_.z4, keep_du(k_.du_f), stats_d2, norm_d2, row_cot, RB))

    def keep_result(p, v):
        for i in range(nx):
            k_.ob[i, p] = v[i * dm.cd : (i + 1) * dm.cd].astype(BF16).astype(k_.ob.dtype)

    norm_rows(k_.z4, stats_d2, norm_d2, keep_result, RB)
    total_d2 = fine_totals(2)
    norm_back_fine(k_.z4, back_factors(stats_d2, norm_d2, total_d2, dm.fine_total), xz4)
    fine_start(xz4, "dz4")
    weights_start(1)
    weights_start(0)
    for t in range(1, nx):
        tox = lax.rem(x + t, nx)

        def send_result(t=t, tox=tox):
            return peer_copy(
                k_.ob.at[tox], k_.oi.at[x], k_.o_send.at[1, t], k_.o_recv.at[1, t], place, 2 * tox + core
            )

        launch(None, send_result)
    turn_fine(xz4)
    weight_grad(row_xd, 3)
    fine_pass(xz4, "dz4")
    cross_start(3)
    weights_finish(3)
    fine_wait(xz4, "dz4")

    def keep_grad(d, results, carry):
        for j, v in enumerate(results):
            k_.gg[d * RB + j] = v
        return carry

    conv(blocks_of(xz4), wb[3][...], dm.cf, 1, keep_grad, 0)
    fine_sums(3, norm_back_sums(k_.z3, keep_du(k_.du_f), stats_d1, norm_d1, lambda p: k_.gg[p], RB))
    cross_finish(3)
    total_d1 = fine_totals(3)
    norm_back_fine(k_.z3, back_factors(stats_d1, norm_d1, total_d1, dm.fine_total), xz3)
    fine_start(xz3, "dz3")
    turn_fine(xz3)
    weights_finish(2)
    weight_grad(row_d1, 2)
    fine_pass(xz3, "dz3")
    cross_start(2)
    pair_finish(3)
    rows_out(k_.out, k_.ob, k_.oi, 1, dm.cd)
    fine_wait(xz3, "dz3")

    ups = nx * dm.ce

    def gate_back(d, results, carry):
        bias, psi = carry
        lows = []
        for j, both in enumerate(results):
            p = d * RB + j
            v = both[ups:]
            grad = jnp.sum(v * flat(xs, d + 1, 1 + j).astype(F32), axis=0, keepdims=True)
            alpha = k_.alpha[d + 1, 1 + j]
            logit = grad * alpha * (1.0 - alpha)
            pre = k_.pre[d + 1, 1 + j]
            sigma = jax.nn.sigmoid(pre)
            psi = psi + pre * sigma * logit
            low = (logit * gout * sigma * (1.0 + pre * (1.0 - sigma))).astype(BF16)
            bias = bias + low.astype(F32)
            k_.pg[p] = low
            lows.append(low)
            k_.ug[d, 3 + j] = both[0:ups]
            for i in range(nc):
                k_.gv[i] = v[i * dm.cs : (i + 1) * dm.cs]
            for i in range(nx):
                k_.sgp[i, p] = alpha * k_.gv[2 * i + core]
        back = dot(k_.gate_own[...].astype(BF16), jnp.concatenate(lows, 1))
        for j in range(len(results)):
            p = d * RB + j
            lanes = slice(j * LANES, (j + 1) * LANES)
            k_.ug[d, 3 + j] += back[0:ups, lanes]
            for i in range(nx):
                v = k_.sgp[i, p] + back[ups + i * dm.cs : ups + (i + 1) * dm.cs, lanes]
                k_.sgp[i, p] = v
                k_.sgb[i, p] = v.astype(BF16).astype(k_.sgb.dtype)
        return bias, psi

    blank = jnp.zeros((dm.g, LANES), F32)
    bias, psi = conv(blocks_of(xz3), wb[2][...], ups + dm.skip_all, 1, gate_back, (blank, blank))

    ug, cb, cg = k_.ug, k_.cb, k_.cg
    for q in range(RB // 2 + 2):
        terms = []
        for d in range(S):
            v = 0.75 * (ug[d, 2 * q + 1] + ug[d, 2 * q + 2]) + 0.25 * (ug[d, 2 * q + 3] + ug[d, 2 * q])
            if q == 1:
                v += jnp.where(top, 0.25 * ug[d, 3], 0.0)
            if q == RB // 2:
                v += jnp.where(bottom, 0.25 * ug[d, RB + 2], 0.0)
            terms.append(split(v))
        v = dot(jnp.concatenate(terms, 0), down)
        for d in range(S):
            cb[d, h0 + q] = v[d * ups : (d + 1) * ups]

    def to_slabs(i, carry):
        even, odd = (cb[d, 2 * i + 1] + pltpu.roll(cb[d, 2 * i + 2], half, 1) for d in range(S))
        middle = 0.75 * (even + odd) + jnp.where(first, 0.25 * even, 0.0) + jnp.where(last, 0.25 * odd, 0.0)
        for part, v in enumerate((0.25 * even, middle, 0.25 * odd)):
            for j in range(nx):
                block = v[j * dm.ce : (j + 1) * dm.ce]
                k_.fs[part, j, i] = block.astype(BF16).astype(k_.fs.dtype)
                if part == 1:
                    k_.fm[j, i] = block
        return carry

    lax.fori_loop(0, Q, to_slabs, 0)

    reach = min((RB // 2 + 1) // 2 + 1, Q)

    def reach_of(at):
        return pl.ds(jnp.clip(lax.div(at * (RB // 2) + 1, 2) - 1, 0, Q - reach), reach)

    def fold_parts():
        for step in (-1, 1, 0):
            sends = (no(first), None, no(last))[step + 1]
            gets = (no(last), None, no(first))[step + 1]
            for t in range(nx):
                if (step, t) != (0, 0):
                    tox, fromx = lax.rem(x + t, nx), lax.rem(x + nx - t, nx)
                    sems = (k_.f_send.at[step + 1, t], k_.f_recv.at[step + 1, t])
                    rows = reach_of(x)
                    theirs = k_.fr.at[step + 1, fromx, reach_of(fromx)]
                    yield (
                        sends, gets, fromx, step + 1,
                        functools.partial(
                            peer_copy, k_.fs.at[step + 1, tox, rows], k_.fr.at[step + 1, x, rows], *sems,
                            place + step, 2 * tox + core,
                        ),
                        functools.partial(peer_copy, theirs, theirs, *sems, place, 2 * fromx + core),
                    )

    for sends, _, _, _, out, _ in fold_parts():
        launch(sends, out)
    for t in range(1, nx):
        tox = lax.rem(x + t, nx)

        def send_skip(t=t, tox=tox):
            return peer_copy(
                k_.sgb.at[tox], k_.sgi.at[x], k_.o_send.at[2, t], k_.o_recv.at[2, t], place, 2 * tox + core
            )

        launch(None, send_skip)

    reduce_finish(3)
    cross_finish(2)

    k_.gw[...] = jnp.zeros(k_.gw.shape, F32)

    def gate_weight(d, carry):
        v = jnp.concatenate(
            [
                jnp.concatenate([d1[1 + d, 1 + j, 0 : dm.enc_all] for j in range(RB)], 1),
                jnp.concatenate([flat(xs, 1 + d, 1 + j) for j in range(RB)], 1),
            ],
            0,
        )
        y = jnp.concatenate([k_.pg[d * RB + j] for j in range(RB)], 1)
        k_.gw[0:columns, 0 : dm.g] += dot_nt(v, y)
        return carry

    lax.fori_loop(0, S, gate_weight, 0)
    gate_grad = jnp.transpose(k_.gw[...])
    lane = iota((dm.g, LANES), 1)
    vectors = jnp.where(
        lane == 0,
        jnp.sum(bias, axis=1, keepdims=True),
        jnp.where(lane == 1, jnp.sum(psi, axis=1, keepdims=True), 0.0),
    )
    gate_block = k_.gate_block
    for j in range(nc):
        mine = slice(j * gq, (j + 1) * gq)
        gate_block[j, :, 0 : 2 * LANES] = gate_grad[mine]
        gate_block[j, :, 2 * LANES :] = vectors[mine]
    sum_start(everyone, k_.sv, 4, 0, gate_block[me], lambda chan: gate_block.at[chan])
    cg[...] = k_.fm[x]
    for _, gets, fromx, part, _, back in fold_parts():

        def fold_in(back=back, part=part, fromx=fromx):
            back().wait_recv()
            rows = reach_of(fromx)
            cg[rows] += k_.fr[part, fromx, rows].astype(F32)

        guarded(gets, fold_in)

    coarse_sums(2, norm_back_sums(k_.z2, keep_du(k_.du_c), stats_e2, norm_e2, lambda p: cg[p], Q))
    pair_finish(2)
    share_pass(3)
    weights_finish(1)
    total_e2 = coarse_totals(2)
    norm_back_coarse(k_.z2, back_factors(stats_e2, norm_e2, total_e2, dm.coarse_total), k_.xz2)
    gather_start(k_.xz2, "dz2")
    turn_coarse(k_.xz2)
    weight_grad_coarse(k_.xh, 1)
    gather_pass(k_.xz2, "dz2")
    reduce_start(1)
    weights_finish(0)
    reduce_finish(2)
    rows_out(k_.sg, k_.sgp, k_.sgi, 2, dm.cs)
    gather_wait(k_.xz2, "dz2")
    for i, v in enumerate(conv_coarse(k_.xz2, wb[1], dm.ce)):
        cg[i] = v
    coarse_sums(3, norm_back_sums(k_.z1, keep_du(k_.du_c), stats_e1, norm_e1, lambda p: cg[p], Q))
    pair_finish(1)
    share_pass(2)
    gradient_out(3)
    total_e1 = coarse_totals(3)
    norm_back_coarse(k_.z1, back_factors(stats_e1, norm_e1, total_e1, dm.coarse_total), k_.xz1)
    gather_start(k_.xz1, "dz1")
    turn_coarse(k_.xz1)
    weight_grad_coarse(xp, 0)
    reduce_start(0)
    reduce_finish(1)
    gather_pass(k_.xz1, "dz1")
    gradient_out(2)

    share_pass(1)
    reduce_finish(0)
    gather_wait(k_.xz1, "dz1")
    for i, v in enumerate(conv_coarse(k_.xz1, wb[0], dm.cs)):
        v = dot(split(v), spread2) * 0.125
        for j in range(4):
            part = v[:, (j // 2) * LANES : (j // 2 + 1) * LANES]
            for d in range(S):
                at = (d * R + 4 * i + j) * dm.cs
                k_.sg[at : at + dm.cs] += part
    gradient_out(1)
    gate_total = sum_finish(everyone, k_.sv, 4, 0)
    k_.ggate[...] = gate_total[:, 0:columns]
    k_.gvector[0:1] = row_of(gate_total[:, 2 * LANES : 2 * LANES + 1])
    k_.gvector[1:2] = row_of(gate_total[:, 2 * LANES + 1 : 2 * LANES + 2])

    def own_part(col):
        parts = [jnp.where(x == i, col[i * dm.cd : (i + 1) * dm.cd], 0.0) for i in range(nx)]
        return functools.reduce(jnp.add, parts)

    for ref, pair, pick in ((k_.gen, (total_e1, total_e2), lambda v: v), (k_.gdn, (total_d1, total_d2), own_part)):
        for layer, total in enumerate(pair):
            ref[0, layer : layer + 1] = row_of(pick(total[1]))
            ref[1, layer : layer + 1] = row_of(pick(total[0]))
    gradient_out(0)
    drain()


def adamw(weight, grad, moment, square, rate):
    new_moment = 0.9 * moment + 0.1 * grad
    new_square = 0.999 * square + 0.001 * grad * grad
    moment_hat = new_moment / (1.0 - 0.9**STEP)
    square_hat = new_square / (1.0 - 0.999**STEP)
    new_weight = weight - rate * (moment_hat / (jnp.sqrt(square_hat) + 1e-08) + 0.01 * weight)
    return (new_weight, new_moment, new_square)


RATES = (CONV_RATE, CONV_RATE, GATE_RATE, VECTOR_RATE, CONV_RATE, CONV_RATE, VECTOR_RATE, VECTOR_RATE)


def update_kernel(*refs):
    n = len(RATES)
    sources, targets = refs[: 2 + 4 * n], refs[2 + 4 * n : 4 + 7 * n]
    inside, outside = refs[4 + 7 * n : 6 + 11 * n], refs[6 + 11 * n : 8 + 14 * n]
    in_sem, out_sem = refs[8 + 14 * n :]
    order = (4, 1, 0, 5, 2, 3, 6, 7)

    def load(i):
        return pltpu.make_async_copy(sources[i], inside[i], in_sem.at[i])

    def store(i):
        return pltpu.make_async_copy(outside[i], targets[i], out_sem.at[i])

    for i in (1, 0):
        load(i).start()
    for k in order:
        for part in range(4):
            load(2 + part * n + k).start()
    for i in (1, 0):
        load(i).wait()
        chans, (slabs, rows) = outside[i].shape[0], outside[i].shape[1:3]
        for c in range(chans):
            v = inside[i][pl.ds(c, slabs * rows, stride=chans)]
            outside[i][c] = v.reshape(slabs, rows, LANES).astype(outside[i].dtype)
        store(i).start()
    for k in order:
        own = [2 + part * n + k for part in range(4)]
        for i in own:
            load(i).wait()
        rows = inside[own[0]].shape[0]
        step = 8 if rows % 8 == 0 and rows > 8 else rows
        for r in range(0, rows, step):
            at = slice(r, r + step)
            new = adamw(*(inside[i][at] for i in own), RATES[k])
            for part, value in enumerate(new):
                outside[2 + 3 * k + part][at] = value
        for part in range(3):
            store(2 + 3 * k + part).start()
    for i in range(len(targets)):
        store(i).wait()


def per_device(
    skip, cotangent, enc_conv1, enc_conv2, gate_proj, gate_vector, dec_conv1, dec_conv2, enc_norms, dec_norms, *states
):
    nd, nc = lax.axis_size("depth"), lax.axis_size("chan")
    dm = Dims(nd, nc, skip.shape, enc_conv1.shape[0], dec_conv1.shape[0], gate_proj.shape[0] * nc)
    S, R, H, nx, RB, E = dm.s, dm.rows, dm.half, dm.nx, dm.rb, dm.ext
    Q = H // 2
    cin3 = dm.enc_all + dm.skip_all

    def own_block(size):
        return (size, lambda j: pl.multiple_of(j * size, size), 0)

    def core_blocks(size):
        return tuple(
            (size, lambda j, i=i: pl.multiple_of((2 * i + lax.rem(j, 2)) * size, size), i * size) for i in range(nx)
        )

    dm.convs = convs = (
        Conv(dm, dm.ce, dm.skip_all, (own_block(dm.cs),)),
        Conv(dm, dm.ce, dm.enc_all, (own_block(dm.ce),)),
        Conv(dm, dm.cd, cin3, core_blocks(dm.ce) + ((dm.skip_all, lambda j: dm.enc_all, nx * dm.ce),)),
        Conv(dm, dm.cd, dm.dec_all, core_blocks(dm.cd)),
    )
    params = (enc_conv1, enc_conv2, gate_proj, gate_vector, dec_conv1, dec_conv2, enc_norms, dec_norms)
    inputs = dict(
        skip=skip, cot=cotangent, w0=enc_conv1, w1=enc_conv2, w2=dec_conv1, w3=dec_conv2,
        gate=gate_proj, vector=gate_vector, en=enc_norms, dn=dec_norms,
    )
    shape = jax.ShapeDtypeStruct
    outs = dict(
        out=shape((S * R * dm.cd, LANES), F32),
        sg=shape((S * R * dm.cs, LANES), F32),
        **{f"g{i}": shape(a.shape, F32) for i, a in enumerate((enc_conv1, enc_conv2, dec_conv1, dec_conv2))},
        **{
            name: shape(a.shape, F32)
            for name, a in (("ggate", gate_proj), ("gvector", gate_vector), ("gen", enc_norms), ("gdn", dec_norms))
        },
    )
    gq = dm.g // nc

    def coarse(block):
        return pltpu.VMEM((2, nx, 3, Q, block, LANES), storage(block))

    def fine():
        return pltpu.VMEM((2, S + 2, E, dm.cf, LANES), storage(dm.cd))

    def f32(*dims):
        return pltpu.VMEM((*dims, LANES), F32)

    def tiles(*dims):
        return pltpu.VMEM((*dims, 16, LANES), BF16)

    def blocks(block, *dims):
        return pltpu.VMEM((*dims, block, LANES), storage(block))

    def sems(*dims):
        return pltpu.SemaphoreType.DMA(dims)

    scratch = dict(
        xp=coarse(dm.cs), xh=coarse(dm.ce), xc=coarse(dm.ce), xz2=coarse(dm.ce), xz1=coarse(dm.ce),
        own_skip=blocks(dm.cs, S, R + 2), xs=blocks(dm.cs, 2, nx, S + 2, E),
        own_cot=blocks(dm.cd, S, R), cots=blocks(dm.cd, nx, S, RB),
        d1=pltpu.VMEM((S + 2, E, cin3, LANES), BF16), xd=fine(), xz4=fine(), xz3=fine(),
        z1=f32(Q, dm.ce), z2=f32(Q, dm.ce), z3=f32(S * RB, dm.cf), z4=f32(S * RB, dm.cf),
        du_c=f32(Q, dm.ce), du_f=f32(S * RB, dm.cf), gg=f32(S * RB, dm.cf), cg=f32(Q, dm.ce),
        pre=f32(S + 2, E, dm.g), alpha=f32(S + 2, E, 1), pg=pltpu.VMEM((S * RB, dm.g, LANES), BF16),
        ug=f32(S, RB + 6, nx * dm.ce), cb=f32(S, H + 2, nx * dm.ce), dt=f32(S + 2, H, dm.enc_all),
        gv=f32(nc, dm.cs), sgp=f32(nx, S * RB, dm.cs), sgb=blocks(dm.cs, nx, S * RB), sgi=blocks(dm.cs, nx, S * RB),
        ob=blocks(dm.cd, nx, S * RB), oi=blocks(dm.cd, nx, S * RB),
        dzt=pltpu.VMEM((S, (RB + 4) * LANES, LANES), BF16), dzct=pltpu.VMEM((Q * LANES + 2 * dm.hcols, LANES), BF16),
        gw=f32(2 * LANES), dense=pltpu.VMEM((max(3 * cv.c for cv in convs), 3 * LANES), F32),
        fs=blocks(dm.ce, 3, nx, Q), fr=blocks(dm.ce, 3, nx, Q), fm=f32(nx, Q, dm.ce),
        st=f32(4, nd, 1), su=f32(4, nd * nx, 1), sv=pltpu.VMEM((1, nd * nx, gq, 3 * LANES), F32),
        norm_all=f32(nc, 8), rows=f32(max(dm.cs, dm.cd) * S * R),
        turned=f32(max(cv.chunks for cv in convs) * LANES),
        acc=pltpu.VMEM((max(3 * cv.c for cv in convs), 3 * LANES), F32),
        gate_all=pltpu.VMEM((nc, gq, 3 * LANES), F32), gate_t=pltpu.VMEM((2 * LANES, dm.g), F32),
        gate_own=pltpu.VMEM((nx * (dm.ce + dm.cs), dm.g), F32), gate_block=pltpu.VMEM((nc, gq, 3 * LANES), F32),
        **{f"wt{i}": pltpu.VMEM((3, cv.c, cv.wide), cv.kind) for i, cv in enumerate(convs)},
        **{
            f"wf{i}": pltpu.VMEM((cv.taps, 3 * cv.c) if i < 2 else (nx, cv.stored, 9 * cv.c), BF16)
            for i, cv in enumerate(convs)
        },
        **{f"wx{i}": pltpu.VMEM((nc, 3, cv.needed, cv.wide), cv.kind) for i, cv in enumerate(convs)},
        **{
            f"wb{i}": pltpu.VMEM((9 * cv.needed, 3 * nc * cv.o) if i < 2 else (3 * cv.needed, 9 * nc * cv.o), BF16)
            for i, cv in enumerate(convs)
        },
        flip=pltpu.VMEM((max(cv.tiles for cv in convs[2:]) * LANES, max(3 * cv.c for cv in convs[2:])), F32),
        **{f"gt{i}": tiles(cv.share * nd) for i, cv in enumerate(convs)},
        **{f"gr{i}": tiles(nd if i == 0 else nd // 2, cv.share) for i, cv in enumerate(convs)},
        **{f"gp{i}": tiles(nd // 2 * cv.share) for i, cv in enumerate(convs) if i > 0},
        **{f"ga{i}": tiles(cv.share * nd) for i, cv in enumerate(convs)},
        **{f"gs{i}": tiles(nx, convs[i].count) for i in (2, 3)},
        **{f"gx{i}": tiles(nx, convs[i].count) for i in (2, 3)},
        g_send=sems(len(GATHERS), 3, nx), g_recv=sems(len(GATHERS), 3),
        h_send=sems(len(GATHERS), 2 + nx), h_recv=sems(len(GATHERS)),
        x_send=sems(len(FINE), 3, 5), x_recv=sems(len(FINE), 3, 5),
        y_send=sems(len(FINE), 3), y_recv=sems(len(FINE), 3),
        t_send=sems(4), t_recv=sems(4), u_send=sems(5), u_recv=sems(5),
        f_send=sems(3, nx), f_recv=sems(3, nx), w_send=sems(4, nx + 1, nc), w_recv=sems(4, nx + 1, nc),
        p_send=sems(2, nx), p_recv=sems(2, nx), c_send=sems(2, nx), c_recv=sems(2, nx),
        o_send=sems(3, nx), o_recv=sems(3, nx), v_send=sems(2, nc), v_recv=sems(2, nc),
        r_send=sems(4), r_recv=sems(4), a_send=sems(4), a_recv=sems(4), q_send=sems(4, 2), q_recv=sems(4, 2),
    )
    vmem = pl.BlockSpec(memory_space=pltpu.VMEM)
    out, sg, grad1, grad2, grad3, grad4, ggate, gvector, gen, gdn = pl.pallas_call(
        functools.partial(kernel, dm, (*inputs, *outs, *scratch)),
        out_shape=tuple(outs.values()),
        in_specs=[vmem] * len(inputs),
        out_specs=[vmem] * len(outs),
        scratch_shapes=list(scratch.values()),
        compiler_params=pltpu.CompilerParams(
            has_side_effects=True, collective_id=0, vmem_limit_bytes=60 * 1024 * 1024
        ),
        name="step",
    )(*inputs.values())
    grads = (grad1, grad2, ggate, gvector, grad3, grad4, gen, gdn)
    operands = (out, sg, *params, *grads, *states)
    updated = (
        shape(cotangent.shape, BF16),
        shape(skip.shape, F32),
        *(shape(p.shape, F32) for p in params for _ in range(3)),
    )
    anywhere = pl.BlockSpec(memory_space=pl.ANY)
    return pl.pallas_call(
        update_kernel,
        out_shape=updated,
        in_specs=[anywhere] * len(operands),
        out_specs=[anywhere] * len(updated),
        scratch_shapes=[
            *(pltpu.VMEM(a.shape, a.dtype) for a in operands),
            *(pltpu.VMEM(a.shape, a.dtype) for a in updated),
            pltpu.SemaphoreType.DMA((len(operands),)),
            pltpu.SemaphoreType.DMA((len(updated),)),
        ],
        compiler_params=pltpu.CompilerParams(vmem_limit_bytes=60 * 1024 * 1024),
        name="update",
    )(*operands)


def solution(mesh):
    volume = P("chan", "depth", None, None)
    row, column, norms = P("chan", None), P(None, "chan"), P(None, None, "chan")
    params = (row, row, row, column, row, row, norms, norms)
    return jax.shard_map(
        per_device,
        mesh=mesh,
        in_specs=(volume, volume) + params * 3,
        out_specs=(volume, volume) + tuple(spec for spec in params for _ in range(3)),
        check_vma=False,
    )
```

```python
import functools
import types

import jax
import jax.numpy as jnp
from jax import lax
from jax.experimental import pallas as pl
from jax.experimental.pallas import tpu as pltpu
from jax.sharding import PartitionSpec as P

STEP = 5
EPS = 1e-05
CONV_RATE = 0.03
GATE_RATE = 0.1
VECTOR_RATE = 0.5
LANES = 128
MESH = pl.DeviceIdType.MESH
F32 = jnp.float32
BF16 = jnp.bfloat16


def iota(shape, dim):
    return lax.broadcasted_iota(jnp.int32, shape, dim)


def dot(a, b):
    return jnp.dot(a, b, preferred_element_type=F32)


def dot_nt(a, b):
    return lax.dot_general(a, b, (((1,), (1,)), ((), ())), preferred_element_type=F32)


def dot_tn(a, b):
    return lax.dot_general(a, b, (((0,), (0,)), ((), ())), preferred_element_type=F32)


def sigmoid(v):
    return 0.5 * jnp.tanh(0.5 * v) + 0.5


def from_left(v, width):
    return jnp.where(iota(v.shape, 1) % width == 0, 0.0, pltpu.roll(v, 1, 1))


def from_right(v, width):
    return jnp.where(iota(v.shape, 1) % width == width - 1, 0.0, pltpu.roll(v, LANES - 1, 1))


def halves(low, high):
    return pltpu.roll(jnp.where(iota(low.shape, 1) < LANES // 2, low, high), LANES // 2, 1)


def split(v):
    high = v.astype(BF16)
    return jnp.concatenate([high, (v - high.astype(F32)).astype(BF16)], 1)


def storage(block):
    return BF16 if block % 16 == 0 else F32


def flat(ref, s, r):
    if len(ref.shape) == 4:
        return ref[s, r]
    v = ref[:, :, s, r]
    return jnp.concatenate([v[c, i] for i in range(v.shape[1]) for c in range(2)], 0).astype(BF16)


class Dims:
    def __init__(self, nd, nc, skip, enc, dec, gate):
        self.nd, self.nc, self.nx = nd, nc, nc // 2
        self.s, self.rows, self.cols = skip[1:]
        self.cs, self.ce, self.cd, self.g = skip[0], enc, dec, gate
        self.half, self.hcols = self.rows // 2, self.cols // 2
        self.fine_total = nd * self.s * self.rows * self.cols
        self.coarse_total = self.fine_total // 8
        self.enc_all = nc * enc
        self.skip_all = nc * skip[0]
        self.dec_all = nc * dec
        self.rb = self.rows // self.nx
        self.ext = self.rb + 2
        self.cf = self.nx * dec


GATHERS = ("pooled", "skip", "hidden", "coarse", "dz2", "dz1")
FINE = ("hidden", "dz4", "dz3")


class Conv:
    def __init__(self, dm, o, c, blocks):
        self.o, self.c, self.blocks = o, c, blocks
        self.length = 27 * c
        self.chunks = -(-self.length // LANES)
        self.per = LANES // o
        self.tiles = -(-9 // self.per)
        self.wide = self.tiles * LANES
        self.kind = storage(min(size for size, _, _ in blocks))
        self.needed = sum(size for size, _, _ in blocks)
        self.full = max(1, 9 // self.per)
        self.left = max(0, 9 - self.full * self.per)
        self.group = 3 * self.full + (self.left > 0)
        self.count = c // 16 * self.group
        self.share = -(-self.count // dm.nd)
        self.taps = 9 * o
        self.stored = -(-3 * o // 16) * 16


def kernel(dm, names, *refs):
    k_ = types.SimpleNamespace(**dict(zip(names, refs)))
    nd, nc, nx, S, R, H = dm.nd, dm.nc, dm.nx, dm.s, dm.rows, dm.half
    W, V = dm.cols, dm.hcols
    Q, RB, E = H // 2, dm.rb, dm.ext
    place = lax.axis_index("depth")
    me = lax.axis_index("chan")
    x, core = lax.div(me, 2), lax.rem(me, 2)
    other = 1 - core
    mate = 2 * x + other
    row0, h0 = x * RB, x * (RB // 2)
    first, last = place == 0, place == nd - 1
    top, bottom = x == 0, x == nx - 1
    convs = dm.convs
    pending = []
    wt, wf, wx, wb = ([getattr(k_, f"{kind}{i}") for i in range(4)] for kind in ("wt", "wf", "wx", "wb"))
    gp = (k_.gp1, k_.gp2, k_.gp3)
    gt, gr, ga = ([getattr(k_, f"{kind}{i}") for i in range(4)] for kind in ("gt", "gr", "ga"))
    weights = (k_.w0, k_.w1, k_.w2, k_.w3)
    grads = (k_.g0, k_.g1, k_.g2, k_.g3)
    turned, acc = k_.turned, k_.acc

    def no(cond):
        return jnp.logical_not(cond)

    def peer_copy(src, dst, send, recv, depth, chan):
        return pltpu.make_async_remote_copy(
            src_ref=src, dst_ref=dst, send_sem=send, recv_sem=recv,
            device_id={"depth": depth, "chan": chan}, device_id_type=MESH,
        )

    def guarded(cond, fn):
        if cond is None:
            fn()
        else:
            pl.when(cond)(fn)

    def drain(count=None):
        for cond, fn in pending[:count]:
            guarded(cond, fn)
        del pending[:count]

    def launch(cond, copy):
        guarded(cond, lambda: copy().start())
        pending.append((cond, lambda: copy().wait_send()))

    def arrive(cond, copy):
        guarded(cond, lambda: copy().wait_recv())

    def both(a, b):
        return b if a is None else a if b is None else jnp.logical_and(a, b)

    can_send = (no(last), None, no(first))
    can_recv = (no(first), None, no(last))

    def slices(side, n):
        return (pl.ds(n, 1), pl.ds(1, n), pl.ds(1, 1))[side], (pl.ds(0, 1), pl.ds(1, n), pl.ds(n + 1, 1))[side]

    def at_x(t):
        up, down = x + t, x - t
        return jnp.where(up >= nx, up - nx, up), jnp.where(down < 0, down + nx, down)


    def gather_start(ref, which, source_at=None):
        n = ref.shape[2] - 2
        k = GATHERS.index(which)
        for side in (0, 2, 1):
            own, theirs = slices(side, n)
            for t in range(nx):
                if side == 1 and t == 0:
                    continue
                tox = at_x(t)[0]

                def copy(side=side, t=t, own=own, theirs=theirs, tox=tox):
                    start = (n, 1, 1)[side] - 1
                    size = (1, n, 1)[side]
                    src = ref.at[core, x, own] if source_at is None else source_at(pl.ds(start, size), tox)
                    return peer_copy(
                        src, ref.at[core, x, theirs], k_.g_send.at[k, side, t], k_.g_recv.at[k, side],
                        place + 1 - side, 2 * tox + core,
                    )

                launch(can_send[side], copy)
        gather_own(ref, which)

    def handed(ref, k, piece, i):
        return peer_copy(piece, piece, k_.h_send.at[k, i], k_.h_recv.at[k], place, mate)

    def gather_own(ref, which):
        k = GATHERS.index(which)
        launch(None, lambda: handed(ref, k, ref.at[core, x, pl.ds(1, ref.shape[2] - 2)], 0))

    def gather_pass(ref, which):
        n = ref.shape[2] - 2
        k = GATHERS.index(which)
        for side in (1, 0, 2):
            theirs = slices(side, n)[1]
            if side != 1:
                pieces = [ref.at[core, :, theirs]]
            else:
                pieces = [ref.at[core, at_x(t)[1], theirs] for t in range(1, nx)]
            for i, got in enumerate(pieces):
                arrive(
                    can_recv[side],
                    lambda got=got, side=side: peer_copy(
                        got, got, k_.g_send.at[k, side, 0], k_.g_recv.at[k, side], place, mate
                    ),
                )
                launch(None, lambda got=got, i=i, side=side: handed(ref, k, got, 1 + (side // 2 if side != 1 else 2 + i)))

    def gather_wait(ref, which):
        handed(ref, GATHERS.index(which), ref.at[other], 0).wait_recv()

    def fine_parts(ref, which, side):
        k = FINE.index(which)
        own, theirs = slices(side, S)
        inner = pl.ds(1, RB)
        rows = [(None, None, inner, inner, x, core, core)] if side != 1 else [(None, None, inner, inner, x, other, other)]
        if nx > 1:
            for c in range(2):
                rows.append((no(top), no(bottom), pl.ds(1, 1), pl.ds(E - 1, 1), x - 1, c, c))
                rows.append((no(bottom), no(top), pl.ds(RB, 1), pl.ds(0, 1), x + 1, c, c))
        parts = []
        for i, (sends, gets, row, at, tox, to, source) in enumerate(rows):
            target = ref.at[core, theirs, at]
            theirs_ = ref.at[source, theirs, at]
            up = (i - 1) % 2
            arrived = 0 if i == 0 else 1 + up * 2 + core
            expected = 0 if i == 0 else 1 + up * 2 + source
            send = k_.x_send.at[k, side, i]
            parts.append((
                both(can_send[side], sends), both(can_recv[side], gets),
                functools.partial(
                    peer_copy, ref.at[core, own, row], target, send, k_.x_recv.at[k, side, arrived],
                    place + 1 - side, 2 * tox + to,
                ),
                functools.partial(peer_copy, theirs_, theirs_, send, k_.x_recv.at[k, side, expected], place, mate),
            ))
        return parts

    def fine_start(ref, which):
        for side in (0, 2, 1):
            for sends, _, out, _ in fine_parts(ref, which, side):
                launch(sends, out)

    def fine_halo(ref, which, side, c):
        k = FINE.index(which)
        block = ref.at[c, slices(side, S)[1], pl.ds(1, RB)]
        return peer_copy(block, block, k_.y_send.at[k, side], k_.y_recv.at[k, side], place, mate)

    def fine_pass(ref, which):
        for side in (0, 2):
            _, gets, _, back = fine_parts(ref, which, side)[0]
            arrive(gets, back)
            launch(gets, functools.partial(fine_halo, ref, which, side, core))

    def fine_wait(ref, which):
        for side in (1, 0, 2):
            for _, gets, _, back in fine_parts(ref, which, side)[side != 1 :]:
                arrive(gets, back)
            if side != 1:
                arrive(can_recv[side], functools.partial(fine_halo, ref, which, side, other))

    def natural(ref, s, r):
        v = ref[:, s, r]
        size = dm.cd
        return jnp.concatenate(
            [v[c, i * size : (i + 1) * size] for i in range(nx) for c in range(2)], 0
        ).astype(BF16)

    def in_turn(count, fn):
        if count <= 16:
            for i in range(count):
                fn(i)
        else:

            def body(i, carry):
                fn(i)
                return carry

            lax.fori_loop(0, count, body, 0)

    def slab_peers(i):
        to = place + 1 + i
        return jnp.where(to >= nd, to - nd, to), me

    def wide_peers(i):
        i = i + 1
        dt, xt = (i // nx, i % nx) if isinstance(i, int) else (lax.div(i, nx), lax.rem(i, nx))
        to, tox = place + dt, x + xt
        return jnp.where(to >= nd, to - nd, to), 2 * jnp.where(tox >= nx, tox - nx, tox) + core

    def exchange(n, peers, copy):
        in_turn(n - 1, lambda i: copy(*peers(i)).start())

    def sum_start(group, ref, k, slot, tile, source=None):
        n, own, peers, send, recv = group
        ref[slot, own] = tile

        def copy(depth, chan):
            src = ref.at[slot, own] if source is None else source(chan)
            return peer_copy(src, ref.at[slot, own], send.at[k], recv.at[k], depth, chan)

        exchange(n, peers, copy)
        pending.append((None, lambda: all_of(group, ref, k, slot).wait_send()))

    def all_of(group, ref, k, slot):
        n, _, _, send, recv = group
        every = ref.at[slot, pl.ds(0, n - 1)]
        return peer_copy(every, every, send.at[k], recv.at[k], place, mate)

    def sum_finish(group, ref, k, slot):
        all_of(group, ref, k, slot).wait_recv()
        return jnp.sum(ref[slot], axis=0)

    slabs = (nd, place, slab_peers, k_.t_send, k_.t_recv)
    everyone = (nd * nx, place * nx + x, wide_peers, k_.u_send, k_.u_recv)

    def columns_of(row, m):
        lane, channel = iota((m, LANES), 1), iota((m, LANES), 0)
        return tuple(
            jnp.sum(jnp.where(lane == channel + i * m, row, 0.0), axis=1, keepdims=True) for i in range(2)
        )

    def coarse_sums(slot, sums):
        sum_start(slabs, k_.st, slot, slot, pack(*sums))

    def coarse_totals(slot):
        return columns_of(sum_finish(slabs, k_.st, slot, slot), dm.ce)

    def fine_sums(slot, sums):
        sum_start(everyone, k_.su, slot, slot, pack(*sums))

    def fine_totals(slot):
        return columns_of(sum_finish(everyone, k_.su, slot, slot), dm.cf)

    def prepare(k):
        cv, w, own = convs[k], weights[k], wt[k]
        out = wf[k] if k < 2 else wf[k].at[x]
        eye = (iota((LANES, LANES), 0) == iota((LANES, LANES), 1)).astype(BF16)

        def chunk(a):
            return dot_nt(eye, jnp.concatenate([a] * cv.per, 0).astype(BF16))

        full = cv.length // LANES

        def body(i, carry):
            at = pl.multiple_of(i * LANES, LANES)
            turned[pl.ds(at, LANES)] = chunk(w[:, pl.ds(at, LANES)])
            return carry

        lax.fori_loop(0, full, body, 0, unroll=4)
        if full < cv.chunks:
            a = w[:, full * LANES :]
            a = jnp.concatenate([a, jnp.zeros((cv.o, LANES - a.shape[1]), F32)], 1)
            turned[full * LANES : (full + 1) * LANES] = chunk(a)
        group = iota((cv.c, LANES), 1) // cv.o
        for kz in range(3):
            for j in range(cv.tiles):
                tile = None
                for g in range(cv.per):
                    u = j * cv.per + g
                    if u < 9:
                        kx, ky = u // 3, u % 3
                        v = turned[pl.ds(9 * kz + 3 * ky + kx, cv.c, stride=27)]
                        tile = v if tile is None else jnp.where(group == g, v, tile)
                own[kz, :, j * LANES : (j + 1) * LANES] = tile.astype(BF16).astype(own.dtype)
        for j in range(cv.tiles):
            v = jnp.concatenate([own[kz, :, j * LANES : (j + 1) * LANES] for kz in range(3)], 0)
            size = min(LANES, cv.taps - j * LANES)
            v = dot_nt(eye, v.astype(BF16))[0:size]
            if k < 2:
                out[j * LANES : j * LANES + size] = v.astype(BF16)
            else:
                k_.flip[j * LANES : j * LANES + size, 0 : 3 * cv.c] = v
        if k >= 2:
            out[0 : 3 * cv.o] = jnp.concatenate(
                [
                    jnp.concatenate(
                        [
                            k_.flip[(3 * kx + ky) * cv.o : (3 * kx + ky + 1) * cv.o, kz * cv.c : (kz + 1) * cv.c]
                            for kx in range(3)
                        ],
                        0,
                    )
                    for kz in range(3)
                    for ky in range(3)
                ],
                1,
            ).astype(BF16)

    def forward_copy(k, t):
        block = wf[k].at[x]
        return peer_copy(
            block, block, k_.p_send.at[k - 2, t], k_.p_recv.at[k - 2, t], place, 2 * lax.rem(x + t, nx) + core
        )

    def forward_start(k):
        for t in range(1, nx):
            launch(None, functools.partial(forward_copy, k, t))

    def forward_wait(k):
        for t in range(1, nx):
            fromx = lax.rem(x + nx - t, nx)
            block = wf[k].at[fromx]
            peer_copy(
                block, block, k_.p_send.at[k - 2, t], k_.p_recv.at[k - 2, t], place, 2 * fromx + core
            ).wait_recv()

    def forward_weight(k):
        return jnp.concatenate([wf[k][i, 0 : 3 * convs[k].o] for i in range(nx)], 0)

    def weights_start(k):
        cv = convs[k]
        for b, (size, start, at) in enumerate(cv.blocks):
            wx[k][me, :, at : at + size] = wt[k][:, pl.ds(start(me), size)]
            for t in range(1, nc):
                to = lax.rem(me + t, nc)

                def copy(to=to, t=t, b=b, size=size, start=start, at=at):
                    return peer_copy(
                        wt[k].at[:, pl.ds(start(to), size)], wx[k].at[me, :, pl.ds(at, size)],
                        k_.w_send.at[k, b, t], k_.w_recv.at[k, b, t], place, to,
                    )

                launch(None, copy)

    def weights_finish(k):
        cv = convs[k]
        for b, (size, _, at) in enumerate(cv.blocks):
            for t in range(1, nc):
                source = lax.rem(me + nc - t, nc)
                theirs = wx[k].at[source, :, pl.ds(at, size)]
                peer_copy(theirs, theirs, k_.w_send.at[k, b, t], k_.w_recv.at[k, b, t], place, source).wait_recv()

        parts = 9 if k < 2 else 3
        lanes = cv.taps // parts
        for i in range(parts):
            at = (parts - 1 - i) * lanes
            found = [wx[k][j, 2 - kz, :, at : at + lanes].astype(F32) for kz in range(3) for j in range(nc)]
            wb[k][i * cv.needed : (i + 1) * cv.needed] = jnp.concatenate(found, 1).astype(BF16)

    def tiles_of(k, part, put):
        cv, dense = convs[k], k_.dense
        rows, size = 3 * cv.c, 3 * cv.o
        for ky in range(3):
            at = ky * LANES + part * size
            dense[0:rows, ky * size : (ky + 1) * size] = acc[0:rows, at : at + size]

        def tile(i, carry):
            left = []
            for kz in range(3):
                at = pl.ds(pl.multiple_of(kz * cv.c + i * 16, 16), 16)
                for j in range(cv.full):
                    put(i * cv.group + kz * cv.full + j, dense[at, j * LANES : (j + 1) * LANES].astype(BF16))
                left.append(dense[at, cv.full * LANES : cv.full * LANES + cv.left * cv.o])
            if cv.left:
                used = 3 * cv.left * cv.o
                v = jnp.concatenate(left + [jnp.zeros((16, LANES - used), F32)], 1)
                put(i * cv.group + 3 * cv.full, v.astype(BF16))
            return carry

        lax.fori_loop(0, cv.c // 16, tile, 0, unroll=2)

    def cross_start(k):
        gs, gx = (k_.gs2, k_.gs3)[k - 2], (k_.gx2, k_.gx3)[k - 2]

        for part in range(nx):

            def put(i, v, part=part):
                gs[part, i] = v

            tiles_of(k, part, put)
        for t in range(1, nx):

            def copy(t=t):
                tox = at_x(t)[0]
                return peer_copy(
                    gs.at[tox], gx.at[x], k_.c_send.at[k - 2, t], k_.c_recv.at[k - 2, t], place, 2 * tox + core
                )

            launch(None, copy)

    def cross_finish(k):
        cv, gs, gx = convs[k], (k_.gs2, k_.gs3)[k - 2], (k_.gx2, k_.gx3)[k - 2]
        sources = [at_x(t)[1] for t in range(1, nx)]
        for t, fromx in enumerate(sources, 1):
            theirs = gx.at[fromx]
            peer_copy(
                theirs, theirs, k_.c_send.at[k - 2, t], k_.c_recv.at[k - 2, t], place, 2 * fromx + core
            ).wait_recv()

        def add(i, carry):
            for j in range(cv.group):
                p = cv.group * i + j
                v = gs[x, p].astype(F32)
                for fromx in sources:
                    v += gx[fromx, p].astype(F32)
                gt[k][p] = v.astype(BF16)
            return carry

        lax.fori_loop(0, cv.c // 16, add, 0, unroll=2)
        reduce_send(k)

    def reduce_start(k):
        def put(i, v):
            gt[k][i] = v

        tiles_of(k, 0, put)
        reduce_send(k)

    nh = nd // 2
    par, rank = lax.rem(place, 2), lax.div(place, 2)
    partner = place + 1 - 2 * par

    def rank_peers(i):
        to = rank + 1 + i
        return 2 * jnp.where(to >= nh, to - nh, to) + par, me

    def half_of(k, which):
        size = nh * convs[k].share
        return pl.ds(which * size, size)

    def share_of(k, owner):
        size = convs[k].share
        if k == 0:
            return pl.ds(owner * size, size)
        return pl.ds((lax.rem(owner, 2) * nh + lax.div(owner, 2)) * size, size)

    def level(k):
        return (nd, slab_peers, place) if k == 0 else (nh, rank_peers, rank)

    def pair_copy(src, dst, k, i):
        return peer_copy(src, dst, k_.q_send.at[k, i], k_.q_recv.at[k, i], partner, me)

    def reduce_send(k):
        cv = convs[k]
        for i in range(cv.count, cv.share * nd):
            gt[k][i] = jnp.zeros((16, LANES), BF16)
        if k == 0:
            spread_shares(k)
        else:
            launch(None, lambda: pair_copy(gt[k].at[half_of(k, 1 - par)], gp[k - 1], k, 0))

    def pair_finish(k):
        pair_copy(gp[k - 1], gp[k - 1], k, 0).wait_recv()
        own = half_of(k, par)
        gt[k][own] = (gt[k][own].astype(F32) + gp[k - 1][...].astype(F32)).astype(BF16)
        spread_shares(k)

    def spread_shares(k):
        n, peers, own = level(k)
        gr[k][own] = gt[k][share_of(k, place)]

        def copy(to, chan):
            return peer_copy(gt[k].at[share_of(k, to)], gr[k].at[own], k_.r_send.at[k], k_.r_recv.at[k], to, chan)

        exchange(n, peers, copy)
        pending.append((None, lambda: reduce_all(k).wait_send()))

    def reduce_all(k):
        every = gr[k].at[pl.ds(0, level(k)[0] - 1)]
        return peer_copy(every, every, k_.r_send.at[k], k_.r_recv.at[k], place, mate)

    def share_all(k):
        every = ga[k].at[pl.ds(0, (level(k)[0] - 1) * convs[k].share)]
        return peer_copy(every, every, k_.a_send.at[k], k_.a_recv.at[k], place, mate)

    def reduce_finish(k):
        reduce_all(k).wait_recv()
        own = share_of(k, place)
        ga[k][own] = jnp.sum(gr[k][...].astype(F32), axis=0).astype(BF16)

        def copy(to, chan):
            return peer_copy(ga[k].at[own], ga[k].at[own], k_.a_send.at[k], k_.a_recv.at[k], to, chan)

        n, peers, _ = level(k)
        exchange(n, peers, copy)
        pending.append((None, lambda: share_all(k).wait_send()))

    def share_pass(k):
        share_all(k).wait_recv()
        own = ga[k].at[half_of(k, par)]
        launch(None, lambda: pair_copy(own, own, k, 1))

    def gradient_out(k):
        cv, out = convs[k], grads[k]
        if k == 0:
            share_all(k).wait_recv()
        else:
            theirs = ga[k].at[half_of(k, 1 - par)]
            pair_copy(theirs, theirs, k, 1).wait_recv()
        group = iota((16, LANES), 1) // cv.o

        def scatter(i, carry):
            def put(v, g, kz, t):
                turned[pl.ds(9 * kz + t + i * (16 * 27), 16, stride=27)] = jnp.where(group == g, v, 0.0)

            for kz in range(3):
                for j in range(cv.full):
                    v = ga[k][i * cv.group + kz * cv.full + j].astype(F32)
                    for g in range(min(cv.per, 9)):
                        put(v, g, kz, j * cv.per + g)
            if cv.left:
                v = ga[k][i * cv.group + 3 * cv.full].astype(F32)
                for kz in range(3):
                    for g in range(cv.left):
                        put(v, kz * cv.left + g, kz, cv.full * cv.per + g)
            return carry

        lax.fori_loop(0, cv.c // 16, scatter, 0, unroll=2)

        pick = (iota((cv.o, LANES), 1) % cv.o == iota((cv.o, LANES), 0)).astype(BF16)
        step = 8 * LANES
        for at in range(0, cv.length, step):
            size = min(step, cv.length - at)
            v = dot_nt(pick, turned[at : at + -(-size // LANES) * LANES].astype(BF16))
            out[:, at : at + size] = v[:, 0:size]

    def column(row):
        n = row.shape[1]
        eye = iota((n, n), 0) == iota((n, n), 1)
        return jnp.sum(jnp.where(eye, row, 0.0), axis=1, keepdims=True)

    def row_of(col):
        n = col.shape[0]
        eye = iota((n, n), 0) == iota((n, n), 1)
        return jnp.sum(jnp.where(eye, col, 0.0), axis=0, keepdims=True)

    def clear_halos(ref):
        def clear(at):
            if len(ref.shape) == 5:
                for c in range(2):
                    ref[c, at] = jnp.zeros(ref.shape[2:], ref.dtype)
            else:
                for i in range(nx):
                    ref[core, i, at] = jnp.zeros(ref.shape[3:], ref.dtype)

        pl.when(first)(lambda: clear(0))
        pl.when(last)(lambda: clear(ref.shape[-4] - 1))

    def clear_rows(ref):
        def clear(at):
            for c in range(2):
                for i in range(S + 2):
                    ref[c, i, at] = jnp.zeros(ref.shape[3:], ref.dtype)

        pl.when(top)(lambda: clear(0))
        pl.when(bottom)(lambda: clear(E - 1))

    def conv(operand, weight, m, groups, emit, init):
        def body(d, carry):
            v = operand(d)
            y = dot(weight, v)
            results = []
            for j in range(RB):
                lanes = slice(j * LANES, (j + 1) * LANES)
                parts = []
                for g in range(groups):
                    a = [y[(3 * g + kx) * m : (3 * g + kx + 1) * m, lanes] for kx in range(3)]
                    parts.append(from_left(a[0], W) + a[1] + from_right(a[2], W))
                results.append(jnp.concatenate(parts, 0) if groups > 1 else parts[0])
            return emit(d, results, carry)

        return lax.fori_loop(0, S, body, init)

    def rows_of(row):
        return lambda d: jnp.concatenate(
            [jnp.concatenate([row(d + kz, ky + j) for j in range(RB)], 1) for kz in range(3) for ky in range(3)], 0
        )

    def blocks_of(ref):
        size = dm.cd
        return lambda d: jnp.concatenate(
            [
                jnp.concatenate([ref[c, d + kz, 2 - ky + j, i * size : (i + 1) * size] for j in range(RB)], 1)
                for kz in range(3)
                for i in range(nx)
                for c in range(2)
                for ky in range(3)
            ],
            0,
        ).astype(BF16)

    def conv_stats(row, weight, z):
        def emit(d, results, carry):
            total, square = carry
            for j, v in enumerate(results):
                z[d * RB + j] = v
                total, square = total + v, square + v * v
            return total, square

        blank = jnp.zeros((dm.cf, LANES), F32)
        return conv(rows_of(row), weight, dm.cd, nx, emit, (blank, blank))

    def weight_grad(row, k):
        cv = convs[k]

        def part(d):
            v = jnp.concatenate([jnp.concatenate([row(d + kz, j) for j in range(E)], 1) for kz in range(3)], 0)
            y = jnp.concatenate(
                [k_.dzt[d, (2 - ky) * LANES : (2 - ky + E) * LANES] for ky in range(3)], 1
            )
            return dot(v, y)

        acc[0 : 3 * cv.c] = part(0)

        def more(d, carry):
            acc[0 : 3 * cv.c] += part(d)
            return carry

        lax.fori_loop(1, S, more, 0)

    def conv_coarse(ref, weight, m):
        v = jnp.concatenate(
            [jnp.concatenate([flat(ref, kz, i) for i in range(Q)], 1) for kz in range(3)], 0
        )
        y = dot(weight[...], v)
        blank = jnp.zeros((m, LANES), F32)

        def shifted(ky, i):
            if not 0 <= i < Q:
                return blank
            a, b, c = (
                y[(3 * kx + ky) * m : (3 * kx + ky + 1) * m, i * LANES : (i + 1) * LANES] for kx in range(3)
            )
            return from_left(a, V) + b + from_right(c, V)

        before = [shifted(0, i) for i in range(-1, Q)]
        after = [shifted(2, i) for i in range(Q + 1)]
        return [
            shifted(1, i) + halves(before[i + 1] + after[i + 1], before[i] + after[i]) for i in range(Q)
        ]

    def conv_stats_coarse(ref, weight, z, m):
        total = square = jnp.zeros((m, LANES), F32)
        for i, v in enumerate(conv_coarse(ref, weight, m)):
            z[i] = v
            total, square = total + v, square + v * v
        return total, square

    def weight_grad_coarse(ref, k):
        cv = convs[k]
        v = jnp.concatenate(
            [jnp.concatenate([flat(ref, kz, i) for i in range(Q)], 1) for kz in range(3)], 0
        )
        y = jnp.concatenate([k_.dzct[(2 - ky) * V : (2 - ky) * V + Q * LANES] for ky in range(3)], 1)
        acc[0 : 3 * cv.c] = dot(v, y)

    def pack(a, b):
        m = a.shape[0]
        a = jnp.sum(a, axis=1, keepdims=True)
        b = jnp.sum(b, axis=1, keepdims=True)
        lane, channel = iota((m, LANES), 1), iota((m, LANES), 0)
        both = jnp.where(lane == channel, a, jnp.where(lane == channel + m, b, 0.0))
        return jnp.sum(both, axis=0, keepdims=True)

    def moments(total, count):
        mean = total[0] / count
        var = total[1] / count - mean * mean
        return mean, lax.rsqrt(var + EPS)

    def wide(column):
        return jnp.broadcast_to(column, (column.shape[0], LANES))

    def factors(stats, norm):
        mean, inv = stats
        gain, shift = norm
        return wide(mean), wide(gain * inv), wide(shift)

    def norm_rows(z, stats, norm, emit, n):
        mean, scale, shift = factors(stats, norm)

        def body(i, carry):
            for j in range(n):
                p = i * n + j
                u = (z[p] - mean) * scale + shift
                emit(p, u * sigmoid(u))
            return carry

        lax.fori_loop(0, z.shape[0] // n, body, 0)

    def norm_back_sums(z, keep_du, stats, norm, grad, n):
        mean, scale, shift = factors(stats, norm)
        inv = wide(stats[1])
        m = z.shape[1]

        def body(i, carry):
            a, b = carry
            for j in range(n):
                p = i * n + j
                centred = z[p] - mean
                u = centred * scale + shift
                sigma = sigmoid(u)
                v = grad(p) * sigma * (1.0 + u * (1.0 - sigma))
                keep_du(p, v)
                a, b = a + v, b + v * (centred * inv)
            return a, b

        blank = jnp.zeros((m, LANES), F32)
        return lax.fori_loop(0, z.shape[0] // n, body, (blank, blank))

    def back_factors(stats, norm, total, count):
        mean, inv = stats
        scale = norm[0] * inv
        return wide(mean), wide(scale), wide(-scale * total[0] / count), wide(-scale * inv * total[1] / count)

    def columns_first(copies, groups):
        size = copies[0].shape[0] // groups
        rows = [v[g * size : (g + 1) * size] for g in range(groups) for v in copies]
        used = 3 * groups * size
        if used < LANES:
            rows.append(jnp.zeros((LANES - used, LANES), F32))
        return jnp.transpose(jnp.concatenate(rows, 0)).astype(BF16)

    def norm_back_fine(z, given, ref):
        mean, scale, level, slope = given

        def body(d, carry):
            for r in range(RB):
                p = d * RB + r
                v = scale * k_.du_f[p] + level + slope * (z[p] - mean)
                ref[core, 1 + d, 1 + r] = v.astype(BF16).astype(ref.dtype)
            return carry

        lax.fori_loop(0, S, body, 0)

    def turn_fine(ref):
        n = 4 if RB % 4 == 0 else 2

        def body(i, carry):
            d = lax.div(i, RB // n)
            r0 = (i - d * (RB // n)) * n
            for j in range(n):
                v = ref[core, 1 + d, 1 + r0 + j].astype(F32)
                at = pl.ds(pl.multiple_of((2 + r0 + j) * LANES, LANES), LANES)
                k_.dzt[d, at] = columns_first((from_right(v, W), v, from_left(v, W)), nx)
            return carry

        lax.fori_loop(0, S * RB // n, body, 0)

    def norm_back_coarse(z, given, ref):
        mean, scale, level, slope = given
        for i in range(Q):
            v = scale * k_.du_c[i] + level + slope * (z[i] - mean)
            ref[core, x, 1, i] = v.astype(BF16).astype(ref.dtype)

    def turn_coarse(ref):
        for i in range(Q):
            v = ref[core, x, 1, i].astype(F32)
            k_.dzct[V + i * LANES : V + (i + 1) * LANES] = columns_first((from_right(v, V), v, from_left(v, V)), 1)

    def keep_du(ref):
        def store(p, v):
            ref[p] = v

        return store

    barrier = pltpu.get_barrier_semaphore()

    def greet(depth, chan):
        pl.semaphore_signal(barrier, inc=1, device_id={"depth": depth, "chan": chan}, device_id_type=MESH)

    exchange(nd * nx, wide_peers, lambda depth, chan: types.SimpleNamespace(start=lambda: greet(depth, chan)))
    for t in range(nx):
        to = 2 * at_x(t)[0] + other
        greet(place, to)
        if t > 0:
            pl.when(no(first))(lambda to=to: greet(place - 1, to))
            pl.when(no(last))(lambda to=to: greet(place + 1, to))

    hc = iota((LANES, LANES), 0)
    fc = iota((LANES, LANES), 1)
    half = LANES // 2

    def up_table(coarse, fine):
        base = fine // 2
        beside = jnp.clip(base + jnp.where(fine % 2 == 0, -1, 1), 0, V - 1)
        near = (coarse == base).astype(F32)
        far = (coarse == beside).astype(F32)
        return (0.75 * near + 0.25 * far).astype(BF16)

    pool = jnp.concatenate([(hc // 2 == fc - at).astype(BF16) for at in (0, half)], 0)
    spread = jnp.concatenate([(hc - at == fc // 2).astype(BF16) for at in (0, half)], 1)
    up = jnp.concatenate([up_table(hc - at, fc) for at in (0, half)], 1)
    down = jnp.concatenate([up_table(fc, hc)] * 2, 0)
    spread2 = jnp.concatenate([spread, spread], 0)

    def take_rows(ref):
        for c in range(ref.shape[0]):
            k_.rows[c * S * R : (c + 1) * S * R] = ref[c].astype(F32).reshape(S * R, LANES)

    def row_of_all(p, chans):
        return k_.rows[pl.ds(p, chans, stride=S * R)]

    xp, xs, own_skip = k_.xp, k_.xs, k_.own_skip
    clear_halos(xp)
    take_rows(k_.skip)
    for i in range(S):
        for r in (0, R + 1):
            own_skip[i, r] = jnp.zeros((dm.cs, LANES), own_skip.dtype)

    def take_skip(i, carry):
        parts = []
        for d in range(S):
            v = [row_of_all(d * R + 4 * i + j, dm.cs).astype(BF16) for j in range(4)]
            for j in range(4):
                own_skip[d, 1 + 4 * i + j] = v[j].astype(own_skip.dtype)
            parts += [jnp.concatenate([v[j], v[2 + j]], 1) for j in range(2)]
        v = dot(jnp.concatenate(parts, 0), pool).reshape(2 * S, dm.cs, LANES)
        xp[core, x, 1, i] = (jnp.sum(v, axis=0) * 0.125).astype(BF16).astype(xp.dtype)
        return carry

    lax.fori_loop(0, Q, take_skip, 0, unroll=3)
    beside = jnp.where(first, 0, 1) + jnp.where(last, 0, 1)
    pl.semaphore_wait(barrier, nd * nx - 1 + nx + (nx - 1) * beside)
    gather_start(xp, "pooled")
    clear_halos(xs)
    xs[core, x, 1 : S + 1] = own_skip[:, pl.ds(row0, E)]
    gather_start(xs, "skip", lambda at, tox: own_skip.at[at, pl.ds(tox * RB, E)])

    gq = dm.g // nc
    columns = dm.enc_all + dm.skip_all
    gate_all, norm_all = k_.gate_all, k_.norm_all
    gate_all[me, :, 0:columns] = k_.gate[...]
    lane = iota((gq, LANES), 1)
    gate_all[me, :, 2 * LANES :] = jnp.where(
        lane == 0, column(k_.vector[0:1]), jnp.where(lane == 1, column(k_.vector[1:2]), 0.0)
    )
    for layer in range(2):
        for part in range(2):
            at = 2 * layer + part
            norm_all[me, at : at + 1, 0 : dm.cd] = k_.dn[part, layer : layer + 1]

    def constants(i, t, source, to):
        ref = (norm_all, gate_all)[i]
        return peer_copy(ref.at[source], ref.at[source], k_.v_send.at[i, t], k_.v_recv.at[i, t], place, to)

    for i in range(2):
        for t in range(1, nc):
            launch(None, functools.partial(constants, i, t, me, lax.rem(me + t, nc)))
    prepare(0)
    xd, xz4, xz3, d1 = k_.xd, k_.xz4, k_.xz3, k_.d1
    for ref in (xd, xz4, xz3):
        clear_rows(ref)
        clear_halos(ref)
    for ref in (k_.xh, k_.xz2, k_.xz1):
        clear_halos(ref)
    for i in range(S):
        for at in (0, (RB + 2) * LANES):
            k_.dzt[i, at : at + 2 * LANES] = jnp.zeros((2 * LANES, LANES), BF16)
        for r in range(3):
            k_.ug[i, r] = jnp.zeros(k_.ug.shape[2:], F32)
            k_.ug[i, RB + 3 + r] = jnp.zeros(k_.ug.shape[2:], F32)
        for r in range(H + 2):
            k_.cb[i, r] = jnp.zeros(k_.cb.shape[2:], F32)

    for at in (0, V + Q * LANES):
        k_.dzct[at : at + V] = jnp.zeros((V, LANES), BF16)

    def norm_of(layer):
        return column(k_.en[0, layer : layer + 1]), column(k_.en[1, layer : layer + 1])

    norm_e1, norm_e2 = norm_of(0), norm_of(1)

    gather_pass(xp, "pooled")
    gather_wait(xp, "pooled")
    coarse_sums(0, conv_stats_coarse(xp, wf[0], k_.z1, dm.ce))
    prepare(1)
    stats_e1 = moments(coarse_totals(0), dm.coarse_total)

    def keep_coarse(ref):
        def store(p, v):
            ref[core, x, 1, p] = v.astype(BF16).astype(ref.dtype)

        return store

    norm_rows(k_.z1, stats_e1, norm_e1, keep_coarse(k_.xh), Q)
    gather_start(k_.xh, "hidden")
    prepare(2)
    forward_start(2)
    gather_pass(k_.xh, "hidden")
    gather_pass(xs, "skip")
    gather_wait(k_.xh, "hidden")
    coarse_sums(1, conv_stats_coarse(k_.xh, wf[1], k_.z2, dm.ce))
    take_rows(k_.cot)

    def take_cot(i, carry):
        for d in range(S):
            for j in range(4):
                v = row_of_all(d * R + 4 * i + j, dm.cd).astype(BF16)
                k_.own_cot[d, 4 * i + j] = v.astype(k_.own_cot.dtype)
        return carry

    lax.fori_loop(0, Q, take_cot, 0)
    k_.cots[x] = k_.own_cot[:, pl.ds(row0, RB)]
    stats_e2 = moments(coarse_totals(1), dm.coarse_total)
    norm_rows(k_.z2, stats_e2, norm_e2, keep_coarse(k_.xc), Q)
    gather_start(k_.xc, "coarse")
    prepare(3)
    for t in range(1, nc):
        for i in range(2):
            source = lax.rem(me + nc - t, nc)
            constants(i, t, source, source).wait_recv()
    gate_full = gate_all[...].reshape(dm.g, 3 * LANES)
    wg = gate_full[:, 0:columns].astype(BF16)
    gbias = gate_full[:, 2 * LANES : 2 * LANES + 1]
    gout = gate_full[:, 2 * LANES + 1 : 2 * LANES + 2]
    k_.gate_t[...] = jnp.transpose(gate_full[:, 0 : 2 * LANES])
    own_rows = [k_.gate_t[pl.ds(pl.multiple_of((2 * i + core) * dm.ce, dm.ce), dm.ce)] for i in range(nx)]
    own_rows += [
        k_.gate_t[pl.ds(pl.multiple_of(dm.enc_all + (2 * i + core) * dm.cs, dm.cs), dm.cs)] for i in range(nx)
    ]
    k_.gate_own[...] = jnp.concatenate(own_rows, 0)

    def norm_fine(layer):
        return tuple(
            jnp.concatenate(
                [column(norm_all[2 * i + core, 2 * layer + part : 2 * layer + part + 1, 0 : dm.cd]) for i in range(nx)], 0
            )
            for part in range(2)
        )

    norm_d1, norm_d2 = norm_fine(0), norm_fine(1)
    gather_pass(k_.xc, "coarse")
    gather_wait(k_.xc, "coarse")
    forward_start(3)

    dt = k_.dt

    def up_depth(i, carry):
        t = []
        for j in range(3):
            v = dot(flat(k_.xc, j, i), up)
            t.append(jnp.stack([v[:, 0:LANES], v[:, LANES:]], 0))
        below = jnp.where(first, t[1], t[0])
        above = jnp.where(last, t[1], t[2])
        near = 0.75 * t[1]
        here = 0.25 * t[1]
        rows = pl.ds(i * 2, 2)
        dt[0, rows] = jnp.where(first, 0.0, 0.75 * below + here)
        dt[1, rows] = near + 0.25 * below
        dt[2, rows] = near + 0.25 * above
        dt[3, rows] = jnp.where(last, 0.0, 0.75 * above + here)
        return carry

    lax.fori_loop(0, Q, up_depth, 0)

    def up_rows(i, carry):
        here = h0 + i
        before, after = jnp.maximum(here - 1, 0), jnp.minimum(here + 1, H - 1)
        for j in range(S + 2):
            v = 0.75 * dt[j, here]
            d1[j, 1 + 2 * i, 0 : dm.enc_all] = (v + 0.25 * dt[j, before]).astype(BF16)
            d1[j, 2 + 2 * i, 0 : dm.enc_all] = (v + 0.25 * dt[j, after]).astype(BF16)
        return carry

    lax.fori_loop(0, RB // 2, up_rows, 0)
    for edge, at, near, far in (
        (top, 0, jnp.maximum(h0 - 1, 0), h0),
        (bottom, E - 1, jnp.minimum(h0 + RB // 2, H - 1), h0 + RB // 2 - 1),
    ):
        for j in range(S + 2):
            v = jnp.where(edge, 0.0, 0.75 * dt[j, near] + 0.25 * dt[j, far])
            d1[j, at, 0 : dm.enc_all] = v.astype(BF16)
    for t in range(1, nx):
        tox = lax.rem(x + t, nx)

        def send_cot(t=t, tox=tox):
            return peer_copy(
                k_.own_cot.at[:, pl.ds(tox * RB, RB)], k_.cots.at[x], k_.o_send.at[0, t], k_.o_recv.at[0, t],
                place, 2 * tox + core,
            )

        launch(None, send_cot)

    gather_wait(xs, "skip")
    gate_n = E // 2

    def gate(i, carry):
        j = lax.div(i, 2)
        r0 = (i - 2 * j) * gate_n
        skips = [flat(xs, j, r0 + q) for q in range(gate_n)]
        v = jnp.concatenate(
            [
                jnp.concatenate([d1[j, r0 + q, 0 : dm.enc_all] for q in range(gate_n)], 1),
                jnp.concatenate(skips, 1),
            ],
            0,
        )
        pre = dot(wg, v) + gbias
        act = pre * sigmoid(pre)
        alpha = sigmoid(jnp.sum(gout * act, axis=0, keepdims=True))
        for q in range(gate_n):
            lanes = slice(q * LANES, (q + 1) * LANES)
            d1[j, r0 + q, dm.enc_all :] = (alpha[:, lanes] * skips[q].astype(F32)).astype(BF16)
            k_.pre[j, r0 + q] = pre[:, lanes]
            k_.alpha[j, r0 + q] = alpha[:, lanes]
        return carry

    lax.fori_loop(0, (S + 2) * 2, gate, 0)
    def row_d1(j, r):
        return d1[j, r]

    def row_xd(j, r):
        return natural(xd, j, r)

    forward_wait(2)
    fine_sums(0, conv_stats(row_d1, forward_weight(2), k_.z3))
    forward_wait(3)
    stats_d1 = moments(fine_totals(0), dm.fine_total)

    def keep_dec(p, v):
        d = lax.div(p, RB)
        xd[core, 1 + d, 1 + p - d * RB] = v.astype(BF16).astype(xd.dtype)

    norm_rows(k_.z3, stats_d1, norm_d1, keep_dec, RB)
    fine_start(xd, "hidden")
    weights_start(3)
    weights_start(2)
    for t in range(1, nx):
        fromx = lax.rem(x + nx - t, nx)
        theirs = k_.cots.at[fromx]
        peer_copy(theirs, theirs, k_.o_send.at[0, t], k_.o_recv.at[0, t], place, 2 * fromx + core).wait_recv()
    fine_pass(xd, "hidden")
    fine_wait(xd, "hidden")
    fine_sums(1, conv_stats(row_xd, forward_weight(3), k_.z4))
    stats_d2 = moments(fine_totals(1), dm.fine_total)

    def rows_out(ref, own, theirs, kind, size):
        def copy_rows(read, at):
            def body(d, carry):
                for r in range(RB):
                    p = (d * R + at * RB + r) * size
                    ref[pl.ds(pl.multiple_of(p, size), size)] = read(d * RB + r).astype(F32)
                return carry

            lax.fori_loop(0, S, body, 0)

        copy_rows(lambda p: own[x, p], x)
        for t in range(1, nx):
            fromx = lax.rem(x + nx - t, nx)
            block = theirs.at[fromx]
            peer_copy(block, block, k_.o_send.at[kind, t], k_.o_recv.at[kind, t], place, 2 * fromx + core).wait_recv()
            copy_rows(lambda p, fromx=fromx: theirs[fromx, p], fromx)

    def row_cot(p):
        d = lax.div(p, RB)
        return jnp.concatenate([k_.cots[i, d, p - d * RB] for i in range(nx)], 0).astype(F32)

    fine_sums(2, norm_back_sums(k_.z4, keep_du(k_.du_f), stats_d2, norm_d2, row_cot, RB))

    def keep_result(p, v):
        for i in range(nx):
            k_.ob[i, p] = v[i * dm.cd : (i + 1) * dm.cd].astype(BF16).astype(k_.ob.dtype)

    norm_rows(k_.z4, stats_d2, norm_d2, keep_result, RB)
    total_d2 = fine_totals(2)
    norm_back_fine(k_.z4, back_factors(stats_d2, norm_d2, total_d2, dm.fine_total), xz4)
    fine_start(xz4, "dz4")
    weights_start(1)
    weights_start(0)
    for t in range(1, nx):
        tox = lax.rem(x + t, nx)

        def send_result(t=t, tox=tox):
            return peer_copy(
                k_.ob.at[tox], k_.oi.at[x], k_.o_send.at[1, t], k_.o_recv.at[1, t], place, 2 * tox + core
            )

        launch(None, send_result)
    turn_fine(xz4)
    weight_grad(row_xd, 3)
    fine_pass(xz4, "dz4")
    older = len(pending)
    cross_start(3)
    weights_finish(3)
    fine_wait(xz4, "dz4")

    def keep_grad(d, results, carry):
        for j, v in enumerate(results):
            k_.gg[d * RB + j] = v
        return carry

    conv(blocks_of(xz4), wb[3][...], dm.cf, 1, keep_grad, 0)
    fine_sums(3, norm_back_sums(k_.z3, keep_du(k_.du_f), stats_d1, norm_d1, lambda p: k_.gg[p], RB))
    cross_finish(3)
    total_d1 = fine_totals(3)
    norm_back_fine(k_.z3, back_factors(stats_d1, norm_d1, total_d1, dm.fine_total), xz3)
    fine_start(xz3, "dz3")
    turn_fine(xz3)
    weights_finish(2)
    weight_grad(row_d1, 2)
    fine_pass(xz3, "dz3")
    cross_start(2)
    pair_finish(3)
    rows_out(k_.out, k_.ob, k_.oi, 1, dm.cd)
    fine_wait(xz3, "dz3")

    ups = nx * dm.ce

    def gate_back(d, results, carry):
        bias, psi = carry
        lows = []
        for j, both in enumerate(results):
            p = d * RB + j
            v = both[ups:]
            grad = jnp.sum(v * flat(xs, d + 1, 1 + j).astype(F32), axis=0, keepdims=True)
            alpha = k_.alpha[d + 1, 1 + j]
            logit = grad * alpha * (1.0 - alpha)
            pre = k_.pre[d + 1, 1 + j]
            sigma = sigmoid(pre)
            psi = psi + pre * sigma * logit
            low = (logit * gout * sigma * (1.0 + pre * (1.0 - sigma))).astype(BF16)
            bias = bias + low.astype(F32)
            k_.pg[p] = low
            lows.append(low)
            k_.ug[d, 3 + j] = both[0:ups]
            for i in range(nc):
                k_.gv[i] = v[i * dm.cs : (i + 1) * dm.cs]
            for i in range(nx):
                k_.sgp[i, p] = alpha * k_.gv[2 * i + core]
        back = dot(k_.gate_own[...].astype(BF16), jnp.concatenate(lows, 1))
        for j in range(len(results)):
            p = d * RB + j
            lanes = slice(j * LANES, (j + 1) * LANES)
            k_.ug[d, 3 + j] += back[0:ups, lanes]
            for i in range(nx):
                v = k_.sgp[i, p] + back[ups + i * dm.cs : ups + (i + 1) * dm.cs, lanes]
                k_.sgp[i, p] = v
                k_.sgb[i, p] = v.astype(BF16).astype(k_.sgb.dtype)
        return bias, psi

    blank = jnp.zeros((dm.g, LANES), F32)
    bias, psi = conv(blocks_of(xz3), wb[2][...], ups + dm.skip_all, 1, gate_back, (blank, blank))

    ug, cb, cg = k_.ug, k_.cb, k_.cg
    for q in range(RB // 2 + 2):
        terms = []
        for d in range(S):
            v = 0.75 * (ug[d, 2 * q + 1] + ug[d, 2 * q + 2]) + 0.25 * (ug[d, 2 * q + 3] + ug[d, 2 * q])
            if q == 1:
                v += jnp.where(top, 0.25 * ug[d, 3], 0.0)
            if q == RB // 2:
                v += jnp.where(bottom, 0.25 * ug[d, RB + 2], 0.0)
            terms.append(split(v))
        v = dot(jnp.concatenate(terms, 0), down)
        for d in range(S):
            cb[d, h0 + q] = v[d * ups : (d + 1) * ups]

    def to_slabs(i, carry):
        even, odd = (cb[d, 2 * i + 1] + pltpu.roll(cb[d, 2 * i + 2], half, 1) for d in range(S))
        middle = 0.75 * (even + odd) + jnp.where(first, 0.25 * even, 0.0) + jnp.where(last, 0.25 * odd, 0.0)
        for part, v in enumerate((0.25 * even, middle, 0.25 * odd)):
            for j in range(nx):
                block = v[j * dm.ce : (j + 1) * dm.ce]
                k_.fs[part, j, i] = block.astype(BF16).astype(k_.fs.dtype)
                if part == 1:
                    k_.fm[j, i] = block
        return carry

    lax.fori_loop(0, Q, to_slabs, 0)

    reach = min((RB // 2 + 1) // 2 + 1, Q)

    def reach_of(at):
        return pl.ds(jnp.clip(lax.div(at * (RB // 2) + 1, 2) - 1, 0, Q - reach), reach)

    def fold_parts():
        for step in (-1, 1, 0):
            sends = (no(first), None, no(last))[step + 1]
            gets = (no(last), None, no(first))[step + 1]
            for t in range(nx):
                if (step, t) != (0, 0):
                    tox, fromx = lax.rem(x + t, nx), lax.rem(x + nx - t, nx)
                    sems = (k_.f_send.at[step + 1, t], k_.f_recv.at[step + 1, t])
                    rows = reach_of(x)
                    theirs = k_.fr.at[step + 1, fromx, reach_of(fromx)]
                    yield (
                        sends, gets, fromx, step + 1,
                        functools.partial(
                            peer_copy, k_.fs.at[step + 1, tox, rows], k_.fr.at[step + 1, x, rows], *sems,
                            place + step, 2 * tox + core,
                        ),
                        functools.partial(peer_copy, theirs, theirs, *sems, place, 2 * fromx + core),
                    )

    for sends, _, _, _, out, _ in fold_parts():
        launch(sends, out)
    for t in range(1, nx):
        tox = lax.rem(x + t, nx)

        def send_skip(t=t, tox=tox):
            return peer_copy(
                k_.sgb.at[tox], k_.sgi.at[x], k_.o_send.at[2, t], k_.o_recv.at[2, t], place, 2 * tox + core
            )

        launch(None, send_skip)

    reduce_finish(3)
    cross_finish(2)

    k_.gw[...] = jnp.zeros(k_.gw.shape, F32)

    def gate_weight(d, carry):
        v = jnp.concatenate(
            [
                jnp.concatenate([d1[1 + d, 1 + j, 0 : dm.enc_all] for j in range(RB)], 1),
                jnp.concatenate([flat(xs, 1 + d, 1 + j) for j in range(RB)], 1),
            ],
            0,
        )
        y = jnp.concatenate([k_.pg[d * RB + j] for j in range(RB)], 1)
        k_.gw[0:columns, 0 : dm.g] += dot_nt(v, y)
        return carry

    lax.fori_loop(0, S, gate_weight, 0)
    gate_grad = jnp.transpose(k_.gw[...])
    lane = iota((dm.g, LANES), 1)
    vectors = jnp.where(
        lane == 0,
        jnp.sum(bias, axis=1, keepdims=True),
        jnp.where(lane == 1, jnp.sum(psi, axis=1, keepdims=True), 0.0),
    )
    gate_block = k_.gate_block
    for j in range(nc):
        mine = slice(j * gq, (j + 1) * gq)
        gate_block[j, :, 0 : 2 * LANES] = gate_grad[mine]
        gate_block[j, :, 2 * LANES :] = vectors[mine]
    sum_start(everyone, k_.sv, 4, 0, gate_block[me], lambda chan: gate_block.at[chan])
    cg[...] = k_.fm[x]
    for _, gets, fromx, part, _, back in fold_parts():

        def fold_in(back=back, part=part, fromx=fromx):
            back().wait_recv()
            rows = reach_of(fromx)
            cg[rows] += k_.fr[part, fromx, rows].astype(F32)

        guarded(gets, fold_in)

    coarse_sums(2, norm_back_sums(k_.z2, keep_du(k_.du_c), stats_e2, norm_e2, lambda p: cg[p], Q))
    pair_finish(2)
    share_pass(3)
    weights_finish(1)
    total_e2 = coarse_totals(2)
    norm_back_coarse(k_.z2, back_factors(stats_e2, norm_e2, total_e2, dm.coarse_total), k_.xz2)
    gather_start(k_.xz2, "dz2")
    turn_coarse(k_.xz2)
    weight_grad_coarse(k_.xh, 1)
    reduce_start(1)
    gather_pass(k_.xz2, "dz2")
    reduce_finish(2)
    gradient_out(3)
    weights_finish(0)
    rows_out(k_.sg, k_.sgp, k_.sgi, 2, dm.cs)
    drain(older)
    share_pass(2)
    gather_wait(k_.xz2, "dz2")
    for i, v in enumerate(conv_coarse(k_.xz2, wb[1], dm.ce)):
        cg[i] = v
    coarse_sums(3, norm_back_sums(k_.z1, keep_du(k_.du_c), stats_e1, norm_e1, lambda p: cg[p], Q))
    pair_finish(1)
    gradient_out(2)
    total_e1 = coarse_totals(3)
    norm_back_coarse(k_.z1, back_factors(stats_e1, norm_e1, total_e1, dm.coarse_total), k_.xz1)
    gather_start(k_.xz1, "dz1")
    turn_coarse(k_.xz1)
    weight_grad_coarse(xp, 0)
    reduce_start(0)
    reduce_finish(1)
    gather_pass(k_.xz1, "dz1")
    share_pass(1)
    reduce_finish(0)
    gradient_out(1)
    gather_wait(k_.xz1, "dz1")
    for i, v in enumerate(conv_coarse(k_.xz1, wb[0], dm.cs)):
        v = dot(split(v), spread2) * 0.125
        for j in range(4):
            part = v[:, (j // 2) * LANES : (j // 2 + 1) * LANES]
            for d in range(S):
                at = (d * R + 4 * i + j) * dm.cs
                k_.sg[at : at + dm.cs] += part
    gate_total = sum_finish(everyone, k_.sv, 4, 0)
    k_.ggate[...] = gate_total[:, 0:columns]
    k_.gvector[0:1] = row_of(gate_total[:, 2 * LANES : 2 * LANES + 1])
    k_.gvector[1:2] = row_of(gate_total[:, 2 * LANES + 1 : 2 * LANES + 2])

    def own_part(col):
        parts = [jnp.where(x == i, col[i * dm.cd : (i + 1) * dm.cd], 0.0) for i in range(nx)]
        return functools.reduce(jnp.add, parts)

    for ref, pair, pick in ((k_.gen, (total_e1, total_e2), lambda v: v), (k_.gdn, (total_d1, total_d2), own_part)):
        for layer, total in enumerate(pair):
            ref[0, layer : layer + 1] = row_of(pick(total[1]))
            ref[1, layer : layer + 1] = row_of(pick(total[0]))
    gradient_out(0)
    drain()


def adamw(weight, grad, moment, square, rate):
    new_moment = 0.9 * moment + 0.1 * grad
    new_square = 0.999 * square + 0.001 * grad * grad
    moment_hat = new_moment * (1.0 / (1.0 - 0.9**STEP))
    square_hat = new_square * (1.0 / (1.0 - 0.999**STEP))
    new_weight = weight - rate * (moment_hat / (jnp.sqrt(square_hat) + 1e-08) + 0.01 * weight)
    return (new_weight, new_moment, new_square)


RATES = (CONV_RATE, CONV_RATE, GATE_RATE, VECTOR_RATE, CONV_RATE, CONV_RATE, VECTOR_RATE, VECTOR_RATE)


def update_kernel(*refs):
    n = len(RATES)
    sources, targets = refs[: 2 + 4 * n], refs[2 + 4 * n : 4 + 7 * n]
    inside, outside = refs[4 + 7 * n : 6 + 11 * n], refs[6 + 11 * n : 8 + 14 * n]
    in_sem, out_sem = refs[8 + 14 * n :]
    order = (4, 1, 0, 5, 2, 3, 6, 7)

    def load(i):
        return pltpu.make_async_copy(sources[i], inside[i], in_sem.at[i])

    def store(i):
        return pltpu.make_async_copy(outside[i], targets[i], out_sem.at[i])

    for i in (1, 0):
        load(i).start()
    for k in order:
        for part in range(4):
            load(2 + part * n + k).start()
    for i in (1, 0):
        load(i).wait()
        chans, (slabs, rows) = outside[i].shape[0], outside[i].shape[1:3]
        for c in range(chans):
            v = inside[i][pl.ds(c, slabs * rows, stride=chans)]
            outside[i][c] = v.reshape(slabs, rows, LANES).astype(outside[i].dtype)
        store(i).start()
    for k in order:
        own = [2 + part * n + k for part in range(4)]
        for i in own:
            load(i).wait()
        rows = inside[own[0]].shape[0]
        step = 8 if rows % 8 == 0 and rows > 8 else rows
        for r in range(0, rows, step):
            at = slice(r, r + step)
            new = adamw(*(inside[i][at] for i in own), RATES[k])
            for part, value in enumerate(new):
                outside[2 + 3 * k + part][at] = value
        for part in range(3):
            store(2 + 3 * k + part).start()
    for i in range(len(targets)):
        store(i).wait()


def per_device(
    skip, cotangent, enc_conv1, enc_conv2, gate_proj, gate_vector, dec_conv1, dec_conv2, enc_norms, dec_norms, *states
):
    nd, nc = lax.axis_size("depth"), lax.axis_size("chan")
    dm = Dims(nd, nc, skip.shape, enc_conv1.shape[0], dec_conv1.shape[0], gate_proj.shape[0] * nc)
    S, R, H, nx, RB, E = dm.s, dm.rows, dm.half, dm.nx, dm.rb, dm.ext
    Q = H // 2
    cin3 = dm.enc_all + dm.skip_all

    def own_block(size):
        return (size, lambda j: pl.multiple_of(j * size, size), 0)

    def core_blocks(size):
        return tuple(
            (size, lambda j, i=i: pl.multiple_of((2 * i + lax.rem(j, 2)) * size, size), i * size) for i in range(nx)
        )

    dm.convs = convs = (
        Conv(dm, dm.ce, dm.skip_all, (own_block(dm.cs),)),
        Conv(dm, dm.ce, dm.enc_all, (own_block(dm.ce),)),
        Conv(dm, dm.cd, cin3, core_blocks(dm.ce) + ((dm.skip_all, lambda j: dm.enc_all, nx * dm.ce),)),
        Conv(dm, dm.cd, dm.dec_all, core_blocks(dm.cd)),
    )
    params = (enc_conv1, enc_conv2, gate_proj, gate_vector, dec_conv1, dec_conv2, enc_norms, dec_norms)
    inputs = dict(
        skip=skip, cot=cotangent, w0=enc_conv1, w1=enc_conv2, w2=dec_conv1, w3=dec_conv2,
        gate=gate_proj, vector=gate_vector, en=enc_norms, dn=dec_norms,
    )
    shape = jax.ShapeDtypeStruct
    outs = dict(
        out=shape((S * R * dm.cd, LANES), F32),
        sg=shape((S * R * dm.cs, LANES), F32),
        **{f"g{i}": shape(a.shape, F32) for i, a in enumerate((enc_conv1, enc_conv2, dec_conv1, dec_conv2))},
        **{
            name: shape(a.shape, F32)
            for name, a in (("ggate", gate_proj), ("gvector", gate_vector), ("gen", enc_norms), ("gdn", dec_norms))
        },
    )
    gq = dm.g // nc

    def coarse(block):
        return pltpu.VMEM((2, nx, 3, Q, block, LANES), storage(block))

    def fine():
        return pltpu.VMEM((2, S + 2, E, dm.cf, LANES), storage(dm.cd))

    def f32(*dims):
        return pltpu.VMEM((*dims, LANES), F32)

    def tiles(*dims):
        return pltpu.VMEM((*dims, 16, LANES), BF16)

    def blocks(block, *dims):
        return pltpu.VMEM((*dims, block, LANES), storage(block))

    def sems(*dims):
        return pltpu.SemaphoreType.DMA(dims)

    scratch = dict(
        xp=coarse(dm.cs), xh=coarse(dm.ce), xc=coarse(dm.ce), xz2=coarse(dm.ce), xz1=coarse(dm.ce),
        own_skip=blocks(dm.cs, S, R + 2), xs=blocks(dm.cs, 2, nx, S + 2, E),
        own_cot=blocks(dm.cd, S, R), cots=blocks(dm.cd, nx, S, RB),
        d1=pltpu.VMEM((S + 2, E, cin3, LANES), BF16), xd=fine(), xz4=fine(), xz3=fine(),
        z1=f32(Q, dm.ce), z2=f32(Q, dm.ce), z3=f32(S * RB, dm.cf), z4=f32(S * RB, dm.cf),
        du_c=f32(Q, dm.ce), du_f=f32(S * RB, dm.cf), gg=f32(S * RB, dm.cf), cg=f32(Q, dm.ce),
        pre=f32(S + 2, E, dm.g), alpha=f32(S + 2, E, 1), pg=pltpu.VMEM((S * RB, dm.g, LANES), BF16),
        ug=f32(S, RB + 6, nx * dm.ce), cb=f32(S, H + 2, nx * dm.ce), dt=f32(S + 2, H, dm.enc_all),
        gv=f32(nc, dm.cs), sgp=f32(nx, S * RB, dm.cs), sgb=blocks(dm.cs, nx, S * RB), sgi=blocks(dm.cs, nx, S * RB),
        ob=blocks(dm.cd, nx, S * RB), oi=blocks(dm.cd, nx, S * RB),
        dzt=pltpu.VMEM((S, (RB + 4) * LANES, LANES), BF16), dzct=pltpu.VMEM((Q * LANES + 2 * dm.hcols, LANES), BF16),
        gw=f32(2 * LANES), dense=pltpu.VMEM((max(3 * cv.c for cv in convs), 3 * LANES), F32),
        fs=blocks(dm.ce, 3, nx, Q), fr=blocks(dm.ce, 3, nx, Q), fm=f32(nx, Q, dm.ce),
        st=f32(4, nd, 1), su=f32(4, nd * nx, 1), sv=pltpu.VMEM((1, nd * nx, gq, 3 * LANES), F32),
        norm_all=f32(nc, 8), rows=f32(max(dm.cs, dm.cd) * S * R),
        turned=f32(max(cv.chunks for cv in convs) * LANES),
        acc=pltpu.VMEM((max(3 * cv.c for cv in convs), 3 * LANES), F32),
        gate_all=pltpu.VMEM((nc, gq, 3 * LANES), F32), gate_t=pltpu.VMEM((2 * LANES, dm.g), F32),
        gate_own=pltpu.VMEM((nx * (dm.ce + dm.cs), dm.g), F32), gate_block=pltpu.VMEM((nc, gq, 3 * LANES), F32),
        **{f"wt{i}": pltpu.VMEM((3, cv.c, cv.wide), cv.kind) for i, cv in enumerate(convs)},
        **{
            f"wf{i}": pltpu.VMEM((cv.taps, 3 * cv.c) if i < 2 else (nx, cv.stored, 9 * cv.c), BF16)
            for i, cv in enumerate(convs)
        },
        **{f"wx{i}": pltpu.VMEM((nc, 3, cv.needed, cv.wide), cv.kind) for i, cv in enumerate(convs)},
        **{
            f"wb{i}": pltpu.VMEM((9 * cv.needed, 3 * nc * cv.o) if i < 2 else (3 * cv.needed, 9 * nc * cv.o), BF16)
            for i, cv in enumerate(convs)
        },
        flip=pltpu.VMEM((max(cv.tiles for cv in convs[2:]) * LANES, max(3 * cv.c for cv in convs[2:])), F32),
        **{f"gt{i}": tiles(cv.share * nd) for i, cv in enumerate(convs)},
        **{f"gr{i}": tiles(nd if i == 0 else nd // 2, cv.share) for i, cv in enumerate(convs)},
        **{f"gp{i}": tiles(nd // 2 * cv.share) for i, cv in enumerate(convs) if i > 0},
        **{f"ga{i}": tiles(cv.share * nd) for i, cv in enumerate(convs)},
        **{f"gs{i}": tiles(nx, convs[i].count) for i in (2, 3)},
        **{f"gx{i}": tiles(nx, convs[i].count) for i in (2, 3)},
        g_send=sems(len(GATHERS), 3, nx), g_recv=sems(len(GATHERS), 3),
        h_send=sems(len(GATHERS), 2 + nx), h_recv=sems(len(GATHERS)),
        x_send=sems(len(FINE), 3, 5), x_recv=sems(len(FINE), 3, 5),
        y_send=sems(len(FINE), 3), y_recv=sems(len(FINE), 3),
        t_send=sems(4), t_recv=sems(4), u_send=sems(5), u_recv=sems(5),
        f_send=sems(3, nx), f_recv=sems(3, nx), w_send=sems(4, nx + 1, nc), w_recv=sems(4, nx + 1, nc),
        p_send=sems(2, nx), p_recv=sems(2, nx), c_send=sems(2, nx), c_recv=sems(2, nx),
        o_send=sems(3, nx), o_recv=sems(3, nx), v_send=sems(2, nc), v_recv=sems(2, nc),
        r_send=sems(4), r_recv=sems(4), a_send=sems(4), a_recv=sems(4), q_send=sems(4, 2), q_recv=sems(4, 2),
    )
    vmem = pl.BlockSpec(memory_space=pltpu.VMEM)
    out, sg, grad1, grad2, grad3, grad4, ggate, gvector, gen, gdn = pl.pallas_call(
        functools.partial(kernel, dm, (*inputs, *outs, *scratch)),
        out_shape=tuple(outs.values()),
        in_specs=[vmem] * len(inputs),
        out_specs=[vmem] * len(outs),
        scratch_shapes=list(scratch.values()),
        compiler_params=pltpu.CompilerParams(
            has_side_effects=True, collective_id=0, vmem_limit_bytes=60 * 1024 * 1024
        ),
        name="step",
    )(*inputs.values())
    grads = (grad1, grad2, ggate, gvector, grad3, grad4, gen, gdn)
    operands = (out, sg, *params, *grads, *states)
    updated = (
        shape(cotangent.shape, BF16),
        shape(skip.shape, F32),
        *(shape(p.shape, F32) for p in params for _ in range(3)),
    )
    anywhere = pl.BlockSpec(memory_space=pl.ANY)
    return pl.pallas_call(
        update_kernel,
        out_shape=updated,
        in_specs=[anywhere] * len(operands),
        out_specs=[anywhere] * len(updated),
        scratch_shapes=[
            *(pltpu.VMEM(a.shape, a.dtype) for a in operands),
            *(pltpu.VMEM(a.shape, a.dtype) for a in updated),
            pltpu.SemaphoreType.DMA((len(operands),)),
            pltpu.SemaphoreType.DMA((len(updated),)),
        ],
        compiler_params=pltpu.CompilerParams(vmem_limit_bytes=60 * 1024 * 1024),
        name="update",
    )(*operands)


def solution(mesh):
    volume = P("chan", "depth", None, None)
    row, column, norms = P("chan", None), P(None, "chan"), P(None, None, "chan")
    params = (row, row, row, column, row, row, norms, norms)
    return jax.shard_map(
        per_device,
        mesh=mesh,
        in_specs=(volume, volume) + params * 3,
        out_specs=(volume, volume) + tuple(spec for spec in params for _ in range(3)),
        check_vma=False,
    )
```

```python
import functools
import types

import jax
import jax.numpy as jnp
from jax import lax
from jax.experimental import pallas as pl
from jax.experimental.pallas import tpu as pltpu
from jax.sharding import PartitionSpec as P

STEP = 5
EPS = 1e-05
CONV_RATE = 0.03
GATE_RATE = 0.1
VECTOR_RATE = 0.5
LANES = 128
MESH = pl.DeviceIdType.MESH
F32 = jnp.float32
BF16 = jnp.bfloat16


def iota(shape, dim):
    return lax.broadcasted_iota(jnp.int32, shape, dim)


def dot(a, b):
    return jnp.dot(a, b, preferred_element_type=F32)


def dot_nt(a, b):
    return lax.dot_general(a, b, (((1,), (1,)), ((), ())), preferred_element_type=F32)


def dot_tn(a, b):
    return lax.dot_general(a, b, (((0,), (0,)), ((), ())), preferred_element_type=F32)


def sigmoid(v):
    return 0.5 * jnp.tanh(0.5 * v) + 0.5


def from_left(v, width):
    return jnp.where(iota(v.shape, 1) % width == 0, 0.0, pltpu.roll(v, 1, 1))


def from_right(v, width):
    return jnp.where(iota(v.shape, 1) % width == width - 1, 0.0, pltpu.roll(v, LANES - 1, 1))


def halves(low, high):
    return pltpu.roll(jnp.where(iota(low.shape, 1) < LANES // 2, low, high), LANES // 2, 1)


def split(v):
    high = v.astype(BF16)
    return jnp.concatenate([high, (v - high.astype(F32)).astype(BF16)], 1)


def storage(block):
    return BF16 if block % 16 == 0 else F32


def flat(ref, s, r):
    if len(ref.shape) == 4:
        return ref[s, r]
    v = ref[:, :, s, r]
    return jnp.concatenate([v[c, i] for i in range(v.shape[1]) for c in range(2)], 0).astype(BF16)


class Dims:
    def __init__(self, nd, nc, skip, enc, dec, gate):
        self.nd, self.nc, self.nx = nd, nc, nc // 2
        self.s, self.rows, self.cols = skip[1:]
        self.cs, self.ce, self.cd, self.g = skip[0], enc, dec, gate
        self.half, self.hcols = self.rows // 2, self.cols // 2
        self.fine_total = nd * self.s * self.rows * self.cols
        self.coarse_total = self.fine_total // 8
        self.enc_all = nc * enc
        self.skip_all = nc * skip[0]
        self.dec_all = nc * dec
        self.rb = self.rows // self.nx
        self.ext = self.rb + 2
        self.cf = self.nx * dec


GATHERS = ("pooled", "skip", "hidden", "coarse", "dz2", "dz1")
FINE = ("hidden", "dz4", "dz3")


class Conv:
    def __init__(self, dm, o, c, blocks):
        self.o, self.c, self.blocks = o, c, blocks
        self.length = 27 * c
        self.chunks = -(-self.length // LANES)
        self.per = LANES // o
        self.tiles = -(-9 // self.per)
        self.wide = self.tiles * LANES
        self.kind = storage(min(size for size, _, _ in blocks))
        self.needed = sum(size for size, _, _ in blocks)
        self.full = max(1, 9 // self.per)
        self.left = max(0, 9 - self.full * self.per)
        self.group = 3 * self.full + (self.left > 0)
        self.count = c // 16 * self.group
        self.share = -(-self.count // dm.nd)
        self.taps = 9 * o
        self.stored = -(-3 * o // 16) * 16


def kernel(dm, names, *refs):
    k_ = types.SimpleNamespace(**dict(zip(names, refs)))
    nd, nc, nx, S, R, H = dm.nd, dm.nc, dm.nx, dm.s, dm.rows, dm.half
    W, V = dm.cols, dm.hcols
    Q, RB, E = H // 2, dm.rb, dm.ext
    place = lax.axis_index("depth")
    me = lax.axis_index("chan")
    x, core = lax.div(me, 2), lax.rem(me, 2)
    other = 1 - core
    mate = 2 * x + other
    row0, h0 = x * RB, x * (RB // 2)
    first, last = place == 0, place == nd - 1
    top, bottom = x == 0, x == nx - 1
    convs = dm.convs
    pending = []
    wt, wf, wx, wb = ([getattr(k_, f"{kind}{i}") for i in range(4)] for kind in ("wt", "wf", "wx", "wb"))
    gp = (k_.gp1, k_.gp2, k_.gp3)
    gt, gr, ga = ([getattr(k_, f"{kind}{i}") for i in range(4)] for kind in ("gt", "gr", "ga"))
    weights = (k_.w0, k_.w1, k_.w2, k_.w3)
    grads = (k_.g0, k_.g1, k_.g2, k_.g3)
    turned, acc = k_.turned, k_.acc

    def no(cond):
        return jnp.logical_not(cond)

    def peer_copy(src, dst, send, recv, depth, chan):
        return pltpu.make_async_remote_copy(
            src_ref=src, dst_ref=dst, send_sem=send, recv_sem=recv,
            device_id={"depth": depth, "chan": chan}, device_id_type=MESH,
        )

    def guarded(cond, fn):
        if cond is None:
            fn()
        else:
            pl.when(cond)(fn)

    def drain(count=None):
        for cond, fn in pending[:count]:
            guarded(cond, fn)
        del pending[:count]

    def launch(cond, copy):
        guarded(cond, lambda: copy().start())
        pending.append((cond, lambda: copy().wait_send()))

    def arrive(cond, copy):
        guarded(cond, lambda: copy().wait_recv())

    def both(a, b):
        return b if a is None else a if b is None else jnp.logical_and(a, b)

    can_send = (no(last), None, no(first))
    can_recv = (no(first), None, no(last))

    def slices(side, n):
        return (pl.ds(n, 1), pl.ds(1, n), pl.ds(1, 1))[side], (pl.ds(0, 1), pl.ds(1, n), pl.ds(n + 1, 1))[side]

    def at_x(t):
        up, down = x + t, x - t
        return jnp.where(up >= nx, up - nx, up), jnp.where(down < 0, down + nx, down)


    def gather_start(ref, which, source_at=None):
        n = ref.shape[2] - 2
        k = GATHERS.index(which)
        for side in (0, 2, 1):
            own, theirs = slices(side, n)
            for t in range(nx):
                if side == 1 and t == 0:
                    continue
                tox = at_x(t)[0]

                def copy(side=side, t=t, own=own, theirs=theirs, tox=tox):
                    start = (n, 1, 1)[side] - 1
                    size = (1, n, 1)[side]
                    src = ref.at[core, x, own] if source_at is None else source_at(pl.ds(start, size), tox)
                    return peer_copy(
                        src, ref.at[core, x, theirs], k_.g_send.at[k, side, t], k_.g_recv.at[k, side],
                        place + 1 - side, 2 * tox + core,
                    )

                launch(can_send[side], copy)
        gather_own(ref, which)

    def handed(ref, k, piece, i):
        return peer_copy(piece, piece, k_.h_send.at[k, i], k_.h_recv.at[k], place, mate)

    def gather_own(ref, which):
        k = GATHERS.index(which)
        launch(None, lambda: handed(ref, k, ref.at[core, x, pl.ds(1, ref.shape[2] - 2)], 0))

    def gather_pass(ref, which):
        n = ref.shape[2] - 2
        k = GATHERS.index(which)
        for side in (1, 0, 2):
            theirs = slices(side, n)[1]
            if side != 1:
                pieces = [ref.at[core, :, theirs]]
            else:
                pieces = [ref.at[core, at_x(t)[1], theirs] for t in range(1, nx)]
            for i, got in enumerate(pieces):
                arrive(
                    can_recv[side],
                    lambda got=got, side=side: peer_copy(
                        got, got, k_.g_send.at[k, side, 0], k_.g_recv.at[k, side], place, mate
                    ),
                )
                launch(None, lambda got=got, i=i, side=side: handed(ref, k, got, 1 + (side // 2 if side != 1 else 2 + i)))

    def gather_wait(ref, which):
        handed(ref, GATHERS.index(which), ref.at[other], 0).wait_recv()

    def fine_parts(ref, which, side):
        k = FINE.index(which)
        own, theirs = slices(side, S)
        inner = pl.ds(1, RB)
        rows = [(None, None, inner, inner, x, core, core)] if side != 1 else [(None, None, inner, inner, x, other, other)]
        if nx > 1:
            for c in range(2):
                rows.append((no(top), no(bottom), pl.ds(1, 1), pl.ds(E - 1, 1), x - 1, c, c))
                rows.append((no(bottom), no(top), pl.ds(RB, 1), pl.ds(0, 1), x + 1, c, c))
        parts = []
        for i, (sends, gets, row, at, tox, to, source) in enumerate(rows):
            target = ref.at[core, theirs, at]
            theirs_ = ref.at[source, theirs, at]
            up = (i - 1) % 2
            arrived = 0 if i == 0 else 1 + up * 2 + core
            expected = 0 if i == 0 else 1 + up * 2 + source
            send = k_.x_send.at[k, side, i]
            parts.append((
                both(can_send[side], sends), both(can_recv[side], gets),
                functools.partial(
                    peer_copy, ref.at[core, own, row], target, send, k_.x_recv.at[k, side, arrived],
                    place + 1 - side, 2 * tox + to,
                ),
                functools.partial(peer_copy, theirs_, theirs_, send, k_.x_recv.at[k, side, expected], place, mate),
            ))
        return parts

    def fine_start(ref, which):
        for side in (0, 2, 1):
            for sends, _, out, _ in fine_parts(ref, which, side):
                launch(sends, out)

    def fine_halo(ref, which, side, c):
        k = FINE.index(which)
        block = ref.at[c, slices(side, S)[1], pl.ds(1, RB)]
        return peer_copy(block, block, k_.y_send.at[k, side], k_.y_recv.at[k, side], place, mate)

    def fine_pass(ref, which):
        for side in (0, 2):
            _, gets, _, back = fine_parts(ref, which, side)[0]
            arrive(gets, back)
            launch(gets, functools.partial(fine_halo, ref, which, side, core))

    def fine_wait(ref, which):
        for side in (1, 0, 2):
            for _, gets, _, back in fine_parts(ref, which, side)[side != 1 :]:
                arrive(gets, back)
            if side != 1:
                arrive(can_recv[side], functools.partial(fine_halo, ref, which, side, other))

    def natural(ref, s, r):
        v = ref[:, s, r]
        size = dm.cd
        return jnp.concatenate(
            [v[c, i * size : (i + 1) * size] for i in range(nx) for c in range(2)], 0
        ).astype(BF16)

    def in_turn(count, fn):
        if count <= 16:
            for i in range(count):
                fn(i)
        else:

            def body(i, carry):
                fn(i)
                return carry

            lax.fori_loop(0, count, body, 0)

    def slab_peers(i):
        to = place + 1 + i
        return jnp.where(to >= nd, to - nd, to), me

    def wide_peers(i):
        i = i + 1
        dt, xt = (i // nx, i % nx) if isinstance(i, int) else (lax.div(i, nx), lax.rem(i, nx))
        to, tox = place + dt, x + xt
        return jnp.where(to >= nd, to - nd, to), 2 * jnp.where(tox >= nx, tox - nx, tox) + core

    def exchange(n, peers, copy):
        in_turn(n - 1, lambda i: copy(*peers(i)).start())

    def sum_start(group, ref, k, slot, tile, source=None):
        n, own, peers, send, recv = group
        ref[slot, own] = tile

        def copy(depth, chan):
            src = ref.at[slot, own] if source is None else source(chan)
            return peer_copy(src, ref.at[slot, own], send.at[k], recv.at[k], depth, chan)

        exchange(n, peers, copy)
        pending.append((None, lambda: all_of(group, ref, k, slot).wait_send()))

    def all_of(group, ref, k, slot):
        n, _, _, send, recv = group
        every = ref.at[slot, pl.ds(0, n - 1)]
        return peer_copy(every, every, send.at[k], recv.at[k], place, mate)

    def sum_finish(group, ref, k, slot):
        all_of(group, ref, k, slot).wait_recv()
        return jnp.sum(ref[slot], axis=0)

    slabs = (nd, place, slab_peers, k_.t_send, k_.t_recv)
    everyone = (nd * nx, place * nx + x, wide_peers, k_.u_send, k_.u_recv)

    def columns_of(row, m):
        lane, channel = iota((m, LANES), 1), iota((m, LANES), 0)
        return tuple(
            jnp.sum(jnp.where(lane == channel + i * m, row, 0.0), axis=1, keepdims=True) for i in range(2)
        )

    def coarse_sums(slot, sums):
        sum_start(slabs, k_.st, slot, slot, pack(*sums))

    def coarse_totals(slot):
        return columns_of(sum_finish(slabs, k_.st, slot, slot), dm.ce)

    def fine_sums(slot, sums):
        sum_start(everyone, k_.su, slot, slot, pack(*sums))

    def fine_totals(slot):
        return columns_of(sum_finish(everyone, k_.su, slot, slot), dm.cf)

    def prepare(k):
        cv, w, own = convs[k], weights[k], wt[k]
        out = wf[k] if k < 2 else wf[k].at[x]
        eye = (iota((LANES, LANES), 0) == iota((LANES, LANES), 1)).astype(BF16)

        def chunk(a):
            return dot_nt(eye, jnp.concatenate([a] * cv.per, 0).astype(BF16))

        full = cv.length // LANES

        def body(i, carry):
            at = pl.multiple_of(i * LANES, LANES)
            turned[pl.ds(at, LANES)] = chunk(w[:, pl.ds(at, LANES)])
            return carry

        lax.fori_loop(0, full, body, 0, unroll=4)
        if full < cv.chunks:
            a = w[:, full * LANES :]
            a = jnp.concatenate([a, jnp.zeros((cv.o, LANES - a.shape[1]), F32)], 1)
            turned[full * LANES : (full + 1) * LANES] = chunk(a)
        group = iota((cv.c, LANES), 1) // cv.o
        for kz in range(3):
            for j in range(cv.tiles):
                tile = None
                for g in range(cv.per):
                    u = j * cv.per + g
                    if u < 9:
                        kx, ky = u // 3, u % 3
                        v = turned[pl.ds(9 * kz + 3 * ky + kx, cv.c, stride=27)]
                        tile = v if tile is None else jnp.where(group == g, v, tile)
                own[kz, :, j * LANES : (j + 1) * LANES] = tile.astype(BF16).astype(own.dtype)
        for j in range(cv.tiles):
            v = jnp.concatenate([own[kz, :, j * LANES : (j + 1) * LANES] for kz in range(3)], 0)
            size = min(LANES, cv.taps - j * LANES)
            v = dot_nt(eye, v.astype(BF16))[0:size]
            if k < 2:
                out[j * LANES : j * LANES + size] = v.astype(BF16)
            else:
                k_.flip[j * LANES : j * LANES + size, 0 : 3 * cv.c] = v
        if k >= 2:
            out[0 : 3 * cv.o] = jnp.concatenate(
                [
                    jnp.concatenate(
                        [
                            k_.flip[(3 * kx + ky) * cv.o : (3 * kx + ky + 1) * cv.o, kz * cv.c : (kz + 1) * cv.c]
                            for kx in range(3)
                        ],
                        0,
                    )
                    for kz in range(3)
                    for ky in range(3)
                ],
                1,
            ).astype(BF16)

    def forward_copy(k, t):
        block = wf[k].at[x]
        return peer_copy(
            block, block, k_.p_send.at[k - 2, t], k_.p_recv.at[k - 2, t], place, 2 * lax.rem(x + t, nx) + core
        )

    def forward_start(k):
        for t in range(1, nx):
            launch(None, functools.partial(forward_copy, k, t))

    def forward_wait(k):
        for t in range(1, nx):
            fromx = lax.rem(x + nx - t, nx)
            block = wf[k].at[fromx]
            peer_copy(
                block, block, k_.p_send.at[k - 2, t], k_.p_recv.at[k - 2, t], place, 2 * fromx + core
            ).wait_recv()

    def forward_weight(k):
        return jnp.concatenate([wf[k][i, 0 : 3 * convs[k].o] for i in range(nx)], 0)

    def weights_start(k):
        cv = convs[k]
        for b, (size, start, at) in enumerate(cv.blocks):
            wx[k][me, :, at : at + size] = wt[k][:, pl.ds(start(me), size)]
            for t in range(1, nc):
                to = lax.rem(me + t, nc)

                def copy(to=to, t=t, b=b, size=size, start=start, at=at):
                    return peer_copy(
                        wt[k].at[:, pl.ds(start(to), size)], wx[k].at[me, :, pl.ds(at, size)],
                        k_.w_send.at[k, b, t], k_.w_recv.at[k, b, t], place, to,
                    )

                launch(None, copy)

    def weights_finish(k):
        cv = convs[k]
        for b, (size, _, at) in enumerate(cv.blocks):
            for t in range(1, nc):
                source = lax.rem(me + nc - t, nc)
                theirs = wx[k].at[source, :, pl.ds(at, size)]
                peer_copy(theirs, theirs, k_.w_send.at[k, b, t], k_.w_recv.at[k, b, t], place, source).wait_recv()

        parts = 9 if k < 2 else 3
        lanes = cv.taps // parts
        for i in range(parts):
            at = (parts - 1 - i) * lanes
            found = [wx[k][j, 2 - kz, :, at : at + lanes].astype(F32) for kz in range(3) for j in range(nc)]
            wb[k][i * cv.needed : (i + 1) * cv.needed] = jnp.concatenate(found, 1).astype(BF16)

    def tiles_of(k, part, put):
        cv, dense = convs[k], k_.dense
        rows, size = 3 * cv.c, 3 * cv.o
        for ky in range(3):
            at = ky * LANES + part * size
            dense[0:rows, ky * size : (ky + 1) * size] = acc[0:rows, at : at + size]

        def tile(i, carry):
            left = []
            for kz in range(3):
                at = pl.ds(pl.multiple_of(kz * cv.c + i * 16, 16), 16)
                for j in range(cv.full):
                    put(i * cv.group + kz * cv.full + j, dense[at, j * LANES : (j + 1) * LANES].astype(BF16))
                left.append(dense[at, cv.full * LANES : cv.full * LANES + cv.left * cv.o])
            if cv.left:
                used = 3 * cv.left * cv.o
                v = jnp.concatenate(left + [jnp.zeros((16, LANES - used), F32)], 1)
                put(i * cv.group + 3 * cv.full, v.astype(BF16))
            return carry

        lax.fori_loop(0, cv.c // 16, tile, 0, unroll=2)

    def cross_start(k):
        gs, gx = (k_.gs2, k_.gs3)[k - 2], (k_.gx2, k_.gx3)[k - 2]

        for part in range(nx):

            def put(i, v, part=part):
                gs[part, i] = v

            tiles_of(k, part, put)
        for t in range(1, nx):

            def copy(t=t):
                tox = at_x(t)[0]
                return peer_copy(
                    gs.at[tox], gx.at[x], k_.c_send.at[k - 2, t], k_.c_recv.at[k - 2, t], place, 2 * tox + core
                )

            launch(None, copy)

    def cross_finish(k):
        cv, gs, gx = convs[k], (k_.gs2, k_.gs3)[k - 2], (k_.gx2, k_.gx3)[k - 2]
        sources = [at_x(t)[1] for t in range(1, nx)]
        for t, fromx in enumerate(sources, 1):
            theirs = gx.at[fromx]
            peer_copy(
                theirs, theirs, k_.c_send.at[k - 2, t], k_.c_recv.at[k - 2, t], place, 2 * fromx + core
            ).wait_recv()

        def add(i, carry):
            for j in range(cv.group):
                p = cv.group * i + j
                v = gs[x, p].astype(F32)
                for fromx in sources:
                    v += gx[fromx, p].astype(F32)
                gt[k][p] = v.astype(BF16)
            return carry

        lax.fori_loop(0, cv.c // 16, add, 0, unroll=2)
        reduce_send(k)

    def reduce_start(k):
        def put(i, v):
            gt[k][i] = v

        tiles_of(k, 0, put)
        reduce_send(k)

    nh = nd // 2
    par, rank = lax.rem(place, 2), lax.div(place, 2)
    partner = place + 1 - 2 * par

    def rank_peers(i):
        to = rank + 1 + i
        return 2 * jnp.where(to >= nh, to - nh, to) + par, me

    def half_of(k, which):
        size = nh * convs[k].share
        return pl.ds(which * size, size)

    def share_of(k, owner):
        size = convs[k].share
        if k == 0:
            return pl.ds(owner * size, size)
        return pl.ds((lax.rem(owner, 2) * nh + lax.div(owner, 2)) * size, size)

    def level(k):
        return (nd, slab_peers, place) if k == 0 else (nh, rank_peers, rank)

    def pair_copy(src, dst, k, i):
        return peer_copy(src, dst, k_.q_send.at[k, i], k_.q_recv.at[k, i], partner, me)

    def reduce_send(k):
        cv = convs[k]
        for i in range(cv.count, cv.share * nd):
            gt[k][i] = jnp.zeros((16, LANES), BF16)
        if k == 0:
            spread_shares(k)
        else:
            launch(None, lambda: pair_copy(gt[k].at[half_of(k, 1 - par)], gp[k - 1], k, 0))

    def pair_finish(k):
        pair_copy(gp[k - 1], gp[k - 1], k, 0).wait_recv()
        own = half_of(k, par)
        gt[k][own] = (gt[k][own].astype(F32) + gp[k - 1][...].astype(F32)).astype(BF16)
        spread_shares(k)

    def spread_shares(k):
        n, peers, own = level(k)
        gr[k][own] = gt[k][share_of(k, place)]

        def copy(to, chan):
            return peer_copy(gt[k].at[share_of(k, to)], gr[k].at[own], k_.r_send.at[k], k_.r_recv.at[k], to, chan)

        exchange(n, peers, copy)
        pending.append((None, lambda: reduce_all(k).wait_send()))

    def reduce_all(k):
        every = gr[k].at[pl.ds(0, level(k)[0] - 1)]
        return peer_copy(every, every, k_.r_send.at[k], k_.r_recv.at[k], place, mate)

    def share_all(k):
        every = ga[k].at[pl.ds(0, (level(k)[0] - 1) * convs[k].share)]
        return peer_copy(every, every, k_.a_send.at[k], k_.a_recv.at[k], place, mate)

    def reduce_finish(k):
        reduce_all(k).wait_recv()
        own = share_of(k, place)
        ga[k][own] = jnp.sum(gr[k][...].astype(F32), axis=0).astype(BF16)

        def copy(to, chan):
            return peer_copy(ga[k].at[own], ga[k].at[own], k_.a_send.at[k], k_.a_recv.at[k], to, chan)

        n, peers, _ = level(k)
        exchange(n, peers, copy)
        pending.append((None, lambda: share_all(k).wait_send()))

    def share_pass(k):
        share_all(k).wait_recv()
        own = ga[k].at[half_of(k, par)]
        launch(None, lambda: pair_copy(own, own, k, 1))

    def gradient_out(k):
        cv, out = convs[k], grads[k]
        if k == 0:
            share_all(k).wait_recv()
        else:
            theirs = ga[k].at[half_of(k, 1 - par)]
            pair_copy(theirs, theirs, k, 1).wait_recv()
        group = iota((16, LANES), 1) // cv.o

        def scatter(i, carry):
            def put(v, g, kz, t):
                turned[pl.ds(9 * kz + t + i * (16 * 27), 16, stride=27)] = jnp.where(group == g, v, 0.0)

            for kz in range(3):
                for j in range(cv.full):
                    v = ga[k][i * cv.group + kz * cv.full + j].astype(F32)
                    for g in range(min(cv.per, 9)):
                        put(v, g, kz, j * cv.per + g)
            if cv.left:
                v = ga[k][i * cv.group + 3 * cv.full].astype(F32)
                for kz in range(3):
                    for g in range(cv.left):
                        put(v, kz * cv.left + g, kz, cv.full * cv.per + g)
            return carry

        lax.fori_loop(0, cv.c // 16, scatter, 0, unroll=2)

        pick = (iota((cv.o, LANES), 1) % cv.o == iota((cv.o, LANES), 0)).astype(BF16)
        step = 8 * LANES
        for at in range(0, cv.length, step):
            size = min(step, cv.length - at)
            v = dot_nt(pick, turned[at : at + -(-size // LANES) * LANES].astype(BF16))
            out[:, at : at + size] = v[:, 0:size]

    def column(row):
        n = row.shape[1]
        eye = iota((n, n), 0) == iota((n, n), 1)
        return jnp.sum(jnp.where(eye, row, 0.0), axis=1, keepdims=True)

    def row_of(col):
        n = col.shape[0]
        eye = iota((n, n), 0) == iota((n, n), 1)
        return jnp.sum(jnp.where(eye, col, 0.0), axis=0, keepdims=True)

    def clear_halos(ref):
        def clear(at):
            if len(ref.shape) == 5:
                for c in range(2):
                    ref[c, at] = jnp.zeros(ref.shape[2:], ref.dtype)
            else:
                for i in range(nx):
                    ref[core, i, at] = jnp.zeros(ref.shape[3:], ref.dtype)

        pl.when(first)(lambda: clear(0))
        pl.when(last)(lambda: clear(ref.shape[-4] - 1))

    def clear_rows(ref):
        def clear(at):
            for c in range(2):
                for i in range(S + 2):
                    ref[c, i, at] = jnp.zeros(ref.shape[3:], ref.dtype)

        pl.when(top)(lambda: clear(0))
        pl.when(bottom)(lambda: clear(E - 1))

    def conv(operand, weight, m, groups, emit, init):
        def body(d, carry):
            v = operand(d)
            y = dot(weight, v)
            results = []
            for j in range(RB):
                lanes = slice(j * LANES, (j + 1) * LANES)
                parts = []
                for g in range(groups):
                    a = [y[(3 * g + kx) * m : (3 * g + kx + 1) * m, lanes] for kx in range(3)]
                    parts.append(from_left(a[0], W) + a[1] + from_right(a[2], W))
                results.append(jnp.concatenate(parts, 0) if groups > 1 else parts[0])
            return emit(d, results, carry)

        return lax.fori_loop(0, S, body, init)

    def rows_of(row):
        return lambda d: jnp.concatenate(
            [jnp.concatenate([row(d + kz, ky + j) for j in range(RB)], 1) for kz in range(3) for ky in range(3)], 0
        )

    def blocks_of(ref):
        size = dm.cd
        return lambda d: jnp.concatenate(
            [
                jnp.concatenate([ref[c, d + kz, 2 - ky + j, i * size : (i + 1) * size] for j in range(RB)], 1)
                for kz in range(3)
                for i in range(nx)
                for c in range(2)
                for ky in range(3)
            ],
            0,
        ).astype(BF16)

    def conv_stats(row, weight, z):
        def emit(d, results, carry):
            total, square = carry
            for j, v in enumerate(results):
                z[d * RB + j] = v
                total, square = total + v, square + v * v
            return total, square

        blank = jnp.zeros((dm.cf, LANES), F32)
        return conv(rows_of(row), weight, dm.cd, nx, emit, (blank, blank))

    def weight_grad(row, k):
        cv = convs[k]

        def part(d):
            v = jnp.concatenate([jnp.concatenate([row(d + kz, j) for j in range(E)], 1) for kz in range(3)], 0)
            y = jnp.concatenate(
                [k_.dzt[d, (2 - ky) * LANES : (2 - ky + E) * LANES] for ky in range(3)], 1
            )
            return dot(v, y)

        acc[0 : 3 * cv.c] = part(0)

        def more(d, carry):
            acc[0 : 3 * cv.c] += part(d)
            return carry

        lax.fori_loop(1, S, more, 0)

    def conv_coarse(ref, weight, m):
        v = jnp.concatenate(
            [jnp.concatenate([flat(ref, kz, i) for i in range(Q)], 1) for kz in range(3)], 0
        )
        y = dot(weight[...], v)
        blank = jnp.zeros((m, LANES), F32)

        def shifted(ky, i):
            if not 0 <= i < Q:
                return blank
            a, b, c = (
                y[(3 * kx + ky) * m : (3 * kx + ky + 1) * m, i * LANES : (i + 1) * LANES] for kx in range(3)
            )
            return from_left(a, V) + b + from_right(c, V)

        before = [shifted(0, i) for i in range(-1, Q)]
        after = [shifted(2, i) for i in range(Q + 1)]
        return [
            shifted(1, i) + halves(before[i + 1] + after[i + 1], before[i] + after[i]) for i in range(Q)
        ]

    def conv_stats_coarse(ref, weight, z, m):
        total = square = jnp.zeros((m, LANES), F32)
        for i, v in enumerate(conv_coarse(ref, weight, m)):
            z[i] = v
            total, square = total + v, square + v * v
        return total, square

    def weight_grad_coarse(ref, k):
        cv = convs[k]
        v = jnp.concatenate(
            [jnp.concatenate([flat(ref, kz, i) for i in range(Q)], 1) for kz in range(3)], 0
        )
        y = jnp.concatenate([k_.dzct[(2 - ky) * V : (2 - ky) * V + Q * LANES] for ky in range(3)], 1)
        acc[0 : 3 * cv.c] = dot(v, y)

    def pack(a, b):
        m = a.shape[0]
        a = jnp.sum(a, axis=1, keepdims=True)
        b = jnp.sum(b, axis=1, keepdims=True)
        lane, channel = iota((m, LANES), 1), iota((m, LANES), 0)
        both = jnp.where(lane == channel, a, jnp.where(lane == channel + m, b, 0.0))
        return jnp.sum(both, axis=0, keepdims=True)

    def moments(total, count):
        mean = total[0] / count
        var = total[1] / count - mean * mean
        return mean, lax.rsqrt(var + EPS)

    def wide(column):
        return jnp.broadcast_to(column, (column.shape[0], LANES))

    def factors(stats, norm):
        mean, inv = stats
        gain, shift = norm
        return wide(mean), wide(gain * inv), wide(shift)

    def norm_rows(z, stats, norm, emit, n):
        mean, scale, shift = factors(stats, norm)

        def body(i, carry):
            for j in range(n):
                p = i * n + j
                u = (z[p] - mean) * scale + shift
                emit(p, u * sigmoid(u))
            return carry

        lax.fori_loop(0, z.shape[0] // n, body, 0)

    def norm_back_sums(z, keep_du, stats, norm, grad, n):
        mean, scale, shift = factors(stats, norm)
        inv = wide(stats[1])
        m = z.shape[1]

        def body(i, carry):
            a, b = carry
            for j in range(n):
                p = i * n + j
                centred = z[p] - mean
                u = centred * scale + shift
                sigma = sigmoid(u)
                v = grad(p) * sigma * (1.0 + u * (1.0 - sigma))
                keep_du(p, v)
                a, b = a + v, b + v * (centred * inv)
            return a, b

        blank = jnp.zeros((m, LANES), F32)
        return lax.fori_loop(0, z.shape[0] // n, body, (blank, blank))

    def back_factors(stats, norm, total, count):
        mean, inv = stats
        scale = norm[0] * inv
        return wide(mean), wide(scale), wide(-scale * total[0] / count), wide(-scale * inv * total[1] / count)

    def columns_first(copies, groups):
        size = copies[0].shape[0] // groups
        rows = [v[g * size : (g + 1) * size] for g in range(groups) for v in copies]
        used = 3 * groups * size
        if used < LANES:
            rows.append(jnp.zeros((LANES - used, LANES), F32))
        return jnp.transpose(jnp.concatenate(rows, 0)).astype(BF16)

    def norm_back_fine(z, given, ref):
        mean, scale, level, slope = given

        def body(d, carry):
            for r in range(RB):
                p = d * RB + r
                v = scale * k_.du_f[p] + level + slope * (z[p] - mean)
                ref[core, 1 + d, 1 + r] = v.astype(BF16).astype(ref.dtype)
            return carry

        lax.fori_loop(0, S, body, 0)

    def turn_fine(ref):
        n = 4 if RB % 4 == 0 else 2

        def body(i, carry):
            d = lax.div(i, RB // n)
            r0 = (i - d * (RB // n)) * n
            for j in range(n):
                v = ref[core, 1 + d, 1 + r0 + j].astype(F32)
                at = pl.ds(pl.multiple_of((2 + r0 + j) * LANES, LANES), LANES)
                k_.dzt[d, at] = columns_first((from_right(v, W), v, from_left(v, W)), nx)
            return carry

        lax.fori_loop(0, S * RB // n, body, 0)

    def norm_back_coarse(z, given, ref):
        mean, scale, level, slope = given
        for i in range(Q):
            v = scale * k_.du_c[i] + level + slope * (z[i] - mean)
            ref[core, x, 1, i] = v.astype(BF16).astype(ref.dtype)

    def turn_coarse(ref):
        for i in range(Q):
            v = ref[core, x, 1, i].astype(F32)
            k_.dzct[V + i * LANES : V + (i + 1) * LANES] = columns_first((from_right(v, V), v, from_left(v, V)), 1)

    def keep_du(ref):
        def store(p, v):
            ref[p] = v

        return store

    barrier = pltpu.get_barrier_semaphore()

    def greet(depth, chan):
        pl.semaphore_signal(barrier, inc=1, device_id={"depth": depth, "chan": chan}, device_id_type=MESH)

    exchange(nd * nx, wide_peers, lambda depth, chan: types.SimpleNamespace(start=lambda: greet(depth, chan)))
    for t in range(nx):
        to = 2 * at_x(t)[0] + other
        greet(place, to)
        if t > 0:
            pl.when(no(first))(lambda to=to: greet(place - 1, to))
            pl.when(no(last))(lambda to=to: greet(place + 1, to))

    hc = iota((LANES, LANES), 0)
    fc = iota((LANES, LANES), 1)
    half = LANES // 2

    def up_table(coarse, fine):
        base = fine // 2
        beside = jnp.clip(base + jnp.where(fine % 2 == 0, -1, 1), 0, V - 1)
        near = (coarse == base).astype(F32)
        far = (coarse == beside).astype(F32)
        return (0.75 * near + 0.25 * far).astype(BF16)

    pool = jnp.concatenate([(hc // 2 == fc - at).astype(BF16) for at in (0, half)], 0)
    spread = jnp.concatenate([(hc - at == fc // 2).astype(BF16) for at in (0, half)], 1)
    up = jnp.concatenate([up_table(hc - at, fc) for at in (0, half)], 1)
    down = jnp.concatenate([up_table(fc, hc)] * 2, 0)
    spread2 = jnp.concatenate([spread, spread], 0)

    def take_rows(ref):
        for c in range(ref.shape[0]):
            k_.rows[c * S * R : (c + 1) * S * R] = ref[c].astype(F32).reshape(S * R, LANES)

    def row_of_all(p, chans):
        return k_.rows[pl.ds(p, chans, stride=S * R)]

    xp, xs, own_skip = k_.xp, k_.xs, k_.own_skip
    clear_halos(xp)
    take_rows(k_.skip)
    for i in range(S):
        for r in (0, R + 1):
            own_skip[i, r] = jnp.zeros((dm.cs, LANES), own_skip.dtype)

    def take_skip(i, carry):
        parts = []
        for d in range(S):
            v = [row_of_all(d * R + 4 * i + j, dm.cs).astype(BF16) for j in range(4)]
            for j in range(4):
                own_skip[d, 1 + 4 * i + j] = v[j].astype(own_skip.dtype)
            parts += [jnp.concatenate([v[j], v[2 + j]], 1) for j in range(2)]
        v = dot(jnp.concatenate(parts, 0), pool).reshape(2 * S, dm.cs, LANES)
        xp[core, x, 1, i] = (jnp.sum(v, axis=0) * 0.125).astype(BF16).astype(xp.dtype)
        return carry

    lax.fori_loop(0, Q, take_skip, 0, unroll=3)
    beside = jnp.where(first, 0, 1) + jnp.where(last, 0, 1)
    pl.semaphore_wait(barrier, nd * nx - 1 + nx + (nx - 1) * beside)
    gather_start(xp, "pooled")
    clear_halos(xs)
    xs[core, x, 1 : S + 1] = own_skip[:, pl.ds(row0, E)]
    gather_start(xs, "skip", lambda at, tox: own_skip.at[at, pl.ds(tox * RB, E)])

    gq = dm.g // nc
    columns = dm.enc_all + dm.skip_all
    gate_all, norm_all = k_.gate_all, k_.norm_all
    gate_all[me, :, 0:columns] = k_.gate[...]
    lane = iota((gq, LANES), 1)
    gate_all[me, :, 2 * LANES :] = jnp.where(
        lane == 0, column(k_.vector[0:1]), jnp.where(lane == 1, column(k_.vector[1:2]), 0.0)
    )
    for layer in range(2):
        for part in range(2):
            at = 2 * layer + part
            norm_all[me, at : at + 1, 0 : dm.cd] = k_.dn[part, layer : layer + 1]

    def constants(i, t, source, to):
        ref = (norm_all, gate_all)[i]
        return peer_copy(ref.at[source], ref.at[source], k_.v_send.at[i, t], k_.v_recv.at[i, t], place, to)

    for i in range(2):
        for t in range(1, nc):
            launch(None, functools.partial(constants, i, t, me, lax.rem(me + t, nc)))
    prepare(0)
    xd, xz4, xz3, d1 = k_.xd, k_.xz4, k_.xz3, k_.d1
    for ref in (xd, xz4, xz3):
        clear_rows(ref)
        clear_halos(ref)
    for ref in (k_.xh, k_.xz2, k_.xz1):
        clear_halos(ref)
    for i in range(S):
        for at in (0, (RB + 2) * LANES):
            k_.dzt[i, at : at + 2 * LANES] = jnp.zeros((2 * LANES, LANES), BF16)
        for r in range(3):
            k_.ug[i, r] = jnp.zeros(k_.ug.shape[2:], F32)
            k_.ug[i, RB + 3 + r] = jnp.zeros(k_.ug.shape[2:], F32)
        for r in range(H + 2):
            k_.cb[i, r] = jnp.zeros(k_.cb.shape[2:], F32)

    for at in (0, V + Q * LANES):
        k_.dzct[at : at + V] = jnp.zeros((V, LANES), BF16)

    def norm_of(layer):
        return column(k_.en[0, layer : layer + 1]), column(k_.en[1, layer : layer + 1])

    norm_e1, norm_e2 = norm_of(0), norm_of(1)

    gather_pass(xp, "pooled")
    gather_wait(xp, "pooled")
    coarse_sums(0, conv_stats_coarse(xp, wf[0], k_.z1, dm.ce))
    prepare(1)
    stats_e1 = moments(coarse_totals(0), dm.coarse_total)

    def keep_coarse(ref):
        def store(p, v):
            ref[core, x, 1, p] = v.astype(BF16).astype(ref.dtype)

        return store

    norm_rows(k_.z1, stats_e1, norm_e1, keep_coarse(k_.xh), Q)
    gather_start(k_.xh, "hidden")
    prepare(2)
    forward_start(2)
    gather_pass(k_.xh, "hidden")
    gather_pass(xs, "skip")
    gather_wait(k_.xh, "hidden")
    coarse_sums(1, conv_stats_coarse(k_.xh, wf[1], k_.z2, dm.ce))
    take_rows(k_.cot)

    def take_cot(i, carry):
        for d in range(S):
            for j in range(4):
                v = row_of_all(d * R + 4 * i + j, dm.cd).astype(BF16)
                k_.own_cot[d, 4 * i + j] = v.astype(k_.own_cot.dtype)
        return carry

    lax.fori_loop(0, Q, take_cot, 0)
    k_.cots[x] = k_.own_cot[:, pl.ds(row0, RB)]
    stats_e2 = moments(coarse_totals(1), dm.coarse_total)
    norm_rows(k_.z2, stats_e2, norm_e2, keep_coarse(k_.xc), Q)
    gather_start(k_.xc, "coarse")
    prepare(3)
    for t in range(1, nc):
        for i in range(2):
            source = lax.rem(me + nc - t, nc)
            constants(i, t, source, source).wait_recv()
    gate_full = gate_all[...].reshape(dm.g, 3 * LANES)
    wg = gate_full[:, 0:columns].astype(BF16)
    gbias = gate_full[:, 2 * LANES : 2 * LANES + 1]
    gout = gate_full[:, 2 * LANES + 1 : 2 * LANES + 2]
    k_.gate_t[...] = jnp.transpose(gate_full[:, 0 : 2 * LANES])
    own_rows = [k_.gate_t[pl.ds(pl.multiple_of((2 * i + core) * dm.ce, dm.ce), dm.ce)] for i in range(nx)]
    own_rows += [
        k_.gate_t[pl.ds(pl.multiple_of(dm.enc_all + (2 * i + core) * dm.cs, dm.cs), dm.cs)] for i in range(nx)
    ]
    k_.gate_own[...] = jnp.concatenate(own_rows, 0)

    def norm_fine(layer):
        return tuple(
            jnp.concatenate(
                [column(norm_all[2 * i + core, 2 * layer + part : 2 * layer + part + 1, 0 : dm.cd]) for i in range(nx)], 0
            )
            for part in range(2)
        )

    norm_d1, norm_d2 = norm_fine(0), norm_fine(1)
    gather_pass(k_.xc, "coarse")
    gather_wait(k_.xc, "coarse")
    forward_start(3)

    dt = k_.dt

    def up_depth(i, carry):
        t = []
        for j in range(3):
            v = dot(flat(k_.xc, j, i), up)
            t.append(jnp.stack([v[:, 0:LANES], v[:, LANES:]], 0))
        below = jnp.where(first, t[1], t[0])
        above = jnp.where(last, t[1], t[2])
        near = 0.75 * t[1]
        here = 0.25 * t[1]
        rows = pl.ds(i * 2, 2)
        dt[0, rows] = jnp.where(first, 0.0, 0.75 * below + here)
        dt[1, rows] = near + 0.25 * below
        dt[2, rows] = near + 0.25 * above
        dt[3, rows] = jnp.where(last, 0.0, 0.75 * above + here)
        return carry

    lax.fori_loop(0, Q, up_depth, 0)

    def up_rows(i, carry):
        here = h0 + i
        before, after = jnp.maximum(here - 1, 0), jnp.minimum(here + 1, H - 1)
        for j in range(S + 2):
            v = 0.75 * dt[j, here]
            d1[j, 1 + 2 * i, 0 : dm.enc_all] = (v + 0.25 * dt[j, before]).astype(BF16)
            d1[j, 2 + 2 * i, 0 : dm.enc_all] = (v + 0.25 * dt[j, after]).astype(BF16)
        return carry

    lax.fori_loop(0, RB // 2, up_rows, 0)
    for edge, at, near, far in (
        (top, 0, jnp.maximum(h0 - 1, 0), h0),
        (bottom, E - 1, jnp.minimum(h0 + RB // 2, H - 1), h0 + RB // 2 - 1),
    ):
        for j in range(S + 2):
            v = jnp.where(edge, 0.0, 0.75 * dt[j, near] + 0.25 * dt[j, far])
            d1[j, at, 0 : dm.enc_all] = v.astype(BF16)
    for t in range(1, nx):
        tox = lax.rem(x + t, nx)

        def send_cot(t=t, tox=tox):
            return peer_copy(
                k_.own_cot.at[:, pl.ds(tox * RB, RB)], k_.cots.at[x], k_.o_send.at[0, t], k_.o_recv.at[0, t],
                place, 2 * tox + core,
            )

        launch(None, send_cot)

    gather_wait(xs, "skip")
    gate_n = E // 2

    def gate(i, carry):
        j = lax.div(i, 2)
        r0 = (i - 2 * j) * gate_n
        skips = [flat(xs, j, r0 + q) for q in range(gate_n)]
        v = jnp.concatenate(
            [
                jnp.concatenate([d1[j, r0 + q, 0 : dm.enc_all] for q in range(gate_n)], 1),
                jnp.concatenate(skips, 1),
            ],
            0,
        )
        pre = dot(wg, v) + gbias
        act = pre * sigmoid(pre)
        alpha = sigmoid(jnp.sum(gout * act, axis=0, keepdims=True))
        for q in range(gate_n):
            lanes = slice(q * LANES, (q + 1) * LANES)
            d1[j, r0 + q, dm.enc_all :] = (alpha[:, lanes] * skips[q].astype(F32)).astype(BF16)
            k_.pre[j, r0 + q] = pre[:, lanes]
            k_.alpha[j, r0 + q] = alpha[:, lanes]
        return carry

    lax.fori_loop(0, (S + 2) * 2, gate, 0)
    def row_d1(j, r):
        return d1[j, r]

    def row_xd(j, r):
        return natural(xd, j, r)

    forward_wait(2)
    fine_sums(0, conv_stats(row_d1, forward_weight(2), k_.z3))
    forward_wait(3)
    stats_d1 = moments(fine_totals(0), dm.fine_total)

    def keep_dec(p, v):
        d = lax.div(p, RB)
        xd[core, 1 + d, 1 + p - d * RB] = v.astype(BF16).astype(xd.dtype)

    norm_rows(k_.z3, stats_d1, norm_d1, keep_dec, RB)
    fine_start(xd, "hidden")
    weights_start(3)
    weights_start(2)
    for t in range(1, nx):
        fromx = lax.rem(x + nx - t, nx)
        theirs = k_.cots.at[fromx]
        peer_copy(theirs, theirs, k_.o_send.at[0, t], k_.o_recv.at[0, t], place, 2 * fromx + core).wait_recv()
    fine_pass(xd, "hidden")
    fine_wait(xd, "hidden")
    fine_sums(1, conv_stats(row_xd, forward_weight(3), k_.z4))
    stats_d2 = moments(fine_totals(1), dm.fine_total)

    def rows_out(ref, own, theirs, kind, size):
        def copy_rows(read, at):
            def body(d, carry):
                for r in range(RB):
                    p = (d * R + at * RB + r) * size
                    ref[pl.ds(pl.multiple_of(p, size), size)] = read(d * RB + r).astype(F32)
                return carry

            lax.fori_loop(0, S, body, 0)

        copy_rows(lambda p: own[x, p], x)
        for t in range(1, nx):
            fromx = lax.rem(x + nx - t, nx)
            block = theirs.at[fromx]
            peer_copy(block, block, k_.o_send.at[kind, t], k_.o_recv.at[kind, t], place, 2 * fromx + core).wait_recv()
            copy_rows(lambda p, fromx=fromx: theirs[fromx, p], fromx)

    def row_cot(p):
        d = lax.div(p, RB)
        return jnp.concatenate([k_.cots[i, d, p - d * RB] for i in range(nx)], 0).astype(F32)

    fine_sums(2, norm_back_sums(k_.z4, keep_du(k_.du_f), stats_d2, norm_d2, row_cot, RB))

    def keep_result(p, v):
        for i in range(nx):
            k_.ob[i, p] = v[i * dm.cd : (i + 1) * dm.cd].astype(BF16).astype(k_.ob.dtype)

    norm_rows(k_.z4, stats_d2, norm_d2, keep_result, RB)
    total_d2 = fine_totals(2)
    norm_back_fine(k_.z4, back_factors(stats_d2, norm_d2, total_d2, dm.fine_total), xz4)
    fine_start(xz4, "dz4")
    weights_start(1)
    weights_start(0)
    for t in range(1, nx):
        tox = lax.rem(x + t, nx)

        def send_result(t=t, tox=tox):
            return peer_copy(
                k_.ob.at[tox], k_.oi.at[x], k_.o_send.at[1, t], k_.o_recv.at[1, t], place, 2 * tox + core
            )

        launch(None, send_result)
    turn_fine(xz4)
    weight_grad(row_xd, 3)
    fine_pass(xz4, "dz4")
    older = len(pending)
    cross_start(3)
    weights_finish(3)
    fine_wait(xz4, "dz4")

    def keep_grad(d, results, carry):
        for j, v in enumerate(results):
            k_.gg[d * RB + j] = v
        return carry

    conv(blocks_of(xz4), wb[3][...], dm.cf, 1, keep_grad, 0)
    fine_sums(3, norm_back_sums(k_.z3, keep_du(k_.du_f), stats_d1, norm_d1, lambda p: k_.gg[p], RB))
    cross_finish(3)
    total_d1 = fine_totals(3)
    norm_back_fine(k_.z3, back_factors(stats_d1, norm_d1, total_d1, dm.fine_total), xz3)
    fine_start(xz3, "dz3")
    turn_fine(xz3)
    weights_finish(2)
    weight_grad(row_d1, 2)
    fine_pass(xz3, "dz3")
    cross_start(2)
    pair_finish(3)
    rows_out(k_.out, k_.ob, k_.oi, 1, dm.cd)
    fine_wait(xz3, "dz3")

    ups = nx * dm.ce

    def gate_back(d, results, carry):
        bias, psi = carry
        lows = []
        for j, both in enumerate(results):
            p = d * RB + j
            v = both[ups:]
            grad = jnp.sum(v * flat(xs, d + 1, 1 + j).astype(F32), axis=0, keepdims=True)
            alpha = k_.alpha[d + 1, 1 + j]
            logit = grad * alpha * (1.0 - alpha)
            pre = k_.pre[d + 1, 1 + j]
            sigma = sigmoid(pre)
            psi = psi + pre * sigma * logit
            low = (logit * gout * sigma * (1.0 + pre * (1.0 - sigma))).astype(BF16)
            bias = bias + low.astype(F32)
            k_.pg[p] = low
            lows.append(low)
            k_.ug[d, 3 + j] = both[0:ups]
            for i in range(nc):
                k_.gv[i] = v[i * dm.cs : (i + 1) * dm.cs]
            for i in range(nx):
                k_.sgp[i, p] = alpha * k_.gv[2 * i + core]
        back = dot(k_.gate_own[...].astype(BF16), jnp.concatenate(lows, 1))
        for j in range(len(results)):
            p = d * RB + j
            lanes = slice(j * LANES, (j + 1) * LANES)
            k_.ug[d, 3 + j] += back[0:ups, lanes]
            for i in range(nx):
                v = k_.sgp[i, p] + back[ups + i * dm.cs : ups + (i + 1) * dm.cs, lanes]
                k_.sgp[i, p] = v
                k_.sgb[i, p] = v.astype(BF16).astype(k_.sgb.dtype)
        return bias, psi

    blank = jnp.zeros((dm.g, LANES), F32)
    bias, psi = conv(blocks_of(xz3), wb[2][...], ups + dm.skip_all, 1, gate_back, (blank, blank))

    ug, cb, cg = k_.ug, k_.cb, k_.cg
    for q in range(RB // 2 + 2):
        terms = []
        for d in range(S):
            v = 0.75 * (ug[d, 2 * q + 1] + ug[d, 2 * q + 2]) + 0.25 * (ug[d, 2 * q + 3] + ug[d, 2 * q])
            if q == 1:
                v += jnp.where(top, 0.25 * ug[d, 3], 0.0)
            if q == RB // 2:
                v += jnp.where(bottom, 0.25 * ug[d, RB + 2], 0.0)
            terms.append(split(v))
        v = dot(jnp.concatenate(terms, 0), down)
        for d in range(S):
            cb[d, h0 + q] = v[d * ups : (d + 1) * ups]

    def to_slabs(i, carry):
        even, odd = (cb[d, 2 * i + 1] + pltpu.roll(cb[d, 2 * i + 2], half, 1) for d in range(S))
        middle = 0.75 * (even + odd) + jnp.where(first, 0.25 * even, 0.0) + jnp.where(last, 0.25 * odd, 0.0)
        for part, v in enumerate((0.25 * even, middle, 0.25 * odd)):
            for j in range(nx):
                block = v[j * dm.ce : (j + 1) * dm.ce]
                k_.fs[part, j, i] = block.astype(BF16).astype(k_.fs.dtype)
                if part == 1:
                    k_.fm[j, i] = block
        return carry

    lax.fori_loop(0, Q, to_slabs, 0)

    reach = min((RB // 2 + 1) // 2 + 1, Q)

    def reach_of(at):
        return pl.ds(jnp.clip(lax.div(at * (RB // 2) + 1, 2) - 1, 0, Q - reach), reach)

    def fold_parts():
        for step in (-1, 1, 0):
            sends = (no(first), None, no(last))[step + 1]
            gets = (no(last), None, no(first))[step + 1]
            for t in range(nx):
                if (step, t) != (0, 0):
                    tox, fromx = lax.rem(x + t, nx), lax.rem(x + nx - t, nx)
                    sems = (k_.f_send.at[step + 1, t], k_.f_recv.at[step + 1, t])
                    rows = reach_of(x)
                    theirs = k_.fr.at[step + 1, fromx, reach_of(fromx)]
                    yield (
                        sends, gets, fromx, step + 1,
                        functools.partial(
                            peer_copy, k_.fs.at[step + 1, tox, rows], k_.fr.at[step + 1, x, rows], *sems,
                            place + step, 2 * tox + core,
                        ),
                        functools.partial(peer_copy, theirs, theirs, *sems, place, 2 * fromx + core),
                    )

    for sends, _, _, _, out, _ in fold_parts():
        launch(sends, out)
    for t in range(1, nx):
        tox = lax.rem(x + t, nx)

        def send_skip(t=t, tox=tox):
            return peer_copy(
                k_.sgb.at[tox], k_.sgi.at[x], k_.o_send.at[2, t], k_.o_recv.at[2, t], place, 2 * tox + core
            )

        launch(None, send_skip)

    reduce_finish(3)
    cross_finish(2)

    k_.gw[...] = jnp.zeros(k_.gw.shape, F32)

    def gate_weight(d, carry):
        v = jnp.concatenate(
            [
                jnp.concatenate([d1[1 + d, 1 + j, 0 : dm.enc_all] for j in range(RB)], 1),
                jnp.concatenate([flat(xs, 1 + d, 1 + j) for j in range(RB)], 1),
            ],
            0,
        )
        y = jnp.concatenate([k_.pg[d * RB + j] for j in range(RB)], 1)
        k_.gw[0:columns, 0 : dm.g] += dot_nt(v, y)
        return carry

    lax.fori_loop(0, S, gate_weight, 0)
    gate_grad = jnp.transpose(k_.gw[...])
    lane = iota((dm.g, LANES), 1)
    vectors = jnp.where(
        lane == 0,
        jnp.sum(bias, axis=1, keepdims=True),
        jnp.where(lane == 1, jnp.sum(psi, axis=1, keepdims=True), 0.0),
    )
    gate_block = k_.gate_block
    for j in range(nc):
        mine = slice(j * gq, (j + 1) * gq)
        gate_block[j, :, 0 : 2 * LANES] = gate_grad[mine]
        gate_block[j, :, 2 * LANES :] = vectors[mine]
    sum_start(everyone, k_.sv, 4, 0, gate_block[me], lambda chan: gate_block.at[chan])
    cg[...] = k_.fm[x]
    for _, gets, fromx, part, _, back in fold_parts():

        def fold_in(back=back, part=part, fromx=fromx):
            back().wait_recv()
            rows = reach_of(fromx)
            cg[rows] += k_.fr[part, fromx, rows].astype(F32)

        guarded(gets, fold_in)

    coarse_sums(2, norm_back_sums(k_.z2, keep_du(k_.du_c), stats_e2, norm_e2, lambda p: cg[p], Q))
    pair_finish(2)
    share_pass(3)
    weights_finish(1)
    total_e2 = coarse_totals(2)
    norm_back_coarse(k_.z2, back_factors(stats_e2, norm_e2, total_e2, dm.coarse_total), k_.xz2)
    gather_start(k_.xz2, "dz2")
    turn_coarse(k_.xz2)
    weight_grad_coarse(k_.xh, 1)
    gather_pass(k_.xz2, "dz2")
    reduce_start(1)
    weights_finish(0)
    reduce_finish(2)
    rows_out(k_.sg, k_.sgp, k_.sgi, 2, dm.cs)
    drain(older)
    gather_wait(k_.xz2, "dz2")
    for i, v in enumerate(conv_coarse(k_.xz2, wb[1], dm.ce)):
        cg[i] = v
    coarse_sums(3, norm_back_sums(k_.z1, keep_du(k_.du_c), stats_e1, norm_e1, lambda p: cg[p], Q))
    pair_finish(1)
    share_pass(2)
    gradient_out(3)
    total_e1 = coarse_totals(3)
    norm_back_coarse(k_.z1, back_factors(stats_e1, norm_e1, total_e1, dm.coarse_total), k_.xz1)
    gather_start(k_.xz1, "dz1")
    turn_coarse(k_.xz1)
    weight_grad_coarse(xp, 0)
    reduce_start(0)
    reduce_finish(1)
    gather_pass(k_.xz1, "dz1")
    gradient_out(2)
    share_pass(1)
    reduce_finish(0)
    gather_wait(k_.xz1, "dz1")
    for i, v in enumerate(conv_coarse(k_.xz1, wb[0], dm.cs)):
        v = dot(split(v), spread2) * 0.125
        for j in range(4):
            part = v[:, (j // 2) * LANES : (j // 2 + 1) * LANES]
            for d in range(S):
                at = (d * R + 4 * i + j) * dm.cs
                k_.sg[at : at + dm.cs] += part
    gradient_out(1)
    gate_total = sum_finish(everyone, k_.sv, 4, 0)
    k_.ggate[...] = gate_total[:, 0:columns]
    k_.gvector[0:1] = row_of(gate_total[:, 2 * LANES : 2 * LANES + 1])
    k_.gvector[1:2] = row_of(gate_total[:, 2 * LANES + 1 : 2 * LANES + 2])

    def own_part(col):
        parts = [jnp.where(x == i, col[i * dm.cd : (i + 1) * dm.cd], 0.0) for i in range(nx)]
        return functools.reduce(jnp.add, parts)

    for ref, pair, pick in ((k_.gen, (total_e1, total_e2), lambda v: v), (k_.gdn, (total_d1, total_d2), own_part)):
        for layer, total in enumerate(pair):
            ref[0, layer : layer + 1] = row_of(pick(total[1]))
            ref[1, layer : layer + 1] = row_of(pick(total[0]))
    gradient_out(0)
    drain()


def adamw(weight, grad, moment, square, rate):
    new_moment = 0.9 * moment + 0.1 * grad
    new_square = 0.999 * square + 0.001 * grad * grad
    moment_hat = new_moment * (1.0 / (1.0 - 0.9**STEP))
    square_hat = new_square * (1.0 / (1.0 - 0.999**STEP))
    new_weight = weight - rate * (moment_hat / (jnp.sqrt(square_hat) + 1e-08) + 0.01 * weight)
    return (new_weight, new_moment, new_square)


RATES = (CONV_RATE, CONV_RATE, GATE_RATE, VECTOR_RATE, CONV_RATE, CONV_RATE, VECTOR_RATE, VECTOR_RATE)


def update_kernel(*refs):
    n = len(RATES)
    sources, targets = refs[: 2 + 4 * n], refs[2 + 4 * n : 4 + 7 * n]
    inside, outside = refs[4 + 7 * n : 6 + 11 * n], refs[6 + 11 * n : 8 + 14 * n]
    in_sem, out_sem = refs[8 + 14 * n :]
    order = (4, 1, 0, 5, 2, 3, 6, 7)

    def load(i):
        return pltpu.make_async_copy(sources[i], inside[i], in_sem.at[i])

    def store(i):
        return pltpu.make_async_copy(outside[i], targets[i], out_sem.at[i])

    for i in (1, 0):
        load(i).start()
    for k in order:
        for part in range(4):
            load(2 + part * n + k).start()
    for i in (1, 0):
        load(i).wait()
        chans, (slabs, rows) = outside[i].shape[0], outside[i].shape[1:3]
        for c in range(chans):
            v = inside[i][pl.ds(c, slabs * rows, stride=chans)]
            outside[i][c] = v.reshape(slabs, rows, LANES).astype(outside[i].dtype)
        store(i).start()
    for k in order:
        own = [2 + part * n + k for part in range(4)]
        for i in own:
            load(i).wait()
        rows = inside[own[0]].shape[0]
        step = 8 if rows % 8 == 0 and rows > 8 else rows
        for r in range(0, rows, step):
            at = slice(r, r + step)
            new = adamw(*(inside[i][at] for i in own), RATES[k])
            for part, value in enumerate(new):
                outside[2 + 3 * k + part][at] = value
        for part in range(3):
            store(2 + 3 * k + part).start()
    for i in range(len(targets)):
        store(i).wait()


def per_device(
    skip, cotangent, enc_conv1, enc_conv2, gate_proj, gate_vector, dec_conv1, dec_conv2, enc_norms, dec_norms, *states
):
    nd, nc = lax.axis_size("depth"), lax.axis_size("chan")
    dm = Dims(nd, nc, skip.shape, enc_conv1.shape[0], dec_conv1.shape[0], gate_proj.shape[0] * nc)
    S, R, H, nx, RB, E = dm.s, dm.rows, dm.half, dm.nx, dm.rb, dm.ext
    Q = H // 2
    cin3 = dm.enc_all + dm.skip_all

    def own_block(size):
        return (size, lambda j: pl.multiple_of(j * size, size), 0)

    def core_blocks(size):
        return tuple(
            (size, lambda j, i=i: pl.multiple_of((2 * i + lax.rem(j, 2)) * size, size), i * size) for i in range(nx)
        )

    dm.convs = convs = (
        Conv(dm, dm.ce, dm.skip_all, (own_block(dm.cs),)),
        Conv(dm, dm.ce, dm.enc_all, (own_block(dm.ce),)),
        Conv(dm, dm.cd, cin3, core_blocks(dm.ce) + ((dm.skip_all, lambda j: dm.enc_all, nx * dm.ce),)),
        Conv(dm, dm.cd, dm.dec_all, core_blocks(dm.cd)),
    )
    params = (enc_conv1, enc_conv2, gate_proj, gate_vector, dec_conv1, dec_conv2, enc_norms, dec_norms)
    inputs = dict(
        skip=skip, cot=cotangent, w0=enc_conv1, w1=enc_conv2, w2=dec_conv1, w3=dec_conv2,
        gate=gate_proj, vector=gate_vector, en=enc_norms, dn=dec_norms,
    )
    shape = jax.ShapeDtypeStruct
    outs = dict(
        out=shape((S * R * dm.cd, LANES), F32),
        sg=shape((S * R * dm.cs, LANES), F32),
        **{f"g{i}": shape(a.shape, F32) for i, a in enumerate((enc_conv1, enc_conv2, dec_conv1, dec_conv2))},
        **{
            name: shape(a.shape, F32)
            for name, a in (("ggate", gate_proj), ("gvector", gate_vector), ("gen", enc_norms), ("gdn", dec_norms))
        },
    )
    gq = dm.g // nc

    def coarse(block):
        return pltpu.VMEM((2, nx, 3, Q, block, LANES), storage(block))

    def fine():
        return pltpu.VMEM((2, S + 2, E, dm.cf, LANES), storage(dm.cd))

    def f32(*dims):
        return pltpu.VMEM((*dims, LANES), F32)

    def tiles(*dims):
        return pltpu.VMEM((*dims, 16, LANES), BF16)

    def blocks(block, *dims):
        return pltpu.VMEM((*dims, block, LANES), storage(block))

    def sems(*dims):
        return pltpu.SemaphoreType.DMA(dims)

    scratch = dict(
        xp=coarse(dm.cs), xh=coarse(dm.ce), xc=coarse(dm.ce), xz2=coarse(dm.ce), xz1=coarse(dm.ce),
        own_skip=blocks(dm.cs, S, R + 2), xs=blocks(dm.cs, 2, nx, S + 2, E),
        own_cot=blocks(dm.cd, S, R), cots=blocks(dm.cd, nx, S, RB),
        d1=pltpu.VMEM((S + 2, E, cin3, LANES), BF16), xd=fine(), xz4=fine(), xz3=fine(),
        z1=f32(Q, dm.ce), z2=f32(Q, dm.ce), z3=f32(S * RB, dm.cf), z4=f32(S * RB, dm.cf),
        du_c=f32(Q, dm.ce), du_f=f32(S * RB, dm.cf), gg=f32(S * RB, dm.cf), cg=f32(Q, dm.ce),
        pre=f32(S + 2, E, dm.g), alpha=f32(S + 2, E, 1), pg=pltpu.VMEM((S * RB, dm.g, LANES), BF16),
        ug=f32(S, RB + 6, nx * dm.ce), cb=f32(S, H + 2, nx * dm.ce), dt=f32(S + 2, H, dm.enc_all),
        gv=f32(nc, dm.cs), sgp=f32(nx, S * RB, dm.cs), sgb=blocks(dm.cs, nx, S * RB), sgi=blocks(dm.cs, nx, S * RB),
        ob=blocks(dm.cd, nx, S * RB), oi=blocks(dm.cd, nx, S * RB),
        dzt=pltpu.VMEM((S, (RB + 4) * LANES, LANES), BF16), dzct=pltpu.VMEM((Q * LANES + 2 * dm.hcols, LANES), BF16),
        gw=f32(2 * LANES), dense=pltpu.VMEM((max(3 * cv.c for cv in convs), 3 * LANES), F32),
        fs=blocks(dm.ce, 3, nx, Q), fr=blocks(dm.ce, 3, nx, Q), fm=f32(nx, Q, dm.ce),
        st=f32(4, nd, 1), su=f32(4, nd * nx, 1), sv=pltpu.VMEM((1, nd * nx, gq, 3 * LANES), F32),
        norm_all=f32(nc, 8), rows=f32(max(dm.cs, dm.cd) * S * R),
        turned=f32(max(cv.chunks for cv in convs) * LANES),
        acc=pltpu.VMEM((max(3 * cv.c for cv in convs), 3 * LANES), F32),
        gate_all=pltpu.VMEM((nc, gq, 3 * LANES), F32), gate_t=pltpu.VMEM((2 * LANES, dm.g), F32),
        gate_own=pltpu.VMEM((nx * (dm.ce + dm.cs), dm.g), F32), gate_block=pltpu.VMEM((nc, gq, 3 * LANES), F32),
        **{f"wt{i}": pltpu.VMEM((3, cv.c, cv.wide), cv.kind) for i, cv in enumerate(convs)},
        **{
            f"wf{i}": pltpu.VMEM((cv.taps, 3 * cv.c) if i < 2 else (nx, cv.stored, 9 * cv.c), BF16)
            for i, cv in enumerate(convs)
        },
        **{f"wx{i}": pltpu.VMEM((nc, 3, cv.needed, cv.wide), cv.kind) for i, cv in enumerate(convs)},
        **{
            f"wb{i}": pltpu.VMEM((9 * cv.needed, 3 * nc * cv.o) if i < 2 else (3 * cv.needed, 9 * nc * cv.o), BF16)
            for i, cv in enumerate(convs)
        },
        flip=pltpu.VMEM((max(cv.tiles for cv in convs[2:]) * LANES, max(3 * cv.c for cv in convs[2:])), F32),
        **{f"gt{i}": tiles(cv.share * nd) for i, cv in enumerate(convs)},
        **{f"gr{i}": tiles(nd if i == 0 else nd // 2, cv.share) for i, cv in enumerate(convs)},
        **{f"gp{i}": tiles(nd // 2 * cv.share) for i, cv in enumerate(convs) if i > 0},
        **{f"ga{i}": tiles(cv.share * nd) for i, cv in enumerate(convs)},
        **{f"gs{i}": tiles(nx, convs[i].count) for i in (2, 3)},
        **{f"gx{i}": tiles(nx, convs[i].count) for i in (2, 3)},
        g_send=sems(len(GATHERS), 3, nx), g_recv=sems(len(GATHERS), 3),
        h_send=sems(len(GATHERS), 2 + nx), h_recv=sems(len(GATHERS)),
        x_send=sems(len(FINE), 3, 5), x_recv=sems(len(FINE), 3, 5),
        y_send=sems(len(FINE), 3), y_recv=sems(len(FINE), 3),
        t_send=sems(4), t_recv=sems(4), u_send=sems(5), u_recv=sems(5),
        f_send=sems(3, nx), f_recv=sems(3, nx), w_send=sems(4, nx + 1, nc), w_recv=sems(4, nx + 1, nc),
        p_send=sems(2, nx), p_recv=sems(2, nx), c_send=sems(2, nx), c_recv=sems(2, nx),
        o_send=sems(3, nx), o_recv=sems(3, nx), v_send=sems(2, nc), v_recv=sems(2, nc),
        r_send=sems(4), r_recv=sems(4), a_send=sems(4), a_recv=sems(4), q_send=sems(4, 2), q_recv=sems(4, 2),
    )
    vmem = pl.BlockSpec(memory_space=pltpu.VMEM)
    out, sg, grad1, grad2, grad3, grad4, ggate, gvector, gen, gdn = pl.pallas_call(
        functools.partial(kernel, dm, (*inputs, *outs, *scratch)),
        out_shape=tuple(outs.values()),
        in_specs=[vmem] * len(inputs),
        out_specs=[vmem] * len(outs),
        scratch_shapes=list(scratch.values()),
        compiler_params=pltpu.CompilerParams(
            has_side_effects=True, collective_id=0, vmem_limit_bytes=60 * 1024 * 1024
        ),
        name="step",
    )(*inputs.values())
    grads = (grad1, grad2, ggate, gvector, grad3, grad4, gen, gdn)
    operands = (out, sg, *params, *grads, *states)
    updated = (
        shape(cotangent.shape, BF16),
        shape(skip.shape, F32),
        *(shape(p.shape, F32) for p in params for _ in range(3)),
    )
    anywhere = pl.BlockSpec(memory_space=pl.ANY)
    return pl.pallas_call(
        update_kernel,
        out_shape=updated,
        in_specs=[anywhere] * len(operands),
        out_specs=[anywhere] * len(updated),
        scratch_shapes=[
            *(pltpu.VMEM(a.shape, a.dtype) for a in operands),
            *(pltpu.VMEM(a.shape, a.dtype) for a in updated),
            pltpu.SemaphoreType.DMA((len(operands),)),
            pltpu.SemaphoreType.DMA((len(updated),)),
        ],
        compiler_params=pltpu.CompilerParams(vmem_limit_bytes=60 * 1024 * 1024),
        name="update",
    )(*operands)


def solution(mesh):
    volume = P("chan", "depth", None, None)
    row, column, norms = P("chan", None), P(None, "chan"), P(None, None, "chan")
    params = (row, row, row, column, row, row, norms, norms)
    return jax.shard_map(
        per_device,
        mesh=mesh,
        in_specs=(volume, volume) + params * 3,
        out_specs=(volume, volume) + tuple(spec for spec in params for _ in range(3)),
        check_vma=False,
    )
```

```python
import functools
import types

import jax
import jax.numpy as jnp
from jax import lax
from jax.experimental import pallas as pl
from jax.experimental.pallas import tpu as pltpu
from jax.sharding import PartitionSpec as P

STEP = 5
EPS = 1e-05
CONV_RATE = 0.03
GATE_RATE = 0.1
VECTOR_RATE = 0.5
LANES = 128
MESH = pl.DeviceIdType.MESH
F32 = jnp.float32
BF16 = jnp.bfloat16


def iota(shape, dim):
    return lax.broadcasted_iota(jnp.int32, shape, dim)


def dot(a, b):
    return jnp.dot(a, b, preferred_element_type=F32)


def dot_nt(a, b):
    return lax.dot_general(a, b, (((1,), (1,)), ((), ())), preferred_element_type=F32)


def dot_tn(a, b):
    return lax.dot_general(a, b, (((0,), (0,)), ((), ())), preferred_element_type=F32)


def sigmoid(v):
    return 0.5 * jnp.tanh(0.5 * v) + 0.5


def from_left(v, width):
    return jnp.where(iota(v.shape, 1) % width == 0, 0.0, pltpu.roll(v, 1, 1))


def from_right(v, width):
    return jnp.where(iota(v.shape, 1) % width == width - 1, 0.0, pltpu.roll(v, LANES - 1, 1))


def halves(low, high):
    return pltpu.roll(jnp.where(iota(low.shape, 1) < LANES // 2, low, high), LANES // 2, 1)


def split(v):
    high = v.astype(BF16)
    return jnp.concatenate([high, (v - high.astype(F32)).astype(BF16)], 1)


def storage(block):
    return BF16 if block % 16 == 0 else F32


def flat(ref, s, r):
    if len(ref.shape) == 4:
        return ref[s, r]
    v = ref[:, :, s, r]
    return jnp.concatenate([v[c, i] for i in range(v.shape[1]) for c in range(2)], 0).astype(BF16)


class Dims:
    def __init__(self, nd, nc, skip, enc, dec, gate):
        self.nd, self.nc, self.nx = nd, nc, nc // 2
        self.s, self.rows, self.cols = skip[1:]
        self.cs, self.ce, self.cd, self.g = skip[0], enc, dec, gate
        self.half, self.hcols = self.rows // 2, self.cols // 2
        self.fine_total = nd * self.s * self.rows * self.cols
        self.coarse_total = self.fine_total // 8
        self.enc_all = nc * enc
        self.skip_all = nc * skip[0]
        self.dec_all = nc * dec
        self.rb = self.rows // self.nx
        self.ext = self.rb + 2
        self.cf = self.nx * dec


GATHERS = ("pooled", "skip", "hidden", "coarse", "dz2", "dz1")
FINE = ("hidden", "dz4", "dz3")


class Conv:
    def __init__(self, dm, o, c, blocks):
        self.o, self.c, self.blocks = o, c, blocks
        self.length = 27 * c
        self.chunks = -(-self.length // LANES)
        self.per = LANES // o
        self.tiles = -(-9 // self.per)
        self.wide = self.tiles * LANES
        self.kind = storage(min(size for size, _, _ in blocks))
        self.needed = sum(size for size, _, _ in blocks)
        self.full = max(1, 9 // self.per)
        self.left = max(0, 9 - self.full * self.per)
        self.group = 3 * self.full + (self.left > 0)
        self.count = c // 16 * self.group
        self.share = -(-self.count // dm.nd)
        self.taps = 9 * o
        self.stored = -(-3 * o // 16) * 16


def kernel(dm, names, *refs):
    k_ = types.SimpleNamespace(**dict(zip(names, refs)))
    nd, nc, nx, S, R, H = dm.nd, dm.nc, dm.nx, dm.s, dm.rows, dm.half
    W, V = dm.cols, dm.hcols
    Q, RB, E = H // 2, dm.rb, dm.ext
    place = lax.axis_index("depth")
    me = lax.axis_index("chan")
    x, core = lax.div(me, 2), lax.rem(me, 2)
    other = 1 - core
    mate = 2 * x + other
    row0, h0 = x * RB, x * (RB // 2)
    first, last = place == 0, place == nd - 1
    top, bottom = x == 0, x == nx - 1
    convs = dm.convs
    pending = []
    wt, wf, wx, wb = ([getattr(k_, f"{kind}{i}") for i in range(4)] for kind in ("wt", "wf", "wx", "wb"))
    gp = (k_.gp1, k_.gp2, k_.gp3)
    gt, gr, ga = ([getattr(k_, f"{kind}{i}") for i in range(4)] for kind in ("gt", "gr", "ga"))
    weights = (k_.w0, k_.w1, k_.w2, k_.w3)
    grads = (k_.g0, k_.g1, k_.g2, k_.g3)
    turned, acc = k_.turned, k_.acc

    def no(cond):
        return jnp.logical_not(cond)

    def peer_copy(src, dst, send, recv, depth, chan):
        return pltpu.make_async_remote_copy(
            src_ref=src, dst_ref=dst, send_sem=send, recv_sem=recv,
            device_id={"depth": depth, "chan": chan}, device_id_type=MESH,
        )

    def guarded(cond, fn):
        if cond is None:
            fn()
        else:
            pl.when(cond)(fn)

    def drain(count=None):
        for cond, fn in pending[:count]:
            guarded(cond, fn)
        del pending[:count]

    def launch(cond, copy):
        guarded(cond, lambda: copy().start())
        pending.append((cond, lambda: copy().wait_send()))

    def arrive(cond, copy):
        guarded(cond, lambda: copy().wait_recv())

    def both(a, b):
        return b if a is None else a if b is None else jnp.logical_and(a, b)

    can_send = (no(last), None, no(first))
    can_recv = (no(first), None, no(last))

    def slices(side, n):
        return (pl.ds(n, 1), pl.ds(1, n), pl.ds(1, 1))[side], (pl.ds(0, 1), pl.ds(1, n), pl.ds(n + 1, 1))[side]

    def at_x(t):
        up, down = x + t, x - t
        return jnp.where(up >= nx, up - nx, up), jnp.where(down < 0, down + nx, down)


    def gather_start(ref, which, source_at=None):
        n = ref.shape[2] - 2
        k = GATHERS.index(which)
        for side in (0, 2, 1):
            own, theirs = slices(side, n)
            for t in range(nx):
                if side == 1 and t == 0:
                    continue
                tox = at_x(t)[0]

                def copy(side=side, t=t, own=own, theirs=theirs, tox=tox):
                    start = (n, 1, 1)[side] - 1
                    size = (1, n, 1)[side]
                    src = ref.at[core, x, own] if source_at is None else source_at(pl.ds(start, size), tox)
                    return peer_copy(
                        src, ref.at[core, x, theirs], k_.g_send.at[k, side, t], k_.g_recv.at[k, side],
                        place + 1 - side, 2 * tox + core,
                    )

                launch(can_send[side], copy)
        gather_own(ref, which)

    def handed(ref, k, piece, i):
        return peer_copy(piece, piece, k_.h_send.at[k, i], k_.h_recv.at[k], place, mate)

    def gather_own(ref, which):
        k = GATHERS.index(which)
        launch(None, lambda: handed(ref, k, ref.at[core, x, pl.ds(1, ref.shape[2] - 2)], 0))

    def gather_pass(ref, which):
        n = ref.shape[2] - 2
        k = GATHERS.index(which)
        for side in (1, 0, 2):
            theirs = slices(side, n)[1]
            if side != 1:
                pieces = [ref.at[core, :, theirs]]
            else:
                pieces = [ref.at[core, at_x(t)[1], theirs] for t in range(1, nx)]
            for i, got in enumerate(pieces):
                arrive(
                    can_recv[side],
                    lambda got=got, side=side: peer_copy(
                        got, got, k_.g_send.at[k, side, 0], k_.g_recv.at[k, side], place, mate
                    ),
                )
                launch(None, lambda got=got, i=i, side=side: handed(ref, k, got, 1 + (side // 2 if side != 1 else 2 + i)))

    def gather_wait(ref, which):
        handed(ref, GATHERS.index(which), ref.at[other], 0).wait_recv()

    def fine_parts(ref, which, side):
        k = FINE.index(which)
        own, theirs = slices(side, S)
        inner = pl.ds(1, RB)
        rows = [(None, None, inner, inner, x, core, core)] if side != 1 else [(None, None, inner, inner, x, other, other)]
        if nx > 1:
            for c in range(2):
                rows.append((no(top), no(bottom), pl.ds(1, 1), pl.ds(E - 1, 1), x - 1, c, c))
                rows.append((no(bottom), no(top), pl.ds(RB, 1), pl.ds(0, 1), x + 1, c, c))
        parts = []
        for i, (sends, gets, row, at, tox, to, source) in enumerate(rows):
            target = ref.at[core, theirs, at]
            theirs_ = ref.at[source, theirs, at]
            up = (i - 1) % 2
            arrived = 0 if i == 0 else 1 + up * 2 + core
            expected = 0 if i == 0 else 1 + up * 2 + source
            send = k_.x_send.at[k, side, i]
            parts.append((
                both(can_send[side], sends), both(can_recv[side], gets),
                functools.partial(
                    peer_copy, ref.at[core, own, row], target, send, k_.x_recv.at[k, side, arrived],
                    place + 1 - side, 2 * tox + to,
                ),
                functools.partial(peer_copy, theirs_, theirs_, send, k_.x_recv.at[k, side, expected], place, mate),
            ))
        return parts

    def fine_start(ref, which):
        for side in (0, 2, 1):
            for sends, _, out, _ in fine_parts(ref, which, side):
                launch(sends, out)

    def fine_halo(ref, which, side, c):
        k = FINE.index(which)
        block = ref.at[c, slices(side, S)[1], pl.ds(1, RB)]
        return peer_copy(block, block, k_.y_send.at[k, side], k_.y_recv.at[k, side], place, mate)

    def fine_pass(ref, which):
        for side in (0, 2):
            _, gets, _, back = fine_parts(ref, which, side)[0]
            arrive(gets, back)
            launch(gets, functools.partial(fine_halo, ref, which, side, core))

    def fine_wait(ref, which):
        for side in (1, 0, 2):
            for _, gets, _, back in fine_parts(ref, which, side)[side != 1 :]:
                arrive(gets, back)
            if side != 1:
                arrive(can_recv[side], functools.partial(fine_halo, ref, which, side, other))

    def natural(ref, s, r):
        v = ref[:, s, r]
        size = dm.cd
        return jnp.concatenate(
            [v[c, i * size : (i + 1) * size] for i in range(nx) for c in range(2)], 0
        ).astype(BF16)

    def in_turn(count, fn):
        if count <= 16:
            for i in range(count):
                fn(i)
        else:

            def body(i, carry):
                fn(i)
                return carry

            lax.fori_loop(0, count, body, 0)

    def slab_peers(i):
        to = place + 1 + i
        return jnp.where(to >= nd, to - nd, to), me

    def wide_peers(i):
        i = i + 1
        dt, xt = (i // nx, i % nx) if isinstance(i, int) else (lax.div(i, nx), lax.rem(i, nx))
        to, tox = place + dt, x + xt
        return jnp.where(to >= nd, to - nd, to), 2 * jnp.where(tox >= nx, tox - nx, tox) + core

    def exchange(n, peers, copy):
        in_turn(n - 1, lambda i: copy(*peers(i)).start())

    def sum_start(group, ref, k, slot, tile, source=None):
        n, own, peers, send, recv = group
        ref[slot, own] = tile

        def copy(depth, chan):
            src = ref.at[slot, own] if source is None else source(chan)
            return peer_copy(src, ref.at[slot, own], send.at[k], recv.at[k], depth, chan)

        exchange(n, peers, copy)
        pending.append((None, lambda: all_of(group, ref, k, slot).wait_send()))

    def all_of(group, ref, k, slot):
        n, _, _, send, recv = group
        every = ref.at[slot, pl.ds(0, n - 1)]
        return peer_copy(every, every, send.at[k], recv.at[k], place, mate)

    def sum_finish(group, ref, k, slot):
        all_of(group, ref, k, slot).wait_recv()
        return jnp.sum(ref[slot], axis=0)

    slabs = (nd, place, slab_peers, k_.t_send, k_.t_recv)
    everyone = (nd * nx, place * nx + x, wide_peers, k_.u_send, k_.u_recv)

    def columns_of(row, m):
        lane, channel = iota((m, LANES), 1), iota((m, LANES), 0)
        return tuple(
            jnp.sum(jnp.where(lane == channel + i * m, row, 0.0), axis=1, keepdims=True) for i in range(2)
        )

    def coarse_sums(slot, sums):
        sum_start(slabs, k_.st, slot, slot, pack(*sums))

    def coarse_totals(slot):
        return columns_of(sum_finish(slabs, k_.st, slot, slot), dm.ce)

    def fine_sums(slot, sums):
        sum_start(everyone, k_.su, slot, slot, pack(*sums))

    def fine_totals(slot):
        return columns_of(sum_finish(everyone, k_.su, slot, slot), dm.cf)

    def prepare(k):
        cv, w, own = convs[k], weights[k], wt[k]
        out = wf[k] if k < 2 else wf[k].at[x]
        eye = (iota((LANES, LANES), 0) == iota((LANES, LANES), 1)).astype(BF16)

        def chunk(a):
            return dot_nt(eye, jnp.concatenate([a] * cv.per, 0).astype(BF16))

        full = cv.length // LANES

        def body(i, carry):
            at = pl.multiple_of(i * LANES, LANES)
            turned[pl.ds(at, LANES)] = chunk(w[:, pl.ds(at, LANES)])
            return carry

        lax.fori_loop(0, full, body, 0, unroll=4)
        if full < cv.chunks:
            a = w[:, full * LANES :]
            a = jnp.concatenate([a, jnp.zeros((cv.o, LANES - a.shape[1]), F32)], 1)
            turned[full * LANES : (full + 1) * LANES] = chunk(a)
        group = iota((cv.c, LANES), 1) // cv.o
        for kz in range(3):
            for j in range(cv.tiles):
                tile = None
                for g in range(cv.per):
                    u = j * cv.per + g
                    if u < 9:
                        kx, ky = u // 3, u % 3
                        v = turned[pl.ds(9 * kz + 3 * ky + kx, cv.c, stride=27)]
                        tile = v if tile is None else jnp.where(group == g, v, tile)
                own[kz, :, j * LANES : (j + 1) * LANES] = tile.astype(BF16).astype(own.dtype)
        for j in range(cv.tiles):
            v = jnp.concatenate([own[kz, :, j * LANES : (j + 1) * LANES] for kz in range(3)], 0)
            size = min(LANES, cv.taps - j * LANES)
            v = dot_nt(eye, v.astype(BF16))[0:size]
            if k < 2:
                out[j * LANES : j * LANES + size] = v.astype(BF16)
            else:
                k_.flip[j * LANES : j * LANES + size, 0 : 3 * cv.c] = v
        if k >= 2:
            out[0 : 3 * cv.o] = jnp.concatenate(
                [
                    jnp.concatenate(
                        [
                            k_.flip[(3 * kx + ky) * cv.o : (3 * kx + ky + 1) * cv.o, kz * cv.c : (kz + 1) * cv.c]
                            for kx in range(3)
                        ],
                        0,
                    )
                    for kz in range(3)
                    for ky in range(3)
                ],
                1,
            ).astype(BF16)

    def forward_copy(k, t):
        block = wf[k].at[x]
        return peer_copy(
            block, block, k_.p_send.at[k - 2, t], k_.p_recv.at[k - 2, t], place, 2 * lax.rem(x + t, nx) + core
        )

    def forward_start(k):
        for t in range(1, nx):
            launch(None, functools.partial(forward_copy, k, t))

    def forward_wait(k):
        for t in range(1, nx):
            fromx = lax.rem(x + nx - t, nx)
            block = wf[k].at[fromx]
            peer_copy(
                block, block, k_.p_send.at[k - 2, t], k_.p_recv.at[k - 2, t], place, 2 * fromx + core
            ).wait_recv()

    def forward_weight(k):
        return jnp.concatenate([wf[k][i, 0 : 3 * convs[k].o] for i in range(nx)], 0)

    def weights_start(k):
        cv = convs[k]
        for b, (size, start, at) in enumerate(cv.blocks):
            wx[k][me, :, at : at + size] = wt[k][:, pl.ds(start(me), size)]
            for t in range(1, nc):
                to = lax.rem(me + t, nc)

                def copy(to=to, t=t, b=b, size=size, start=start, at=at):
                    return peer_copy(
                        wt[k].at[:, pl.ds(start(to), size)], wx[k].at[me, :, pl.ds(at, size)],
                        k_.w_send.at[k, b, t], k_.w_recv.at[k, b, t], place, to,
                    )

                launch(None, copy)

    def weights_finish(k):
        cv = convs[k]
        for b, (size, _, at) in enumerate(cv.blocks):
            for t in range(1, nc):
                source = lax.rem(me + nc - t, nc)
                theirs = wx[k].at[source, :, pl.ds(at, size)]
                peer_copy(theirs, theirs, k_.w_send.at[k, b, t], k_.w_recv.at[k, b, t], place, source).wait_recv()

        parts = 9 if k < 2 else 3
        lanes = cv.taps // parts
        for i in range(parts):
            at = (parts - 1 - i) * lanes
            found = [wx[k][j, 2 - kz, :, at : at + lanes].astype(F32) for kz in range(3) for j in range(nc)]
            wb[k][i * cv.needed : (i + 1) * cv.needed] = jnp.concatenate(found, 1).astype(BF16)

    def tiles_of(k, part, put):
        cv, dense = convs[k], k_.dense
        rows, size = 3 * cv.c, 3 * cv.o
        for ky in range(3):
            at = ky * LANES + part * size
            dense[0:rows, ky * size : (ky + 1) * size] = acc[0:rows, at : at + size]

        def tile(i, carry):
            left = []
            for kz in range(3):
                at = pl.ds(pl.multiple_of(kz * cv.c + i * 16, 16), 16)
                for j in range(cv.full):
                    put(i * cv.group + kz * cv.full + j, dense[at, j * LANES : (j + 1) * LANES].astype(BF16))
                left.append(dense[at, cv.full * LANES : cv.full * LANES + cv.left * cv.o])
            if cv.left:
                used = 3 * cv.left * cv.o
                v = jnp.concatenate(left + [jnp.zeros((16, LANES - used), F32)], 1)
                put(i * cv.group + 3 * cv.full, v.astype(BF16))
            return carry

        lax.fori_loop(0, cv.c // 16, tile, 0, unroll=2)

    def cross_start(k):
        gs, gx = (k_.gs2, k_.gs3)[k - 2], (k_.gx2, k_.gx3)[k - 2]

        for part in range(nx):

            def put(i, v, part=part):
                gs[part, i] = v

            tiles_of(k, part, put)
        for t in range(1, nx):

            def copy(t=t):
                tox = at_x(t)[0]
                return peer_copy(
                    gs.at[tox], gx.at[x], k_.c_send.at[k - 2, t], k_.c_recv.at[k - 2, t], place, 2 * tox + core
                )

            launch(None, copy)

    def cross_finish(k):
        cv, gs, gx = convs[k], (k_.gs2, k_.gs3)[k - 2], (k_.gx2, k_.gx3)[k - 2]
        sources = [at_x(t)[1] for t in range(1, nx)]
        for t, fromx in enumerate(sources, 1):
            theirs = gx.at[fromx]
            peer_copy(
                theirs, theirs, k_.c_send.at[k - 2, t], k_.c_recv.at[k - 2, t], place, 2 * fromx + core
            ).wait_recv()

        def add(i, carry):
            for j in range(cv.group):
                p = cv.group * i + j
                v = gs[x, p].astype(F32)
                for fromx in sources:
                    v += gx[fromx, p].astype(F32)
                gt[k][p] = v.astype(BF16)
            return carry

        lax.fori_loop(0, cv.c // 16, add, 0, unroll=2)
        reduce_send(k)

    def reduce_start(k):
        def put(i, v):
            gt[k][i] = v

        tiles_of(k, 0, put)
        reduce_send(k)

    nh = nd // 2
    par, rank = lax.rem(place, 2), lax.div(place, 2)
    partner = place + 1 - 2 * par

    def rank_peers(i):
        to = rank + 1 + i
        return 2 * jnp.where(to >= nh, to - nh, to) + par, me

    def half_of(k, which):
        size = nh * convs[k].share
        return pl.ds(which * size, size)

    def share_of(k, owner):
        size = convs[k].share
        if k == 0:
            return pl.ds(owner * size, size)
        return pl.ds((lax.rem(owner, 2) * nh + lax.div(owner, 2)) * size, size)

    def level(k):
        return (nd, slab_peers, place) if k == 0 else (nh, rank_peers, rank)

    def pair_copy(src, dst, k, i):
        return peer_copy(src, dst, k_.q_send.at[k, i], k_.q_recv.at[k, i], partner, me)

    def reduce_send(k):
        cv = convs[k]
        for i in range(cv.count, cv.share * nd):
            gt[k][i] = jnp.zeros((16, LANES), BF16)
        if k == 0:
            spread_shares(k)
        else:
            launch(None, lambda: pair_copy(gt[k].at[half_of(k, 1 - par)], gp[k - 1], k, 0))

    def pair_finish(k):
        pair_copy(gp[k - 1], gp[k - 1], k, 0).wait_recv()
        own = half_of(k, par)
        gt[k][own] = (gt[k][own].astype(F32) + gp[k - 1][...].astype(F32)).astype(BF16)
        spread_shares(k)

    def spread_shares(k):
        n, peers, own = level(k)
        gr[k][own] = gt[k][share_of(k, place)]

        def copy(to, chan):
            return peer_copy(gt[k].at[share_of(k, to)], gr[k].at[own], k_.r_send.at[k], k_.r_recv.at[k], to, chan)

        exchange(n, peers, copy)
        pending.append((None, lambda: reduce_all(k).wait_send()))

    def reduce_all(k):
        every = gr[k].at[pl.ds(0, level(k)[0] - 1)]
        return peer_copy(every, every, k_.r_send.at[k], k_.r_recv.at[k], place, mate)

    def share_all(k):
        every = ga[k].at[pl.ds(0, (level(k)[0] - 1) * convs[k].share)]
        return peer_copy(every, every, k_.a_send.at[k], k_.a_recv.at[k], place, mate)

    def reduce_finish(k):
        reduce_all(k).wait_recv()
        own = share_of(k, place)
        ga[k][own] = jnp.sum(gr[k][...].astype(F32), axis=0).astype(BF16)

        def copy(to, chan):
            return peer_copy(ga[k].at[own], ga[k].at[own], k_.a_send.at[k], k_.a_recv.at[k], to, chan)

        n, peers, _ = level(k)
        exchange(n, peers, copy)
        pending.append((None, lambda: share_all(k).wait_send()))

    def share_pass(k):
        share_all(k).wait_recv()
        own = ga[k].at[half_of(k, par)]
        launch(None, lambda: pair_copy(own, own, k, 1))

    def gradient_out(k):
        cv, out = convs[k], grads[k]
        if k == 0:
            share_all(k).wait_recv()
        else:
            theirs = ga[k].at[half_of(k, 1 - par)]
            pair_copy(theirs, theirs, k, 1).wait_recv()
        group = iota((16, LANES), 1) // cv.o

        def scatter(i, carry):
            def put(v, g, kz, t):
                turned[pl.ds(9 * kz + t + i * (16 * 27), 16, stride=27)] = jnp.where(group == g, v, 0.0)

            for kz in range(3):
                for j in range(cv.full):
                    v = ga[k][i * cv.group + kz * cv.full + j].astype(F32)
                    for g in range(min(cv.per, 9)):
                        put(v, g, kz, j * cv.per + g)
            if cv.left:
                v = ga[k][i * cv.group + 3 * cv.full].astype(F32)
                for kz in range(3):
                    for g in range(cv.left):
                        put(v, kz * cv.left + g, kz, cv.full * cv.per + g)
            return carry

        lax.fori_loop(0, cv.c // 16, scatter, 0, unroll=2)

        pick = (iota((cv.o, LANES), 1) % cv.o == iota((cv.o, LANES), 0)).astype(BF16)
        step = 8 * LANES
        for at in range(0, cv.length, step):
            size = min(step, cv.length - at)
            v = dot_nt(pick, turned[at : at + -(-size // LANES) * LANES].astype(BF16))
            out[:, at : at + size] = v[:, 0:size]

    def column(row):
        n = row.shape[1]
        eye = iota((n, n), 0) == iota((n, n), 1)
        return jnp.sum(jnp.where(eye, row, 0.0), axis=1, keepdims=True)

    def row_of(col):
        n = col.shape[0]
        eye = iota((n, n), 0) == iota((n, n), 1)
        return jnp.sum(jnp.where(eye, col, 0.0), axis=0, keepdims=True)

    def clear_halos(ref):
        def clear(at):
            if len(ref.shape) == 5:
                for c in range(2):
                    ref[c, at] = jnp.zeros(ref.shape[2:], ref.dtype)
            else:
                for i in range(nx):
                    ref[core, i, at] = jnp.zeros(ref.shape[3:], ref.dtype)

        pl.when(first)(lambda: clear(0))
        pl.when(last)(lambda: clear(ref.shape[-4] - 1))

    def clear_rows(ref):
        def clear(at):
            for c in range(2):
                for i in range(S + 2):
                    ref[c, i, at] = jnp.zeros(ref.shape[3:], ref.dtype)

        pl.when(top)(lambda: clear(0))
        pl.when(bottom)(lambda: clear(E - 1))

    def conv(operand, weight, m, groups, emit, init):
        def body(d, carry):
            v = operand(d)
            y = dot(weight, v)
            results = []
            for j in range(RB):
                lanes = slice(j * LANES, (j + 1) * LANES)
                parts = []
                for g in range(groups):
                    a = [y[(3 * g + kx) * m : (3 * g + kx + 1) * m, lanes] for kx in range(3)]
                    parts.append(from_left(a[0], W) + a[1] + from_right(a[2], W))
                results.append(jnp.concatenate(parts, 0) if groups > 1 else parts[0])
            return emit(d, results, carry)

        return lax.fori_loop(0, S, body, init)

    def rows_of(row):
        return lambda d: jnp.concatenate(
            [jnp.concatenate([row(d + kz, ky + j) for j in range(RB)], 1) for kz in range(3) for ky in range(3)], 0
        )

    def blocks_of(ref):
        size = dm.cd
        return lambda d: jnp.concatenate(
            [
                jnp.concatenate([ref[c, d + kz, 2 - ky + j, i * size : (i + 1) * size] for j in range(RB)], 1)
                for kz in range(3)
                for i in range(nx)
                for c in range(2)
                for ky in range(3)
            ],
            0,
        ).astype(BF16)

    def conv_stats(row, weight, z):
        def emit(d, results, carry):
            total, square = carry
            for j, v in enumerate(results):
                z[d * RB + j] = v
                total, square = total + v, square + v * v
            return total, square

        blank = jnp.zeros((dm.cf, LANES), F32)
        return conv(rows_of(row), weight, dm.cd, nx, emit, (blank, blank))

    def weight_grad(row, k):
        cv = convs[k]

        def part(d):
            v = jnp.concatenate([jnp.concatenate([row(d + kz, j) for j in range(E)], 1) for kz in range(3)], 0)
            y = jnp.concatenate(
                [k_.dzt[d, (2 - ky) * LANES : (2 - ky + E) * LANES] for ky in range(3)], 1
            )
            return dot(v, y)

        acc[0 : 3 * cv.c] = part(0)

        def more(d, carry):
            acc[0 : 3 * cv.c] += part(d)
            return carry

        lax.fori_loop(1, S, more, 0)

    def conv_coarse(ref, weight, m):
        v = jnp.concatenate(
            [jnp.concatenate([flat(ref, kz, i) for i in range(Q)], 1) for kz in range(3)], 0
        )
        y = dot(weight[...], v)
        blank = jnp.zeros((m, LANES), F32)

        def shifted(ky, i):
            if not 0 <= i < Q:
                return blank
            a, b, c = (
                y[(3 * kx + ky) * m : (3 * kx + ky + 1) * m, i * LANES : (i + 1) * LANES] for kx in range(3)
            )
            return from_left(a, V) + b + from_right(c, V)

        before = [shifted(0, i) for i in range(-1, Q)]
        after = [shifted(2, i) for i in range(Q + 1)]
        return [
            shifted(1, i) + halves(before[i + 1] + after[i + 1], before[i] + after[i]) for i in range(Q)
        ]

    def conv_stats_coarse(ref, weight, z, m):
        total = square = jnp.zeros((m, LANES), F32)
        for i, v in enumerate(conv_coarse(ref, weight, m)):
            z[i] = v
            total, square = total + v, square + v * v
        return total, square

    def weight_grad_coarse(ref, k):
        cv = convs[k]
        v = jnp.concatenate(
            [jnp.concatenate([flat(ref, kz, i) for i in range(Q)], 1) for kz in range(3)], 0
        )
        y = jnp.concatenate([k_.dzct[(2 - ky) * V : (2 - ky) * V + Q * LANES] for ky in range(3)], 1)
        acc[0 : 3 * cv.c] = dot(v, y)

    def pack(a, b):
        m = a.shape[0]
        a = jnp.sum(a, axis=1, keepdims=True)
        b = jnp.sum(b, axis=1, keepdims=True)
        lane, channel = iota((m, LANES), 1), iota((m, LANES), 0)
        both = jnp.where(lane == channel, a, jnp.where(lane == channel + m, b, 0.0))
        return jnp.sum(both, axis=0, keepdims=True)

    def moments(total, count):
        mean = total[0] / count
        var = total[1] / count - mean * mean
        return mean, lax.rsqrt(var + EPS)

    def wide(column):
        return jnp.broadcast_to(column, (column.shape[0], LANES))

    def factors(stats, norm):
        mean, inv = stats
        gain, shift = norm
        return wide(mean), wide(gain * inv), wide(shift)

    def norm_rows(z, stats, norm, emit, n):
        mean, scale, shift = factors(stats, norm)

        def body(i, carry):
            for j in range(n):
                p = i * n + j
                u = (z[p] - mean) * scale + shift
                emit(p, u * sigmoid(u))
            return carry

        lax.fori_loop(0, z.shape[0] // n, body, 0)

    def norm_back_sums(z, keep_du, stats, norm, grad, n):
        mean, scale, shift = factors(stats, norm)
        inv = wide(stats[1])
        m = z.shape[1]

        def body(i, carry):
            a, b = carry
            for j in range(n):
                p = i * n + j
                centred = z[p] - mean
                u = centred * scale + shift
                sigma = sigmoid(u)
                v = grad(p) * sigma * (1.0 + u * (1.0 - sigma))
                keep_du(p, v)
                a, b = a + v, b + v * (centred * inv)
            return a, b

        blank = jnp.zeros((m, LANES), F32)
        return lax.fori_loop(0, z.shape[0] // n, body, (blank, blank))

    def back_factors(stats, norm, total, count):
        mean, inv = stats
        scale = norm[0] * inv
        return wide(mean), wide(scale), wide(-scale * total[0] / count), wide(-scale * inv * total[1] / count)

    def columns_first(copies, groups):
        size = copies[0].shape[0] // groups
        rows = [v[g * size : (g + 1) * size] for g in range(groups) for v in copies]
        used = 3 * groups * size
        if used < LANES:
            rows.append(jnp.zeros((LANES - used, LANES), F32))
        return jnp.transpose(jnp.concatenate(rows, 0)).astype(BF16)

    def norm_back_fine(z, given, ref):
        mean, scale, level, slope = given

        def body(d, carry):
            for r in range(RB):
                p = d * RB + r
                v = scale * k_.du_f[p] + level + slope * (z[p] - mean)
                ref[core, 1 + d, 1 + r] = v.astype(BF16).astype(ref.dtype)
            return carry

        lax.fori_loop(0, S, body, 0)

    def turn_fine(ref):
        n = 4 if RB % 4 == 0 else 2

        def body(i, carry):
            d = lax.div(i, RB // n)
            r0 = (i - d * (RB // n)) * n
            for j in range(n):
                v = ref[core, 1 + d, 1 + r0 + j].astype(F32)
                at = pl.ds(pl.multiple_of((2 + r0 + j) * LANES, LANES), LANES)
                k_.dzt[d, at] = columns_first((from_right(v, W), v, from_left(v, W)), nx)
            return carry

        lax.fori_loop(0, S * RB // n, body, 0)

    def norm_back_coarse(z, given, ref):
        mean, scale, level, slope = given
        for i in range(Q):
            v = scale * k_.du_c[i] + level + slope * (z[i] - mean)
            ref[core, x, 1, i] = v.astype(BF16).astype(ref.dtype)

    def turn_coarse(ref):
        for i in range(Q):
            v = ref[core, x, 1, i].astype(F32)
            k_.dzct[V + i * LANES : V + (i + 1) * LANES] = columns_first((from_right(v, V), v, from_left(v, V)), 1)

    def keep_du(ref):
        def store(p, v):
            ref[p] = v

        return store

    barrier = pltpu.get_barrier_semaphore()

    def greet(depth, chan):
        pl.semaphore_signal(barrier, inc=1, device_id={"depth": depth, "chan": chan}, device_id_type=MESH)

    exchange(nd * nx, wide_peers, lambda depth, chan: types.SimpleNamespace(start=lambda: greet(depth, chan)))
    for t in range(nx):
        to = 2 * at_x(t)[0] + other
        greet(place, to)
        if t > 0:
            pl.when(no(first))(lambda to=to: greet(place - 1, to))
            pl.when(no(last))(lambda to=to: greet(place + 1, to))

    hc = iota((LANES, LANES), 0)
    fc = iota((LANES, LANES), 1)
    half = LANES // 2

    def up_table(coarse, fine):
        base = fine // 2
        beside = jnp.clip(base + jnp.where(fine % 2 == 0, -1, 1), 0, V - 1)
        near = (coarse == base).astype(F32)
        far = (coarse == beside).astype(F32)
        return (0.75 * near + 0.25 * far).astype(BF16)

    pool = jnp.concatenate([(hc // 2 == fc - at).astype(BF16) for at in (0, half)], 0)
    spread = jnp.concatenate([(hc - at == fc // 2).astype(BF16) for at in (0, half)], 1)
    up = jnp.concatenate([up_table(hc - at, fc) for at in (0, half)], 1)
    down = jnp.concatenate([up_table(fc, hc)] * 2, 0)
    spread2 = jnp.concatenate([spread, spread], 0)

    def take_rows(ref):
        for c in range(ref.shape[0]):
            k_.rows[c * S * R : (c + 1) * S * R] = ref[c].astype(F32).reshape(S * R, LANES)

    def row_of_all(p, chans):
        return k_.rows[pl.ds(p, chans, stride=S * R)]

    xp, xs, own_skip = k_.xp, k_.xs, k_.own_skip
    clear_halos(xp)
    take_rows(k_.skip)
    for i in range(S):
        for r in (0, R + 1):
            own_skip[i, r] = jnp.zeros((dm.cs, LANES), own_skip.dtype)

    def take_skip(i, carry):
        parts = []
        for d in range(S):
            v = [row_of_all(d * R + 4 * i + j, dm.cs).astype(BF16) for j in range(4)]
            for j in range(4):
                own_skip[d, 1 + 4 * i + j] = v[j].astype(own_skip.dtype)
            parts += [jnp.concatenate([v[j], v[2 + j]], 1) for j in range(2)]
        v = dot(jnp.concatenate(parts, 0), pool).reshape(2 * S, dm.cs, LANES)
        xp[core, x, 1, i] = (jnp.sum(v, axis=0) * 0.125).astype(BF16).astype(xp.dtype)
        return carry

    lax.fori_loop(0, Q, take_skip, 0, unroll=3)
    beside = jnp.where(first, 0, 1) + jnp.where(last, 0, 1)
    pl.semaphore_wait(barrier, nd * nx - 1 + nx + (nx - 1) * beside)
    gather_start(xp, "pooled")
    clear_halos(xs)
    xs[core, x, 1 : S + 1] = own_skip[:, pl.ds(row0, E)]
    gather_start(xs, "skip", lambda at, tox: own_skip.at[at, pl.ds(tox * RB, E)])

    gq = dm.g // nc
    columns = dm.enc_all + dm.skip_all
    gate_all, norm_all = k_.gate_all, k_.norm_all
    gate_all[me, :, 0:columns] = k_.gate[...]
    lane = iota((gq, LANES), 1)
    gate_all[me, :, 2 * LANES :] = jnp.where(
        lane == 0, column(k_.vector[0:1]), jnp.where(lane == 1, column(k_.vector[1:2]), 0.0)
    )
    for layer in range(2):
        for part in range(2):
            at = 2 * layer + part
            norm_all[me, at : at + 1, 0 : dm.cd] = k_.dn[part, layer : layer + 1]

    def constants(i, t, source, to):
        ref = (norm_all, gate_all)[i]
        return peer_copy(ref.at[source], ref.at[source], k_.v_send.at[i, t], k_.v_recv.at[i, t], place, to)

    for i in range(2):
        for t in range(1, nc):
            launch(None, functools.partial(constants, i, t, me, lax.rem(me + t, nc)))
    prepare(0)
    xd, xz4, xz3, d1 = k_.xd, k_.xz4, k_.xz3, k_.d1
    for ref in (xd, xz4, xz3):
        clear_rows(ref)
        clear_halos(ref)
    for ref in (k_.xh, k_.xz2, k_.xz1):
        clear_halos(ref)
    for i in range(S):
        for at in (0, (RB + 2) * LANES):
            k_.dzt[i, at : at + 2 * LANES] = jnp.zeros((2 * LANES, LANES), BF16)
        for r in range(3):
            k_.ug[i, r] = jnp.zeros(k_.ug.shape[2:], F32)
            k_.ug[i, RB + 3 + r] = jnp.zeros(k_.ug.shape[2:], F32)
        for r in range(H + 2):
            k_.cb[i, r] = jnp.zeros(k_.cb.shape[2:], F32)

    for at in (0, V + Q * LANES):
        k_.dzct[at : at + V] = jnp.zeros((V, LANES), BF16)

    def norm_of(layer):
        return column(k_.en[0, layer : layer + 1]), column(k_.en[1, layer : layer + 1])

    norm_e1, norm_e2 = norm_of(0), norm_of(1)

    gather_pass(xp, "pooled")
    gather_wait(xp, "pooled")
    coarse_sums(0, conv_stats_coarse(xp, wf[0], k_.z1, dm.ce))
    prepare(1)
    stats_e1 = moments(coarse_totals(0), dm.coarse_total)

    def keep_coarse(ref):
        def store(p, v):
            ref[core, x, 1, p] = v.astype(BF16).astype(ref.dtype)

        return store

    norm_rows(k_.z1, stats_e1, norm_e1, keep_coarse(k_.xh), Q)
    gather_start(k_.xh, "hidden")
    prepare(2)
    forward_start(2)
    gather_pass(k_.xh, "hidden")
    gather_pass(xs, "skip")
    gather_wait(k_.xh, "hidden")
    coarse_sums(1, conv_stats_coarse(k_.xh, wf[1], k_.z2, dm.ce))
    take_rows(k_.cot)

    def take_cot(i, carry):
        for d in range(S):
            for j in range(4):
                v = row_of_all(d * R + 4 * i + j, dm.cd).astype(BF16)
                k_.own_cot[d, 4 * i + j] = v.astype(k_.own_cot.dtype)
        return carry

    lax.fori_loop(0, Q, take_cot, 0)
    k_.cots[x] = k_.own_cot[:, pl.ds(row0, RB)]
    stats_e2 = moments(coarse_totals(1), dm.coarse_total)
    norm_rows(k_.z2, stats_e2, norm_e2, keep_coarse(k_.xc), Q)
    gather_start(k_.xc, "coarse")
    prepare(3)
    for t in range(1, nc):
        for i in range(2):
            source = lax.rem(me + nc - t, nc)
            constants(i, t, source, source).wait_recv()
    gate_full = gate_all[...].reshape(dm.g, 3 * LANES)
    wg = gate_full[:, 0:columns].astype(BF16)
    gbias = gate_full[:, 2 * LANES : 2 * LANES + 1]
    gout = gate_full[:, 2 * LANES + 1 : 2 * LANES + 2]
    k_.gate_t[...] = jnp.transpose(gate_full[:, 0 : 2 * LANES])
    own_rows = [k_.gate_t[pl.ds(pl.multiple_of((2 * i + core) * dm.ce, dm.ce), dm.ce)] for i in range(nx)]
    own_rows += [
        k_.gate_t[pl.ds(pl.multiple_of(dm.enc_all + (2 * i + core) * dm.cs, dm.cs), dm.cs)] for i in range(nx)
    ]
    k_.gate_own[...] = jnp.concatenate(own_rows, 0)

    def norm_fine(layer):
        return tuple(
            jnp.concatenate(
                [column(norm_all[2 * i + core, 2 * layer + part : 2 * layer + part + 1, 0 : dm.cd]) for i in range(nx)], 0
            )
            for part in range(2)
        )

    norm_d1, norm_d2 = norm_fine(0), norm_fine(1)
    gather_pass(k_.xc, "coarse")
    gather_wait(k_.xc, "coarse")
    forward_start(3)

    dt = k_.dt

    def up_depth(i, carry):
        t = []
        for j in range(3):
            v = dot(flat(k_.xc, j, i), up)
            t.append(jnp.stack([v[:, 0:LANES], v[:, LANES:]], 0))
        below = jnp.where(first, t[1], t[0])
        above = jnp.where(last, t[1], t[2])
        near = 0.75 * t[1]
        here = 0.25 * t[1]
        rows = pl.ds(i * 2, 2)
        dt[0, rows] = jnp.where(first, 0.0, 0.75 * below + here)
        dt[1, rows] = near + 0.25 * below
        dt[2, rows] = near + 0.25 * above
        dt[3, rows] = jnp.where(last, 0.0, 0.75 * above + here)
        return carry

    lax.fori_loop(0, Q, up_depth, 0)

    def up_rows(i, carry):
        here = h0 + i
        before, after = jnp.maximum(here - 1, 0), jnp.minimum(here + 1, H - 1)
        for j in range(S + 2):
            v = 0.75 * dt[j, here]
            d1[j, 1 + 2 * i, 0 : dm.enc_all] = (v + 0.25 * dt[j, before]).astype(BF16)
            d1[j, 2 + 2 * i, 0 : dm.enc_all] = (v + 0.25 * dt[j, after]).astype(BF16)
        return carry

    lax.fori_loop(0, RB // 2, up_rows, 0)
    for edge, at, near, far in (
        (top, 0, jnp.maximum(h0 - 1, 0), h0),
        (bottom, E - 1, jnp.minimum(h0 + RB // 2, H - 1), h0 + RB // 2 - 1),
    ):
        for j in range(S + 2):
            v = jnp.where(edge, 0.0, 0.75 * dt[j, near] + 0.25 * dt[j, far])
            d1[j, at, 0 : dm.enc_all] = v.astype(BF16)
    for t in range(1, nx):
        tox = lax.rem(x + t, nx)

        def send_cot(t=t, tox=tox):
            return peer_copy(
                k_.own_cot.at[:, pl.ds(tox * RB, RB)], k_.cots.at[x], k_.o_send.at[0, t], k_.o_recv.at[0, t],
                place, 2 * tox + core,
            )

        launch(None, send_cot)

    gather_wait(xs, "skip")
    gate_n = E // 2

    def gate(i, carry):
        j = lax.div(i, 2)
        r0 = (i - 2 * j) * gate_n
        skips = [flat(xs, j, r0 + q) for q in range(gate_n)]
        v = jnp.concatenate(
            [
                jnp.concatenate([d1[j, r0 + q, 0 : dm.enc_all] for q in range(gate_n)], 1),
                jnp.concatenate(skips, 1),
            ],
            0,
        )
        pre = dot(wg, v) + gbias
        act = pre * sigmoid(pre)
        alpha = sigmoid(jnp.sum(gout * act, axis=0, keepdims=True))
        for q in range(gate_n):
            lanes = slice(q * LANES, (q + 1) * LANES)
            d1[j, r0 + q, dm.enc_all :] = (alpha[:, lanes] * skips[q].astype(F32)).astype(BF16)
            k_.pre[j, r0 + q] = pre[:, lanes]
            k_.alpha[j, r0 + q] = alpha[:, lanes]
        return carry

    lax.fori_loop(0, (S + 2) * 2, gate, 0)
    def row_d1(j, r):
        return d1[j, r]

    def row_xd(j, r):
        return natural(xd, j, r)

    forward_wait(2)
    fine_sums(0, conv_stats(row_d1, forward_weight(2), k_.z3))
    forward_wait(3)
    stats_d1 = moments(fine_totals(0), dm.fine_total)

    def keep_dec(p, v):
        d = lax.div(p, RB)
        xd[core, 1 + d, 1 + p - d * RB] = v.astype(BF16).astype(xd.dtype)

    norm_rows(k_.z3, stats_d1, norm_d1, keep_dec, RB)
    fine_start(xd, "hidden")
    weights_start(3)
    weights_start(2)
    for t in range(1, nx):
        fromx = lax.rem(x + nx - t, nx)
        theirs = k_.cots.at[fromx]
        peer_copy(theirs, theirs, k_.o_send.at[0, t], k_.o_recv.at[0, t], place, 2 * fromx + core).wait_recv()
    fine_pass(xd, "hidden")
    fine_wait(xd, "hidden")
    fine_sums(1, conv_stats(row_xd, forward_weight(3), k_.z4))
    stats_d2 = moments(fine_totals(1), dm.fine_total)

    def rows_out(ref, own, theirs, kind, size):
        def copy_rows(read, at):
            def body(d, carry):
                for r in range(RB):
                    p = (d * R + at * RB + r) * size
                    ref[pl.ds(pl.multiple_of(p, size), size)] = read(d * RB + r).astype(F32)
                return carry

            lax.fori_loop(0, S, body, 0)

        copy_rows(lambda p: own[x, p], x)
        for t in range(1, nx):
            fromx = lax.rem(x + nx - t, nx)
            block = theirs.at[fromx]
            peer_copy(block, block, k_.o_send.at[kind, t], k_.o_recv.at[kind, t], place, 2 * fromx + core).wait_recv()
            copy_rows(lambda p, fromx=fromx: theirs[fromx, p], fromx)

    def row_cot(p):
        d = lax.div(p, RB)
        return jnp.concatenate([k_.cots[i, d, p - d * RB] for i in range(nx)], 0).astype(F32)

    fine_sums(2, norm_back_sums(k_.z4, keep_du(k_.du_f), stats_d2, norm_d2, row_cot, RB))

    def keep_result(p, v):
        for i in range(nx):
            k_.ob[i, p] = v[i * dm.cd : (i + 1) * dm.cd].astype(BF16).astype(k_.ob.dtype)

    norm_rows(k_.z4, stats_d2, norm_d2, keep_result, RB)
    total_d2 = fine_totals(2)
    norm_back_fine(k_.z4, back_factors(stats_d2, norm_d2, total_d2, dm.fine_total), xz4)
    fine_start(xz4, "dz4")
    weights_start(1)
    weights_start(0)
    for t in range(1, nx):
        tox = lax.rem(x + t, nx)

        def send_result(t=t, tox=tox):
            return peer_copy(
                k_.ob.at[tox], k_.oi.at[x], k_.o_send.at[1, t], k_.o_recv.at[1, t], place, 2 * tox + core
            )

        launch(None, send_result)
    turn_fine(xz4)
    weight_grad(row_xd, 3)
    fine_pass(xz4, "dz4")
    older = len(pending)
    cross_start(3)
    weights_finish(3)
    fine_wait(xz4, "dz4")

    def keep_grad(d, results, carry):
        for j, v in enumerate(results):
            k_.gg[d * RB + j] = v
        return carry

    conv(blocks_of(xz4), wb[3][...], dm.cf, 1, keep_grad, 0)
    fine_sums(3, norm_back_sums(k_.z3, keep_du(k_.du_f), stats_d1, norm_d1, lambda p: k_.gg[p], RB))
    cross_finish(3)
    total_d1 = fine_totals(3)
    norm_back_fine(k_.z3, back_factors(stats_d1, norm_d1, total_d1, dm.fine_total), xz3)
    fine_start(xz3, "dz3")
    turn_fine(xz3)
    weights_finish(2)
    fine_pass(xz3, "dz3")
    weight_grad(row_d1, 2)
    cross_start(2)
    pair_finish(3)
    rows_out(k_.out, k_.ob, k_.oi, 1, dm.cd)
    fine_wait(xz3, "dz3")

    ups = nx * dm.ce

    def gate_back(d, results, carry):
        bias, psi = carry
        lows = []
        for j, both in enumerate(results):
            p = d * RB + j
            v = both[ups:]
            grad = jnp.sum(v * flat(xs, d + 1, 1 + j).astype(F32), axis=0, keepdims=True)
            alpha = k_.alpha[d + 1, 1 + j]
            logit = grad * alpha * (1.0 - alpha)
            pre = k_.pre[d + 1, 1 + j]
            sigma = sigmoid(pre)
            psi = psi + pre * sigma * logit
            low = (logit * gout * sigma * (1.0 + pre * (1.0 - sigma))).astype(BF16)
            bias = bias + low.astype(F32)
            k_.pg[p] = low
            lows.append(low)
            k_.ug[d, 3 + j] = both[0:ups]
            for i in range(nc):
                k_.gv[i] = v[i * dm.cs : (i + 1) * dm.cs]
            for i in range(nx):
                k_.sgp[i, p] = alpha * k_.gv[2 * i + core]
        back = dot(k_.gate_own[...].astype(BF16), jnp.concatenate(lows, 1))
        for j in range(len(results)):
            p = d * RB + j
            lanes = slice(j * LANES, (j + 1) * LANES)
            k_.ug[d, 3 + j] += back[0:ups, lanes]
            for i in range(nx):
                v = k_.sgp[i, p] + back[ups + i * dm.cs : ups + (i + 1) * dm.cs, lanes]
                k_.sgp[i, p] = v
                k_.sgb[i, p] = v.astype(BF16).astype(k_.sgb.dtype)
        return bias, psi

    blank = jnp.zeros((dm.g, LANES), F32)
    bias, psi = conv(blocks_of(xz3), wb[2][...], ups + dm.skip_all, 1, gate_back, (blank, blank))

    ug, cb, cg = k_.ug, k_.cb, k_.cg
    for q in range(RB // 2 + 2):
        terms = []
        for d in range(S):
            v = 0.75 * (ug[d, 2 * q + 1] + ug[d, 2 * q + 2]) + 0.25 * (ug[d, 2 * q + 3] + ug[d, 2 * q])
            if q == 1:
                v += jnp.where(top, 0.25 * ug[d, 3], 0.0)
            if q == RB // 2:
                v += jnp.where(bottom, 0.25 * ug[d, RB + 2], 0.0)
            terms.append(split(v))
        v = dot(jnp.concatenate(terms, 0), down)
        for d in range(S):
            cb[d, h0 + q] = v[d * ups : (d + 1) * ups]

    def to_slabs(i, carry):
        even, odd = (cb[d, 2 * i + 1] + pltpu.roll(cb[d, 2 * i + 2], half, 1) for d in range(S))
        middle = 0.75 * (even + odd) + jnp.where(first, 0.25 * even, 0.0) + jnp.where(last, 0.25 * odd, 0.0)
        for part, v in enumerate((0.25 * even, middle, 0.25 * odd)):
            for j in range(nx):
                block = v[j * dm.ce : (j + 1) * dm.ce]
                k_.fs[part, j, i] = block.astype(BF16).astype(k_.fs.dtype)
                if part == 1:
                    k_.fm[j, i] = block
        return carry

    lax.fori_loop(0, Q, to_slabs, 0)

    reach = min((RB // 2 + 1) // 2 + 1, Q)

    def reach_of(at):
        return pl.ds(jnp.clip(lax.div(at * (RB // 2) + 1, 2) - 1, 0, Q - reach), reach)

    def fold_parts():
        for step in (-1, 1, 0):
            sends = (no(first), None, no(last))[step + 1]
            gets = (no(last), None, no(first))[step + 1]
            for t in range(nx):
                if (step, t) != (0, 0):
                    tox, fromx = lax.rem(x + t, nx), lax.rem(x + nx - t, nx)
                    sems = (k_.f_send.at[step + 1, t], k_.f_recv.at[step + 1, t])
                    rows = reach_of(x)
                    theirs = k_.fr.at[step + 1, fromx, reach_of(fromx)]
                    yield (
                        sends, gets, fromx, step + 1,
                        functools.partial(
                            peer_copy, k_.fs.at[step + 1, tox, rows], k_.fr.at[step + 1, x, rows], *sems,
                            place + step, 2 * tox + core,
                        ),
                        functools.partial(peer_copy, theirs, theirs, *sems, place, 2 * fromx + core),
                    )

    for sends, _, _, _, out, _ in fold_parts():
        launch(sends, out)
    for t in range(1, nx):
        tox = lax.rem(x + t, nx)

        def send_skip(t=t, tox=tox):
            return peer_copy(
                k_.sgb.at[tox], k_.sgi.at[x], k_.o_send.at[2, t], k_.o_recv.at[2, t], place, 2 * tox + core
            )

        launch(None, send_skip)

    reduce_finish(3)
    cross_finish(2)

    k_.gw[...] = jnp.zeros(k_.gw.shape, F32)

    def gate_weight(d, carry):
        v = jnp.concatenate(
            [
                jnp.concatenate([d1[1 + d, 1 + j, 0 : dm.enc_all] for j in range(RB)], 1),
                jnp.concatenate([flat(xs, 1 + d, 1 + j) for j in range(RB)], 1),
            ],
            0,
        )
        y = jnp.concatenate([k_.pg[d * RB + j] for j in range(RB)], 1)
        k_.gw[0:columns, 0 : dm.g] += dot_nt(v, y)
        return carry

    lax.fori_loop(0, S, gate_weight, 0)
    gate_grad = jnp.transpose(k_.gw[...])
    lane = iota((dm.g, LANES), 1)
    vectors = jnp.where(
        lane == 0,
        jnp.sum(bias, axis=1, keepdims=True),
        jnp.where(lane == 1, jnp.sum(psi, axis=1, keepdims=True), 0.0),
    )
    gate_block = k_.gate_block
    for j in range(nc):
        mine = slice(j * gq, (j + 1) * gq)
        gate_block[j, :, 0 : 2 * LANES] = gate_grad[mine]
        gate_block[j, :, 2 * LANES :] = vectors[mine]
    sum_start(everyone, k_.sv, 4, 0, gate_block[me], lambda chan: gate_block.at[chan])
    cg[...] = k_.fm[x]
    for _, gets, fromx, part, _, back in fold_parts():

        def fold_in(back=back, part=part, fromx=fromx):
            back().wait_recv()
            rows = reach_of(fromx)
            cg[rows] += k_.fr[part, fromx, rows].astype(F32)

        guarded(gets, fold_in)

    coarse_sums(2, norm_back_sums(k_.z2, keep_du(k_.du_c), stats_e2, norm_e2, lambda p: cg[p], Q))
    share_pass(3)
    weights_finish(1)
    total_e2 = coarse_totals(2)
    norm_back_coarse(k_.z2, back_factors(stats_e2, norm_e2, total_e2, dm.coarse_total), k_.xz2)
    gather_start(k_.xz2, "dz2")
    pair_finish(2)
    turn_coarse(k_.xz2)
    weight_grad_coarse(k_.xh, 1)
    gather_pass(k_.xz2, "dz2")
    reduce_start(1)
    weights_finish(0)
    reduce_finish(2)
    rows_out(k_.sg, k_.sgp, k_.sgi, 2, dm.cs)
    drain(older)
    gather_wait(k_.xz2, "dz2")
    for i, v in enumerate(conv_coarse(k_.xz2, wb[1], dm.ce)):
        cg[i] = v
    coarse_sums(3, norm_back_sums(k_.z1, keep_du(k_.du_c), stats_e1, norm_e1, lambda p: cg[p], Q))
    pair_finish(1)
    gradient_out(3)
    total_e1 = coarse_totals(3)
    norm_back_coarse(k_.z1, back_factors(stats_e1, norm_e1, total_e1, dm.coarse_total), k_.xz1)
    gather_start(k_.xz1, "dz1")
    share_pass(2)
    turn_coarse(k_.xz1)
    weight_grad_coarse(xp, 0)
    reduce_start(0)
    reduce_finish(1)
    gather_pass(k_.xz1, "dz1")
    gradient_out(2)
    share_pass(1)
    reduce_finish(0)
    gather_wait(k_.xz1, "dz1")
    for i, v in enumerate(conv_coarse(k_.xz1, wb[0], dm.cs)):
        v = dot(split(v), spread2) * 0.125
        for j in range(4):
            part = v[:, (j // 2) * LANES : (j // 2 + 1) * LANES]
            for d in range(S):
                at = (d * R + 4 * i + j) * dm.cs
                k_.sg[at : at + dm.cs] += part
    gradient_out(1)
    gate_total = sum_finish(everyone, k_.sv, 4, 0)
    k_.ggate[...] = gate_total[:, 0:columns]
    k_.gvector[0:1] = row_of(gate_total[:, 2 * LANES : 2 * LANES + 1])
    k_.gvector[1:2] = row_of(gate_total[:, 2 * LANES + 1 : 2 * LANES + 2])

    def own_part(col):
        parts = [jnp.where(x == i, col[i * dm.cd : (i + 1) * dm.cd], 0.0) for i in range(nx)]
        return functools.reduce(jnp.add, parts)

    for ref, pair, pick in ((k_.gen, (total_e1, total_e2), lambda v: v), (k_.gdn, (total_d1, total_d2), own_part)):
        for layer, total in enumerate(pair):
            ref[0, layer : layer + 1] = row_of(pick(total[1]))
            ref[1, layer : layer + 1] = row_of(pick(total[0]))
    gradient_out(0)
    drain()


def adamw(weight, grad, moment, square, rate):
    new_moment = 0.9 * moment + 0.1 * grad
    new_square = 0.999 * square + 0.001 * grad * grad
    moment_hat = new_moment * (1.0 / (1.0 - 0.9**STEP))
    square_hat = new_square * (1.0 / (1.0 - 0.999**STEP))
    new_weight = weight - rate * (moment_hat / (jnp.sqrt(square_hat) + 1e-08) + 0.01 * weight)
    return (new_weight, new_moment, new_square)


RATES = (CONV_RATE, CONV_RATE, GATE_RATE, VECTOR_RATE, CONV_RATE, CONV_RATE, VECTOR_RATE, VECTOR_RATE)


def update_kernel(*refs):
    n = len(RATES)
    sources, targets = refs[: 2 + 4 * n], refs[2 + 4 * n : 4 + 7 * n]
    inside, outside = refs[4 + 7 * n : 6 + 11 * n], refs[6 + 11 * n : 8 + 14 * n]
    in_sem, out_sem = refs[8 + 14 * n :]
    order = (4, 1, 0, 5, 2, 3, 6, 7)

    def load(i):
        return pltpu.make_async_copy(sources[i], inside[i], in_sem.at[i])

    def store(i):
        return pltpu.make_async_copy(outside[i], targets[i], out_sem.at[i])

    for i in (1, 0):
        load(i).start()
    for k in order:
        for part in range(4):
            load(2 + part * n + k).start()
    for i in (1, 0):
        load(i).wait()
        chans, (slabs, rows) = outside[i].shape[0], outside[i].shape[1:3]
        for c in range(chans):
            v = inside[i][pl.ds(c, slabs * rows, stride=chans)]
            outside[i][c] = v.reshape(slabs, rows, LANES).astype(outside[i].dtype)
        store(i).start()
    for k in order:
        own = [2 + part * n + k for part in range(4)]
        for i in own:
            load(i).wait()
        rows = inside[own[0]].shape[0]
        step = 8 if rows % 8 == 0 and rows > 8 else rows
        for r in range(0, rows, step):
            at = slice(r, r + step)
            new = adamw(*(inside[i][at] for i in own), RATES[k])
            for part, value in enumerate(new):
                outside[2 + 3 * k + part][at] = value
        for part in range(3):
            store(2 + 3 * k + part).start()
    for i in range(len(targets)):
        store(i).wait()


def per_device(
    skip, cotangent, enc_conv1, enc_conv2, gate_proj, gate_vector, dec_conv1, dec_conv2, enc_norms, dec_norms, *states
):
    nd, nc = lax.axis_size("depth"), lax.axis_size("chan")
    dm = Dims(nd, nc, skip.shape, enc_conv1.shape[0], dec_conv1.shape[0], gate_proj.shape[0] * nc)
    S, R, H, nx, RB, E = dm.s, dm.rows, dm.half, dm.nx, dm.rb, dm.ext
    Q = H // 2
    cin3 = dm.enc_all + dm.skip_all

    def own_block(size):
        return (size, lambda j: pl.multiple_of(j * size, size), 0)

    def core_blocks(size):
        return tuple(
            (size, lambda j, i=i: pl.multiple_of((2 * i + lax.rem(j, 2)) * size, size), i * size) for i in range(nx)
        )

    dm.convs = convs = (
        Conv(dm, dm.ce, dm.skip_all, (own_block(dm.cs),)),
        Conv(dm, dm.ce, dm.enc_all, (own_block(dm.ce),)),
        Conv(dm, dm.cd, cin3, core_blocks(dm.ce) + ((dm.skip_all, lambda j: dm.enc_all, nx * dm.ce),)),
        Conv(dm, dm.cd, dm.dec_all, core_blocks(dm.cd)),
    )
    params = (enc_conv1, enc_conv2, gate_proj, gate_vector, dec_conv1, dec_conv2, enc_norms, dec_norms)
    inputs = dict(
        skip=skip, cot=cotangent, w0=enc_conv1, w1=enc_conv2, w2=dec_conv1, w3=dec_conv2,
        gate=gate_proj, vector=gate_vector, en=enc_norms, dn=dec_norms,
    )
    shape = jax.ShapeDtypeStruct
    outs = dict(
        out=shape((S * R * dm.cd, LANES), F32),
        sg=shape((S * R * dm.cs, LANES), F32),
        **{f"g{i}": shape(a.shape, F32) for i, a in enumerate((enc_conv1, enc_conv2, dec_conv1, dec_conv2))},
        **{
            name: shape(a.shape, F32)
            for name, a in (("ggate", gate_proj), ("gvector", gate_vector), ("gen", enc_norms), ("gdn", dec_norms))
        },
    )
    gq = dm.g // nc

    def coarse(block):
        return pltpu.VMEM((2, nx, 3, Q, block, LANES), storage(block))

    def fine():
        return pltpu.VMEM((2, S + 2, E, dm.cf, LANES), storage(dm.cd))

    def f32(*dims):
        return pltpu.VMEM((*dims, LANES), F32)

    def tiles(*dims):
        return pltpu.VMEM((*dims, 16, LANES), BF16)

    def blocks(block, *dims):
        return pltpu.VMEM((*dims, block, LANES), storage(block))

    def sems(*dims):
        return pltpu.SemaphoreType.DMA(dims)

    scratch = dict(
        xp=coarse(dm.cs), xh=coarse(dm.ce), xc=coarse(dm.ce), xz2=coarse(dm.ce), xz1=coarse(dm.ce),
        own_skip=blocks(dm.cs, S, R + 2), xs=blocks(dm.cs, 2, nx, S + 2, E),
        own_cot=blocks(dm.cd, S, R), cots=blocks(dm.cd, nx, S, RB),
        d1=pltpu.VMEM((S + 2, E, cin3, LANES), BF16), xd=fine(), xz4=fine(), xz3=fine(),
        z1=f32(Q, dm.ce), z2=f32(Q, dm.ce), z3=f32(S * RB, dm.cf), z4=f32(S * RB, dm.cf),
        du_c=f32(Q, dm.ce), du_f=f32(S * RB, dm.cf), gg=f32(S * RB, dm.cf), cg=f32(Q, dm.ce),
        pre=f32(S + 2, E, dm.g), alpha=f32(S + 2, E, 1), pg=pltpu.VMEM((S * RB, dm.g, LANES), BF16),
        ug=f32(S, RB + 6, nx * dm.ce), cb=f32(S, H + 2, nx * dm.ce), dt=f32(S + 2, H, dm.enc_all),
        gv=f32(nc, dm.cs), sgp=f32(nx, S * RB, dm.cs), sgb=blocks(dm.cs, nx, S * RB), sgi=blocks(dm.cs, nx, S * RB),
        ob=blocks(dm.cd, nx, S * RB), oi=blocks(dm.cd, nx, S * RB),
        dzt=pltpu.VMEM((S, (RB + 4) * LANES, LANES), BF16), dzct=pltpu.VMEM((Q * LANES + 2 * dm.hcols, LANES), BF16),
        gw=f32(2 * LANES), dense=pltpu.VMEM((max(3 * cv.c for cv in convs), 3 * LANES), F32),
        fs=blocks(dm.ce, 3, nx, Q), fr=blocks(dm.ce, 3, nx, Q), fm=f32(nx, Q, dm.ce),
        st=f32(4, nd, 1), su=f32(4, nd * nx, 1), sv=pltpu.VMEM((1, nd * nx, gq, 3 * LANES), F32),
        norm_all=f32(nc, 8), rows=f32(max(dm.cs, dm.cd) * S * R),
        turned=f32(max(cv.chunks for cv in convs) * LANES),
        acc=pltpu.VMEM((max(3 * cv.c for cv in convs), 3 * LANES), F32),
        gate_all=pltpu.VMEM((nc, gq, 3 * LANES), F32), gate_t=pltpu.VMEM((2 * LANES, dm.g), F32),
        gate_own=pltpu.VMEM((nx * (dm.ce + dm.cs), dm.g), F32), gate_block=pltpu.VMEM((nc, gq, 3 * LANES), F32),
        **{f"wt{i}": pltpu.VMEM((3, cv.c, cv.wide), cv.kind) for i, cv in enumerate(convs)},
        **{
            f"wf{i}": pltpu.VMEM((cv.taps, 3 * cv.c) if i < 2 else (nx, cv.stored, 9 * cv.c), BF16)
            for i, cv in enumerate(convs)
        },
        **{f"wx{i}": pltpu.VMEM((nc, 3, cv.needed, cv.wide), cv.kind) for i, cv in enumerate(convs)},
        **{
            f"wb{i}": pltpu.VMEM((9 * cv.needed, 3 * nc * cv.o) if i < 2 else (3 * cv.needed, 9 * nc * cv.o), BF16)
            for i, cv in enumerate(convs)
        },
        flip=pltpu.VMEM((max(cv.tiles for cv in convs[2:]) * LANES, max(3 * cv.c for cv in convs[2:])), F32),
        **{f"gt{i}": tiles(cv.share * nd) for i, cv in enumerate(convs)},
        **{f"gr{i}": tiles(nd if i == 0 else nd // 2, cv.share) for i, cv in enumerate(convs)},
        **{f"gp{i}": tiles(nd // 2 * cv.share) for i, cv in enumerate(convs) if i > 0},
        **{f"ga{i}": tiles(cv.share * nd) for i, cv in enumerate(convs)},
        **{f"gs{i}": tiles(nx, convs[i].count) for i in (2, 3)},
        **{f"gx{i}": tiles(nx, convs[i].count) for i in (2, 3)},
        g_send=sems(len(GATHERS), 3, nx), g_recv=sems(len(GATHERS), 3),
        h_send=sems(len(GATHERS), 2 + nx), h_recv=sems(len(GATHERS)),
        x_send=sems(len(FINE), 3, 5), x_recv=sems(len(FINE), 3, 5),
        y_send=sems(len(FINE), 3), y_recv=sems(len(FINE), 3),
        t_send=sems(4), t_recv=sems(4), u_send=sems(5), u_recv=sems(5),
        f_send=sems(3, nx), f_recv=sems(3, nx), w_send=sems(4, nx + 1, nc), w_recv=sems(4, nx + 1, nc),
        p_send=sems(2, nx), p_recv=sems(2, nx), c_send=sems(2, nx), c_recv=sems(2, nx),
        o_send=sems(3, nx), o_recv=sems(3, nx), v_send=sems(2, nc), v_recv=sems(2, nc),
        r_send=sems(4), r_recv=sems(4), a_send=sems(4), a_recv=sems(4), q_send=sems(4, 2), q_recv=sems(4, 2),
    )
    vmem = pl.BlockSpec(memory_space=pltpu.VMEM)
    out, sg, grad1, grad2, grad3, grad4, ggate, gvector, gen, gdn = pl.pallas_call(
        functools.partial(kernel, dm, (*inputs, *outs, *scratch)),
        out_shape=tuple(outs.values()),
        in_specs=[vmem] * len(inputs),
        out_specs=[vmem] * len(outs),
        scratch_shapes=list(scratch.values()),
        compiler_params=pltpu.CompilerParams(
            has_side_effects=True, collective_id=0, vmem_limit_bytes=60 * 1024 * 1024
        ),
        name="step",
    )(*inputs.values())
    grads = (grad1, grad2, ggate, gvector, grad3, grad4, gen, gdn)
    operands = (out, sg, *params, *grads, *states)
    updated = (
        shape(cotangent.shape, BF16),
        shape(skip.shape, F32),
        *(shape(p.shape, F32) for p in params for _ in range(3)),
    )
    anywhere = pl.BlockSpec(memory_space=pl.ANY)
    return pl.pallas_call(
        update_kernel,
        out_shape=updated,
        in_specs=[anywhere] * len(operands),
        out_specs=[anywhere] * len(updated),
        scratch_shapes=[
            *(pltpu.VMEM(a.shape, a.dtype) for a in operands),
            *(pltpu.VMEM(a.shape, a.dtype) for a in updated),
            pltpu.SemaphoreType.DMA((len(operands),)),
            pltpu.SemaphoreType.DMA((len(updated),)),
        ],
        compiler_params=pltpu.CompilerParams(vmem_limit_bytes=60 * 1024 * 1024),
        name="update",
    )(*operands)


def solution(mesh):
    volume = P("chan", "depth", None, None)
    row, column, norms = P("chan", None), P(None, "chan"), P(None, None, "chan")
    params = (row, row, row, column, row, row, norms, norms)
    return jax.shard_map(
        per_device,
        mesh=mesh,
        in_specs=(volume, volume) + params * 3,
        out_specs=(volume, volume) + tuple(spec for spec in params for _ in range(3)),
        check_vma=False,
    )
```
